32 devices in a mesh: dp: 16 (over z, y, x), tensor: 2 (over core).
Axes of the slice: x: 2, y: 2, z: 4, core: 2. Of those that a mesh axis runs over, the one named last changes fastest.
Arguments:
- tokens: bfloat16 [24576, 1024], P(('dp', 'tensor')), may hold values from -6 to 6
- cotangent: bfloat16 [24576, 1024], P(('dp', 'tensor')), may hold values from -6 to 6
- lengths: int32 [16, 4], P('dp'), may hold values from 1 to 1024, 1536 in all within a row
- dealing: int32 [16, 4], P('dp'), may hold values from 0 to 3, each once within a row
- project_weight: float32 [3, 1024, 1024], P(None, 'dp', 'tensor'), may hold values from -0.1875 to 0.1875
- project_first: float32 [3, 1024, 1024], P(None, 'dp', 'tensor'), may hold values from -80 to 80
- project_second: float32 [3, 1024, 1024], P(None, 'dp', 'tensor'), may hold values from 12.288 to 49.152
- merge_weight: float32 [1024, 1024], P('tensor', 'dp'), may hold values from -3.5 to 3.5
- merge_first: float32 [1024, 1024], P('tensor', 'dp'), may hold values from -4 to 4
- merge_second: float32 [1024, 1024], P('tensor', 'dp'), may hold values from 0.072 to 0.288
- expand_weight: float32 [1024, 4096], P('dp', 'tensor'), may hold values from -0.1875 to 0.1875
- expand_first: float32 [1024, 4096], P('dp', 'tensor'), may hold values from -56 to 56
- expand_second: float32 [1024, 4096], P('dp', 'tensor'), may hold values from 6.144 to 24.576
- reduce_weight: float32 [4096, 1024], P('tensor', 'dp'), may hold values from -0.09375 to 0.09375
- reduce_first: float32 [4096, 1024], P('tensor', 'dp'), may hold values from -56 to 56
- reduce_second: float32 [4096, 1024], P('tensor', 'dp'), may hold values from 6.144 to 24.576
- vectors: float32 [8, 1024], replicated, may hold values from -1.5 to 3.33, as said below
- vector_first: float32 [8, 1024], replicated, may hold values from -112 to 112
- vector_second: float32 [8, 1024], replicated, may hold values from 24.576 to 98.304
- hidden_bias: float32 [4096], replicated, may hold values from -1.5 to 1.5
- hidden_first: float32 [4096], replicated, may hold values from -56 to 56
- hidden_second: float32 [4096], replicated, may hold values from 6.144 to 24.576
Outputs:
- encoded: bfloat16 [24576, 1024], P(('dp', 'tensor'))
- input_grad: bfloat16 [24576, 1024], P(('dp', 'tensor'))
- project_moment: float32 [3, 1024, 1024], P(None, 'dp', 'tensor')
- project_square: float32 [3, 1024, 1024], P(None, 'dp', 'tensor')
- project_master: float32 [3, 1024, 1024], P(None, 'dp', 'tensor')
- merge_moment: float32 [1024, 1024], P('tensor', 'dp')
- merge_square: float32 [1024, 1024], P('tensor', 'dp')
- merge_master: float32 [1024, 1024], P('tensor', 'dp')
- expand_moment: float32 [1024, 4096], P('dp', 'tensor')
- expand_square: float32 [1024, 4096], P('dp', 'tensor')
- expand_master: float32 [1024, 4096], P('dp', 'tensor')
- reduce_moment: float32 [4096, 1024], P('tensor', 'dp')
- reduce_square: float32 [4096, 1024], P('tensor', 'dp')
- reduce_master: float32 [4096, 1024], P('tensor', 'dp')
- vector_moment: float32 [8, 1024], replicated
- vector_square: float32 [8, 1024], replicated
- vector_master: float32 [8, 1024], replicated
- hidden_moment: float32 [4096], replicated
- hidden_square: float32 [4096], replicated
- hidden_master: float32 [4096], replicated
- vector_gradient: float32 [8, 1024], replicated
The draws below stay inside these ranges and needn't reach their ends.
Inputs may be any that keep to these rules, and one draw needn't show every extreme that they name: Each row holds the lengths of a group's 4 sequences, summing to 1536; the longest of every row is exactly 1024. `dealing`: each row is a permutation of the numbers of a group's sequences. `vectors`: rows in order: query bias, value bias, attention output bias, first norm's gain and shift, feed-forward output bias, second norm's gain and shift; gains are positive.
All inputs are finite; a program needn't handle non-finite values.
Results may differ from the reference program's by a relative error of at most 0.02.
Values may be sent and summed in bfloat16 or wider, within the bound.
A program may use at most 256 MiB of HBM per device.

```python
import math
import jax
import jax.numpy as jnp
import numpy as np
from jax import lax

D = 1024
HEADS = 16
HEAD_DIM = 64
FF = 4096
LEN = 1024
SEQ_GRP = 4
TOK_GRP = 1536
STEP = 10
GROUPS = 16
TOKENS = 24576


def draw_vectors(key, part):
    key = jax.random.fold_in(key, 11)
    bias_scales = jnp.array([0.5, 0.05, 0.3, 0.0, 0.3, 0.3, 0.0, 0.3], jnp.float32)[:, None]
    gain_rows = jnp.array([0.0, 0.0, 0.0, 1.0, 0.0, 0.0, 1.0, 0.0], jnp.float32)[:, None]
    base = jnp.clip(jax.random.normal(key, (8, D), jnp.float32), -3.0, 3.0)
    return gain_rows * jnp.exp(0.4 * base) + bias_scales * base


def level_of(rng, shape, cuts, low, largest):
    loudness, own = 1.0, jax.random.fold_in(rng, 6)
    for dim, shards_of in cuts:
        heights = jnp.exp(jax.random.uniform(jax.random.fold_in(own, dim), (shards_of,), jnp.float32, low / len(cuts), largest / len(cuts)))
        loudness = loudness * jnp.repeat(heights, shape[dim] // shards_of).reshape([-1 if axis == dim else 1 for axis in range(len(shape))])
    return loudness


def split_up(amount, total, most, skew):
    portions = [(1 << 20) // math.isqrt(grade ** skew) + 1 for grade in range(2, amount + 1)]
    rest, given = total - most - (amount - 1), [1] * (amount - 1)
    while rest > 0:
        movable = [i for i in range(amount - 1) if given[i] < most]
        whole, left = sum([portions[i] for i in movable]), rest
        for i in movable:
            addition = min(most - given[i], max(1, left * portions[i] // whole), rest)
            given[i] = given[i] + addition
            rest = rest - addition
    return np.array([most] + given)


def ragged_sizes(key, number_of, total, reach, skew):
    if number_of == 2:
        one = jax.random.randint(key, (), max(1, total - reach), min(reach, total - 1) + 1)
        return jnp.stack([one, total - one])
    sizes = jnp.asarray(split_up(number_of, total, reach, skew), jnp.int32)
    pairs = (number_of - 1) // 2
    source_of, receiver = sizes[1:1 + 2 * pairs:2], sizes[2:2 + 2 * pairs:2]
    slack = jnp.minimum(source_of - 1, reach - receiver)
    passed = jax.random.randint(jax.random.fold_in(key, 1), (pairs,), 0, 1 << 20) % (slack + 1)
    sizes = sizes.at[1:1 + 2 * pairs:2].set(source_of - passed).at[2:2 + 2 * pairs:2].set(receiver + passed)
    return sizes[jax.random.permutation(jax.random.fold_in(key, 2), number_of)]


def normal_values(rng, shape, width, bound, split=(), kind=jnp.bfloat16):
    result = width * jax.random.normal(rng, shape, jnp.float32)
    if split:
        result = result * level_of(rng, shape, split, -0.22, 0.18)
    return jnp.clip(result, -bound, bound).astype(kind)


def setup_inputs(seed: int = 0) -> dict:
    streams_of = jax.random.split(jax.random.key(seed), 23)
    return {
        "tokens": normal_values(streams_of[0], (TOKENS, D), 1.0, 6.0, ((0, 32),)),
        "cotangent": normal_values(streams_of[1], (TOKENS, D), 1.0, 6.0, ((0, 32),)),
        "lengths": jax.vmap(lambda own: ragged_sizes(own, SEQ_GRP, TOK_GRP, LEN, 2))(jax.random.split(streams_of[2], GROUPS)).reshape((GROUPS, SEQ_GRP)).astype(jnp.int32),
        "dealing": jax.vmap(lambda own: jax.random.permutation(own, SEQ_GRP))(jax.random.split(streams_of[3], GROUPS)).reshape((GROUPS, SEQ_GRP)).astype(jnp.int32),
        "project_weight": normal_values(streams_of[4], (3, D, D), D ** -0.5, 0.1875, ((1, 16), (2, 2)), jnp.float32),
        "project_first": normal_values(streams_of[5], (3, D, D), (0.08 * TOKENS ** 0.5), 80.0, ((1, 16), (2, 2)), jnp.float32),
        "project_second": jnp.clip(jnp.exp(math.log(49.152) - 1.3862944 * jax.random.uniform(streams_of[6], (3, D, D), jnp.float32) ** level_of(streams_of[6], (3, D, D), ((1, 16), (2, 2)), -0.2, 0.2)), 12.288, 49.152),
        "merge_weight": normal_values(streams_of[7], (D, D), (max(1, 3 * D // LEN)) ** -0.5, 3.5, ((0, 2), (1, 16)), jnp.float32),
        "merge_first": normal_values(streams_of[8], (D, D), (0.11 * (3 * TOKENS // LEN) ** 0.5), 4.0, ((0, 2), (1, 16)), jnp.float32),
        "merge_second": jnp.clip(jnp.exp(math.log(0.288) - 1.3862944 * jax.random.uniform(streams_of[9], (D, D), jnp.float32) ** level_of(streams_of[9], (D, D), ((0, 2), (1, 16)), -0.2, 0.2)), 0.072, 0.288),
        "expand_weight": normal_values(streams_of[10], (D, FF), D ** -0.5, 0.1875, ((0, 16), (1, 2)), jnp.float32),
        "expand_first": normal_values(streams_of[11], (D, FF), (0.055 * TOKENS ** 0.5), 56.0, ((0, 16), (1, 2)), jnp.float32),
        "expand_second": jnp.clip(jnp.exp(math.log(24.576) - 1.3862944 * jax.random.uniform(streams_of[12], (D, FF), jnp.float32) ** level_of(streams_of[12], (D, FF), ((0, 16), (1, 2)), -0.2, 0.2)), 6.144, 24.576),
        "reduce_weight": normal_values(streams_of[13], (FF, D), FF ** -0.5, 0.09375, ((0, 2), (1, 16)), jnp.float32),
        "reduce_first": normal_values(streams_of[14], (FF, D), (0.055 * TOKENS ** 0.5), 56.0, ((0, 2), (1, 16)), jnp.float32),
        "reduce_second": jnp.clip(jnp.exp(math.log(24.576) - 1.3862944 * jax.random.uniform(streams_of[15], (FF, D), jnp.float32) ** level_of(streams_of[15], (FF, D), ((0, 2), (1, 16)), -0.2, 0.2)), 6.144, 24.576),
        "vectors": draw_vectors(jax.random.fold_in(streams_of[22], 71), 0),
        "vector_first": normal_values(streams_of[17], (8, D), (0.11 * TOKENS ** 0.5), 112.0, (), jnp.float32),
        "vector_second": jnp.clip(jnp.exp(jax.random.uniform(streams_of[18], (8, D), jnp.float32, math.log(24.576), math.log(98.304))), 24.576, 98.304),
        "hidden_bias": normal_values(streams_of[19], (FF,), 0.3, 1.5, (), jnp.float32),
        "hidden_first": normal_values(streams_of[20], (FF,), (0.055 * TOKENS ** 0.5), 56.0, (), jnp.float32),
        "hidden_second": jnp.clip(jnp.exp(jax.random.uniform(streams_of[21], (FF,), jnp.float32, math.log(6.144), math.log(24.576))), 6.144, 24.576),
    }


beta_one = 0.9
beta_two = 0.999
adam_epsilon = 1e-08
weight_decay = 0.01
norm_epsilon = 1e-05
masked_score = -1e+30
rate_project = 0.03
rate_merge = 0.3
rate_expand = 0.03
rate_reduce = 0.015
rate_vectors = 0.4
rate_hidden = 0.1
highest = lax.Precision.HIGHEST

@jax.custom_vjp
def low(v):
    return lax.optimization_barrier(v.astype(jnp.bfloat16)).astype(jnp.float32)

@jax.custom_vjp
def low_back(v):
    return v

def low_keep(v):
    return (low(v), None)

def low_pass(kept, grad):
    return (grad,)

def back_keep(v):
    return (v, None)

def back_low(kept, grad):
    return (low(grad),)
low.defvjp(low_keep, low_pass)
low_back.defvjp(back_keep, back_low)

def arrange(lengths_row, dealing_row, total_rows):
    slot_ids = jnp.arange(lengths_row.shape[0], dtype=jnp.int32)
    rank_of = lax.optimization_barrier(jnp.sum(jnp.where(dealing_row[None, :] == slot_ids[:, None], slot_ids[None, :], 0), axis=1)).astype(jnp.int32)
    loader_start = (jnp.cumsum(lengths_row) - lengths_row).astype(jnp.int32)
    dealt_start = lax.optimization_barrier(jnp.sum(jnp.where(rank_of[None, :] < rank_of[:, None], lengths_row[None, :], 0), axis=1)).astype(jnp.int32)
    places = jnp.arange(total_rows, dtype=jnp.int32)
    inside_dealt = (places[:, None] >= dealt_start[None, :]) & (places[:, None] < (dealt_start + lengths_row)[None, :])
    segment = lax.optimization_barrier(jnp.sum(jnp.where(inside_dealt, slot_ids[None, :], 0), axis=1)).astype(jnp.int32)
    source = places + lax.optimization_barrier(jnp.sum(jnp.where(inside_dealt, (loader_start - dealt_start)[None, :], 0), axis=1)).astype(jnp.int32)
    inside_loader = (places[:, None] >= loader_start[None, :]) & (places[:, None] < (loader_start + lengths_row)[None, :])
    target = places + lax.optimization_barrier(jnp.sum(jnp.where(inside_loader, (dealt_start - loader_start)[None, :], 0), axis=1)).astype(jnp.int32)
    return (source, target, segment)

def normalize(values, gain_row, shift_row):
    center = values - lax.optimization_barrier(jnp.mean(values, axis=-1, keepdims=True))
    spread = lax.optimization_barrier(jnp.mean(center * center, axis=-1, keepdims=True))
    return center * lax.rsqrt(spread + norm_epsilon) * gain_row + shift_row

def encoder_layer(inputs, lengths_row, dealing_row, params):
    project_weight, merge_weight, expand_weight, reduce_weight, vectors, hidden_bias = params
    total_rows = inputs.shape[0]
    source, target, segment = arrange(lengths_row, dealing_row, total_rows)
    hidden = jnp.take(inputs, source, axis=0)
    mixed_rows = jnp.einsum('rd,cde->cre', hidden, low(project_weight), precision=highest)
    queries = low_back(low(mixed_rows[0] + vectors[0]))
    key_rows = low_back(low(mixed_rows[1]))
    value_rows = low_back(low(mixed_rows[2] + vectors[1]))
    same_sequence = segment[:, None] == segment[None, :]

    def split_heads(matrix):
        return matrix.reshape(total_rows, HEADS, HEAD_DIM).transpose(1, 0, 2)

    def one_head(triple):
        query_head, key_head, value_head = triple
        scores = jnp.dot(query_head, key_head.T, precision=highest) * HEAD_DIM ** (-0.5)
        scores = low_back(jnp.where(same_sequence, scores, masked_score))
        row_top = lax.optimization_barrier(jnp.max(scores, axis=-1, keepdims=True))
        exponent = jnp.exp(scores - row_top)
        probabilities = exponent / lax.optimization_barrier(jnp.sum(exponent, axis=-1, keepdims=True))
        return jnp.dot(low(probabilities), value_head, precision=highest)
    context = lax.map(jax.checkpoint(one_head), (split_heads(queries), split_heads(key_rows), split_heads(value_rows)))
    context = context.transpose(1, 0, 2).reshape(total_rows, D)
    context = low_back(low(context))
    branch = low_back(jnp.dot(context, low(merge_weight), precision=highest) + vectors[2])
    normed = normalize(hidden + branch, vectors[3], vectors[4])
    gelu_input = low_back(jnp.dot(low(normed), low(expand_weight), precision=highest) + hidden_bias)
    activated = low(jax.nn.gelu(gelu_input, approximate=False))
    feed_out = low_back(jnp.dot(activated, low(reduce_weight), precision=highest) + vectors[5])
    return normalize(normed + feed_out, vectors[6], vectors[7])

def adamw_update(master, moment, square, gradient, step_rate, decay_rate):
    moment_new = beta_one * moment + (1.0 - beta_one) * gradient
    square_new = beta_two * square + (1.0 - beta_two) * gradient * gradient
    moment_hat = moment_new / (1.0 - beta_one ** STEP)
    square_hat = square_new / (1.0 - beta_two ** STEP)
    master_new = master - step_rate * (moment_hat / (jnp.sqrt(square_hat) + adam_epsilon) + decay_rate * master)
    return (moment_new, square_new, master_new)

def reference(tokens, cotangent, lengths, dealing, project_weight, project_first, project_second, merge_weight, merge_first, merge_second, expand_weight, expand_first, expand_second, reduce_weight, reduce_first, reduce_second, vectors, vector_first, vector_second, hidden_bias, hidden_first, hidden_second):
    groups = lengths.shape[0]
    inputs = tokens.astype(jnp.float32).reshape(groups, TOK_GRP, D)
    params = (project_weight, merge_weight, expand_weight, reduce_weight, vectors, hidden_bias)

    def forward(inputs, params):
        checked = jax.checkpoint(encoder_layer)

        def advance(running, group_item):
            return (running, checked(group_item[0], group_item[1], group_item[2], params))
        unused, outputs = lax.scan(advance, jnp.zeros((), jnp.float32), (inputs, lengths, dealing))
        return outputs
    outputs, pullback = jax.vjp(forward, inputs, params)
    input_grads, grads = pullback(cotangent.astype(jnp.float32).reshape(outputs.shape))
    project_grad, merge_grad, expand_grad, reduce_grad, vector_grad, hidden_grads = grads
    project_moment, project_square, project_master = adamw_update(project_weight, project_first, project_second, project_grad, rate_project, weight_decay)
    merge_moment, merge_square, merge_master = adamw_update(merge_weight, merge_first, merge_second, merge_grad, rate_merge, weight_decay)
    expand_moment, expand_square, expand_master = adamw_update(expand_weight, expand_first, expand_second, expand_grad, rate_expand, weight_decay)
    reduce_moment, reduce_square, reduce_master = adamw_update(reduce_weight, reduce_first, reduce_second, reduce_grad, rate_reduce, weight_decay)
    vector_moment, vector_square, vector_master = adamw_update(vectors, vector_first, vector_second, vector_grad, rate_vectors, 0.0)
    hidden_moment, hidden_square, hidden_master = adamw_update(hidden_bias, hidden_first, hidden_second, hidden_grads, rate_hidden, 0.0)
    encoded = outputs.reshape(groups * TOK_GRP, D).astype(jnp.bfloat16)
    input_grad = input_grads.reshape(groups * TOK_GRP, D).astype(jnp.bfloat16)
    return (encoded, input_grad, project_moment, project_square, project_master, merge_moment, merge_square, merge_master, expand_moment, expand_square, expand_master, reduce_moment, reduce_square, reduce_master, vector_moment, vector_square, vector_master, hidden_moment, hidden_square, hidden_master, vector_grad)
```

```python
import functools

import jax
import jax.numpy as jnp
from jax import lax
from jax.experimental import pallas as pl
from jax.experimental.pallas import tpu as pltpu
from jax.sharding import PartitionSpec as P

HEAD_DIM = 64
LONGEST = 1024
STEP = 10
PAIR = 2 * HEAD_DIM
TILE = 256
MIB = 1024 * 1024
MESH = pl.DeviceIdType.MESH
LOW = jnp.bfloat16
WIDE = jnp.float32

beta_one = 0.9
beta_two = 0.999
adam_epsilon = 1e-08
weight_decay = 0.01
norm_epsilon = 1e-05
masked_score = -1e30
rate_project = 0.03
rate_merge = 0.3
rate_expand = 0.03
rate_reduce = 0.015
rate_vectors = 0.4
rate_hidden = 0.1


def dot_nn(a, b):
    return jnp.dot(a, b, preferred_element_type=WIDE)


def dot_nt(a, b):
    return lax.dot_general(a, b, (((1,), (1,)), ((), ())), preferred_element_type=WIDE)


def dot_tn(a, b):
    return lax.dot_general(a, b, (((0,), (0,)), ((), ())), preferred_element_type=WIDE)


def layout(lengths_row, dealing_row, total_rows):
    slots = jnp.arange(lengths_row.shape[0], dtype=jnp.int32)
    places = jnp.arange(total_rows, dtype=jnp.int32)
    rank_of = jnp.sum(jnp.where(dealing_row[None, :] == slots[:, None], slots[None, :], 0), axis=1)
    own_start = jnp.cumsum(lengths_row) - lengths_row
    dealt_start = jnp.sum(
        jnp.where(rank_of[None, :] < rank_of[:, None], lengths_row[None, :], 0), axis=1
    )
    longest = lengths_row == LONGEST
    short = jnp.where(longest, 0, lengths_row)
    start = jnp.where(longest, 0, LONGEST + jnp.cumsum(short) - short)

    def inside(begin):
        return (places[:, None] >= begin[None, :]) & (
            places[:, None] < (begin + lengths_row)[None, :]
        )

    def moved(begin, end):
        return places + jnp.sum(jnp.where(inside(begin), (end - begin)[None, :], 0), axis=1)

    segment = jnp.sum(jnp.where(inside(start), slots[None, :], 0), axis=1)
    return (
        segment,
        moved(start, own_start),
        moved(start, dealt_start),
        moved(own_start, start),
        moved(dealt_start, start),
    )


def pick_rows(index, rows):
    places = jnp.arange(rows, dtype=jnp.int32)
    return (index[:, None] == places[None, :]).astype(LOW)


def attend_kernel(qkv_ref, bias_ref, context_ref, total_ref):
    rows = qkv_ref.shape[0]
    lane = lax.broadcasted_iota(jnp.int32, (1, PAIR), 1)
    scale = HEAD_DIM ** (-0.5)
    for begin, size in ((0, LONGEST), (LONGEST, rows - LONGEST)):

        @pl.loop(0, size // TILE)
        def _(step):
            first = pl.multiple_of(begin + step * TILE, TILE)
            query = qkv_ref[pl.ds(first, TILE), 0:PAIR]
            key = qkv_ref[begin : begin + size, PAIR : 2 * PAIR]
            value = qkv_ref[begin : begin + size, 2 * PAIR : 3 * PAIR]
            outcome = []
            for head in range(2):
                chosen = jnp.where(lane // HEAD_DIM == head, scale, 0.0).astype(LOW)
                scores = dot_nt(query * chosen, key)
                if begin:
                    inner = pl.multiple_of(step * TILE, TILE)
                    scores = scores + bias_ref[pl.ds(inner, TILE), :]
                top = jnp.max(scores, axis=1, keepdims=True)
                exponent = jnp.exp(scores - top)
                total = jnp.sum(exponent, axis=1, keepdims=True)
                outcome.append(dot_nn(exponent.astype(LOW), value) / total)
                log_total = jnp.broadcast_to(top + jnp.log(total), (TILE, PAIR))
                total_ref[0, head : head + 1, pl.ds(first, TILE)] = log_total.T[0:1, :]
            context_ref[pl.ds(first, TILE), :] = jnp.where(
                lane < HEAD_DIM, outcome[0], outcome[1]
            ).astype(LOW)


def attend(qkv, bias):
    rows, width = qkv.shape
    pairs = width // (3 * PAIR)
    return pl.pallas_call(
        attend_kernel,
        grid=(pairs,),
        in_specs=[
            pl.BlockSpec((rows, 3 * PAIR), lambda p: (0, p)),
            pl.BlockSpec(bias.shape, lambda p: (0, 0)),
        ],
        out_specs=[
            pl.BlockSpec((rows, PAIR), lambda p: (0, p)),
            pl.BlockSpec((1, 8, rows), lambda p: (p, 0, 0)),
        ],
        out_shape=[
            jax.ShapeDtypeStruct((rows, pairs * PAIR), LOW),
            jax.ShapeDtypeStruct((pairs, 8, rows), WIDE),
        ],
        compiler_params=pltpu.CompilerParams(vmem_limit_bytes=48 * MIB),
        cost_estimate=pl.CostEstimate(
            flops=8 * pairs * PAIR * 1310720, bytes_accessed=8 * rows * width, transcendentals=0
        ),
    )(qkv, bias)


def attend_back_kernel(
    qkv_ref, bias_ref, context_ref, grad_ref, total_ref, out_ref, dot_ref, turned_ref, query_ref,
    upper_ref, sum_ref,
):
    rows = qkv_ref.shape[0]
    lane = lax.broadcasted_iota(jnp.int32, (1, PAIR), 1)
    scale = HEAD_DIM ** (-0.5)
    product = (grad_ref[...].astype(WIDE) * context_ref[...].astype(WIDE)).T
    for head in range(2):
        band = slice(head * HEAD_DIM, (head + 1) * HEAD_DIM)
        dot_ref[head : head + 1, :] = jnp.sum(product[band, :], axis=0, keepdims=True)
        chosen = lane // HEAD_DIM == head
        query_ref[head] = qkv_ref[:, 0:PAIR] * jnp.where(chosen, scale, 0.0).astype(LOW)
        upper_ref[head] = grad_ref[...] * jnp.where(chosen, 1.0, 0.0).astype(LOW)
    turned_ref[...] = qkv_ref[:, PAIR : 2 * PAIR].astype(WIDE).T.astype(LOW)
    for begin, size in ((0, LONGEST), (LONGEST, rows - LONGEST)):
        block = slice(begin, begin + size)
        sum_ref[:, block] = jnp.zeros((PAIR, size), WIDE)

        @pl.loop(0, size // TILE)
        def _(step):
            first = pl.multiple_of(begin + step * TILE, TILE)
            key = qkv_ref[pl.ds(first, TILE), PAIR : 2 * PAIR]
            value = qkv_ref[pl.ds(first, TILE), 2 * PAIR : 3 * PAIR]
            key_sum = jnp.zeros((TILE, PAIR), WIDE)
            value_sum = jnp.zeros((TILE, PAIR), WIDE)
            for head in range(2):
                band = slice(head * HEAD_DIM, (head + 1) * HEAD_DIM)
                query = query_ref[head, block, :]
                upper = upper_ref[head, block, :]
                scores = dot_nt(key, query)
                if begin:
                    inner = pl.multiple_of(step * TILE, TILE)
                    scores = scores + bias_ref[pl.ds(inner, TILE), :]
                probability = jnp.exp(scores - total_ref[0, head : head + 1, block])
                weight_grads = dot_nt(value, upper)
                score_grads = (
                    probability * (weight_grads - dot_ref[head : head + 1, block])
                ).astype(LOW)
                value_sum = value_sum + dot_nn(probability.astype(LOW), upper)
                key_sum = key_sum + dot_nn(score_grads, query)
                sum_ref[band, block] += dot_nn(turned_ref[band, pl.ds(first, TILE)], score_grads)
            out_ref[pl.ds(first, TILE), PAIR : 2 * PAIR] = key_sum.astype(LOW)
            out_ref[pl.ds(first, TILE), 2 * PAIR : 3 * PAIR] = value_sum.astype(LOW)

        out_ref[block, 0:PAIR] = (sum_ref[:, block] * scale).T.astype(LOW)


def attend_back(qkv, bias, context, grad, totals):
    rows, width = qkv.shape
    pairs = width // (3 * PAIR)
    return pl.pallas_call(
        attend_back_kernel,
        grid=(pairs,),
        in_specs=[
            pl.BlockSpec((rows, 3 * PAIR), lambda p: (0, p)),
            pl.BlockSpec(bias.shape, lambda p: (0, 0)),
            pl.BlockSpec((rows, PAIR), lambda p: (0, p)),
            pl.BlockSpec((rows, PAIR), lambda p: (0, p)),
            pl.BlockSpec((1, 8, rows), lambda p: (p, 0, 0)),
        ],
        out_specs=pl.BlockSpec((rows, 3 * PAIR), lambda p: (0, p)),
        out_shape=jax.ShapeDtypeStruct((rows, width), LOW),
        scratch_shapes=[
            pltpu.VMEM((8, rows), WIDE),
            pltpu.VMEM((PAIR, rows), LOW),
            pltpu.VMEM((2, rows, PAIR), LOW),
            pltpu.VMEM((2, rows, PAIR), LOW),
            pltpu.VMEM((PAIR, rows), WIDE),
        ],
        compiler_params=pltpu.CompilerParams(vmem_limit_bytes=48 * MIB),
        cost_estimate=pl.CostEstimate(
            flops=20 * pairs * PAIR * 1310720, bytes_accessed=12 * rows * width, transcendentals=0
        ),
    )(qkv, bias, context, grad, totals)


def place():
    me = lax.axis_index("dp")
    z, y, x = me // 4, (me // 2) % 2, me % 2
    return me, z, y, x


def line_slots(z, depth):
    slots = []
    for step in range(depth - 1):
        slots.append((z - 1 - step, z - 1 - step >= 0, 1))
        slots.append((z + 1 + step, z + 1 + step < depth, -1))
    return slots


def remote(source, target, send, receive, device):
    return pltpu.make_async_remote_copy(
        src_ref=source,
        dst_ref=target,
        send_sem=send,
        recv_sem=receive,
        device_id={"dp": device},
        device_id_type=MESH,
    )


def greet_line(me, z, y, x, depth, extra=()):
    barrier = pltpu.get_barrier_semaphore()
    for peer in (z * 4 + y * 2 + 1 - x, z * 4 + (1 - y) * 2 + x):
        pl.semaphore_signal(barrier, inc=1, device_id={"dp": peer}, device_id_type=MESH)

    @pl.when(z > 0)
    def _():
        pl.semaphore_signal(barrier, inc=1, device_id={"dp": me - 4}, device_id_type=MESH)

    @pl.when(z < depth - 1)
    def _():
        pl.semaphore_signal(barrier, inc=1, device_id={"dp": me + 4}, device_id_type=MESH)

    for peer in extra:
        pl.semaphore_signal(barrier, inc=1, device_id=peer, device_id_type=MESH)
    ends = jnp.where(z > 0, 1, 0) + jnp.where(z < depth - 1, 1, 0)
    pl.semaphore_wait(barrier, 2 + len(extra) + ends)


def gather_kernel(depth, count, *refs):
    shards, wholes = refs[:count], refs[count : 2 * count]
    own_sem, z_send, z_recv, xa_send, xa_recv, yb_send, yb_recv, ya_send, ya_recv, xb_send, xb_recv = refs[2 * count :]
    me, z, y, x = place()
    x_peer, y_peer = z * 4 + y * 2 + 1 - x, z * 4 + (1 - y) * 2 + x

    def block(zb, yb, xb):
        return zb * 4 + yb * 2 + xb

    def columns(i, second):
        half = wholes[i].shape[2] // 2
        return pl.ds(half if second else 0, half)

    def along_z(i, zb, way):
        part = wholes[i].at[block(zb, y, x)]
        return remote(part, part, z_send.at[i, zb], z_recv.at[i, zb], me + 4 * way)

    def part_copy(i, blk, second, send, receive, peer):
        part = wholes[i].at[blk, :, columns(i, second)]
        return remote(part, part, send, receive, peer)

    def xa(i, zb, xb):
        return part_copy(i, block(zb, y, xb), False, xa_send.at[i, zb], xa_recv.at[i, zb], x_peer)

    def yb(i, zb, yy):
        return part_copy(i, block(zb, yy, x), True, yb_send.at[i, zb], yb_recv.at[i, zb], y_peer)

    def ya(i, zb, yy, xb):
        return part_copy(
            i, block(zb, yy, xb), False, ya_send.at[i, zb, xb], ya_recv.at[i, zb, xb], y_peer
        )

    def xb(i, zb, yy, xx):
        return part_copy(
            i, block(zb, yy, xx), True, xb_send.at[i, zb, yy], xb_recv.at[i, zb, yy], x_peer
        )

    def first_stage(zb):
        for i in range(count):
            xa(i, zb, x).start()
            yb(i, zb, y).start()
            ya(i, zb, y, x).start()
            xb(i, zb, y, x).start()

    def second_stage(zb):
        for i in range(count):
            xa(i, zb, 1 - x).wait_recv()
            ya(i, zb, y, 1 - x).start()
            yb(i, zb, 1 - y).wait_recv()
            xb(i, zb, 1 - y, x).start()

    for i in range(count):
        pltpu.make_async_copy(shards[i], wholes[i].at[me], own_sem.at[i]).start()
    greet_line(me, z, y, x, depth)
    for i in range(count):
        pltpu.make_async_copy(shards[i], wholes[i].at[me], own_sem.at[i]).wait()

    @pl.when(z < depth - 1)
    def _():
        for i in range(count):
            along_z(i, z, 1).start()

    @pl.when(z > 0)
    def _():
        for i in range(count):
            part = wholes[i].at[me]
            remote(part, part, z_send.at[i, depth], z_recv.at[i, z], me - 4).start()

    first_stage(z)
    slots = line_slots(z, depth)
    late = [(z, None)]
    for step in range(depth - 1):
        for zb, valid, way in slots[2 * step : 2 * step + 2]:

            @pl.when(valid)
            def _(zb=zb, way=way):
                on = (z + way >= 0) & (z + way < depth)
                for i in range(count):
                    along_z(i, zb, way).wait_recv()

                    @pl.when(on)
                    def _():
                        along_z(i, zb, way).start()

                first_stage(zb)

        for zb, valid in late:
            if valid is None:
                second_stage(zb)
            else:

                @pl.when(valid)
                def _(zb=zb):
                    second_stage(zb)

        late = [(zb, valid) for zb, valid, _ in slots[2 * step : 2 * step + 2]]
    for zb, valid in late:

        @pl.when(valid)
        def _(zb=zb):
            second_stage(zb)

    for i in range(count):
        for zb in range(depth):
            for other in range(2):
                ya(i, zb, 1 - y, other).wait_recv()
                xb(i, zb, other, 1 - x).wait_recv()
                ya(i, zb, y, other).wait_send()
                xb(i, zb, other, x).wait_send()
            xa(i, zb, x).wait_send()
            yb(i, zb, y).wait_send()

        @pl.when(z < depth - 1)
        def _():
            along_z(i, z, 1).wait_send()

        @pl.when(z > 0)
        def _():
            part = wholes[i].at[me]
            remote(part, part, z_send.at[i, depth], z_recv.at[i, z], me - 4).wait_send()

        for zb, valid, way in slots:

            @pl.when(valid & (z + way >= 0) & (z + way < depth))
            def _(zb=zb, way=way):
                along_z(i, zb, way).wait_send()


def gather(shards, parts):
    depth, count = parts // 4, len(shards)
    sem = pltpu.SemaphoreType.DMA
    whole = pl.pallas_call(
        functools.partial(gather_kernel, depth, count),
        in_specs=[pl.BlockSpec(memory_space=pl.ANY)] * count,
        out_specs=[pl.BlockSpec(memory_space=pl.ANY)] * count,
        out_shape=[jax.ShapeDtypeStruct((parts, *s.shape), s.dtype) for s in shards],
        scratch_shapes=[
            sem((count,)),
            sem((count, depth + 1)),
            sem((count, depth)),
            *[sem((count, depth))] * 4,
            *[sem((count, depth, 2))] * 4,
        ],
        compiler_params=pltpu.CompilerParams(collective_id=0, has_side_effects=True),
    )(*shards)
    return [w.reshape(parts * w.shape[1], w.shape[2]) for w in whole]


def scatter_kernel(depth, count, *refs):
    grads, vector_ref = refs[:count], refs[count]
    shards, vector_out = refs[count + 1 : 2 * count + 1], refs[2 * count + 1]
    refs = refs[2 * count + 2 :]
    buffers = [refs[10 * i : 10 * i + 10] for i in range(count)]
    (
        vector_buffer, vector_send, vector_recv, a1_send, a1_recv, b1_send, b1_recv,
        a2_send, a2_recv, b2_send, b2_recv, z_send, z_recv,
    ) = refs[10 * count :]
    me, z, y, x = place()
    member = lax.axis_index("tensor")
    x_peer, y_peer = z * 4 + y * 2 + 1 - x, z * 4 + (1 - y) * 2 + x
    chunk = 16
    levels = depth.bit_length() - 1

    def block(zb, yb, xb):
        return zb * 4 + yb * 2 + xb

    partners = [{"tensor": 1 - member}, {"dp": x_peer}, {"dp": y_peer}]
    for level in range(levels):
        reach = 1 << level
        partners.append({"dp": me + 4 * reach * (1 - 2 * ((z // reach) % 2))})

    def vector_copy(step):
        return pltpu.make_async_remote_copy(
            src_ref=vector_buffer.at[step],
            dst_ref=vector_buffer.at[len(partners) + 1 + step],
            send_sem=vector_send.at[step],
            recv_sem=vector_recv.at[step],
            device_id=partners[step],
            device_id_type=MESH,
        )

    def vector_step(step):
        if step == 0:
            vector_buffer[0] = vector_ref[...]
        elif step <= len(partners):
            vector_copy(step - 1).wait_recv()
            vector_buffer[step] = vector_buffer[step - 1] + vector_buffer[len(partners) + step]
        if step < len(partners):
            vector_copy(step).start()
        if step == len(partners):
            vector_out[...] = vector_buffer[step]

    def a1(i, zb):
        half = grads[i].shape[2] // 2
        return remote(
            grads[i].at[pl.ds(block(zb, 1 - y, 0), 2), :, pl.ds(0, half)],
            buffers[i][0].at[zb],
            a1_send.at[i, zb],
            a1_recv.at[i, zb],
            y_peer,
        )

    def b1(i, zb, yy):
        half = grads[i].shape[2] // 2
        return remote(
            grads[i].at[block(zb, yy, 1 - x), :, pl.ds(half, half)],
            buffers[i][1].at[zb, yy],
            b1_send.at[i, zb, yy],
            b1_recv.at[i, zb, yy],
            x_peer,
        )

    def a2(i, zb):
        return remote(
            buffers[i][2].at[zb], buffers[i][4].at[zb], a2_send.at[i, zb], a2_recv.at[i, zb], x_peer
        )

    def b2(i, zb):
        return remote(
            buffers[i][3].at[zb], buffers[i][5].at[zb], b2_send.at[i, zb], b2_recv.at[i, zb], y_peer
        )

    def along_z(i, zb, way):
        slot = zb if way > 0 else zb + (depth - zb) * jnp.where(zb == z - 1, 1, 0)
        return remote(
            buffers[i][9].at[zb],
            buffers[i][8].at[slot],
            z_send.at[i, zb],
            z_recv.at[i, slot],
            me + 4 * way,
        )

    def from_z(i, slot):
        return remote(
            buffers[i][9].at[0], buffers[i][8].at[slot], z_send.at[i, 0], z_recv.at[i, slot], me
        )

    def open_slot(zb):
        for i in range(count):
            a1(i, zb).start()
            b1(i, zb, 0).start()
            b1(i, zb, 1).start()

    def first_sum(zb):
        for i in range(count):
            half = grads[i].shape[2] // 2
            r1a, r1b, t1a, t1b, _, _, s2a, s2b, _, _ = buffers[i]
            a1(i, zb).wait_recv()

            @pl.loop(0, t1a.shape[1] // chunk)
            def _(step):
                rows = pl.ds(pl.multiple_of(step * chunk, chunk), chunk)
                t1a[zb, rows, :] = (
                    grads[i][block(zb, y, 1 - x), rows, 0:half].astype(WIDE)
                    + r1a[zb, 1 - x, rows, :].astype(WIDE)
                ).astype(LOW)

            a2(i, zb).start()
            b1(i, zb, 0).wait_recv()
            b1(i, zb, 1).wait_recv()

            @pl.loop(0, t1a.shape[1] // chunk)
            def _(step):
                rows = pl.ds(pl.multiple_of(step * chunk, chunk), chunk)
                t1b[zb, rows, :] = (
                    grads[i][block(zb, 1 - y, x), rows, half : 2 * half].astype(WIDE)
                    + r1b[zb, 1 - y, rows, :].astype(WIDE)
                ).astype(LOW)

            b2(i, zb).start()

            @pl.loop(0, t1a.shape[1] // chunk)
            def _(step):
                rows = pl.ds(pl.multiple_of(step * chunk, chunk), chunk)
                s2a[zb, rows, :] = grads[i][block(zb, y, x), rows, 0:half].astype(WIDE) + r1a[
                    zb, x, rows, :
                ].astype(WIDE)
                s2b[zb, rows, :] = grads[i][block(zb, y, x), rows, half : 2 * half].astype(
                    WIDE
                ) + r1b[zb, y, rows, :].astype(WIDE)

    def second_sum(i, zb):
        _, _, _, _, r2a, r2b, s2a, s2b, _, _ = buffers[i]
        a2(i, zb).wait_recv()
        b2(i, zb).wait_recv()

        @pl.loop(0, r2a.shape[1] // chunk)
        def _(step):
            rows = pl.ds(pl.multiple_of(step * chunk, chunk), chunk)
            s2a[zb, rows, :] += r2a[zb, rows, :].astype(WIDE)
            s2b[zb, rows, :] += r2b[zb, rows, :].astype(WIDE)

    def add_z(i, zb, slot):
        _, _, _, _, _, _, s2a, s2b, rz, _ = buffers[i]
        half = grads[i].shape[2] // 2
        from_z(i, slot).wait_recv()

        @pl.loop(0, s2a.shape[1] // chunk)
        def _(step):
            rows = pl.ds(pl.multiple_of(step * chunk, chunk), chunk)
            s2a[zb, rows, :] += rz[slot, rows, 0:half].astype(WIDE)
            s2b[zb, rows, :] += rz[slot, rows, half : 2 * half].astype(WIDE)

    def pass_on(zb, way):
        for i in range(count):
            _, _, _, _, _, _, s2a, s2b, _, tz = buffers[i]
            half = grads[i].shape[2] // 2
            second_sum(i, zb)

            @pl.when((z - way >= 0) & (z - way < depth))
            def _():
                add_z(i, zb, zb)

            @pl.loop(0, s2a.shape[1] // chunk)
            def _(step):
                rows = pl.ds(pl.multiple_of(step * chunk, chunk), chunk)
                tz[zb, rows, 0:half] = s2a[zb, rows, :].astype(LOW)
                tz[zb, rows, half : 2 * half] = s2b[zb, rows, :].astype(LOW)

            along_z(i, zb, way).start()

    def finish():
        for i in range(count):
            _, _, _, _, _, _, s2a, s2b, _, _ = buffers[i]
            half = grads[i].shape[2] // 2
            second_sum(i, z)

            @pl.when(z > 0)
            def _():
                add_z(i, z, z)

            @pl.when(z < depth - 1)
            def _():
                add_z(i, z, depth)

            @pl.loop(0, s2a.shape[1] // chunk)
            def _(step):
                rows = pl.ds(pl.multiple_of(step * chunk, chunk), chunk)
                shards[i][rows, 0:half] = s2a[z, rows, :]
                shards[i][rows, half : 2 * half] = s2b[z, rows, :]

    def when(valid, act):
        if valid is None:
            act()
        else:
            pl.when(valid)(act)

    groups = []
    for step in reversed(range(depth - 1)):
        groups.append([(z + 1 + step, z + 1 + step < depth, 1), (z - 1 - step, z - 1 - step >= 0, -1)])
    groups.append([(z, None, 0)])

    greet_line(me, z, y, x, depth, [partners[0], *partners[3:]])
    vector_step(0)
    for group in groups[:2]:
        for zb, valid, _ in group:
            when(valid, functools.partial(open_slot, zb))
    vector_at = 1
    for at, group in enumerate(groups):
        for zb, valid, _ in group:
            when(valid, functools.partial(first_sum, zb))
        if at + 2 < len(groups):
            for zb, valid, _ in groups[at + 2]:
                when(valid, functools.partial(open_slot, zb))
        vector_step(vector_at)
        vector_at += 1
        if at:
            for zb, valid, way in groups[at - 1]:
                when(valid, functools.partial(pass_on, zb, way))
    while vector_at <= len(partners):
        vector_step(vector_at)
        vector_at += 1
    finish()

    for step in range(len(partners)):
        vector_copy(step).wait_send()
    for i in range(count):
        for zb in range(depth):
            a1(i, zb).wait_send()
            b1(i, zb, 0).wait_send()
            b1(i, zb, 1).wait_send()
            a2(i, zb).wait_send()
            b2(i, zb).wait_send()
        for group in groups[:-1]:
            for zb, valid, way in group:

                @pl.when(valid)
                def _(zb=zb, way=way):
                    along_z(i, zb, way).wait_send()


def scatter(grads, vector, parts):
    depth, count = parts // 4, len(grads)
    rows = grads[0].shape[0] // parts
    sem = pltpu.SemaphoreType.DMA
    partners = 3 + depth.bit_length() - 1
    scratch = []
    for g in grads:
        n = g.shape[1]
        half = n // 2
        scratch += [pltpu.VMEM((depth, 2, rows, half), LOW)] * 2
        scratch += [pltpu.VMEM((depth, rows, half), LOW)] * 4
        scratch += [pltpu.VMEM((depth, rows, half), WIDE)] * 2
        scratch += [pltpu.VMEM((depth + 1, rows, n), LOW), pltpu.VMEM((depth, rows, n), LOW)]
    vmem = pl.BlockSpec(memory_space=pltpu.VMEM)
    return pl.pallas_call(
        functools.partial(scatter_kernel, depth, count),
        in_specs=[vmem] * (count + 1),
        out_specs=[vmem] * (count + 1),
        out_shape=[
            *[jax.ShapeDtypeStruct((rows, g.shape[1]), WIDE) for g in grads],
            jax.ShapeDtypeStruct(vector.shape, WIDE),
        ],
        scratch_shapes=[
            *scratch,
            pltpu.VMEM((2 * partners + 1, *vector.shape), WIDE),
            sem((partners,)),
            sem((partners,)),
            *[sem((count, depth))] * 2,
            *[sem((count, depth, 2))] * 2,
            *[sem((count, depth))] * 4,
            sem((count, depth)),
            sem((count, depth + 1)),
        ],
        compiler_params=pltpu.CompilerParams(
            collective_id=1, has_side_effects=True, vmem_limit_bytes=60 * MIB
        ),
    )(*[g.reshape(parts, rows, g.shape[1]) for g in grads], vector)


def normalize_parts(values):
    center = values - jnp.mean(values, axis=-1, keepdims=True)
    spread = jnp.mean(center * center, axis=-1, keepdims=True)
    inverse = lax.rsqrt(spread + norm_epsilon)
    return (center * inverse, inverse)


def normal_back(upstream, gain_row, normal, inverse):
    scaled = upstream * gain_row
    return inverse * (
        scaled
        - jnp.mean(scaled, axis=-1, keepdims=True)
        - normal * jnp.mean(scaled * normal, axis=-1, keepdims=True)
    )


def gelu_slope(gelu_input):
    return (
        0.5 * (1.0 + lax.erf(gelu_input * 0.7071067811865476))
        + gelu_input * jnp.exp(-0.5 * gelu_input * gelu_input) * 0.3989422804014327
    )


def adamw_update(master, moment, square, gradient, step_rate, decay_rate):
    moment_new = beta_one * moment + (1.0 - beta_one) * gradient
    square_new = beta_two * square + (1.0 - beta_two) * gradient * gradient
    moment_hat = moment_new / (1.0 - beta_one**STEP)
    square_hat = square_new / (1.0 - beta_two**STEP)
    master_new = master - step_rate * (
        moment_hat / (jnp.sqrt(square_hat) + adam_epsilon) + decay_rate * master
    )
    return (moment_new, square_new, master_new)


def local(
    tokens,
    cotangent,
    lengths,
    dealing,
    project_weight,
    project_first,
    project_second,
    merge_weight,
    merge_first,
    merge_second,
    expand_weight,
    expand_first,
    expand_second,
    reduce_weight,
    reduce_first,
    reduce_second,
    vectors,
    vector_first,
    vector_second,
    hidden_bias,
    hidden_first,
    hidden_second,
):
    parts = lax.axis_size("dp")
    member = lax.axis_index("tensor")
    other = 1 - member
    half_rows, model_width = tokens.shape
    total_rows = 2 * half_rows
    width_half = project_weight.shape[2]
    pairs = width_half // PAIR
    hidden_half = expand_weight.shape[1]
    shard_rows = expand_weight.shape[0]
    own_begin = member * half_rows
    by_kernel = parts % 4 == 0 and (parts & (parts - 1)) == 0 and shard_rows % 16 == 0

    def swap(value):
        return lax.ppermute(value, "tensor", [(0, 1), (1, 0)])

    def own(value, size, which=member):
        return lax.dynamic_slice_in_dim(value, which * size, size, 0)

    segment, own_of, dealt_of, from_own, from_dealt = layout(lengths[0], dealing[0], total_rows)

    def own_first(index):
        return lax.rem(index - own_begin + total_rows, total_rows)

    shards = [
        project_weight.astype(LOW)
        .reshape(3, shard_rows, pairs, PAIR)
        .transpose(1, 2, 0, 3)
        .reshape(shard_rows, 3 * width_half),
        merge_weight.astype(LOW).T,
        expand_weight.astype(LOW),
        reduce_weight.astype(LOW).T,
    ]
    token_pair = jnp.concatenate([tokens, swap(tokens)], axis=0)
    upper_pair = jnp.concatenate([cotangent, swap(cotangent)], axis=0)
    if by_kernel:
        project, merge, expand, reduce = gather(shards, parts)
    else:
        project, merge, expand, reduce = [
            lax.all_gather(s, "dp", axis=0, tiled=True) for s in shards
        ]
    merge_far, expand_far, reduce_far = swap(merge), swap(expand), swap(reduce)

    hidden = dot_nn(pick_rows(own_first(own_of), total_rows), token_pair).astype(LOW)
    upstream = dot_nn(pick_rows(own_first(own(dealt_of, half_rows)), total_rows), upper_pair)
    zeros_pair = jnp.zeros((pairs, PAIR), WIDE)
    bias_row = jnp.stack(
        [
            own(vectors[0], width_half).reshape(pairs, PAIR),
            zeros_pair,
            own(vectors[1], width_half).reshape(pairs, PAIR),
        ],
        axis=1,
    ).reshape(-1)
    qkv = (dot_nn(hidden, project) + bias_row).astype(LOW)
    short = segment[LONGEST:]
    score_bias = jnp.where(short[:, None] == short[None, :], 0.0, masked_score).astype(WIDE)
    context, totals = attend(qkv, score_bias)

    context_own = own(context, half_rows)
    context_far = swap(own(context, half_rows, other))
    branch = dot_nt(context_own, merge) + dot_nt(context_far, merge_far)
    hidden_own = own(hidden, half_rows).astype(WIDE)
    normal_early, inverse_early = normalize_parts(hidden_own + branch + vectors[2])
    normed = normal_early * vectors[3] + vectors[4]
    normed_low = normed.astype(LOW)
    bias_own = own(hidden_bias, hidden_half)
    bias_far = own(hidden_bias, hidden_half, other)
    inner_own = dot_nn(normed_low, expand) + bias_own
    inner_far = dot_nn(normed_low, expand_far) + bias_far
    active_own = jax.nn.gelu(inner_own, approximate=False).astype(LOW)
    active_far = jax.nn.gelu(inner_far, approximate=False).astype(LOW)
    feed = dot_nt(active_own, reduce) + dot_nt(active_far, reduce_far) + vectors[5]
    normal_late, inverse_late = normalize_parts(normed + feed)
    encoded = (normal_late * vectors[6] + vectors[7]).astype(LOW)
    encoded_pair = jnp.concatenate([encoded, swap(encoded)], axis=0)
    encoded_out = dot_nn(
        pick_rows(own_first(own(from_dealt, half_rows)), total_rows), encoded_pair
    ).astype(LOW)
    late_gain = jnp.sum(upstream * normal_late, axis=0)
    late_shift = jnp.sum(upstream, axis=0)
    feed_grad = normal_back(upstream, vectors[6], normal_late, inverse_late)
    feed_low = feed_grad.astype(LOW)
    feed_bias = jnp.sum(feed_low.astype(WIDE), axis=0)

    inner_grad_far = (dot_nn(feed_low, reduce_far) * gelu_slope(inner_far)).astype(LOW)
    reduce_grad_far = swap(dot_tn(feed_low, active_far).astype(LOW))
    expand_grad_far = swap(dot_tn(normed_low, inner_grad_far).astype(LOW))
    inner_grad_own = (dot_nn(feed_low, reduce) * gelu_slope(inner_own)).astype(LOW)
    reduce_grad = dot_tn(feed_low, active_own) + reduce_grad_far.astype(WIDE)
    expand_grad = dot_tn(normed_low, inner_grad_own) + expand_grad_far.astype(WIDE)
    hidden_part_own = jnp.sum(inner_grad_own.astype(WIDE), axis=0)
    hidden_part_far = jnp.sum(inner_grad_far.astype(WIDE), axis=0)
    normed_grad = dot_nt(inner_grad_own, expand) + dot_nt(inner_grad_far, expand_far) + feed_grad
    early_gain = jnp.sum(normed_grad * normal_early, axis=0)
    early_shift = jnp.sum(normed_grad, axis=0)
    branch_grad = normal_back(normed_grad, vectors[3], normal_early, inverse_early)
    branch_low = branch_grad.astype(LOW)
    merge_bias = jnp.sum(branch_low.astype(WIDE), axis=0)

    grad_own = dot_nn(branch_low, merge).astype(LOW)
    grad_far = swap(dot_nn(branch_low, merge_far).astype(LOW))
    context_grad = jnp.where(
        member == 0,
        jnp.concatenate([grad_own, grad_far], axis=0),
        jnp.concatenate([grad_far, grad_own], axis=0),
    )
    merge_grad_far = swap(dot_tn(branch_low, context_far).astype(LOW))
    merge_grad = dot_tn(branch_low, context_own) + merge_grad_far.astype(WIDE)
    mixed_grads = attend_back(qkv, score_bias, context, context_grad, totals)
    project_grad = dot_tn(hidden, mixed_grads)
    mixed_sums = jnp.sum(mixed_grads.astype(WIDE), axis=0).reshape(pairs, 3, PAIR)
    input_terms = dot_nt(mixed_grads, project)
    own_part = own(input_terms, half_rows) + branch_grad
    input_terms = lax.dynamic_update_slice_in_dim(input_terms, own_part, own_begin, 0).astype(LOW)
    input_far = swap(
        dot_nn(pick_rows(own(from_own, half_rows, other), total_rows), input_terms).astype(LOW)
    )
    input_grad = (
        dot_nn(pick_rows(own(from_own, half_rows), total_rows), input_terms)
        + input_far.astype(WIDE)
    ).astype(LOW)

    zeros_width = jnp.zeros((model_width,), WIDE)
    zeros_hidden = jnp.zeros_like(hidden_bias)
    hidden_total = lax.dynamic_update_slice_in_dim(
        lax.dynamic_update_slice_in_dim(
            zeros_hidden, hidden_part_own, member * hidden_half, 0
        ),
        hidden_part_far,
        other * hidden_half,
        0,
    )
    vector_rows = [
        lax.dynamic_update_slice_in_dim(
            zeros_width, mixed_sums[:, 0].reshape(-1), member * width_half, 0
        ),
        lax.dynamic_update_slice_in_dim(
            zeros_width, mixed_sums[:, 2].reshape(-1), member * width_half, 0
        ),
        merge_bias,
        early_gain,
        early_shift,
        feed_bias,
        late_gain,
        late_shift,
    ]
    small = jnp.concatenate(
        [
            jnp.stack(vector_rows),
            hidden_total.reshape(-1, model_width),
            jnp.zeros((4, model_width), WIDE),
        ],
        axis=0,
    )
    grads = [g.astype(LOW) for g in (project_grad, merge_grad, expand_grad, reduce_grad)]
    if by_kernel:
        *grads, small = scatter(grads, small, parts)
    else:
        grads = [lax.psum_scatter(g, "dp", scatter_dimension=0, tiled=True) for g in grads]
        grads = [g.astype(WIDE) for g in grads]
        small = lax.psum(small, ("dp", "tensor"))
    project_shard, merge_shard, expand_shard, reduce_shard = grads
    project_shard = (
        project_shard.reshape(shard_rows, pairs, 3, PAIR)
        .transpose(2, 0, 1, 3)
        .reshape(3, shard_rows, width_half)
    )
    vector_grad = small[:8]
    hidden_grad = small[8:12].reshape(-1)
    return (
        encoded_out,
        input_grad,
        *adamw_update(
            project_weight, project_first, project_second, project_shard, rate_project, weight_decay
        ),
        *adamw_update(
            merge_weight, merge_first, merge_second, merge_shard.T, rate_merge, weight_decay
        ),
        *adamw_update(
            expand_weight, expand_first, expand_second, expand_shard, rate_expand, weight_decay
        ),
        *adamw_update(
            reduce_weight, reduce_first, reduce_second, reduce_shard.T, rate_reduce, weight_decay
        ),
        *adamw_update(vectors, vector_first, vector_second, vector_grad, rate_vectors, 0.0),
        *adamw_update(hidden_bias, hidden_first, hidden_second, hidden_grad, rate_hidden, 0.0),
        vector_grad,
    )


def solution(mesh):
    sharded = (
        P("dp", None),
        P("dp", None),
        *[P(None, "dp", "tensor")] * 3,
        *[P("tensor", "dp")] * 3,
        *[P("dp", "tensor")] * 3,
        *[P("tensor", "dp")] * 3,
        *[P()] * 6,
    )
    rows = P(("dp", "tensor"), None)
    return jax.shard_map(
        local,
        mesh=mesh,
        in_specs=(rows, rows, *sharded),
        out_specs=(rows, rows, *sharded[2:], P()),
        check_vma=False,
    )
```

```python
import functools

import jax
import jax.numpy as jnp
from jax import lax
from jax.experimental import pallas as pl
from jax.experimental.pallas import tpu as pltpu
from jax.sharding import PartitionSpec as P

HEAD_DIM = 64
LONGEST = 1024
STEP = 10
PAIR = 2 * HEAD_DIM
TILE = 256
MIB = 1024 * 1024
MESH = pl.DeviceIdType.MESH
LOW = jnp.bfloat16
WIDE = jnp.float32

beta_one = 0.9
beta_two = 0.999
adam_epsilon = 1e-08
weight_decay = 0.01
norm_epsilon = 1e-05
masked_score = -1e30
rate_project = 0.03
rate_merge = 0.3
rate_expand = 0.03
rate_reduce = 0.015
rate_vectors = 0.4
rate_hidden = 0.1


def dot_nn(a, b):
    return jnp.dot(a, b, preferred_element_type=WIDE)


def dot_nt(a, b):
    return lax.dot_general(a, b, (((1,), (1,)), ((), ())), preferred_element_type=WIDE)


def dot_tn(a, b):
    return lax.dot_general(a, b, (((0,), (0,)), ((), ())), preferred_element_type=WIDE)


def layout(lengths_row, dealing_row, total_rows):
    slots = jnp.arange(lengths_row.shape[0], dtype=jnp.int32)
    places = jnp.arange(total_rows, dtype=jnp.int32)
    rank_of = jnp.sum(jnp.where(dealing_row[None, :] == slots[:, None], slots[None, :], 0), axis=1)
    own_start = jnp.cumsum(lengths_row) - lengths_row
    dealt_start = jnp.sum(
        jnp.where(rank_of[None, :] < rank_of[:, None], lengths_row[None, :], 0), axis=1
    )
    longest = lengths_row == LONGEST
    short = jnp.where(longest, 0, lengths_row)
    start = jnp.where(longest, 0, LONGEST + jnp.cumsum(short) - short)

    def inside(begin):
        return (places[:, None] >= begin[None, :]) & (
            places[:, None] < (begin + lengths_row)[None, :]
        )

    def moved(begin, end):
        return places + jnp.sum(jnp.where(inside(begin), (end - begin)[None, :], 0), axis=1)

    segment = jnp.sum(jnp.where(inside(start), slots[None, :], 0), axis=1)
    return (
        segment,
        moved(start, own_start),
        moved(start, dealt_start),
        moved(own_start, start),
        moved(dealt_start, start),
    )


def pick_rows(index, rows):
    places = jnp.arange(rows, dtype=jnp.int32)
    return (index[:, None] == places[None, :]).astype(LOW)


def attend_kernel(qkv_ref, bias_ref, context_ref, total_ref):
    rows = qkv_ref.shape[0]
    lane = lax.broadcasted_iota(jnp.int32, (1, PAIR), 1)
    scale = HEAD_DIM ** (-0.5)
    for begin, size in ((0, LONGEST), (LONGEST, rows - LONGEST)):

        @pl.loop(0, size // TILE)
        def _(step):
            first = pl.multiple_of(begin + step * TILE, TILE)
            query = qkv_ref[pl.ds(first, TILE), 0:PAIR]
            key = qkv_ref[begin : begin + size, PAIR : 2 * PAIR]
            value = qkv_ref[begin : begin + size, 2 * PAIR : 3 * PAIR]
            outcome = []
            for head in range(2):
                chosen = jnp.where(lane // HEAD_DIM == head, scale, 0.0).astype(LOW)
                scores = dot_nt(query * chosen, key)
                if begin:
                    inner = pl.multiple_of(step * TILE, TILE)
                    scores = scores + bias_ref[pl.ds(inner, TILE), :]
                top = jnp.max(scores, axis=1, keepdims=True)
                exponent = jnp.exp(scores - top)
                total = jnp.sum(exponent, axis=1, keepdims=True)
                outcome.append(dot_nn(exponent.astype(LOW), value) / total)
                log_total = jnp.broadcast_to(top + jnp.log(total), (TILE, PAIR))
                total_ref[0, head : head + 1, pl.ds(first, TILE)] = log_total.T[0:1, :]
            context_ref[pl.ds(first, TILE), :] = jnp.where(
                lane < HEAD_DIM, outcome[0], outcome[1]
            ).astype(LOW)


def attend(qkv, bias):
    rows, width = qkv.shape
    pairs = width // (3 * PAIR)
    return pl.pallas_call(
        attend_kernel,
        grid=(pairs,),
        in_specs=[
            pl.BlockSpec((rows, 3 * PAIR), lambda p: (0, p)),
            pl.BlockSpec(bias.shape, lambda p: (0, 0)),
        ],
        out_specs=[
            pl.BlockSpec((rows, PAIR), lambda p: (0, p)),
            pl.BlockSpec((1, 8, rows), lambda p: (p, 0, 0)),
        ],
        out_shape=[
            jax.ShapeDtypeStruct((rows, pairs * PAIR), LOW),
            jax.ShapeDtypeStruct((pairs, 8, rows), WIDE),
        ],
        compiler_params=pltpu.CompilerParams(vmem_limit_bytes=48 * MIB),
        cost_estimate=pl.CostEstimate(
            flops=8 * pairs * PAIR * 1310720, bytes_accessed=8 * rows * width, transcendentals=0
        ),
    )(qkv, bias)


def attend_back_kernel(
    qkv_ref, bias_ref, context_ref, grad_ref, total_ref, out_ref, dot_ref, turned_ref, query_ref,
    upper_ref, sum_ref,
):
    rows = qkv_ref.shape[0]
    lane = lax.broadcasted_iota(jnp.int32, (1, PAIR), 1)
    scale = HEAD_DIM ** (-0.5)
    product = (grad_ref[...].astype(WIDE) * context_ref[...].astype(WIDE)).T
    for head in range(2):
        band = slice(head * HEAD_DIM, (head + 1) * HEAD_DIM)
        dot_ref[head : head + 1, :] = jnp.sum(product[band, :], axis=0, keepdims=True)
        chosen = lane // HEAD_DIM == head
        query_ref[head] = qkv_ref[:, 0:PAIR] * jnp.where(chosen, scale, 0.0).astype(LOW)
        upper_ref[head] = grad_ref[...] * jnp.where(chosen, 1.0, 0.0).astype(LOW)
    turned_ref[...] = qkv_ref[:, PAIR : 2 * PAIR].astype(WIDE).T.astype(LOW)
    for begin, size in ((0, LONGEST), (LONGEST, rows - LONGEST)):
        block = slice(begin, begin + size)
        sum_ref[:, block] = jnp.zeros((PAIR, size), WIDE)

        @pl.loop(0, size // TILE)
        def _(step):
            first = pl.multiple_of(begin + step * TILE, TILE)
            key = qkv_ref[pl.ds(first, TILE), PAIR : 2 * PAIR]
            value = qkv_ref[pl.ds(first, TILE), 2 * PAIR : 3 * PAIR]
            key_sum = jnp.zeros((TILE, PAIR), WIDE)
            value_sum = jnp.zeros((TILE, PAIR), WIDE)
            for head in range(2):
                band = slice(head * HEAD_DIM, (head + 1) * HEAD_DIM)
                query = query_ref[head, block, :]
                upper = upper_ref[head, block, :]
                scores = dot_nt(key, query)
                if begin:
                    inner = pl.multiple_of(step * TILE, TILE)
                    scores = scores + bias_ref[pl.ds(inner, TILE), :]
                probability = jnp.exp(scores - total_ref[0, head : head + 1, block])
                weight_grads = dot_nt(value, upper)
                score_grads = (
                    probability * (weight_grads - dot_ref[head : head + 1, block])
                ).astype(LOW)
                value_sum = value_sum + dot_nn(probability.astype(LOW), upper)
                key_sum = key_sum + dot_nn(score_grads, query)
                sum_ref[band, block] += dot_nn(turned_ref[band, pl.ds(first, TILE)], score_grads)
            out_ref[pl.ds(first, TILE), PAIR : 2 * PAIR] = key_sum.astype(LOW)
            out_ref[pl.ds(first, TILE), 2 * PAIR : 3 * PAIR] = value_sum.astype(LOW)

        out_ref[block, 0:PAIR] = (sum_ref[:, block] * scale).T.astype(LOW)


def attend_back(qkv, bias, context, grad, totals):
    rows, width = qkv.shape
    pairs = width // (3 * PAIR)
    return pl.pallas_call(
        attend_back_kernel,
        grid=(pairs,),
        in_specs=[
            pl.BlockSpec((rows, 3 * PAIR), lambda p: (0, p)),
            pl.BlockSpec(bias.shape, lambda p: (0, 0)),
            pl.BlockSpec((rows, PAIR), lambda p: (0, p)),
            pl.BlockSpec((rows, PAIR), lambda p: (0, p)),
            pl.BlockSpec((1, 8, rows), lambda p: (p, 0, 0)),
        ],
        out_specs=pl.BlockSpec((rows, 3 * PAIR), lambda p: (0, p)),
        out_shape=jax.ShapeDtypeStruct((rows, width), LOW),
        scratch_shapes=[
            pltpu.VMEM((8, rows), WIDE),
            pltpu.VMEM((PAIR, rows), LOW),
            pltpu.VMEM((2, rows, PAIR), LOW),
            pltpu.VMEM((2, rows, PAIR), LOW),
            pltpu.VMEM((PAIR, rows), WIDE),
        ],
        compiler_params=pltpu.CompilerParams(vmem_limit_bytes=48 * MIB),
        cost_estimate=pl.CostEstimate(
            flops=20 * pairs * PAIR * 1310720, bytes_accessed=12 * rows * width, transcendentals=0
        ),
    )(qkv, bias, context, grad, totals)


def place():
    me = lax.axis_index("dp")
    z, y, x = me // 4, (me // 2) % 2, me % 2
    return me, z, y, x


def line_slots(z, depth):
    slots = []
    for step in range(depth - 1):
        slots.append((z - 1 - step, z - 1 - step >= 0, 1))
        slots.append((z + 1 + step, z + 1 + step < depth, -1))
    return slots


def remote(source, target, send, receive, device):
    return pltpu.make_async_remote_copy(
        src_ref=source,
        dst_ref=target,
        send_sem=send,
        recv_sem=receive,
        device_id={"dp": device},
        device_id_type=MESH,
    )


def greet_line(me, z, y, x, depth, extra=()):
    barrier = pltpu.get_barrier_semaphore()
    for peer in (z * 4 + y * 2 + 1 - x, z * 4 + (1 - y) * 2 + x):
        pl.semaphore_signal(barrier, inc=1, device_id={"dp": peer}, device_id_type=MESH)

    @pl.when(z > 0)
    def _():
        pl.semaphore_signal(barrier, inc=1, device_id={"dp": me - 4}, device_id_type=MESH)

    @pl.when(z < depth - 1)
    def _():
        pl.semaphore_signal(barrier, inc=1, device_id={"dp": me + 4}, device_id_type=MESH)

    for peer in extra:
        pl.semaphore_signal(barrier, inc=1, device_id=peer, device_id_type=MESH)
    ends = jnp.where(z > 0, 1, 0) + jnp.where(z < depth - 1, 1, 0)
    pl.semaphore_wait(barrier, 2 + len(extra) + ends)


def gather_kernel(depth, count, *refs):
    shards, wholes = refs[:count], refs[count : 2 * count]
    own_sem, z_send, z_recv, xa_send, xa_recv, yb_send, yb_recv, ya_send, ya_recv, xb_send, xb_recv = refs[2 * count :]
    me, z, y, x = place()
    x_peer, y_peer = z * 4 + y * 2 + 1 - x, z * 4 + (1 - y) * 2 + x

    def block(zb, yb, xb):
        return zb * 4 + yb * 2 + xb

    def columns(i, second):
        half = wholes[i].shape[2] // 2
        return pl.ds(half if second else 0, half)

    def along_z(i, zb, way):
        part = wholes[i].at[block(zb, y, x)]
        return remote(part, part, z_send.at[i, zb], z_recv.at[i, zb], me + 4 * way)

    def part_copy(i, blk, second, send, receive, peer):
        part = wholes[i].at[blk, :, columns(i, second)]
        return remote(part, part, send, receive, peer)

    def xa(i, zb, xb):
        return part_copy(i, block(zb, y, xb), False, xa_send.at[i, zb], xa_recv.at[i, zb], x_peer)

    def yb(i, zb, yy):
        return part_copy(i, block(zb, yy, x), True, yb_send.at[i, zb], yb_recv.at[i, zb], y_peer)

    def ya(i, zb, yy, xb):
        return part_copy(
            i, block(zb, yy, xb), False, ya_send.at[i, zb, xb], ya_recv.at[i, zb, xb], y_peer
        )

    def xb(i, zb, yy, xx):
        return part_copy(
            i, block(zb, yy, xx), True, xb_send.at[i, zb, yy], xb_recv.at[i, zb, yy], x_peer
        )

    def first_stage(zb):
        for i in range(count):
            xa(i, zb, x).start()
            yb(i, zb, y).start()
            ya(i, zb, y, x).start()
            xb(i, zb, y, x).start()

    def second_stage(zb):
        for i in range(count):
            xa(i, zb, 1 - x).wait_recv()
            ya(i, zb, y, 1 - x).start()
            yb(i, zb, 1 - y).wait_recv()
            xb(i, zb, 1 - y, x).start()

    for i in range(count):
        pltpu.make_async_copy(shards[i], wholes[i].at[me], own_sem.at[i]).start()
    greet_line(me, z, y, x, depth)
    for i in range(count):
        pltpu.make_async_copy(shards[i], wholes[i].at[me], own_sem.at[i]).wait()

    @pl.when(z < depth - 1)
    def _():
        for i in range(count):
            along_z(i, z, 1).start()

    @pl.when(z > 0)
    def _():
        for i in range(count):
            part = wholes[i].at[me]
            remote(part, part, z_send.at[i, depth], z_recv.at[i, z], me - 4).start()

    first_stage(z)
    slots = line_slots(z, depth)
    late = [(z, None)]
    for step in range(depth - 1):
        for zb, valid, way in slots[2 * step : 2 * step + 2]:

            @pl.when(valid)
            def _(zb=zb, way=way):
                on = (z + way >= 0) & (z + way < depth)
                for i in range(count):
                    along_z(i, zb, way).wait_recv()

                    @pl.when(on)
                    def _():
                        along_z(i, zb, way).start()

                first_stage(zb)

        for zb, valid in late:
            if valid is None:
                second_stage(zb)
            else:

                @pl.when(valid)
                def _(zb=zb):
                    second_stage(zb)

        late = [(zb, valid) for zb, valid, _ in slots[2 * step : 2 * step + 2]]
    for zb, valid in late:

        @pl.when(valid)
        def _(zb=zb):
            second_stage(zb)

    for i in range(count):
        for zb in range(depth):
            for other in range(2):
                ya(i, zb, 1 - y, other).wait_recv()
                xb(i, zb, other, 1 - x).wait_recv()
                ya(i, zb, y, other).wait_send()
                xb(i, zb, other, x).wait_send()
            xa(i, zb, x).wait_send()
            yb(i, zb, y).wait_send()

        @pl.when(z < depth - 1)
        def _():
            along_z(i, z, 1).wait_send()

        @pl.when(z > 0)
        def _():
            part = wholes[i].at[me]
            remote(part, part, z_send.at[i, depth], z_recv.at[i, z], me - 4).wait_send()

        for zb, valid, way in slots:

            @pl.when(valid & (z + way >= 0) & (z + way < depth))
            def _(zb=zb, way=way):
                along_z(i, zb, way).wait_send()


def gather(shards, parts):
    depth, count = parts // 4, len(shards)
    sem = pltpu.SemaphoreType.DMA
    whole = pl.pallas_call(
        functools.partial(gather_kernel, depth, count),
        in_specs=[pl.BlockSpec(memory_space=pl.ANY)] * count,
        out_specs=[pl.BlockSpec(memory_space=pl.ANY)] * count,
        out_shape=[jax.ShapeDtypeStruct((parts, *s.shape), s.dtype) for s in shards],
        scratch_shapes=[
            sem((count,)),
            sem((count, depth + 1)),
            sem((count, depth)),
            *[sem((count, depth))] * 4,
            *[sem((count, depth, 2))] * 4,
        ],
        compiler_params=pltpu.CompilerParams(collective_id=0, has_side_effects=True),
    )(*shards)
    return [w.reshape(parts * w.shape[1], w.shape[2]) for w in whole]


def scatter_kernel(depth, count, *refs):
    grads, vector_ref = refs[:count], refs[count]
    shards, vector_out = refs[count + 1 : 2 * count + 1], refs[2 * count + 1]
    refs = refs[2 * count + 2 :]
    buffers = [refs[10 * i : 10 * i + 10] for i in range(count)]
    (
        vector_buffer, vector_send, vector_recv, a1_send, a1_recv, b1_send, b1_recv,
        a2_send, a2_recv, b2_send, b2_recv, z_send, z_recv,
    ) = refs[10 * count :]
    me, z, y, x = place()
    member = lax.axis_index("tensor")
    x_peer, y_peer = z * 4 + y * 2 + 1 - x, z * 4 + (1 - y) * 2 + x
    chunk = 16
    levels = depth.bit_length() - 1

    def block(zb, yb, xb):
        return zb * 4 + yb * 2 + xb

    partners = [{"tensor": 1 - member}, {"dp": x_peer}, {"dp": y_peer}]
    for level in range(levels):
        reach = 1 << level
        partners.append({"dp": me + 4 * reach * (1 - 2 * ((z // reach) % 2))})

    def vector_copy(step):
        return pltpu.make_async_remote_copy(
            src_ref=vector_buffer.at[step],
            dst_ref=vector_buffer.at[len(partners) + 1 + step],
            send_sem=vector_send.at[step],
            recv_sem=vector_recv.at[step],
            device_id=partners[step],
            device_id_type=MESH,
        )

    def vector_step(step):
        if step == 0:
            vector_buffer[0] = vector_ref[...]
        elif step <= len(partners):
            vector_copy(step - 1).wait_recv()
            vector_buffer[step] = vector_buffer[step - 1] + vector_buffer[len(partners) + step]
        if step < len(partners):
            vector_copy(step).start()
        if step == len(partners):
            vector_out[...] = vector_buffer[step]

    def a1(i, zb):
        half = grads[i].shape[2] // 2
        return remote(
            grads[i].at[pl.ds(block(zb, 1 - y, 0), 2), :, pl.ds(0, half)],
            buffers[i][0].at[zb],
            a1_send.at[i, zb],
            a1_recv.at[i, zb],
            y_peer,
        )

    def b1(i, zb, yy):
        half = grads[i].shape[2] // 2
        return remote(
            grads[i].at[block(zb, yy, 1 - x), :, pl.ds(half, half)],
            buffers[i][1].at[zb, yy],
            b1_send.at[i, zb, yy],
            b1_recv.at[i, zb, yy],
            x_peer,
        )

    def a2(i, zb):
        return remote(
            buffers[i][2].at[zb], buffers[i][4].at[zb], a2_send.at[i, zb], a2_recv.at[i, zb], x_peer
        )

    def b2(i, zb):
        return remote(
            buffers[i][3].at[zb], buffers[i][5].at[zb], b2_send.at[i, zb], b2_recv.at[i, zb], y_peer
        )

    def along_z(i, zb, way):
        slot = zb if way > 0 else zb + (depth - zb) * jnp.where(zb == z - 1, 1, 0)
        return remote(
            buffers[i][9].at[zb],
            buffers[i][8].at[slot],
            z_send.at[i, zb],
            z_recv.at[i, slot],
            me + 4 * way,
        )

    def from_z(i, slot):
        return remote(
            buffers[i][9].at[0], buffers[i][8].at[slot], z_send.at[i, 0], z_recv.at[i, slot], me
        )

    def open_slot(zb):
        for i in range(count):
            a1(i, zb).start()
            b1(i, zb, 0).start()
            b1(i, zb, 1).start()

    def first_sum(zb):
        for i in range(count):
            half = grads[i].shape[2] // 2
            r1a, r1b, t1a, t1b, _, _, s2a, s2b, _, _ = buffers[i]
            a1(i, zb).wait_recv()

            @pl.loop(0, t1a.shape[1] // chunk)
            def _(step):
                rows = pl.ds(pl.multiple_of(step * chunk, chunk), chunk)
                t1a[zb, rows, :] = (
                    grads[i][block(zb, y, 1 - x), rows, 0:half].astype(WIDE)
                    + r1a[zb, 1 - x, rows, :].astype(WIDE)
                ).astype(LOW)

            a2(i, zb).start()
            b1(i, zb, 0).wait_recv()
            b1(i, zb, 1).wait_recv()

            @pl.loop(0, t1a.shape[1] // chunk)
            def _(step):
                rows = pl.ds(pl.multiple_of(step * chunk, chunk), chunk)
                t1b[zb, rows, :] = (
                    grads[i][block(zb, 1 - y, x), rows, half : 2 * half].astype(WIDE)
                    + r1b[zb, 1 - y, rows, :].astype(WIDE)
                ).astype(LOW)

            b2(i, zb).start()

            @pl.loop(0, t1a.shape[1] // chunk)
            def _(step):
                rows = pl.ds(pl.multiple_of(step * chunk, chunk), chunk)
                s2a[zb, rows, :] = grads[i][block(zb, y, x), rows, 0:half].astype(WIDE) + r1a[
                    zb, x, rows, :
                ].astype(WIDE)
                s2b[zb, rows, :] = grads[i][block(zb, y, x), rows, half : 2 * half].astype(
                    WIDE
                ) + r1b[zb, y, rows, :].astype(WIDE)

    def second_sum(i, zb):
        _, _, _, _, r2a, r2b, s2a, s2b, _, _ = buffers[i]
        a2(i, zb).wait_recv()
        b2(i, zb).wait_recv()

        @pl.loop(0, r2a.shape[1] // chunk)
        def _(step):
            rows = pl.ds(pl.multiple_of(step * chunk, chunk), chunk)
            s2a[zb, rows, :] += r2a[zb, rows, :].astype(WIDE)
            s2b[zb, rows, :] += r2b[zb, rows, :].astype(WIDE)

    def add_z(i, zb, slot):
        _, _, _, _, _, _, s2a, s2b, rz, _ = buffers[i]
        half = grads[i].shape[2] // 2
        from_z(i, slot).wait_recv()

        @pl.loop(0, s2a.shape[1] // chunk)
        def _(step):
            rows = pl.ds(pl.multiple_of(step * chunk, chunk), chunk)
            s2a[zb, rows, :] += rz[slot, rows, 0:half].astype(WIDE)
            s2b[zb, rows, :] += rz[slot, rows, half : 2 * half].astype(WIDE)

    def pass_on(zb, way):
        for i in range(count):
            _, _, _, _, _, _, s2a, s2b, _, tz = buffers[i]
            half = grads[i].shape[2] // 2
            second_sum(i, zb)

            @pl.when((z - way >= 0) & (z - way < depth))
            def _():
                add_z(i, zb, zb)

            @pl.loop(0, s2a.shape[1] // chunk)
            def _(step):
                rows = pl.ds(pl.multiple_of(step * chunk, chunk), chunk)
                tz[zb, rows, 0:half] = s2a[zb, rows, :].astype(LOW)
                tz[zb, rows, half : 2 * half] = s2b[zb, rows, :].astype(LOW)

            along_z(i, zb, way).start()

    def finish():
        for i in range(count):
            _, _, _, _, _, _, s2a, s2b, _, _ = buffers[i]
            half = grads[i].shape[2] // 2
            second_sum(i, z)

            @pl.when(z > 0)
            def _():
                add_z(i, z, z)

            @pl.when(z < depth - 1)
            def _():
                add_z(i, z, depth)

            @pl.loop(0, s2a.shape[1] // chunk)
            def _(step):
                rows = pl.ds(pl.multiple_of(step * chunk, chunk), chunk)
                shards[i][rows, 0:half] = s2a[z, rows, :]
                shards[i][rows, half : 2 * half] = s2b[z, rows, :]

    def when(valid, act):
        if valid is None:
            act()
        else:
            pl.when(valid)(act)

    groups = []
    for step in reversed(range(depth - 1)):
        groups.append([(z + 1 + step, z + 1 + step < depth, 1), (z - 1 - step, z - 1 - step >= 0, -1)])
    groups.append([(z, None, 0)])

    greet_line(me, z, y, x, depth, [partners[0], *partners[3:]])
    vector_step(0)
    for group in groups[:2]:
        for zb, valid, _ in group:
            when(valid, functools.partial(open_slot, zb))
    vector_at = 1
    for at, group in enumerate(groups):
        for zb, valid, _ in group:
            when(valid, functools.partial(first_sum, zb))
        if at + 2 < len(groups):
            for zb, valid, _ in groups[at + 2]:
                when(valid, functools.partial(open_slot, zb))
        vector_step(vector_at)
        vector_at += 1
        if at:
            for zb, valid, way in groups[at - 1]:
                when(valid, functools.partial(pass_on, zb, way))
    while vector_at <= len(partners):
        vector_step(vector_at)
        vector_at += 1
    finish()

    for step in range(len(partners)):
        vector_copy(step).wait_send()
    for i in range(count):
        for zb in range(depth):
            a1(i, zb).wait_send()
            b1(i, zb, 0).wait_send()
            b1(i, zb, 1).wait_send()
            a2(i, zb).wait_send()
            b2(i, zb).wait_send()
        for group in groups[:-1]:
            for zb, valid, way in group:

                @pl.when(valid)
                def _(zb=zb, way=way):
                    along_z(i, zb, way).wait_send()


def scatter(grads, vector, parts):
    depth, count = parts // 4, len(grads)
    rows = grads[0].shape[0] // parts
    sem = pltpu.SemaphoreType.DMA
    partners = 3 + depth.bit_length() - 1
    scratch = []
    for g in grads:
        n = g.shape[1]
        half = n // 2
        scratch += [pltpu.VMEM((depth, 2, rows, half), LOW)] * 2
        scratch += [pltpu.VMEM((depth, rows, half), LOW)] * 4
        scratch += [pltpu.VMEM((depth, rows, half), WIDE)] * 2
        scratch += [pltpu.VMEM((depth + 1, rows, n), LOW), pltpu.VMEM((depth, rows, n), LOW)]
    vmem = pl.BlockSpec(memory_space=pltpu.VMEM)
    return pl.pallas_call(
        functools.partial(scatter_kernel, depth, count),
        in_specs=[vmem] * (count + 1),
        out_specs=[vmem] * (count + 1),
        out_shape=[
            *[jax.ShapeDtypeStruct((rows, g.shape[1]), WIDE) for g in grads],
            jax.ShapeDtypeStruct(vector.shape, WIDE),
        ],
        scratch_shapes=[
            *scratch,
            pltpu.VMEM((2 * partners + 1, *vector.shape), WIDE),
            sem((partners,)),
            sem((partners,)),
            *[sem((count, depth))] * 2,
            *[sem((count, depth, 2))] * 2,
            *[sem((count, depth))] * 4,
            sem((count, depth)),
            sem((count, depth + 1)),
        ],
        compiler_params=pltpu.CompilerParams(
            collective_id=1, has_side_effects=True, vmem_limit_bytes=60 * MIB
        ),
    )(*[g.reshape(parts, rows, g.shape[1]) for g in grads], vector)


def normal_cells(value):
    bell = jnp.exp(value * value * -0.5)
    t = 1.0 / (1.0 + 0.39 * 0.7071067811865476 * jnp.abs(value))
    tail = -0.2275377237624147
    for factor in (
        0.8866668177122106,
        -0.6354042576077721,
        0.649562611731642,
        0.0913871257655044,
        0.23532542445435511,
    ):
        tail = tail * t + factor
    tail = 0.5 * tail * t * bell
    return jnp.where(value < 0.0, tail, 1.0 - tail), bell


def feed_kernel(
    context_ref, merge_ref, merge_far_ref, expand_ref, expand_far_ref, reduce_ref, reduce_far_ref,
    hidden_ref, upstream_ref, vectors_ref, bias_ref,
    encoded_ref, branch_ref, grad_ref, merge_grad_ref, expand_grad_ref, reduce_grad_ref, sums_ref, hidden_sums_ref,
    own_ctx, far_ctx, acc, normal, inverse, low, turned, late, late_turned, active, slope, inner_grad,
    expand_buf, reduce_buf, arrived, leaving, kept, done, grad_own, grad_far, merge_send, merge_recv,
    ctx_sem, load_sem, send_sem, recv_sem, out_sem, last_sem,
):
    rows = hidden_ref.shape[0]
    chunks, _, both = bias_ref.shape
    half = both // 2
    member = lax.axis_index("tensor")
    peer = {"tensor": 1 - member}
    tall, short = 256, 128
    width = hidden_ref.shape[1]

    def across(source, target, send, receive):
        return pltpu.make_async_remote_copy(
            src_ref=source,
            dst_ref=target,
            send_sem=send,
            recv_sem=receive,
            device_id=peer,
            device_id_type=MESH,
        )

    def rows_of(which):
        return pl.ds(pl.multiple_of(which * rows, rows), rows)

    def tile(step, size):
        return pl.ds(pl.multiple_of(step * size, size), size)

    def loads(j, slot):
        cols = pl.ds(pl.multiple_of(j * half, half), half)
        copies = []
        for kind, (buf, far, own) in enumerate(
            ((expand_buf, expand_far_ref, expand_ref), (reduce_buf, reduce_far_ref, reduce_ref))
        ):
            for side, source in enumerate((far, own)):
                copies.append(
                    pltpu.make_async_copy(
                        source.at[:, cols],
                        buf.at[slot, :, pl.ds(side * half, half)],
                        load_sem.at[slot, kind, side],
                    )
                )
        return copies

    for copy in loads(0, 0):
        copy.start()
    barrier = pltpu.get_barrier_semaphore()
    pl.semaphore_signal(barrier, inc=1, device_id=peer, device_id_type=MESH)
    pl.semaphore_wait(barrier, 1)
    out_ctx = across(context_ref.at[rows_of(1 - member)], far_ctx, ctx_sem.at[0], ctx_sem.at[1])
    out_ctx.start()
    in_ctx = pltpu.make_async_copy(context_ref.at[rows_of(member)], own_ctx, ctx_sem.at[2])
    in_ctx.start()
    sums_ref[...] = jnp.zeros_like(sums_ref)
    in_ctx.wait()
    out_ctx.wait()

    def norm(values):
        center = values - jnp.mean(values, axis=1, keepdims=True)
        spread = jnp.mean(center * center, axis=1, keepdims=True)
        scale = lax.rsqrt(spread + norm_epsilon)
        return center * scale, scale

    def norm_back(scaled, unit, scale):
        return scale * (
            scaled
            - jnp.mean(scaled, axis=1, keepdims=True)
            - unit * jnp.mean(scaled * unit, axis=1, keepdims=True)
        )

    def add_sum(row, values):
        sums_ref[row : row + 1, :] += jnp.sum(values, axis=0, keepdims=True)

    @pl.loop(0, rows // short)
    def _(step):
        at = tile(step, short)
        branch = dot_nt(own_ctx[at, :], merge_ref[...]) + dot_nt(far_ctx[at, :], merge_far_ref[...])
        unit, scale = norm(hidden_ref[at, :].astype(WIDE) + branch + vectors_ref[2:3, :])
        normed = unit * vectors_ref[3:4, :] + vectors_ref[4:5, :]
        normal[at, :] = unit
        inverse[at, :] = jnp.broadcast_to(scale, (short, 128))
        low[at, :] = normed.astype(LOW)
        turned[:, at] = normed.T.astype(LOW)
        acc[at, :] = normed + vectors_ref[5:6, :]

    @pl.loop(0, chunks)
    def _(j):
        slot = lax.rem(j, 2)
        for copy in loads(j, slot):
            copy.wait()

        @pl.when(j + 1 < chunks)
        def _():
            for copy in loads(j + 1, 1 - slot):
                copy.start()

        for step in range(rows // tall):
            at = slice(step * tall, (step + 1) * tall)
            inner = dot_nn(low[at, :], expand_buf[slot]) + bias_ref[j]
            below, bell = normal_cells(inner)
            held = (inner * below).astype(LOW)
            active[j, at, :] = held
            slope[j, at, :] = (below + inner * bell * 0.3989422804014327).astype(LOW)
            acc[at, :] += dot_nt(held, reduce_buf[slot])

    for copy in loads(0, 0):
        copy.start()

    @pl.loop(0, rows // short)
    def _(step):
        at = tile(step, short)
        unit, scale = norm(acc[at, :])
        encoded_ref[at, :] = (unit * vectors_ref[6:7, :] + vectors_ref[7:8, :]).astype(LOW)
        upper = upstream_ref[at, :].astype(WIDE)
        add_sum(6, upper * unit)
        add_sum(7, upper)
        grad = norm_back(upper * vectors_ref[6:7, :], unit, scale)
        grad_low = grad.astype(LOW)
        add_sum(5, grad_low.astype(WIDE))
        acc[at, :] = grad
        late[at, :] = grad_low
        late_turned[:, at] = grad.T.astype(LOW)

    def send(j, kind):
        return across(
            leaving.at[lax.rem(j, 2), kind],
            arrived.at[lax.rem(j, 4), kind],
            send_sem.at[lax.rem(j, 2), kind],
            recv_sem.at[lax.rem(j, 4), kind],
        )

    def store(j, kind):
        target = (expand_grad_ref, reduce_grad_ref)[kind]
        cols = pl.ds(pl.multiple_of(j * half, half), half)
        return pltpu.make_async_copy(
            done.at[lax.rem(j, 2), kind], target.at[:, cols], out_sem.at[lax.rem(j, 2), kind]
        )

    def finish(j):
        for kind in range(2):
            send(j, kind).wait_recv()

            @pl.when(j >= 2)
            def _():
                store(j - 2, kind).wait()

            @pl.loop(0, width // tall)
            def _(step):
                at = tile(step, tall)
                done[lax.rem(j, 2), kind, at, :] = (
                    kept[lax.rem(j, 2), kind, at, :]
                    + arrived[lax.rem(j, 4), kind, at, :].astype(WIDE)
                ).astype(LOW)

            store(j, kind).start()

    @pl.loop(0, chunks)
    def _(j):
        slot = lax.rem(j, 2)
        for copy in loads(j, slot):
            copy.wait()

        @pl.when(j + 1 < chunks)
        def _():
            for copy in loads(j + 1, 1 - slot):
                copy.start()

        total = jnp.zeros((1, both), WIDE)
        for step in range(rows // tall):
            at = slice(step * tall, (step + 1) * tall)
            grad = dot_nn(late[at, :], reduce_buf[slot]) * slope[j, at, :].astype(WIDE)
            grad = grad.astype(LOW)
            inner_grad[at, :] = grad
            total = total + jnp.sum(grad.astype(WIDE), axis=0, keepdims=True)
            acc[at, :] += dot_nt(grad, expand_buf[slot])
        hidden_sums_ref[j] = total

        @pl.when(j >= 2)
        def _():
            for kind in range(2):
                send(j - 2, kind).wait_send()

        for kind, (left, right) in enumerate(((turned, inner_grad), (late_turned, active.at[j]))):
            for step in range(width // tall):
                at = slice(step * tall, (step + 1) * tall)
                part = dot_nn(left[at, :], right[...])
                leaving[slot, kind, at, :] = part[:, 0:half].astype(LOW)
                kept[slot, kind, at, :] = part[:, half:both]
            send(j, kind).start()

        @pl.when(j >= 1)
        def _():
            finish(j - 1)

    @pl.loop(0, rows // short)
    def _(step):
        at = tile(step, short)
        grad = acc[at, :]
        unit = normal[at, :]
        add_sum(3, grad * unit)
        add_sum(4, grad)
        branch_grad = norm_back(grad * vectors_ref[3:4, :], unit, inverse[at, 0:1])
        branch_low = branch_grad.astype(LOW)
        add_sum(2, branch_low.astype(WIDE))
        branch_ref[at, :] = branch_grad
        turned[:, at] = branch_grad.T.astype(LOW)
        grad_far[at, :] = dot_nn(branch_low, merge_far_ref[...]).astype(LOW)
        grad_own[at, :] = dot_nn(branch_low, merge_ref[...]).astype(LOW)

    out_grad = across(grad_far, grad_ref.at[rows_of(member)], ctx_sem.at[0], ctx_sem.at[1])
    out_grad.start()
    in_grad = pltpu.make_async_copy(grad_own, grad_ref.at[rows_of(member)], ctx_sem.at[2])
    in_grad.start()
    for step in range(width // tall):
        at = slice(step * tall, (step + 1) * tall)
        merge_send[at, :] = dot_nn(turned[at, :], far_ctx[...]).astype(LOW)
    out_merge = across(merge_send, merge_recv, last_sem.at[0], last_sem.at[1])
    out_merge.start()
    finish(chunks - 1)
    for kind in range(2):
        send(chunks - 2, kind).wait_send()
        send(chunks - 1, kind).wait_send()
        store(chunks - 2, kind).wait()
        store(chunks - 1, kind).wait()
    out_merge.wait()
    for step in range(width // tall):
        at = slice(step * tall, (step + 1) * tall)
        merge_grad_ref[at, :] = (
            dot_nn(turned[at, :], own_ctx[...]) + merge_recv[at, :].astype(WIDE)
        ).astype(LOW)
    out_grad.wait()
    in_grad.wait()


def feed_block(context, weights, hidden_own, upstream, vectors, bias_own, bias_far):
    total_rows, inner = context.shape
    rows, width = hidden_own.shape
    hidden = weights[2].shape[1]
    half = 256
    chunks = hidden // half
    both = 2 * half
    bias = jnp.concatenate(
        [bias_far.reshape(chunks, 1, half), bias_own.reshape(chunks, 1, half)], axis=2
    )
    vmem, anywhere = pl.BlockSpec(memory_space=pltpu.VMEM), pl.BlockSpec(memory_space=pl.ANY)
    sem = pltpu.SemaphoreType.DMA
    shape = jax.ShapeDtypeStruct
    *results, hidden_sums = pl.pallas_call(
        feed_kernel,
        in_specs=[anywhere, vmem, vmem, *[anywhere] * 4, *[vmem] * 4],
        out_specs=[vmem, vmem, anywhere, vmem, anywhere, anywhere, vmem, vmem],
        out_shape=[
            shape((rows, width), LOW),
            shape((rows, width), WIDE),
            shape((total_rows, inner), LOW),
            shape((width, inner), LOW),
            shape((width, hidden), LOW),
            shape((width, hidden), LOW),
            shape((8, width), WIDE),
            shape((chunks, 1, both), WIDE),
        ],
        scratch_shapes=[
            pltpu.VMEM((rows, inner), LOW),
            pltpu.VMEM((rows, inner), LOW),
            pltpu.VMEM((rows, width), WIDE),
            pltpu.VMEM((rows, width), WIDE),
            pltpu.VMEM((rows, 128), WIDE),
            pltpu.VMEM((rows, width), LOW),
            pltpu.VMEM((width, rows), LOW),
            pltpu.VMEM((rows, width), LOW),
            pltpu.VMEM((width, rows), LOW),
            pltpu.VMEM((chunks, rows, both), LOW),
            pltpu.VMEM((chunks, rows, both), LOW),
            pltpu.VMEM((rows, both), LOW),
            pltpu.VMEM((2, width, both), LOW),
            pltpu.VMEM((2, width, both), LOW),
            pltpu.VMEM((4, 2, width, half), LOW),
            pltpu.VMEM((2, 2, width, half), LOW),
            pltpu.VMEM((2, 2, width, half), WIDE),
            pltpu.VMEM((2, 2, width, half), LOW),
            pltpu.VMEM((rows, inner), LOW),
            pltpu.VMEM((rows, inner), LOW),
            pltpu.VMEM((width, inner), LOW),
            pltpu.VMEM((width, inner), LOW),
            sem((3,)),
            sem((2, 2, 2)),
            sem((2, 2)),
            sem((4, 2)),
            sem((2, 2)),
            sem((2,)),
        ],
        compiler_params=pltpu.CompilerParams(
            collective_id=2, has_side_effects=True, vmem_limit_bytes=60 * MIB
        ),
        cost_estimate=pl.CostEstimate(
            flops=12 * rows * width * 2 * hidden, bytes_accessed=8 * width * hidden * 4, transcendentals=0
        ),
    )(context, *weights, hidden_own, upstream, vectors, bias)
    hidden_far = hidden_sums[:, 0, :half].reshape(-1)
    hidden_near = hidden_sums[:, 0, half:].reshape(-1)
    return (*results, hidden_near, hidden_far)


def adamw_update(master, moment, square, gradient, step_rate, decay_rate):
    moment_new = beta_one * moment + (1.0 - beta_one) * gradient
    square_new = beta_two * square + (1.0 - beta_two) * gradient * gradient
    moment_hat = moment_new / (1.0 - beta_one**STEP)
    square_hat = square_new / (1.0 - beta_two**STEP)
    master_new = master - step_rate * (
        moment_hat / (jnp.sqrt(square_hat) + adam_epsilon) + decay_rate * master
    )
    return (moment_new, square_new, master_new)


def local(
    tokens,
    cotangent,
    lengths,
    dealing,
    project_weight,
    project_first,
    project_second,
    merge_weight,
    merge_first,
    merge_second,
    expand_weight,
    expand_first,
    expand_second,
    reduce_weight,
    reduce_first,
    reduce_second,
    vectors,
    vector_first,
    vector_second,
    hidden_bias,
    hidden_first,
    hidden_second,
):
    parts = lax.axis_size("dp")
    member = lax.axis_index("tensor")
    other = 1 - member
    half_rows, model_width = tokens.shape
    total_rows = 2 * half_rows
    width_half = project_weight.shape[2]
    pairs = width_half // PAIR
    hidden_half = expand_weight.shape[1]
    shard_rows = expand_weight.shape[0]
    own_begin = member * half_rows
    by_kernel = parts % 4 == 0 and (parts & (parts - 1)) == 0 and shard_rows % 16 == 0

    def swap(value):
        return lax.ppermute(value, "tensor", [(0, 1), (1, 0)])

    def own(value, size, which=member):
        return lax.dynamic_slice_in_dim(value, which * size, size, 0)

    segment, own_of, dealt_of, from_own, from_dealt = layout(lengths[0], dealing[0], total_rows)

    def own_first(index):
        return lax.rem(index - own_begin + total_rows, total_rows)

    shards = [
        project_weight.astype(LOW)
        .reshape(3, shard_rows, pairs, PAIR)
        .transpose(1, 2, 0, 3)
        .reshape(shard_rows, 3 * width_half),
        merge_weight.astype(LOW).T,
        expand_weight.astype(LOW),
        reduce_weight.astype(LOW).T,
    ]
    token_pair = jnp.concatenate([tokens, swap(tokens)], axis=0)
    upper_pair = jnp.concatenate([cotangent, swap(cotangent)], axis=0)
    if by_kernel:
        project, merge, expand, reduce = gather(shards, parts)
    else:
        project, merge, expand, reduce = [
            lax.all_gather(s, "dp", axis=0, tiled=True) for s in shards
        ]
    merge_far, expand_far, reduce_far = swap(merge), swap(expand), swap(reduce)

    hidden = dot_nn(pick_rows(own_first(own_of), total_rows), token_pair).astype(LOW)
    upstream = dot_nn(pick_rows(own_first(own(dealt_of, half_rows)), total_rows), upper_pair)
    zeros_pair = jnp.zeros((pairs, PAIR), WIDE)
    bias_row = jnp.stack(
        [
            own(vectors[0], width_half).reshape(pairs, PAIR),
            zeros_pair,
            own(vectors[1], width_half).reshape(pairs, PAIR),
        ],
        axis=1,
    ).reshape(-1)
    qkv = (dot_nn(hidden, project) + bias_row).astype(LOW)
    short = segment[LONGEST:]
    score_bias = jnp.where(short[:, None] == short[None, :], 0.0, masked_score).astype(WIDE)
    context, totals = attend(qkv, score_bias)

    (
        encoded, branch_grad, context_grad, merge_grad, expand_grad, reduce_grad, sums, hidden_part_own, hidden_part_far,
    ) = feed_block(
        context,
        [merge, merge_far, expand, expand_far, reduce, reduce_far],
        own(hidden, half_rows),
        upstream.astype(LOW),
        vectors,
        own(hidden_bias, hidden_half),
        own(hidden_bias, hidden_half, other),
    )
    encoded_pair = jnp.concatenate([encoded, swap(encoded)], axis=0)
    encoded_out = dot_nn(
        pick_rows(own_first(own(from_dealt, half_rows)), total_rows), encoded_pair
    ).astype(LOW)
    mixed_grads = attend_back(qkv, score_bias, context, context_grad, totals)
    project_grad = dot_tn(hidden, mixed_grads)
    mixed_sums = jnp.sum(mixed_grads.astype(WIDE), axis=0).reshape(pairs, 3, PAIR)
    input_terms = dot_nt(mixed_grads, project)
    own_part = own(input_terms, half_rows) + branch_grad
    input_terms = lax.dynamic_update_slice_in_dim(input_terms, own_part, own_begin, 0).astype(LOW)
    input_far = swap(
        dot_nn(pick_rows(own(from_own, half_rows, other), total_rows), input_terms).astype(LOW)
    )
    input_grad = (
        dot_nn(pick_rows(own(from_own, half_rows), total_rows), input_terms)
        + input_far.astype(WIDE)
    ).astype(LOW)

    zeros_width = jnp.zeros((model_width,), WIDE)
    zeros_hidden = jnp.zeros_like(hidden_bias)
    hidden_total = lax.dynamic_update_slice_in_dim(
        lax.dynamic_update_slice_in_dim(
            zeros_hidden, hidden_part_own, member * hidden_half, 0
        ),
        hidden_part_far,
        other * hidden_half,
        0,
    )
    vector_rows = [
        lax.dynamic_update_slice_in_dim(
            zeros_width, mixed_sums[:, c].reshape(-1), member * width_half, 0
        )
        for c in (0, 2)
    ]
    small = jnp.concatenate(
        [
            jnp.stack(vector_rows),
            sums[2:],
            hidden_total.reshape(-1, model_width),
            jnp.zeros((4, model_width), WIDE),
        ],
        axis=0,
    )
    grads = [g.astype(LOW) for g in (project_grad, merge_grad, expand_grad, reduce_grad)]
    if by_kernel:
        *grads, small = scatter(grads, small, parts)
    else:
        grads = [lax.psum_scatter(g, "dp", scatter_dimension=0, tiled=True) for g in grads]
        grads = [g.astype(WIDE) for g in grads]
        small = lax.psum(small, ("dp", "tensor"))
    project_shard, merge_shard, expand_shard, reduce_shard = grads
    project_shard = (
        project_shard.reshape(shard_rows, pairs, 3, PAIR)
        .transpose(2, 0, 1, 3)
        .reshape(3, shard_rows, width_half)
    )
    vector_grad = small[:8]
    hidden_grad = small[8:12].reshape(-1)
    return (
        encoded_out,
        input_grad,
        *adamw_update(
            project_weight, project_first, project_second, project_shard, rate_project, weight_decay
        ),
        *adamw_update(
            merge_weight, merge_first, merge_second, merge_shard.T, rate_merge, weight_decay
        ),
        *adamw_update(
            expand_weight, expand_first, expand_second, expand_shard, rate_expand, weight_decay
        ),
        *adamw_update(
            reduce_weight, reduce_first, reduce_second, reduce_shard.T, rate_reduce, weight_decay
        ),
        *adamw_update(vectors, vector_first, vector_second, vector_grad, rate_vectors, 0.0),
        *adamw_update(hidden_bias, hidden_first, hidden_second, hidden_grad, rate_hidden, 0.0),
        vector_grad,
    )


def solution(mesh):
    sharded = (
        P("dp", None),
        P("dp", None),
        *[P(None, "dp", "tensor")] * 3,
        *[P("tensor", "dp")] * 3,
        *[P("dp", "tensor")] * 3,
        *[P("tensor", "dp")] * 3,
        *[P()] * 6,
    )
    rows = P(("dp", "tensor"), None)
    return jax.shard_map(
        local,
        mesh=mesh,
        in_specs=(rows, rows, *sharded),
        out_specs=(rows, rows, *sharded[2:], P()),
        check_vma=False,
    )
```

```python
import functools

import jax
import jax.numpy as jnp
from jax import lax
from jax.experimental import pallas as pl
from jax.experimental.pallas import tpu as pltpu
from jax.sharding import PartitionSpec as P

HEAD_DIM = 64
LONGEST = 1024
STEP = 10
PAIR = 2 * HEAD_DIM
TILE = 256
MIB = 1024 * 1024
MESH = pl.DeviceIdType.MESH
LOW = jnp.bfloat16
WIDE = jnp.float32

beta_one = 0.9
beta_two = 0.999
adam_epsilon = 1e-08
weight_decay = 0.01
norm_epsilon = 1e-05
masked_score = -1e30
rate_project = 0.03
rate_merge = 0.3
rate_expand = 0.03
rate_reduce = 0.015
rate_vectors = 0.4
rate_hidden = 0.1


def dot_nn(a, b):
    return jnp.dot(a, b, preferred_element_type=WIDE)


def dot_nt(a, b):
    return lax.dot_general(a, b, (((1,), (1,)), ((), ())), preferred_element_type=WIDE)


def dot_tn(a, b):
    return lax.dot_general(a, b, (((0,), (0,)), ((), ())), preferred_element_type=WIDE)


def layout(lengths_row, dealing_row, total_rows):
    slots = jnp.arange(lengths_row.shape[0], dtype=jnp.int32)
    places = jnp.arange(total_rows, dtype=jnp.int32)
    rank_of = jnp.sum(jnp.where(dealing_row[None, :] == slots[:, None], slots[None, :], 0), axis=1)
    own_start = jnp.cumsum(lengths_row) - lengths_row
    dealt_start = jnp.sum(
        jnp.where(rank_of[None, :] < rank_of[:, None], lengths_row[None, :], 0), axis=1
    )
    longest = lengths_row == LONGEST
    short = jnp.where(longest, 0, lengths_row)
    start = jnp.where(longest, 0, LONGEST + jnp.cumsum(short) - short)

    def inside(begin):
        return (places[:, None] >= begin[None, :]) & (
            places[:, None] < (begin + lengths_row)[None, :]
        )

    def moved(begin, end):
        return places + jnp.sum(jnp.where(inside(begin), (end - begin)[None, :], 0), axis=1)

    segment = jnp.sum(jnp.where(inside(start), slots[None, :], 0), axis=1)
    return (
        segment,
        moved(start, own_start),
        moved(start, dealt_start),
        moved(own_start, start),
        moved(dealt_start, start),
    )


def pick_rows(index, rows):
    places = jnp.arange(rows, dtype=jnp.int32)
    return (index[:, None] == places[None, :]).astype(LOW)


def attend_tile(qkv_ref, pair, bias_ref, begin, size, step, context_ref, columns, total_ref):
    lane = lax.broadcasted_iota(jnp.int32, (1, PAIR), 1)
    scale = HEAD_DIM ** (-0.5)
    first = pl.multiple_of(begin + step * TILE, TILE)
    query = qkv_ref[pair, pl.ds(first, TILE), 0:PAIR]
    key = qkv_ref[pair, begin : begin + size, PAIR : 2 * PAIR]
    value = qkv_ref[pair, begin : begin + size, 2 * PAIR : 3 * PAIR]
    outcome = []
    for head in range(2):
        chosen = jnp.where(lane // HEAD_DIM == head, scale, 0.0).astype(LOW)
        scores = dot_nt(query * chosen, key)
        if begin:
            inner = pl.multiple_of(step * TILE, TILE)
            scores = scores + bias_ref[pl.ds(inner, TILE), :]
        top = jnp.max(scores, axis=1, keepdims=True)
        exponent = jnp.exp(scores - top)
        total = jnp.sum(exponent, axis=1, keepdims=True)
        outcome.append(dot_nn(exponent.astype(LOW), value) / total)
        log_total = jnp.broadcast_to(top + jnp.log(total), (TILE, PAIR))
        total_ref[pair, head : head + 1, pl.ds(first, TILE)] = log_total.T[0:1, :]
    context_ref[pl.ds(first, TILE), columns] = jnp.where(
        lane < HEAD_DIM, outcome[0], outcome[1]
    ).astype(LOW)


def attend_kernel(qkv_ref, bias_ref, context_ref, total_ref):
    rows = qkv_ref.shape[1]
    for begin, size in ((0, LONGEST), (LONGEST, rows - LONGEST)):

        @pl.loop(0, size // TILE)
        def _(step):
            attend_tile(
                qkv_ref, 0, bias_ref, begin, size, step, context_ref, slice(0, PAIR), total_ref
            )


def attend(qkv, bias):
    pairs, rows, width = qkv.shape
    return pl.pallas_call(
        attend_kernel,
        grid=(pairs,),
        in_specs=[
            pl.BlockSpec((1, rows, width), lambda p: (p, 0, 0)),
            pl.BlockSpec(bias.shape, lambda p: (0, 0)),
        ],
        out_specs=[
            pl.BlockSpec((rows, PAIR), lambda p: (0, p)),
            pl.BlockSpec((1, 8, rows), lambda p: (p, 0, 0)),
        ],
        out_shape=[
            jax.ShapeDtypeStruct((rows, pairs * PAIR), LOW),
            jax.ShapeDtypeStruct((pairs, 8, rows), WIDE),
        ],
        compiler_params=pltpu.CompilerParams(vmem_limit_bytes=48 * MIB),
    )(qkv, bias)


def attend_back_kernel(
    qkv_ref, bias_ref, context_ref, grad_ref, total_ref, out_ref, dot_ref, turned_ref, query_ref,
    upper_ref, sum_ref,
):
    rows = qkv_ref.shape[1]
    lane = lax.broadcasted_iota(jnp.int32, (1, PAIR), 1)
    scale = HEAD_DIM ** (-0.5)
    product = (grad_ref[...].astype(WIDE) * context_ref[...].astype(WIDE)).T
    for head in range(2):
        band = slice(head * HEAD_DIM, (head + 1) * HEAD_DIM)
        dot_ref[head : head + 1, :] = jnp.sum(product[band, :], axis=0, keepdims=True)
        chosen = lane // HEAD_DIM == head
        query_ref[head] = qkv_ref[0, :, 0:PAIR] * jnp.where(chosen, scale, 0.0).astype(LOW)
        upper_ref[head] = grad_ref[...] * jnp.where(chosen, 1.0, 0.0).astype(LOW)
    turned_ref[...] = qkv_ref[0, :, PAIR : 2 * PAIR].astype(WIDE).T.astype(LOW)
    for begin, size in ((0, LONGEST), (LONGEST, rows - LONGEST)):
        block = slice(begin, begin + size)
        sum_ref[:, block] = jnp.zeros((PAIR, size), WIDE)

        @pl.loop(0, size // TILE)
        def _(step):
            first = pl.multiple_of(begin + step * TILE, TILE)
            key = qkv_ref[0, pl.ds(first, TILE), PAIR : 2 * PAIR]
            value = qkv_ref[0, pl.ds(first, TILE), 2 * PAIR : 3 * PAIR]
            key_sum = jnp.zeros((TILE, PAIR), WIDE)
            value_sum = jnp.zeros((TILE, PAIR), WIDE)
            for head in range(2):
                band = slice(head * HEAD_DIM, (head + 1) * HEAD_DIM)
                query = query_ref[head, block, :]
                upper = upper_ref[head, block, :]
                scores = dot_nt(key, query)
                if begin:
                    inner = pl.multiple_of(step * TILE, TILE)
                    scores = scores + bias_ref[pl.ds(inner, TILE), :]
                probability = jnp.exp(scores - total_ref[0, head : head + 1, block])
                weight_grads = dot_nt(value, upper)
                score_grads = (
                    probability * (weight_grads - dot_ref[head : head + 1, block])
                ).astype(LOW)
                value_sum = value_sum + dot_nn(probability.astype(LOW), upper)
                key_sum = key_sum + dot_nn(score_grads, query)
                sum_ref[band, block] += dot_nn(turned_ref[band, pl.ds(first, TILE)], score_grads)
            out_ref[0, pl.ds(first, TILE), PAIR : 2 * PAIR] = key_sum.astype(LOW)
            out_ref[0, pl.ds(first, TILE), 2 * PAIR : 3 * PAIR] = value_sum.astype(LOW)

        out_ref[0, block, 0:PAIR] = (sum_ref[:, block] * scale).T.astype(LOW)


def attend_back(qkv, bias, context, grad, totals):
    pairs, rows, width = qkv.shape
    return pl.pallas_call(
        attend_back_kernel,
        grid=(pairs,),
        in_specs=[
            pl.BlockSpec((1, rows, width), lambda p: (p, 0, 0)),
            pl.BlockSpec(bias.shape, lambda p: (0, 0)),
            pl.BlockSpec((rows, PAIR), lambda p: (0, p)),
            pl.BlockSpec((rows, PAIR), lambda p: (0, p)),
            pl.BlockSpec((1, 8, rows), lambda p: (p, 0, 0)),
        ],
        out_specs=pl.BlockSpec((1, rows, width), lambda p: (p, 0, 0)),
        out_shape=jax.ShapeDtypeStruct(qkv.shape, LOW),
        scratch_shapes=[
            pltpu.VMEM((8, rows), WIDE),
            pltpu.VMEM((PAIR, rows), LOW),
            pltpu.VMEM((2, rows, PAIR), LOW),
            pltpu.VMEM((2, rows, PAIR), LOW),
            pltpu.VMEM((PAIR, rows), WIDE),
        ],
        compiler_params=pltpu.CompilerParams(vmem_limit_bytes=48 * MIB),
    )(qkv, bias, context, grad, totals)


def place():
    me = lax.axis_index("dp")
    z, y, x = me // 4, (me // 2) % 2, me % 2
    return me, z, y, x


def line_slots(z, depth):
    slots = []
    for step in range(depth - 1):
        slots.append((z - 1 - step, z - 1 - step >= 0, 1))
        slots.append((z + 1 + step, z + 1 + step < depth, -1))
    return slots


def remote(source, target, send, receive, device):
    return pltpu.make_async_remote_copy(
        src_ref=source,
        dst_ref=target,
        send_sem=send,
        recv_sem=receive,
        device_id={"dp": device},
        device_id_type=MESH,
    )


def greet_line(me, z, y, x, depth, extra=()):
    barrier = pltpu.get_barrier_semaphore()
    for peer in (z * 4 + y * 2 + 1 - x, z * 4 + (1 - y) * 2 + x):
        pl.semaphore_signal(barrier, inc=1, device_id={"dp": peer}, device_id_type=MESH)

    @pl.when(z > 0)
    def _():
        pl.semaphore_signal(barrier, inc=1, device_id={"dp": me - 4}, device_id_type=MESH)

    @pl.when(z < depth - 1)
    def _():
        pl.semaphore_signal(barrier, inc=1, device_id={"dp": me + 4}, device_id_type=MESH)

    for peer in extra:
        pl.semaphore_signal(barrier, inc=1, device_id=peer, device_id_type=MESH)
    ends = jnp.where(z > 0, 1, 0) + jnp.where(z < depth - 1, 1, 0)
    pl.semaphore_wait(barrier, 2 + len(extra) + ends)


def other_core(source, target, send, receive):
    return pltpu.make_async_remote_copy(
        src_ref=source,
        dst_ref=target,
        send_sem=send,
        recv_sem=receive,
        device_id={"tensor": 1 - lax.axis_index("tensor")},
        device_id_type=MESH,
    )


class Gather:
    def __init__(self, depth, parts, whole, far, sems):
        self.whole, self.far = whole, far
        self.depth = depth
        self.me, self.z, self.y, self.x = place()
        self.x_peer = self.z * 4 + self.y * 2 + 1 - self.x
        self.y_peer = self.z * 4 + (1 - self.y) * 2 + self.x
        self.rows = whole.shape[1] // parts
        width = whole.shape[2]
        self.third = width // 4
        side = (width - self.third) // 2
        self.a, self.b = (0, side), (side, side)
        self.ab, self.c, self.all = (0, 2 * side), (2 * side, self.third), (0, width)
        (
            self.z_send, self.z_recv, self.zc_send, self.zc_recv, self.xa_send, self.xa_recv, self.yb_send, self.yb_recv,
            self.ya_send, self.ya_recv, self.xb_send, self.xb_recv, self.c_send, self.c_recv, self.far_send, self.far_recv,
        ) = sems
        self.slots = line_slots(self.z, depth)

    @staticmethod
    def semaphores(depth, pieces):
        sem = pltpu.SemaphoreType.DMA
        return [
            *[sem((pieces, depth + 1)), sem((pieces, depth))] * 2,
            *[sem((pieces, depth))] * 4,
            *[sem((pieces, depth, 2))] * 4,
            sem((pieces, 2)),
            sem((pieces, 2)),
            sem((pieces,)),
            sem((pieces,)),
        ]

    def block(self, zb, yb, xb):
        return zb * 4 + yb * 2 + xb

    def cut(self, ref, p, block, count, columns):
        first = pl.multiple_of(block * self.rows, self.rows)
        return ref.at[p, pl.ds(first, count * self.rows), pl.ds(*columns)]

    def copy(self, p, block, count, columns, send, receive, device):
        part = self.cut(self.whole, p, block, count, columns)
        return remote(part, part, send, receive, device)

    def forward(self, p, block, count, columns):
        if p == 0 and columns[0] + columns[1] <= self.c[0]:
            return
        if p == 0:
            columns = self.c
        other_core(
            self.cut(self.whole, p, block, count, columns),
            self.cut(self.far, p, block, count, columns),
            self.far_send.at[p],
            self.far_recv.at[p],
        ).start()

    def far_copy(self, p):
        columns = self.c if p == 0 else self.all
        part = self.far.at[p, :, pl.ds(*columns)]
        return other_core(part, part, self.far_send.at[p], self.far_recv.at[p])

    def z_copy(self, p, zb, way, back=False):
        block = self.block(zb, self.y, self.x)
        sem = self.depth if back else zb
        return self.copy(
            p, block, 1, self.ab, self.z_send.at[p, sem], self.z_recv.at[p, zb], self.me + 4 * way
        )

    def zc_copy(self, p, zb, way, back=False):
        sem = self.depth if back else zb
        return self.copy(
            p, zb * 4, 4, self.c, self.zc_send.at[p, sem], self.zc_recv.at[p, zb], self.me + 4 * way
        )

    def xa(self, p, zb, xb):
        block = self.block(zb, self.y, xb)
        return self.copy(
            p, block, 1, self.a, self.xa_send.at[p, zb], self.xa_recv.at[p, zb], self.x_peer
        )

    def yb(self, p, zb, yb):
        block = self.block(zb, yb, self.x)
        return self.copy(
            p, block, 1, self.b, self.yb_send.at[p, zb], self.yb_recv.at[p, zb], self.y_peer
        )

    def ya(self, p, zb, yb, xb):
        block = self.block(zb, yb, xb)
        return self.copy(
            p, block, 1, self.a, self.ya_send.at[p, zb, xb], self.ya_recv.at[p, zb, xb], self.y_peer
        )

    def xb(self, p, zb, yb, xb):
        block = self.block(zb, yb, xb)
        return self.copy(
            p, block, 1, self.b, self.xb_send.at[p, zb, yb], self.xb_recv.at[p, zb, yb], self.x_peer
        )

    def xc(self, p, xb):
        block = self.block(self.z, self.y, xb)
        return self.copy(
            p, block, 1, self.c, self.c_send.at[p, 0], self.c_recv.at[p, 0], self.x_peer
        )

    def yc(self, p, yb):
        block = self.block(self.z, yb, 0)
        return self.copy(
            p, block, 2, self.c, self.c_send.at[p, 1], self.c_recv.at[p, 1], self.y_peer
        )

    def both_ways(self, copy, act):
        @pl.when(self.z < self.depth - 1)
        def _():
            act(copy(self.z, 1))

        @pl.when(self.z > 0)
        def _():
            act(copy(self.z, -1, True))

    def spread(self, p, zb):
        self.xa(p, zb, self.x).start()
        self.yb(p, zb, self.y).start()
        self.ya(p, zb, self.y, self.x).start()
        self.xb(p, zb, self.y, self.x).start()

    def turn(self, p, zb):
        self.xa(p, zb, 1 - self.x).wait_recv()
        self.ya(p, zb, self.y, 1 - self.x).start()
        self.forward(p, self.block(zb, self.y, 1 - self.x), 1, self.a)
        self.yb(p, zb, 1 - self.y).wait_recv()
        self.xb(p, zb, 1 - self.y, self.x).start()
        self.forward(p, self.block(zb, 1 - self.y, self.x), 1, self.b)

    def at_step(self, step, act):
        for zb, valid, way in self.slots[2 * step : 2 * step + 2]:
            on = (self.z + way >= 0) & (self.z + way < self.depth)
            pl.when(valid)(functools.partial(act, zb, way, on))

    def arrive(self, p, step):
        def act(zb, way, on):
            self.z_copy(p, zb, way).wait_recv()
            pl.when(on)(lambda: self.z_copy(p, zb, way).start())
            self.spread(p, zb)
            self.forward(p, self.block(zb, self.y, self.x), 1, self.ab)

        self.at_step(step, act)

    def arrive_c(self, p, step):
        def act(zb, way, on):
            self.zc_copy(p, zb, way).wait_recv()
            pl.when(on)(lambda: self.zc_copy(p, zb, way).start())
            self.forward(p, zb * 4, 4, self.c)

        self.at_step(step, act)

    def stage(self, p, s):
        depth = self.depth
        if s == 0:
            self.both_ways(lambda *way: self.z_copy(p, *way), lambda copy: copy.start())
            self.xc(p, self.x).start()
            self.spread(p, self.z)
            self.forward(p, self.me, 1, self.all)
            return
        if s == 1:
            self.xc(p, 1 - self.x).wait_recv()
            self.yc(p, self.y).start()
            self.forward(p, self.block(self.z, self.y, 1 - self.x), 1, self.c)
        if s == 2:
            self.yc(p, 1 - self.y).wait_recv()
            self.both_ways(lambda *way: self.zc_copy(p, *way), lambda copy: copy.start())
            self.forward(p, self.block(self.z, 1 - self.y, 0), 2, self.c)
        if 1 <= s < depth:
            self.arrive(p, s - 1)
        if 3 <= s < depth + 2:
            self.arrive_c(p, s - 3)
        if s == 2:
            self.turn(p, self.z)
        if 3 <= s < depth + 2:
            self.at_step(s - 3, lambda zb, way, on: self.turn(p, zb))
        if s == depth + 2:
            for zb in range(depth):
                for other in range(2):
                    self.ya(p, zb, 1 - self.y, other).wait_recv()
                    self.forward(p, self.block(zb, 1 - self.y, other), 1, self.a)
                    self.xb(p, zb, other, 1 - self.x).wait_recv()
                    self.forward(p, self.block(zb, other, 1 - self.x), 1, self.b)

    def finish(self, p):
        def sent(copy):
            copy.wait_send()

        self.far_copy(p).wait_recv()
        self.far_copy(p).wait_send()
        self.both_ways(lambda *way: self.z_copy(p, *way), sent)
        self.both_ways(lambda *way: self.zc_copy(p, *way), sent)
        for zb in range(self.depth):
            self.xa(p, zb, self.x).wait_send()
            self.yb(p, zb, self.y).wait_send()
            for other in range(2):
                self.ya(p, zb, self.y, other).wait_send()
                self.xb(p, zb, other, self.x).wait_send()
        self.xc(p, self.x).wait_send()
        self.yc(p, self.y).wait_send()

        def passed(zb, way, on):
            pl.when(on)(lambda: sent(self.z_copy(p, zb, way)))
            pl.when(on)(lambda: sent(self.zc_copy(p, zb, way)))

        for step in range(self.depth - 1):
            self.at_step(step, passed)


def looped(count, body, between):
    @pl.loop(0, count)
    def _(i):
        body(i)
        for step, acts in between.items():

            @pl.when(i == step)
            def _():
                for act in acts:
                    act()


def front_kernel(
    depth, shards_ref, tokens_ref, cotangent_ref, own_of_ref, dealt_of_ref, bias_ref, score_bias_ref,
    whole_ref, far_ref, qkv_out, hidden_out, upstream_ref, context_ref, total_ref,
    token, upper, hidden, weight, qkv, local_sem, core_sem, *sems,
):
    pieces = whole_ref.shape[0]
    half_rows, width = tokens_ref.shape
    rows = 2 * half_rows
    pairs = qkv.shape[0]
    member = lax.axis_index("tensor")
    lines = Gather(depth, 4 * depth, whole_ref, far_ref, sems)
    me = lines.me

    own = [
        pltpu.make_async_copy(
            shards_ref.at[p], lines.cut(whole_ref, p, me, 1, lines.all), local_sem.at[p]
        )
        for p in range(pieces)
    ]
    own += [
        pltpu.make_async_copy(tokens_ref, token.at[member], local_sem.at[pieces]),
        pltpu.make_async_copy(cotangent_ref, upper.at[member], local_sem.at[pieces + 1]),
    ]
    for copy in own:
        copy.start()
    greet_line(me, lines.z, lines.y, lines.x, depth, [{"tensor": 1 - member}])
    crossing = [
        other_core(tokens_ref, token.at[member], core_sem.at[0, 0], core_sem.at[0, 1]),
        other_core(cotangent_ref, upper.at[member], core_sem.at[1, 0], core_sem.at[1, 1]),
    ]
    for copy in own[:pieces]:
        copy.wait()
    lines.stage(0, 0)
    for copy in crossing:
        copy.start()
    for copy in own[pieces:]:
        copy.wait()

    def picked(index_ref, source, at):
        index = index_ref[at, :]
        total = None
        for which in range(2):
            places = lax.broadcasted_iota(jnp.int32, (TILE, half_rows), 1) + which * half_rows
            chosen = jnp.where(index == places, 1.0, 0.0).astype(LOW)
            part = dot_nn(chosen, source[which])
            total = part if total is None else total + part
        return total.astype(LOW)

    def tile(step):
        return pl.ds(pl.multiple_of(step * TILE, TILE), TILE)

    def hidden_tile(step):
        hidden[tile(step), :] = picked(own_of_ref, token, tile(step))

    def upstream_tile(step):
        upstream_ref[tile(step), :] = picked(dealt_of_ref, upper, tile(step))

    crossing[0].wait()
    looped(rows // TILE, hidden_tile, {})
    hidden_copy = pltpu.make_async_copy(hidden, hidden_out, local_sem.at[0])
    hidden_copy.start()
    lines.stage(0, 1)
    crossing[1].wait()
    looped(half_rows // TILE, upstream_tile, {})
    for p, s in ((0, 2), (0, 3), (1, 0), (0, 4), (1, 1), (0, 5), (1, 2), (0, 6)):
        lines.stage(p, s)
    weight_copy = pltpu.make_async_copy(
        whole_ref.at[0, :, pl.ds(0, pairs * 3 * PAIR)], weight, local_sem.at[1]
    )
    weight_copy.start()
    lines.stage(1, 3)
    lines.stage(2, 0)
    weight_copy.wait()

    tall = 2 * TILE

    def project_tile(i):
        pair, step = i // (rows // tall), lax.rem(i, rows // tall)
        at = pl.ds(pl.multiple_of(step * tall, tall), tall)
        columns = pl.ds(pl.multiple_of(pair * 3 * PAIR, PAIR), 3 * PAIR)
        qkv[pair, at, :] = (dot_nn(hidden[at, :], weight[:, columns]) + bias_ref[pair]).astype(LOW)

    looped(pairs * rows // tall, project_tile, {5: [lambda: lines.stage(1, 4)]})
    qkv_copy = pltpu.make_async_copy(qkv, qkv_out, local_sem.at[2])
    qkv_copy.start()

    def attend_step(begin, size):
        def step_of(i):
            pair, step = i // (size // TILE), lax.rem(i, size // TILE)
            columns = pl.ds(pl.multiple_of(pair * PAIR, PAIR), PAIR)
            attend_tile(
                qkv, pair, score_bias_ref, begin, size, step, context_ref, columns, total_ref
            )

        return step_of

    def then(*stages):
        return [functools.partial(lines.stage, *stage) for stage in stages]

    looped(
        pairs * LONGEST // TILE,
        attend_step(0, LONGEST),
        {0: then((2, 1)), 4: then((1, 5)), 8: then((2, 2)), 12: then((1, 6))},
    )
    looped(
        pairs * (rows - LONGEST) // TILE,
        attend_step(LONGEST, rows - LONGEST),
        {0: then((2, 3)), 5: then((2, 4))},
    )
    lines.stage(2, 5)
    lines.stage(2, 6)
    for p in range(pieces):
        lines.finish(p)
    hidden_copy.wait()
    qkv_copy.wait()


def front(shards, tokens, cotangent, own_of, dealt_of, bias, score_bias, parts):
    pieces, shard_rows, columns = shards.shape
    half_rows, width = tokens.shape
    rows, pairs, depth = 2 * half_rows, bias.shape[0], parts // 4
    shape, sem = jax.ShapeDtypeStruct, pltpu.SemaphoreType.DMA
    vmem, anywhere = pl.BlockSpec(memory_space=pltpu.VMEM), pl.BlockSpec(memory_space=pl.ANY)
    return pl.pallas_call(
        functools.partial(front_kernel, depth),
        in_specs=[*[anywhere] * 3, *[vmem] * 4],
        out_specs=[*[anywhere] * 4, *[vmem] * 3],
        out_shape=[
            shape((pieces, parts * shard_rows, columns), LOW),
            shape((pieces, parts * shard_rows, columns), LOW),
            shape((pairs, rows, 3 * PAIR), LOW),
            shape((rows, width), LOW),
            shape((half_rows, width), LOW),
            shape((rows, pairs * PAIR), LOW),
            shape((pairs, 8, rows), WIDE),
        ],
        scratch_shapes=[
            pltpu.VMEM((2, half_rows, width), LOW),
            pltpu.VMEM((2, half_rows, width), LOW),
            pltpu.VMEM((rows, width), LOW),
            pltpu.VMEM((width, pairs * 3 * PAIR), LOW),
            pltpu.VMEM((pairs, rows, 3 * PAIR), LOW),
            sem((pieces + 2,)),
            sem((2, 2)),
            *Gather.semaphores(depth, pieces),
        ],
        compiler_params=pltpu.CompilerParams(
            collective_id=0, has_side_effects=True, vmem_limit_bytes=60 * MIB
        ),
    )(shards, tokens, cotangent, own_of[:, None], dealt_of[:, None], bias, score_bias)


def scatter_kernel(depth, count, *refs):
    grads, vector_ref = refs[:count], refs[count]
    shards, vector_out = refs[count + 1 : 2 * count + 1], refs[2 * count + 1]
    refs = refs[2 * count + 2 :]
    buffers = [refs[10 * i : 10 * i + 10] for i in range(count)]
    (
        vector_buffer, vector_send, vector_recv, a1_send, a1_recv, b1_send, b1_recv,
        a2_send, a2_recv, b2_send, b2_recv, z_send, z_recv,
    ) = refs[10 * count :]
    me, z, y, x = place()
    member = lax.axis_index("tensor")
    x_peer, y_peer = z * 4 + y * 2 + 1 - x, z * 4 + (1 - y) * 2 + x
    chunk = 16
    levels = depth.bit_length() - 1

    def block(zb, yb, xb):
        return zb * 4 + yb * 2 + xb

    partners = [{"tensor": 1 - member}, {"dp": x_peer}, {"dp": y_peer}]
    for level in range(levels):
        reach = 1 << level
        partners.append({"dp": me + 4 * reach * (1 - 2 * ((z // reach) % 2))})

    def vector_copy(step):
        return pltpu.make_async_remote_copy(
            src_ref=vector_buffer.at[step],
            dst_ref=vector_buffer.at[len(partners) + 1 + step],
            send_sem=vector_send.at[step],
            recv_sem=vector_recv.at[step],
            device_id=partners[step],
            device_id_type=MESH,
        )

    def vector_step(step):
        if step == 0:
            vector_buffer[0] = vector_ref[...]
        elif step <= len(partners):
            vector_copy(step - 1).wait_recv()
            vector_buffer[step] = vector_buffer[step - 1] + vector_buffer[len(partners) + step]
        if step < len(partners):
            vector_copy(step).start()
        if step == len(partners):
            vector_out[...] = vector_buffer[step]

    def a1(i, zb):
        half = grads[i].shape[2] // 2
        return remote(
            grads[i].at[pl.ds(block(zb, 1 - y, 0), 2), :, pl.ds(0, half)],
            buffers[i][0].at[zb],
            a1_send.at[i, zb],
            a1_recv.at[i, zb],
            y_peer,
        )

    def b1(i, zb, yy):
        half = grads[i].shape[2] // 2
        return remote(
            grads[i].at[block(zb, yy, 1 - x), :, pl.ds(half, half)],
            buffers[i][1].at[zb, yy],
            b1_send.at[i, zb, yy],
            b1_recv.at[i, zb, yy],
            x_peer,
        )

    def a2(i, zb):
        return remote(
            buffers[i][2].at[zb], buffers[i][4].at[zb], a2_send.at[i, zb], a2_recv.at[i, zb], x_peer
        )

    def b2(i, zb):
        return remote(
            buffers[i][3].at[zb], buffers[i][5].at[zb], b2_send.at[i, zb], b2_recv.at[i, zb], y_peer
        )

    def along_z(i, zb, way):
        slot = zb if way > 0 else zb + (depth - zb) * jnp.where(zb == z - 1, 1, 0)
        return remote(
            buffers[i][9].at[zb],
            buffers[i][8].at[slot],
            z_send.at[i, zb],
            z_recv.at[i, slot],
            me + 4 * way,
        )

    def from_z(i, slot):
        return remote(
            buffers[i][9].at[0], buffers[i][8].at[slot], z_send.at[i, 0], z_recv.at[i, slot], me
        )

    def open_slot(zb):
        for i in range(count):
            a1(i, zb).start()
            b1(i, zb, 0).start()
            b1(i, zb, 1).start()

    def first_sum(zb):
        for i in range(count):
            half = grads[i].shape[2] // 2
            r1a, r1b, t1a, t1b, _, _, s2a, s2b, _, _ = buffers[i]
            a1(i, zb).wait_recv()

            @pl.loop(0, t1a.shape[1] // chunk)
            def _(step):
                rows = pl.ds(pl.multiple_of(step * chunk, chunk), chunk)
                t1a[zb, rows, :] = (
                    grads[i][block(zb, y, 1 - x), rows, 0:half].astype(WIDE)
                    + r1a[zb, 1 - x, rows, :].astype(WIDE)
                ).astype(LOW)

            a2(i, zb).start()
            b1(i, zb, 0).wait_recv()
            b1(i, zb, 1).wait_recv()

            @pl.loop(0, t1a.shape[1] // chunk)
            def _(step):
                rows = pl.ds(pl.multiple_of(step * chunk, chunk), chunk)
                t1b[zb, rows, :] = (
                    grads[i][block(zb, 1 - y, x), rows, half : 2 * half].astype(WIDE)
                    + r1b[zb, 1 - y, rows, :].astype(WIDE)
                ).astype(LOW)

            b2(i, zb).start()

            @pl.loop(0, t1a.shape[1] // chunk)
            def _(step):
                rows = pl.ds(pl.multiple_of(step * chunk, chunk), chunk)
                s2a[zb, rows, :] = grads[i][block(zb, y, x), rows, 0:half].astype(WIDE) + r1a[
                    zb, x, rows, :
                ].astype(WIDE)
                s2b[zb, rows, :] = grads[i][block(zb, y, x), rows, half : 2 * half].astype(
                    WIDE
                ) + r1b[zb, y, rows, :].astype(WIDE)

    def second_sum(i, zb):
        _, _, _, _, r2a, r2b, s2a, s2b, _, _ = buffers[i]
        a2(i, zb).wait_recv()
        b2(i, zb).wait_recv()

        @pl.loop(0, r2a.shape[1] // chunk)
        def _(step):
            rows = pl.ds(pl.multiple_of(step * chunk, chunk), chunk)
            s2a[zb, rows, :] += r2a[zb, rows, :].astype(WIDE)
            s2b[zb, rows, :] += r2b[zb, rows, :].astype(WIDE)

    def add_z(i, zb, slot):
        _, _, _, _, _, _, s2a, s2b, rz, _ = buffers[i]
        half = grads[i].shape[2] // 2
        from_z(i, slot).wait_recv()

        @pl.loop(0, s2a.shape[1] // chunk)
        def _(step):
            rows = pl.ds(pl.multiple_of(step * chunk, chunk), chunk)
            s2a[zb, rows, :] += rz[slot, rows, 0:half].astype(WIDE)
            s2b[zb, rows, :] += rz[slot, rows, half : 2 * half].astype(WIDE)

    def pass_on(zb, way):
        for i in range(count):
            _, _, _, _, _, _, s2a, s2b, _, tz = buffers[i]
            half = grads[i].shape[2] // 2
            second_sum(i, zb)

            @pl.when((z - way >= 0) & (z - way < depth))
            def _():
                add_z(i, zb, zb)

            @pl.loop(0, s2a.shape[1] // chunk)
            def _(step):
                rows = pl.ds(pl.multiple_of(step * chunk, chunk), chunk)
                tz[zb, rows, 0:half] = s2a[zb, rows, :].astype(LOW)
                tz[zb, rows, half : 2 * half] = s2b[zb, rows, :].astype(LOW)

            along_z(i, zb, way).start()

    def finish():
        for i in range(count):
            _, _, _, _, _, _, s2a, s2b, _, _ = buffers[i]
            half = grads[i].shape[2] // 2
            second_sum(i, z)

            @pl.when(z > 0)
            def _():
                add_z(i, z, z)

            @pl.when(z < depth - 1)
            def _():
                add_z(i, z, depth)

            @pl.loop(0, s2a.shape[1] // chunk)
            def _(step):
                rows = pl.ds(pl.multiple_of(step * chunk, chunk), chunk)
                shards[i][rows, 0:half] = s2a[z, rows, :]
                shards[i][rows, half : 2 * half] = s2b[z, rows, :]

    def when(valid, act):
        if valid is None:
            act()
        else:
            pl.when(valid)(act)

    groups = []
    for step in reversed(range(depth - 1)):
        groups.append([(z + 1 + step, z + 1 + step < depth, 1), (z - 1 - step, z - 1 - step >= 0, -1)])
    groups.append([(z, None, 0)])

    greet_line(me, z, y, x, depth, [partners[0], *partners[3:]])
    vector_step(0)
    for group in groups[:2]:
        for zb, valid, _ in group:
            when(valid, functools.partial(open_slot, zb))
    vector_at = 1
    for at, group in enumerate(groups):
        for zb, valid, _ in group:
            when(valid, functools.partial(first_sum, zb))
        if at + 2 < len(groups):
            for zb, valid, _ in groups[at + 2]:
                when(valid, functools.partial(open_slot, zb))
        vector_step(vector_at)
        vector_at += 1
        if at:
            for zb, valid, way in groups[at - 1]:
                when(valid, functools.partial(pass_on, zb, way))
    while vector_at <= len(partners):
        vector_step(vector_at)
        vector_at += 1
    finish()

    for step in range(len(partners)):
        vector_copy(step).wait_send()
    for i in range(count):
        for zb in range(depth):
            a1(i, zb).wait_send()
            b1(i, zb, 0).wait_send()
            b1(i, zb, 1).wait_send()
            a2(i, zb).wait_send()
            b2(i, zb).wait_send()
        for group in groups[:-1]:
            for zb, valid, way in group:

                @pl.when(valid)
                def _(zb=zb, way=way):
                    along_z(i, zb, way).wait_send()


def scatter(grads, vector, parts):
    depth, count = parts // 4, len(grads)
    rows = grads[0].shape[0] // parts
    sem = pltpu.SemaphoreType.DMA
    partners = 3 + depth.bit_length() - 1
    scratch = []
    for g in grads:
        n = g.shape[1]
        half = n // 2
        scratch += [pltpu.VMEM((depth, 2, rows, half), LOW)] * 2
        scratch += [pltpu.VMEM((depth, rows, half), LOW)] * 4
        scratch += [pltpu.VMEM((depth, rows, half), WIDE)] * 2
        scratch += [pltpu.VMEM((depth + 1, rows, n), LOW), pltpu.VMEM((depth, rows, n), LOW)]
    vmem = pl.BlockSpec(memory_space=pltpu.VMEM)
    return pl.pallas_call(
        functools.partial(scatter_kernel, depth, count),
        in_specs=[vmem] * (count + 1),
        out_specs=[vmem] * (count + 1),
        out_shape=[
            *[jax.ShapeDtypeStruct((rows, g.shape[1]), WIDE) for g in grads],
            jax.ShapeDtypeStruct(vector.shape, WIDE),
        ],
        scratch_shapes=[
            *scratch,
            pltpu.VMEM((2 * partners + 1, *vector.shape), WIDE),
            sem((partners,)),
            sem((partners,)),
            *[sem((count, depth))] * 2,
            *[sem((count, depth, 2))] * 2,
            *[sem((count, depth))] * 4,
            sem((count, depth)),
            sem((count, depth + 1)),
        ],
        compiler_params=pltpu.CompilerParams(
            collective_id=1, has_side_effects=True, vmem_limit_bytes=60 * MIB
        ),
    )(*[g.reshape(parts, rows, g.shape[1]) for g in grads], vector)


def normal_cells(value):
    bell = jnp.exp(value * value * -0.5)
    t = 1.0 / (1.0 + 0.39 * 0.7071067811865476 * jnp.abs(value))
    tail = -0.2275377237624147
    for factor in (
        0.8866668177122106,
        -0.6354042576077721,
        0.649562611731642,
        0.0913871257655044,
        0.23532542445435511,
    ):
        tail = tail * t + factor
    tail = 0.5 * tail * t * bell
    return jnp.where(value < 0.0, tail, 1.0 - tail), bell


def feed_kernel(
    context_ref, merge_ref, merge_far_ref, whole_ref, far_ref, hidden_ref, upstream_ref, vectors_ref, bias_ref,
    encoded_ref, branch_ref, grad_ref, merge_grad_ref, expand_grad_ref, reduce_grad_ref, sums_ref, hidden_sums_ref,
    own_ctx, far_ctx, acc, normal, inverse, low, turned, late, late_turned, active, slope, inner_grad,
    expand_buf, reduce_buf, arrived, leaving, kept, done, grad_own, grad_far, merge_send, merge_recv,
    ctx_sem, load_sem, send_sem, recv_sem, out_sem, last_sem,
):
    rows = hidden_ref.shape[0]
    chunks, _, both = bias_ref.shape
    half = both // 2
    per_piece = whole_ref.shape[2] // (2 * half)
    member = lax.axis_index("tensor")
    peer = {"tensor": 1 - member}
    tall, short = 256, 128
    width = hidden_ref.shape[1]

    def across(source, target, send, receive):
        return pltpu.make_async_remote_copy(
            src_ref=source,
            dst_ref=target,
            send_sem=send,
            recv_sem=receive,
            device_id=peer,
            device_id_type=MESH,
        )

    def rows_of(which):
        return pl.ds(pl.multiple_of(which * rows, rows), rows)

    def tile(step, size):
        return pl.ds(pl.multiple_of(step * size, size), size)

    def loads(j, slot):
        piece, at = 1 + j // per_piece, lax.rem(j, per_piece) * half
        copies = []
        for kind, buf in enumerate((expand_buf, reduce_buf)):
            first = pl.multiple_of(at + kind * per_piece * half, half)
            for side, source in enumerate((far_ref, whole_ref)):
                copies.append(
                    pltpu.make_async_copy(
                        source.at[piece, :, pl.ds(first, half)],
                        buf.at[slot, :, pl.ds(side * half, half)],
                        load_sem.at[slot, kind, side],
                    )
                )
        return copies

    for copy in loads(0, 0):
        copy.start()
    barrier = pltpu.get_barrier_semaphore()
    pl.semaphore_signal(barrier, inc=1, device_id=peer, device_id_type=MESH)
    pl.semaphore_wait(barrier, 1)
    out_ctx = across(context_ref.at[rows_of(1 - member)], far_ctx, ctx_sem.at[0], ctx_sem.at[1])
    out_ctx.start()
    in_ctx = pltpu.make_async_copy(context_ref.at[rows_of(member)], own_ctx, ctx_sem.at[2])
    in_ctx.start()
    sums_ref[...] = jnp.zeros_like(sums_ref)
    in_ctx.wait()
    out_ctx.wait()

    def norm(values):
        center = values - jnp.mean(values, axis=1, keepdims=True)
        spread = jnp.mean(center * center, axis=1, keepdims=True)
        scale = lax.rsqrt(spread + norm_epsilon)
        return center * scale, scale

    def norm_back(scaled, unit, scale):
        return scale * (
            scaled
            - jnp.mean(scaled, axis=1, keepdims=True)
            - unit * jnp.mean(scaled * unit, axis=1, keepdims=True)
        )

    def add_sum(row, values):
        sums_ref[row : row + 1, :] += jnp.sum(values, axis=0, keepdims=True)

    @pl.loop(0, rows // short)
    def _(step):
        at = tile(step, short)
        branch = dot_nt(own_ctx[at, :], merge_ref[...]) + dot_nt(far_ctx[at, :], merge_far_ref[...])
        unit, scale = norm(hidden_ref[at, :].astype(WIDE) + branch + vectors_ref[2:3, :])
        normed = unit * vectors_ref[3:4, :] + vectors_ref[4:5, :]
        normal[at, :] = unit
        inverse[at, :] = jnp.broadcast_to(scale, (short, 128))
        low[at, :] = normed.astype(LOW)
        turned[:, at] = normed.T.astype(LOW)
        acc[at, :] = normed + vectors_ref[5:6, :]

    @pl.loop(0, chunks)
    def _(j):
        slot = lax.rem(j, 2)
        for copy in loads(j, slot):
            copy.wait()

        @pl.when(j + 1 < chunks)
        def _():
            for copy in loads(j + 1, 1 - slot):
                copy.start()

        for step in range(rows // tall):
            at = slice(step * tall, (step + 1) * tall)
            inner = dot_nn(low[at, :], expand_buf[slot]) + bias_ref[j]
            below, bell = normal_cells(inner)
            held = (inner * below).astype(LOW)
            active[j, at, :] = held
            slope[j, at, :] = (below + inner * bell * 0.3989422804014327).astype(LOW)
            acc[at, :] += dot_nt(held, reduce_buf[slot])

    for copy in loads(0, 0):
        copy.start()

    @pl.loop(0, rows // short)
    def _(step):
        at = tile(step, short)
        unit, scale = norm(acc[at, :])
        encoded_ref[at, :] = (unit * vectors_ref[6:7, :] + vectors_ref[7:8, :]).astype(LOW)
        upper = upstream_ref[at, :].astype(WIDE)
        add_sum(6, upper * unit)
        add_sum(7, upper)
        grad = norm_back(upper * vectors_ref[6:7, :], unit, scale)
        grad_low = grad.astype(LOW)
        add_sum(5, grad_low.astype(WIDE))
        acc[at, :] = grad
        late[at, :] = grad_low
        late_turned[:, at] = grad.T.astype(LOW)

    def send(j, kind):
        return across(
            leaving.at[lax.rem(j, 2), kind],
            arrived.at[lax.rem(j, 4), kind],
            send_sem.at[lax.rem(j, 2), kind],
            recv_sem.at[lax.rem(j, 4), kind],
        )

    def store(j, kind):
        target = (expand_grad_ref, reduce_grad_ref)[kind]
        cols = pl.ds(pl.multiple_of(j * half, half), half)
        return pltpu.make_async_copy(
            done.at[lax.rem(j, 2), kind], target.at[:, cols], out_sem.at[lax.rem(j, 2), kind]
        )

    def finish(j):
        for kind in range(2):
            send(j, kind).wait_recv()

            @pl.when(j >= 2)
            def _():
                store(j - 2, kind).wait()

            @pl.loop(0, width // tall)
            def _(step):
                at = tile(step, tall)
                done[lax.rem(j, 2), kind, at, :] = (
                    kept[lax.rem(j, 2), kind, at, :]
                    + arrived[lax.rem(j, 4), kind, at, :].astype(WIDE)
                ).astype(LOW)

            store(j, kind).start()

    @pl.loop(0, chunks)
    def _(j):
        slot = lax.rem(j, 2)
        for copy in loads(j, slot):
            copy.wait()

        @pl.when(j + 1 < chunks)
        def _():
            for copy in loads(j + 1, 1 - slot):
                copy.start()

        total = jnp.zeros((1, both), WIDE)
        for step in range(rows // tall):
            at = slice(step * tall, (step + 1) * tall)
            grad = dot_nn(late[at, :], reduce_buf[slot]) * slope[j, at, :].astype(WIDE)
            grad = grad.astype(LOW)
            inner_grad[at, :] = grad
            total = total + jnp.sum(grad.astype(WIDE), axis=0, keepdims=True)
            acc[at, :] += dot_nt(grad, expand_buf[slot])
        hidden_sums_ref[j] = total

        @pl.when(j >= 2)
        def _():
            for kind in range(2):
                send(j - 2, kind).wait_send()

        for kind, (left, right) in enumerate(((turned, inner_grad), (late_turned, active.at[j]))):
            for step in range(width // tall):
                at = slice(step * tall, (step + 1) * tall)
                part = dot_nn(left[at, :], right[...])
                leaving[slot, kind, at, :] = part[:, 0:half].astype(LOW)
                kept[slot, kind, at, :] = part[:, half:both]
            send(j, kind).start()

        @pl.when(j >= 1)
        def _():
            finish(j - 1)

    @pl.loop(0, rows // short)
    def _(step):
        at = tile(step, short)
        grad = acc[at, :]
        unit = normal[at, :]
        add_sum(3, grad * unit)
        add_sum(4, grad)
        branch_grad = norm_back(grad * vectors_ref[3:4, :], unit, inverse[at, 0:1])
        branch_low = branch_grad.astype(LOW)
        add_sum(2, branch_low.astype(WIDE))
        branch_ref[at, :] = branch_grad
        turned[:, at] = branch_grad.T.astype(LOW)
        grad_far[at, :] = dot_nn(branch_low, merge_far_ref[...]).astype(LOW)
        grad_own[at, :] = dot_nn(branch_low, merge_ref[...]).astype(LOW)

    out_grad = across(grad_far, grad_ref.at[rows_of(member)], ctx_sem.at[0], ctx_sem.at[1])
    out_grad.start()
    in_grad = pltpu.make_async_copy(grad_own, grad_ref.at[rows_of(member)], ctx_sem.at[2])
    in_grad.start()
    for step in range(width // tall):
        at = slice(step * tall, (step + 1) * tall)
        merge_send[at, :] = dot_nn(turned[at, :], far_ctx[...]).astype(LOW)
    out_merge = across(merge_send, merge_recv, last_sem.at[0], last_sem.at[1])
    out_merge.start()
    finish(chunks - 1)
    for kind in range(2):
        send(chunks - 2, kind).wait_send()
        send(chunks - 1, kind).wait_send()
        store(chunks - 2, kind).wait()
        store(chunks - 1, kind).wait()
    out_merge.wait()
    for step in range(width // tall):
        at = slice(step * tall, (step + 1) * tall)
        merge_grad_ref[at, :] = (
            dot_nn(turned[at, :], own_ctx[...]) + merge_recv[at, :].astype(WIDE)
        ).astype(LOW)
    out_grad.wait()
    in_grad.wait()


def feed_block(context, whole, far, hidden_own, upstream, vectors, bias_own, bias_far):
    total_rows, inner = context.shape
    rows, width = hidden_own.shape
    hidden = bias_own.shape[0]
    merge, merge_far = whole[0, :, -inner:], far[0, :, -inner:]
    half = 256
    chunks = hidden // half
    both = 2 * half
    bias = jnp.concatenate(
        [bias_far.reshape(chunks, 1, half), bias_own.reshape(chunks, 1, half)], axis=2
    )
    vmem, anywhere = pl.BlockSpec(memory_space=pltpu.VMEM), pl.BlockSpec(memory_space=pl.ANY)
    sem = pltpu.SemaphoreType.DMA
    shape = jax.ShapeDtypeStruct
    *results, hidden_sums = pl.pallas_call(
        feed_kernel,
        in_specs=[anywhere, vmem, vmem, *[anywhere] * 2, *[vmem] * 4],
        out_specs=[vmem, vmem, anywhere, vmem, anywhere, anywhere, vmem, vmem],
        out_shape=[
            shape((rows, width), LOW),
            shape((rows, width), WIDE),
            shape((total_rows, inner), LOW),
            shape((width, inner), LOW),
            shape((width, hidden), LOW),
            shape((width, hidden), LOW),
            shape((8, width), WIDE),
            shape((chunks, 1, both), WIDE),
        ],
        scratch_shapes=[
            pltpu.VMEM((rows, inner), LOW),
            pltpu.VMEM((rows, inner), LOW),
            pltpu.VMEM((rows, width), WIDE),
            pltpu.VMEM((rows, width), WIDE),
            pltpu.VMEM((rows, 128), WIDE),
            pltpu.VMEM((rows, width), LOW),
            pltpu.VMEM((width, rows), LOW),
            pltpu.VMEM((rows, width), LOW),
            pltpu.VMEM((width, rows), LOW),
            pltpu.VMEM((chunks, rows, both), LOW),
            pltpu.VMEM((chunks, rows, both), LOW),
            pltpu.VMEM((rows, both), LOW),
            pltpu.VMEM((2, width, both), LOW),
            pltpu.VMEM((2, width, both), LOW),
            pltpu.VMEM((4, 2, width, half), LOW),
            pltpu.VMEM((2, 2, width, half), LOW),
            pltpu.VMEM((2, 2, width, half), WIDE),
            pltpu.VMEM((2, 2, width, half), LOW),
            pltpu.VMEM((rows, inner), LOW),
            pltpu.VMEM((rows, inner), LOW),
            pltpu.VMEM((width, inner), LOW),
            pltpu.VMEM((width, inner), LOW),
            sem((3,)),
            sem((2, 2, 2)),
            sem((2, 2)),
            sem((4, 2)),
            sem((2, 2)),
            sem((2,)),
        ],
        compiler_params=pltpu.CompilerParams(
            collective_id=2, has_side_effects=True, vmem_limit_bytes=60 * MIB
        ),
        cost_estimate=pl.CostEstimate(
            flops=12 * rows * width * 2 * hidden, bytes_accessed=8 * width * hidden * 4, transcendentals=0
        ),
    )(context, merge, merge_far, whole, far, hidden_own, upstream, vectors, bias)
    hidden_far = hidden_sums[:, 0, :half].reshape(-1)
    hidden_near = hidden_sums[:, 0, half:].reshape(-1)
    return (*results, hidden_near, hidden_far)


def adamw_update(master, moment, square, gradient, step_rate, decay_rate):
    moment_new = beta_one * moment + (1.0 - beta_one) * gradient
    square_new = beta_two * square + (1.0 - beta_two) * gradient * gradient
    moment_hat = moment_new / (1.0 - beta_one**STEP)
    square_hat = square_new / (1.0 - beta_two**STEP)
    master_new = master - step_rate * (
        moment_hat / (jnp.sqrt(square_hat) + adam_epsilon) + decay_rate * master
    )
    return (moment_new, square_new, master_new)


def local(
    tokens,
    cotangent,
    lengths,
    dealing,
    project_weight,
    project_first,
    project_second,
    merge_weight,
    merge_first,
    merge_second,
    expand_weight,
    expand_first,
    expand_second,
    reduce_weight,
    reduce_first,
    reduce_second,
    vectors,
    vector_first,
    vector_second,
    hidden_bias,
    hidden_first,
    hidden_second,
):
    parts = lax.axis_size("dp")
    member = lax.axis_index("tensor")
    other = 1 - member
    half_rows, model_width = tokens.shape
    total_rows = 2 * half_rows
    width_half = project_weight.shape[2]
    pairs = width_half // PAIR
    hidden_half = expand_weight.shape[1]
    shard_rows = expand_weight.shape[0]
    own_begin = member * half_rows
    by_kernel = parts % 4 == 0 and (parts & (parts - 1)) == 0 and shard_rows % 16 == 0

    def swap(value):
        return lax.ppermute(value, "tensor", [(0, 1), (1, 0)])

    def own(value, size, which=member):
        return lax.dynamic_slice_in_dim(value, which * size, size, 0)

    segment, own_of, dealt_of, from_own, from_dealt = layout(lengths[0], dealing[0], total_rows)
    dealt_of = own(dealt_of, half_rows)
    short = segment[LONGEST:]
    score_bias = jnp.where(short[:, None] == short[None, :], 0.0, masked_score).astype(WIDE)

    def own_first(index):
        return lax.rem(index - own_begin + total_rows, total_rows)

    projections = (
        project_weight.reshape(3, shard_rows, pairs, PAIR)
        .transpose(1, 2, 0, 3)
        .reshape(shard_rows, 3 * width_half)
    )
    quarter = hidden_half // 2
    reduce_turned = reduce_weight.T
    shards = jnp.stack(
        [
            jnp.concatenate([projections, merge_weight.T], axis=1),
            jnp.concatenate([expand_weight[:, :quarter], reduce_turned[:, :quarter]], axis=1),
            jnp.concatenate([expand_weight[:, quarter:], reduce_turned[:, quarter:]], axis=1),
        ]
    ).astype(LOW)
    zeros_pair = jnp.zeros((pairs, PAIR), WIDE)
    bias_row = jnp.concatenate(
        [
            own(vectors[0], width_half).reshape(pairs, PAIR),
            zeros_pair,
            own(vectors[1], width_half).reshape(pairs, PAIR),
        ],
        axis=1,
    ).reshape(pairs, 1, 3 * PAIR)
    if by_kernel:
        whole, far, qkv, hidden, upstream, context, totals = front(
            shards, tokens, cotangent, own_of, dealt_of, bias_row, score_bias, parts
        )
    else:
        whole = lax.all_gather(shards, "dp", axis=1, tiled=True)
        far = swap(whole)
        token_pair = jnp.concatenate([tokens, swap(tokens)], axis=0)
        upper_pair = jnp.concatenate([cotangent, swap(cotangent)], axis=0)
        hidden = dot_nn(pick_rows(own_first(own_of), total_rows), token_pair).astype(LOW)
        upstream = dot_nn(pick_rows(own_first(dealt_of), total_rows), upper_pair).astype(LOW)
        qkv = jnp.einsum(
            "rd,dpc->prc",
            hidden,
            whole[0, :, : 3 * width_half].reshape(model_width, pairs, 3 * PAIR),
            preferred_element_type=WIDE,
        )
        qkv = (qkv + bias_row).astype(LOW)
        context, totals = attend(qkv, score_bias)

    (
        encoded, branch_grad, context_grad, merge_grad, expand_grad, reduce_grad, sums, hidden_part_own, hidden_part_far,
    ) = feed_block(
        context,
        whole,
        far,
        own(hidden, half_rows),
        upstream,
        vectors,
        own(hidden_bias, hidden_half),
        own(hidden_bias, hidden_half, other),
    )
    encoded_pair = jnp.concatenate([encoded, swap(encoded)], axis=0)
    encoded_out = dot_nn(
        pick_rows(own_first(own(from_dealt, half_rows)), total_rows), encoded_pair
    ).astype(LOW)
    mixed_grads = attend_back(qkv, score_bias, context, context_grad, totals)
    mixed_sums = jnp.sum(mixed_grads.astype(WIDE), axis=1).reshape(pairs, 3, PAIR)
    mixed_grads = mixed_grads.transpose(1, 0, 2).reshape(total_rows, 3 * width_half)
    project_grad = dot_tn(hidden, mixed_grads)
    input_terms = dot_nt(mixed_grads, whole[0, :, : 3 * width_half])
    own_part = own(input_terms, half_rows) + branch_grad
    input_terms = lax.dynamic_update_slice_in_dim(input_terms, own_part, own_begin, 0).astype(LOW)
    input_far = swap(
        dot_nn(pick_rows(own(from_own, half_rows, other), total_rows), input_terms).astype(LOW)
    )
    input_grad = (
        dot_nn(pick_rows(own(from_own, half_rows), total_rows), input_terms)
        + input_far.astype(WIDE)
    ).astype(LOW)

    zeros_width = jnp.zeros((model_width,), WIDE)
    zeros_hidden = jnp.zeros_like(hidden_bias)
    hidden_total = lax.dynamic_update_slice_in_dim(
        lax.dynamic_update_slice_in_dim(
            zeros_hidden, hidden_part_own, member * hidden_half, 0
        ),
        hidden_part_far,
        other * hidden_half,
        0,
    )
    vector_rows = [
        lax.dynamic_update_slice_in_dim(
            zeros_width, mixed_sums[:, c].reshape(-1), member * width_half, 0
        )
        for c in (0, 2)
    ]
    small = jnp.concatenate(
        [
            jnp.stack(vector_rows),
            sums[2:],
            hidden_total.reshape(-1, model_width),
            jnp.zeros((4, model_width), WIDE),
        ],
        axis=0,
    )
    grads = [g.astype(LOW) for g in (project_grad, merge_grad, expand_grad, reduce_grad)]
    if by_kernel:
        *grads, small = scatter(grads, small, parts)
    else:
        grads = [lax.psum_scatter(g, "dp", scatter_dimension=0, tiled=True) for g in grads]
        grads = [g.astype(WIDE) for g in grads]
        small = lax.psum(small, ("dp", "tensor"))
    project_shard, merge_shard, expand_shard, reduce_shard = grads
    project_shard = (
        project_shard.reshape(shard_rows, pairs, 3, PAIR)
        .transpose(2, 0, 1, 3)
        .reshape(3, shard_rows, width_half)
    )
    vector_grad = small[:8]
    hidden_grad = small[8:12].reshape(-1)
    return (
        encoded_out,
        input_grad,
        *adamw_update(
            project_weight, project_first, project_second, project_shard, rate_project, weight_decay
        ),
        *adamw_update(
            merge_weight, merge_first, merge_second, merge_shard.T, rate_merge, weight_decay
        ),
        *adamw_update(
            expand_weight, expand_first, expand_second, expand_shard, rate_expand, weight_decay
        ),
        *adamw_update(
            reduce_weight, reduce_first, reduce_second, reduce_shard.T, rate_reduce, weight_decay
        ),
        *adamw_update(vectors, vector_first, vector_second, vector_grad, rate_vectors, 0.0),
        *adamw_update(hidden_bias, hidden_first, hidden_second, hidden_grad, rate_hidden, 0.0),
        vector_grad,
    )


def solution(mesh):
    sharded = (
        P("dp", None),
        P("dp", None),
        *[P(None, "dp", "tensor")] * 3,
        *[P("tensor", "dp")] * 3,
        *[P("dp", "tensor")] * 3,
        *[P("tensor", "dp")] * 3,
        *[P()] * 6,
    )
    rows = P(("dp", "tensor"), None)
    return jax.shard_map(
        local,
        mesh=mesh,
        in_specs=(rows, rows, *sharded),
        out_specs=(rows, rows, *sharded[2:], P()),
        check_vma=False,
    )
```

```python
import functools

import jax
import jax.numpy as jnp
from jax import lax
from jax.experimental import pallas as pl
from jax.experimental.pallas import tpu as pltpu
from jax.sharding import PartitionSpec as P

HEAD_DIM = 64
LONGEST = 1024
STEP = 10
PAIR = 2 * HEAD_DIM
TILE = 256
MIB = 1024 * 1024
MESH = pl.DeviceIdType.MESH
LOW = jnp.bfloat16
WIDE = jnp.float32

beta_one = 0.9
beta_two = 0.999
adam_epsilon = 1e-08
weight_decay = 0.01
norm_epsilon = 1e-05
masked_score = -1e30
rate_project = 0.03
rate_merge = 0.3
rate_expand = 0.03
rate_reduce = 0.015
rate_vectors = 0.4
rate_hidden = 0.1


def dot_nn(a, b):
    return jnp.dot(a, b, preferred_element_type=WIDE)


def dot_nt(a, b):
    return lax.dot_general(a, b, (((1,), (1,)), ((), ())), preferred_element_type=WIDE)


def dot_tn(a, b):
    return lax.dot_general(a, b, (((0,), (0,)), ((), ())), preferred_element_type=WIDE)


def layout(lengths_row, dealing_row, total_rows):
    slots = jnp.arange(lengths_row.shape[0], dtype=jnp.int32)
    places = jnp.arange(total_rows, dtype=jnp.int32)
    rank_of = jnp.sum(jnp.where(dealing_row[None, :] == slots[:, None], slots[None, :], 0), axis=1)
    own_start = jnp.cumsum(lengths_row) - lengths_row
    dealt_start = jnp.sum(
        jnp.where(rank_of[None, :] < rank_of[:, None], lengths_row[None, :], 0), axis=1
    )
    longest = lengths_row == LONGEST
    short = jnp.where(longest, 0, lengths_row)
    start = jnp.where(longest, 0, LONGEST + jnp.cumsum(short) - short)

    def inside(begin):
        return (places[:, None] >= begin[None, :]) & (
            places[:, None] < (begin + lengths_row)[None, :]
        )

    def moved(begin, end):
        return places + jnp.sum(jnp.where(inside(begin), (end - begin)[None, :], 0), axis=1)

    segment = jnp.sum(jnp.where(inside(start), slots[None, :], 0), axis=1)
    return (
        segment,
        moved(start, own_start),
        moved(start, dealt_start),
        moved(own_start, start),
        moved(dealt_start, start),
    )


def pick_rows(index, rows):
    places = jnp.arange(rows, dtype=jnp.int32)
    return (index[:, None] == places[None, :]).astype(LOW)


def attend_tile(qkv_ref, pair, bias_ref, begin, size, step, context_ref, columns, total_ref):
    lane = lax.broadcasted_iota(jnp.int32, (1, PAIR), 1)
    scale = HEAD_DIM ** (-0.5)
    first = pl.multiple_of(begin + step * TILE, TILE)
    query = qkv_ref[pair, pl.ds(first, TILE), 0:PAIR]
    key = qkv_ref[pair, begin : begin + size, PAIR : 2 * PAIR]
    value = qkv_ref[pair, begin : begin + size, 2 * PAIR : 3 * PAIR]
    outcome = []
    for head in range(2):
        chosen = jnp.where(lane // HEAD_DIM == head, scale, 0.0).astype(LOW)
        scores = dot_nt(query * chosen, key)
        if begin:
            inner = pl.multiple_of(step * TILE, TILE)
            scores = scores + bias_ref[pl.ds(inner, TILE), :]
        top = jnp.max(scores, axis=1, keepdims=True)
        exponent = jnp.exp(scores - top)
        total = jnp.sum(exponent, axis=1, keepdims=True)
        outcome.append(dot_nn(exponent.astype(LOW), value) / total)
        log_total = jnp.broadcast_to(top + jnp.log(total), (TILE, PAIR))
        total_ref[pair, head : head + 1, pl.ds(first, TILE)] = log_total.T[0:1, :]
    context_ref[pl.ds(first, TILE), columns] = jnp.where(
        lane < HEAD_DIM, outcome[0], outcome[1]
    ).astype(LOW)


def attend_kernel(qkv_ref, bias_ref, context_ref, total_ref):
    rows = qkv_ref.shape[1]
    for begin, size in ((0, LONGEST), (LONGEST, rows - LONGEST)):

        @pl.loop(0, size // TILE)
        def _(step):
            attend_tile(
                qkv_ref, 0, bias_ref, begin, size, step, context_ref, slice(0, PAIR), total_ref
            )


def attend(qkv, bias):
    pairs, rows, width = qkv.shape
    return pl.pallas_call(
        attend_kernel,
        grid=(pairs,),
        in_specs=[
            pl.BlockSpec((1, rows, width), lambda p: (p, 0, 0)),
            pl.BlockSpec(bias.shape, lambda p: (0, 0)),
        ],
        out_specs=[
            pl.BlockSpec((rows, PAIR), lambda p: (0, p)),
            pl.BlockSpec((1, 8, rows), lambda p: (p, 0, 0)),
        ],
        out_shape=[
            jax.ShapeDtypeStruct((rows, pairs * PAIR), LOW),
            jax.ShapeDtypeStruct((pairs, 8, rows), WIDE),
        ],
        compiler_params=pltpu.CompilerParams(vmem_limit_bytes=48 * MIB),
    )(qkv, bias)


def attend_back_open(qkv_ref, context_ref, upper_ref, dots, key_turned, queries, uppers):
    lane = lax.broadcasted_iota(jnp.int32, (1, PAIR), 1)
    product = (upper_ref[...].astype(WIDE) * context_ref[...].astype(WIDE)).T
    for head in range(2):
        band = slice(head * HEAD_DIM, (head + 1) * HEAD_DIM)
        dots[head : head + 1, :] = jnp.sum(product[band, :], axis=0, keepdims=True)
        chosen = lane // HEAD_DIM == head
        queries[head] = qkv_ref[:, 0:PAIR] * jnp.where(chosen, HEAD_DIM ** (-0.5), 0.0).astype(LOW)
        uppers[head] = upper_ref[...] * jnp.where(chosen, 1.0, 0.0).astype(LOW)
    key_turned[...] = qkv_ref[:, PAIR : 2 * PAIR].astype(WIDE).T.astype(LOW)


def attend_back_tile(
    qkv_ref, bias_ref, total_ref, dots, key_turned, queries, uppers, query_sum, begin, size, step
):
    block = slice(begin, begin + size)
    first = pl.multiple_of(begin + step * TILE, TILE)
    key = qkv_ref[pl.ds(first, TILE), PAIR : 2 * PAIR]
    value = qkv_ref[pl.ds(first, TILE), 2 * PAIR : 3 * PAIR]
    key_sum = jnp.zeros((TILE, PAIR), WIDE)
    value_sum = jnp.zeros((TILE, PAIR), WIDE)
    for head in range(2):
        band = slice(head * HEAD_DIM, (head + 1) * HEAD_DIM)
        query = queries[head, block, :]
        upper = uppers[head, block, :]
        scores = dot_nt(key, query)
        if begin:
            inner = pl.multiple_of(step * TILE, TILE)
            scores = scores + bias_ref[pl.ds(inner, TILE), :]
        probability = jnp.exp(scores - total_ref[head : head + 1, block])
        weight_grads = dot_nt(value, upper)
        score_grads = (probability * (weight_grads - dots[head : head + 1, block])).astype(LOW)
        value_sum = value_sum + dot_nn(probability.astype(LOW), upper)
        key_sum = key_sum + dot_nn(score_grads, query)
        query_sum[band, block] += dot_nn(key_turned[band, pl.ds(first, TILE)], score_grads)
    return pl.ds(first, TILE), key_sum, value_sum


def attend_back_kernel(
    qkv_ref, bias_ref, context_ref, grad_ref, total_ref, out_ref, dots, key_turned, queries, uppers, query_sum
):
    rows = qkv_ref.shape[1]
    qkv = qkv_ref.at[0]
    attend_back_open(qkv, context_ref, grad_ref, dots, key_turned, queries, uppers)
    for begin, size in ((0, LONGEST), (LONGEST, rows - LONGEST)):
        block = slice(begin, begin + size)
        query_sum[:, block] = jnp.zeros((PAIR, size), WIDE)

        @pl.loop(0, size // TILE)
        def _(step):
            at, key_sum, value_sum = attend_back_tile(
                qkv, bias_ref, total_ref.at[0], dots, key_turned, queries, uppers, query_sum, begin, size, step
            )
            out_ref[0, at, PAIR : 2 * PAIR] = key_sum.astype(LOW)
            out_ref[0, at, 2 * PAIR : 3 * PAIR] = value_sum.astype(LOW)

        out_ref[0, block, 0:PAIR] = (query_sum[:, block] * HEAD_DIM ** (-0.5)).T.astype(LOW)


def attend_back(qkv, bias, context, grad, totals):
    pairs, rows, width = qkv.shape
    return pl.pallas_call(
        attend_back_kernel,
        grid=(pairs,),
        in_specs=[
            pl.BlockSpec((1, rows, width), lambda p: (p, 0, 0)),
            pl.BlockSpec(bias.shape, lambda p: (0, 0)),
            pl.BlockSpec((rows, PAIR), lambda p: (0, p)),
            pl.BlockSpec((rows, PAIR), lambda p: (0, p)),
            pl.BlockSpec((1, 8, rows), lambda p: (p, 0, 0)),
        ],
        out_specs=pl.BlockSpec((1, rows, width), lambda p: (p, 0, 0)),
        out_shape=jax.ShapeDtypeStruct(qkv.shape, LOW),
        scratch_shapes=[
            pltpu.VMEM((8, rows), WIDE),
            pltpu.VMEM((PAIR, rows), LOW),
            pltpu.VMEM((2, rows, PAIR), LOW),
            pltpu.VMEM((2, rows, PAIR), LOW),
            pltpu.VMEM((PAIR, rows), WIDE),
        ],
        compiler_params=pltpu.CompilerParams(vmem_limit_bytes=48 * MIB),
    )(qkv, bias, context, grad, totals)


def place():
    me = lax.axis_index("dp")
    z, y, x = me // 4, (me // 2) % 2, me % 2
    return me, z, y, x


def line_slots(z, depth):
    slots = []
    for step in range(depth - 1):
        slots.append((z - 1 - step, z - 1 - step >= 0, 1))
        slots.append((z + 1 + step, z + 1 + step < depth, -1))
    return slots


def remote(source, target, send, receive, device):
    return pltpu.make_async_remote_copy(
        src_ref=source,
        dst_ref=target,
        send_sem=send,
        recv_sem=receive,
        device_id={"dp": device},
        device_id_type=MESH,
    )


def greet_line(me, z, y, x, depth, extra=()):
    barrier = pltpu.get_barrier_semaphore()
    for peer in (z * 4 + y * 2 + 1 - x, z * 4 + (1 - y) * 2 + x):
        pl.semaphore_signal(barrier, inc=1, device_id={"dp": peer}, device_id_type=MESH)

    @pl.when(z > 0)
    def _():
        pl.semaphore_signal(barrier, inc=1, device_id={"dp": me - 4}, device_id_type=MESH)

    @pl.when(z < depth - 1)
    def _():
        pl.semaphore_signal(barrier, inc=1, device_id={"dp": me + 4}, device_id_type=MESH)

    for peer in extra:
        pl.semaphore_signal(barrier, inc=1, device_id=peer, device_id_type=MESH)
    ends = jnp.where(z > 0, 1, 0) + jnp.where(z < depth - 1, 1, 0)
    pl.semaphore_wait(barrier, 2 + len(extra) + ends)


def other_core(source, target, send, receive):
    return pltpu.make_async_remote_copy(
        src_ref=source,
        dst_ref=target,
        send_sem=send,
        recv_sem=receive,
        device_id={"tensor": 1 - lax.axis_index("tensor")},
        device_id_type=MESH,
    )


class Gather:
    def __init__(self, depth, parts, whole, far, sems):
        self.whole, self.far = whole, far
        self.depth = depth
        self.me, self.z, self.y, self.x = place()
        self.x_peer = self.z * 4 + self.y * 2 + 1 - self.x
        self.y_peer = self.z * 4 + (1 - self.y) * 2 + self.x
        self.rows = whole.shape[1] // parts
        width = whole.shape[2]
        self.third = width // 4
        side = (width - self.third) // 2
        self.a, self.b = (0, side), (side, side)
        self.ab, self.c, self.all = (0, 2 * side), (2 * side, self.third), (0, width)
        (
            self.z_send, self.z_recv, self.zc_send, self.zc_recv, self.xa_send, self.xa_recv, self.yb_send, self.yb_recv,
            self.ya_send, self.ya_recv, self.xb_send, self.xb_recv, self.c_send, self.c_recv, self.far_send, self.far_recv,
        ) = sems
        self.slots = line_slots(self.z, depth)

    @staticmethod
    def semaphores(depth, pieces):
        sem = pltpu.SemaphoreType.DMA
        return [
            *[sem((pieces, depth + 1)), sem((pieces, depth))] * 2,
            *[sem((pieces, depth))] * 4,
            *[sem((pieces, depth, 2))] * 4,
            sem((pieces, 2)),
            sem((pieces, 2)),
            sem((pieces,)),
            sem((pieces,)),
        ]

    def block(self, zb, yb, xb):
        return zb * 4 + yb * 2 + xb

    def cut(self, ref, p, block, count, columns):
        first = pl.multiple_of(block * self.rows, self.rows)
        return ref.at[p, pl.ds(first, count * self.rows), pl.ds(*columns)]

    def copy(self, p, block, count, columns, send, receive, device):
        part = self.cut(self.whole, p, block, count, columns)
        return remote(part, part, send, receive, device)

    def forward(self, p, block, count, columns):
        if p == 0 and columns[0] + columns[1] <= self.c[0]:
            return
        if p == 0:
            columns = self.c
        other_core(
            self.cut(self.whole, p, block, count, columns),
            self.cut(self.far, p, block, count, columns),
            self.far_send.at[p],
            self.far_recv.at[p],
        ).start()

    def far_copy(self, p):
        columns = self.c if p == 0 else self.all
        part = self.far.at[p, :, pl.ds(*columns)]
        return other_core(part, part, self.far_send.at[p], self.far_recv.at[p])

    def z_copy(self, p, zb, way, back=False):
        block = self.block(zb, self.y, self.x)
        sem = self.depth if back else zb
        return self.copy(
            p, block, 1, self.ab, self.z_send.at[p, sem], self.z_recv.at[p, zb], self.me + 4 * way
        )

    def zc_copy(self, p, zb, way, back=False):
        sem = self.depth if back else zb
        return self.copy(
            p, zb * 4, 4, self.c, self.zc_send.at[p, sem], self.zc_recv.at[p, zb], self.me + 4 * way
        )

    def xa(self, p, zb, xb):
        block = self.block(zb, self.y, xb)
        return self.copy(
            p, block, 1, self.a, self.xa_send.at[p, zb], self.xa_recv.at[p, zb], self.x_peer
        )

    def yb(self, p, zb, yb):
        block = self.block(zb, yb, self.x)
        return self.copy(
            p, block, 1, self.b, self.yb_send.at[p, zb], self.yb_recv.at[p, zb], self.y_peer
        )

    def ya(self, p, zb, yb, xb):
        block = self.block(zb, yb, xb)
        return self.copy(
            p, block, 1, self.a, self.ya_send.at[p, zb, xb], self.ya_recv.at[p, zb, xb], self.y_peer
        )

    def xb(self, p, zb, yb, xb):
        block = self.block(zb, yb, xb)
        return self.copy(
            p, block, 1, self.b, self.xb_send.at[p, zb, yb], self.xb_recv.at[p, zb, yb], self.x_peer
        )

    def xc(self, p, xb):
        block = self.block(self.z, self.y, xb)
        return self.copy(
            p, block, 1, self.c, self.c_send.at[p, 0], self.c_recv.at[p, 0], self.x_peer
        )

    def yc(self, p, yb):
        block = self.block(self.z, yb, 0)
        return self.copy(
            p, block, 2, self.c, self.c_send.at[p, 1], self.c_recv.at[p, 1], self.y_peer
        )

    def both_ways(self, copy, act):
        @pl.when(self.z < self.depth - 1)
        def _():
            act(copy(self.z, 1))

        @pl.when(self.z > 0)
        def _():
            act(copy(self.z, -1, True))

    def spread(self, p, zb):
        self.xa(p, zb, self.x).start()
        self.yb(p, zb, self.y).start()
        self.ya(p, zb, self.y, self.x).start()
        self.xb(p, zb, self.y, self.x).start()

    def turn(self, p, zb):
        self.xa(p, zb, 1 - self.x).wait_recv()
        self.ya(p, zb, self.y, 1 - self.x).start()
        self.forward(p, self.block(zb, self.y, 1 - self.x), 1, self.a)
        self.yb(p, zb, 1 - self.y).wait_recv()
        self.xb(p, zb, 1 - self.y, self.x).start()
        self.forward(p, self.block(zb, 1 - self.y, self.x), 1, self.b)

    def at_step(self, step, act):
        for zb, valid, way in self.slots[2 * step : 2 * step + 2]:
            on = (self.z + way >= 0) & (self.z + way < self.depth)
            pl.when(valid)(functools.partial(act, zb, way, on))

    def arrive(self, p, step):
        def act(zb, way, on):
            self.z_copy(p, zb, way).wait_recv()
            pl.when(on)(lambda: self.z_copy(p, zb, way).start())
            self.spread(p, zb)
            self.forward(p, self.block(zb, self.y, self.x), 1, self.ab)

        self.at_step(step, act)

    def arrive_c(self, p, step):
        def act(zb, way, on):
            self.zc_copy(p, zb, way).wait_recv()
            pl.when(on)(lambda: self.zc_copy(p, zb, way).start())
            self.forward(p, zb * 4, 4, self.c)

        self.at_step(step, act)

    def stage(self, p, s):
        depth = self.depth
        if s == 0:
            self.both_ways(lambda *way: self.z_copy(p, *way), lambda copy: copy.start())
            self.xc(p, self.x).start()
            self.spread(p, self.z)
            self.forward(p, self.me, 1, self.all)
            return
        if s == 1:
            self.xc(p, 1 - self.x).wait_recv()
            self.yc(p, self.y).start()
            self.forward(p, self.block(self.z, self.y, 1 - self.x), 1, self.c)
        if s == 2:
            self.yc(p, 1 - self.y).wait_recv()
            self.both_ways(lambda *way: self.zc_copy(p, *way), lambda copy: copy.start())
            self.forward(p, self.block(self.z, 1 - self.y, 0), 2, self.c)
        if 1 <= s < depth:
            self.arrive(p, s - 1)
        if 3 <= s < depth + 2:
            self.arrive_c(p, s - 3)
        if s == 2:
            self.turn(p, self.z)
        if 3 <= s < depth + 2:
            self.at_step(s - 3, lambda zb, way, on: self.turn(p, zb))
        if s == depth + 2:
            for zb in range(depth):
                for other in range(2):
                    self.ya(p, zb, 1 - self.y, other).wait_recv()
                    self.forward(p, self.block(zb, 1 - self.y, other), 1, self.a)
                    self.xb(p, zb, other, 1 - self.x).wait_recv()
                    self.forward(p, self.block(zb, other, 1 - self.x), 1, self.b)

    def finish(self, p):
        def sent(copy):
            copy.wait_send()

        self.far_copy(p).wait_recv()
        self.far_copy(p).wait_send()
        self.both_ways(lambda *way: self.z_copy(p, *way), sent)
        self.both_ways(lambda *way: self.zc_copy(p, *way), sent)
        for zb in range(self.depth):
            self.xa(p, zb, self.x).wait_send()
            self.yb(p, zb, self.y).wait_send()
            for other in range(2):
                self.ya(p, zb, self.y, other).wait_send()
                self.xb(p, zb, other, self.x).wait_send()
        self.xc(p, self.x).wait_send()
        self.yc(p, self.y).wait_send()

        def passed(zb, way, on):
            pl.when(on)(lambda: sent(self.z_copy(p, zb, way)))
            pl.when(on)(lambda: sent(self.zc_copy(p, zb, way)))

        for step in range(self.depth - 1):
            self.at_step(step, passed)


def looped(count, body, between):
    @pl.loop(0, count)
    def _(i):
        body(i)
        for step, acts in between.items():

            @pl.when(i == step)
            def _():
                for act in acts:
                    act()


def front_kernel(
    depth, shards_ref, tokens_ref, cotangent_ref, own_of_ref, dealt_of_ref, bias_ref, score_bias_ref,
    whole_ref, far_ref, qkv_out, hidden_out, turned_ref, upstream_ref, context_ref, total_ref,
    token, upper, hidden, weight, qkv, local_sem, core_sem, *sems,
):
    pieces = whole_ref.shape[0]
    half_rows, width = tokens_ref.shape
    rows = 2 * half_rows
    pairs = qkv.shape[0]
    member = lax.axis_index("tensor")
    lines = Gather(depth, 4 * depth, whole_ref, far_ref, sems)
    me = lines.me

    own = [
        pltpu.make_async_copy(
            shards_ref.at[p], lines.cut(whole_ref, p, me, 1, lines.all), local_sem.at[p]
        )
        for p in range(pieces)
    ]
    own += [
        pltpu.make_async_copy(tokens_ref, token.at[member], local_sem.at[pieces]),
        pltpu.make_async_copy(cotangent_ref, upper.at[member], local_sem.at[pieces + 1]),
    ]
    for copy in own:
        copy.start()
    greet_line(me, lines.z, lines.y, lines.x, depth, [{"tensor": 1 - member}])
    crossing = [
        other_core(tokens_ref, token.at[member], core_sem.at[0, 0], core_sem.at[0, 1]),
        other_core(cotangent_ref, upper.at[member], core_sem.at[1, 0], core_sem.at[1, 1]),
    ]
    for copy in own[:pieces]:
        copy.wait()
    lines.stage(0, 0)
    for copy in crossing:
        copy.start()
    for copy in own[pieces:]:
        copy.wait()

    def picked(index_ref, source, at):
        index = index_ref[at, :]
        total = None
        for which in range(2):
            places = lax.broadcasted_iota(jnp.int32, (TILE, half_rows), 1) + which * half_rows
            chosen = jnp.where(index == places, 1.0, 0.0).astype(LOW)
            part = dot_nn(chosen, source[which])
            total = part if total is None else total + part
        return total

    def tile(step):
        return pl.ds(pl.multiple_of(step * TILE, TILE), TILE)

    def hidden_tile(step):
        rows_here = picked(own_of_ref, token, tile(step))
        hidden[tile(step), :] = rows_here.astype(LOW)
        turned_ref[:, tile(step)] = rows_here.T.astype(LOW)

    def upstream_tile(step):
        upstream_ref[tile(step), :] = picked(dealt_of_ref, upper, tile(step)).astype(LOW)

    crossing[0].wait()
    looped(rows // TILE, hidden_tile, {})
    hidden_copy = pltpu.make_async_copy(hidden, hidden_out, local_sem.at[0])
    hidden_copy.start()
    lines.stage(0, 1)
    crossing[1].wait()
    looped(half_rows // TILE, upstream_tile, {})
    for p, s in ((0, 2), (0, 3), (1, 0), (0, 4), (1, 1), (0, 5), (1, 2), (0, 6)):
        lines.stage(p, s)
    weight_copy = pltpu.make_async_copy(
        whole_ref.at[0, :, pl.ds(0, pairs * 3 * PAIR)], weight, local_sem.at[1]
    )
    weight_copy.start()
    lines.stage(1, 3)
    lines.stage(2, 0)
    weight_copy.wait()

    tall = 2 * TILE

    def project_tile(i):
        pair, step = i // (rows // tall), lax.rem(i, rows // tall)
        at = pl.ds(pl.multiple_of(step * tall, tall), tall)
        columns = pl.ds(pl.multiple_of(pair * 3 * PAIR, PAIR), 3 * PAIR)
        qkv[pair, at, :] = (dot_nn(hidden[at, :], weight[:, columns]) + bias_ref[pair]).astype(LOW)

    looped(pairs * rows // tall, project_tile, {5: [lambda: lines.stage(1, 4)]})
    qkv_copy = pltpu.make_async_copy(qkv, qkv_out, local_sem.at[2])
    qkv_copy.start()

    def attend_step(begin, size):
        def step_of(i):
            pair, step = i // (size // TILE), lax.rem(i, size // TILE)
            columns = pl.ds(pl.multiple_of(pair * PAIR, PAIR), PAIR)
            attend_tile(
                qkv, pair, score_bias_ref, begin, size, step, context_ref, columns, total_ref
            )

        return step_of

    def then(*stages):
        return [functools.partial(lines.stage, *stage) for stage in stages]

    looped(
        pairs * LONGEST // TILE,
        attend_step(0, LONGEST),
        {0: then((2, 1)), 4: then((1, 5)), 8: then((2, 2)), 12: then((1, 6))},
    )
    looped(
        pairs * (rows - LONGEST) // TILE,
        attend_step(LONGEST, rows - LONGEST),
        {0: then((2, 3)), 5: then((2, 4))},
    )
    lines.stage(2, 5)
    lines.stage(2, 6)
    for p in range(pieces):
        lines.finish(p)
    hidden_copy.wait()
    qkv_copy.wait()


def front(shards, tokens, cotangent, own_of, dealt_of, bias, score_bias, parts):
    pieces, shard_rows, columns = shards.shape
    half_rows, width = tokens.shape
    rows, pairs, depth = 2 * half_rows, bias.shape[0], parts // 4
    shape, sem = jax.ShapeDtypeStruct, pltpu.SemaphoreType.DMA
    vmem, anywhere = pl.BlockSpec(memory_space=pltpu.VMEM), pl.BlockSpec(memory_space=pl.ANY)
    return pl.pallas_call(
        functools.partial(front_kernel, depth),
        in_specs=[*[anywhere] * 3, *[vmem] * 4],
        out_specs=[*[anywhere] * 4, *[vmem] * 4],
        out_shape=[
            shape((pieces, parts * shard_rows, columns), LOW),
            shape((pieces, parts * shard_rows, columns), LOW),
            shape((pairs, rows, 3 * PAIR), LOW),
            shape((rows, width), LOW),
            shape((width, rows), LOW),
            shape((half_rows, width), LOW),
            shape((rows, pairs * PAIR), LOW),
            shape((pairs, 8, rows), WIDE),
        ],
        scratch_shapes=[
            pltpu.VMEM((2, half_rows, width), LOW),
            pltpu.VMEM((2, half_rows, width), LOW),
            pltpu.VMEM((rows, width), LOW),
            pltpu.VMEM((width, pairs * 3 * PAIR), LOW),
            pltpu.VMEM((pairs, rows, 3 * PAIR), LOW),
            sem((pieces + 2,)),
            sem((2, 2)),
            *Gather.semaphores(depth, pieces),
        ],
        compiler_params=pltpu.CompilerParams(
            collective_id=0, has_side_effects=True, vmem_limit_bytes=60 * MIB
        ),
    )(shards, tokens, cotangent, own_of[:, None], dealt_of[:, None], bias, score_bias)


def normal_cells(value):
    bell = jnp.exp(value * value * -0.5)
    t = 1.0 / (1.0 + 0.39 * 0.7071067811865476 * jnp.abs(value))
    tail = -0.2275377237624147
    for factor in (
        0.8866668177122106,
        -0.6354042576077721,
        0.649562611731642,
        0.0913871257655044,
        0.23532542445435511,
    ):
        tail = tail * t + factor
    tail = 0.5 * tail * t * bell
    return jnp.where(value < 0.0, tail, 1.0 - tail), bell


def norm(values):
    center = values - jnp.mean(values, axis=1, keepdims=True)
    spread = jnp.mean(center * center, axis=1, keepdims=True)
    scale = lax.rsqrt(spread + norm_epsilon)
    return center * scale, scale


def norm_back(scaled, unit, scale):
    return scale * (
        scaled
        - jnp.mean(scaled, axis=1, keepdims=True)
        - unit * jnp.mean(scaled * unit, axis=1, keepdims=True)
    )


def middle_kernel(
    context_ref, merge_ref, merge_far_ref, whole_ref, far_ref, hidden_ref, vectors_ref, bias_ref,
    acc, normal, inverse, turned, active, slope, far_ctx,
    own_ctx, low, expand_buf, reduce_buf, ctx_sem, load_sem,
):
    rows = hidden_ref.shape[0]
    chunks, _, both = bias_ref.shape
    half = both // 2
    per_piece = whole_ref.shape[2] // (2 * half)
    member = lax.axis_index("tensor")
    peer = {"tensor": 1 - member}
    tall, short = 256, 128

    def across(source, target, send, receive):
        return pltpu.make_async_remote_copy(
            src_ref=source,
            dst_ref=target,
            send_sem=send,
            recv_sem=receive,
            device_id=peer,
            device_id_type=MESH,
        )

    def rows_of(which):
        return pl.ds(pl.multiple_of(which * rows, rows), rows)

    def tile(step, size):
        return pl.ds(pl.multiple_of(step * size, size), size)

    def loads(j, slot):
        piece, at = 1 + j // per_piece, lax.rem(j, per_piece) * half
        copies = []
        for kind, buf in enumerate((expand_buf, reduce_buf)):
            first = pl.multiple_of(at + kind * per_piece * half, half)
            for side, source in enumerate((far_ref, whole_ref)):
                copies.append(
                    pltpu.make_async_copy(
                        source.at[piece, :, pl.ds(first, half)],
                        buf.at[slot, :, pl.ds(side * half, half)],
                        load_sem.at[slot, kind, side],
                    )
                )
        return copies

    for copy in loads(0, 0):
        copy.start()
    barrier = pltpu.get_barrier_semaphore()
    pl.semaphore_signal(barrier, inc=1, device_id=peer, device_id_type=MESH)
    pl.semaphore_wait(barrier, 1)
    out_ctx = across(context_ref.at[rows_of(1 - member)], far_ctx, ctx_sem.at[0], ctx_sem.at[1])
    out_ctx.start()
    in_ctx = pltpu.make_async_copy(context_ref.at[rows_of(member)], own_ctx, ctx_sem.at[2])
    in_ctx.start()
    in_ctx.wait()
    out_ctx.wait()

    @pl.loop(0, rows // short)
    def _(step):
        at = tile(step, short)
        branch = dot_nt(own_ctx[at, :], merge_ref[...]) + dot_nt(far_ctx[at, :], merge_far_ref[...])
        unit, scale = norm(hidden_ref[at, :].astype(WIDE) + branch + vectors_ref[2:3, :])
        normed = unit * vectors_ref[3:4, :] + vectors_ref[4:5, :]
        normal[at, :] = unit
        inverse[at, :] = jnp.broadcast_to(scale, (short, 128))
        low[at, :] = normed.astype(LOW)
        turned[:, at] = normed.T.astype(LOW)
        acc[at, :] = normed + vectors_ref[5:6, :]

    @pl.loop(0, chunks)
    def _(j):
        slot = lax.rem(j, 2)
        for copy in loads(j, slot):
            copy.wait()

        @pl.when(j + 1 < chunks)
        def _():
            for copy in loads(j + 1, 1 - slot):
                copy.start()

        for step in range(rows // tall):
            at = slice(step * tall, (step + 1) * tall)
            inner = dot_nn(low[at, :], expand_buf[slot]) + bias_ref[j]
            below, bell = normal_cells(inner)
            held = (inner * below).astype(LOW)
            active[j, at, :] = held
            slope[j, at, :] = (below + inner * bell * 0.3989422804014327).astype(LOW)
            acc[at, :] += dot_nt(held, reduce_buf[slot])


def middle_block(context, whole, far, hidden_own, vectors, bias_own, bias_far):
    total_rows, inner = context.shape
    rows, width = hidden_own.shape
    merge, merge_far = whole[0, :, -inner:], far[0, :, -inner:]
    half = 256
    chunks = bias_own.shape[0] // half
    both = 2 * half
    bias = jnp.concatenate(
        [bias_far.reshape(chunks, 1, half), bias_own.reshape(chunks, 1, half)], axis=2
    )
    vmem, anywhere = pl.BlockSpec(memory_space=pltpu.VMEM), pl.BlockSpec(memory_space=pl.ANY)
    sem = pltpu.SemaphoreType.DMA
    shape = jax.ShapeDtypeStruct
    return pl.pallas_call(
        middle_kernel,
        in_specs=[anywhere, vmem, vmem, anywhere, anywhere, vmem, vmem, vmem],
        out_specs=[vmem] * 7,
        out_shape=[
            shape((rows, width), WIDE),
            shape((rows, width), WIDE),
            shape((rows, 128), WIDE),
            shape((width, rows), LOW),
            shape((chunks, rows, both), LOW),
            shape((chunks, rows, both), LOW),
            shape((rows, inner), LOW),
        ],
        scratch_shapes=[
            pltpu.VMEM((rows, inner), LOW),
            pltpu.VMEM((rows, width), LOW),
            pltpu.VMEM((2, width, both), LOW),
            pltpu.VMEM((2, width, both), LOW),
            sem((3,)),
            sem((2, 2, 2)),
        ],
        compiler_params=pltpu.CompilerParams(
            collective_id=3, has_side_effects=True, vmem_limit_bytes=60 * MIB
        ),
    )(context, merge, merge_far, whole, far, hidden_own, vectors, bias)


def feed_kernel(
    context_ref, merge_ref, merge_far_ref, whole_ref, far_ref, hidden_ref, upstream_ref, vectors_ref, bias_ref,
    encoded_ref, branch_ref, grad_ref, merge_grad_ref, expand_grad_ref, reduce_grad_ref, sums_ref, hidden_sums_ref,
    own_ctx, far_ctx, acc, normal, inverse, low, turned, late, late_turned, active, slope, inner_grad,
    expand_buf, reduce_buf, arrived, leaving, kept, done, grad_own, grad_far, merge_send, merge_recv,
    ctx_sem, load_sem, send_sem, recv_sem, out_sem, last_sem,
):
    rows = hidden_ref.shape[0]
    chunks, _, both = bias_ref.shape
    half = both // 2
    per_piece = whole_ref.shape[2] // (2 * half)
    member = lax.axis_index("tensor")
    peer = {"tensor": 1 - member}
    tall, short = 256, 128
    width = hidden_ref.shape[1]

    def across(source, target, send, receive):
        return pltpu.make_async_remote_copy(
            src_ref=source,
            dst_ref=target,
            send_sem=send,
            recv_sem=receive,
            device_id=peer,
            device_id_type=MESH,
        )

    def rows_of(which):
        return pl.ds(pl.multiple_of(which * rows, rows), rows)

    def tile(step, size):
        return pl.ds(pl.multiple_of(step * size, size), size)

    def loads(j, slot):
        piece, at = 1 + j // per_piece, lax.rem(j, per_piece) * half
        copies = []
        for kind, buf in enumerate((expand_buf, reduce_buf)):
            first = pl.multiple_of(at + kind * per_piece * half, half)
            for side, source in enumerate((far_ref, whole_ref)):
                copies.append(
                    pltpu.make_async_copy(
                        source.at[piece, :, pl.ds(first, half)],
                        buf.at[slot, :, pl.ds(side * half, half)],
                        load_sem.at[slot, kind, side],
                    )
                )
        return copies

    for copy in loads(0, 0):
        copy.start()
    barrier = pltpu.get_barrier_semaphore()
    pl.semaphore_signal(barrier, inc=1, device_id=peer, device_id_type=MESH)
    pl.semaphore_wait(barrier, 1)
    out_ctx = across(context_ref.at[rows_of(1 - member)], far_ctx, ctx_sem.at[0], ctx_sem.at[1])
    out_ctx.start()
    in_ctx = pltpu.make_async_copy(context_ref.at[rows_of(member)], own_ctx, ctx_sem.at[2])
    in_ctx.start()
    sums_ref[...] = jnp.zeros_like(sums_ref)
    in_ctx.wait()
    out_ctx.wait()

    def add_sum(row, values):
        sums_ref[row : row + 1, :] += jnp.sum(values, axis=0, keepdims=True)

    @pl.loop(0, rows // short)
    def _(step):
        at = tile(step, short)
        branch = dot_nt(own_ctx[at, :], merge_ref[...]) + dot_nt(far_ctx[at, :], merge_far_ref[...])
        unit, scale = norm(hidden_ref[at, :].astype(WIDE) + branch + vectors_ref[2:3, :])
        normed = unit * vectors_ref[3:4, :] + vectors_ref[4:5, :]
        normal[at, :] = unit
        inverse[at, :] = jnp.broadcast_to(scale, (short, 128))
        low[at, :] = normed.astype(LOW)
        turned[:, at] = normed.T.astype(LOW)
        acc[at, :] = normed + vectors_ref[5:6, :]

    @pl.loop(0, chunks)
    def _(j):
        slot = lax.rem(j, 2)
        for copy in loads(j, slot):
            copy.wait()

        @pl.when(j + 1 < chunks)
        def _():
            for copy in loads(j + 1, 1 - slot):
                copy.start()

        for step in range(rows // tall):
            at = slice(step * tall, (step + 1) * tall)
            inner = dot_nn(low[at, :], expand_buf[slot]) + bias_ref[j]
            below, bell = normal_cells(inner)
            held = (inner * below).astype(LOW)
            active[j, at, :] = held
            slope[j, at, :] = (below + inner * bell * 0.3989422804014327).astype(LOW)
            acc[at, :] += dot_nt(held, reduce_buf[slot])

    for copy in loads(0, 0):
        copy.start()

    @pl.loop(0, rows // short)
    def _(step):
        at = tile(step, short)
        unit, scale = norm(acc[at, :])
        encoded_ref[at, :] = (unit * vectors_ref[6:7, :] + vectors_ref[7:8, :]).astype(LOW)
        upper = upstream_ref[at, :].astype(WIDE)
        add_sum(6, upper * unit)
        add_sum(7, upper)
        grad = norm_back(upper * vectors_ref[6:7, :], unit, scale)
        grad_low = grad.astype(LOW)
        add_sum(5, grad_low.astype(WIDE))
        acc[at, :] = grad
        late[at, :] = grad_low
        late_turned[:, at] = grad.T.astype(LOW)

    def send(j, kind):
        return across(
            leaving.at[lax.rem(j, 2), kind],
            arrived.at[lax.rem(j, 4), kind],
            send_sem.at[lax.rem(j, 2), kind],
            recv_sem.at[lax.rem(j, 4), kind],
        )

    def store(j, kind):
        target = (expand_grad_ref, reduce_grad_ref)[kind]
        cols = pl.ds(pl.multiple_of(j * half, half), half)
        return pltpu.make_async_copy(
            done.at[lax.rem(j, 2), kind], target.at[:, cols], out_sem.at[lax.rem(j, 2), kind]
        )

    def finish(j):
        for kind in range(2):
            send(j, kind).wait_recv()

            @pl.when(j >= 2)
            def _():
                store(j - 2, kind).wait()

            @pl.loop(0, width // tall)
            def _(step):
                at = tile(step, tall)
                done[lax.rem(j, 2), kind, at, :] = (
                    kept[lax.rem(j, 2), kind, at, :]
                    + arrived[lax.rem(j, 4), kind, at, :].astype(WIDE)
                ).astype(LOW)

            store(j, kind).start()

    @pl.loop(0, chunks)
    def _(j):
        slot = lax.rem(j, 2)
        for copy in loads(j, slot):
            copy.wait()

        @pl.when(j + 1 < chunks)
        def _():
            for copy in loads(j + 1, 1 - slot):
                copy.start()

        total = jnp.zeros((1, both), WIDE)
        for step in range(rows // tall):
            at = slice(step * tall, (step + 1) * tall)
            grad = dot_nn(late[at, :], reduce_buf[slot]) * slope[j, at, :].astype(WIDE)
            grad = grad.astype(LOW)
            inner_grad[at, :] = grad
            total = total + jnp.sum(grad.astype(WIDE), axis=0, keepdims=True)
            acc[at, :] += dot_nt(grad, expand_buf[slot])
        hidden_sums_ref[j] = total

        @pl.when(j >= 2)
        def _():
            for kind in range(2):
                send(j - 2, kind).wait_send()

        for kind, (left, right) in enumerate(((turned, inner_grad), (late_turned, active.at[j]))):
            for step in range(width // tall):
                at = slice(step * tall, (step + 1) * tall)
                part = dot_nn(left[at, :], right[...])
                leaving[slot, kind, at, :] = part[:, 0:half].astype(LOW)
                kept[slot, kind, at, :] = part[:, half:both]
            send(j, kind).start()

        @pl.when(j >= 1)
        def _():
            finish(j - 1)

    @pl.loop(0, rows // short)
    def _(step):
        at = tile(step, short)
        grad = acc[at, :]
        unit = normal[at, :]
        add_sum(3, grad * unit)
        add_sum(4, grad)
        branch_grad = norm_back(grad * vectors_ref[3:4, :], unit, inverse[at, 0:1])
        branch_low = branch_grad.astype(LOW)
        add_sum(2, branch_low.astype(WIDE))
        branch_ref[at, :] = branch_grad
        turned[:, at] = branch_grad.T.astype(LOW)
        grad_far[at, :] = dot_nn(branch_low, merge_far_ref[...]).astype(LOW)
        grad_own[at, :] = dot_nn(branch_low, merge_ref[...]).astype(LOW)

    out_grad = across(grad_far, grad_ref.at[rows_of(member)], ctx_sem.at[0], ctx_sem.at[1])
    out_grad.start()
    in_grad = pltpu.make_async_copy(grad_own, grad_ref.at[rows_of(member)], ctx_sem.at[2])
    in_grad.start()
    for step in range(width // tall):
        at = slice(step * tall, (step + 1) * tall)
        merge_send[at, :] = dot_nn(turned[at, :], far_ctx[...]).astype(LOW)
    out_merge = across(merge_send, merge_recv, last_sem.at[0], last_sem.at[1])
    out_merge.start()
    finish(chunks - 1)
    for kind in range(2):
        send(chunks - 2, kind).wait_send()
        send(chunks - 1, kind).wait_send()
        store(chunks - 2, kind).wait()
        store(chunks - 1, kind).wait()
    out_merge.wait()
    for step in range(width // tall):
        at = slice(step * tall, (step + 1) * tall)
        merge_grad_ref[at, :] = (
            dot_nn(turned[at, :], own_ctx[...]) + merge_recv[at, :].astype(WIDE)
        ).astype(LOW)
    out_grad.wait()
    in_grad.wait()


def feed_block(context, whole, far, hidden_own, upstream, vectors, bias_own, bias_far):
    total_rows, inner = context.shape
    rows, width = hidden_own.shape
    hidden = bias_own.shape[0]
    merge, merge_far = whole[0, :, -inner:], far[0, :, -inner:]
    half = 256
    chunks = hidden // half
    both = 2 * half
    bias = jnp.concatenate(
        [bias_far.reshape(chunks, 1, half), bias_own.reshape(chunks, 1, half)], axis=2
    )
    vmem, anywhere = pl.BlockSpec(memory_space=pltpu.VMEM), pl.BlockSpec(memory_space=pl.ANY)
    sem = pltpu.SemaphoreType.DMA
    shape = jax.ShapeDtypeStruct
    *results, hidden_sums = pl.pallas_call(
        feed_kernel,
        in_specs=[anywhere, vmem, vmem, *[anywhere] * 2, *[vmem] * 4],
        out_specs=[vmem, vmem, anywhere, vmem, anywhere, anywhere, vmem, vmem],
        out_shape=[
            shape((rows, width), LOW),
            shape((rows, width), WIDE),
            shape((total_rows, inner), LOW),
            shape((width, inner), LOW),
            shape((width, hidden), LOW),
            shape((width, hidden), LOW),
            shape((8, width), WIDE),
            shape((chunks, 1, both), WIDE),
        ],
        scratch_shapes=[
            pltpu.VMEM((rows, inner), LOW),
            pltpu.VMEM((rows, inner), LOW),
            pltpu.VMEM((rows, width), WIDE),
            pltpu.VMEM((rows, width), WIDE),
            pltpu.VMEM((rows, 128), WIDE),
            pltpu.VMEM((rows, width), LOW),
            pltpu.VMEM((width, rows), LOW),
            pltpu.VMEM((rows, width), LOW),
            pltpu.VMEM((width, rows), LOW),
            pltpu.VMEM((chunks, rows, both), LOW),
            pltpu.VMEM((chunks, rows, both), LOW),
            pltpu.VMEM((rows, both), LOW),
            pltpu.VMEM((2, width, both), LOW),
            pltpu.VMEM((2, width, both), LOW),
            pltpu.VMEM((4, 2, width, half), LOW),
            pltpu.VMEM((2, 2, width, half), LOW),
            pltpu.VMEM((2, 2, width, half), WIDE),
            pltpu.VMEM((2, 2, width, half), LOW),
            pltpu.VMEM((rows, inner), LOW),
            pltpu.VMEM((rows, inner), LOW),
            pltpu.VMEM((width, inner), LOW),
            pltpu.VMEM((width, inner), LOW),
            sem((3,)),
            sem((2, 2, 2)),
            sem((2, 2)),
            sem((4, 2)),
            sem((2, 2)),
            sem((2,)),
        ],
        compiler_params=pltpu.CompilerParams(
            collective_id=2, has_side_effects=True, vmem_limit_bytes=60 * MIB
        ),
        cost_estimate=pl.CostEstimate(
            flops=12 * rows * width * 2 * hidden, bytes_accessed=8 * width * hidden * 4, transcendentals=0
        ),
    )(context, merge, merge_far, whole, far, hidden_own, upstream, vectors, bias)
    hidden_far = hidden_sums[:, 0, :half].reshape(-1)
    hidden_near = hidden_sums[:, 0, half:].reshape(-1)
    return (*results, hidden_near, hidden_far)


class Scatter:
    buffers = 8

    def __init__(self, depth, grads, shards, buffers, sems):
        self.depth, self.grads, self.shards = depth, grads, shards
        self.held = [buffers[8 * p : 8 * p + 8] for p in range(len(grads))]
        self.me, self.z, self.y, self.x = place()
        self.x_peer = self.z * 4 + self.y * 2 + 1 - self.x
        self.y_peer = self.z * 4 + (1 - self.y) * 2 + self.x
        self.rows = grads[0].shape[0] // (4 * depth)
        (
            self.a1_send, self.a1_recv, self.a2_send, self.a2_recv, self.b2_send, self.b2_recv, self.b1_send, self.b1_recv,
            self.z_send, self.z_recv, self.zc_send, self.zc_recv, self.c_send, self.c_recv,
        ) = sems

    @staticmethod
    def scratch(depth, rows, classes):
        found = []
        for a, b, c in classes:
            found += [
                pltpu.VMEM((depth, 2 * rows, a), LOW),
                pltpu.VMEM((depth, 2, rows, b), LOW),
                pltpu.VMEM((depth, rows, a), LOW),
                pltpu.VMEM((depth, rows, b), LOW),
                pltpu.VMEM((depth + 1, rows, a + b), LOW),
                pltpu.VMEM((depth + 1, 4 * rows, c), LOW),
                pltpu.VMEM((2 * rows, c), LOW),
                pltpu.VMEM((rows, c), LOW),
            ]
        return found

    @staticmethod
    def semaphores(depth, pieces):
        sem = pltpu.SemaphoreType.DMA
        return [
            *[sem((pieces, depth))] * 6,
            *[sem((pieces, depth, 2))] * 2,
            *[sem((pieces, depth)), sem((pieces, depth + 1))] * 2,
            sem((pieces, 2)),
            sem((pieces, 2)),
        ]

    def columns(self, p):
        a, b, c = (self.held[p][i].shape[-1] for i in (0, 1, 5))
        return pl.ds(0, a), pl.ds(a, b), pl.ds(a + b, c)

    def block(self, zb, yb, xb):
        return zb * 4 + yb * 2 + xb

    def span(self, block, count=1):
        return pl.ds(pl.multiple_of(block * self.rows, self.rows), count * self.rows)

    def add(self, count, put, *terms):
        @pl.loop(0, count // 16)
        def _(step):
            at = pl.multiple_of(step * 16, 16)
            total = terms[0](at)
            for term in terms[1:]:
                total = total + term(at)
            put(at, total)

    def a1(self, p, zb):
        return remote(
            self.grads[p].at[self.span(self.block(zb, 1 - self.y, 0), 2), self.columns(p)[0]],
            self.held[p][0].at[zb],
            self.a1_send.at[p, zb],
            self.a1_recv.at[p, zb],
            self.y_peer,
        )

    def b1(self, p, zb, yb):
        return remote(
            self.grads[p].at[self.span(self.block(zb, yb, 1 - self.x)), self.columns(p)[1]],
            self.held[p][1].at[zb, yb],
            self.b1_send.at[p, zb, yb],
            self.b1_recv.at[p, zb, yb],
            self.x_peer,
        )

    def a2(self, p, zb):
        return remote(
            self.held[p][0].at[zb, self.span(1 - self.x)],
            self.held[p][2].at[zb],
            self.a2_send.at[p, zb],
            self.a2_recv.at[p, zb],
            self.x_peer,
        )

    def b2(self, p, zb):
        return remote(
            self.held[p][1].at[zb, 1 - self.y],
            self.held[p][3].at[zb],
            self.b2_send.at[p, zb],
            self.b2_recv.at[p, zb],
            self.y_peer,
        )

    def slot(self, zb, way):
        return zb if way > 0 else zb + (self.depth - zb) * jnp.where(zb == self.z - 1, 1, 0)

    def z_copy(self, p, zb, way):
        slot = self.slot(zb, way)
        return remote(
            self.held[p][4].at[zb],
            self.held[p][4].at[slot],
            self.z_send.at[p, zb],
            self.z_recv.at[p, slot],
            self.me + 4 * way,
        )

    def zc_copy(self, p, zb, way, first):
        slot = self.slot(zb, way)
        source = self.held[p][5].at[zb]
        if first:
            source = self.grads[p].at[self.span(zb * 4, 4), self.columns(p)[2]]
        return remote(
            source,
            self.held[p][5].at[slot],
            self.zc_send.at[p, zb],
            self.zc_recv.at[p, slot],
            self.me + 4 * way,
        )

    def arrived(self, ref, sem, slot):
        part = ref.at[slot]
        remote(part, part, sem, sem, self.me).wait_recv()

    def cy(self, p):
        return remote(
            self.held[p][5].at[self.z, self.span(2 * (1 - self.y), 2)],
            self.held[p][6],
            self.c_send.at[p, 0],
            self.c_recv.at[p, 0],
            self.y_peer,
        )

    def cx(self, p):
        return remote(
            self.held[p][5].at[self.z, self.span(2 * self.y + 1 - self.x)],
            self.held[p][7],
            self.c_send.at[p, 1],
            self.c_recv.at[p, 1],
            self.x_peer,
        )

    def grad(self, p, block, columns):
        def term(at):
            first = pl.multiple_of(block * self.rows + at, 16)
            return self.grads[p][pl.ds(first, 16), columns].astype(WIDE)

        return term

    def part(self, ref, lead, block, columns=None):
        columns = slice(None) if columns is None else columns

        def term(at):
            first = pl.multiple_of(block * self.rows + at, 16)
            return ref[(*lead, pl.ds(first, 16), columns)].astype(WIDE)

        return term

    def put(self, ref, lead, block, columns=None):
        columns = slice(None) if columns is None else columns

        def act(at, total):
            first = pl.multiple_of(block * self.rows + at, 16)
            ref[(*lead, pl.ds(first, 16), columns)] = total.astype(ref.dtype)

        return act

    def open(self, p, zb):
        self.a1(p, zb).start()
        self.b1(p, zb, 0).start()
        self.b1(p, zb, 1).start()

    def first(self, p, zb):
        z, y, x = self.z, self.y, self.x
        a, b, _ = self.columns(p)
        r1a, r1b = self.held[p][0], self.held[p][1]
        self.a1(p, zb).wait_recv()
        self.add(
            self.rows,
            self.put(r1a, (zb,), 1 - x),
            self.part(r1a, (zb,), 1 - x),
            self.grad(p, self.block(zb, y, 1 - x), a),
        )
        self.a2(p, zb).start()
        self.b1(p, zb, 0).wait_recv()
        self.b1(p, zb, 1).wait_recv()
        self.add(
            self.rows,
            self.put(r1b, (zb, 1 - y), 0),
            self.part(r1b, (zb, 1 - y), 0),
            self.grad(p, self.block(zb, 1 - y, x), b),
        )
        self.b2(p, zb).start()

    def terms(self, p, zb):
        z, y, x = self.z, self.y, self.x
        a, b, _ = self.columns(p)
        r1a, r1b, r2a, r2b = self.held[p][:4]
        own = self.block(zb, y, x)
        return (
            [self.grad(p, own, a), self.part(r1a, (zb,), x), self.part(r2a, (zb,), 0)],
            [self.grad(p, own, b), self.part(r1b, (zb, y), 0), self.part(r2b, (zb,), 0)],
        )

    def pass_on(self, p, zb, way):
        a, b, _ = self.columns(p)
        rz = self.held[p][4]
        self.a2(p, zb).wait_recv()
        self.b2(p, zb).wait_recv()
        from_line = (self.z - way >= 0) & (self.z - way < self.depth)

        @pl.when(from_line)
        def _():
            self.arrived(rz, self.z_recv.at[p, zb], zb)
            for terms, columns in zip(self.terms(p, zb), (a, b), strict=True):
                self.add(
                    self.rows,
                    self.put(rz, (zb,), 0, columns),
                    *terms,
                    self.part(rz, (zb,), 0, columns),
                )

        @pl.when(jnp.logical_not(from_line))
        def _():
            for terms, columns in zip(self.terms(p, zb), (a, b), strict=True):
                self.add(self.rows, self.put(rz, (zb,), 0, columns), *terms)

        self.z_copy(p, zb, way).start()

    def pass_c(self, p, zb, way):
        c = self.columns(p)[2]
        rc = self.held[p][5]
        from_line = (self.z - way >= 0) & (self.z - way < self.depth)

        @pl.when(from_line)
        def _():
            self.arrived(rc, self.zc_recv.at[p, zb], zb)
            self.add(
                4 * self.rows,
                self.put(rc, (zb,), 0),
                self.part(rc, (zb,), 0),
                self.grad(p, zb * 4, c),
            )
            self.zc_copy(p, zb, way, False).start()

        @pl.when(jnp.logical_not(from_line))
        def _():
            self.zc_copy(p, zb, way, True).start()

    def own_c(self, p):
        z, depth = self.z, self.depth
        c = self.columns(p)[2]
        rc = self.held[p][5]
        grad = self.grad(p, z * 4, c)
        lower, upper = self.part(rc, (z,), 0), self.part(rc, (depth,), 0)
        put = self.put(rc, (z,), 0)

        @pl.when(z > 0)
        def _():
            self.arrived(rc, self.zc_recv.at[p, z], z)

        @pl.when(z < depth - 1)
        def _():
            self.arrived(rc, self.zc_recv.at[p, depth], depth)

        @pl.when((z > 0) & (z < depth - 1))
        def _():
            self.add(4 * self.rows, put, grad, lower, upper)

        @pl.when(z == 0)
        def _():
            self.add(4 * self.rows, put, grad, upper)

        @pl.when(z == depth - 1)
        def _():
            self.add(4 * self.rows, put, grad, lower)

        self.cy(p).start()

    def turn_c(self, p):
        rc, rcy = self.held[p][5], self.held[p][6]
        self.cy(p).wait_recv()
        self.add(
            2 * self.rows,
            self.put(rc, (self.z,), 2 * self.y),
            self.part(rc, (self.z,), 2 * self.y),
            self.part(rcy, (), 0),
        )
        self.cx(p).start()

    def close(self, p):
        z, depth = self.z, self.depth
        a, b, c = self.columns(p)
        rz, rc, rcx = self.held[p][4], self.held[p][5], self.held[p][7]
        self.a2(p, z).wait_recv()
        self.b2(p, z).wait_recv()

        @pl.when(z > 0)
        def _():
            self.arrived(rz, self.z_recv.at[p, z], z)

        @pl.when(z < depth - 1)
        def _():
            self.arrived(rz, self.z_recv.at[p, depth], depth)

        def total(*slots):
            for terms, columns in zip(self.terms(p, z), (a, b), strict=True):
                lines = [self.part(rz, (slot,), 0, columns) for slot in slots]
                self.add(self.rows, self.put(self.shards[p], (), 0, columns), *terms, *lines)

        pl.when((z > 0) & (z < depth - 1))(lambda: total(z, depth))
        pl.when(z == 0)(lambda: total(depth))
        pl.when(z == depth - 1)(lambda: total(z))
        self.cx(p).wait_recv()
        self.add(
            self.rows,
            self.put(self.shards[p], (), 0, c),
            self.part(rc, (z,), 2 * self.y + self.x),
            self.part(rcx, (), 0),
        )

    def at_step(self, step, act):
        z, depth = self.z, self.depth
        if step < 0:
            act(z, 0)
            return
        for zb, valid, way in (
            (z + 1 + step, z + 1 + step < depth, 1),
            (z - 1 - step, z - 1 - step >= 0, -1),
        ):
            pl.when(valid)(functools.partial(act, zb, way))

    def stage(self, p, s):
        last = self.depth - 2

        def opened(step):
            self.at_step(step, lambda zb, way: self.open(p, zb))

        def added(step):
            self.at_step(step, lambda zb, way: self.first(p, zb))

        def passed(step):
            self.at_step(step, lambda zb, way: self.pass_on(p, zb, way))

        def passed_c(step):
            self.at_step(step, lambda zb, way: self.pass_c(p, zb, way))

        if s == 0:
            opened(last)
            opened(last - 1)
            passed_c(last)
            return
        if s <= last + 2:
            added(last + 1 - s)
        if last - 1 - s >= -1:
            opened(last - 1 - s)
        if last - s >= 0:
            passed_c(last - s)
        if s >= 2 and last + 2 - s >= 0:
            passed(last + 2 - s)
        if s == last + 1:
            self.own_c(p)
        if s == last + 2:
            self.turn_c(p)
        if s == last + 3:
            self.close(p)

    def sent(self, p):
        def line(zb, way):
            from_line = (self.z - way >= 0) & (self.z - way < self.depth)
            self.z_copy(p, zb, way).wait_send()
            pl.when(from_line)(lambda: self.zc_copy(p, zb, way, False).wait_send())
            pl.when(jnp.logical_not(from_line))(lambda: self.zc_copy(p, zb, way, True).wait_send())

        for zb in range(self.depth):
            self.a1(p, zb).wait_send()
            self.b1(p, zb, 0).wait_send()
            self.b1(p, zb, 1).wait_send()
            self.a2(p, zb).wait_send()
            self.b2(p, zb).wait_send()
        for step in range(self.depth - 1):
            self.at_step(step, line)
        self.cy(p).wait_send()
        self.cx(p).wait_send()


class SmallSum:
    def __init__(self, lines, buffer, send, recv):
        member = lax.axis_index("tensor")
        self.partners = [{"tensor": 1 - member}, {"dp": lines.x_peer}, {"dp": lines.y_peer}]
        for level in range(lines.depth.bit_length() - 1):
            reach = 1 << level
            way = 1 - 2 * ((lines.z // reach) % 2)
            self.partners.append({"dp": lines.me + 4 * reach * way})
        self.buffer, self.send, self.recv = buffer, send, recv

    def copy(self, step):
        return pltpu.make_async_remote_copy(
            src_ref=self.buffer.at[step],
            dst_ref=self.buffer.at[len(self.partners) + 1 + step],
            send_sem=self.send.at[step],
            recv_sem=self.recv.at[step],
            device_id=self.partners[step],
            device_id_type=MESH,
        )

    def step(self, step):
        if step:
            self.copy(step - 1).wait_recv()
            self.buffer[step] = self.buffer[step - 1] + self.buffer[len(self.partners) + step]
        if step < len(self.partners):
            self.copy(step).start()

    def sent(self):
        for step in range(len(self.partners)):
            self.copy(step).wait_send()


def back_kernel(
    depth, acc_in, turned_in, upstream_in, normal_in, inverse_in, active_in, slope_in, far_ctx_in, context_in, qkv_in,
    totals_in, hidden_turned_in, whole_ref, far_ref, vectors_ref, score_bias_in, from_own_in, from_dealt_in,
    encoded_ref, input_ref, shard0, shard1, shard2, shard3, small_ref, enc_pair, grad_ref, input_far,
    acc, arrived, merge_recv, small, grad0, grad1, grad2, grad3, *rest,
):
    buffers, rest = rest[: 4 * Scatter.buffers], rest[4 * Scatter.buffers :]
    small_send, small_recv, in_sem, load_sem, ctx_sem, far_send, far_recv, merge_sem, enc_sem, input_sem, *sems = rest
    grads = (grad0, grad1, grad2, grad3)
    lines = Scatter(depth, grads, (shard0, shard1, shard2, shard3), buffers, sems)
    sums = SmallSum(lines, small, small_send, small_recv)
    member = lax.axis_index("tensor")
    rows, width = acc.shape
    total_rows = 2 * rows
    chunks, _, both = active_in.shape
    half = both // 2
    per_piece = chunks // 2
    pairs = qkv_in.shape[0]
    inner = pairs * PAIR
    tall, short = 256, 128

    def rows_of(which):
        return pl.ds(pl.multiple_of(which * rows, rows), rows)

    def tile(step, size):
        return pl.ds(pl.multiple_of(step * size, size), size)

    def fetch(source, target, sem):
        return pltpu.make_async_copy(source, target, in_sem.at[sem])

    def stage(p, s):
        return functools.partial(lines.stage, p, s)

    def add_sum(row, values):
        small[0, row : row + 1, :] += jnp.sum(values, axis=0, keepdims=True)

    acc_copy = fetch(acc_in, acc, 0)
    acc_copy.start()
    greet_line(
        lines.me, lines.z, lines.y, lines.x, depth, [sums.partners[0], *sums.partners[3:]]
    )
    small[0] = jnp.zeros(small.shape[1:], WIDE)

    def feed_phase(late, late_turned, turned, upstream, active, slope, inner_grad, expand_buf, reduce_buf, leaving, encoded):
        def loads(j, slot):
            piece, at = 1 + j // per_piece, lax.rem(j, per_piece) * half
            copies = [
                pltpu.make_async_copy(active_in.at[j], active.at[slot], load_sem.at[slot, 4]),
                pltpu.make_async_copy(slope_in.at[j], slope.at[slot], load_sem.at[slot, 5]),
            ]
            for kind, buf in enumerate((expand_buf, reduce_buf)):
                first = pl.multiple_of(at + kind * per_piece * half, half)
                for side, source in enumerate((far_ref, whole_ref)):
                    copies.append(
                        pltpu.make_async_copy(
                            source.at[piece, :, pl.ds(first, half)],
                            buf.at[slot, :, pl.ds(side * half, half)],
                            load_sem.at[slot, 2 * kind + side],
                        )
                    )
            return copies

        fetches = [fetch(upstream_in, upstream, 1), fetch(turned_in, turned, 2)]
        for copy in fetches:
            copy.start()
        for copy in loads(0, 0):
            copy.start()
        acc_copy.wait()
        for copy in fetches:
            copy.wait()

        @pl.loop(0, rows // short)
        def _(step):
            at = tile(step, short)
            unit, scale = norm(acc[at, :])
            encoded[at, :] = (unit * vectors_ref[6:7, :] + vectors_ref[7:8, :]).astype(LOW)
            upper = upstream[at, :].astype(WIDE)
            add_sum(6, upper * unit)
            add_sum(7, upper)
            grad = norm_back(upper * vectors_ref[6:7, :], unit, scale)
            grad_low = grad.astype(LOW)
            add_sum(5, grad_low.astype(WIDE))
            acc[at, :] = grad
            late[at, :] = grad_low
            late_turned[:, at] = grad.T.astype(LOW)

        enc_near = pltpu.make_async_copy(encoded, enc_pair.at[member], enc_sem.at[2])
        enc_far = other_core(encoded, enc_pair.at[member], enc_sem.at[0], enc_sem.at[1])
        enc_near.start()
        enc_far.start()

        def send(j, kind):
            slot = lax.rem(j, 2)
            return other_core(
                leaving.at[slot, kind],
                arrived.at[slot, kind],
                far_send.at[slot, kind],
                far_recv.at[slot, kind],
            )

        def finish(j):
            for piece in range(2):

                @pl.when(j // per_piece == piece)
                def _():
                    for kind in range(2):
                        send(j, kind).wait_recv()
                        column = (lax.rem(j, per_piece) + kind * per_piece) * half
                        columns = pl.ds(pl.multiple_of(column, half), half)

                        @pl.loop(0, width // 64)
                        def _(step):
                            at = tile(step, 64)
                            grads[piece][at, columns] = (
                                grads[piece][at, columns].astype(WIDE)
                                + arrived[lax.rem(j, 2), kind, at, :].astype(WIDE)
                            ).astype(LOW)

        def chunk(j):
            slot = lax.rem(j, 2)
            for copy in loads(j, slot):
                copy.wait()

            @pl.when(j + 1 < chunks)
            def _():
                for copy in loads(j + 1, 1 - slot):
                    copy.start()

            total = jnp.zeros((1, both), WIDE)
            for step in range(rows // tall):
                at = slice(step * tall, (step + 1) * tall)
                grad = dot_nn(late[at, :], reduce_buf[slot]) * slope[slot, at, :].astype(WIDE)
                grad = grad.astype(LOW)
                inner_grad[at, :] = grad
                total = total + jnp.sum(grad.astype(WIDE), axis=0, keepdims=True)
                acc[at, :] += dot_nt(grad, expand_buf[slot])
            place_in = pl.ds(pl.multiple_of(lax.rem(j, per_piece) * half, half), half)
            for which, side in ((1 - member, 0), (member, half)):
                row = 8 + which * 2 + j // per_piece
                small[0, pl.ds(row, 1), place_in] = total[:, side : side + half]

            @pl.when(j >= 2)
            def _():
                for kind in range(2):
                    send(j - 2, kind).wait_send()

            for kind, (left, right) in enumerate(
                ((turned, inner_grad), (late_turned, active.at[slot]))
            ):
                column = (lax.rem(j, per_piece) + kind * per_piece) * half
                columns = pl.ds(pl.multiple_of(column, half), half)
                for step in range(width // tall):
                    at = slice(step * tall, (step + 1) * tall)
                    part = dot_nn(left[at, :], right[...])
                    leaving[slot, kind, at, :] = part[:, 0:half].astype(LOW)
                    for piece in range(2):

                        @pl.when(j // per_piece == piece)
                        def _():
                            grads[piece][at, columns] = part[:, half:both].astype(LOW)

            @pl.when(j >= 1)
            def _():
                finish(j - 1)

            for kind in range(2):
                send(j, kind).start()

        between = {per_piece + i: [stage(0, i)] for i in range(chunks - per_piece)}
        looped(chunks, chunk, between)
        finish(chunks - 1)
        for kind in range(2):
            send(chunks - 2, kind).wait_send()
            send(chunks - 1, kind).wait_send()
        enc_near.wait()
        enc_far.wait()

    pl.run_scoped(
        feed_phase,
        pltpu.VMEM((rows, width), LOW),
        pltpu.VMEM((width, rows), LOW),
        pltpu.VMEM((width, rows), LOW),
        pltpu.VMEM((rows, width), LOW),
        pltpu.VMEM((2, rows, both), LOW),
        pltpu.VMEM((2, rows, both), LOW),
        pltpu.VMEM((rows, both), LOW),
        pltpu.VMEM((2, width, both), LOW),
        pltpu.VMEM((2, width, both), LOW),
        pltpu.VMEM((2, 2, width, half), LOW),
        pltpu.VMEM((rows, width), LOW),
    )
    lines.stage(1, 0)
    lines.stage(0, per_piece)

    def merge_phase(normal, inverse, turned, near_ctx, far_ctx, merge, merge_far, grad_own, grad_far, merge_send):
        merge_columns = pl.ds(whole_ref.shape[2] - inner, inner)
        fetches = [
            fetch(normal_in, normal, 0),
            fetch(inverse_in, inverse, 1),
            fetch(context_in.at[rows_of(member)], near_ctx, 2),
            fetch(far_ctx_in, far_ctx, 3),
            fetch(whole_ref.at[0, :, merge_columns], merge, 4),
            fetch(far_ref.at[0, :, merge_columns], merge_far, 5),
        ]
        for copy in fetches:
            copy.start()
        for copy in fetches:
            copy.wait()

        def norm_tile(step):
            at = tile(step, short)
            grad = acc[at, :]
            unit = normal[at, :]
            add_sum(3, grad * unit)
            add_sum(4, grad)
            branch_grad = norm_back(grad * vectors_ref[3:4, :], unit, inverse[at, 0:1])
            branch_low = branch_grad.astype(LOW)
            add_sum(2, branch_low.astype(WIDE))
            acc[at, :] = branch_grad
            turned[:, at] = branch_grad.T.astype(LOW)
            grad_far[at, :] = dot_nn(branch_low, merge_far[...]).astype(LOW)
            grad_own[at, :] = dot_nn(branch_low, merge[...]).astype(LOW)

        looped(rows // short, norm_tile, {2: [stage(1, 1)]})
        out_grad = other_core(grad_far, grad_ref.at[rows_of(member)], ctx_sem.at[0], ctx_sem.at[1])
        in_grad = pltpu.make_async_copy(grad_own, grad_ref.at[rows_of(member)], ctx_sem.at[2])
        out_grad.start()
        in_grad.start()
        for step in range(width // tall):
            at = slice(step * tall, (step + 1) * tall)
            merge_send[at, :] = dot_nn(turned[at, :], far_ctx[...]).astype(LOW)
        out_merge = other_core(merge_send, merge_recv, merge_sem.at[0], merge_sem.at[1])
        out_merge.start()
        lines.stage(0, per_piece + 1)
        out_merge.wait()
        for step in range(width // tall):
            at = slice(step * tall, (step + 1) * tall)
            grad2[at, 0:inner] = (
                dot_nn(turned[at, :], near_ctx[...]) + merge_recv[at, :].astype(WIDE)
            ).astype(LOW)
        out_grad.wait()
        in_grad.wait()

    pl.run_scoped(
        merge_phase,
        pltpu.VMEM((rows, width), WIDE),
        pltpu.VMEM((rows, 128), WIDE),
        pltpu.VMEM((width, rows), LOW),
        pltpu.VMEM((rows, inner), LOW),
        pltpu.VMEM((rows, inner), LOW),
        pltpu.VMEM((width, inner), LOW),
        pltpu.VMEM((width, inner), LOW),
        pltpu.VMEM((rows, inner), LOW),
        pltpu.VMEM((rows, inner), LOW),
        pltpu.VMEM((width, inner), LOW),
    )
    lines.stage(1, 2)

    def last_phase(mixed):
        def attend_phase(qkv, context, upper, totals, score_bias, dots, key_turned, queries, uppers, query_sum, hidden_turned):
            def loads(pair, slot):
                columns = pl.ds(pl.multiple_of(pair * PAIR, PAIR), PAIR)
                return [
                    pltpu.make_async_copy(qkv_in.at[pair], qkv.at[slot], load_sem.at[slot, 0]),
                    pltpu.make_async_copy(
                        context_in.at[:, columns], context.at[slot], load_sem.at[slot, 1]
                    ),
                    pltpu.make_async_copy(
                        grad_ref.at[:, columns], upper.at[slot], load_sem.at[slot, 2]
                    ),
                ]

            fetches = [fetch(totals_in, totals, 0), fetch(score_bias_in, score_bias, 1)]
            for copy in [*loads(0, 0), *fetches]:
                copy.start()
            for copy in fetches:
                copy.wait()
            blocks = ((0, LONGEST), (LONGEST, total_rows - LONGEST))

            def hidden_tile(step, slot):
                return pltpu.make_async_copy(
                    hidden_turned_in.at[tile(step, tall), :],
                    hidden_turned.at[slot],
                    load_sem.at[slot, 3],
                )

            def project(second):
                grad, first = (grad3, 0) if second else (grad2, inner)
                span = (pairs // 2) * 3 * PAIR
                columns = slice(span if second else 0, span * 2 if second else span)
                hidden_tile(0, 0).start()
                for step in range(width // tall):
                    if step + 1 < width // tall:
                        hidden_tile(step + 1, (step + 1) % 2).start()
                    hidden_tile(step, step % 2).wait()
                    grad[step * tall : (step + 1) * tall, first : first + span] = dot_nn(
                        hidden_turned[step % 2], mixed[:, columns]
                    ).astype(LOW)

            def pair_body(pair):
                slot = lax.rem(pair, 2)
                for copy in loads(pair, slot):
                    copy.wait()

                @pl.when(pair + 1 < pairs)
                def _():
                    for copy in loads(pair + 1, 1 - slot):
                        copy.start()

                attend_back_open(
                    qkv.at[slot], context.at[slot], upper.at[slot], dots, key_turned, queries, uppers
                )
                base = pair * 3 * PAIR

                def columns(which):
                    return pl.ds(pl.multiple_of(base + which * PAIR, PAIR), PAIR)

                for begin, size in blocks:
                    block = slice(begin, begin + size)
                    query_sum[:, block] = jnp.zeros((PAIR, size), WIDE)

                    def key_tile(step, begin=begin, size=size):
                        at, key_sum, value_sum = attend_back_tile(
                            qkv.at[slot], score_bias, totals.at[pair], dots, key_turned, queries, uppers, query_sum,
                            begin, size, step,
                        )
                        mixed[at, columns(1)] = key_sum.astype(LOW)
                        mixed[at, columns(2)] = value_sum.astype(LOW)

                    looped(size // TILE, key_tile, {})
                    for act_pair, act in pair_stages.get(begin, ()):
                        pl.when(pair == act_pair)(act)
                    mixed[block, columns(0)] = (
                        (query_sum[:, block] * HEAD_DIM ** (-0.5)).T.astype(LOW)
                    )
                for which, row in ((0, 0), (2, 1)):
                    part = mixed[:, columns(which)].astype(WIDE)
                    spot = pl.multiple_of(member * inner + pair * PAIR, PAIR)
                    small[0, row : row + 1, pl.ds(spot, PAIR)] = jnp.sum(
                        part, axis=0, keepdims=True
                    )

            pair_stages = {
                0: [(0, stage(1, 3)), (1, stage(1, 5)), (2, stage(2, 1)), (3, stage(2, 3))],
                LONGEST: [(0, stage(1, 4)), (2, stage(2, 2)), (3, stage(2, 4))],
            }
            looped(
                pairs,
                pair_body,
                {
                    1: [functools.partial(project, False), stage(2, 0)],
                    3: [functools.partial(project, True), stage(3, 0)],
                },
            )

        pl.run_scoped(
            attend_phase,
            pltpu.VMEM((2, total_rows, 3 * PAIR), LOW),
            pltpu.VMEM((2, total_rows, PAIR), LOW),
            pltpu.VMEM((2, total_rows, PAIR), LOW),
            pltpu.VMEM(totals_in.shape, WIDE),
            pltpu.VMEM(score_bias_in.shape, WIDE),
            pltpu.VMEM((8, total_rows), WIDE),
            pltpu.VMEM((PAIR, total_rows), LOW),
            pltpu.VMEM((2, total_rows, PAIR), LOW),
            pltpu.VMEM((2, total_rows, PAIR), LOW),
            pltpu.VMEM((PAIR, total_rows), WIDE),
            pltpu.VMEM((2, tall, total_rows), LOW),
        )
        sums.step(0)

        def input_phase(weight, terms, from_own, leaving):
            fetches = [
                fetch(whole_ref.at[0, :, pl.ds(0, pairs * 3 * PAIR)], weight, 0),
                fetch(from_own_in, from_own, 1),
            ]
            for copy in fetches:
                copy.start()
            for copy in fetches:
                copy.wait()

            def term_tile(step):
                at = tile(step, tall)
                total = dot_nt(mixed[at, :], weight[...])
                own = rows // tall
                mine = step // own == member

                @pl.when(mine)
                def _():
                    terms[at, :] = (total + acc[tile(lax.rem(step, own), tall), :]).astype(LOW)

                @pl.when(jnp.logical_not(mine))
                def _():
                    terms[at, :] = total.astype(LOW)

            looped(
                total_rows // tall, term_tile, {1: [stage(3, 1)], 3: [stage(2, 5)], 4: [stage(3, 2)]}
            )
            sums.step(1)

            def far_tile(step):
                at = pl.ds(pl.multiple_of((1 - member) * rows + step * tall, tall), tall)
                leaving[tile(step, tall), :] = picked_rows(from_own, terms, at).astype(LOW)

            looped(rows // tall, far_tile, {})
            crossing = other_core(leaving, input_far, input_sem.at[0], input_sem.at[1])
            crossing.start()
            lines.stage(3, 3)
            sums.step(2)

            def near_tile(step):
                at = pl.ds(pl.multiple_of(member * rows + step * tall, tall), tall)
                acc[tile(step, tall), :] = picked_rows(from_own, terms, at)

            looped(rows // tall, near_tile, {})
            lines.stage(3, 4)
            sums.step(3)
            crossing.wait()
            back = fetch(input_far, leaving, 2)
            back.start()
            back.wait()

            def last_tile(step):
                at = tile(step, short)
                input_ref[at, :] = (acc[at, :] + leaving[at, :].astype(WIDE)).astype(LOW)

            looped(rows // short, last_tile, {})

        pl.run_scoped(
            input_phase,
            pltpu.VMEM((width, pairs * 3 * PAIR), LOW),
            pltpu.VMEM((total_rows, width), LOW),
            pltpu.VMEM((total_rows, 1), jnp.int32),
            pltpu.VMEM((rows, width), LOW),
        )

    pl.run_scoped(last_phase, pltpu.VMEM((total_rows, pairs * 3 * PAIR), LOW))

    def encoded_phase(pair, from_dealt):
        fetches = [fetch(enc_pair.at[i], pair.at[rows_of(i)], i) for i in range(2)]
        fetches.append(fetch(from_dealt_in, from_dealt, 2))
        for copy in fetches:
            copy.start()
        for copy in fetches:
            copy.wait()

        def encoded_tile(step):
            at = tile(step, tall)
            encoded_ref[at, :] = picked_rows(from_dealt, pair, at).astype(LOW)

        looped(rows // tall, encoded_tile, {})

    pl.run_scoped(
        encoded_phase, pltpu.VMEM((total_rows, width), LOW), pltpu.VMEM((rows, 1), jnp.int32)
    )
    for step in range(4, len(sums.partners) + 1):
        sums.step(step)
    small_ref[...] = small[len(sums.partners)]
    lines.stage(3, 5)
    sums.sent()
    for p in range(4):
        lines.sent(p)


def picked_rows(index_ref, source, at):
    index = index_ref[at, :]
    places = lax.broadcasted_iota(jnp.int32, (TILE, source.shape[0]), 1)
    return dot_nn(jnp.where(index == places, 1.0, 0.0).astype(LOW), source[...])


def back(middle, context, qkv, totals, hidden_turned, upstream, whole, far, vectors, score_bias, from_own, from_dealt, parts):
    acc, normal, inverse, turned, active, slope, far_ctx = middle
    rows, width = acc.shape
    total_rows, inner = context.shape
    depth, shard_rows = parts // 4, width // parts
    half, pair_span = 256, 3 * PAIR * (qkv.shape[0] // 2)
    piece = whole.shape[2]
    spans = (piece, piece, inner + pair_span, pair_span)
    classes = []
    for span in spans:
        third = max(128, span // 5 // 128 * 128)
        if (span - third) % 256:
            third += 128
        classes.append(((span - third) // 2, (span - third) // 2, third))
    shape, sem = jax.ShapeDtypeStruct, pltpu.SemaphoreType.DMA
    vmem, anywhere = pl.BlockSpec(memory_space=pltpu.VMEM), pl.BlockSpec(memory_space=pl.ANY)
    steps = 3 + depth.bit_length() - 1
    results = pl.pallas_call(
        functools.partial(back_kernel, depth),
        in_specs=[*[anywhere] * 14, vmem, *[anywhere] * 3],
        out_specs=[*[vmem] * 7, *[anywhere] * 3],
        out_shape=[
            shape((rows, width), LOW),
            shape((rows, width), LOW),
            *[shape((shard_rows, span), WIDE) for span in spans],
            shape((16, width), WIDE),
            shape((2, rows, width), LOW),
            shape((total_rows, inner), LOW),
            shape((rows, width), LOW),
        ],
        scratch_shapes=[
            pltpu.VMEM((rows, width), WIDE),
            pltpu.VMEM((2, 2, width, half), LOW),
            pltpu.VMEM((width, inner), LOW),
            pltpu.VMEM((2 * steps + 1, 16, width), WIDE),
            *[pltpu.VMEM((width, span), LOW) for span in spans],
            *Scatter.scratch(depth, shard_rows, classes),
            sem((steps,)),
            sem((steps,)),
            sem((6,)),
            sem((2, 6)),
            sem((3,)),
            sem((2, 2)),
            sem((2, 2)),
            sem((2,)),
            sem((3,)),
            sem((2,)),
            *Scatter.semaphores(depth, len(spans)),
        ],
        compiler_params=pltpu.CompilerParams(
            collective_id=1, has_side_effects=True, vmem_limit_bytes=63 * MIB
        ),
    )(
        acc, turned, upstream, normal, inverse, active, slope, far_ctx, context, qkv, totals, hidden_turned, whole, far,
        vectors, score_bias, from_own[:, None], from_dealt[:, None],
    )
    encoded, input_grad, first, second, third, fourth, small = results[:7]
    project = jnp.concatenate([third[:, inner:], fourth], axis=1)
    hidden = piece // 2
    return (
        encoded,
        input_grad,
        project,
        third[:, :inner],
        jnp.concatenate([first[:, :hidden], second[:, :hidden]], axis=1),
        jnp.concatenate([first[:, hidden:], second[:, hidden:]], axis=1),
        small,
    )


def adamw_update(master, moment, square, gradient, step_rate, decay_rate):
    moment_new = beta_one * moment + (1.0 - beta_one) * gradient
    square_new = beta_two * square + (1.0 - beta_two) * gradient * gradient
    moment_hat = moment_new / (1.0 - beta_one**STEP)
    square_hat = square_new / (1.0 - beta_two**STEP)
    master_new = master - step_rate * (
        moment_hat / (jnp.sqrt(square_hat) + adam_epsilon) + decay_rate * master
    )
    return (moment_new, square_new, master_new)


def local(
    tokens,
    cotangent,
    lengths,
    dealing,
    project_weight,
    project_first,
    project_second,
    merge_weight,
    merge_first,
    merge_second,
    expand_weight,
    expand_first,
    expand_second,
    reduce_weight,
    reduce_first,
    reduce_second,
    vectors,
    vector_first,
    vector_second,
    hidden_bias,
    hidden_first,
    hidden_second,
):
    parts = lax.axis_size("dp")
    member = lax.axis_index("tensor")
    other = 1 - member
    half_rows, model_width = tokens.shape
    total_rows = 2 * half_rows
    width_half = project_weight.shape[2]
    pairs = width_half // PAIR
    hidden_half = expand_weight.shape[1]
    shard_rows = expand_weight.shape[0]
    own_begin = member * half_rows
    by_kernel = parts % 4 == 0 and (parts & (parts - 1)) == 0 and shard_rows % 16 == 0

    def swap(value):
        return lax.ppermute(value, "tensor", [(0, 1), (1, 0)])

    def own(value, size, which=member):
        return lax.dynamic_slice_in_dim(value, which * size, size, 0)

    segment, own_of, dealt_of, from_own, from_dealt = layout(lengths[0], dealing[0], total_rows)
    dealt_of = own(dealt_of, half_rows)
    short = segment[LONGEST:]
    score_bias = jnp.where(short[:, None] == short[None, :], 0.0, masked_score).astype(WIDE)

    def own_first(index):
        return lax.rem(index - own_begin + total_rows, total_rows)

    projections = (
        project_weight.reshape(3, shard_rows, pairs, PAIR)
        .transpose(1, 2, 0, 3)
        .reshape(shard_rows, 3 * width_half)
    )
    quarter = hidden_half // 2
    reduce_turned = reduce_weight.T
    shards = jnp.stack(
        [
            jnp.concatenate([projections, merge_weight.T], axis=1),
            jnp.concatenate([expand_weight[:, :quarter], reduce_turned[:, :quarter]], axis=1),
            jnp.concatenate([expand_weight[:, quarter:], reduce_turned[:, quarter:]], axis=1),
        ]
    ).astype(LOW)
    zeros_pair = jnp.zeros((pairs, PAIR), WIDE)
    bias_row = jnp.concatenate(
        [
            own(vectors[0], width_half).reshape(pairs, PAIR),
            zeros_pair,
            own(vectors[1], width_half).reshape(pairs, PAIR),
        ],
        axis=1,
    ).reshape(pairs, 1, 3 * PAIR)
    if by_kernel:
        whole, far, qkv, hidden, hidden_turned, upstream, context, totals = front(
            shards, tokens, cotangent, own_of, dealt_of, bias_row, score_bias, parts
        )
        middle = middle_block(
            context,
            whole,
            far,
            own(hidden, half_rows),
            vectors,
            own(hidden_bias, hidden_half),
            own(hidden_bias, hidden_half, other),
        )
        encoded_out, input_grad, *grads, small = back(
            middle, context, qkv, totals, hidden_turned, upstream, whole, far, vectors, score_bias, from_own,
            own(from_dealt, half_rows), parts,
        )
    else:
        whole = lax.all_gather(shards, "dp", axis=1, tiled=True)
        far = swap(whole)
        token_pair = jnp.concatenate([tokens, swap(tokens)], axis=0)
        upper_pair = jnp.concatenate([cotangent, swap(cotangent)], axis=0)
        hidden = dot_nn(pick_rows(own_first(own_of), total_rows), token_pair).astype(LOW)
        upstream = dot_nn(pick_rows(own_first(dealt_of), total_rows), upper_pair).astype(LOW)
        qkv = jnp.einsum(
            "rd,dpc->prc",
            hidden,
            whole[0, :, : 3 * width_half].reshape(model_width, pairs, 3 * PAIR),
            preferred_element_type=WIDE,
        )
        qkv = (qkv + bias_row).astype(LOW)
        context, totals = attend(qkv, score_bias)

        (
            encoded, branch_grad, context_grad, merge_grad, expand_grad, reduce_grad, sums, hidden_part_own, hidden_part_far,
        ) = feed_block(
            context,
            whole,
            far,
            own(hidden, half_rows),
            upstream,
            vectors,
            own(hidden_bias, hidden_half),
            own(hidden_bias, hidden_half, other),
        )
        encoded_pair = jnp.concatenate([encoded, swap(encoded)], axis=0)
        encoded_out = dot_nn(
            pick_rows(own_first(own(from_dealt, half_rows)), total_rows), encoded_pair
        ).astype(LOW)
        mixed_grads = attend_back(qkv, score_bias, context, context_grad, totals)
        mixed_sums = jnp.sum(mixed_grads.astype(WIDE), axis=1).reshape(pairs, 3, PAIR)
        mixed_grads = mixed_grads.transpose(1, 0, 2).reshape(total_rows, 3 * width_half)
        project_grad = dot_tn(hidden, mixed_grads)
        input_terms = dot_nt(mixed_grads, whole[0, :, : 3 * width_half])
        own_part = own(input_terms, half_rows) + branch_grad
        input_terms = lax.dynamic_update_slice_in_dim(input_terms, own_part, own_begin, 0).astype(LOW)
        input_far = swap(
            dot_nn(pick_rows(own(from_own, half_rows, other), total_rows), input_terms).astype(LOW)
        )
        input_grad = (
            dot_nn(pick_rows(own(from_own, half_rows), total_rows), input_terms)
            + input_far.astype(WIDE)
        ).astype(LOW)
        zeros_width = jnp.zeros((model_width,), WIDE)
        zeros_hidden = jnp.zeros_like(hidden_bias)
        hidden_total = lax.dynamic_update_slice_in_dim(
            lax.dynamic_update_slice_in_dim(
                zeros_hidden, hidden_part_own, member * hidden_half, 0
            ),
            hidden_part_far,
            other * hidden_half,
            0,
        )
        vector_rows = [
            lax.dynamic_update_slice_in_dim(
                zeros_width, mixed_sums[:, c].reshape(-1), member * width_half, 0
            )
            for c in (0, 2)
        ]
        small = jnp.concatenate(
            [
                jnp.stack(vector_rows),
                sums[2:],
                hidden_total.reshape(-1, model_width),
                jnp.zeros((4, model_width), WIDE),
            ],
            axis=0,
        )
        grads = [
            lax.psum_scatter(g.astype(LOW), "dp", scatter_dimension=0, tiled=True).astype(WIDE)
            for g in (project_grad, merge_grad, expand_grad, reduce_grad)
        ]
        small = lax.psum(small, ("dp", "tensor"))
    project_shard, merge_shard, expand_shard, reduce_shard = grads
    project_shard = (
        project_shard.reshape(shard_rows, pairs, 3, PAIR)
        .transpose(2, 0, 1, 3)
        .reshape(3, shard_rows, width_half)
    )
    vector_grad = small[:8]
    hidden_grad = small[8:12].reshape(-1)
    return (
        encoded_out,
        input_grad,
        *adamw_update(
            project_weight, project_first, project_second, project_shard, rate_project, weight_decay
        ),
        *adamw_update(
            merge_weight, merge_first, merge_second, merge_shard.T, rate_merge, weight_decay
        ),
        *adamw_update(
            expand_weight, expand_first, expand_second, expand_shard, rate_expand, weight_decay
        ),
        *adamw_update(
            reduce_weight, reduce_first, reduce_second, reduce_shard.T, rate_reduce, weight_decay
        ),
        *adamw_update(vectors, vector_first, vector_second, vector_grad, rate_vectors, 0.0),
        *adamw_update(hidden_bias, hidden_first, hidden_second, hidden_grad, rate_hidden, 0.0),
        vector_grad,
    )


def solution(mesh):
    sharded = (
        P("dp", None),
        P("dp", None),
        *[P(None, "dp", "tensor")] * 3,
        *[P("tensor", "dp")] * 3,
        *[P("dp", "tensor")] * 3,
        *[P("tensor", "dp")] * 3,
        *[P()] * 6,
    )
    rows = P(("dp", "tensor"), None)
    return jax.shard_map(
        local,
        mesh=mesh,
        in_specs=(rows, rows, *sharded),
        out_specs=(rows, rows, *sharded[2:], P()),
        check_vma=False,
    )
```

```python
import functools

import jax
import jax.numpy as jnp
from jax import lax
from jax.experimental import pallas as pl
from jax.experimental.pallas import tpu as pltpu
from jax.sharding import PartitionSpec as P

HEAD_DIM = 64
LONGEST = 1024
STEP = 10
PAIR = 2 * HEAD_DIM
TILE = 256
MIB = 1024 * 1024
MESH = pl.DeviceIdType.MESH
LOW = jnp.bfloat16
WIDE = jnp.float32

beta_one = 0.9
beta_two = 0.999
adam_epsilon = 1e-08
weight_decay = 0.01
norm_epsilon = 1e-05
masked_score = -1e30
rate_project = 0.03
rate_merge = 0.3
rate_expand = 0.03
rate_reduce = 0.015
rate_vectors = 0.4
rate_hidden = 0.1


def dot_nn(a, b):
    return jnp.dot(a, b, preferred_element_type=WIDE)


def dot_nt(a, b):
    return lax.dot_general(a, b, (((1,), (1,)), ((), ())), preferred_element_type=WIDE)


def dot_tn(a, b):
    return lax.dot_general(a, b, (((0,), (0,)), ((), ())), preferred_element_type=WIDE)


def layout(lengths_row, dealing_row, total_rows):
    slots = jnp.arange(lengths_row.shape[0], dtype=jnp.int32)
    places = jnp.arange(total_rows, dtype=jnp.int32)
    rank_of = jnp.sum(jnp.where(dealing_row[None, :] == slots[:, None], slots[None, :], 0), axis=1)
    own_start = jnp.cumsum(lengths_row) - lengths_row
    dealt_start = jnp.sum(
        jnp.where(rank_of[None, :] < rank_of[:, None], lengths_row[None, :], 0), axis=1
    )
    longest = lengths_row == LONGEST
    short = jnp.where(longest, 0, lengths_row)
    start = jnp.where(longest, 0, LONGEST + jnp.cumsum(short) - short)

    def inside(begin):
        return (places[:, None] >= begin[None, :]) & (
            places[:, None] < (begin + lengths_row)[None, :]
        )

    def moved(begin, end):
        return places + jnp.sum(jnp.where(inside(begin), (end - begin)[None, :], 0), axis=1)

    segment = jnp.sum(jnp.where(inside(start), slots[None, :], 0), axis=1)
    return (
        segment,
        moved(start, own_start),
        moved(start, dealt_start),
        moved(own_start, start),
        moved(dealt_start, start),
    )


def pick_rows(index, rows):
    places = jnp.arange(rows, dtype=jnp.int32)
    return (index[:, None] == places[None, :]).astype(LOW)


def attend_tile(qkv_ref, pair, bias_ref, begin, size, step, context_ref, columns, total_ref):
    lane = lax.broadcasted_iota(jnp.int32, (1, PAIR), 1)
    scale = HEAD_DIM ** (-0.5)
    first = pl.multiple_of(begin + step * TILE, TILE)
    query = qkv_ref[pair, pl.ds(first, TILE), 0:PAIR]
    key = qkv_ref[pair, begin : begin + size, PAIR : 2 * PAIR]
    value = qkv_ref[pair, begin : begin + size, 2 * PAIR : 3 * PAIR]
    outcome = []
    for head in range(2):
        chosen = jnp.where(lane // HEAD_DIM == head, scale, 0.0).astype(LOW)
        scores = dot_nt(query * chosen, key)
        if begin:
            inner = pl.multiple_of(step * TILE, TILE)
            scores = scores + bias_ref[pl.ds(inner, TILE), :]
        top = jnp.max(scores, axis=1, keepdims=True)
        exponent = jnp.exp(scores - top)
        total = jnp.sum(exponent, axis=1, keepdims=True)
        outcome.append(dot_nn(exponent.astype(LOW), value) / total)
        log_total = jnp.broadcast_to(top + jnp.log(total), (TILE, PAIR))
        total_ref[pair, head : head + 1, pl.ds(first, TILE)] = log_total.T[0:1, :]
    context_ref[pl.ds(first, TILE), columns] = jnp.where(
        lane < HEAD_DIM, outcome[0], outcome[1]
    ).astype(LOW)


def attend_kernel(qkv_ref, bias_ref, context_ref, total_ref):
    rows = qkv_ref.shape[1]
    for begin, size in ((0, LONGEST), (LONGEST, rows - LONGEST)):

        @pl.loop(0, size // TILE)
        def _(step):
            attend_tile(
                qkv_ref, 0, bias_ref, begin, size, step, context_ref, slice(0, PAIR), total_ref
            )


def attend(qkv, bias):
    pairs, rows, width = qkv.shape
    return pl.pallas_call(
        attend_kernel,
        grid=(pairs,),
        in_specs=[
            pl.BlockSpec((1, rows, width), lambda p: (p, 0, 0)),
            pl.BlockSpec(bias.shape, lambda p: (0, 0)),
        ],
        out_specs=[
            pl.BlockSpec((rows, PAIR), lambda p: (0, p)),
            pl.BlockSpec((1, 8, rows), lambda p: (p, 0, 0)),
        ],
        out_shape=[
            jax.ShapeDtypeStruct((rows, pairs * PAIR), LOW),
            jax.ShapeDtypeStruct((pairs, 8, rows), WIDE),
        ],
        compiler_params=pltpu.CompilerParams(vmem_limit_bytes=48 * MIB),
    )(qkv, bias)


def attend_back_open(qkv_ref, context_ref, upper_ref, dots, key_turned, queries, uppers):
    lane = lax.broadcasted_iota(jnp.int32, (1, PAIR), 1)
    product = (upper_ref[...].astype(WIDE) * context_ref[...].astype(WIDE)).T
    for head in range(2):
        band = slice(head * HEAD_DIM, (head + 1) * HEAD_DIM)
        dots[head : head + 1, :] = jnp.sum(product[band, :], axis=0, keepdims=True)
        chosen = lane // HEAD_DIM == head
        queries[head] = qkv_ref[:, 0:PAIR] * jnp.where(chosen, HEAD_DIM ** (-0.5), 0.0).astype(LOW)
        uppers[head] = upper_ref[...] * jnp.where(chosen, 1.0, 0.0).astype(LOW)
    key_turned[...] = qkv_ref[:, PAIR : 2 * PAIR].astype(WIDE).T.astype(LOW)


def attend_back_tile(
    qkv_ref, bias_ref, total_ref, dots, key_turned, queries, uppers, query_sum, begin, size, step
):
    block = slice(begin, begin + size)
    first = pl.multiple_of(begin + step * TILE, TILE)
    key = qkv_ref[pl.ds(first, TILE), PAIR : 2 * PAIR]
    value = qkv_ref[pl.ds(first, TILE), 2 * PAIR : 3 * PAIR]
    key_sum = jnp.zeros((TILE, PAIR), WIDE)
    value_sum = jnp.zeros((TILE, PAIR), WIDE)
    for head in range(2):
        band = slice(head * HEAD_DIM, (head + 1) * HEAD_DIM)
        query = queries[head, block, :]
        upper = uppers[head, block, :]
        scores = dot_nt(key, query)
        if begin:
            inner = pl.multiple_of(step * TILE, TILE)
            scores = scores + bias_ref[pl.ds(inner, TILE), :]
        probability = jnp.exp(scores - total_ref[head : head + 1, block])
        weight_grads = dot_nt(value, upper)
        score_grads = (probability * (weight_grads - dots[head : head + 1, block])).astype(LOW)
        value_sum = value_sum + dot_nn(probability.astype(LOW), upper)
        key_sum = key_sum + dot_nn(score_grads, query)
        query_sum[band, block] += dot_nn(key_turned[band, pl.ds(first, TILE)], score_grads)
    return pl.ds(first, TILE), key_sum, value_sum


def attend_back_kernel(
    qkv_ref, bias_ref, context_ref, grad_ref, total_ref, out_ref, dots, key_turned, queries, uppers, query_sum
):
    rows = qkv_ref.shape[1]
    qkv = qkv_ref.at[0]
    attend_back_open(qkv, context_ref, grad_ref, dots, key_turned, queries, uppers)
    for begin, size in ((0, LONGEST), (LONGEST, rows - LONGEST)):
        block = slice(begin, begin + size)
        query_sum[:, block] = jnp.zeros((PAIR, size), WIDE)

        @pl.loop(0, size // TILE)
        def _(step):
            at, key_sum, value_sum = attend_back_tile(
                qkv, bias_ref, total_ref.at[0], dots, key_turned, queries, uppers, query_sum, begin, size, step
            )
            out_ref[0, at, PAIR : 2 * PAIR] = key_sum.astype(LOW)
            out_ref[0, at, 2 * PAIR : 3 * PAIR] = value_sum.astype(LOW)

        out_ref[0, block, 0:PAIR] = (query_sum[:, block] * HEAD_DIM ** (-0.5)).T.astype(LOW)


def attend_back(qkv, bias, context, grad, totals):
    pairs, rows, width = qkv.shape
    return pl.pallas_call(
        attend_back_kernel,
        grid=(pairs,),
        in_specs=[
            pl.BlockSpec((1, rows, width), lambda p: (p, 0, 0)),
            pl.BlockSpec(bias.shape, lambda p: (0, 0)),
            pl.BlockSpec((rows, PAIR), lambda p: (0, p)),
            pl.BlockSpec((rows, PAIR), lambda p: (0, p)),
            pl.BlockSpec((1, 8, rows), lambda p: (p, 0, 0)),
        ],
        out_specs=pl.BlockSpec((1, rows, width), lambda p: (p, 0, 0)),
        out_shape=jax.ShapeDtypeStruct(qkv.shape, LOW),
        scratch_shapes=[
            pltpu.VMEM((8, rows), WIDE),
            pltpu.VMEM((PAIR, rows), LOW),
            pltpu.VMEM((2, rows, PAIR), LOW),
            pltpu.VMEM((2, rows, PAIR), LOW),
            pltpu.VMEM((PAIR, rows), WIDE),
        ],
        compiler_params=pltpu.CompilerParams(vmem_limit_bytes=48 * MIB),
    )(qkv, bias, context, grad, totals)


def place():
    me = lax.axis_index("dp")
    z, y, x = me // 4, (me // 2) % 2, me % 2
    return me, z, y, x


def line_slots(z, depth):
    slots = []
    for step in range(depth - 1):
        slots.append((z - 1 - step, z - 1 - step >= 0, 1))
        slots.append((z + 1 + step, z + 1 + step < depth, -1))
    return slots


def remote(source, target, send, receive, device):
    return pltpu.make_async_remote_copy(
        src_ref=source,
        dst_ref=target,
        send_sem=send,
        recv_sem=receive,
        device_id={"dp": device},
        device_id_type=MESH,
    )


def greet_line(me, z, y, x, depth, extra=()):
    barrier = pltpu.get_barrier_semaphore()
    for peer in (z * 4 + y * 2 + 1 - x, z * 4 + (1 - y) * 2 + x):
        pl.semaphore_signal(barrier, inc=1, device_id={"dp": peer}, device_id_type=MESH)

    @pl.when(z > 0)
    def _():
        pl.semaphore_signal(barrier, inc=1, device_id={"dp": me - 4}, device_id_type=MESH)

    @pl.when(z < depth - 1)
    def _():
        pl.semaphore_signal(barrier, inc=1, device_id={"dp": me + 4}, device_id_type=MESH)

    for peer in extra:
        pl.semaphore_signal(barrier, inc=1, device_id=peer, device_id_type=MESH)
    ends = jnp.where(z > 0, 1, 0) + jnp.where(z < depth - 1, 1, 0)
    pl.semaphore_wait(barrier, 2 + len(extra) + ends)


def other_core(source, target, send, receive):
    return pltpu.make_async_remote_copy(
        src_ref=source,
        dst_ref=target,
        send_sem=send,
        recv_sem=receive,
        device_id={"tensor": 1 - lax.axis_index("tensor")},
        device_id_type=MESH,
    )


class Gather:
    def __init__(self, depth, parts, whole, far, sems):
        self.whole, self.far = whole, far
        self.depth = depth
        self.me, self.z, self.y, self.x = place()
        self.x_peer = self.z * 4 + self.y * 2 + 1 - self.x
        self.y_peer = self.z * 4 + (1 - self.y) * 2 + self.x
        self.rows = whole.shape[1] // parts
        width = whole.shape[2]
        self.third = width // 4
        side = (width - self.third) // 2
        self.a, self.b = (0, side), (side, side)
        self.ab, self.c, self.all = (0, 2 * side), (2 * side, self.third), (0, width)
        (
            self.z_send, self.z_recv, self.zc_send, self.zc_recv, self.xa_send, self.xa_recv, self.yb_send, self.yb_recv,
            self.ya_send, self.ya_recv, self.xb_send, self.xb_recv, self.c_send, self.c_recv, self.far_send, self.far_recv,
        ) = sems
        self.slots = line_slots(self.z, depth)

    @staticmethod
    def semaphores(depth, pieces):
        sem = pltpu.SemaphoreType.DMA
        return [
            *[sem((pieces, depth + 1)), sem((pieces, depth))] * 2,
            *[sem((pieces, depth))] * 4,
            *[sem((pieces, depth, 2))] * 4,
            sem((pieces, 2)),
            sem((pieces, 2)),
            sem((pieces,)),
            sem((pieces,)),
        ]

    def block(self, zb, yb, xb):
        return zb * 4 + yb * 2 + xb

    def cut(self, ref, p, block, count, columns):
        first = pl.multiple_of(block * self.rows, self.rows)
        return ref.at[p, pl.ds(first, count * self.rows), pl.ds(*columns)]

    def copy(self, p, block, count, columns, send, receive, device):
        part = self.cut(self.whole, p, block, count, columns)
        return remote(part, part, send, receive, device)

    def forward(self, p, block, count, columns):
        if p == 0 and columns[0] + columns[1] <= self.c[0]:
            return
        if p == 0:
            columns = self.c
        other_core(
            self.cut(self.whole, p, block, count, columns),
            self.cut(self.far, p, block, count, columns),
            self.far_send.at[p],
            self.far_recv.at[p],
        ).start()

    def far_copy(self, p):
        columns = self.c if p == 0 else self.all
        part = self.far.at[p, :, pl.ds(*columns)]
        return other_core(part, part, self.far_send.at[p], self.far_recv.at[p])

    def z_copy(self, p, zb, way, back=False):
        block = self.block(zb, self.y, self.x)
        sem = self.depth if back else zb
        return self.copy(
            p, block, 1, self.ab, self.z_send.at[p, sem], self.z_recv.at[p, zb], self.me + 4 * way
        )

    def zc_copy(self, p, zb, way, back=False):
        sem = self.depth if back else zb
        return self.copy(
            p, zb * 4, 4, self.c, self.zc_send.at[p, sem], self.zc_recv.at[p, zb], self.me + 4 * way
        )

    def xa(self, p, zb, xb):
        block = self.block(zb, self.y, xb)
        return self.copy(
            p, block, 1, self.a, self.xa_send.at[p, zb], self.xa_recv.at[p, zb], self.x_peer
        )

    def yb(self, p, zb, yb):
        block = self.block(zb, yb, self.x)
        return self.copy(
            p, block, 1, self.b, self.yb_send.at[p, zb], self.yb_recv.at[p, zb], self.y_peer
        )

    def ya(self, p, zb, yb, xb):
        block = self.block(zb, yb, xb)
        return self.copy(
            p, block, 1, self.a, self.ya_send.at[p, zb, xb], self.ya_recv.at[p, zb, xb], self.y_peer
        )

    def xb(self, p, zb, yb, xb):
        block = self.block(zb, yb, xb)
        return self.copy(
            p, block, 1, self.b, self.xb_send.at[p, zb, yb], self.xb_recv.at[p, zb, yb], self.x_peer
        )

    def xc(self, p, xb):
        block = self.block(self.z, self.y, xb)
        return self.copy(
            p, block, 1, self.c, self.c_send.at[p, 0], self.c_recv.at[p, 0], self.x_peer
        )

    def yc(self, p, yb):
        block = self.block(self.z, yb, 0)
        return self.copy(
            p, block, 2, self.c, self.c_send.at[p, 1], self.c_recv.at[p, 1], self.y_peer
        )

    def both_ways(self, copy, act):
        @pl.when(self.z < self.depth - 1)
        def _():
            act(copy(self.z, 1))

        @pl.when(self.z > 0)
        def _():
            act(copy(self.z, -1, True))

    def spread(self, p, zb):
        self.xa(p, zb, self.x).start()
        self.yb(p, zb, self.y).start()
        self.ya(p, zb, self.y, self.x).start()
        self.xb(p, zb, self.y, self.x).start()

    def turn(self, p, zb):
        self.xa(p, zb, 1 - self.x).wait_recv()
        self.ya(p, zb, self.y, 1 - self.x).start()
        self.forward(p, self.block(zb, self.y, 1 - self.x), 1, self.a)
        self.yb(p, zb, 1 - self.y).wait_recv()
        self.xb(p, zb, 1 - self.y, self.x).start()
        self.forward(p, self.block(zb, 1 - self.y, self.x), 1, self.b)

    def at_step(self, step, act):
        for zb, valid, way in self.slots[2 * step : 2 * step + 2]:
            on = (self.z + way >= 0) & (self.z + way < self.depth)
            pl.when(valid)(functools.partial(act, zb, way, on))

    def arrive(self, p, step):
        def act(zb, way, on):
            self.z_copy(p, zb, way).wait_recv()
            pl.when(on)(lambda: self.z_copy(p, zb, way).start())
            self.spread(p, zb)
            self.forward(p, self.block(zb, self.y, self.x), 1, self.ab)

        self.at_step(step, act)

    def arrive_c(self, p, step):
        def act(zb, way, on):
            self.zc_copy(p, zb, way).wait_recv()
            pl.when(on)(lambda: self.zc_copy(p, zb, way).start())
            self.forward(p, zb * 4, 4, self.c)

        self.at_step(step, act)

    def stage(self, p, s):
        depth = self.depth
        if s == 0:
            self.both_ways(lambda *way: self.z_copy(p, *way), lambda copy: copy.start())
            self.xc(p, self.x).start()
            self.spread(p, self.z)
            self.forward(p, self.me, 1, self.all)
            return
        if s == 1:
            self.xc(p, 1 - self.x).wait_recv()
            self.yc(p, self.y).start()
            self.forward(p, self.block(self.z, self.y, 1 - self.x), 1, self.c)
        if s == 2:
            self.yc(p, 1 - self.y).wait_recv()
            self.both_ways(lambda *way: self.zc_copy(p, *way), lambda copy: copy.start())
            self.forward(p, self.block(self.z, 1 - self.y, 0), 2, self.c)
        if 1 <= s < depth:
            self.arrive(p, s - 1)
        if 3 <= s < depth + 2:
            self.arrive_c(p, s - 3)
        if s == 2:
            self.turn(p, self.z)
        if 3 <= s < depth + 2:
            self.at_step(s - 3, lambda zb, way, on: self.turn(p, zb))
        if s == depth + 2:
            for zb in range(depth):
                for other in range(2):
                    self.ya(p, zb, 1 - self.y, other).wait_recv()
                    self.forward(p, self.block(zb, 1 - self.y, other), 1, self.a)
                    self.xb(p, zb, other, 1 - self.x).wait_recv()
                    self.forward(p, self.block(zb, other, 1 - self.x), 1, self.b)

    def finish(self, p):
        def sent(copy):
            copy.wait_send()

        self.far_copy(p).wait_send()
        self.both_ways(lambda *way: self.z_copy(p, *way), sent)
        self.both_ways(lambda *way: self.zc_copy(p, *way), sent)
        for zb in range(self.depth):
            self.xa(p, zb, self.x).wait_send()
            self.yb(p, zb, self.y).wait_send()
            for other in range(2):
                self.ya(p, zb, self.y, other).wait_send()
                self.xb(p, zb, other, self.x).wait_send()
        self.xc(p, self.x).wait_send()
        self.yc(p, self.y).wait_send()

        def passed(zb, way, on):
            pl.when(on)(lambda: sent(self.z_copy(p, zb, way)))
            pl.when(on)(lambda: sent(self.zc_copy(p, zb, way)))

        for step in range(self.depth - 1):
            self.at_step(step, passed)


def looped(count, body, between):
    @pl.loop(0, count)
    def _(i):
        body(i)
        for step, acts in between.items():

            @pl.when(i == step)
            def _():
                for act in acts:
                    act()


GATHER_AT = {
    "hidden": {-1: [(0, 1)], 0: [(0, 2)], 3: [(0, 3), (0, 4)]},
    "upstream": {-1: [(1, 0)], 0: [(0, 5)], 1: [(2, 0)]},
    "project": {-1: [(0, 6)], 0: [(1, 1)]},
    "long": {-1: [(1, 2)], 2: [(2, 1)], 9: [(1, 3)], 11: [(2, 2)]},
    "short": {4: [(1, 4)]},
    "norm": {1: [(1, 5), (2, 3)]},
    "feed": {-1: [(1, 6)], 0: [(2, 4)], 1: [(2, 5)]},
    "last": {-1: [(2, 6)]},
}


def front_kernel(
    depth, shards_ref, tokens_ref, cotangent_ref, own_of_ref, dealt_of_ref, bias_ref, score_bias_ref, vectors_ref, hidden_bias_ref,
    whole_ref, far_ref, qkv_out, turned_out, upstream_out, context_out, total_out,
    acc_out, normal_out, inverse_out, low_turned_out, active_out, slope_out, far_context_out,
    token, upper, hidden, turned, upstream, weight, qkv, context, total,
    acc, normal, inverse, low, low_turned, active, slope, far_context, merge, merge_far, expand_buf, reduce_buf,
    local_sem, core_sem, out_sem, load_sem, chunk_sem, *sems,
):
    pieces = whole_ref.shape[0]
    half_rows, width = tokens_ref.shape
    rows = 2 * half_rows
    pairs = qkv.shape[0]
    inner = pairs * PAIR
    chunks, _, both = hidden_bias_ref.shape
    half = both // 2
    per_piece = chunks // (pieces - 1)
    member = lax.axis_index("tensor")
    lines = Gather(depth, 4 * depth, whole_ref, far_ref, sems)
    me = lines.me
    tall, short = 2 * TILE, TILE // 2

    own = [
        pltpu.make_async_copy(
            shards_ref.at[p], lines.cut(whole_ref, p, me, 1, lines.all), local_sem.at[p]
        )
        for p in range(pieces)
    ]
    own += [
        pltpu.make_async_copy(tokens_ref, token.at[member], local_sem.at[pieces]),
        pltpu.make_async_copy(cotangent_ref, upper.at[member], local_sem.at[pieces + 1]),
    ]
    for copy in own:
        copy.start()
    greet_line(me, lines.z, lines.y, lines.x, depth, [{"tensor": 1 - member}])
    crossing = [
        other_core(tokens_ref, token.at[member], core_sem.at[0, 0], core_sem.at[0, 1]),
        other_core(cotangent_ref, upper.at[member], core_sem.at[1, 0], core_sem.at[1, 1]),
    ]
    own[0].wait()
    lines.stage(0, 0)
    for copy in crossing:
        copy.start()
    for copy in own[1:]:
        copy.wait()

    leaving = []

    def leave(source, target):
        copy = pltpu.make_async_copy(source, target, out_sem.at[len(leaving)])
        copy.start()
        leaving.append(copy)

    def phase(name, count, body):
        between = {
            step: [functools.partial(lines.stage, *stage) for stage in stages]
            for step, stages in GATHER_AT[name].items()
        }
        for act in between.pop(-1, ()):
            act()
        looped(count, body, between)

    def picked(index_ref, source, at):
        index = index_ref[at, :]
        total = None
        for which in range(2):
            places = lax.broadcasted_iota(jnp.int32, (TILE, half_rows), 1) + which * half_rows
            chosen = jnp.where(index == places, 1.0, 0.0).astype(LOW)
            part = dot_nn(chosen, source[which])
            total = part if total is None else total + part
        return total

    def tile(step, size=TILE):
        return pl.ds(pl.multiple_of(step * size, size), size)

    def hidden_tile(step):
        rows_here = picked(own_of_ref, token, tile(step))
        hidden[tile(step), :] = rows_here.astype(LOW)
        turned[:, tile(step)] = rows_here.T.astype(LOW)

    def upstream_tile(step):
        upstream[tile(step), :] = picked(dealt_of_ref, upper, tile(step)).astype(LOW)

    crossing[0].wait()
    phase("hidden", rows // TILE, hidden_tile)
    leave(turned, turned_out)
    crossing[1].wait()
    phase("upstream", half_rows // TILE, upstream_tile)
    leave(upstream, upstream_out)

    weight_copy = pltpu.make_async_copy(
        whole_ref.at[0, :, pl.ds(0, pairs * 3 * PAIR)], weight, local_sem.at[1]
    )

    def project_tile(i):
        @pl.when(i == 0)
        def _():
            weight_copy.start()
            weight_copy.wait()

        pair, step = i // (rows // tall), lax.rem(i, rows // tall)
        at = tile(step, tall)
        columns = pl.ds(pl.multiple_of(pair * 3 * PAIR, PAIR), 3 * PAIR)
        qkv[pair, at, :] = (dot_nn(hidden[at, :], weight[:, columns]) + bias_ref[pair]).astype(LOW)

    phase("project", pairs * rows // tall, project_tile)
    leave(qkv, qkv_out)

    def attend_step(begin, size):
        def step_of(i):
            pair, step = i // (size // TILE), lax.rem(i, size // TILE)
            columns = pl.ds(pl.multiple_of(pair * PAIR, PAIR), PAIR)
            attend_tile(qkv, pair, score_bias_ref, begin, size, step, context, columns, total)

        return step_of

    phase("long", pairs * LONGEST // TILE, attend_step(0, LONGEST))
    phase("short", pairs * (rows - LONGEST) // TILE, attend_step(LONGEST, rows - LONGEST))
    leave(context, context_out)
    leave(total, total_out)

    own_first = member * half_rows
    other_rows = pl.ds(pl.multiple_of((1 - member) * half_rows, half_rows), half_rows)
    crossing = other_core(context.at[other_rows], far_context, core_sem.at[2, 0], core_sem.at[2, 1])
    crossing.start()
    lines.far_copy(0).wait_recv()
    merge_columns = pl.ds(whole_ref.shape[2] - inner, inner)
    fetches = [
        pltpu.make_async_copy(whole_ref.at[0, :, merge_columns], merge, local_sem.at[2]),
        pltpu.make_async_copy(far_ref.at[0, :, merge_columns], merge_far, local_sem.at[3]),
    ]
    for copy in fetches:
        copy.start()
    for copy in fetches:
        copy.wait()
    crossing.wait()
    leave(far_context, far_context_out)

    def norm_tile(step):
        at = tile(step, short)
        own_at = pl.ds(pl.multiple_of(own_first + step * short, short), short)
        branch = dot_nt(context[own_at, :], merge[...]) + dot_nt(far_context[at, :], merge_far[...])
        unit, scale = norm(hidden[own_at, :].astype(WIDE) + branch + vectors_ref[2:3, :])
        normed = unit * vectors_ref[3:4, :] + vectors_ref[4:5, :]
        normal[at, :] = unit
        inverse[at, :] = jnp.broadcast_to(scale, (short, 128))
        low[at, :] = normed.astype(LOW)
        low_turned[:, at] = normed.T.astype(LOW)
        acc[at, :] = normed + vectors_ref[5:6, :]

    phase("norm", half_rows // short, norm_tile)
    leave(normal, normal_out)
    leave(inverse, inverse_out)
    leave(low_turned, low_turned_out)

    def loads(j):
        slot, piece, at = lax.rem(j, 2), 1 + j // per_piece, lax.rem(j, per_piece) * half
        copies = []
        for kind, buf in enumerate((expand_buf, reduce_buf)):
            first = pl.multiple_of(at + kind * per_piece * half, half)
            for side, source in enumerate((far_ref, whole_ref)):
                copies.append(
                    pltpu.make_async_copy(
                        source.at[piece, :, pl.ds(first, half)],
                        buf.at[slot, :, pl.ds(side * half, half)],
                        load_sem.at[slot, kind, side],
                    )
                )
        return copies

    def results(j):
        slot = lax.rem(j, 2)
        return [
            pltpu.make_async_copy(active.at[slot], active_out.at[j], chunk_sem.at[slot, 0]),
            pltpu.make_async_copy(slope.at[slot], slope_out.at[j], chunk_sem.at[slot, 1]),
        ]

    def chunk_of(first_chunk):
        def chunk(i):
            j = first_chunk + i
            slot = lax.rem(j, 2)

            @pl.when(i == 0)
            def _():
                lines.far_copy(1 + first_chunk // per_piece).wait_recv()
                for copy in loads(j):
                    copy.start()

            for copy in loads(j):
                copy.wait()

            @pl.when(i + 1 < per_piece)
            def _():
                for copy in loads(j + 1):
                    copy.start()

            @pl.when(j >= 2)
            def _():
                for copy in results(j - 2):
                    copy.wait()

            for step in range(half_rows // TILE):
                at = slice(step * TILE, (step + 1) * TILE)
                value = dot_nn(low[at, :], expand_buf[slot]) + hidden_bias_ref[j]
                below, bell = normal_cells(value)
                held = (value * below).astype(LOW)
                active[slot, at, :] = held
                slope[slot, at, :] = (below + value * bell * 0.3989422804014327).astype(LOW)
                acc[at, :] += dot_nt(held, reduce_buf[slot])
            for copy in results(j):
                copy.start()

        return chunk

    phase("feed", per_piece, chunk_of(0))
    phase("last", per_piece, chunk_of(per_piece))
    leave(acc, acc_out)
    for p in range(pieces):
        lines.finish(p)
    for j in (chunks - 2, chunks - 1):
        for copy in results(j):
            copy.wait()
    for copy in leaving:
        copy.wait()


def front(shards, tokens, cotangent, own_of, dealt_of, bias, score_bias, vectors, bias_own, bias_far, parts):
    pieces, shard_rows, columns = shards.shape
    half_rows, width = tokens.shape
    rows, pairs, depth = 2 * half_rows, bias.shape[0], parts // 4
    inner, half = pairs * PAIR, 256
    chunks, both = bias_own.shape[0] // half, 2 * half
    hidden_bias = jnp.concatenate(
        [bias_far.reshape(chunks, 1, half), bias_own.reshape(chunks, 1, half)], axis=2
    )
    shape, sem = jax.ShapeDtypeStruct, pltpu.SemaphoreType.DMA
    vmem, anywhere = pl.BlockSpec(memory_space=pltpu.VMEM), pl.BlockSpec(memory_space=pl.ANY)
    held = [
        ((pairs, rows, 3 * PAIR), LOW),
        ((width, rows), LOW),
        ((half_rows, width), LOW),
        ((rows, inner), LOW),
        ((pairs, 8, rows), WIDE),
        ((half_rows, width), WIDE),
        ((half_rows, width), WIDE),
        ((half_rows, 128), WIDE),
        ((width, half_rows), LOW),
        ((chunks, half_rows, both), LOW),
        ((chunks, half_rows, both), LOW),
        ((half_rows, inner), LOW),
    ]
    return pl.pallas_call(
        functools.partial(front_kernel, depth),
        in_specs=[*[anywhere] * 3, *[vmem] * 6],
        out_specs=[anywhere] * 14,
        out_shape=[
            shape((pieces, parts * shard_rows, columns), LOW),
            shape((pieces, parts * shard_rows, columns), LOW),
            *[shape(*one) for one in held],
        ],
        scratch_shapes=[
            pltpu.VMEM((2, half_rows, width), LOW),
            pltpu.VMEM((2, half_rows, width), LOW),
            pltpu.VMEM((rows, width), LOW),
            pltpu.VMEM((width, rows), LOW),
            pltpu.VMEM((half_rows, width), LOW),
            pltpu.VMEM((width, pairs * 3 * PAIR), LOW),
            pltpu.VMEM((pairs, rows, 3 * PAIR), LOW),
            pltpu.VMEM((rows, inner), LOW),
            pltpu.VMEM((pairs, 8, rows), WIDE),
            pltpu.VMEM((half_rows, width), WIDE),
            pltpu.VMEM((half_rows, width), WIDE),
            pltpu.VMEM((half_rows, 128), WIDE),
            pltpu.VMEM((half_rows, width), LOW),
            pltpu.VMEM((width, half_rows), LOW),
            pltpu.VMEM((2, half_rows, both), LOW),
            pltpu.VMEM((2, half_rows, both), LOW),
            pltpu.VMEM((half_rows, inner), LOW),
            pltpu.VMEM((width, inner), LOW),
            pltpu.VMEM((width, inner), LOW),
            pltpu.VMEM((2, width, both), LOW),
            pltpu.VMEM((2, width, both), LOW),
            sem((pieces + 2,)),
            sem((3, 2)),
            sem((10,)),
            sem((2, 2, 2)),
            sem((2, 2)),
            *Gather.semaphores(depth, pieces),
        ],
        compiler_params=pltpu.CompilerParams(
            collective_id=0, has_side_effects=True, vmem_limit_bytes=62 * MIB
        ),
    )(
        shards, tokens, cotangent, own_of[:, None], dealt_of[:, None], bias, score_bias, vectors, hidden_bias
    )


def normal_cells(value):
    bell = jnp.exp(value * value * -0.5)
    t = 1.0 / (1.0 + 0.39 * 0.7071067811865476 * jnp.abs(value))
    tail = -0.2275377237624147
    for factor in (
        0.8866668177122106,
        -0.6354042576077721,
        0.649562611731642,
        0.0913871257655044,
        0.23532542445435511,
    ):
        tail = tail * t + factor
    tail = 0.5 * tail * t * bell
    return jnp.where(value < 0.0, tail, 1.0 - tail), bell


def norm(values):
    center = values - jnp.mean(values, axis=1, keepdims=True)
    spread = jnp.mean(center * center, axis=1, keepdims=True)
    scale = lax.rsqrt(spread + norm_epsilon)
    return center * scale, scale


def norm_back(scaled, unit, scale):
    return scale * (
        scaled
        - jnp.mean(scaled, axis=1, keepdims=True)
        - unit * jnp.mean(scaled * unit, axis=1, keepdims=True)
    )


def feed_kernel(
    context_ref, merge_ref, merge_far_ref, whole_ref, far_ref, hidden_ref, upstream_ref, vectors_ref, bias_ref,
    encoded_ref, branch_ref, grad_ref, merge_grad_ref, expand_grad_ref, reduce_grad_ref, sums_ref, hidden_sums_ref,
    own_ctx, far_ctx, acc, normal, inverse, low, turned, late, late_turned, active, slope, inner_grad,
    expand_buf, reduce_buf, arrived, leaving, kept, done, grad_own, grad_far, merge_send, merge_recv,
    ctx_sem, load_sem, send_sem, recv_sem, out_sem, last_sem,
):
    rows = hidden_ref.shape[0]
    chunks, _, both = bias_ref.shape
    half = both // 2
    per_piece = whole_ref.shape[2] // (2 * half)
    member = lax.axis_index("tensor")
    peer = {"tensor": 1 - member}
    tall, short = 256, 128
    width = hidden_ref.shape[1]

    def across(source, target, send, receive):
        return pltpu.make_async_remote_copy(
            src_ref=source,
            dst_ref=target,
            send_sem=send,
            recv_sem=receive,
            device_id=peer,
            device_id_type=MESH,
        )

    def rows_of(which):
        return pl.ds(pl.multiple_of(which * rows, rows), rows)

    def tile(step, size):
        return pl.ds(pl.multiple_of(step * size, size), size)

    def loads(j, slot):
        piece, at = 1 + j // per_piece, lax.rem(j, per_piece) * half
        copies = []
        for kind, buf in enumerate((expand_buf, reduce_buf)):
            first = pl.multiple_of(at + kind * per_piece * half, half)
            for side, source in enumerate((far_ref, whole_ref)):
                copies.append(
                    pltpu.make_async_copy(
                        source.at[piece, :, pl.ds(first, half)],
                        buf.at[slot, :, pl.ds(side * half, half)],
                        load_sem.at[slot, kind, side],
                    )
                )
        return copies

    for copy in loads(0, 0):
        copy.start()
    barrier = pltpu.get_barrier_semaphore()
    pl.semaphore_signal(barrier, inc=1, device_id=peer, device_id_type=MESH)
    pl.semaphore_wait(barrier, 1)
    out_ctx = across(context_ref.at[rows_of(1 - member)], far_ctx, ctx_sem.at[0], ctx_sem.at[1])
    out_ctx.start()
    in_ctx = pltpu.make_async_copy(context_ref.at[rows_of(member)], own_ctx, ctx_sem.at[2])
    in_ctx.start()
    sums_ref[...] = jnp.zeros_like(sums_ref)
    in_ctx.wait()
    out_ctx.wait()

    def add_sum(row, values):
        sums_ref[row : row + 1, :] += jnp.sum(values, axis=0, keepdims=True)

    @pl.loop(0, rows // short)
    def _(step):
        at = tile(step, short)
        branch = dot_nt(own_ctx[at, :], merge_ref[...]) + dot_nt(far_ctx[at, :], merge_far_ref[...])
        unit, scale = norm(hidden_ref[at, :].astype(WIDE) + branch + vectors_ref[2:3, :])
        normed = unit * vectors_ref[3:4, :] + vectors_ref[4:5, :]
        normal[at, :] = unit
        inverse[at, :] = jnp.broadcast_to(scale, (short, 128))
        low[at, :] = normed.astype(LOW)
        turned[:, at] = normed.T.astype(LOW)
        acc[at, :] = normed + vectors_ref[5:6, :]

    @pl.loop(0, chunks)
    def _(j):
        slot = lax.rem(j, 2)
        for copy in loads(j, slot):
            copy.wait()

        @pl.when(j + 1 < chunks)
        def _():
            for copy in loads(j + 1, 1 - slot):
                copy.start()

        for step in range(rows // tall):
            at = slice(step * tall, (step + 1) * tall)
            inner = dot_nn(low[at, :], expand_buf[slot]) + bias_ref[j]
            below, bell = normal_cells(inner)
            held = (inner * below).astype(LOW)
            active[j, at, :] = held
            slope[j, at, :] = (below + inner * bell * 0.3989422804014327).astype(LOW)
            acc[at, :] += dot_nt(held, reduce_buf[slot])

    for copy in loads(0, 0):
        copy.start()

    @pl.loop(0, rows // short)
    def _(step):
        at = tile(step, short)
        unit, scale = norm(acc[at, :])
        encoded_ref[at, :] = (unit * vectors_ref[6:7, :] + vectors_ref[7:8, :]).astype(LOW)
        upper = upstream_ref[at, :].astype(WIDE)
        add_sum(6, upper * unit)
        add_sum(7, upper)
        grad = norm_back(upper * vectors_ref[6:7, :], unit, scale)
        grad_low = grad.astype(LOW)
        add_sum(5, grad_low.astype(WIDE))
        acc[at, :] = grad
        late[at, :] = grad_low
        late_turned[:, at] = grad.T.astype(LOW)

    def send(j, kind):
        return across(
            leaving.at[lax.rem(j, 2), kind],
            arrived.at[lax.rem(j, 4), kind],
            send_sem.at[lax.rem(j, 2), kind],
            recv_sem.at[lax.rem(j, 4), kind],
        )

    def store(j, kind):
        target = (expand_grad_ref, reduce_grad_ref)[kind]
        cols = pl.ds(pl.multiple_of(j * half, half), half)
        return pltpu.make_async_copy(
            done.at[lax.rem(j, 2), kind], target.at[:, cols], out_sem.at[lax.rem(j, 2), kind]
        )

    def finish(j):
        for kind in range(2):
            send(j, kind).wait_recv()

            @pl.when(j >= 2)
            def _():
                store(j - 2, kind).wait()

            @pl.loop(0, width // tall)
            def _(step):
                at = tile(step, tall)
                done[lax.rem(j, 2), kind, at, :] = (
                    kept[lax.rem(j, 2), kind, at, :]
                    + arrived[lax.rem(j, 4), kind, at, :].astype(WIDE)
                ).astype(LOW)

            store(j, kind).start()

    @pl.loop(0, chunks)
    def _(j):
        slot = lax.rem(j, 2)
        for copy in loads(j, slot):
            copy.wait()

        @pl.when(j + 1 < chunks)
        def _():
            for copy in loads(j + 1, 1 - slot):
                copy.start()

        total = jnp.zeros((1, both), WIDE)
        for step in range(rows // tall):
            at = slice(step * tall, (step + 1) * tall)
            grad = dot_nn(late[at, :], reduce_buf[slot]) * slope[j, at, :].astype(WIDE)
            grad = grad.astype(LOW)
            inner_grad[at, :] = grad
            total = total + jnp.sum(grad.astype(WIDE), axis=0, keepdims=True)
            acc[at, :] += dot_nt(grad, expand_buf[slot])
        hidden_sums_ref[j] = total

        @pl.when(j >= 2)
        def _():
            for kind in range(2):
                send(j - 2, kind).wait_send()

        for kind, (left, right) in enumerate(((turned, inner_grad), (late_turned, active.at[j]))):
            for step in range(width // tall):
                at = slice(step * tall, (step + 1) * tall)
                part = dot_nn(left[at, :], right[...])
                leaving[slot, kind, at, :] = part[:, 0:half].astype(LOW)
                kept[slot, kind, at, :] = part[:, half:both]
            send(j, kind).start()

        @pl.when(j >= 1)
        def _():
            finish(j - 1)

    @pl.loop(0, rows // short)
    def _(step):
        at = tile(step, short)
        grad = acc[at, :]
        unit = normal[at, :]
        add_sum(3, grad * unit)
        add_sum(4, grad)
        branch_grad = norm_back(grad * vectors_ref[3:4, :], unit, inverse[at, 0:1])
        branch_low = branch_grad.astype(LOW)
        add_sum(2, branch_low.astype(WIDE))
        branch_ref[at, :] = branch_grad
        turned[:, at] = branch_grad.T.astype(LOW)
        grad_far[at, :] = dot_nn(branch_low, merge_far_ref[...]).astype(LOW)
        grad_own[at, :] = dot_nn(branch_low, merge_ref[...]).astype(LOW)

    out_grad = across(grad_far, grad_ref.at[rows_of(member)], ctx_sem.at[0], ctx_sem.at[1])
    out_grad.start()
    in_grad = pltpu.make_async_copy(grad_own, grad_ref.at[rows_of(member)], ctx_sem.at[2])
    in_grad.start()
    for step in range(width // tall):
        at = slice(step * tall, (step + 1) * tall)
        merge_send[at, :] = dot_nn(turned[at, :], far_ctx[...]).astype(LOW)
    out_merge = across(merge_send, merge_recv, last_sem.at[0], last_sem.at[1])
    out_merge.start()
    finish(chunks - 1)
    for kind in range(2):
        send(chunks - 2, kind).wait_send()
        send(chunks - 1, kind).wait_send()
        store(chunks - 2, kind).wait()
        store(chunks - 1, kind).wait()
    out_merge.wait()
    for step in range(width // tall):
        at = slice(step * tall, (step + 1) * tall)
        merge_grad_ref[at, :] = (
            dot_nn(turned[at, :], own_ctx[...]) + merge_recv[at, :].astype(WIDE)
        ).astype(LOW)
    out_grad.wait()
    in_grad.wait()


def feed_block(context, whole, far, hidden_own, upstream, vectors, bias_own, bias_far):
    total_rows, inner = context.shape
    rows, width = hidden_own.shape
    hidden = bias_own.shape[0]
    merge, merge_far = whole[0, :, -inner:], far[0, :, -inner:]
    half = 256
    chunks = hidden // half
    both = 2 * half
    bias = jnp.concatenate(
        [bias_far.reshape(chunks, 1, half), bias_own.reshape(chunks, 1, half)], axis=2
    )
    vmem, anywhere = pl.BlockSpec(memory_space=pltpu.VMEM), pl.BlockSpec(memory_space=pl.ANY)
    sem = pltpu.SemaphoreType.DMA
    shape = jax.ShapeDtypeStruct
    *results, hidden_sums = pl.pallas_call(
        feed_kernel,
        in_specs=[anywhere, vmem, vmem, *[anywhere] * 2, *[vmem] * 4],
        out_specs=[vmem, vmem, anywhere, vmem, anywhere, anywhere, vmem, vmem],
        out_shape=[
            shape((rows, width), LOW),
            shape((rows, width), WIDE),
            shape((total_rows, inner), LOW),
            shape((width, inner), LOW),
            shape((width, hidden), LOW),
            shape((width, hidden), LOW),
            shape((8, width), WIDE),
            shape((chunks, 1, both), WIDE),
        ],
        scratch_shapes=[
            pltpu.VMEM((rows, inner), LOW),
            pltpu.VMEM((rows, inner), LOW),
            pltpu.VMEM((rows, width), WIDE),
            pltpu.VMEM((rows, width), WIDE),
            pltpu.VMEM((rows, 128), WIDE),
            pltpu.VMEM((rows, width), LOW),
            pltpu.VMEM((width, rows), LOW),
            pltpu.VMEM((rows, width), LOW),
            pltpu.VMEM((width, rows), LOW),
            pltpu.VMEM((chunks, rows, both), LOW),
            pltpu.VMEM((chunks, rows, both), LOW),
            pltpu.VMEM((rows, both), LOW),
            pltpu.VMEM((2, width, both), LOW),
            pltpu.VMEM((2, width, both), LOW),
            pltpu.VMEM((4, 2, width, half), LOW),
            pltpu.VMEM((2, 2, width, half), LOW),
            pltpu.VMEM((2, 2, width, half), WIDE),
            pltpu.VMEM((2, 2, width, half), LOW),
            pltpu.VMEM((rows, inner), LOW),
            pltpu.VMEM((rows, inner), LOW),
            pltpu.VMEM((width, inner), LOW),
            pltpu.VMEM((width, inner), LOW),
            sem((3,)),
            sem((2, 2, 2)),
            sem((2, 2)),
            sem((4, 2)),
            sem((2, 2)),
            sem((2,)),
        ],
        compiler_params=pltpu.CompilerParams(
            collective_id=2, has_side_effects=True, vmem_limit_bytes=60 * MIB
        ),
        cost_estimate=pl.CostEstimate(
            flops=12 * rows * width * 2 * hidden, bytes_accessed=8 * width * hidden * 4, transcendentals=0
        ),
    )(context, merge, merge_far, whole, far, hidden_own, upstream, vectors, bias)
    hidden_far = hidden_sums[:, 0, :half].reshape(-1)
    hidden_near = hidden_sums[:, 0, half:].reshape(-1)
    return (*results, hidden_near, hidden_far)


class Scatter:
    buffers = 8

    def __init__(self, depth, grads, shards, buffers, sems):
        self.depth, self.grads, self.shards = depth, grads, shards
        self.held = [buffers[8 * p : 8 * p + 8] for p in range(len(grads))]
        self.me, self.z, self.y, self.x = place()
        self.x_peer = self.z * 4 + self.y * 2 + 1 - self.x
        self.y_peer = self.z * 4 + (1 - self.y) * 2 + self.x
        self.rows = grads[0].shape[0] // (4 * depth)
        (
            self.a1_send, self.a1_recv, self.a2_send, self.a2_recv, self.b2_send, self.b2_recv, self.b1_send, self.b1_recv,
            self.z_send, self.z_recv, self.zc_send, self.zc_recv, self.c_send, self.c_recv,
        ) = sems

    @staticmethod
    def scratch(depth, rows, classes):
        found = []
        for a, b, c in classes:
            found += [
                pltpu.VMEM((depth, 2 * rows, a), LOW),
                pltpu.VMEM((depth, 2, rows, b), LOW),
                pltpu.VMEM((depth, rows, a), LOW),
                pltpu.VMEM((depth, rows, b), LOW),
                pltpu.VMEM((depth + 1, rows, a + b), LOW),
                pltpu.VMEM((depth + 1, 4 * rows, c), LOW),
                pltpu.VMEM((2 * rows, c), LOW),
                pltpu.VMEM((rows, c), LOW),
            ]
        return found

    @staticmethod
    def semaphores(depth, pieces):
        sem = pltpu.SemaphoreType.DMA
        return [
            *[sem((pieces, depth))] * 6,
            *[sem((pieces, depth, 2))] * 2,
            *[sem((pieces, depth)), sem((pieces, depth + 1))] * 2,
            sem((pieces, 2)),
            sem((pieces, 2)),
        ]

    def columns(self, p):
        a, b, c = (self.held[p][i].shape[-1] for i in (0, 1, 5))
        return pl.ds(0, a), pl.ds(a, b), pl.ds(a + b, c)

    def block(self, zb, yb, xb):
        return zb * 4 + yb * 2 + xb

    def span(self, block, count=1):
        return pl.ds(pl.multiple_of(block * self.rows, self.rows), count * self.rows)

    def add(self, count, put, *terms):
        @pl.loop(0, count // 16)
        def _(step):
            at = pl.multiple_of(step * 16, 16)
            total = terms[0](at)
            for term in terms[1:]:
                total = total + term(at)
            put(at, total)

    def a1(self, p, zb):
        return remote(
            self.grads[p].at[self.span(self.block(zb, 1 - self.y, 0), 2), self.columns(p)[0]],
            self.held[p][0].at[zb],
            self.a1_send.at[p, zb],
            self.a1_recv.at[p, zb],
            self.y_peer,
        )

    def b1(self, p, zb, yb):
        return remote(
            self.grads[p].at[self.span(self.block(zb, yb, 1 - self.x)), self.columns(p)[1]],
            self.held[p][1].at[zb, yb],
            self.b1_send.at[p, zb, yb],
            self.b1_recv.at[p, zb, yb],
            self.x_peer,
        )

    def a2(self, p, zb):
        return remote(
            self.held[p][0].at[zb, self.span(1 - self.x)],
            self.held[p][2].at[zb],
            self.a2_send.at[p, zb],
            self.a2_recv.at[p, zb],
            self.x_peer,
        )

    def b2(self, p, zb):
        return remote(
            self.held[p][1].at[zb, 1 - self.y],
            self.held[p][3].at[zb],
            self.b2_send.at[p, zb],
            self.b2_recv.at[p, zb],
            self.y_peer,
        )

    def slot(self, zb, way):
        return zb if way > 0 else zb + (self.depth - zb) * jnp.where(zb == self.z - 1, 1, 0)

    def z_copy(self, p, zb, way):
        slot = self.slot(zb, way)
        return remote(
            self.held[p][4].at[zb],
            self.held[p][4].at[slot],
            self.z_send.at[p, zb],
            self.z_recv.at[p, slot],
            self.me + 4 * way,
        )

    def zc_copy(self, p, zb, way, first):
        slot = self.slot(zb, way)
        source = self.held[p][5].at[zb]
        if first:
            source = self.grads[p].at[self.span(zb * 4, 4), self.columns(p)[2]]
        return remote(
            source,
            self.held[p][5].at[slot],
            self.zc_send.at[p, zb],
            self.zc_recv.at[p, slot],
            self.me + 4 * way,
        )

    def arrived(self, ref, sem, slot):
        part = ref.at[slot]
        remote(part, part, sem, sem, self.me).wait_recv()

    def cy(self, p):
        return remote(
            self.held[p][5].at[self.z, self.span(2 * (1 - self.y), 2)],
            self.held[p][6],
            self.c_send.at[p, 0],
            self.c_recv.at[p, 0],
            self.y_peer,
        )

    def cx(self, p):
        return remote(
            self.held[p][5].at[self.z, self.span(2 * self.y + 1 - self.x)],
            self.held[p][7],
            self.c_send.at[p, 1],
            self.c_recv.at[p, 1],
            self.x_peer,
        )

    def grad(self, p, block, columns):
        def term(at):
            first = pl.multiple_of(block * self.rows + at, 16)
            return self.grads[p][pl.ds(first, 16), columns].astype(WIDE)

        return term

    def part(self, ref, lead, block, columns=None):
        columns = slice(None) if columns is None else columns

        def term(at):
            first = pl.multiple_of(block * self.rows + at, 16)
            return ref[(*lead, pl.ds(first, 16), columns)].astype(WIDE)

        return term

    def put(self, ref, lead, block, columns=None):
        columns = slice(None) if columns is None else columns

        def act(at, total):
            first = pl.multiple_of(block * self.rows + at, 16)
            ref[(*lead, pl.ds(first, 16), columns)] = total.astype(ref.dtype)

        return act

    def open(self, p, zb):
        self.a1(p, zb).start()
        self.b1(p, zb, 0).start()
        self.b1(p, zb, 1).start()

    def first(self, p, zb):
        z, y, x = self.z, self.y, self.x
        a, b, _ = self.columns(p)
        r1a, r1b = self.held[p][0], self.held[p][1]
        self.a1(p, zb).wait_recv()
        self.add(
            self.rows,
            self.put(r1a, (zb,), 1 - x),
            self.part(r1a, (zb,), 1 - x),
            self.grad(p, self.block(zb, y, 1 - x), a),
        )
        self.a2(p, zb).start()
        self.b1(p, zb, 0).wait_recv()
        self.b1(p, zb, 1).wait_recv()
        self.add(
            self.rows,
            self.put(r1b, (zb, 1 - y), 0),
            self.part(r1b, (zb, 1 - y), 0),
            self.grad(p, self.block(zb, 1 - y, x), b),
        )
        self.b2(p, zb).start()

    def terms(self, p, zb):
        z, y, x = self.z, self.y, self.x
        a, b, _ = self.columns(p)
        r1a, r1b, r2a, r2b = self.held[p][:4]
        own = self.block(zb, y, x)
        return (
            [self.grad(p, own, a), self.part(r1a, (zb,), x), self.part(r2a, (zb,), 0)],
            [self.grad(p, own, b), self.part(r1b, (zb, y), 0), self.part(r2b, (zb,), 0)],
        )

    def pass_on(self, p, zb, way):
        a, b, _ = self.columns(p)
        rz = self.held[p][4]
        self.a2(p, zb).wait_recv()
        self.b2(p, zb).wait_recv()
        from_line = (self.z - way >= 0) & (self.z - way < self.depth)

        @pl.when(from_line)
        def _():
            self.arrived(rz, self.z_recv.at[p, zb], zb)
            for terms, columns in zip(self.terms(p, zb), (a, b), strict=True):
                self.add(
                    self.rows,
                    self.put(rz, (zb,), 0, columns),
                    *terms,
                    self.part(rz, (zb,), 0, columns),
                )

        @pl.when(jnp.logical_not(from_line))
        def _():
            for terms, columns in zip(self.terms(p, zb), (a, b), strict=True):
                self.add(self.rows, self.put(rz, (zb,), 0, columns), *terms)

        self.z_copy(p, zb, way).start()

    def pass_c(self, p, zb, way):
        c = self.columns(p)[2]
        rc = self.held[p][5]
        from_line = (self.z - way >= 0) & (self.z - way < self.depth)

        @pl.when(from_line)
        def _():
            self.arrived(rc, self.zc_recv.at[p, zb], zb)
            self.add(
                4 * self.rows,
                self.put(rc, (zb,), 0),
                self.part(rc, (zb,), 0),
                self.grad(p, zb * 4, c),
            )
            self.zc_copy(p, zb, way, False).start()

        @pl.when(jnp.logical_not(from_line))
        def _():
            self.zc_copy(p, zb, way, True).start()

    def own_c(self, p):
        z, depth = self.z, self.depth
        c = self.columns(p)[2]
        rc = self.held[p][5]
        grad = self.grad(p, z * 4, c)
        lower, upper = self.part(rc, (z,), 0), self.part(rc, (depth,), 0)
        put = self.put(rc, (z,), 0)

        @pl.when(z > 0)
        def _():
            self.arrived(rc, self.zc_recv.at[p, z], z)

        @pl.when(z < depth - 1)
        def _():
            self.arrived(rc, self.zc_recv.at[p, depth], depth)

        @pl.when((z > 0) & (z < depth - 1))
        def _():
            self.add(4 * self.rows, put, grad, lower, upper)

        @pl.when(z == 0)
        def _():
            self.add(4 * self.rows, put, grad, upper)

        @pl.when(z == depth - 1)
        def _():
            self.add(4 * self.rows, put, grad, lower)

        self.cy(p).start()

    def turn_c(self, p):
        rc, rcy = self.held[p][5], self.held[p][6]
        self.cy(p).wait_recv()
        self.add(
            2 * self.rows,
            self.put(rc, (self.z,), 2 * self.y),
            self.part(rc, (self.z,), 2 * self.y),
            self.part(rcy, (), 0),
        )
        self.cx(p).start()

    def close(self, p):
        z, depth = self.z, self.depth
        a, b, c = self.columns(p)
        rz, rc, rcx = self.held[p][4], self.held[p][5], self.held[p][7]
        self.a2(p, z).wait_recv()
        self.b2(p, z).wait_recv()

        @pl.when(z > 0)
        def _():
            self.arrived(rz, self.z_recv.at[p, z], z)

        @pl.when(z < depth - 1)
        def _():
            self.arrived(rz, self.z_recv.at[p, depth], depth)

        def total(*slots):
            for terms, columns in zip(self.terms(p, z), (a, b), strict=True):
                lines = [self.part(rz, (slot,), 0, columns) for slot in slots]
                self.add(self.rows, self.put(self.shards[p], (), 0, columns), *terms, *lines)

        pl.when((z > 0) & (z < depth - 1))(lambda: total(z, depth))
        pl.when(z == 0)(lambda: total(depth))
        pl.when(z == depth - 1)(lambda: total(z))
        self.cx(p).wait_recv()
        self.add(
            self.rows,
            self.put(self.shards[p], (), 0, c),
            self.part(rc, (z,), 2 * self.y + self.x),
            self.part(rcx, (), 0),
        )

    def at_step(self, step, act):
        z, depth = self.z, self.depth
        if step < 0:
            act(z, 0)
            return
        for zb, valid, way in (
            (z + 1 + step, z + 1 + step < depth, 1),
            (z - 1 - step, z - 1 - step >= 0, -1),
        ):
            pl.when(valid)(functools.partial(act, zb, way))

    def stage(self, p, s):
        last = self.depth - 2

        def opened(step):
            self.at_step(step, lambda zb, way: self.open(p, zb))

        def added(step):
            self.at_step(step, lambda zb, way: self.first(p, zb))

        def passed(step):
            self.at_step(step, lambda zb, way: self.pass_on(p, zb, way))

        def passed_c(step):
            self.at_step(step, lambda zb, way: self.pass_c(p, zb, way))

        if s == 0:
            opened(last)
            opened(last - 1)
            passed_c(last)
            return
        if s <= last + 2:
            added(last + 1 - s)
        if last - 1 - s >= -1:
            opened(last - 1 - s)
        if last - s >= 0:
            passed_c(last - s)
        if s >= 2 and last + 2 - s >= 0:
            passed(last + 2 - s)
        if s == last + 1:
            self.own_c(p)
        if s == last + 2:
            self.turn_c(p)
        if s == last + 3:
            self.close(p)

    def sent(self, p):
        def line(zb, way):
            from_line = (self.z - way >= 0) & (self.z - way < self.depth)
            self.z_copy(p, zb, way).wait_send()
            pl.when(from_line)(lambda: self.zc_copy(p, zb, way, False).wait_send())
            pl.when(jnp.logical_not(from_line))(lambda: self.zc_copy(p, zb, way, True).wait_send())

        for zb in range(self.depth):
            self.a1(p, zb).wait_send()
            self.b1(p, zb, 0).wait_send()
            self.b1(p, zb, 1).wait_send()
            self.a2(p, zb).wait_send()
            self.b2(p, zb).wait_send()
        for step in range(self.depth - 1):
            self.at_step(step, line)
        self.cy(p).wait_send()
        self.cx(p).wait_send()


class SmallSum:
    def __init__(self, lines, buffer, send, recv):
        member = lax.axis_index("tensor")
        self.partners = [{"tensor": 1 - member}, {"dp": lines.x_peer}, {"dp": lines.y_peer}]
        for level in range(lines.depth.bit_length() - 1):
            reach = 1 << level
            way = 1 - 2 * ((lines.z // reach) % 2)
            self.partners.append({"dp": lines.me + 4 * reach * way})
        self.buffer, self.send, self.recv = buffer, send, recv

    def copy(self, step):
        return pltpu.make_async_remote_copy(
            src_ref=self.buffer.at[step],
            dst_ref=self.buffer.at[len(self.partners) + 1 + step],
            send_sem=self.send.at[step],
            recv_sem=self.recv.at[step],
            device_id=self.partners[step],
            device_id_type=MESH,
        )

    def step(self, step):
        if step:
            self.copy(step - 1).wait_recv()
            self.buffer[step] = self.buffer[step - 1] + self.buffer[len(self.partners) + step]
        if step < len(self.partners):
            self.copy(step).start()

    def sent(self):
        for step in range(len(self.partners)):
            self.copy(step).wait_send()


def back_kernel(
    depth, acc_in, turned_in, upstream_in, normal_in, inverse_in, active_in, slope_in, far_ctx_in, context_in, qkv_in,
    totals_in, hidden_turned_in, whole_ref, far_ref, vectors_ref, score_bias_in, from_own_in, from_dealt_in,
    encoded_ref, input_ref, shard0, shard1, shard2, shard3, small_ref, enc_pair, grad_ref, input_far,
    acc, arrived, merge_recv, small, grad0, grad1, grad2, grad3, *rest,
):
    buffers, rest = rest[: 4 * Scatter.buffers], rest[4 * Scatter.buffers :]
    small_send, small_recv, in_sem, load_sem, ctx_sem, far_send, far_recv, merge_sem, enc_sem, input_sem, *sems = rest
    grads = (grad0, grad1, grad2, grad3)
    lines = Scatter(depth, grads, (shard0, shard1, shard2, shard3), buffers, sems)
    sums = SmallSum(lines, small, small_send, small_recv)
    member = lax.axis_index("tensor")
    rows, width = acc.shape
    total_rows = 2 * rows
    chunks, _, both = active_in.shape
    half = both // 2
    per_piece = chunks // 2
    pairs = qkv_in.shape[0]
    inner = pairs * PAIR
    tall, short = 256, 128

    def rows_of(which):
        return pl.ds(pl.multiple_of(which * rows, rows), rows)

    def tile(step, size):
        return pl.ds(pl.multiple_of(step * size, size), size)

    def fetch(source, target, sem):
        return pltpu.make_async_copy(source, target, in_sem.at[sem])

    def stage(p, s):
        return functools.partial(lines.stage, p, s)

    def add_sum(row, values):
        small[0, row : row + 1, :] += jnp.sum(values, axis=0, keepdims=True)

    acc_copy = fetch(acc_in, acc, 0)
    acc_copy.start()
    greet_line(
        lines.me, lines.z, lines.y, lines.x, depth, [sums.partners[0], *sums.partners[3:]]
    )
    small[0] = jnp.zeros(small.shape[1:], WIDE)

    def feed_phase(late, late_turned, turned, upstream, active, slope, inner_grad, expand_buf, reduce_buf, leaving, encoded):
        def loads(j, slot):
            piece, at = 1 + j // per_piece, lax.rem(j, per_piece) * half
            copies = [
                pltpu.make_async_copy(active_in.at[j], active.at[slot], load_sem.at[slot, 4]),
                pltpu.make_async_copy(slope_in.at[j], slope.at[slot], load_sem.at[slot, 5]),
            ]
            for kind, buf in enumerate((expand_buf, reduce_buf)):
                first = pl.multiple_of(at + kind * per_piece * half, half)
                for side, source in enumerate((far_ref, whole_ref)):
                    copies.append(
                        pltpu.make_async_copy(
                            source.at[piece, :, pl.ds(first, half)],
                            buf.at[slot, :, pl.ds(side * half, half)],
                            load_sem.at[slot, 2 * kind + side],
                        )
                    )
            return copies

        fetches = [fetch(upstream_in, upstream, 1), fetch(turned_in, turned, 2)]
        for copy in fetches:
            copy.start()
        for copy in loads(0, 0):
            copy.start()
        acc_copy.wait()
        for copy in fetches:
            copy.wait()

        @pl.loop(0, rows // short)
        def _(step):
            at = tile(step, short)
            unit, scale = norm(acc[at, :])
            encoded[at, :] = (unit * vectors_ref[6:7, :] + vectors_ref[7:8, :]).astype(LOW)
            upper = upstream[at, :].astype(WIDE)
            add_sum(6, upper * unit)
            add_sum(7, upper)
            grad = norm_back(upper * vectors_ref[6:7, :], unit, scale)
            grad_low = grad.astype(LOW)
            add_sum(5, grad_low.astype(WIDE))
            acc[at, :] = grad
            late[at, :] = grad_low
            late_turned[:, at] = grad.T.astype(LOW)

        enc_near = pltpu.make_async_copy(encoded, enc_pair.at[member], enc_sem.at[2])
        enc_far = other_core(encoded, enc_pair.at[member], enc_sem.at[0], enc_sem.at[1])
        enc_near.start()
        enc_far.start()

        def send(j, kind):
            slot = lax.rem(j, 2)
            return other_core(
                leaving.at[slot, kind],
                arrived.at[slot, kind],
                far_send.at[slot, kind],
                far_recv.at[slot, kind],
            )

        def finish(j):
            for piece in range(2):

                @pl.when(j // per_piece == piece)
                def _():
                    for kind in range(2):
                        send(j, kind).wait_recv()
                        column = (lax.rem(j, per_piece) + kind * per_piece) * half
                        columns = pl.ds(pl.multiple_of(column, half), half)

                        @pl.loop(0, width // 64)
                        def _(step):
                            at = tile(step, 64)
                            grads[piece][at, columns] = (
                                grads[piece][at, columns].astype(WIDE)
                                + arrived[lax.rem(j, 2), kind, at, :].astype(WIDE)
                            ).astype(LOW)

        def chunk(j):
            slot = lax.rem(j, 2)
            for copy in loads(j, slot):
                copy.wait()

            @pl.when(j + 1 < chunks)
            def _():
                for copy in loads(j + 1, 1 - slot):
                    copy.start()

            total = jnp.zeros((1, both), WIDE)
            for step in range(rows // tall):
                at = slice(step * tall, (step + 1) * tall)
                grad = dot_nn(late[at, :], reduce_buf[slot]) * slope[slot, at, :].astype(WIDE)
                grad = grad.astype(LOW)
                inner_grad[at, :] = grad
                total = total + jnp.sum(grad.astype(WIDE), axis=0, keepdims=True)
                acc[at, :] += dot_nt(grad, expand_buf[slot])
            place_in = pl.ds(pl.multiple_of(lax.rem(j, per_piece) * half, half), half)
            for which, side in ((1 - member, 0), (member, half)):
                row = 8 + which * 2 + j // per_piece
                small[0, pl.ds(row, 1), place_in] = total[:, side : side + half]

            @pl.when(j >= 2)
            def _():
                for kind in range(2):
                    send(j - 2, kind).wait_send()

            for kind, (left, right) in enumerate(
                ((turned, inner_grad), (late_turned, active.at[slot]))
            ):
                column = (lax.rem(j, per_piece) + kind * per_piece) * half
                columns = pl.ds(pl.multiple_of(column, half), half)
                for step in range(width // tall):
                    at = slice(step * tall, (step + 1) * tall)
                    part = dot_nn(left[at, :], right[...])
                    leaving[slot, kind, at, :] = part[:, 0:half].astype(LOW)
                    for piece in range(2):

                        @pl.when(j // per_piece == piece)
                        def _():
                            grads[piece][at, columns] = part[:, half:both].astype(LOW)

            @pl.when(j >= 1)
            def _():
                finish(j - 1)

            for kind in range(2):
                send(j, kind).start()

        between = {per_piece + i: [stage(0, i)] for i in range(chunks - per_piece)}
        looped(chunks, chunk, between)
        finish(chunks - 1)
        for kind in range(2):
            send(chunks - 2, kind).wait_send()
            send(chunks - 1, kind).wait_send()
        enc_near.wait()
        enc_far.wait()

    pl.run_scoped(
        feed_phase,
        pltpu.VMEM((rows, width), LOW),
        pltpu.VMEM((width, rows), LOW),
        pltpu.VMEM((width, rows), LOW),
        pltpu.VMEM((rows, width), LOW),
        pltpu.VMEM((2, rows, both), LOW),
        pltpu.VMEM((2, rows, both), LOW),
        pltpu.VMEM((rows, both), LOW),
        pltpu.VMEM((2, width, both), LOW),
        pltpu.VMEM((2, width, both), LOW),
        pltpu.VMEM((2, 2, width, half), LOW),
        pltpu.VMEM((rows, width), LOW),
    )
    lines.stage(1, 0)
    lines.stage(0, per_piece)

    def merge_phase(normal, inverse, turned, near_ctx, far_ctx, merge, merge_far, grad_own, grad_far, merge_send):
        merge_columns = pl.ds(whole_ref.shape[2] - inner, inner)
        fetches = [
            fetch(normal_in, normal, 0),
            fetch(inverse_in, inverse, 1),
            fetch(context_in.at[rows_of(member)], near_ctx, 2),
            fetch(far_ctx_in, far_ctx, 3),
            fetch(whole_ref.at[0, :, merge_columns], merge, 4),
            fetch(far_ref.at[0, :, merge_columns], merge_far, 5),
        ]
        for copy in fetches:
            copy.start()
        for copy in fetches:
            copy.wait()

        def norm_tile(step):
            at = tile(step, short)
            grad = acc[at, :]
            unit = normal[at, :]
            add_sum(3, grad * unit)
            add_sum(4, grad)
            branch_grad = norm_back(grad * vectors_ref[3:4, :], unit, inverse[at, 0:1])
            branch_low = branch_grad.astype(LOW)
            add_sum(2, branch_low.astype(WIDE))
            acc[at, :] = branch_grad
            turned[:, at] = branch_grad.T.astype(LOW)
            grad_far[at, :] = dot_nn(branch_low, merge_far[...]).astype(LOW)
            grad_own[at, :] = dot_nn(branch_low, merge[...]).astype(LOW)

        looped(rows // short, norm_tile, {2: [stage(1, 1)]})
        out_grad = other_core(grad_far, grad_ref.at[rows_of(member)], ctx_sem.at[0], ctx_sem.at[1])
        in_grad = pltpu.make_async_copy(grad_own, grad_ref.at[rows_of(member)], ctx_sem.at[2])
        out_grad.start()
        in_grad.start()
        for step in range(width // tall):
            at = slice(step * tall, (step + 1) * tall)
            merge_send[at, :] = dot_nn(turned[at, :], far_ctx[...]).astype(LOW)
        out_merge = other_core(merge_send, merge_recv, merge_sem.at[0], merge_sem.at[1])
        out_merge.start()
        lines.stage(0, per_piece + 1)
        out_merge.wait()
        for step in range(width // tall):
            at = slice(step * tall, (step + 1) * tall)
            grad2[at, 0:inner] = (
                dot_nn(turned[at, :], near_ctx[...]) + merge_recv[at, :].astype(WIDE)
            ).astype(LOW)
        out_grad.wait()
        in_grad.wait()

    pl.run_scoped(
        merge_phase,
        pltpu.VMEM((rows, width), WIDE),
        pltpu.VMEM((rows, 128), WIDE),
        pltpu.VMEM((width, rows), LOW),
        pltpu.VMEM((rows, inner), LOW),
        pltpu.VMEM((rows, inner), LOW),
        pltpu.VMEM((width, inner), LOW),
        pltpu.VMEM((width, inner), LOW),
        pltpu.VMEM((rows, inner), LOW),
        pltpu.VMEM((rows, inner), LOW),
        pltpu.VMEM((width, inner), LOW),
    )
    lines.stage(1, 2)

    def last_phase(mixed):
        def attend_phase(qkv, context, upper, totals, score_bias, dots, key_turned, queries, uppers, query_sum, hidden_turned):
            def loads(pair, slot):
                columns = pl.ds(pl.multiple_of(pair * PAIR, PAIR), PAIR)
                return [
                    pltpu.make_async_copy(qkv_in.at[pair], qkv.at[slot], load_sem.at[slot, 0]),
                    pltpu.make_async_copy(
                        context_in.at[:, columns], context.at[slot], load_sem.at[slot, 1]
                    ),
                    pltpu.make_async_copy(
                        grad_ref.at[:, columns], upper.at[slot], load_sem.at[slot, 2]
                    ),
                ]

            fetches = [fetch(totals_in, totals, 0), fetch(score_bias_in, score_bias, 1)]
            for copy in [*loads(0, 0), *fetches]:
                copy.start()
            for copy in fetches:
                copy.wait()
            blocks = ((0, LONGEST), (LONGEST, total_rows - LONGEST))

            def hidden_tile(step, slot):
                return pltpu.make_async_copy(
                    hidden_turned_in.at[tile(step, tall), :],
                    hidden_turned.at[slot],
                    load_sem.at[slot, 3],
                )

            def project(second):
                grad, first = (grad3, 0) if second else (grad2, inner)
                span = (pairs // 2) * 3 * PAIR
                columns = slice(span if second else 0, span * 2 if second else span)
                hidden_tile(0, 0).start()
                for step in range(width // tall):
                    if step + 1 < width // tall:
                        hidden_tile(step + 1, (step + 1) % 2).start()
                    hidden_tile(step, step % 2).wait()
                    grad[step * tall : (step + 1) * tall, first : first + span] = dot_nn(
                        hidden_turned[step % 2], mixed[:, columns]
                    ).astype(LOW)

            def pair_body(pair):
                slot = lax.rem(pair, 2)
                for copy in loads(pair, slot):
                    copy.wait()

                @pl.when(pair + 1 < pairs)
                def _():
                    for copy in loads(pair + 1, 1 - slot):
                        copy.start()

                attend_back_open(
                    qkv.at[slot], context.at[slot], upper.at[slot], dots, key_turned, queries, uppers
                )
                base = pair * 3 * PAIR

                def columns(which):
                    return pl.ds(pl.multiple_of(base + which * PAIR, PAIR), PAIR)

                for begin, size in blocks:
                    block = slice(begin, begin + size)
                    query_sum[:, block] = jnp.zeros((PAIR, size), WIDE)

                    def key_tile(step, begin=begin, size=size):
                        at, key_sum, value_sum = attend_back_tile(
                            qkv.at[slot], score_bias, totals.at[pair], dots, key_turned, queries, uppers, query_sum,
                            begin, size, step,
                        )
                        mixed[at, columns(1)] = key_sum.astype(LOW)
                        mixed[at, columns(2)] = value_sum.astype(LOW)

                    looped(size // TILE, key_tile, {})
                    for act_pair, act in pair_stages.get(begin, ()):
                        pl.when(pair == act_pair)(act)
                    mixed[block, columns(0)] = (
                        (query_sum[:, block] * HEAD_DIM ** (-0.5)).T.astype(LOW)
                    )
                for which, row in ((0, 0), (2, 1)):
                    part = mixed[:, columns(which)].astype(WIDE)
                    spot = pl.multiple_of(member * inner + pair * PAIR, PAIR)
                    small[0, row : row + 1, pl.ds(spot, PAIR)] = jnp.sum(
                        part, axis=0, keepdims=True
                    )

            pair_stages = {
                0: [(0, stage(1, 3)), (1, stage(1, 5)), (2, stage(2, 1)), (3, stage(2, 3))],
                LONGEST: [(0, stage(1, 4)), (2, stage(2, 2)), (3, stage(2, 4))],
            }
            looped(
                pairs,
                pair_body,
                {
                    1: [functools.partial(project, False), stage(2, 0)],
                    3: [functools.partial(project, True), stage(3, 0)],
                },
            )

        pl.run_scoped(
            attend_phase,
            pltpu.VMEM((2, total_rows, 3 * PAIR), LOW),
            pltpu.VMEM((2, total_rows, PAIR), LOW),
            pltpu.VMEM((2, total_rows, PAIR), LOW),
            pltpu.VMEM(totals_in.shape, WIDE),
            pltpu.VMEM(score_bias_in.shape, WIDE),
            pltpu.VMEM((8, total_rows), WIDE),
            pltpu.VMEM((PAIR, total_rows), LOW),
            pltpu.VMEM((2, total_rows, PAIR), LOW),
            pltpu.VMEM((2, total_rows, PAIR), LOW),
            pltpu.VMEM((PAIR, total_rows), WIDE),
            pltpu.VMEM((2, tall, total_rows), LOW),
        )
        sums.step(0)

        def input_phase(weight, terms, from_own, leaving):
            fetches = [
                fetch(whole_ref.at[0, :, pl.ds(0, pairs * 3 * PAIR)], weight, 0),
                fetch(from_own_in, from_own, 1),
            ]
            for copy in fetches:
                copy.start()
            for copy in fetches:
                copy.wait()

            def term_tile(step):
                at = tile(step, tall)
                total = dot_nt(mixed[at, :], weight[...])
                own = rows // tall
                mine = step // own == member

                @pl.when(mine)
                def _():
                    terms[at, :] = (total + acc[tile(lax.rem(step, own), tall), :]).astype(LOW)

                @pl.when(jnp.logical_not(mine))
                def _():
                    terms[at, :] = total.astype(LOW)

            looped(
                total_rows // tall, term_tile, {1: [stage(3, 1)], 3: [stage(2, 5)], 4: [stage(3, 2)]}
            )
            sums.step(1)

            def far_tile(step):
                at = pl.ds(pl.multiple_of((1 - member) * rows + step * tall, tall), tall)
                leaving[tile(step, tall), :] = picked_rows(from_own, terms, at).astype(LOW)

            looped(rows // tall, far_tile, {})
            crossing = other_core(leaving, input_far, input_sem.at[0], input_sem.at[1])
            crossing.start()
            lines.stage(3, 3)
            sums.step(2)

            def near_tile(step):
                at = pl.ds(pl.multiple_of(member * rows + step * tall, tall), tall)
                acc[tile(step, tall), :] = picked_rows(from_own, terms, at)

            looped(rows // tall, near_tile, {})
            lines.stage(3, 4)
            sums.step(3)
            crossing.wait()
            back = fetch(input_far, leaving, 2)
            back.start()
            back.wait()

            def last_tile(step):
                at = tile(step, short)
                input_ref[at, :] = (acc[at, :] + leaving[at, :].astype(WIDE)).astype(LOW)

            looped(rows // short, last_tile, {})

        pl.run_scoped(
            input_phase,
            pltpu.VMEM((width, pairs * 3 * PAIR), LOW),
            pltpu.VMEM((total_rows, width), LOW),
            pltpu.VMEM((total_rows, 1), jnp.int32),
            pltpu.VMEM((rows, width), LOW),
        )

    pl.run_scoped(last_phase, pltpu.VMEM((total_rows, pairs * 3 * PAIR), LOW))

    def encoded_phase(pair, from_dealt):
        fetches = [fetch(enc_pair.at[i], pair.at[rows_of(i)], i) for i in range(2)]
        fetches.append(fetch(from_dealt_in, from_dealt, 2))
        for copy in fetches:
            copy.start()
        for copy in fetches:
            copy.wait()

        def encoded_tile(step):
            at = tile(step, tall)
            encoded_ref[at, :] = picked_rows(from_dealt, pair, at).astype(LOW)

        looped(rows // tall, encoded_tile, {})

    pl.run_scoped(
        encoded_phase, pltpu.VMEM((total_rows, width), LOW), pltpu.VMEM((rows, 1), jnp.int32)
    )
    for step in range(4, len(sums.partners) + 1):
        sums.step(step)
    small_ref[...] = small[len(sums.partners)]
    lines.stage(3, 5)
    sums.sent()
    for p in range(4):
        lines.sent(p)


def picked_rows(index_ref, source, at):
    index = index_ref[at, :]
    places = lax.broadcasted_iota(jnp.int32, (TILE, source.shape[0]), 1)
    return dot_nn(jnp.where(index == places, 1.0, 0.0).astype(LOW), source[...])


def back(middle, context, qkv, totals, hidden_turned, upstream, whole, far, vectors, score_bias, from_own, from_dealt, parts):
    acc, normal, inverse, turned, active, slope, far_ctx = middle
    rows, width = acc.shape
    total_rows, inner = context.shape
    depth, shard_rows = parts // 4, width // parts
    half, pair_span = 256, 3 * PAIR * (qkv.shape[0] // 2)
    piece = whole.shape[2]
    spans = (piece, piece, inner + pair_span, pair_span)
    classes = []
    for span in spans:
        third = max(128, span // 5 // 128 * 128)
        if (span - third) % 256:
            third += 128
        classes.append(((span - third) // 2, (span - third) // 2, third))
    shape, sem = jax.ShapeDtypeStruct, pltpu.SemaphoreType.DMA
    vmem, anywhere = pl.BlockSpec(memory_space=pltpu.VMEM), pl.BlockSpec(memory_space=pl.ANY)
    steps = 3 + depth.bit_length() - 1
    results = pl.pallas_call(
        functools.partial(back_kernel, depth),
        in_specs=[*[anywhere] * 14, vmem, *[anywhere] * 3],
        out_specs=[*[vmem] * 7, *[anywhere] * 3],
        out_shape=[
            shape((rows, width), LOW),
            shape((rows, width), LOW),
            *[shape((shard_rows, span), WIDE) for span in spans],
            shape((16, width), WIDE),
            shape((2, rows, width), LOW),
            shape((total_rows, inner), LOW),
            shape((rows, width), LOW),
        ],
        scratch_shapes=[
            pltpu.VMEM((rows, width), WIDE),
            pltpu.VMEM((2, 2, width, half), LOW),
            pltpu.VMEM((width, inner), LOW),
            pltpu.VMEM((2 * steps + 1, 16, width), WIDE),
            *[pltpu.VMEM((width, span), LOW) for span in spans],
            *Scatter.scratch(depth, shard_rows, classes),
            sem((steps,)),
            sem((steps,)),
            sem((6,)),
            sem((2, 6)),
            sem((3,)),
            sem((2, 2)),
            sem((2, 2)),
            sem((2,)),
            sem((3,)),
            sem((2,)),
            *Scatter.semaphores(depth, len(spans)),
        ],
        compiler_params=pltpu.CompilerParams(
            collective_id=1, has_side_effects=True, vmem_limit_bytes=63 * MIB
        ),
    )(
        acc, turned, upstream, normal, inverse, active, slope, far_ctx, context, qkv, totals, hidden_turned, whole, far,
        vectors, score_bias, from_own[:, None], from_dealt[:, None],
    )
    encoded, input_grad, first, second, third, fourth, small = results[:7]
    project = jnp.concatenate([third[:, inner:], fourth], axis=1)
    hidden = piece // 2
    return (
        encoded,
        input_grad,
        project,
        third[:, :inner],
        jnp.concatenate([first[:, :hidden], second[:, :hidden]], axis=1),
        jnp.concatenate([first[:, hidden:], second[:, hidden:]], axis=1),
        small,
    )


def adamw_update(master, moment, square, gradient, step_rate, decay_rate):
    moment_new = beta_one * moment + (1.0 - beta_one) * gradient
    square_new = beta_two * square + (1.0 - beta_two) * gradient * gradient
    moment_hat = moment_new / (1.0 - beta_one**STEP)
    square_hat = square_new / (1.0 - beta_two**STEP)
    master_new = master - step_rate * (
        moment_hat / (jnp.sqrt(square_hat) + adam_epsilon) + decay_rate * master
    )
    return (moment_new, square_new, master_new)


def local(
    tokens,
    cotangent,
    lengths,
    dealing,
    project_weight,
    project_first,
    project_second,
    merge_weight,
    merge_first,
    merge_second,
    expand_weight,
    expand_first,
    expand_second,
    reduce_weight,
    reduce_first,
    reduce_second,
    vectors,
    vector_first,
    vector_second,
    hidden_bias,
    hidden_first,
    hidden_second,
):
    parts = lax.axis_size("dp")
    member = lax.axis_index("tensor")
    other = 1 - member
    half_rows, model_width = tokens.shape
    total_rows = 2 * half_rows
    width_half = project_weight.shape[2]
    pairs = width_half // PAIR
    hidden_half = expand_weight.shape[1]
    shard_rows = expand_weight.shape[0]
    own_begin = member * half_rows
    by_kernel = parts % 4 == 0 and (parts & (parts - 1)) == 0 and shard_rows % 16 == 0

    def swap(value):
        return lax.ppermute(value, "tensor", [(0, 1), (1, 0)])

    def own(value, size, which=member):
        return lax.dynamic_slice_in_dim(value, which * size, size, 0)

    segment, own_of, dealt_of, from_own, from_dealt = layout(lengths[0], dealing[0], total_rows)
    dealt_of = own(dealt_of, half_rows)
    short = segment[LONGEST:]
    score_bias = jnp.where(short[:, None] == short[None, :], 0.0, masked_score).astype(WIDE)

    def own_first(index):
        return lax.rem(index - own_begin + total_rows, total_rows)

    projections = (
        project_weight.reshape(3, shard_rows, pairs, PAIR)
        .transpose(1, 2, 0, 3)
        .reshape(shard_rows, 3 * width_half)
    )
    quarter = hidden_half // 2
    reduce_turned = reduce_weight.T
    shards = jnp.stack(
        [
            jnp.concatenate([projections, merge_weight.T], axis=1),
            jnp.concatenate([expand_weight[:, :quarter], reduce_turned[:, :quarter]], axis=1),
            jnp.concatenate([expand_weight[:, quarter:], reduce_turned[:, quarter:]], axis=1),
        ]
    ).astype(LOW)
    zeros_pair = jnp.zeros((pairs, PAIR), WIDE)
    bias_row = jnp.concatenate(
        [
            own(vectors[0], width_half).reshape(pairs, PAIR),
            zeros_pair,
            own(vectors[1], width_half).reshape(pairs, PAIR),
        ],
        axis=1,
    ).reshape(pairs, 1, 3 * PAIR)
    if by_kernel:
        whole, far, qkv, hidden_turned, upstream, context, totals, *middle = front(
            shards,
            tokens,
            cotangent,
            own_of,
            dealt_of,
            bias_row,
            score_bias,
            vectors,
            own(hidden_bias, hidden_half),
            own(hidden_bias, hidden_half, other),
            parts,
        )
        encoded_out, input_grad, *grads, small = back(
            middle, context, qkv, totals, hidden_turned, upstream, whole, far, vectors, score_bias, from_own,
            own(from_dealt, half_rows), parts,
        )
    else:
        whole = lax.all_gather(shards, "dp", axis=1, tiled=True)
        far = swap(whole)
        token_pair = jnp.concatenate([tokens, swap(tokens)], axis=0)
        upper_pair = jnp.concatenate([cotangent, swap(cotangent)], axis=0)
        hidden = dot_nn(pick_rows(own_first(own_of), total_rows), token_pair).astype(LOW)
        upstream = dot_nn(pick_rows(own_first(dealt_of), total_rows), upper_pair).astype(LOW)
        qkv = jnp.einsum(
            "rd,dpc->prc",
            hidden,
            whole[0, :, : 3 * width_half].reshape(model_width, pairs, 3 * PAIR),
            preferred_element_type=WIDE,
        )
        qkv = (qkv + bias_row).astype(LOW)
        context, totals = attend(qkv, score_bias)

        (
            encoded, branch_grad, context_grad, merge_grad, expand_grad, reduce_grad, sums, hidden_part_own, hidden_part_far,
        ) = feed_block(
            context,
            whole,
            far,
            own(hidden, half_rows),
            upstream,
            vectors,
            own(hidden_bias, hidden_half),
            own(hidden_bias, hidden_half, other),
        )
        encoded_pair = jnp.concatenate([encoded, swap(encoded)], axis=0)
        encoded_out = dot_nn(
            pick_rows(own_first(own(from_dealt, half_rows)), total_rows), encoded_pair
        ).astype(LOW)
        mixed_grads = attend_back(qkv, score_bias, context, context_grad, totals)
        mixed_sums = jnp.sum(mixed_grads.astype(WIDE), axis=1).reshape(pairs, 3, PAIR)
        mixed_grads = mixed_grads.transpose(1, 0, 2).reshape(total_rows, 3 * width_half)
        project_grad = dot_tn(hidden, mixed_grads)
        input_terms = dot_nt(mixed_grads, whole[0, :, : 3 * width_half])
        own_part = own(input_terms, half_rows) + branch_grad
        input_terms = lax.dynamic_update_slice_in_dim(input_terms, own_part, own_begin, 0).astype(LOW)
        input_far = swap(
            dot_nn(pick_rows(own(from_own, half_rows, other), total_rows), input_terms).astype(LOW)
        )
        input_grad = (
            dot_nn(pick_rows(own(from_own, half_rows), total_rows), input_terms)
            + input_far.astype(WIDE)
        ).astype(LOW)
        zeros_width = jnp.zeros((model_width,), WIDE)
        zeros_hidden = jnp.zeros_like(hidden_bias)
        hidden_total = lax.dynamic_update_slice_in_dim(
            lax.dynamic_update_slice_in_dim(
                zeros_hidden, hidden_part_own, member * hidden_half, 0
            ),
            hidden_part_far,
            other * hidden_half,
            0,
        )
        vector_rows = [
            lax.dynamic_update_slice_in_dim(
                zeros_width, mixed_sums[:, c].reshape(-1), member * width_half, 0
            )
            for c in (0, 2)
        ]
        small = jnp.concatenate(
            [
                jnp.stack(vector_rows),
                sums[2:],
                hidden_total.reshape(-1, model_width),
                jnp.zeros((4, model_width), WIDE),
            ],
            axis=0,
        )
        grads = [
            lax.psum_scatter(g.astype(LOW), "dp", scatter_dimension=0, tiled=True).astype(WIDE)
            for g in (project_grad, merge_grad, expand_grad, reduce_grad)
        ]
        small = lax.psum(small, ("dp", "tensor"))
    project_shard, merge_shard, expand_shard, reduce_shard = grads
    project_shard = (
        project_shard.reshape(shard_rows, pairs, 3, PAIR)
        .transpose(2, 0, 1, 3)
        .reshape(3, shard_rows, width_half)
    )
    vector_grad = small[:8]
    hidden_grad = small[8:12].reshape(-1)
    return (
        encoded_out,
        input_grad,
        *adamw_update(
            project_weight, project_first, project_second, project_shard, rate_project, weight_decay
        ),
        *adamw_update(
            merge_weight, merge_first, merge_second, merge_shard.T, rate_merge, weight_decay
        ),
        *adamw_update(
            expand_weight, expand_first, expand_second, expand_shard, rate_expand, weight_decay
        ),
        *adamw_update(
            reduce_weight, reduce_first, reduce_second, reduce_shard.T, rate_reduce, weight_decay
        ),
        *adamw_update(vectors, vector_first, vector_second, vector_grad, rate_vectors, 0.0),
        *adamw_update(hidden_bias, hidden_first, hidden_second, hidden_grad, rate_hidden, 0.0),
        vector_grad,
    )


def solution(mesh):
    sharded = (
        P("dp", None),
        P("dp", None),
        *[P(None, "dp", "tensor")] * 3,
        *[P("tensor", "dp")] * 3,
        *[P("dp", "tensor")] * 3,
        *[P("tensor", "dp")] * 3,
        *[P()] * 6,
    )
    rows = P(("dp", "tensor"), None)
    return jax.shard_map(
        local,
        mesh=mesh,
        in_specs=(rows, rows, *sharded),
        out_specs=(rows, rows, *sharded[2:], P()),
        check_vma=False,
    )
```

```python
import functools

import jax
import jax.numpy as jnp
from jax import lax
from jax.experimental import pallas as pl
from jax.experimental.pallas import tpu as pltpu
from jax.sharding import PartitionSpec as P

HEAD_DIM = 64
LONGEST = 1024
STEP = 10
PAIR = 2 * HEAD_DIM
TILE = 256
MIB = 1024 * 1024
MESH = pl.DeviceIdType.MESH
LOW = jnp.bfloat16
WIDE = jnp.float32

beta_one = 0.9
beta_two = 0.999
adam_epsilon = 1e-08
weight_decay = 0.01
norm_epsilon = 1e-05
masked_score = -1e30
rate_project = 0.03
rate_merge = 0.3
rate_expand = 0.03
rate_reduce = 0.015
rate_vectors = 0.4
rate_hidden = 0.1


def dot_nn(a, b):
    return jnp.dot(a, b, preferred_element_type=WIDE)


def dot_nt(a, b):
    return lax.dot_general(a, b, (((1,), (1,)), ((), ())), preferred_element_type=WIDE)


def dot_tn(a, b):
    return lax.dot_general(a, b, (((0,), (0,)), ((), ())), preferred_element_type=WIDE)


def layout(lengths_row, dealing_row, total_rows):
    slots = jnp.arange(lengths_row.shape[0], dtype=jnp.int32)
    places = jnp.arange(total_rows, dtype=jnp.int32)
    rank_of = jnp.sum(jnp.where(dealing_row[None, :] == slots[:, None], slots[None, :], 0), axis=1)
    own_start = jnp.cumsum(lengths_row) - lengths_row
    dealt_start = jnp.sum(
        jnp.where(rank_of[None, :] < rank_of[:, None], lengths_row[None, :], 0), axis=1
    )
    longest = lengths_row == LONGEST
    short = jnp.where(longest, 0, lengths_row)
    start = jnp.where(longest, 0, LONGEST + jnp.cumsum(short) - short)

    def inside(begin):
        return (places[:, None] >= begin[None, :]) & (
            places[:, None] < (begin + lengths_row)[None, :]
        )

    def moved(begin, end):
        return places + jnp.sum(jnp.where(inside(begin), (end - begin)[None, :], 0), axis=1)

    segment = jnp.sum(jnp.where(inside(start), slots[None, :], 0), axis=1)
    return (
        segment,
        moved(start, own_start),
        moved(start, dealt_start),
        moved(own_start, start),
        moved(dealt_start, start),
    )


def pick_rows(index, rows):
    places = jnp.arange(rows, dtype=jnp.int32)
    return (index[:, None] == places[None, :]).astype(LOW)


class Group:
    def __init__(self, lengths_ref, dealing_ref):
        count = lengths_ref.shape[1]
        self.lengths = [lengths_ref[0, s] for s in range(count)]
        order = [dealing_ref[0, i] for i in range(count)]
        rank = [sum(jnp.where(order[i] == s, i, 0) for i in range(count)) for s in range(count)]
        short = [jnp.where(length == LONGEST, 0, length) for length in self.lengths]
        self.own, self.dealt, self.first = [], [], []
        own = own_short = jnp.int32(0)
        for s in range(count):
            self.own.append(own)
            self.first.append(jnp.where(self.lengths[s] == LONGEST, 0, LONGEST + own_short))
            self.dealt.append(
                sum(jnp.where(rank[j] < rank[s], self.lengths[j], 0) for j in range(count))
            )
            own, own_short = own + self.lengths[s], own_short + short[s]

    def inside(self, places, begin, s):
        return (places >= begin[s]) & (places < begin[s] + self.lengths[s])

    def moved(self, places, begin, end):
        total = places
        for s in range(len(begin)):
            total = total + jnp.where(self.inside(places, begin, s), end[s] - begin[s], 0)
        return total

    def score_bias(self, count):
        sides = []
        for shape, axis in (((count, 1), 0), ((1, count), 1)):
            places = lax.broadcasted_iota(jnp.int32, shape, axis) + LONGEST
            segment = jnp.zeros_like(places)
            for s in range(len(self.first)):
                segment = segment + jnp.where(self.inside(places, self.first, s), s, 0)
            sides.append(segment)
        return jnp.where(sides[0] == sides[1], 0.0, masked_score).astype(WIDE)


def picked_rows(index, source):
    places = lax.broadcasted_iota(jnp.int32, (index.shape[0], source.shape[0]), 1)
    return dot_nn(jnp.where(index == places, 1.0, 0.0).astype(LOW), source[...])


def attend_tile(qkv_ref, pair, bias_ref, begin, size, step, context_ref, columns, total_ref):
    lane = lax.broadcasted_iota(jnp.int32, (1, PAIR), 1)
    scale = HEAD_DIM ** (-0.5)
    first = pl.multiple_of(begin + step * TILE, TILE)
    query = qkv_ref[pair, pl.ds(first, TILE), 0:PAIR]
    key = qkv_ref[pair, begin : begin + size, PAIR : 2 * PAIR]
    value = qkv_ref[pair, begin : begin + size, 2 * PAIR : 3 * PAIR]
    outcome = []
    for head in range(2):
        chosen = jnp.where(lane // HEAD_DIM == head, scale, 0.0).astype(LOW)
        scores = dot_nt(query * chosen, key)
        if begin:
            inner = pl.multiple_of(step * TILE, TILE)
            scores = scores + bias_ref[pl.ds(inner, TILE), :]
        top = jnp.max(scores, axis=1, keepdims=True)
        exponent = jnp.exp(scores - top)
        total = jnp.sum(exponent, axis=1, keepdims=True)
        outcome.append(dot_nn(exponent.astype(LOW), value) / total)
        log_total = jnp.broadcast_to(top + jnp.log(total), (TILE, PAIR))
        total_ref[pair, head : head + 1, pl.ds(first, TILE)] = log_total.T[0:1, :]
    context_ref[pl.ds(first, TILE), columns] = jnp.where(
        lane < HEAD_DIM, outcome[0], outcome[1]
    ).astype(LOW)


def attend_kernel(qkv_ref, bias_ref, context_ref, total_ref):
    rows = qkv_ref.shape[1]
    for begin, size in ((0, LONGEST), (LONGEST, rows - LONGEST)):

        @pl.loop(0, size // TILE)
        def _(step):
            attend_tile(
                qkv_ref, 0, bias_ref, begin, size, step, context_ref, slice(0, PAIR), total_ref
            )


def attend(qkv, bias):
    pairs, rows, width = qkv.shape
    return pl.pallas_call(
        attend_kernel,
        grid=(pairs,),
        in_specs=[
            pl.BlockSpec((1, rows, width), lambda p: (p, 0, 0)),
            pl.BlockSpec(bias.shape, lambda p: (0, 0)),
        ],
        out_specs=[
            pl.BlockSpec((rows, PAIR), lambda p: (0, p)),
            pl.BlockSpec((1, 8, rows), lambda p: (p, 0, 0)),
        ],
        out_shape=[
            jax.ShapeDtypeStruct((rows, pairs * PAIR), LOW),
            jax.ShapeDtypeStruct((pairs, 8, rows), WIDE),
        ],
        compiler_params=pltpu.CompilerParams(vmem_limit_bytes=48 * MIB),
    )(qkv, bias)


def attend_back_open(qkv_ref, context_ref, upper_ref, dots, key_turned, queries, uppers):
    lane = lax.broadcasted_iota(jnp.int32, (1, PAIR), 1)
    product = (upper_ref[...].astype(WIDE) * context_ref[...].astype(WIDE)).T
    for head in range(2):
        band = slice(head * HEAD_DIM, (head + 1) * HEAD_DIM)
        dots[head : head + 1, :] = jnp.sum(product[band, :], axis=0, keepdims=True)
        chosen = lane // HEAD_DIM == head
        queries[head] = qkv_ref[:, 0:PAIR] * jnp.where(chosen, HEAD_DIM ** (-0.5), 0.0).astype(LOW)
        uppers[head] = upper_ref[...] * jnp.where(chosen, 1.0, 0.0).astype(LOW)
    key_turned[...] = qkv_ref[:, PAIR : 2 * PAIR].astype(WIDE).T.astype(LOW)


def attend_back_tile(
    qkv_ref, bias_ref, total_ref, dots, key_turned, queries, uppers, query_sum, begin, size, step
):
    block = slice(begin, begin + size)
    first = pl.multiple_of(begin + step * TILE, TILE)
    key = qkv_ref[pl.ds(first, TILE), PAIR : 2 * PAIR]
    value = qkv_ref[pl.ds(first, TILE), 2 * PAIR : 3 * PAIR]
    key_sum = jnp.zeros((TILE, PAIR), WIDE)
    value_sum = jnp.zeros((TILE, PAIR), WIDE)
    for head in range(2):
        band = slice(head * HEAD_DIM, (head + 1) * HEAD_DIM)
        query = queries[head, block, :]
        upper = uppers[head, block, :]
        scores = dot_nt(key, query)
        if begin:
            inner = pl.multiple_of(step * TILE, TILE)
            scores = scores + bias_ref[pl.ds(inner, TILE), :]
        probability = jnp.exp(scores - total_ref[head : head + 1, block])
        weight_grads = dot_nt(value, upper)
        score_grads = (probability * (weight_grads - dots[head : head + 1, block])).astype(LOW)
        value_sum = value_sum + dot_nn(probability.astype(LOW), upper)
        key_sum = key_sum + dot_nn(score_grads, query)
        query_sum[band, block] += dot_nn(key_turned[band, pl.ds(first, TILE)], score_grads)
    return pl.ds(first, TILE), key_sum, value_sum


def attend_back_kernel(
    qkv_ref, bias_ref, context_ref, grad_ref, total_ref, out_ref, dots, key_turned, queries, uppers, query_sum
):
    rows = qkv_ref.shape[1]
    qkv = qkv_ref.at[0]
    attend_back_open(qkv, context_ref, grad_ref, dots, key_turned, queries, uppers)
    for begin, size in ((0, LONGEST), (LONGEST, rows - LONGEST)):
        block = slice(begin, begin + size)
        query_sum[:, block] = jnp.zeros((PAIR, size), WIDE)

        @pl.loop(0, size // TILE)
        def _(step):
            at, key_sum, value_sum = attend_back_tile(
                qkv, bias_ref, total_ref.at[0], dots, key_turned, queries, uppers, query_sum, begin, size, step
            )
            out_ref[0, at, PAIR : 2 * PAIR] = key_sum.astype(LOW)
            out_ref[0, at, 2 * PAIR : 3 * PAIR] = value_sum.astype(LOW)

        out_ref[0, block, 0:PAIR] = (query_sum[:, block] * HEAD_DIM ** (-0.5)).T.astype(LOW)


def attend_back(qkv, bias, context, grad, totals):
    pairs, rows, width = qkv.shape
    return pl.pallas_call(
        attend_back_kernel,
        grid=(pairs,),
        in_specs=[
            pl.BlockSpec((1, rows, width), lambda p: (p, 0, 0)),
            pl.BlockSpec(bias.shape, lambda p: (0, 0)),
            pl.BlockSpec((rows, PAIR), lambda p: (0, p)),
            pl.BlockSpec((rows, PAIR), lambda p: (0, p)),
            pl.BlockSpec((1, 8, rows), lambda p: (p, 0, 0)),
        ],
        out_specs=pl.BlockSpec((1, rows, width), lambda p: (p, 0, 0)),
        out_shape=jax.ShapeDtypeStruct(qkv.shape, LOW),
        scratch_shapes=[
            pltpu.VMEM((8, rows), WIDE),
            pltpu.VMEM((PAIR, rows), LOW),
            pltpu.VMEM((2, rows, PAIR), LOW),
            pltpu.VMEM((2, rows, PAIR), LOW),
            pltpu.VMEM((PAIR, rows), WIDE),
        ],
        compiler_params=pltpu.CompilerParams(vmem_limit_bytes=48 * MIB),
    )(qkv, bias, context, grad, totals)


def place():
    me = lax.axis_index("dp")
    z, y, x = me // 4, (me // 2) % 2, me % 2
    return me, z, y, x


def line_slots(z, depth):
    slots = []
    for step in range(depth - 1):
        slots.append((z - 1 - step, z - 1 - step >= 0, 1))
        slots.append((z + 1 + step, z + 1 + step < depth, -1))
    return slots


def remote(source, target, send, receive, device):
    return pltpu.make_async_remote_copy(
        src_ref=source,
        dst_ref=target,
        send_sem=send,
        recv_sem=receive,
        device_id={"dp": device},
        device_id_type=MESH,
    )


def greet_line(me, z, y, x, depth, extra=()):
    barrier = pltpu.get_barrier_semaphore()
    for peer in (z * 4 + y * 2 + 1 - x, z * 4 + (1 - y) * 2 + x):
        pl.semaphore_signal(barrier, inc=1, device_id={"dp": peer}, device_id_type=MESH)

    @pl.when(z > 0)
    def _():
        pl.semaphore_signal(barrier, inc=1, device_id={"dp": me - 4}, device_id_type=MESH)

    @pl.when(z < depth - 1)
    def _():
        pl.semaphore_signal(barrier, inc=1, device_id={"dp": me + 4}, device_id_type=MESH)

    for peer in extra:
        pl.semaphore_signal(barrier, inc=1, device_id=peer, device_id_type=MESH)
    ends = jnp.where(z > 0, 1, 0) + jnp.where(z < depth - 1, 1, 0)
    pl.semaphore_wait(barrier, 2 + len(extra) + ends)


def other_core(source, target, send, receive):
    return pltpu.make_async_remote_copy(
        src_ref=source,
        dst_ref=target,
        send_sem=send,
        recv_sem=receive,
        device_id={"tensor": 1 - lax.axis_index("tensor")},
        device_id_type=MESH,
    )


class Gather:
    def __init__(self, depth, parts, whole, far, sems):
        self.whole, self.far = whole, far
        self.depth = depth
        self.me, self.z, self.y, self.x = place()
        self.x_peer = self.z * 4 + self.y * 2 + 1 - self.x
        self.y_peer = self.z * 4 + (1 - self.y) * 2 + self.x
        self.rows = whole.shape[1] // parts
        width = whole.shape[2]
        self.third = width // 4
        side = (width - self.third) // 2
        self.a, self.b = (0, side), (side, side)
        self.ab, self.c, self.all = (0, 2 * side), (2 * side, self.third), (0, width)
        (
            self.z_send, self.z_recv, self.zc_send, self.zc_recv, self.xa_send, self.xa_recv, self.yb_send, self.yb_recv,
            self.ya_send, self.ya_recv, self.xb_send, self.xb_recv, self.c_send, self.c_recv, self.far_send, self.far_recv,
        ) = sems
        self.slots = line_slots(self.z, depth)

    @staticmethod
    def semaphores(depth, pieces):
        sem = pltpu.SemaphoreType.DMA
        return [
            *[sem((pieces, depth + 1)), sem((pieces, depth))] * 2,
            *[sem((pieces, depth))] * 4,
            *[sem((pieces, depth, 2))] * 4,
            sem((pieces, 2)),
            sem((pieces, 2)),
            sem((pieces,)),
            sem((pieces,)),
        ]

    def block(self, zb, yb, xb):
        return zb * 4 + yb * 2 + xb

    def cut(self, ref, p, block, count, columns):
        first = pl.multiple_of(block * self.rows, self.rows)
        return ref.at[p, pl.ds(first, count * self.rows), pl.ds(*columns)]

    def copy(self, p, block, count, columns, send, receive, device):
        part = self.cut(self.whole, p, block, count, columns)
        return remote(part, part, send, receive, device)

    def forward(self, p, block, count, columns):
        if p == 0 and columns[0] + columns[1] <= self.c[0]:
            return
        if p == 0:
            columns = self.c
        other_core(
            self.cut(self.whole, p, block, count, columns),
            self.cut(self.far, p, block, count, columns),
            self.far_send.at[p],
            self.far_recv.at[p],
        ).start()

    def far_copy(self, p):
        columns = self.c if p == 0 else self.all
        part = self.far.at[p, :, pl.ds(*columns)]
        return other_core(part, part, self.far_send.at[p], self.far_recv.at[p])

    def z_copy(self, p, zb, way, back=False):
        block = self.block(zb, self.y, self.x)
        sem = self.depth if back else zb
        return self.copy(
            p, block, 1, self.ab, self.z_send.at[p, sem], self.z_recv.at[p, zb], self.me + 4 * way
        )

    def zc_copy(self, p, zb, way, back=False):
        sem = self.depth if back else zb
        return self.copy(
            p, zb * 4, 4, self.c, self.zc_send.at[p, sem], self.zc_recv.at[p, zb], self.me + 4 * way
        )

    def xa(self, p, zb, xb):
        block = self.block(zb, self.y, xb)
        return self.copy(
            p, block, 1, self.a, self.xa_send.at[p, zb], self.xa_recv.at[p, zb], self.x_peer
        )

    def yb(self, p, zb, yb):
        block = self.block(zb, yb, self.x)
        return self.copy(
            p, block, 1, self.b, self.yb_send.at[p, zb], self.yb_recv.at[p, zb], self.y_peer
        )

    def ya(self, p, zb, yb, xb):
        block = self.block(zb, yb, xb)
        return self.copy(
            p, block, 1, self.a, self.ya_send.at[p, zb, xb], self.ya_recv.at[p, zb, xb], self.y_peer
        )

    def xb(self, p, zb, yb, xb):
        block = self.block(zb, yb, xb)
        return self.copy(
            p, block, 1, self.b, self.xb_send.at[p, zb, yb], self.xb_recv.at[p, zb, yb], self.x_peer
        )

    def xc(self, p, xb):
        block = self.block(self.z, self.y, xb)
        return self.copy(
            p, block, 1, self.c, self.c_send.at[p, 0], self.c_recv.at[p, 0], self.x_peer
        )

    def yc(self, p, yb):
        block = self.block(self.z, yb, 0)
        return self.copy(
            p, block, 2, self.c, self.c_send.at[p, 1], self.c_recv.at[p, 1], self.y_peer
        )

    def both_ways(self, copy, act):
        @pl.when(self.z < self.depth - 1)
        def _():
            act(copy(self.z, 1))

        @pl.when(self.z > 0)
        def _():
            act(copy(self.z, -1, True))

    def spread(self, p, zb):
        self.xa(p, zb, self.x).start()
        self.yb(p, zb, self.y).start()
        self.ya(p, zb, self.y, self.x).start()
        self.xb(p, zb, self.y, self.x).start()

    def turn(self, p, zb):
        self.xa(p, zb, 1 - self.x).wait_recv()
        self.ya(p, zb, self.y, 1 - self.x).start()
        self.forward(p, self.block(zb, self.y, 1 - self.x), 1, self.a)
        self.yb(p, zb, 1 - self.y).wait_recv()
        self.xb(p, zb, 1 - self.y, self.x).start()
        self.forward(p, self.block(zb, 1 - self.y, self.x), 1, self.b)

    def at_step(self, step, act):
        for zb, valid, way in self.slots[2 * step : 2 * step + 2]:
            on = (self.z + way >= 0) & (self.z + way < self.depth)
            pl.when(valid)(functools.partial(act, zb, way, on))

    def arrive(self, p, step):
        def act(zb, way, on):
            self.z_copy(p, zb, way).wait_recv()
            pl.when(on)(lambda: self.z_copy(p, zb, way).start())
            self.spread(p, zb)
            self.forward(p, self.block(zb, self.y, self.x), 1, self.ab)

        self.at_step(step, act)

    def arrive_c(self, p, step):
        def act(zb, way, on):
            self.zc_copy(p, zb, way).wait_recv()
            pl.when(on)(lambda: self.zc_copy(p, zb, way).start())
            self.forward(p, zb * 4, 4, self.c)

        self.at_step(step, act)

    def stage(self, p, s):
        depth = self.depth
        if s == 0:
            self.both_ways(lambda *way: self.z_copy(p, *way), lambda copy: copy.start())
            self.xc(p, self.x).start()
            self.spread(p, self.z)
            self.forward(p, self.me, 1, self.all)
            return
        if s == 1:
            self.xc(p, 1 - self.x).wait_recv()
            self.yc(p, self.y).start()
            self.forward(p, self.block(self.z, self.y, 1 - self.x), 1, self.c)
        if s == 2:
            self.yc(p, 1 - self.y).wait_recv()
            self.both_ways(lambda *way: self.zc_copy(p, *way), lambda copy: copy.start())
            self.forward(p, self.block(self.z, 1 - self.y, 0), 2, self.c)
        if 1 <= s < depth:
            self.arrive(p, s - 1)
        if 3 <= s < depth + 2:
            self.arrive_c(p, s - 3)
        if s == 2:
            self.turn(p, self.z)
        if 3 <= s < depth + 2:
            self.at_step(s - 3, lambda zb, way, on: self.turn(p, zb))
        if s == depth + 2:
            for zb in range(depth):
                for other in range(2):
                    self.ya(p, zb, 1 - self.y, other).wait_recv()
                    self.forward(p, self.block(zb, 1 - self.y, other), 1, self.a)
                    self.xb(p, zb, other, 1 - self.x).wait_recv()
                    self.forward(p, self.block(zb, other, 1 - self.x), 1, self.b)

    def finish(self, p):
        def sent(copy):
            copy.wait_send()

        self.far_copy(p).wait_send()
        self.both_ways(lambda *way: self.z_copy(p, *way), sent)
        self.both_ways(lambda *way: self.zc_copy(p, *way), sent)
        for zb in range(self.depth):
            self.xa(p, zb, self.x).wait_send()
            self.yb(p, zb, self.y).wait_send()
            for other in range(2):
                self.ya(p, zb, self.y, other).wait_send()
                self.xb(p, zb, other, self.x).wait_send()
        self.xc(p, self.x).wait_send()
        self.yc(p, self.y).wait_send()

        def passed(zb, way, on):
            pl.when(on)(lambda: sent(self.z_copy(p, zb, way)))
            pl.when(on)(lambda: sent(self.zc_copy(p, zb, way)))

        for step in range(self.depth - 1):
            self.at_step(step, passed)


def looped(count, body, between):
    @pl.loop(0, count)
    def _(i):
        body(i)
        for step, acts in between.items():

            @pl.when(i == step)
            def _():
                for act in acts:
                    act()


GATHER_AT = {
    "hidden": {-1: [(0, 1)], 0: [(0, 2)], 3: [(0, 3), (0, 4)]},
    "upstream": {-1: [(1, 0)], 0: [(0, 5)], 1: [(2, 0)]},
    "project": {-1: [(0, 6)], 0: [(1, 1)]},
    "long": {-1: [(1, 2)], 2: [(2, 1)], 9: [(1, 3)], 11: [(2, 2)]},
    "short": {4: [(1, 4)]},
    "norm": {1: [(1, 5), (2, 3)]},
    "feed": {-1: [(1, 6)], 0: [(2, 4)], 1: [(2, 5)]},
    "last": {-1: [(2, 6)]},
}


def front_kernel(
    depth, lengths_ref, dealing_ref, project_ref, merge_ref, expand_ref, reduce_ref, vectors_ref, hidden_bias_ref,
    tokens_ref, cotangent_ref,
    whole_ref, far_ref, qkv_out, turned_out, upstream_out, context_out, total_out,
    acc_out, normal_out, inverse_out, low_turned_out, active_out, slope_out, far_context_out,
    shards, score_bias, token, upper, hidden, turned, upstream, weight, qkv, context, total,
    acc, normal, inverse, low, low_turned, active, slope, far_context, merge, merge_far, expand_buf, reduce_buf,
    local_sem, core_sem, out_sem, load_sem, chunk_sem, *sems,
):
    pieces = whole_ref.shape[0]
    half_rows, width = tokens_ref.shape
    rows = 2 * half_rows
    pairs = qkv.shape[0]
    inner = pairs * PAIR
    both = expand_buf.shape[2]
    half = both // 2
    hidden_half = expand_ref.shape[1]
    chunks = hidden_half // half
    per_piece = chunks // (pieces - 1)
    member = lax.axis_index("tensor")
    lines = Gather(depth, 4 * depth, whole_ref, far_ref, sems)
    me = lines.me
    tall, short = 2 * TILE, TILE // 2

    own = [
        pltpu.make_async_copy(
            shards.at[p], lines.cut(whole_ref, p, me, 1, lines.all), local_sem.at[p]
        )
        for p in range(pieces)
    ]
    own += [
        pltpu.make_async_copy(tokens_ref, token.at[member], local_sem.at[pieces]),
        pltpu.make_async_copy(cotangent_ref, upper.at[member], local_sem.at[pieces + 1]),
    ]
    for copy in own[pieces:]:
        copy.start()
    for pair in range(pairs):
        for c in range(3):
            first = (3 * pair + c) * PAIR
            shards[0, :, first : first + PAIR] = project_ref[
                c, :, pair * PAIR : (pair + 1) * PAIR
            ].astype(LOW)
    shards[0, :, 3 * inner :] = merge_ref[...].astype(LOW)
    quarter = hidden_half // (pieces - 1)
    for p in range(1, pieces):
        columns = slice((p - 1) * quarter, p * quarter)
        shards[p, :, 0:quarter] = expand_ref[:, columns].astype(LOW)
        shards[p, :, quarter:] = reduce_ref[:, columns].astype(LOW)
    for copy in own[:pieces]:
        copy.start()
    greet_line(me, lines.z, lines.y, lines.x, depth, [{"tensor": 1 - member}])
    crossing = [
        other_core(tokens_ref, token.at[member], core_sem.at[0, 0], core_sem.at[0, 1]),
        other_core(cotangent_ref, upper.at[member], core_sem.at[1, 0], core_sem.at[1, 1]),
    ]
    own[0].wait()
    lines.stage(0, 0)
    for copy in crossing:
        copy.start()
    group = Group(lengths_ref, dealing_ref)
    score_bias[...] = group.score_bias(rows - LONGEST)
    for copy in own[1:]:
        copy.wait()

    leaving = []

    def leave(source, target):
        copy = pltpu.make_async_copy(source, target, out_sem.at[len(leaving)])
        copy.start()
        leaving.append(copy)

    def phase(name, count, body):
        between = {
            step: [functools.partial(lines.stage, *stage) for stage in stages]
            for step, stages in GATHER_AT.get(name, {}).items()
        }
        for act in between.pop(-1, ()):
            act()
        looped(count, body, between)

    def places_of(first):
        return first + lax.broadcasted_iota(jnp.int32, (TILE, 1), 0)

    def picked(index, source):
        return picked_rows(index, source.at[0]) + picked_rows(index - half_rows, source.at[1])

    def tile(step, size=TILE):
        return pl.ds(pl.multiple_of(step * size, size), size)

    def hidden_tile(step):
        index = group.moved(places_of(step * TILE), group.first, group.own)
        rows_here = picked(index, token)
        hidden[tile(step), :] = rows_here.astype(LOW)
        turned[:, tile(step)] = rows_here.T.astype(LOW)

    def upstream_tile(step):
        places = places_of(member * half_rows + step * TILE)
        index = group.moved(places, group.first, group.dealt)
        upstream[tile(step), :] = picked(index, upper).astype(LOW)

    crossing[0].wait()
    phase("hidden", rows // TILE, hidden_tile)
    leave(turned, turned_out)
    crossing[1].wait()
    phase("upstream", half_rows // TILE, upstream_tile)
    leave(upstream, upstream_out)

    weight_copy = pltpu.make_async_copy(
        whole_ref.at[0, :, pl.ds(0, pairs * 3 * PAIR)], weight, local_sem.at[1]
    )

    def project_tile(i):
        @pl.when(i == 0)
        def _():
            weight_copy.start()
            weight_copy.wait()

        pair, step = i // (rows // tall), lax.rem(i, rows // tall)
        at = tile(step, tall)
        columns = pl.ds(pl.multiple_of(pair * 3 * PAIR, PAIR), 3 * PAIR)
        bias_columns = pl.ds(pl.multiple_of(member * inner + pair * PAIR, PAIR), PAIR)
        bias = jnp.concatenate(
            [
                vectors_ref[0:1, bias_columns],
                jnp.zeros((1, PAIR), WIDE),
                vectors_ref[1:2, bias_columns],
            ],
            axis=1,
        )
        qkv[pair, at, :] = (dot_nn(hidden[at, :], weight[:, columns]) + bias).astype(LOW)

    phase("project", pairs * rows // tall, project_tile)
    leave(qkv, qkv_out)

    def attend_step(begin, size):
        def step_of(i):
            pair, step = i // (size // TILE), lax.rem(i, size // TILE)
            columns = pl.ds(pl.multiple_of(pair * PAIR, PAIR), PAIR)
            attend_tile(qkv, pair, score_bias, begin, size, step, context, columns, total)

        return step_of

    phase("long", pairs * LONGEST // TILE, attend_step(0, LONGEST))
    phase("short", pairs * (rows - LONGEST) // TILE, attend_step(LONGEST, rows - LONGEST))
    leave(context, context_out)
    leave(total, total_out)

    own_first = member * half_rows
    other_rows = pl.ds(pl.multiple_of((1 - member) * half_rows, half_rows), half_rows)
    crossing = other_core(context.at[other_rows], far_context, core_sem.at[2, 0], core_sem.at[2, 1])
    crossing.start()
    lines.far_copy(0).wait_recv()
    merge_columns = pl.ds(whole_ref.shape[2] - inner, inner)
    fetches = [
        pltpu.make_async_copy(whole_ref.at[0, :, merge_columns], merge, local_sem.at[2]),
        pltpu.make_async_copy(far_ref.at[0, :, merge_columns], merge_far, local_sem.at[3]),
    ]
    for copy in fetches:
        copy.start()
    for copy in fetches:
        copy.wait()
    crossing.wait()
    leave(far_context, far_context_out)

    def norm_tile(step):
        at = tile(step, short)
        own_at = pl.ds(pl.multiple_of(own_first + step * short, short), short)
        branch = dot_nt(context[own_at, :], merge[...]) + dot_nt(far_context[at, :], merge_far[...])
        unit, scale = norm(hidden[own_at, :].astype(WIDE) + branch + vectors_ref[2:3, :])
        normed = unit * vectors_ref[3:4, :] + vectors_ref[4:5, :]
        normal[at, :] = unit
        inverse[at, :] = jnp.broadcast_to(scale, (short, 128))
        low[at, :] = normed.astype(LOW)
        low_turned[:, at] = normed.T.astype(LOW)
        acc[at, :] = normed + vectors_ref[5:6, :]

    phase("norm", half_rows // short, norm_tile)
    leave(normal, normal_out)
    leave(inverse, inverse_out)
    leave(low_turned, low_turned_out)

    def loads(j):
        slot, piece, at = lax.rem(j, 2), 1 + j // per_piece, lax.rem(j, per_piece) * half
        copies = []
        for kind, buf in enumerate((expand_buf, reduce_buf)):
            first = pl.multiple_of(at + kind * per_piece * half, half)
            for side, source in enumerate((far_ref, whole_ref)):
                copies.append(
                    pltpu.make_async_copy(
                        source.at[piece, :, pl.ds(first, half)],
                        buf.at[slot, :, pl.ds(side * half, half)],
                        load_sem.at[slot, kind, side],
                    )
                )
        return copies

    def results(j):
        slot = lax.rem(j, 2)
        return [
            pltpu.make_async_copy(active.at[slot], active_out.at[j], chunk_sem.at[slot, 0]),
            pltpu.make_async_copy(slope.at[slot], slope_out.at[j], chunk_sem.at[slot, 1]),
        ]

    def chunk_of(first_chunk):
        def chunk(i):
            j = first_chunk + i
            slot = lax.rem(j, 2)

            @pl.when(i == 0)
            def _():
                lines.far_copy(1 + first_chunk // per_piece).wait_recv()
                for copy in loads(j):
                    copy.start()

            for copy in loads(j):
                copy.wait()

            @pl.when(i + 1 < per_piece)
            def _():
                for copy in loads(j + 1):
                    copy.start()

            @pl.when(j >= 2)
            def _():
                for copy in results(j - 2):
                    copy.wait()

            biases = []
            for which in (1 - member, member):
                first = pl.multiple_of(which * hidden_half + j * half, half)
                biases.append(hidden_bias_ref[:, pl.ds(first, half)])
            bias = jnp.concatenate(biases, axis=1)
            for step in range(half_rows // TILE):
                at = slice(step * TILE, (step + 1) * TILE)
                value = dot_nn(low[at, :], expand_buf[slot]) + bias
                below, bell = normal_cells(value)
                held = (value * below).astype(LOW)
                active[slot, at, :] = held
                slope[slot, at, :] = (below + value * bell * 0.3989422804014327).astype(LOW)
                acc[at, :] += dot_nt(held, reduce_buf[slot])
            for copy in results(j):
                copy.start()

        return chunk

    phase("feed", per_piece, chunk_of(0))
    phase("last", per_piece, chunk_of(per_piece))
    leave(acc, acc_out)
    for p in range(pieces):
        lines.finish(p)
    for j in (chunks - 2, chunks - 1):
        for copy in results(j):
            copy.wait()
    for copy in leaving:
        copy.wait()


def front(lengths, dealing, project, merge, expand, reduce, vectors, hidden_bias, tokens, cotangent, parts):
    shard_rows, hidden_half = expand.shape
    pieces, columns = 3, hidden_half
    half_rows, width = tokens.shape
    rows, pairs, depth = 2 * half_rows, project.shape[2] // PAIR, parts // 4
    inner, half = pairs * PAIR, 256
    chunks, both = hidden_half // half, 2 * half
    shape, sem = jax.ShapeDtypeStruct, pltpu.SemaphoreType.DMA
    vmem, anywhere = pl.BlockSpec(memory_space=pltpu.VMEM), pl.BlockSpec(memory_space=pl.ANY)
    held = [
        ((pairs, rows, 3 * PAIR), LOW),
        ((width, rows), LOW),
        ((half_rows, width), LOW),
        ((rows, inner), LOW),
        ((pairs, 8, rows), WIDE),
        ((half_rows, width), WIDE),
        ((half_rows, width), WIDE),
        ((half_rows, 128), WIDE),
        ((width, half_rows), LOW),
        ((chunks, half_rows, both), LOW),
        ((chunks, half_rows, both), LOW),
        ((half_rows, inner), LOW),
    ]
    return pl.pallas_call(
        functools.partial(front_kernel, depth),
        in_specs=[*[pl.BlockSpec(memory_space=pltpu.SMEM)] * 2, *[vmem] * 6, *[anywhere] * 2],
        out_specs=[anywhere] * 14,
        out_shape=[
            shape((pieces, parts * shard_rows, columns), LOW),
            shape((pieces, parts * shard_rows, columns), LOW),
            *[shape(*one) for one in held],
        ],
        scratch_shapes=[
            pltpu.VMEM((pieces, shard_rows, columns), LOW),
            pltpu.VMEM((rows - LONGEST, rows - LONGEST), WIDE),
            pltpu.VMEM((2, half_rows, width), LOW),
            pltpu.VMEM((2, half_rows, width), LOW),
            pltpu.VMEM((rows, width), LOW),
            pltpu.VMEM((width, rows), LOW),
            pltpu.VMEM((half_rows, width), LOW),
            pltpu.VMEM((width, pairs * 3 * PAIR), LOW),
            pltpu.VMEM((pairs, rows, 3 * PAIR), LOW),
            pltpu.VMEM((rows, inner), LOW),
            pltpu.VMEM((pairs, 8, rows), WIDE),
            pltpu.VMEM((half_rows, width), WIDE),
            pltpu.VMEM((half_rows, width), WIDE),
            pltpu.VMEM((half_rows, 128), WIDE),
            pltpu.VMEM((half_rows, width), LOW),
            pltpu.VMEM((width, half_rows), LOW),
            pltpu.VMEM((2, half_rows, both), LOW),
            pltpu.VMEM((2, half_rows, both), LOW),
            pltpu.VMEM((half_rows, inner), LOW),
            pltpu.VMEM((width, inner), LOW),
            pltpu.VMEM((width, inner), LOW),
            pltpu.VMEM((2, width, both), LOW),
            pltpu.VMEM((2, width, both), LOW),
            sem((pieces + 2,)),
            sem((3, 2)),
            sem((10,)),
            sem((2, 2, 2)),
            sem((2, 2)),
            *Gather.semaphores(depth, pieces),
        ],
        compiler_params=pltpu.CompilerParams(
            collective_id=0, has_side_effects=True, vmem_limit_bytes=62 * MIB
        ),
    )(lengths, dealing, project, merge, expand, reduce, vectors, hidden_bias, tokens, cotangent)


def normal_cells(value):
    bell = jnp.exp(value * value * -0.5)
    t = 1.0 / (1.0 + 0.39 * 0.7071067811865476 * jnp.abs(value))
    tail = -0.2275377237624147
    for factor in (
        0.8866668177122106,
        -0.6354042576077721,
        0.649562611731642,
        0.0913871257655044,
        0.23532542445435511,
    ):
        tail = tail * t + factor
    tail = 0.5 * tail * t * bell
    return jnp.where(value < 0.0, tail, 1.0 - tail), bell


def norm(values):
    center = values - jnp.mean(values, axis=1, keepdims=True)
    spread = jnp.mean(center * center, axis=1, keepdims=True)
    scale = lax.rsqrt(spread + norm_epsilon)
    return center * scale, scale


def norm_back(scaled, unit, scale):
    return scale * (
        scaled
        - jnp.mean(scaled, axis=1, keepdims=True)
        - unit * jnp.mean(scaled * unit, axis=1, keepdims=True)
    )


def feed_kernel(
    context_ref, merge_ref, merge_far_ref, whole_ref, far_ref, hidden_ref, upstream_ref, vectors_ref, bias_ref,
    encoded_ref, branch_ref, grad_ref, merge_grad_ref, expand_grad_ref, reduce_grad_ref, sums_ref, hidden_sums_ref,
    own_ctx, far_ctx, acc, normal, inverse, low, turned, late, late_turned, active, slope, inner_grad,
    expand_buf, reduce_buf, arrived, leaving, kept, done, grad_own, grad_far, merge_send, merge_recv,
    ctx_sem, load_sem, send_sem, recv_sem, out_sem, last_sem,
):
    rows = hidden_ref.shape[0]
    chunks, _, both = bias_ref.shape
    half = both // 2
    per_piece = whole_ref.shape[2] // (2 * half)
    member = lax.axis_index("tensor")
    peer = {"tensor": 1 - member}
    tall, short = 256, 128
    width = hidden_ref.shape[1]

    def across(source, target, send, receive):
        return pltpu.make_async_remote_copy(
            src_ref=source,
            dst_ref=target,
            send_sem=send,
            recv_sem=receive,
            device_id=peer,
            device_id_type=MESH,
        )

    def rows_of(which):
        return pl.ds(pl.multiple_of(which * rows, rows), rows)

    def tile(step, size):
        return pl.ds(pl.multiple_of(step * size, size), size)

    def loads(j, slot):
        piece, at = 1 + j // per_piece, lax.rem(j, per_piece) * half
        copies = []
        for kind, buf in enumerate((expand_buf, reduce_buf)):
            first = pl.multiple_of(at + kind * per_piece * half, half)
            for side, source in enumerate((far_ref, whole_ref)):
                copies.append(
                    pltpu.make_async_copy(
                        source.at[piece, :, pl.ds(first, half)],
                        buf.at[slot, :, pl.ds(side * half, half)],
                        load_sem.at[slot, kind, side],
                    )
                )
        return copies

    for copy in loads(0, 0):
        copy.start()
    barrier = pltpu.get_barrier_semaphore()
    pl.semaphore_signal(barrier, inc=1, device_id=peer, device_id_type=MESH)
    pl.semaphore_wait(barrier, 1)
    out_ctx = across(context_ref.at[rows_of(1 - member)], far_ctx, ctx_sem.at[0], ctx_sem.at[1])
    out_ctx.start()
    in_ctx = pltpu.make_async_copy(context_ref.at[rows_of(member)], own_ctx, ctx_sem.at[2])
    in_ctx.start()
    sums_ref[...] = jnp.zeros_like(sums_ref)
    in_ctx.wait()
    out_ctx.wait()

    def add_sum(row, values):
        sums_ref[row : row + 1, :] += jnp.sum(values, axis=0, keepdims=True)

    @pl.loop(0, rows // short)
    def _(step):
        at = tile(step, short)
        branch = dot_nt(own_ctx[at, :], merge_ref[...]) + dot_nt(far_ctx[at, :], merge_far_ref[...])
        unit, scale = norm(hidden_ref[at, :].astype(WIDE) + branch + vectors_ref[2:3, :])
        normed = unit * vectors_ref[3:4, :] + vectors_ref[4:5, :]
        normal[at, :] = unit
        inverse[at, :] = jnp.broadcast_to(scale, (short, 128))
        low[at, :] = normed.astype(LOW)
        turned[:, at] = normed.T.astype(LOW)
        acc[at, :] = normed + vectors_ref[5:6, :]

    @pl.loop(0, chunks)
    def _(j):
        slot = lax.rem(j, 2)
        for copy in loads(j, slot):
            copy.wait()

        @pl.when(j + 1 < chunks)
        def _():
            for copy in loads(j + 1, 1 - slot):
                copy.start()

        for step in range(rows // tall):
            at = slice(step * tall, (step + 1) * tall)
            inner = dot_nn(low[at, :], expand_buf[slot]) + bias_ref[j]
            below, bell = normal_cells(inner)
            held = (inner * below).astype(LOW)
            active[j, at, :] = held
            slope[j, at, :] = (below + inner * bell * 0.3989422804014327).astype(LOW)
            acc[at, :] += dot_nt(held, reduce_buf[slot])

    for copy in loads(0, 0):
        copy.start()

    @pl.loop(0, rows // short)
    def _(step):
        at = tile(step, short)
        unit, scale = norm(acc[at, :])
        encoded_ref[at, :] = (unit * vectors_ref[6:7, :] + vectors_ref[7:8, :]).astype(LOW)
        upper = upstream_ref[at, :].astype(WIDE)
        add_sum(6, upper * unit)
        add_sum(7, upper)
        grad = norm_back(upper * vectors_ref[6:7, :], unit, scale)
        grad_low = grad.astype(LOW)
        add_sum(5, grad_low.astype(WIDE))
        acc[at, :] = grad
        late[at, :] = grad_low
        late_turned[:, at] = grad.T.astype(LOW)

    def send(j, kind):
        return across(
            leaving.at[lax.rem(j, 2), kind],
            arrived.at[lax.rem(j, 4), kind],
            send_sem.at[lax.rem(j, 2), kind],
            recv_sem.at[lax.rem(j, 4), kind],
        )

    def store(j, kind):
        target = (expand_grad_ref, reduce_grad_ref)[kind]
        cols = pl.ds(pl.multiple_of(j * half, half), half)
        return pltpu.make_async_copy(
            done.at[lax.rem(j, 2), kind], target.at[:, cols], out_sem.at[lax.rem(j, 2), kind]
        )

    def finish(j):
        for kind in range(2):
            send(j, kind).wait_recv()

            @pl.when(j >= 2)
            def _():
                store(j - 2, kind).wait()

            @pl.loop(0, width // tall)
            def _(step):
                at = tile(step, tall)
                done[lax.rem(j, 2), kind, at, :] = (
                    kept[lax.rem(j, 2), kind, at, :]
                    + arrived[lax.rem(j, 4), kind, at, :].astype(WIDE)
                ).astype(LOW)

            store(j, kind).start()

    @pl.loop(0, chunks)
    def _(j):
        slot = lax.rem(j, 2)
        for copy in loads(j, slot):
            copy.wait()

        @pl.when(j + 1 < chunks)
        def _():
            for copy in loads(j + 1, 1 - slot):
                copy.start()

        total = jnp.zeros((1, both), WIDE)
        for step in range(rows // tall):
            at = slice(step * tall, (step + 1) * tall)
            grad = dot_nn(late[at, :], reduce_buf[slot]) * slope[j, at, :].astype(WIDE)
            grad = grad.astype(LOW)
            inner_grad[at, :] = grad
            total = total + jnp.sum(grad.astype(WIDE), axis=0, keepdims=True)
            acc[at, :] += dot_nt(grad, expand_buf[slot])
        hidden_sums_ref[j] = total

        @pl.when(j >= 2)
        def _():
            for kind in range(2):
                send(j - 2, kind).wait_send()

        for kind, (left, right) in enumerate(((turned, inner_grad), (late_turned, active.at[j]))):
            for step in range(width // tall):
                at = slice(step * tall, (step + 1) * tall)
                part = dot_nn(left[at, :], right[...])
                leaving[slot, kind, at, :] = part[:, 0:half].astype(LOW)
                kept[slot, kind, at, :] = part[:, half:both]
            send(j, kind).start()

        @pl.when(j >= 1)
        def _():
            finish(j - 1)

    @pl.loop(0, rows // short)
    def _(step):
        at = tile(step, short)
        grad = acc[at, :]
        unit = normal[at, :]
        add_sum(3, grad * unit)
        add_sum(4, grad)
        branch_grad = norm_back(grad * vectors_ref[3:4, :], unit, inverse[at, 0:1])
        branch_low = branch_grad.astype(LOW)
        add_sum(2, branch_low.astype(WIDE))
        branch_ref[at, :] = branch_grad
        turned[:, at] = branch_grad.T.astype(LOW)
        grad_far[at, :] = dot_nn(branch_low, merge_far_ref[...]).astype(LOW)
        grad_own[at, :] = dot_nn(branch_low, merge_ref[...]).astype(LOW)

    out_grad = across(grad_far, grad_ref.at[rows_of(member)], ctx_sem.at[0], ctx_sem.at[1])
    out_grad.start()
    in_grad = pltpu.make_async_copy(grad_own, grad_ref.at[rows_of(member)], ctx_sem.at[2])
    in_grad.start()
    for step in range(width // tall):
        at = slice(step * tall, (step + 1) * tall)
        merge_send[at, :] = dot_nn(turned[at, :], far_ctx[...]).astype(LOW)
    out_merge = across(merge_send, merge_recv, last_sem.at[0], last_sem.at[1])
    out_merge.start()
    finish(chunks - 1)
    for kind in range(2):
        send(chunks - 2, kind).wait_send()
        send(chunks - 1, kind).wait_send()
        store(chunks - 2, kind).wait()
        store(chunks - 1, kind).wait()
    out_merge.wait()
    for step in range(width // tall):
        at = slice(step * tall, (step + 1) * tall)
        merge_grad_ref[at, :] = (
            dot_nn(turned[at, :], own_ctx[...]) + merge_recv[at, :].astype(WIDE)
        ).astype(LOW)
    out_grad.wait()
    in_grad.wait()


def feed_block(context, whole, far, hidden_own, upstream, vectors, bias_own, bias_far):
    total_rows, inner = context.shape
    rows, width = hidden_own.shape
    hidden = bias_own.shape[0]
    merge, merge_far = whole[0, :, -inner:], far[0, :, -inner:]
    half = 256
    chunks = hidden // half
    both = 2 * half
    bias = jnp.concatenate(
        [bias_far.reshape(chunks, 1, half), bias_own.reshape(chunks, 1, half)], axis=2
    )
    vmem, anywhere = pl.BlockSpec(memory_space=pltpu.VMEM), pl.BlockSpec(memory_space=pl.ANY)
    sem = pltpu.SemaphoreType.DMA
    shape = jax.ShapeDtypeStruct
    *results, hidden_sums = pl.pallas_call(
        feed_kernel,
        in_specs=[anywhere, vmem, vmem, *[anywhere] * 2, *[vmem] * 4],
        out_specs=[vmem, vmem, anywhere, vmem, anywhere, anywhere, vmem, vmem],
        out_shape=[
            shape((rows, width), LOW),
            shape((rows, width), WIDE),
            shape((total_rows, inner), LOW),
            shape((width, inner), LOW),
            shape((width, hidden), LOW),
            shape((width, hidden), LOW),
            shape((8, width), WIDE),
            shape((chunks, 1, both), WIDE),
        ],
        scratch_shapes=[
            pltpu.VMEM((rows, inner), LOW),
            pltpu.VMEM((rows, inner), LOW),
            pltpu.VMEM((rows, width), WIDE),
            pltpu.VMEM((rows, width), WIDE),
            pltpu.VMEM((rows, 128), WIDE),
            pltpu.VMEM((rows, width), LOW),
            pltpu.VMEM((width, rows), LOW),
            pltpu.VMEM((rows, width), LOW),
            pltpu.VMEM((width, rows), LOW),
            pltpu.VMEM((chunks, rows, both), LOW),
            pltpu.VMEM((chunks, rows, both), LOW),
            pltpu.VMEM((rows, both), LOW),
            pltpu.VMEM((2, width, both), LOW),
            pltpu.VMEM((2, width, both), LOW),
            pltpu.VMEM((4, 2, width, half), LOW),
            pltpu.VMEM((2, 2, width, half), LOW),
            pltpu.VMEM((2, 2, width, half), WIDE),
            pltpu.VMEM((2, 2, width, half), LOW),
            pltpu.VMEM((rows, inner), LOW),
            pltpu.VMEM((rows, inner), LOW),
            pltpu.VMEM((width, inner), LOW),
            pltpu.VMEM((width, inner), LOW),
            sem((3,)),
            sem((2, 2, 2)),
            sem((2, 2)),
            sem((4, 2)),
            sem((2, 2)),
            sem((2,)),
        ],
        compiler_params=pltpu.CompilerParams(
            collective_id=2, has_side_effects=True, vmem_limit_bytes=60 * MIB
        ),
        cost_estimate=pl.CostEstimate(
            flops=12 * rows * width * 2 * hidden, bytes_accessed=8 * width * hidden * 4, transcendentals=0
        ),
    )(context, merge, merge_far, whole, far, hidden_own, upstream, vectors, bias)
    hidden_far = hidden_sums[:, 0, :half].reshape(-1)
    hidden_near = hidden_sums[:, 0, half:].reshape(-1)
    return (*results, hidden_near, hidden_far)


class Scatter:
    buffers = 8

    def __init__(self, depth, grads, shards, buffers, sems):
        self.depth, self.grads, self.shards = depth, grads, shards
        self.held = [buffers[8 * p : 8 * p + 8] for p in range(len(grads))]
        self.me, self.z, self.y, self.x = place()
        self.x_peer = self.z * 4 + self.y * 2 + 1 - self.x
        self.y_peer = self.z * 4 + (1 - self.y) * 2 + self.x
        self.rows = grads[0].shape[0] // (4 * depth)
        (
            self.a1_send, self.a1_recv, self.a2_send, self.a2_recv, self.b2_send, self.b2_recv, self.b1_send, self.b1_recv,
            self.z_send, self.z_recv, self.zc_send, self.zc_recv, self.c_send, self.c_recv,
        ) = sems

    @staticmethod
    def scratch(depth, rows, classes):
        found = []
        for a, b, c in classes:
            found += [
                pltpu.VMEM((depth, 2 * rows, a), LOW),
                pltpu.VMEM((depth, 2, rows, b), LOW),
                pltpu.VMEM((depth, rows, a), LOW),
                pltpu.VMEM((depth, rows, b), LOW),
                pltpu.VMEM((depth + 1, rows, a + b), LOW),
                pltpu.VMEM((depth + 1, 4 * rows, c), LOW),
                pltpu.VMEM((2 * rows, c), LOW),
                pltpu.VMEM((rows, c), LOW),
            ]
        return found

    @staticmethod
    def semaphores(depth, pieces):
        sem = pltpu.SemaphoreType.DMA
        return [
            *[sem((pieces, depth))] * 6,
            *[sem((pieces, depth, 2))] * 2,
            *[sem((pieces, depth)), sem((pieces, depth + 1))] * 2,
            sem((pieces, 2)),
            sem((pieces, 2)),
        ]

    def columns(self, p):
        a, b, c = (self.held[p][i].shape[-1] for i in (0, 1, 5))
        return pl.ds(0, a), pl.ds(a, b), pl.ds(a + b, c)

    def block(self, zb, yb, xb):
        return zb * 4 + yb * 2 + xb

    def span(self, block, count=1):
        return pl.ds(pl.multiple_of(block * self.rows, self.rows), count * self.rows)

    def add(self, put, count, *terms):
        chunk = min(count, 64)

        @pl.loop(0, count // chunk)
        def _(step):
            at = pl.multiple_of(step * chunk, chunk)
            parts = [term(at, chunk) for term in terms]
            if len(parts) > 2 or put.wide:
                parts = [part.astype(WIDE) for part in parts]
            total = parts[0]
            for part in parts[1:]:
                total = total + part
            put(at, chunk, total)

    def a1(self, p, zb):
        return remote(
            self.grads[p].at[self.span(self.block(zb, 1 - self.y, 0), 2), self.columns(p)[0]],
            self.held[p][0].at[zb],
            self.a1_send.at[p, zb],
            self.a1_recv.at[p, zb],
            self.y_peer,
        )

    def b1(self, p, zb, yb):
        return remote(
            self.grads[p].at[self.span(self.block(zb, yb, 1 - self.x)), self.columns(p)[1]],
            self.held[p][1].at[zb, yb],
            self.b1_send.at[p, zb, yb],
            self.b1_recv.at[p, zb, yb],
            self.x_peer,
        )

    def a2(self, p, zb):
        return remote(
            self.held[p][0].at[zb, self.span(1 - self.x)],
            self.held[p][2].at[zb],
            self.a2_send.at[p, zb],
            self.a2_recv.at[p, zb],
            self.x_peer,
        )

    def b2(self, p, zb):
        return remote(
            self.held[p][1].at[zb, 1 - self.y],
            self.held[p][3].at[zb],
            self.b2_send.at[p, zb],
            self.b2_recv.at[p, zb],
            self.y_peer,
        )

    def slot(self, zb, way):
        return zb if way > 0 else zb + (self.depth - zb) * jnp.where(zb == self.z - 1, 1, 0)

    def z_copy(self, p, zb, way):
        slot = self.slot(zb, way)
        return remote(
            self.held[p][4].at[zb],
            self.held[p][4].at[slot],
            self.z_send.at[p, zb],
            self.z_recv.at[p, slot],
            self.me + 4 * way,
        )

    def zc_copy(self, p, zb, way, first):
        slot = self.slot(zb, way)
        source = self.held[p][5].at[zb]
        if first:
            source = self.grads[p].at[self.span(zb * 4, 4), self.columns(p)[2]]
        return remote(
            source,
            self.held[p][5].at[slot],
            self.zc_send.at[p, zb],
            self.zc_recv.at[p, slot],
            self.me + 4 * way,
        )

    def arrived(self, ref, sem, slot):
        part = ref.at[slot]
        remote(part, part, sem, sem, self.me).wait_recv()

    def cy(self, p):
        return remote(
            self.held[p][5].at[self.z, self.span(2 * (1 - self.y), 2)],
            self.held[p][6],
            self.c_send.at[p, 0],
            self.c_recv.at[p, 0],
            self.y_peer,
        )

    def cx(self, p):
        return remote(
            self.held[p][5].at[self.z, self.span(2 * self.y + 1 - self.x)],
            self.held[p][7],
            self.c_send.at[p, 1],
            self.c_recv.at[p, 1],
            self.x_peer,
        )

    def grad(self, p, block, columns):
        def term(at, count):
            first = pl.multiple_of(block * self.rows + at, 16)
            return self.grads[p][pl.ds(first, count), columns]

        return term

    def part(self, ref, lead, block, columns=None):
        columns = slice(None) if columns is None else columns

        def term(at, count):
            first = pl.multiple_of(block * self.rows + at, 16)
            return ref[(*lead, pl.ds(first, count), columns)]

        return term

    def put(self, ref, lead, block, columns=None):
        columns = slice(None) if columns is None else columns

        def act(at, count, total):
            first = pl.multiple_of(block * self.rows + at, 16)
            ref[(*lead, pl.ds(first, count), columns)] = total.astype(ref.dtype)

        act.wide = ref.dtype == WIDE
        return act

    def open(self, p, zb):
        self.a1(p, zb).start()
        self.b1(p, zb, 0).start()
        self.b1(p, zb, 1).start()

    def first(self, p, zb):
        z, y, x = self.z, self.y, self.x
        a, b, _ = self.columns(p)
        r1a, r1b = self.held[p][0], self.held[p][1]
        self.a1(p, zb).wait_recv()
        self.add(
            self.put(r1a, (zb,), 1 - x),
            self.rows,
            self.part(r1a, (zb,), 1 - x),
            self.grad(p, self.block(zb, y, 1 - x), a),
        )
        self.a2(p, zb).start()
        self.b1(p, zb, 0).wait_recv()
        self.b1(p, zb, 1).wait_recv()
        self.add(
            self.put(r1b, (zb, 1 - y), 0),
            self.rows,
            self.part(r1b, (zb, 1 - y), 0),
            self.grad(p, self.block(zb, 1 - y, x), b),
        )
        self.b2(p, zb).start()

    def terms(self, p, zb):
        z, y, x = self.z, self.y, self.x
        a, b, _ = self.columns(p)
        r1a, r1b, r2a, r2b = self.held[p][:4]
        own = self.block(zb, y, x)
        return (
            [self.grad(p, own, a), self.part(r1a, (zb,), x), self.part(r2a, (zb,), 0)],
            [self.grad(p, own, b), self.part(r1b, (zb, y), 0), self.part(r2b, (zb,), 0)],
        )

    def pass_on(self, p, zb, way):
        a, b, _ = self.columns(p)
        rz = self.held[p][4]
        self.a2(p, zb).wait_recv()
        self.b2(p, zb).wait_recv()
        from_line = (self.z - way >= 0) & (self.z - way < self.depth)

        @pl.when(from_line)
        def _():
            self.arrived(rz, self.z_recv.at[p, zb], zb)
            for terms, columns in zip(self.terms(p, zb), (a, b), strict=True):
                self.add(
                    self.put(rz, (zb,), 0, columns),
                    self.rows,
                    *terms,
                    self.part(rz, (zb,), 0, columns),
                )

        @pl.when(jnp.logical_not(from_line))
        def _():
            for terms, columns in zip(self.terms(p, zb), (a, b), strict=True):
                self.add(self.put(rz, (zb,), 0, columns), self.rows, *terms)

        self.z_copy(p, zb, way).start()

    def pass_c(self, p, zb, way):
        c = self.columns(p)[2]
        rc = self.held[p][5]
        from_line = (self.z - way >= 0) & (self.z - way < self.depth)

        @pl.when(from_line)
        def _():
            self.arrived(rc, self.zc_recv.at[p, zb], zb)
            self.add(
                self.put(rc, (zb,), 0),
                4 * self.rows,
                self.part(rc, (zb,), 0),
                self.grad(p, zb * 4, c),
            )
            self.zc_copy(p, zb, way, False).start()

        @pl.when(jnp.logical_not(from_line))
        def _():
            self.zc_copy(p, zb, way, True).start()

    def own_c(self, p):
        z, depth = self.z, self.depth
        c = self.columns(p)[2]
        rc = self.held[p][5]
        grad = self.grad(p, z * 4, c)
        lower, upper = self.part(rc, (z,), 0), self.part(rc, (depth,), 0)
        put = self.put(rc, (z,), 0)

        @pl.when(z > 0)
        def _():
            self.arrived(rc, self.zc_recv.at[p, z], z)

        @pl.when(z < depth - 1)
        def _():
            self.arrived(rc, self.zc_recv.at[p, depth], depth)

        @pl.when((z > 0) & (z < depth - 1))
        def _():
            self.add(put, 4 * self.rows, grad, lower, upper)

        @pl.when(z == 0)
        def _():
            self.add(put, 4 * self.rows, grad, upper)

        @pl.when(z == depth - 1)
        def _():
            self.add(put, 4 * self.rows, grad, lower)

        self.cy(p).start()

    def turn_c(self, p):
        rc, rcy = self.held[p][5], self.held[p][6]
        self.cy(p).wait_recv()
        self.add(
            self.put(rc, (self.z,), 2 * self.y),
            2 * self.rows,
            self.part(rc, (self.z,), 2 * self.y),
            self.part(rcy, (), 0),
        )
        self.cx(p).start()

    def close(self, p):
        z, depth = self.z, self.depth
        a, b, c = self.columns(p)
        rz, rc, rcx = self.held[p][4], self.held[p][5], self.held[p][7]
        self.a2(p, z).wait_recv()
        self.b2(p, z).wait_recv()

        @pl.when(z > 0)
        def _():
            self.arrived(rz, self.z_recv.at[p, z], z)

        @pl.when(z < depth - 1)
        def _():
            self.arrived(rz, self.z_recv.at[p, depth], depth)

        def total(*slots):
            for terms, columns in zip(self.terms(p, z), (a, b), strict=True):
                lines = [self.part(rz, (slot,), 0, columns) for slot in slots]
                self.add(self.put(self.shards[p], (), 0, columns), self.rows, *terms, *lines)

        pl.when((z > 0) & (z < depth - 1))(lambda: total(z, depth))
        pl.when(z == 0)(lambda: total(depth))
        pl.when(z == depth - 1)(lambda: total(z))
        self.cx(p).wait_recv()
        self.add(
            self.put(self.shards[p], (), 0, c),
            self.rows,
            self.part(rc, (z,), 2 * self.y + self.x),
            self.part(rcx, (), 0),
        )

    def at_step(self, step, act):
        z, depth = self.z, self.depth
        if step < 0:
            act(z, 0)
            return
        for zb, valid, way in (
            (z + 1 + step, z + 1 + step < depth, 1),
            (z - 1 - step, z - 1 - step >= 0, -1),
        ):
            pl.when(valid)(functools.partial(act, zb, way))

    def stage(self, p, s):
        last = self.depth - 2

        def opened(step):
            self.at_step(step, lambda zb, way: self.open(p, zb))

        def added(step):
            self.at_step(step, lambda zb, way: self.first(p, zb))

        def passed(step):
            self.at_step(step, lambda zb, way: self.pass_on(p, zb, way))

        def passed_c(step):
            self.at_step(step, lambda zb, way: self.pass_c(p, zb, way))

        if s == 0:
            opened(last)
            opened(last - 1)
            passed_c(last)
            return
        if s <= last + 2:
            added(last + 1 - s)
        if last - 1 - s >= -1:
            opened(last - 1 - s)
        if last - s >= 0:
            passed_c(last - s)
        if s >= 2 and last + 2 - s >= 0:
            passed(last + 2 - s)
        if s == last + 1:
            self.own_c(p)
        if s == last + 2:
            self.turn_c(p)
        if s == last + 3:
            self.close(p)

    def sent(self, p):
        def line(zb, way):
            from_line = (self.z - way >= 0) & (self.z - way < self.depth)
            self.z_copy(p, zb, way).wait_send()
            pl.when(from_line)(lambda: self.zc_copy(p, zb, way, False).wait_send())
            pl.when(jnp.logical_not(from_line))(lambda: self.zc_copy(p, zb, way, True).wait_send())

        for zb in range(self.depth):
            self.a1(p, zb).wait_send()
            self.b1(p, zb, 0).wait_send()
            self.b1(p, zb, 1).wait_send()
            self.a2(p, zb).wait_send()
            self.b2(p, zb).wait_send()
        for step in range(self.depth - 1):
            self.at_step(step, line)
        self.cy(p).wait_send()
        self.cx(p).wait_send()


class SmallSum:
    def __init__(self, lines, buffer, send, recv):
        member = lax.axis_index("tensor")
        self.partners = [{"tensor": 1 - member}, {"dp": lines.x_peer}, {"dp": lines.y_peer}]
        for level in range(lines.depth.bit_length() - 1):
            reach = 1 << level
            way = 1 - 2 * ((lines.z // reach) % 2)
            self.partners.append({"dp": lines.me + 4 * reach * way})
        self.buffer, self.send, self.recv = buffer, send, recv

    def copy(self, step):
        return pltpu.make_async_remote_copy(
            src_ref=self.buffer.at[step],
            dst_ref=self.buffer.at[len(self.partners) + 1 + step],
            send_sem=self.send.at[step],
            recv_sem=self.recv.at[step],
            device_id=self.partners[step],
            device_id_type=MESH,
        )

    def step(self, step):
        if step:
            self.copy(step - 1).wait_recv()
            self.buffer[step] = self.buffer[step - 1] + self.buffer[len(self.partners) + step]
        if step < len(self.partners):
            self.copy(step).start()

    def sent(self):
        for step in range(len(self.partners)):
            self.copy(step).wait_send()


def adamw_update(master, moment, square, gradient, step_rate, decay_rate):
    moment_new = beta_one * moment + (1.0 - beta_one) * gradient
    square_new = beta_two * square + (1.0 - beta_two) * gradient * gradient
    moment_hat = moment_new / (1.0 - beta_one**STEP)
    square_hat = square_new / (1.0 - beta_two**STEP)
    master_new = master - step_rate * (
        moment_hat / (jnp.sqrt(square_hat) + adam_epsilon) + decay_rate * master
    )
    return (moment_new, square_new, master_new)


SCATTER_AT = {
    "reduce": {4: [(0, 0)]},
    "expand": {2: [(0, 1), (1, 0)], 4: [(0, 2)], 5: [(1, 1)]},
    "norm": {-1: [(3, 0)], 0: [(1, 2)], 4: [(0, 3)]},
    "merge": {-1: [(3, 1)], 1: [(2, 0)]},
    "attend": {
        0: [(3, 2)], 1: [(2, 1)], 4: [(0, 4)], 9: [(2, 2)], 10: [(1, 3)], 16: [(4, 1)], 18: [(0, 5), (3, 3)], 22: [(4, 2), (2, 3)],
    },
    "project": {0: [(4, 0)], 1: [(5, 0)]},
    "terms": {0: [(4, 3)], 1: [(5, 1)], 3: [(2, 4)], 4: [(3, 4), (5, 2)]},
    "far": {1: [(1, 4)]},
    "near": {-1: [(4, 4), (5, 3)], 0: [(2, 5)]},
    "encoded": {0: [(1, 5)], 1: [(4, 5)]},
    "adam": {-1: [(5, 4)], 0: [(3, 5)]},
    "end": [(5, 5)],
}


def back_kernel(
    depth, lengths_ref, dealing_ref, vectors_ref, vectors_first, vectors_second, hidden_ref, hidden_first, hidden_second,
    whole_ref, far_ref, qkv_in, hidden_turned_in, upstream_in, context_in, totals_in,
    acc_in, normal_in, inverse_in, turned_in, active_in, slope_in, far_ctx_in, *rest,
):
    states_in, rest = rest[:12], rest[12:]
    encoded_out, input_out, vector_grad_ref, *rest = rest
    states_out, small_out, rest = rest[:12], rest[12:18], rest[18:]
    enc_pair, grad_ref, input_far, acc, arrived, merge_recv, small, score_bias, *rest = rest
    grads, shards, rest = rest[:6], rest[6:12], rest[12:]
    buffers, rest = rest[: 6 * Scatter.buffers], rest[6 * Scatter.buffers :]
    small_send, small_recv, in_sem, load_sem, ctx_sem, far_send, far_recv, merge_sem, enc_sem, input_sem, state_sem, *sems = rest
    lines = Scatter(depth, grads, shards, buffers, sems)
    sums = SmallSum(lines, small, small_send, small_recv)
    group = Group(lengths_ref, dealing_ref)
    member = lax.axis_index("tensor")
    rows, width = acc.shape
    total_rows = 2 * rows
    chunks, _, both = active_in.shape
    half = both // 2
    per_piece = chunks // 2
    piece_span = grads[0].shape[1]
    pairs = qkv_in.shape[0]
    inner = pairs * PAIR
    tall, short = 256, 128

    def rows_of(which):
        return pl.ds(pl.multiple_of(which * rows, rows), rows)

    def tile(step, size):
        return pl.ds(pl.multiple_of(step * size, size), size)

    def fetch(source, target, sem):
        return pltpu.make_async_copy(source, target, in_sem.at[sem])

    def phase(name, count, body):
        between = {
            step: [functools.partial(lines.stage, *stage) for stage in stages]
            for step, stages in SCATTER_AT.get(name, {}).items()
        }
        for act in between.pop(-1, ()):
            act()
        looped(count, body, between)

    def places_of(first):
        return first + lax.broadcasted_iota(jnp.int32, (tall, 1), 0)

    def add_sum(row, values):
        small[0, row : row + 1, :] += jnp.sum(values, axis=0, keepdims=True)

    acc_copy = fetch(acc_in, acc, 0)
    acc_copy.start()
    greet_line(
        lines.me, lines.z, lines.y, lines.x, depth, [sums.partners[0], *sums.partners[3:]]
    )
    small[0] = jnp.zeros(small.shape[1:], WIDE)
    score_bias[...] = group.score_bias(total_rows - LONGEST)

    def feed_phase(late, late_turned, turned, upstream, active, slope, inner_grad, expand_buf, reduce_buf, leaving, encoded):
        def active_load(j):
            slot = lax.rem(j, 2)
            return [pltpu.make_async_copy(active_in.at[j], active.at[slot], load_sem.at[slot, 4])]

        def loads(j):
            slot = lax.rem(j, 2)
            piece, at = 1 + j // per_piece, lax.rem(j, per_piece) * half
            copies = [pltpu.make_async_copy(slope_in.at[j], slope.at[slot], load_sem.at[slot, 5])]
            for kind, buf in enumerate((expand_buf, reduce_buf)):
                first = pl.multiple_of(at + kind * per_piece * half, half)
                for side, source in enumerate((far_ref, whole_ref)):
                    copies.append(
                        pltpu.make_async_copy(
                            source.at[piece, :, pl.ds(first, half)],
                            buf.at[slot, :, pl.ds(side * half, half)],
                            load_sem.at[slot, 2 * kind + side],
                        )
                    )
            return copies

        def taken(j, load):
            for copy in load(j):
                copy.wait()

            @pl.when(j + 1 < chunks)
            def _():
                for copy in load(j + 1):
                    copy.start()

        fetches = [fetch(upstream_in, upstream, 1), fetch(turned_in, turned, 2)]
        for copy in fetches:
            copy.start()
        for copy in [*active_load(0), *loads(0)]:
            copy.start()
        acc_copy.wait()
        for copy in fetches:
            copy.wait()

        def late_tile(step):
            at = tile(step, short)
            unit, scale = norm(acc[at, :])
            encoded[at, :] = (unit * vectors_ref[6:7, :] + vectors_ref[7:8, :]).astype(LOW)
            upper = upstream[at, :].astype(WIDE)
            add_sum(6, upper * unit)
            add_sum(7, upper)
            grad = norm_back(upper * vectors_ref[6:7, :], unit, scale)
            grad_low = grad.astype(LOW)
            add_sum(5, grad_low.astype(WIDE))
            acc[at, :] = grad
            late[at, :] = grad_low
            late_turned[:, at] = grad.T.astype(LOW)

        looped(rows // short, late_tile, {})
        enc_near = pltpu.make_async_copy(encoded, enc_pair.at[member], enc_sem.at[2])
        enc_far = other_core(encoded, enc_pair.at[member], enc_sem.at[0], enc_sem.at[1])
        enc_near.start()
        enc_far.start()

        def send(k):
            slot = lax.rem(k, 2)
            return other_core(
                leaving.at[slot], arrived.at[slot], far_send.at[slot], far_recv.at[slot]
            )

        def own_columns(k):
            return pl.ds(pl.multiple_of(lax.rem(k, per_piece) * half, half), half)

        def in_piece(k, act):
            for piece in range(4):
                pl.when(k // per_piece == piece)(functools.partial(act, grads[piece]))

        def finish(k):
            send(k).wait_recv()

            def add(grad):
                @pl.loop(0, width // tall)
                def _(step):
                    at = tile(step, tall)
                    grad[at, own_columns(k)] += arrived[lax.rem(k, 2), at, :]

            in_piece(k, add)

        def products(k, left, right):
            @pl.when(k >= 2)
            def _():
                send(k - 2).wait_send()

            for step in range(width // tall):
                at = slice(step * tall, (step + 1) * tall)
                part = dot_nn(left[at, :], right[...])
                leaving[lax.rem(k, 2), at, :] = part[:, 0:half].astype(LOW)
                own = part[:, half:both].astype(LOW)

                def keep(grad, at=at, own=own):
                    grad[at, own_columns(k)] = own

                in_piece(k, keep)

            @pl.when(k >= 1)
            def _():
                finish(k - 1)

            send(k).start()

        def reduce_chunk(j):
            taken(j, active_load)
            products(j, late_turned, active.at[lax.rem(j, 2)])

        def expand_chunk(j):
            slot = lax.rem(j, 2)
            taken(j, loads)
            total = jnp.zeros((1, both), WIDE)
            for step in range(rows // tall):
                at = slice(step * tall, (step + 1) * tall)
                grad = dot_nn(late[at, :], reduce_buf[slot]) * slope[slot, at, :].astype(WIDE)
                grad = grad.astype(LOW)
                inner_grad[at, :] = grad
                total = total + jnp.sum(grad.astype(WIDE), axis=0, keepdims=True)
                acc[at, :] += dot_nt(grad, expand_buf[slot])
            for which, side in ((1 - member, 0), (member, half)):
                row = 8 + which * 2 + j // per_piece
                small[0, pl.ds(row, 1), own_columns(j)] = total[:, side : side + half]
            products(chunks + j, turned, inner_grad)

        phase("reduce", chunks, reduce_chunk)
        phase("expand", chunks, expand_chunk)
        finish(2 * chunks - 1)
        for k in (2 * chunks - 2, 2 * chunks - 1):
            send(k).wait_send()
        enc_near.wait()
        enc_far.wait()

    pl.run_scoped(
        feed_phase,
        pltpu.VMEM((rows, width), LOW),
        pltpu.VMEM((width, rows), LOW),
        pltpu.VMEM((width, rows), LOW),
        pltpu.VMEM((rows, width), LOW),
        pltpu.VMEM((2, rows, both), LOW),
        pltpu.VMEM((2, rows, both), LOW),
        pltpu.VMEM((rows, both), LOW),
        pltpu.VMEM((2, width, both), LOW),
        pltpu.VMEM((2, width, both), LOW),
        pltpu.VMEM((2, width, half), LOW),
        pltpu.VMEM((rows, width), LOW),
    )

    def merge_phase(normal, inverse, turned, near_ctx, far_ctx, merge, merge_far, grad_own, grad_far, merge_send):
        merge_columns = pl.ds(whole_ref.shape[2] - inner, inner)
        fetches = [
            fetch(normal_in, normal, 0),
            fetch(inverse_in, inverse, 1),
            fetch(context_in.at[rows_of(member)], near_ctx, 2),
            fetch(far_ctx_in, far_ctx, 3),
            fetch(whole_ref.at[0, :, merge_columns], merge, 4),
            fetch(far_ref.at[0, :, merge_columns], merge_far, 5),
        ]
        for copy in fetches:
            copy.start()
        for copy in fetches:
            copy.wait()

        def norm_tile(step):
            at = tile(step, short)
            grad = acc[at, :]
            unit = normal[at, :]
            add_sum(3, grad * unit)
            add_sum(4, grad)
            branch_grad = norm_back(grad * vectors_ref[3:4, :], unit, inverse[at, 0:1])
            branch_low = branch_grad.astype(LOW)
            add_sum(2, branch_low.astype(WIDE))
            acc[at, :] = branch_grad
            turned[:, at] = branch_grad.T.astype(LOW)
            grad_far[at, :] = dot_nn(branch_low, merge_far[...]).astype(LOW)
            grad_own[at, :] = dot_nn(branch_low, merge[...]).astype(LOW)

        phase("norm", rows // short, norm_tile)
        out_grad = other_core(grad_far, grad_ref.at[rows_of(member)], ctx_sem.at[0], ctx_sem.at[1])
        in_grad = pltpu.make_async_copy(grad_own, grad_ref.at[rows_of(member)], ctx_sem.at[2])
        out_grad.start()
        in_grad.start()
        out_merge = other_core(merge_send, merge_recv, merge_sem.at[0], merge_sem.at[1])

        def merge_step(which):
            @pl.when(which == 0)
            def _():
                for step in range(width // tall):
                    at = slice(step * tall, (step + 1) * tall)
                    merge_send[at, :] = dot_nn(turned[at, :], far_ctx[...]).astype(LOW)
                out_merge.start()

            @pl.when(which == 1)
            def _():
                out_merge.wait()
                for step in range(width // tall):
                    at = slice(step * tall, (step + 1) * tall)
                    grads[4][at, 0:inner] = (
                        dot_nn(turned[at, :], near_ctx[...]) + merge_recv[at, :].astype(WIDE)
                    ).astype(LOW)

        phase("merge", 2, merge_step)
        out_grad.wait()
        in_grad.wait()

    pl.run_scoped(
        merge_phase,
        pltpu.VMEM((rows, width), WIDE),
        pltpu.VMEM((rows, 128), WIDE),
        pltpu.VMEM((width, rows), LOW),
        pltpu.VMEM((rows, inner), LOW),
        pltpu.VMEM((rows, inner), LOW),
        pltpu.VMEM((width, inner), LOW),
        pltpu.VMEM((width, inner), LOW),
        pltpu.VMEM((rows, inner), LOW),
        pltpu.VMEM((rows, inner), LOW),
        pltpu.VMEM((width, inner), LOW),
    )
    def last_phase(mixed):
        def attend_phase(qkv, context, upper, totals, dots, key_turned, queries, uppers, query_sum, hidden_turned):
            def loads(pair, slot):
                columns = pl.ds(pl.multiple_of(pair * PAIR, PAIR), PAIR)
                return [
                    pltpu.make_async_copy(qkv_in.at[pair], qkv.at[slot], load_sem.at[slot, 0]),
                    pltpu.make_async_copy(
                        context_in.at[:, columns], context.at[slot], load_sem.at[slot, 1]
                    ),
                    pltpu.make_async_copy(
                        grad_ref.at[:, columns], upper.at[slot], load_sem.at[slot, 2]
                    ),
                ]

            fetches = [fetch(totals_in, totals, 0)]
            for copy in [*loads(0, 0), *fetches]:
                copy.start()
            for copy in fetches:
                copy.wait()
            blocks = ((0, LONGEST), (LONGEST, total_rows - LONGEST))
            per_pair = total_rows // TILE

            def hidden_tile(step, slot):
                return pltpu.make_async_copy(
                    hidden_turned_in.at[tile(step, tall), :],
                    hidden_turned.at[slot],
                    load_sem.at[slot, 3],
                )

            def project(second):
                grad, first = (grads[5], 0) if second else (grads[4], inner)
                span = (pairs // 2) * 3 * PAIR
                columns = slice(span if second else 0, span * 2 if second else span)
                hidden_tile(0, 0).start()
                for step in range(width // tall):
                    if step + 1 < width // tall:
                        hidden_tile(step + 1, (step + 1) % 2).start()
                    hidden_tile(step, step % 2).wait()
                    grad[step * tall : (step + 1) * tall, first : first + span] = dot_nn(
                        hidden_turned[step % 2], mixed[:, columns]
                    ).astype(LOW)

            def pair_body(pair):
                slot = lax.rem(pair, 2)
                for copy in loads(pair, slot):
                    copy.wait()

                @pl.when(pair + 1 < pairs)
                def _():
                    for copy in loads(pair + 1, 1 - slot):
                        copy.start()

                attend_back_open(
                    qkv.at[slot], context.at[slot], upper.at[slot], dots, key_turned, queries, uppers
                )
                base = pair * 3 * PAIR

                def columns(which):
                    return pl.ds(pl.multiple_of(base + which * PAIR, PAIR), PAIR)

                for begin, size in blocks:
                    block = slice(begin, begin + size)
                    query_sum[:, block] = jnp.zeros((PAIR, size), WIDE)

                    def key_tile(step, begin=begin, size=size):
                        at, key_sum, value_sum = attend_back_tile(
                            qkv.at[slot], score_bias, totals.at[pair], dots, key_turned, queries, uppers, query_sum,
                            begin, size, step,
                        )
                        mixed[at, columns(1)] = key_sum.astype(LOW)
                        mixed[at, columns(2)] = value_sum.astype(LOW)

                    between = {}
                    for step in range(size // TILE):
                        number = begin // TILE + step
                        for act_pair in range(pairs):
                            for p, s in SCATTER_AT["attend"].get(act_pair * per_pair + number, ()):

                                def act(act_pair=act_pair, p=p, s=s):
                                    pl.when(pair == act_pair)(lambda: lines.stage(p, s))

                                between.setdefault(step, []).append(act)
                    looped(size // TILE, key_tile, between)
                    mixed[block, columns(0)] = (
                        (query_sum[:, block] * HEAD_DIM ** (-0.5)).T.astype(LOW)
                    )
                for which, row in ((0, 0), (2, 1)):
                    part = mixed[:, columns(which)].astype(WIDE)
                    spot = pl.multiple_of(member * inner + pair * PAIR, PAIR)
                    small[0, row : row + 1, pl.ds(spot, PAIR)] = jnp.sum(
                        part, axis=0, keepdims=True
                    )

            def project_stages(second):
                return [
                    functools.partial(project, second),
                    *[functools.partial(lines.stage, *st) for st in SCATTER_AT["project"][second]],
                ]

            looped(pairs, pair_body, {1: project_stages(0), 3: project_stages(1)})

        pl.run_scoped(
            attend_phase,
            pltpu.VMEM((2, total_rows, 3 * PAIR), LOW),
            pltpu.VMEM((2, total_rows, PAIR), LOW),
            pltpu.VMEM((2, total_rows, PAIR), LOW),
            pltpu.VMEM(totals_in.shape, WIDE),
            pltpu.VMEM((8, total_rows), WIDE),
            pltpu.VMEM((PAIR, total_rows), LOW),
            pltpu.VMEM((2, total_rows, PAIR), LOW),
            pltpu.VMEM((2, total_rows, PAIR), LOW),
            pltpu.VMEM((PAIR, total_rows), WIDE),
            pltpu.VMEM((2, tall, total_rows), LOW),
        )
        sums.step(0)

        def input_phase(weight, terms, leaving):
            fetches = [
                fetch(whole_ref.at[0, :, pl.ds(0, pairs * 3 * PAIR)], weight, 0),
            ]
            for copy in fetches:
                copy.start()
            for copy in fetches:
                copy.wait()

            def term_tile(step):
                at = tile(step, tall)
                total = dot_nt(mixed[at, :], weight[...])
                own = rows // tall
                mine = step // own == member

                @pl.when(mine)
                def _():
                    terms[at, :] = (total + acc[tile(lax.rem(step, own), tall), :]).astype(LOW)

                @pl.when(jnp.logical_not(mine))
                def _():
                    terms[at, :] = total.astype(LOW)

            phase("terms", total_rows // tall, term_tile)
            sums.step(1)

            def own_rows(which, step):
                places = places_of(which * rows + step * tall)
                return picked_rows(group.moved(places, group.own, group.first), terms)

            def far_tile(step):
                leaving[tile(step, tall), :] = own_rows(1 - member, step).astype(LOW)

            phase("far", rows // tall, far_tile)
            crossing = other_core(leaving, input_far, input_sem.at[0], input_sem.at[1])
            crossing.start()
            sums.step(2)

            def near_tile(step):
                acc[tile(step, tall), :] = own_rows(member, step)

            phase("near", rows // tall, near_tile)
            sums.step(3)
            crossing.wait()
            back = fetch(input_far, leaving, 2)
            back.start()
            back.wait()

            @pl.loop(0, rows // short)
            def _(step):
                at = tile(step, short)
                leaving[at, :] = (acc[at, :] + leaving[at, :].astype(WIDE)).astype(LOW)

            done = fetch(leaving, input_out, 2)
            done.start()
            done.wait()

        pl.run_scoped(
            input_phase,
            pltpu.VMEM((width, pairs * 3 * PAIR), LOW),
            pltpu.VMEM((total_rows, width), LOW),
            pltpu.VMEM((rows, width), LOW),
        )

    pl.run_scoped(last_phase, pltpu.VMEM((total_rows, pairs * 3 * PAIR), LOW))

    def end_phase(pair, encoded, *held):
        ins, outs = held[:12], held[12:]
        fetches = [fetch(enc_pair.at[i], pair.at[rows_of(i)], i) for i in range(2)]
        states = [
            pltpu.make_async_copy(states_in[i], ins[i], state_sem.at[i]) for i in range(len(ins))
        ]
        for copy in [*fetches, *states]:
            copy.start()
        for copy in fetches:
            copy.wait()

        def encoded_tile(step):
            places = places_of(member * rows + step * tall)
            index = group.moved(places, group.dealt, group.first)
            encoded[tile(step, tall), :] = picked_rows(index, pair).astype(LOW)

        phase("encoded", rows // tall, encoded_tile)
        leaving = [fetch(encoded, encoded_out, 2)]
        leaving[0].start()
        for copy in states:
            copy.wait()

        def update(matrix, lead, columns, grad, grad_columns):
            rate = (rate_project, rate_merge, rate_expand, rate_reduce)[matrix]

            @pl.loop(0, grad.shape[0] // 16)
            def _(step):
                at = tile(step, 16)
                old = [ins[3 * matrix + i][(*lead, at, columns)] for i in range(3)]
                new = adamw_update(*old, grad[at, grad_columns], rate, weight_decay)
                for i in range(3):
                    outs[3 * matrix + i][(*lead, at, columns)] = new[i]

        def write(matrix):
            for i in range(3 * matrix, 3 * matrix + 3):
                copy = pltpu.make_async_copy(outs[i], states_out[i], state_sem.at[i])
                copy.start()
                leaving.append(copy)

        def adam_step(which):
            for piece, matrix in ((0, 3), (1, 3), (2, 2), (3, 2)):
                first = piece % 2 * piece_span
                columns = slice(first, first + piece_span)

                @pl.when(which == piece)
                def _():
                    update(matrix, (), columns, shards[piece], slice(0, piece_span))

        phase("adam", 4, adam_step)
        write(2)
        write(3)
        for step in range(4, len(sums.partners) + 1):
            sums.step(step)
        total = small.at[len(sums.partners)]
        vector_grad_ref[...] = total[0:8, :]
        new = adamw_update(
            vectors_ref[...],
            vectors_first[...],
            vectors_second[...],
            total[0:8, :],
            rate_vectors,
            0.0,
        )
        for i in range(3):
            small_out[i][...] = new[i]
        for i in range(hidden_ref.shape[1] // width):
            columns = slice(i * width, (i + 1) * width)
            new = adamw_update(
                hidden_ref[:, columns],
                hidden_first[:, columns],
                hidden_second[:, columns],
                total[8 + i : 9 + i, :],
                rate_hidden,
                0.0,
            )
            for n in range(3):
                small_out[3 + n][:, columns] = new[n]

        def project_pairs(piece, begin, first_pair):
            for pair in range(pairs // 2):
                for c in range(3):
                    at = begin + (3 * pair + c) * PAIR
                    to = (first_pair + pair) * PAIR
                    update(
                        0, (c,), slice(to, to + PAIR), shards[piece], slice(at, at + PAIR)
                    )

        update(1, (), slice(None), shards[4], slice(0, inner))
        write(1)
        project_pairs(4, inner, 0)
        for st in SCATTER_AT["end"]:
            lines.stage(*st)
        project_pairs(5, 0, pairs // 2)
        write(0)
        for copy in leaving:
            copy.wait()

    pl.run_scoped(
        end_phase,
        pltpu.VMEM((total_rows, width), LOW),
        pltpu.VMEM((rows, width), LOW),
        *[pltpu.VMEM(one.shape, WIDE) for one in states_in],
        *[pltpu.VMEM(one.shape, WIDE) for one in states_in],
    )
    sums.sent()
    for p in range(len(grads)):
        lines.sent(p)


def back(lengths, dealing, whole, far, kept, matrices, vectors, hidden, parts):
    qkv, hidden_turned, upstream, context, totals, acc, *_ = kept
    rows, width = acc.shape
    total_rows, inner = context.shape
    depth, shard_rows = parts // 4, width // parts
    half, pair_span = 256, 3 * PAIR * (qkv.shape[0] // 2)
    piece_span = whole.shape[2] // 2
    spans = (*[piece_span] * 4, inner + pair_span, pair_span)
    classes = []
    for span in spans:
        third = max(128, span // 5 // 128 * 128)
        if (span - third) % 256:
            third += 128
        classes.append(((span - third) // 2, (span - third) // 2, third))
    shape, sem = jax.ShapeDtypeStruct, pltpu.SemaphoreType.DMA
    vmem, anywhere = pl.BlockSpec(memory_space=pltpu.VMEM), pl.BlockSpec(memory_space=pl.ANY)
    steps = 3 + depth.bit_length() - 1
    states = [one for matrix in matrices for one in matrix]
    results = pl.pallas_call(
        functools.partial(back_kernel, depth),
        in_specs=[
            *[pl.BlockSpec(memory_space=pltpu.SMEM)] * 2,
            *[vmem] * 6,
            *[anywhere] * (2 + len(kept) + len(states)),
        ],
        out_specs=[*[anywhere] * 2, vmem, *[anywhere] * len(states), *[vmem] * 6, *[anywhere] * 3],
        out_shape=[
            shape((rows, width), LOW),
            shape((rows, width), LOW),
            shape((8, width), WIDE),
            *[shape(one.shape, WIDE) for one in (*states, *vectors, *hidden)],
            shape((2, rows, width), LOW),
            shape((total_rows, inner), LOW),
            shape((rows, width), LOW),
        ],
        scratch_shapes=[
            pltpu.VMEM((rows, width), WIDE),
            pltpu.VMEM((2, width, half), LOW),
            pltpu.VMEM((width, inner), LOW),
            pltpu.VMEM((2 * steps + 1, 16, width), WIDE),
            pltpu.VMEM((total_rows - LONGEST, total_rows - LONGEST), WIDE),
            *[pltpu.VMEM((width, span), LOW) for span in spans],
            *[pltpu.VMEM((shard_rows, span), WIDE) for span in spans],
            *Scatter.scratch(depth, shard_rows, classes),
            sem((steps,)),
            sem((steps,)),
            sem((6,)),
            sem((2, 6)),
            sem((3,)),
            sem((2,)),
            sem((2,)),
            sem((2,)),
            sem((3,)),
            sem((2,)),
            sem((len(states),)),
            *Scatter.semaphores(depth, len(spans)),
        ],
        compiler_params=pltpu.CompilerParams(
            collective_id=1, has_side_effects=True, vmem_limit_bytes=63 * MIB
        ),
    )(lengths, dealing, *vectors, *hidden, whole, far, *kept, *states)
    return results[: 3 + len(states) + 6]


def by_kernels(tokens, cotangent, lengths, dealing, project, merge, expand, reduce, vectors, hidden, parts):
    hidden = tuple(one.reshape(1, -1) for one in hidden)
    matrices = (project, merge, expand, reduce)
    whole, far, *kept = front(
        lengths, dealing, *[one[0] for one in matrices], vectors[0], hidden[0], tokens, cotangent, parts
    )
    results = back(lengths, dealing, whole, far, kept, matrices, vectors, hidden, parts)
    encoded, input_grad, vector_grad = results[:3]
    news = [results[3 + 3 * i : 6 + 3 * i] for i in range(6)]
    return (
        encoded,
        input_grad,
        *news[0],
        *[one.T for one in news[1]],
        *news[2],
        *[one.T for one in news[3]],
        *news[4],
        *[one.reshape(-1) for one in news[5]],
        vector_grad,
    )


def local(
    tokens,
    cotangent,
    lengths,
    dealing,
    project_weight,
    project_first,
    project_second,
    merge_weight,
    merge_first,
    merge_second,
    expand_weight,
    expand_first,
    expand_second,
    reduce_weight,
    reduce_first,
    reduce_second,
    vectors,
    vector_first,
    vector_second,
    hidden_bias,
    hidden_first,
    hidden_second,
):
    parts = lax.axis_size("dp")
    member = lax.axis_index("tensor")
    other = 1 - member
    half_rows, model_width = tokens.shape
    total_rows = 2 * half_rows
    width_half = project_weight.shape[2]
    pairs = width_half // PAIR
    hidden_half = expand_weight.shape[1]
    shard_rows = expand_weight.shape[0]
    own_begin = member * half_rows
    by_kernel = parts % 4 == 0 and (parts & (parts - 1)) == 0 and shard_rows % 16 == 0

    def swap(value):
        return lax.ppermute(value, "tensor", [(0, 1), (1, 0)])

    def own(value, size, which=member):
        return lax.dynamic_slice_in_dim(value, which * size, size, 0)

    if by_kernel:
        return by_kernels(
            tokens, cotangent, lengths, dealing,
            (project_weight, project_first, project_second),
            (merge_weight.T, merge_first.T, merge_second.T),
            (expand_weight, expand_first, expand_second),
            (reduce_weight.T, reduce_first.T, reduce_second.T),
            (vectors, vector_first, vector_second),
            (hidden_bias, hidden_first, hidden_second),
            parts,
        )

    segment, own_of, dealt_of, from_own, from_dealt = layout(lengths[0], dealing[0], total_rows)
    dealt_of = own(dealt_of, half_rows)
    short = segment[LONGEST:]
    score_bias = jnp.where(short[:, None] == short[None, :], 0.0, masked_score).astype(WIDE)

    def own_first(index):
        return lax.rem(index - own_begin + total_rows, total_rows)

    projections = (
        project_weight.reshape(3, shard_rows, pairs, PAIR)
        .transpose(1, 2, 0, 3)
        .reshape(shard_rows, 3 * width_half)
    )
    quarter = hidden_half // 2
    reduce_turned = reduce_weight.T
    shards = jnp.stack(
        [
            jnp.concatenate([projections, merge_weight.T], axis=1),
            jnp.concatenate([expand_weight[:, :quarter], reduce_turned[:, :quarter]], axis=1),
            jnp.concatenate([expand_weight[:, quarter:], reduce_turned[:, quarter:]], axis=1),
        ]
    ).astype(LOW)
    zeros_pair = jnp.zeros((pairs, PAIR), WIDE)
    bias_row = jnp.concatenate(
        [
            own(vectors[0], width_half).reshape(pairs, PAIR),
            zeros_pair,
            own(vectors[1], width_half).reshape(pairs, PAIR),
        ],
        axis=1,
    ).reshape(pairs, 1, 3 * PAIR)
    whole = lax.all_gather(shards, "dp", axis=1, tiled=True)
    far = swap(whole)
    token_pair = jnp.concatenate([tokens, swap(tokens)], axis=0)
    upper_pair = jnp.concatenate([cotangent, swap(cotangent)], axis=0)
    hidden = dot_nn(pick_rows(own_first(own_of), total_rows), token_pair).astype(LOW)
    upstream = dot_nn(pick_rows(own_first(dealt_of), total_rows), upper_pair).astype(LOW)
    qkv = jnp.einsum(
        "rd,dpc->prc",
        hidden,
        whole[0, :, : 3 * width_half].reshape(model_width, pairs, 3 * PAIR),
        preferred_element_type=WIDE,
    )
    qkv = (qkv + bias_row).astype(LOW)
    context, totals = attend(qkv, score_bias)

    (
        encoded, branch_grad, context_grad, merge_grad, expand_grad, reduce_grad, sums, hidden_part_own, hidden_part_far,
    ) = feed_block(
        context,
        whole,
        far,
        own(hidden, half_rows),
        upstream,
        vectors,
        own(hidden_bias, hidden_half),
        own(hidden_bias, hidden_half, other),
    )
    encoded_pair = jnp.concatenate([encoded, swap(encoded)], axis=0)
    encoded_out = dot_nn(
        pick_rows(own_first(own(from_dealt, half_rows)), total_rows), encoded_pair
    ).astype(LOW)
    mixed_grads = attend_back(qkv, score_bias, context, context_grad, totals)
    mixed_sums = jnp.sum(mixed_grads.astype(WIDE), axis=1).reshape(pairs, 3, PAIR)
    mixed_grads = mixed_grads.transpose(1, 0, 2).reshape(total_rows, 3 * width_half)
    project_grad = dot_tn(hidden, mixed_grads)
    input_terms = dot_nt(mixed_grads, whole[0, :, : 3 * width_half])
    own_part = own(input_terms, half_rows) + branch_grad
    input_terms = lax.dynamic_update_slice_in_dim(input_terms, own_part, own_begin, 0).astype(LOW)
    input_far = swap(
        dot_nn(pick_rows(own(from_own, half_rows, other), total_rows), input_terms).astype(LOW)
    )
    input_grad = (
        dot_nn(pick_rows(own(from_own, half_rows), total_rows), input_terms)
        + input_far.astype(WIDE)
    ).astype(LOW)
    zeros_width = jnp.zeros((model_width,), WIDE)
    zeros_hidden = jnp.zeros_like(hidden_bias)
    hidden_total = lax.dynamic_update_slice_in_dim(
        lax.dynamic_update_slice_in_dim(
            zeros_hidden, hidden_part_own, member * hidden_half, 0
        ),
        hidden_part_far,
        other * hidden_half,
        0,
    )
    vector_rows = [
        lax.dynamic_update_slice_in_dim(
            zeros_width, mixed_sums[:, c].reshape(-1), member * width_half, 0
        )
        for c in (0, 2)
    ]
    small = jnp.concatenate(
        [
            jnp.stack(vector_rows),
            sums[2:],
            hidden_total.reshape(-1, model_width),
            jnp.zeros((4, model_width), WIDE),
        ],
        axis=0,
    )
    grads = [
        lax.psum_scatter(g.astype(LOW), "dp", scatter_dimension=0, tiled=True).astype(WIDE)
        for g in (project_grad, merge_grad, expand_grad, reduce_grad)
    ]
    small = lax.psum(small, ("dp", "tensor"))
    project_shard, merge_shard, expand_shard, reduce_shard = grads
    project_shard = (
        project_shard.reshape(shard_rows, pairs, 3, PAIR)
        .transpose(2, 0, 1, 3)
        .reshape(3, shard_rows, width_half)
    )
    vector_grad = small[:8]
    hidden_grad = small[8:12].reshape(-1)
    return (
        encoded_out,
        input_grad,
        *adamw_update(
            project_weight, project_first, project_second, project_shard, rate_project, weight_decay
        ),
        *adamw_update(
            merge_weight, merge_first, merge_second, merge_shard.T, rate_merge, weight_decay
        ),
        *adamw_update(
            expand_weight, expand_first, expand_second, expand_shard, rate_expand, weight_decay
        ),
        *adamw_update(
            reduce_weight, reduce_first, reduce_second, reduce_shard.T, rate_reduce, weight_decay
        ),
        *adamw_update(vectors, vector_first, vector_second, vector_grad, rate_vectors, 0.0),
        *adamw_update(hidden_bias, hidden_first, hidden_second, hidden_grad, rate_hidden, 0.0),
        vector_grad,
    )


def solution(mesh):
    sharded = (
        P("dp", None),
        P("dp", None),
        *[P(None, "dp", "tensor")] * 3,
        *[P("tensor", "dp")] * 3,
        *[P("dp", "tensor")] * 3,
        *[P("tensor", "dp")] * 3,
        *[P()] * 6,
    )
    rows = P(("dp", "tensor"), None)
    return jax.shard_map(
        local,
        mesh=mesh,
        in_specs=(rows, rows, *sharded),
        out_specs=(rows, rows, *sharded[2:], P()),
        check_vma=False,
    )
```

```python
import functools

import jax
import jax.numpy as jnp
from jax import lax
from jax.experimental import pallas as pl
from jax.experimental.pallas import tpu as pltpu
from jax.sharding import PartitionSpec as P

HEAD_DIM = 64
LONGEST = 1024
STEP = 10
PAIR = 2 * HEAD_DIM
TILE = 256
MIB = 1024 * 1024
MESH = pl.DeviceIdType.MESH
LOW = jnp.bfloat16
WIDE = jnp.float32

beta_one = 0.9
beta_two = 0.999
adam_epsilon = 1e-08
weight_decay = 0.01
norm_epsilon = 1e-05
masked_score = -1e30
rate_project = 0.03
rate_merge = 0.3
rate_expand = 0.03
rate_reduce = 0.015
rate_vectors = 0.4
rate_hidden = 0.1


def dot_nn(a, b):
    return jnp.dot(a, b, preferred_element_type=WIDE)


def dot_nt(a, b):
    return lax.dot_general(a, b, (((1,), (1,)), ((), ())), preferred_element_type=WIDE)


def dot_tn(a, b):
    return lax.dot_general(a, b, (((0,), (0,)), ((), ())), preferred_element_type=WIDE)


def layout(lengths_row, dealing_row, total_rows):
    slots = jnp.arange(lengths_row.shape[0], dtype=jnp.int32)
    places = jnp.arange(total_rows, dtype=jnp.int32)
    rank_of = jnp.sum(jnp.where(dealing_row[None, :] == slots[:, None], slots[None, :], 0), axis=1)
    own_start = jnp.cumsum(lengths_row) - lengths_row
    dealt_start = jnp.sum(
        jnp.where(rank_of[None, :] < rank_of[:, None], lengths_row[None, :], 0), axis=1
    )
    longest = lengths_row == LONGEST
    short = jnp.where(longest, 0, lengths_row)
    start = jnp.where(longest, 0, LONGEST + jnp.cumsum(short) - short)

    def inside(begin):
        return (places[:, None] >= begin[None, :]) & (
            places[:, None] < (begin + lengths_row)[None, :]
        )

    def moved(begin, end):
        return places + jnp.sum(jnp.where(inside(begin), (end - begin)[None, :], 0), axis=1)

    segment = jnp.sum(jnp.where(inside(start), slots[None, :], 0), axis=1)
    return (
        segment,
        moved(start, own_start),
        moved(start, dealt_start),
        moved(own_start, start),
        moved(dealt_start, start),
    )


def pick_rows(index, rows):
    places = jnp.arange(rows, dtype=jnp.int32)
    return (index[:, None] == places[None, :]).astype(LOW)


class Group:
    def __init__(self, lengths_ref, dealing_ref):
        count = lengths_ref.shape[1]
        self.lengths = [lengths_ref[0, s] for s in range(count)]
        order = [dealing_ref[0, i] for i in range(count)]
        rank = [sum(jnp.where(order[i] == s, i, 0) for i in range(count)) for s in range(count)]
        short = [jnp.where(length == LONGEST, 0, length) for length in self.lengths]
        self.own, self.dealt, self.first = [], [], []
        own = own_short = jnp.int32(0)
        for s in range(count):
            self.own.append(own)
            self.first.append(jnp.where(self.lengths[s] == LONGEST, 0, LONGEST + own_short))
            self.dealt.append(
                sum(jnp.where(rank[j] < rank[s], self.lengths[j], 0) for j in range(count))
            )
            own, own_short = own + self.lengths[s], own_short + short[s]

    def inside(self, places, begin, s):
        return (places >= begin[s]) & (places < begin[s] + self.lengths[s])

    def moved(self, places, begin, end):
        total = places
        for s in range(len(begin)):
            total = total + jnp.where(self.inside(places, begin, s), end[s] - begin[s], 0)
        return total

    def score_bias(self, count):
        sides = []
        for shape, axis in (((count, 1), 0), ((1, count), 1)):
            places = lax.broadcasted_iota(jnp.int32, shape, axis) + LONGEST
            segment = jnp.zeros_like(places)
            for s in range(len(self.first)):
                segment = segment + jnp.where(self.inside(places, self.first, s), s, 0)
            sides.append(segment)
        return jnp.where(sides[0] == sides[1], 0.0, masked_score).astype(WIDE)


def picked_rows(index, source):
    places = lax.broadcasted_iota(jnp.int32, (index.shape[0], source.shape[0]), 1)
    return dot_nn(jnp.where(index == places, 1.0, 0.0).astype(LOW), source[...])


def attend_tile(qkv_ref, value_turned, pair, bias_ref, begin, size, step, keep, context_ref, columns):
    lane = lax.broadcasted_iota(jnp.int32, (1, PAIR), 1)
    first = pl.multiple_of(begin + step * TILE, TILE)
    query = qkv_ref[pair, pl.ds(first, TILE), 0:PAIR]
    key = qkv_ref[pair, begin : begin + size, PAIR : 2 * PAIR]
    outcome = []
    for head in range(2):
        chosen = jnp.where(lane // HEAD_DIM == head, HEAD_DIM ** (-0.5), 0.0).astype(LOW)
        scores = dot_nt(key, query * chosen)
        if begin:
            inner = pl.multiple_of(step * TILE, TILE)
            scores = scores + bias_ref[:, pl.ds(inner, TILE)]
        exponent = jnp.exp(scores - jnp.max(scores, axis=0, keepdims=True))
        total = jnp.sum(exponent, axis=0, keepdims=True)
        probability = (exponent * (1.0 / total)).astype(LOW)
        keep(head, probability)
        band = slice(head * HEAD_DIM, (head + 1) * HEAD_DIM)
        outcome.append(dot_nn(value_turned[pair, band, begin : begin + size], probability))
    context = jnp.concatenate(outcome, axis=0)
    context_ref[pl.ds(first, TILE), columns] = context.T.astype(LOW)


def attend_kernel(qkv_ref, bias_ref, context_ref, long_ref, short_ref, value_turned):
    rows = qkv_ref.shape[1]
    value_turned[0] = qkv_ref[0, :, 2 * PAIR : 3 * PAIR].astype(WIDE).T.astype(LOW)
    for begin, size, kept in ((0, LONGEST, long_ref), (LONGEST, rows - LONGEST, short_ref)):

        @pl.loop(0, size // TILE)
        def _(step):
            def keep(head, probability):
                kept[0, head, :, pl.ds(pl.multiple_of(step * TILE, TILE), TILE)] = probability

            attend_tile(
                qkv_ref, value_turned, 0, bias_ref, begin, size, step, keep, context_ref, slice(0, PAIR)
            )


def attend(qkv, bias):
    pairs, rows, width = qkv.shape
    short = rows - LONGEST
    return pl.pallas_call(
        attend_kernel,
        grid=(pairs,),
        in_specs=[
            pl.BlockSpec((1, rows, width), lambda p: (p, 0, 0)),
            pl.BlockSpec(bias.shape, lambda p: (0, 0)),
        ],
        out_specs=[
            pl.BlockSpec((rows, PAIR), lambda p: (0, p)),
            pl.BlockSpec((1, 2, LONGEST, LONGEST), lambda p: (p, 0, 0, 0)),
            pl.BlockSpec((1, 2, short, short), lambda p: (p, 0, 0, 0)),
        ],
        out_shape=[
            jax.ShapeDtypeStruct((rows, pairs * PAIR), LOW),
            jax.ShapeDtypeStruct((pairs, 2, LONGEST, LONGEST), LOW),
            jax.ShapeDtypeStruct((pairs, 2, short, short), LOW),
        ],
        scratch_shapes=[pltpu.VMEM((1, PAIR, rows), LOW)],
        compiler_params=pltpu.CompilerParams(vmem_limit_bytes=48 * MIB),
    )(qkv, bias)


def attend_back_open(qkv_ref, context_ref, upper_ref, dots, key_turned, queries, uppers):
    lane = lax.broadcasted_iota(jnp.int32, (1, PAIR), 1)
    product = (upper_ref[...].astype(WIDE) * context_ref[...].astype(WIDE)).T
    for head in range(2):
        band = slice(head * HEAD_DIM, (head + 1) * HEAD_DIM)
        dots[head : head + 1, :] = jnp.sum(product[band, :], axis=0, keepdims=True)
        chosen = lane // HEAD_DIM == head
        queries[head] = qkv_ref[:, 0:PAIR] * jnp.where(chosen, HEAD_DIM ** (-0.5), 0.0).astype(LOW)
        uppers[head] = upper_ref[...] * jnp.where(chosen, 1.0, 0.0).astype(LOW)
    key_turned[...] = qkv_ref[:, PAIR : 2 * PAIR].astype(WIDE).T.astype(LOW)


def attend_back_tile(
    qkv_ref, kept, dots, key_turned, queries, uppers, query_sum, begin, size, step
):
    block = slice(begin, begin + size)
    first = pl.multiple_of(begin + step * TILE, TILE)
    value = qkv_ref[pl.ds(first, TILE), 2 * PAIR : 3 * PAIR]
    key_sum = jnp.zeros((TILE, PAIR), WIDE)
    value_sum = jnp.zeros((TILE, PAIR), WIDE)
    for head in range(2):
        band = slice(head * HEAD_DIM, (head + 1) * HEAD_DIM)
        query = queries[head, block, :]
        upper = uppers[head, block, :]
        probability = kept(head)
        weight_grads = dot_nt(value, upper)
        score_grads = probability.astype(WIDE) * (weight_grads - dots[head : head + 1, block])
        score_grads = score_grads.astype(LOW)
        value_sum = value_sum + dot_nn(probability, upper)
        key_sum = key_sum + dot_nn(score_grads, query)
        query_sum[band, block] += dot_nn(key_turned[band, pl.ds(first, TILE)], score_grads)
    return pl.ds(first, TILE), key_sum, value_sum


def attend_back_kernel(
    qkv_ref, context_ref, grad_ref, long_ref, short_ref, out_ref, dots, key_turned, queries, uppers, query_sum
):
    rows = qkv_ref.shape[1]
    qkv = qkv_ref.at[0]
    attend_back_open(qkv, context_ref, grad_ref, dots, key_turned, queries, uppers)
    for begin, size, kept in ((0, LONGEST, long_ref), (LONGEST, rows - LONGEST, short_ref)):
        block = slice(begin, begin + size)
        query_sum[:, block] = jnp.zeros((PAIR, size), WIDE)

        @pl.loop(0, size // TILE)
        def _(step):
            def kept_of(head):
                return kept[0, head, pl.ds(pl.multiple_of(step * TILE, TILE), TILE), :]

            at, key_sum, value_sum = attend_back_tile(
                qkv, kept_of, dots, key_turned, queries, uppers, query_sum, begin, size, step
            )
            out_ref[0, at, PAIR : 2 * PAIR] = key_sum.astype(LOW)
            out_ref[0, at, 2 * PAIR : 3 * PAIR] = value_sum.astype(LOW)

        out_ref[0, block, 0:PAIR] = (query_sum[:, block] * HEAD_DIM ** (-0.5)).T.astype(LOW)


def attend_back(qkv, context, grad, long, short):
    pairs, rows, width = qkv.shape
    return pl.pallas_call(
        attend_back_kernel,
        grid=(pairs,),
        in_specs=[
            pl.BlockSpec((1, rows, width), lambda p: (p, 0, 0)),
            pl.BlockSpec((rows, PAIR), lambda p: (0, p)),
            pl.BlockSpec((rows, PAIR), lambda p: (0, p)),
            pl.BlockSpec((1, *long.shape[1:]), lambda p: (p, 0, 0, 0)),
            pl.BlockSpec((1, *short.shape[1:]), lambda p: (p, 0, 0, 0)),
        ],
        out_specs=pl.BlockSpec((1, rows, width), lambda p: (p, 0, 0)),
        out_shape=jax.ShapeDtypeStruct(qkv.shape, LOW),
        scratch_shapes=[
            pltpu.VMEM((8, rows), WIDE),
            pltpu.VMEM((PAIR, rows), LOW),
            pltpu.VMEM((2, rows, PAIR), LOW),
            pltpu.VMEM((2, rows, PAIR), LOW),
            pltpu.VMEM((PAIR, rows), WIDE),
        ],
        compiler_params=pltpu.CompilerParams(vmem_limit_bytes=48 * MIB),
    )(qkv, context, grad, long, short)


def place():
    me = lax.axis_index("dp")
    z, y, x = me // 4, (me // 2) % 2, me % 2
    return me, z, y, x


def line_slots(z, depth):
    slots = []
    for step in range(depth - 1):
        slots.append((z - 1 - step, z - 1 - step >= 0, 1))
        slots.append((z + 1 + step, z + 1 + step < depth, -1))
    return slots


def remote(source, target, send, receive, device):
    return pltpu.make_async_remote_copy(
        src_ref=source,
        dst_ref=target,
        send_sem=send,
        recv_sem=receive,
        device_id={"dp": device},
        device_id_type=MESH,
    )


def greet_line(me, z, y, x, depth, extra=()):
    barrier = pltpu.get_barrier_semaphore()
    for peer in (z * 4 + y * 2 + 1 - x, z * 4 + (1 - y) * 2 + x):
        pl.semaphore_signal(barrier, inc=1, device_id={"dp": peer}, device_id_type=MESH)

    @pl.when(z > 0)
    def _():
        pl.semaphore_signal(barrier, inc=1, device_id={"dp": me - 4}, device_id_type=MESH)

    @pl.when(z < depth - 1)
    def _():
        pl.semaphore_signal(barrier, inc=1, device_id={"dp": me + 4}, device_id_type=MESH)

    for peer in extra:
        pl.semaphore_signal(barrier, inc=1, device_id=peer, device_id_type=MESH)
    ends = jnp.where(z > 0, 1, 0) + jnp.where(z < depth - 1, 1, 0)
    pl.semaphore_wait(barrier, 2 + len(extra) + ends)


def other_core(source, target, send, receive):
    return pltpu.make_async_remote_copy(
        src_ref=source,
        dst_ref=target,
        send_sem=send,
        recv_sem=receive,
        device_id={"tensor": 1 - lax.axis_index("tensor")},
        device_id_type=MESH,
    )


class Gather:
    def __init__(self, depth, parts, whole, far, sems):
        self.whole, self.far = whole, far
        self.depth = depth
        self.me, self.z, self.y, self.x = place()
        self.x_peer = self.z * 4 + self.y * 2 + 1 - self.x
        self.y_peer = self.z * 4 + (1 - self.y) * 2 + self.x
        self.rows = whole.shape[1] // parts
        width = whole.shape[2]
        self.third = width // 4
        side = (width - self.third) // 2
        self.a, self.b = (0, side), (side, side)
        self.ab, self.c, self.all = (0, 2 * side), (2 * side, self.third), (0, width)
        (
            self.z_send, self.z_recv, self.zc_send, self.zc_recv, self.xa_send, self.xa_recv, self.yb_send, self.yb_recv,
            self.ya_send, self.ya_recv, self.xb_send, self.xb_recv, self.c_send, self.c_recv, self.far_send, self.far_recv,
        ) = sems
        self.slots = line_slots(self.z, depth)

    @staticmethod
    def semaphores(depth, pieces):
        sem = pltpu.SemaphoreType.DMA
        return [
            *[sem((pieces, depth + 1)), sem((pieces, depth))] * 2,
            *[sem((pieces, depth))] * 4,
            *[sem((pieces, depth, 2))] * 4,
            sem((pieces, 2)),
            sem((pieces, 2)),
            sem((pieces,)),
            sem((pieces,)),
        ]

    def block(self, zb, yb, xb):
        return zb * 4 + yb * 2 + xb

    def cut(self, ref, p, block, count, columns):
        first = pl.multiple_of(block * self.rows, self.rows)
        return ref.at[p, pl.ds(first, count * self.rows), pl.ds(*columns)]

    def copy(self, p, block, count, columns, send, receive, device):
        part = self.cut(self.whole, p, block, count, columns)
        return remote(part, part, send, receive, device)

    def forward(self, p, block, count, columns):
        if p == 0 and columns[0] + columns[1] <= self.c[0]:
            return
        if p == 0:
            columns = self.c
        other_core(
            self.cut(self.whole, p, block, count, columns),
            self.cut(self.far, p, block, count, columns),
            self.far_send.at[p],
            self.far_recv.at[p],
        ).start()

    def far_copy(self, p):
        columns = self.c if p == 0 else self.all
        part = self.far.at[p, :, pl.ds(*columns)]
        return other_core(part, part, self.far_send.at[p], self.far_recv.at[p])

    def z_copy(self, p, zb, way, back=False):
        block = self.block(zb, self.y, self.x)
        sem = self.depth if back else zb
        return self.copy(
            p, block, 1, self.ab, self.z_send.at[p, sem], self.z_recv.at[p, zb], self.me + 4 * way
        )

    def zc_copy(self, p, zb, way, back=False):
        sem = self.depth if back else zb
        return self.copy(
            p, zb * 4, 4, self.c, self.zc_send.at[p, sem], self.zc_recv.at[p, zb], self.me + 4 * way
        )

    def xa(self, p, zb, xb):
        block = self.block(zb, self.y, xb)
        return self.copy(
            p, block, 1, self.a, self.xa_send.at[p, zb], self.xa_recv.at[p, zb], self.x_peer
        )

    def yb(self, p, zb, yb):
        block = self.block(zb, yb, self.x)
        return self.copy(
            p, block, 1, self.b, self.yb_send.at[p, zb], self.yb_recv.at[p, zb], self.y_peer
        )

    def ya(self, p, zb, yb, xb):
        block = self.block(zb, yb, xb)
        return self.copy(
            p, block, 1, self.a, self.ya_send.at[p, zb, xb], self.ya_recv.at[p, zb, xb], self.y_peer
        )

    def xb(self, p, zb, yb, xb):
        block = self.block(zb, yb, xb)
        return self.copy(
            p, block, 1, self.b, self.xb_send.at[p, zb, yb], self.xb_recv.at[p, zb, yb], self.x_peer
        )

    def xc(self, p, xb):
        block = self.block(self.z, self.y, xb)
        return self.copy(
            p, block, 1, self.c, self.c_send.at[p, 0], self.c_recv.at[p, 0], self.x_peer
        )

    def yc(self, p, yb):
        block = self.block(self.z, yb, 0)
        return self.copy(
            p, block, 2, self.c, self.c_send.at[p, 1], self.c_recv.at[p, 1], self.y_peer
        )

    def both_ways(self, copy, act):
        @pl.when(self.z < self.depth - 1)
        def _():
            act(copy(self.z, 1))

        @pl.when(self.z > 0)
        def _():
            act(copy(self.z, -1, True))

    def spread(self, p, zb):
        self.xa(p, zb, self.x).start()
        self.yb(p, zb, self.y).start()
        self.ya(p, zb, self.y, self.x).start()
        self.xb(p, zb, self.y, self.x).start()

    def turn(self, p, zb):
        self.xa(p, zb, 1 - self.x).wait_recv()
        self.ya(p, zb, self.y, 1 - self.x).start()
        self.forward(p, self.block(zb, self.y, 1 - self.x), 1, self.a)
        self.yb(p, zb, 1 - self.y).wait_recv()
        self.xb(p, zb, 1 - self.y, self.x).start()
        self.forward(p, self.block(zb, 1 - self.y, self.x), 1, self.b)

    def at_step(self, step, act):
        for zb, valid, way in self.slots[2 * step : 2 * step + 2]:
            on = (self.z + way >= 0) & (self.z + way < self.depth)
            pl.when(valid)(functools.partial(act, zb, way, on))

    def arrive(self, p, step):
        def act(zb, way, on):
            self.z_copy(p, zb, way).wait_recv()
            pl.when(on)(lambda: self.z_copy(p, zb, way).start())
            self.spread(p, zb)
            self.forward(p, self.block(zb, self.y, self.x), 1, self.ab)

        self.at_step(step, act)

    def arrive_c(self, p, step):
        def act(zb, way, on):
            self.zc_copy(p, zb, way).wait_recv()
            pl.when(on)(lambda: self.zc_copy(p, zb, way).start())
            self.forward(p, zb * 4, 4, self.c)

        self.at_step(step, act)

    def stage(self, p, s):
        depth = self.depth
        if s == 0:
            self.both_ways(lambda *way: self.z_copy(p, *way), lambda copy: copy.start())
            self.xc(p, self.x).start()
            self.spread(p, self.z)
            self.forward(p, self.me, 1, self.all)
            return
        if s == 1:
            self.xc(p, 1 - self.x).wait_recv()
            self.yc(p, self.y).start()
            self.forward(p, self.block(self.z, self.y, 1 - self.x), 1, self.c)
        if s == 2:
            self.yc(p, 1 - self.y).wait_recv()
            self.both_ways(lambda *way: self.zc_copy(p, *way), lambda copy: copy.start())
            self.forward(p, self.block(self.z, 1 - self.y, 0), 2, self.c)
        if 1 <= s < depth:
            self.arrive(p, s - 1)
        if 3 <= s < depth + 2:
            self.arrive_c(p, s - 3)
        if s == 2:
            self.turn(p, self.z)
        if 3 <= s < depth + 2:
            self.at_step(s - 3, lambda zb, way, on: self.turn(p, zb))
        if s == depth + 2:
            for zb in range(depth):
                for other in range(2):
                    self.ya(p, zb, 1 - self.y, other).wait_recv()
                    self.forward(p, self.block(zb, 1 - self.y, other), 1, self.a)
                    self.xb(p, zb, other, 1 - self.x).wait_recv()
                    self.forward(p, self.block(zb, other, 1 - self.x), 1, self.b)

    def finish(self, p):
        def sent(copy):
            copy.wait_send()

        self.far_copy(p).wait_send()
        self.both_ways(lambda *way: self.z_copy(p, *way), sent)
        self.both_ways(lambda *way: self.zc_copy(p, *way), sent)
        for zb in range(self.depth):
            self.xa(p, zb, self.x).wait_send()
            self.yb(p, zb, self.y).wait_send()
            for other in range(2):
                self.ya(p, zb, self.y, other).wait_send()
                self.xb(p, zb, other, self.x).wait_send()
        self.xc(p, self.x).wait_send()
        self.yc(p, self.y).wait_send()

        def passed(zb, way, on):
            pl.when(on)(lambda: sent(self.z_copy(p, zb, way)))
            pl.when(on)(lambda: sent(self.zc_copy(p, zb, way)))

        for step in range(self.depth - 1):
            self.at_step(step, passed)


def looped(count, body, between):
    @pl.loop(0, count)
    def _(i):
        body(i)
        for step, acts in between.items():

            @pl.when(i == step)
            def _():
                for act in acts:
                    act()


GATHER_AT = {
    "hidden": {-1: [(0, 1)], 0: [(0, 2)], 3: [(0, 3), (0, 4)]},
    "upstream": {-1: [(1, 0)], 0: [(0, 5)], 1: [(2, 0)]},
    "project": {-1: [(0, 6)], 0: [(1, 1)]},
    "long": {-1: [(1, 2)], 2: [(2, 1)], 9: [(1, 3)], 11: [(2, 2)]},
    "short": {4: [(1, 4)]},
    "norm": {1: [(1, 5), (2, 3)]},
    "feed": {-1: [(1, 6)], 0: [(2, 4)], 1: [(2, 5)]},
    "last": {-1: [(2, 6)]},
}


def front_kernel(
    depth, lengths_ref, dealing_ref, project_ref, merge_ref, expand_ref, reduce_ref, vectors_ref, hidden_bias_ref,
    tokens_ref, cotangent_ref,
    whole_ref, far_ref, qkv_out, turned_out, upstream_out, context_out, long_out, short_out,
    acc_out, normal_out, inverse_out, low_turned_out, active_out, slope_out, far_context_out,
    shards, score_bias, token, upper, hidden, turned, upstream, weight, qkv, context, value_turned, kept,
    acc, normal, inverse, low, low_turned, active, slope, far_context, merge, merge_far, expand_buf, reduce_buf,
    local_sem, core_sem, out_sem, load_sem, chunk_sem, kept_sem, *sems,
):
    pieces = whole_ref.shape[0]
    half_rows, width = tokens_ref.shape
    rows = 2 * half_rows
    pairs = qkv.shape[0]
    inner = pairs * PAIR
    both = expand_buf.shape[2]
    half = both // 2
    hidden_half = expand_ref.shape[1]
    chunks = hidden_half // half
    per_piece = chunks // (pieces - 1)
    member = lax.axis_index("tensor")
    lines = Gather(depth, 4 * depth, whole_ref, far_ref, sems)
    me = lines.me
    tall, short = 2 * TILE, TILE // 2

    own = [
        pltpu.make_async_copy(
            shards.at[p], lines.cut(whole_ref, p, me, 1, lines.all), local_sem.at[p]
        )
        for p in range(pieces)
    ]
    own += [
        pltpu.make_async_copy(tokens_ref, token.at[member], local_sem.at[pieces]),
        pltpu.make_async_copy(cotangent_ref, upper.at[member], local_sem.at[pieces + 1]),
    ]
    for copy in own[pieces:]:
        copy.start()
    for pair in range(pairs):
        for c in range(3):
            first = (3 * pair + c) * PAIR
            shards[0, :, first : first + PAIR] = project_ref[
                c, :, pair * PAIR : (pair + 1) * PAIR
            ].astype(LOW)
    shards[0, :, 3 * inner :] = merge_ref[...].astype(LOW)
    quarter = hidden_half // (pieces - 1)
    for p in range(1, pieces):
        columns = slice((p - 1) * quarter, p * quarter)
        shards[p, :, 0:quarter] = expand_ref[:, columns].astype(LOW)
        shards[p, :, quarter:] = reduce_ref[:, columns].astype(LOW)
    for copy in own[:pieces]:
        copy.start()
    greet_line(me, lines.z, lines.y, lines.x, depth, [{"tensor": 1 - member}])
    crossing = [
        other_core(tokens_ref, token.at[member], core_sem.at[0, 0], core_sem.at[0, 1]),
        other_core(cotangent_ref, upper.at[member], core_sem.at[1, 0], core_sem.at[1, 1]),
    ]
    own[0].wait()
    lines.stage(0, 0)
    for copy in crossing:
        copy.start()
    group = Group(lengths_ref, dealing_ref)
    score_bias[...] = group.score_bias(rows - LONGEST)
    for copy in own[1:]:
        copy.wait()

    leaving = []

    def leave(source, target):
        copy = pltpu.make_async_copy(source, target, out_sem.at[len(leaving)])
        copy.start()
        leaving.append(copy)

    def phase(name, count, body):
        between = {
            step: [functools.partial(lines.stage, *stage) for stage in stages]
            for step, stages in GATHER_AT.get(name, {}).items()
        }
        for act in between.pop(-1, ()):
            act()
        looped(count, body, between)

    def places_of(first):
        return first + lax.broadcasted_iota(jnp.int32, (TILE, 1), 0)

    def picked(index, source):
        return picked_rows(index, source.at[0]) + picked_rows(index - half_rows, source.at[1])

    def tile(step, size=TILE):
        return pl.ds(pl.multiple_of(step * size, size), size)

    def hidden_tile(step):
        index = group.moved(places_of(step * TILE), group.first, group.own)
        rows_here = picked(index, token)
        hidden[tile(step), :] = rows_here.astype(LOW)
        turned[:, tile(step)] = rows_here.T.astype(LOW)

    def upstream_tile(step):
        places = places_of(member * half_rows + step * TILE)
        index = group.moved(places, group.first, group.dealt)
        upstream[tile(step), :] = picked(index, upper).astype(LOW)

    crossing[0].wait()
    phase("hidden", rows // TILE, hidden_tile)
    leave(turned, turned_out)
    crossing[1].wait()
    phase("upstream", half_rows // TILE, upstream_tile)
    leave(upstream, upstream_out)

    weight_copy = pltpu.make_async_copy(
        whole_ref.at[0, :, pl.ds(0, pairs * 3 * PAIR)], weight, local_sem.at[1]
    )

    def project_tile(i):
        @pl.when(i == 0)
        def _():
            weight_copy.start()
            weight_copy.wait()

        pair, step = i // (rows // tall), lax.rem(i, rows // tall)
        at = tile(step, tall)
        columns = pl.ds(pl.multiple_of(pair * 3 * PAIR, PAIR), 3 * PAIR)
        bias_columns = pl.ds(pl.multiple_of(member * inner + pair * PAIR, PAIR), PAIR)
        bias = jnp.concatenate(
            [
                vectors_ref[0:1, bias_columns],
                jnp.zeros((1, PAIR), WIDE),
                vectors_ref[1:2, bias_columns],
            ],
            axis=1,
        )
        mixed = dot_nn(hidden[at, :], weight[:, columns]) + bias
        qkv[pair, at, :] = mixed.astype(LOW)
        value_turned[pair, :, at] = mixed[:, 2 * PAIR :].T.astype(LOW)

    phase("project", pairs * rows // tall, project_tile)
    leave(qkv, qkv_out)

    def attend_steps(name, begin, size, target):
        count = pairs * size // TILE

        def kept_copy(i):
            pair, step = i // (size // TILE), lax.rem(i, size // TILE)
            columns = pl.ds(pl.multiple_of(step * TILE, TILE), TILE)
            slot = lax.rem(i, 2)
            return pltpu.make_async_copy(
                kept.at[slot, :, pl.ds(0, size)], target.at[pair, :, :, columns], kept_sem.at[slot]
            )

        def step_of(i):
            pair, step = i // (size // TILE), lax.rem(i, size // TILE)
            columns = pl.ds(pl.multiple_of(pair * PAIR, PAIR), PAIR)

            @pl.when(i >= 2)
            def _():
                kept_copy(i - 2).wait()

            def keep(head, probability):
                kept[lax.rem(i, 2), head, 0:size, :] = probability

            attend_tile(
                qkv, value_turned, pair, score_bias, begin, size, step, keep, context, columns
            )
            kept_copy(i).start()

        phase(name, count, step_of)
        for i in (count - 2, count - 1):
            kept_copy(i).wait()

    attend_steps("long", 0, LONGEST, long_out)
    attend_steps("short", LONGEST, rows - LONGEST, short_out)
    leave(context, context_out)

    own_first = member * half_rows
    other_rows = pl.ds(pl.multiple_of((1 - member) * half_rows, half_rows), half_rows)
    crossing = other_core(context.at[other_rows], far_context, core_sem.at[2, 0], core_sem.at[2, 1])
    crossing.start()
    lines.far_copy(0).wait_recv()
    merge_columns = pl.ds(whole_ref.shape[2] - inner, inner)
    fetches = [
        pltpu.make_async_copy(whole_ref.at[0, :, merge_columns], merge, local_sem.at[2]),
        pltpu.make_async_copy(far_ref.at[0, :, merge_columns], merge_far, local_sem.at[3]),
    ]
    for copy in fetches:
        copy.start()
    for copy in fetches:
        copy.wait()
    crossing.wait()
    leave(far_context, far_context_out)

    def norm_tile(step):
        at = tile(step, short)
        own_at = pl.ds(pl.multiple_of(own_first + step * short, short), short)
        branch = dot_nt(context[own_at, :], merge[...]) + dot_nt(far_context[at, :], merge_far[...])
        unit, scale = norm(hidden[own_at, :].astype(WIDE) + branch + vectors_ref[2:3, :])
        normed = unit * vectors_ref[3:4, :] + vectors_ref[4:5, :]
        normal[at, :] = unit
        inverse[at, :] = jnp.broadcast_to(scale, (short, 128))
        low[at, :] = normed.astype(LOW)
        low_turned[:, at] = normed.T.astype(LOW)
        acc[at, :] = normed + vectors_ref[5:6, :]

    phase("norm", half_rows // short, norm_tile)
    leave(normal, normal_out)
    leave(inverse, inverse_out)
    leave(low_turned, low_turned_out)

    def loads(j):
        slot, piece, at = lax.rem(j, 2), 1 + j // per_piece, lax.rem(j, per_piece) * half
        copies = []
        for kind, buf in enumerate((expand_buf, reduce_buf)):
            first = pl.multiple_of(at + kind * per_piece * half, half)
            for side, source in enumerate((far_ref, whole_ref)):
                copies.append(
                    pltpu.make_async_copy(
                        source.at[piece, :, pl.ds(first, half)],
                        buf.at[slot, :, pl.ds(side * half, half)],
                        load_sem.at[slot, kind, side],
                    )
                )
        return copies

    def results(j):
        slot = lax.rem(j, 2)
        return [
            pltpu.make_async_copy(active.at[slot], active_out.at[j], chunk_sem.at[slot, 0]),
            pltpu.make_async_copy(slope.at[slot], slope_out.at[j], chunk_sem.at[slot, 1]),
        ]

    def chunk_of(first_chunk):
        def chunk(i):
            j = first_chunk + i
            slot = lax.rem(j, 2)

            @pl.when(i == 0)
            def _():
                lines.far_copy(1 + first_chunk // per_piece).wait_recv()
                for copy in loads(j):
                    copy.start()

            for copy in loads(j):
                copy.wait()

            @pl.when(i + 1 < per_piece)
            def _():
                for copy in loads(j + 1):
                    copy.start()

            @pl.when(j >= 2)
            def _():
                for copy in results(j - 2):
                    copy.wait()

            biases = []
            for which in (1 - member, member):
                first = pl.multiple_of(which * hidden_half + j * half, half)
                biases.append(hidden_bias_ref[:, pl.ds(first, half)])
            bias = jnp.concatenate(biases, axis=1)
            for step in range(half_rows // TILE):
                at = slice(step * TILE, (step + 1) * TILE)
                value = dot_nn(low[at, :], expand_buf[slot]) + bias
                below, bell = normal_cells(value)
                held = (value * below).astype(LOW)
                active[slot, at, :] = held
                slope[slot, at, :] = (below + value * bell * 0.3989422804014327).astype(LOW)
                acc[at, :] += dot_nt(held, reduce_buf[slot])
            for copy in results(j):
                copy.start()

        return chunk

    phase("feed", per_piece, chunk_of(0))
    phase("last", per_piece, chunk_of(per_piece))
    leave(acc, acc_out)
    for p in range(pieces):
        lines.finish(p)
    for j in (chunks - 2, chunks - 1):
        for copy in results(j):
            copy.wait()
    for copy in leaving:
        copy.wait()


def front(lengths, dealing, project, merge, expand, reduce, vectors, hidden_bias, tokens, cotangent, parts):
    shard_rows, hidden_half = expand.shape
    pieces, columns = 3, hidden_half
    half_rows, width = tokens.shape
    rows, pairs, depth = 2 * half_rows, project.shape[2] // PAIR, parts // 4
    inner, half = pairs * PAIR, 256
    chunks, both = hidden_half // half, 2 * half
    shape, sem = jax.ShapeDtypeStruct, pltpu.SemaphoreType.DMA
    vmem, anywhere = pl.BlockSpec(memory_space=pltpu.VMEM), pl.BlockSpec(memory_space=pl.ANY)
    held = [
        ((pairs, rows, 3 * PAIR), LOW),
        ((width, rows), LOW),
        ((half_rows, width), LOW),
        ((rows, inner), LOW),
        ((pairs, 2, LONGEST, LONGEST), LOW),
        ((pairs, 2, rows - LONGEST, rows - LONGEST), LOW),
        ((half_rows, width), WIDE),
        ((half_rows, width), WIDE),
        ((half_rows, 128), WIDE),
        ((width, half_rows), LOW),
        ((chunks, half_rows, both), LOW),
        ((chunks, half_rows, both), LOW),
        ((half_rows, inner), LOW),
    ]
    return pl.pallas_call(
        functools.partial(front_kernel, depth),
        in_specs=[*[pl.BlockSpec(memory_space=pltpu.SMEM)] * 2, *[vmem] * 6, *[anywhere] * 2],
        out_specs=[anywhere] * 15,
        out_shape=[
            shape((pieces, parts * shard_rows, columns), LOW),
            shape((pieces, parts * shard_rows, columns), LOW),
            *[shape(*one) for one in held],
        ],
        scratch_shapes=[
            pltpu.VMEM((pieces, shard_rows, columns), LOW),
            pltpu.VMEM((rows - LONGEST, rows - LONGEST), WIDE),
            pltpu.VMEM((2, half_rows, width), LOW),
            pltpu.VMEM((2, half_rows, width), LOW),
            pltpu.VMEM((rows, width), LOW),
            pltpu.VMEM((width, rows), LOW),
            pltpu.VMEM((half_rows, width), LOW),
            pltpu.VMEM((width, pairs * 3 * PAIR), LOW),
            pltpu.VMEM((pairs, rows, 3 * PAIR), LOW),
            pltpu.VMEM((rows, inner), LOW),
            pltpu.VMEM((pairs, PAIR, rows), LOW),
            pltpu.VMEM((2, 2, LONGEST, TILE), LOW),
            pltpu.VMEM((half_rows, width), WIDE),
            pltpu.VMEM((half_rows, width), WIDE),
            pltpu.VMEM((half_rows, 128), WIDE),
            pltpu.VMEM((half_rows, width), LOW),
            pltpu.VMEM((width, half_rows), LOW),
            pltpu.VMEM((2, half_rows, both), LOW),
            pltpu.VMEM((2, half_rows, both), LOW),
            pltpu.VMEM((half_rows, inner), LOW),
            pltpu.VMEM((width, inner), LOW),
            pltpu.VMEM((width, inner), LOW),
            pltpu.VMEM((2, width, both), LOW),
            pltpu.VMEM((2, width, both), LOW),
            sem((pieces + 2,)),
            sem((3, 2)),
            sem((10,)),
            sem((2, 2, 2)),
            sem((2, 2)),
            sem((2,)),
            *Gather.semaphores(depth, pieces),
        ],
        compiler_params=pltpu.CompilerParams(
            collective_id=0, has_side_effects=True, vmem_limit_bytes=62 * MIB
        ),
    )(lengths, dealing, project, merge, expand, reduce, vectors, hidden_bias, tokens, cotangent)


def normal_cells(value):
    bell = jnp.exp(value * value * -0.5)
    t = 1.0 / (1.0 + 0.39 * 0.7071067811865476 * jnp.abs(value))
    tail = -0.2275377237624147
    for factor in (
        0.8866668177122106,
        -0.6354042576077721,
        0.649562611731642,
        0.0913871257655044,
        0.23532542445435511,
    ):
        tail = tail * t + factor
    tail = 0.5 * tail * t * bell
    return jnp.where(value < 0.0, tail, 1.0 - tail), bell


def norm(values):
    center = values - jnp.mean(values, axis=1, keepdims=True)
    spread = jnp.mean(center * center, axis=1, keepdims=True)
    scale = lax.rsqrt(spread + norm_epsilon)
    return center * scale, scale


def norm_back(scaled, unit, scale):
    return scale * (
        scaled
        - jnp.mean(scaled, axis=1, keepdims=True)
        - unit * jnp.mean(scaled * unit, axis=1, keepdims=True)
    )


def feed_kernel(
    context_ref, merge_ref, merge_far_ref, whole_ref, far_ref, hidden_ref, upstream_ref, vectors_ref, bias_ref,
    encoded_ref, branch_ref, grad_ref, merge_grad_ref, expand_grad_ref, reduce_grad_ref, sums_ref, hidden_sums_ref,
    own_ctx, far_ctx, acc, normal, inverse, low, turned, late, late_turned, active, slope, inner_grad,
    expand_buf, reduce_buf, arrived, leaving, kept, done, grad_own, grad_far, merge_send, merge_recv,
    ctx_sem, load_sem, send_sem, recv_sem, out_sem, last_sem,
):
    rows = hidden_ref.shape[0]
    chunks, _, both = bias_ref.shape
    half = both // 2
    per_piece = whole_ref.shape[2] // (2 * half)
    member = lax.axis_index("tensor")
    peer = {"tensor": 1 - member}
    tall, short = 256, 128
    width = hidden_ref.shape[1]

    def across(source, target, send, receive):
        return pltpu.make_async_remote_copy(
            src_ref=source,
            dst_ref=target,
            send_sem=send,
            recv_sem=receive,
            device_id=peer,
            device_id_type=MESH,
        )

    def rows_of(which):
        return pl.ds(pl.multiple_of(which * rows, rows), rows)

    def tile(step, size):
        return pl.ds(pl.multiple_of(step * size, size), size)

    def loads(j, slot):
        piece, at = 1 + j // per_piece, lax.rem(j, per_piece) * half
        copies = []
        for kind, buf in enumerate((expand_buf, reduce_buf)):
            first = pl.multiple_of(at + kind * per_piece * half, half)
            for side, source in enumerate((far_ref, whole_ref)):
                copies.append(
                    pltpu.make_async_copy(
                        source.at[piece, :, pl.ds(first, half)],
                        buf.at[slot, :, pl.ds(side * half, half)],
                        load_sem.at[slot, kind, side],
                    )
                )
        return copies

    for copy in loads(0, 0):
        copy.start()
    barrier = pltpu.get_barrier_semaphore()
    pl.semaphore_signal(barrier, inc=1, device_id=peer, device_id_type=MESH)
    pl.semaphore_wait(barrier, 1)
    out_ctx = across(context_ref.at[rows_of(1 - member)], far_ctx, ctx_sem.at[0], ctx_sem.at[1])
    out_ctx.start()
    in_ctx = pltpu.make_async_copy(context_ref.at[rows_of(member)], own_ctx, ctx_sem.at[2])
    in_ctx.start()
    sums_ref[...] = jnp.zeros_like(sums_ref)
    in_ctx.wait()
    out_ctx.wait()

    def add_sum(row, values):
        sums_ref[row : row + 1, :] += jnp.sum(values, axis=0, keepdims=True)

    @pl.loop(0, rows // short)
    def _(step):
        at = tile(step, short)
        branch = dot_nt(own_ctx[at, :], merge_ref[...]) + dot_nt(far_ctx[at, :], merge_far_ref[...])
        unit, scale = norm(hidden_ref[at, :].astype(WIDE) + branch + vectors_ref[2:3, :])
        normed = unit * vectors_ref[3:4, :] + vectors_ref[4:5, :]
        normal[at, :] = unit
        inverse[at, :] = jnp.broadcast_to(scale, (short, 128))
        low[at, :] = normed.astype(LOW)
        turned[:, at] = normed.T.astype(LOW)
        acc[at, :] = normed + vectors_ref[5:6, :]

    @pl.loop(0, chunks)
    def _(j):
        slot = lax.rem(j, 2)
        for copy in loads(j, slot):
            copy.wait()

        @pl.when(j + 1 < chunks)
        def _():
            for copy in loads(j + 1, 1 - slot):
                copy.start()

        for step in range(rows // tall):
            at = slice(step * tall, (step + 1) * tall)
            inner = dot_nn(low[at, :], expand_buf[slot]) + bias_ref[j]
            below, bell = normal_cells(inner)
            held = (inner * below).astype(LOW)
            active[j, at, :] = held
            slope[j, at, :] = (below + inner * bell * 0.3989422804014327).astype(LOW)
            acc[at, :] += dot_nt(held, reduce_buf[slot])

    for copy in loads(0, 0):
        copy.start()

    @pl.loop(0, rows // short)
    def _(step):
        at = tile(step, short)
        unit, scale = norm(acc[at, :])
        encoded_ref[at, :] = (unit * vectors_ref[6:7, :] + vectors_ref[7:8, :]).astype(LOW)
        upper = upstream_ref[at, :].astype(WIDE)
        add_sum(6, upper * unit)
        add_sum(7, upper)
        grad = norm_back(upper * vectors_ref[6:7, :], unit, scale)
        grad_low = grad.astype(LOW)
        add_sum(5, grad_low.astype(WIDE))
        acc[at, :] = grad
        late[at, :] = grad_low
        late_turned[:, at] = grad.T.astype(LOW)

    def send(j, kind):
        return across(
            leaving.at[lax.rem(j, 2), kind],
            arrived.at[lax.rem(j, 4), kind],
            send_sem.at[lax.rem(j, 2), kind],
            recv_sem.at[lax.rem(j, 4), kind],
        )

    def store(j, kind):
        target = (expand_grad_ref, reduce_grad_ref)[kind]
        cols = pl.ds(pl.multiple_of(j * half, half), half)
        return pltpu.make_async_copy(
            done.at[lax.rem(j, 2), kind], target.at[:, cols], out_sem.at[lax.rem(j, 2), kind]
        )

    def finish(j):
        for kind in range(2):
            send(j, kind).wait_recv()

            @pl.when(j >= 2)
            def _():
                store(j - 2, kind).wait()

            @pl.loop(0, width // tall)
            def _(step):
                at = tile(step, tall)
                done[lax.rem(j, 2), kind, at, :] = (
                    kept[lax.rem(j, 2), kind, at, :]
                    + arrived[lax.rem(j, 4), kind, at, :].astype(WIDE)
                ).astype(LOW)

            store(j, kind).start()

    @pl.loop(0, chunks)
    def _(j):
        slot = lax.rem(j, 2)
        for copy in loads(j, slot):
            copy.wait()

        @pl.when(j + 1 < chunks)
        def _():
            for copy in loads(j + 1, 1 - slot):
                copy.start()

        total = jnp.zeros((1, both), WIDE)
        for step in range(rows // tall):
            at = slice(step * tall, (step + 1) * tall)
            grad = dot_nn(late[at, :], reduce_buf[slot]) * slope[j, at, :].astype(WIDE)
            grad = grad.astype(LOW)
            inner_grad[at, :] = grad
            total = total + jnp.sum(grad.astype(WIDE), axis=0, keepdims=True)
            acc[at, :] += dot_nt(grad, expand_buf[slot])
        hidden_sums_ref[j] = total

        @pl.when(j >= 2)
        def _():
            for kind in range(2):
                send(j - 2, kind).wait_send()

        for kind, (left, right) in enumerate(((turned, inner_grad), (late_turned, active.at[j]))):
            for step in range(width // tall):
                at = slice(step * tall, (step + 1) * tall)
                part = dot_nn(left[at, :], right[...])
                leaving[slot, kind, at, :] = part[:, 0:half].astype(LOW)
                kept[slot, kind, at, :] = part[:, half:both]
            send(j, kind).start()

        @pl.when(j >= 1)
        def _():
            finish(j - 1)

    @pl.loop(0, rows // short)
    def _(step):
        at = tile(step, short)
        grad = acc[at, :]
        unit = normal[at, :]
        add_sum(3, grad * unit)
        add_sum(4, grad)
        branch_grad = norm_back(grad * vectors_ref[3:4, :], unit, inverse[at, 0:1])
        branch_low = branch_grad.astype(LOW)
        add_sum(2, branch_low.astype(WIDE))
        branch_ref[at, :] = branch_grad
        turned[:, at] = branch_grad.T.astype(LOW)
        grad_far[at, :] = dot_nn(branch_low, merge_far_ref[...]).astype(LOW)
        grad_own[at, :] = dot_nn(branch_low, merge_ref[...]).astype(LOW)

    out_grad = across(grad_far, grad_ref.at[rows_of(member)], ctx_sem.at[0], ctx_sem.at[1])
    out_grad.start()
    in_grad = pltpu.make_async_copy(grad_own, grad_ref.at[rows_of(member)], ctx_sem.at[2])
    in_grad.start()
    for step in range(width // tall):
        at = slice(step * tall, (step + 1) * tall)
        merge_send[at, :] = dot_nn(turned[at, :], far_ctx[...]).astype(LOW)
    out_merge = across(merge_send, merge_recv, last_sem.at[0], last_sem.at[1])
    out_merge.start()
    finish(chunks - 1)
    for kind in range(2):
        send(chunks - 2, kind).wait_send()
        send(chunks - 1, kind).wait_send()
        store(chunks - 2, kind).wait()
        store(chunks - 1, kind).wait()
    out_merge.wait()
    for step in range(width // tall):
        at = slice(step * tall, (step + 1) * tall)
        merge_grad_ref[at, :] = (
            dot_nn(turned[at, :], own_ctx[...]) + merge_recv[at, :].astype(WIDE)
        ).astype(LOW)
    out_grad.wait()
    in_grad.wait()


def feed_block(context, whole, far, hidden_own, upstream, vectors, bias_own, bias_far):
    total_rows, inner = context.shape
    rows, width = hidden_own.shape
    hidden = bias_own.shape[0]
    merge, merge_far = whole[0, :, -inner:], far[0, :, -inner:]
    half = 256
    chunks = hidden // half
    both = 2 * half
    bias = jnp.concatenate(
        [bias_far.reshape(chunks, 1, half), bias_own.reshape(chunks, 1, half)], axis=2
    )
    vmem, anywhere = pl.BlockSpec(memory_space=pltpu.VMEM), pl.BlockSpec(memory_space=pl.ANY)
    sem = pltpu.SemaphoreType.DMA
    shape = jax.ShapeDtypeStruct
    *results, hidden_sums = pl.pallas_call(
        feed_kernel,
        in_specs=[anywhere, vmem, vmem, *[anywhere] * 2, *[vmem] * 4],
        out_specs=[vmem, vmem, anywhere, vmem, anywhere, anywhere, vmem, vmem],
        out_shape=[
            shape((rows, width), LOW),
            shape((rows, width), WIDE),
            shape((total_rows, inner), LOW),
            shape((width, inner), LOW),
            shape((width, hidden), LOW),
            shape((width, hidden), LOW),
            shape((8, width), WIDE),
            shape((chunks, 1, both), WIDE),
        ],
        scratch_shapes=[
            pltpu.VMEM((rows, inner), LOW),
            pltpu.VMEM((rows, inner), LOW),
            pltpu.VMEM((rows, width), WIDE),
            pltpu.VMEM((rows, width), WIDE),
            pltpu.VMEM((rows, 128), WIDE),
            pltpu.VMEM((rows, width), LOW),
            pltpu.VMEM((width, rows), LOW),
            pltpu.VMEM((rows, width), LOW),
            pltpu.VMEM((width, rows), LOW),
            pltpu.VMEM((chunks, rows, both), LOW),
            pltpu.VMEM((chunks, rows, both), LOW),
            pltpu.VMEM((rows, both), LOW),
            pltpu.VMEM((2, width, both), LOW),
            pltpu.VMEM((2, width, both), LOW),
            pltpu.VMEM((4, 2, width, half), LOW),
            pltpu.VMEM((2, 2, width, half), LOW),
            pltpu.VMEM((2, 2, width, half), WIDE),
            pltpu.VMEM((2, 2, width, half), LOW),
            pltpu.VMEM((rows, inner), LOW),
            pltpu.VMEM((rows, inner), LOW),
            pltpu.VMEM((width, inner), LOW),
            pltpu.VMEM((width, inner), LOW),
            sem((3,)),
            sem((2, 2, 2)),
            sem((2, 2)),
            sem((4, 2)),
            sem((2, 2)),
            sem((2,)),
        ],
        compiler_params=pltpu.CompilerParams(
            collective_id=2, has_side_effects=True, vmem_limit_bytes=60 * MIB
        ),
        cost_estimate=pl.CostEstimate(
            flops=12 * rows * width * 2 * hidden, bytes_accessed=8 * width * hidden * 4, transcendentals=0
        ),
    )(context, merge, merge_far, whole, far, hidden_own, upstream, vectors, bias)
    hidden_far = hidden_sums[:, 0, :half].reshape(-1)
    hidden_near = hidden_sums[:, 0, half:].reshape(-1)
    return (*results, hidden_near, hidden_far)


class Scatter:
    buffers = 8

    def __init__(self, depth, grads, shards, buffers, sems):
        self.depth, self.grads, self.shards = depth, grads, shards
        self.held = [buffers[8 * p : 8 * p + 8] for p in range(len(grads))]
        self.me, self.z, self.y, self.x = place()
        self.x_peer = self.z * 4 + self.y * 2 + 1 - self.x
        self.y_peer = self.z * 4 + (1 - self.y) * 2 + self.x
        self.rows = grads[0].shape[0] // (4 * depth)
        (
            self.a1_send, self.a1_recv, self.a2_send, self.a2_recv, self.b2_send, self.b2_recv, self.b1_send, self.b1_recv,
            self.z_send, self.z_recv, self.zc_send, self.zc_recv, self.c_send, self.c_recv,
        ) = sems

    @staticmethod
    def scratch(depth, rows, classes):
        found = []
        for a, b, c in classes:
            found += [
                pltpu.VMEM((depth, 2 * rows, a), LOW),
                pltpu.VMEM((depth, 2, rows, b), LOW),
                pltpu.VMEM((depth, rows, a), LOW),
                pltpu.VMEM((depth, rows, b), LOW),
                pltpu.VMEM((depth + 1, rows, a + b), LOW),
                pltpu.VMEM((depth + 1, 4 * rows, c), LOW),
                pltpu.VMEM((2 * rows, c), LOW),
                pltpu.VMEM((rows, c), LOW),
            ]
        return found

    @staticmethod
    def semaphores(depth, pieces):
        sem = pltpu.SemaphoreType.DMA
        return [
            *[sem((pieces, depth))] * 6,
            *[sem((pieces, depth, 2))] * 2,
            *[sem((pieces, depth)), sem((pieces, depth + 1))] * 2,
            sem((pieces, 2)),
            sem((pieces, 2)),
        ]

    def columns(self, p):
        a, b, c = (self.held[p][i].shape[-1] for i in (0, 1, 5))
        return pl.ds(0, a), pl.ds(a, b), pl.ds(a + b, c)

    def block(self, zb, yb, xb):
        return zb * 4 + yb * 2 + xb

    def span(self, block, count=1):
        return pl.ds(pl.multiple_of(block * self.rows, self.rows), count * self.rows)

    def add(self, put, count, *terms):
        chunk = min(count, 64)

        @pl.loop(0, count // chunk)
        def _(step):
            at = pl.multiple_of(step * chunk, chunk)
            parts = [term(at, chunk) for term in terms]
            if len(parts) > 2 or put.wide:
                parts = [part.astype(WIDE) for part in parts]
            total = parts[0]
            for part in parts[1:]:
                total = total + part
            put(at, chunk, total)

    def a1(self, p, zb):
        return remote(
            self.grads[p].at[self.span(self.block(zb, 1 - self.y, 0), 2), self.columns(p)[0]],
            self.held[p][0].at[zb],
            self.a1_send.at[p, zb],
            self.a1_recv.at[p, zb],
            self.y_peer,
        )

    def b1(self, p, zb, yb):
        return remote(
            self.grads[p].at[self.span(self.block(zb, yb, 1 - self.x)), self.columns(p)[1]],
            self.held[p][1].at[zb, yb],
            self.b1_send.at[p, zb, yb],
            self.b1_recv.at[p, zb, yb],
            self.x_peer,
        )

    def a2(self, p, zb):
        return remote(
            self.held[p][0].at[zb, self.span(1 - self.x)],
            self.held[p][2].at[zb],
            self.a2_send.at[p, zb],
            self.a2_recv.at[p, zb],
            self.x_peer,
        )

    def b2(self, p, zb):
        return remote(
            self.held[p][1].at[zb, 1 - self.y],
            self.held[p][3].at[zb],
            self.b2_send.at[p, zb],
            self.b2_recv.at[p, zb],
            self.y_peer,
        )

    def slot(self, zb, way):
        return zb if way > 0 else zb + (self.depth - zb) * jnp.where(zb == self.z - 1, 1, 0)

    def z_copy(self, p, zb, way):
        slot = self.slot(zb, way)
        return remote(
            self.held[p][4].at[zb],
            self.held[p][4].at[slot],
            self.z_send.at[p, zb],
            self.z_recv.at[p, slot],
            self.me + 4 * way,
        )

    def zc_copy(self, p, zb, way, first):
        slot = self.slot(zb, way)
        source = self.held[p][5].at[zb]
        if first:
            source = self.grads[p].at[self.span(zb * 4, 4), self.columns(p)[2]]
        return remote(
            source,
            self.held[p][5].at[slot],
            self.zc_send.at[p, zb],
            self.zc_recv.at[p, slot],
            self.me + 4 * way,
        )

    def arrived(self, ref, sem, slot):
        part = ref.at[slot]
        remote(part, part, sem, sem, self.me).wait_recv()

    def cy(self, p):
        return remote(
            self.held[p][5].at[self.z, self.span(2 * (1 - self.y), 2)],
            self.held[p][6],
            self.c_send.at[p, 0],
            self.c_recv.at[p, 0],
            self.y_peer,
        )

    def cx(self, p):
        return remote(
            self.held[p][5].at[self.z, self.span(2 * self.y + 1 - self.x)],
            self.held[p][7],
            self.c_send.at[p, 1],
            self.c_recv.at[p, 1],
            self.x_peer,
        )

    def grad(self, p, block, columns):
        def term(at, count):
            first = pl.multiple_of(block * self.rows + at, 16)
            return self.grads[p][pl.ds(first, count), columns]

        return term

    def part(self, ref, lead, block, columns=None):
        columns = slice(None) if columns is None else columns

        def term(at, count):
            first = pl.multiple_of(block * self.rows + at, 16)
            return ref[(*lead, pl.ds(first, count), columns)]

        return term

    def put(self, ref, lead, block, columns=None):
        columns = slice(None) if columns is None else columns

        def act(at, count, total):
            first = pl.multiple_of(block * self.rows + at, 16)
            ref[(*lead, pl.ds(first, count), columns)] = total.astype(ref.dtype)

        act.wide = ref.dtype == WIDE
        return act

    def open(self, p, zb):
        self.a1(p, zb).start()
        self.b1(p, zb, 0).start()
        self.b1(p, zb, 1).start()

    def first(self, p, zb):
        z, y, x = self.z, self.y, self.x
        a, b, _ = self.columns(p)
        r1a, r1b = self.held[p][0], self.held[p][1]
        self.a1(p, zb).wait_recv()
        self.add(
            self.put(r1a, (zb,), 1 - x),
            self.rows,
            self.part(r1a, (zb,), 1 - x),
            self.grad(p, self.block(zb, y, 1 - x), a),
        )
        self.a2(p, zb).start()
        self.b1(p, zb, 0).wait_recv()
        self.b1(p, zb, 1).wait_recv()
        self.add(
            self.put(r1b, (zb, 1 - y), 0),
            self.rows,
            self.part(r1b, (zb, 1 - y), 0),
            self.grad(p, self.block(zb, 1 - y, x), b),
        )
        self.b2(p, zb).start()

    def terms(self, p, zb):
        z, y, x = self.z, self.y, self.x
        a, b, _ = self.columns(p)
        r1a, r1b, r2a, r2b = self.held[p][:4]
        own = self.block(zb, y, x)
        return (
            [self.grad(p, own, a), self.part(r1a, (zb,), x), self.part(r2a, (zb,), 0)],
            [self.grad(p, own, b), self.part(r1b, (zb, y), 0), self.part(r2b, (zb,), 0)],
        )

    def pass_on(self, p, zb, way):
        a, b, _ = self.columns(p)
        rz = self.held[p][4]
        self.a2(p, zb).wait_recv()
        self.b2(p, zb).wait_recv()
        from_line = (self.z - way >= 0) & (self.z - way < self.depth)

        @pl.when(from_line)
        def _():
            self.arrived(rz, self.z_recv.at[p, zb], zb)
            for terms, columns in zip(self.terms(p, zb), (a, b), strict=True):
                self.add(
                    self.put(rz, (zb,), 0, columns),
                    self.rows,
                    *terms,
                    self.part(rz, (zb,), 0, columns),
                )

        @pl.when(jnp.logical_not(from_line))
        def _():
            for terms, columns in zip(self.terms(p, zb), (a, b), strict=True):
                self.add(self.put(rz, (zb,), 0, columns), self.rows, *terms)

        self.z_copy(p, zb, way).start()

    def pass_c(self, p, zb, way):
        c = self.columns(p)[2]
        rc = self.held[p][5]
        from_line = (self.z - way >= 0) & (self.z - way < self.depth)

        @pl.when(from_line)
        def _():
            self.arrived(rc, self.zc_recv.at[p, zb], zb)
            self.add(
                self.put(rc, (zb,), 0),
                4 * self.rows,
                self.part(rc, (zb,), 0),
                self.grad(p, zb * 4, c),
            )
            self.zc_copy(p, zb, way, False).start()

        @pl.when(jnp.logical_not(from_line))
        def _():
            self.zc_copy(p, zb, way, True).start()

    def own_c(self, p):
        z, depth = self.z, self.depth
        c = self.columns(p)[2]
        rc = self.held[p][5]
        grad = self.grad(p, z * 4, c)
        lower, upper = self.part(rc, (z,), 0), self.part(rc, (depth,), 0)
        put = self.put(rc, (z,), 0)

        @pl.when(z > 0)
        def _():
            self.arrived(rc, self.zc_recv.at[p, z], z)

        @pl.when(z < depth - 1)
        def _():
            self.arrived(rc, self.zc_recv.at[p, depth], depth)

        @pl.when((z > 0) & (z < depth - 1))
        def _():
            self.add(put, 4 * self.rows, grad, lower, upper)

        @pl.when(z == 0)
        def _():
            self.add(put, 4 * self.rows, grad, upper)

        @pl.when(z == depth - 1)
        def _():
            self.add(put, 4 * self.rows, grad, lower)

        self.cy(p).start()

    def turn_c(self, p):
        rc, rcy = self.held[p][5], self.held[p][6]
        self.cy(p).wait_recv()
        self.add(
            self.put(rc, (self.z,), 2 * self.y),
            2 * self.rows,
            self.part(rc, (self.z,), 2 * self.y),
            self.part(rcy, (), 0),
        )
        self.cx(p).start()

    def close(self, p):
        z, depth = self.z, self.depth
        a, b, c = self.columns(p)
        rz, rc, rcx = self.held[p][4], self.held[p][5], self.held[p][7]
        self.a2(p, z).wait_recv()
        self.b2(p, z).wait_recv()

        @pl.when(z > 0)
        def _():
            self.arrived(rz, self.z_recv.at[p, z], z)

        @pl.when(z < depth - 1)
        def _():
            self.arrived(rz, self.z_recv.at[p, depth], depth)

        def total(*slots):
            for terms, columns in zip(self.terms(p, z), (a, b), strict=True):
                lines = [self.part(rz, (slot,), 0, columns) for slot in slots]
                self.add(self.put(self.shards[p], (), 0, columns), self.rows, *terms, *lines)

        pl.when((z > 0) & (z < depth - 1))(lambda: total(z, depth))
        pl.when(z == 0)(lambda: total(depth))
        pl.when(z == depth - 1)(lambda: total(z))
        self.cx(p).wait_recv()
        self.add(
            self.put(self.shards[p], (), 0, c),
            self.rows,
            self.part(rc, (z,), 2 * self.y + self.x),
            self.part(rcx, (), 0),
        )

    def at_step(self, step, act):
        z, depth = self.z, self.depth
        if step < 0:
            act(z, 0)
            return
        for zb, valid, way in (
            (z + 1 + step, z + 1 + step < depth, 1),
            (z - 1 - step, z - 1 - step >= 0, -1),
        ):
            pl.when(valid)(functools.partial(act, zb, way))

    def stage(self, p, s):
        last = self.depth - 2

        def opened(step):
            self.at_step(step, lambda zb, way: self.open(p, zb))

        def added(step):
            self.at_step(step, lambda zb, way: self.first(p, zb))

        def passed(step):
            self.at_step(step, lambda zb, way: self.pass_on(p, zb, way))

        def passed_c(step):
            self.at_step(step, lambda zb, way: self.pass_c(p, zb, way))

        if s == 0:
            opened(last)
            opened(last - 1)
            passed_c(last)
            return
        if s <= last + 2:
            added(last + 1 - s)
        if last - 1 - s >= -1:
            opened(last - 1 - s)
        if last - s >= 0:
            passed_c(last - s)
        if s >= 2 and last + 2 - s >= 0:
            passed(last + 2 - s)
        if s == last + 1:
            self.own_c(p)
        if s == last + 2:
            self.turn_c(p)
        if s == last + 3:
            self.close(p)

    def sent(self, p):
        def line(zb, way):
            from_line = (self.z - way >= 0) & (self.z - way < self.depth)
            self.z_copy(p, zb, way).wait_send()
            pl.when(from_line)(lambda: self.zc_copy(p, zb, way, False).wait_send())
            pl.when(jnp.logical_not(from_line))(lambda: self.zc_copy(p, zb, way, True).wait_send())

        for zb in range(self.depth):
            self.a1(p, zb).wait_send()
            self.b1(p, zb, 0).wait_send()
            self.b1(p, zb, 1).wait_send()
            self.a2(p, zb).wait_send()
            self.b2(p, zb).wait_send()
        for step in range(self.depth - 1):
            self.at_step(step, line)
        self.cy(p).wait_send()
        self.cx(p).wait_send()


class SmallSum:
    def __init__(self, lines, buffer, send, recv):
        member = lax.axis_index("tensor")
        self.partners = [{"tensor": 1 - member}, {"dp": lines.x_peer}, {"dp": lines.y_peer}]
        for level in range(lines.depth.bit_length() - 1):
            reach = 1 << level
            way = 1 - 2 * ((lines.z // reach) % 2)
            self.partners.append({"dp": lines.me + 4 * reach * way})
        self.buffer, self.send, self.recv = buffer, send, recv

    def copy(self, step):
        return pltpu.make_async_remote_copy(
            src_ref=self.buffer.at[step],
            dst_ref=self.buffer.at[len(self.partners) + 1 + step],
            send_sem=self.send.at[step],
            recv_sem=self.recv.at[step],
            device_id=self.partners[step],
            device_id_type=MESH,
        )

    def step(self, step):
        if step:
            self.copy(step - 1).wait_recv()
            self.buffer[step] = self.buffer[step - 1] + self.buffer[len(self.partners) + step]
        if step < len(self.partners):
            self.copy(step).start()

    def sent(self):
        for step in range(len(self.partners)):
            self.copy(step).wait_send()


def adamw_update(master, moment, square, gradient, step_rate, decay_rate):
    moment_new = beta_one * moment + (1.0 - beta_one) * gradient
    square_new = beta_two * square + (1.0 - beta_two) * gradient * gradient
    moment_hat = moment_new / (1.0 - beta_one**STEP)
    square_hat = square_new / (1.0 - beta_two**STEP)
    master_new = master - step_rate * (
        moment_hat / (jnp.sqrt(square_hat) + adam_epsilon) + decay_rate * master
    )
    return (moment_new, square_new, master_new)


SCATTER_AT = {
    "reduce": {6: [(0, 0)]},
    "expand": {0: [(1, 0)], 1: [(0, 1)], 2: [(1, 1)], 3: [(0, 2)]},
    "norm": {-1: [(3, 0), (0, 3)], 1: [(2, 0)], 2: [(3, 1), (1, 2)]},
    "merge": {-1: [(0, 4)]},
    "attend": {0: [(3, 2)], 5: [(2, 1)], 7: [(1, 3)], 10: [(3, 3), (2, 2)], 13: [(3, 4)], 18: [(4, 1)], 19: [(0, 5), (2, 3)], 21: [(4, 2), (1, 5)]},
    "project": {0: [(4, 0), (1, 4)], 1: [(5, 0)]},
    "terms": {2: [(5, 1)], 3: [(4, 3)]},
    "far": {-1: [(5, 2)]},
    "near": {-1: [(2, 4), (5, 3)], 0: [(4, 4)]},
    "encoded": {-1: [(5, 4)], 1: [(5, 5)]},
    "end": [(3, 5), (2, 5), (4, 5)],
}


def back_kernel(
    depth, lengths_ref, dealing_ref, vectors_ref,
    whole_ref, far_ref, qkv_in, hidden_turned_in, upstream_in, context_in, long_in, short_in,
    acc_in, normal_in, inverse_in, turned_in, active_in, slope_in, far_ctx_in, *rest,
):
    encoded_out, input_out, small_out, *rest = rest
    shards, rest = rest[:6], rest[6:]
    enc_pair, grad_ref, input_far, acc, arrived, merge_recv, small, *rest = rest
    grads, rest = rest[:6], rest[6:]
    buffers, rest = rest[: 6 * Scatter.buffers], rest[6 * Scatter.buffers :]
    small_send, small_recv, in_sem, load_sem, ctx_sem, far_send, far_recv, merge_sem, enc_sem, input_sem, kept_sem, *sems = rest
    lines = Scatter(depth, grads, shards, buffers, sems)
    sums = SmallSum(lines, small, small_send, small_recv)
    group = Group(lengths_ref, dealing_ref)
    member = lax.axis_index("tensor")
    rows, width = acc.shape
    total_rows = 2 * rows
    chunks, _, both = active_in.shape
    half = both // 2
    per_piece = chunks // 2
    piece_span = grads[0].shape[1]
    pairs = qkv_in.shape[0]
    inner = pairs * PAIR
    tall, short = 256, 128

    def rows_of(which):
        return pl.ds(pl.multiple_of(which * rows, rows), rows)

    def tile(step, size):
        return pl.ds(pl.multiple_of(step * size, size), size)

    def fetch(source, target, sem):
        return pltpu.make_async_copy(source, target, in_sem.at[sem])

    def phase(name, count, body):
        between = {
            step: [functools.partial(lines.stage, *stage) for stage in stages]
            for step, stages in SCATTER_AT.get(name, {}).items()
        }
        for act in between.pop(-1, ()):
            act()
        looped(count, body, between)

    def places_of(first):
        return first + lax.broadcasted_iota(jnp.int32, (tall, 1), 0)

    def add_sum(row, values):
        small[0, row : row + 1, :] += jnp.sum(values, axis=0, keepdims=True)

    acc_copy = fetch(acc_in, acc, 0)
    acc_copy.start()
    greet_line(
        lines.me, lines.z, lines.y, lines.x, depth, [sums.partners[0], *sums.partners[3:]]
    )
    small[0] = jnp.zeros(small.shape[1:], WIDE)

    def feed_phase(late, late_turned, turned, upstream, active, slope, inner_grad, expand_buf, reduce_buf, leaving, encoded):
        def active_load(j):
            slot = lax.rem(j, 2)
            return [pltpu.make_async_copy(active_in.at[j], active.at[slot], load_sem.at[slot, 4])]

        def loads(j):
            slot = lax.rem(j, 2)
            piece, at = 1 + j // per_piece, lax.rem(j, per_piece) * half
            copies = [pltpu.make_async_copy(slope_in.at[j], slope.at[slot], load_sem.at[slot, 5])]
            for kind, buf in enumerate((expand_buf, reduce_buf)):
                first = pl.multiple_of(at + kind * per_piece * half, half)
                for side, source in enumerate((far_ref, whole_ref)):
                    copies.append(
                        pltpu.make_async_copy(
                            source.at[piece, :, pl.ds(first, half)],
                            buf.at[slot, :, pl.ds(side * half, half)],
                            load_sem.at[slot, 2 * kind + side],
                        )
                    )
            return copies

        def taken(j, load):
            for copy in load(j):
                copy.wait()

            @pl.when(j + 1 < chunks)
            def _():
                for copy in load(j + 1):
                    copy.start()

        fetches = [fetch(upstream_in, upstream, 1), fetch(turned_in, turned, 2)]
        for copy in fetches:
            copy.start()
        for copy in [*active_load(0), *loads(0)]:
            copy.start()
        acc_copy.wait()
        for copy in fetches:
            copy.wait()

        def late_tile(step):
            at = tile(step, short)
            unit, scale = norm(acc[at, :])
            encoded[at, :] = (unit * vectors_ref[6:7, :] + vectors_ref[7:8, :]).astype(LOW)
            upper = upstream[at, :].astype(WIDE)
            add_sum(6, upper * unit)
            add_sum(7, upper)
            grad = norm_back(upper * vectors_ref[6:7, :], unit, scale)
            grad_low = grad.astype(LOW)
            add_sum(5, grad_low.astype(WIDE))
            acc[at, :] = grad
            late[at, :] = grad_low
            late_turned[:, at] = grad.T.astype(LOW)

        looped(rows // short, late_tile, {})
        enc_near = pltpu.make_async_copy(encoded, enc_pair.at[member], enc_sem.at[2])
        enc_far = other_core(encoded, enc_pair.at[member], enc_sem.at[0], enc_sem.at[1])
        enc_near.start()
        enc_far.start()

        def send(k):
            slot = lax.rem(k, 2)
            return other_core(
                leaving.at[slot], arrived.at[slot], far_send.at[slot], far_recv.at[slot]
            )

        def own_columns(k):
            return pl.ds(pl.multiple_of(lax.rem(k, per_piece) * half, half), half)

        def in_piece(k, act):
            for piece in range(4):
                pl.when(k // per_piece == piece)(functools.partial(act, grads[piece]))

        def finish(k):
            send(k).wait_recv()

            def add(grad):
                @pl.loop(0, width // tall)
                def _(step):
                    at = tile(step, tall)
                    grad[at, own_columns(k)] += arrived[lax.rem(k, 2), at, :]

            in_piece(k, add)

        def products(k, left, right):
            @pl.when(k >= 2)
            def _():
                send(k - 2).wait_send()

            for step in range(width // tall):
                at = slice(step * tall, (step + 1) * tall)
                part = dot_nn(left[at, :], right[...])
                leaving[lax.rem(k, 2), at, :] = part[:, 0:half].astype(LOW)
                own = part[:, half:both].astype(LOW)

                def keep(grad, at=at, own=own):
                    grad[at, own_columns(k)] = own

                in_piece(k, keep)

            @pl.when(k >= 1)
            def _():
                finish(k - 1)

            send(k).start()

        def reduce_chunk(j):
            taken(j, active_load)
            products(j, late_turned, active.at[lax.rem(j, 2)])

        def expand_chunk(j):
            slot = lax.rem(j, 2)
            taken(j, loads)
            total = jnp.zeros((1, both), WIDE)
            for step in range(rows // tall):
                at = slice(step * tall, (step + 1) * tall)
                grad = dot_nn(late[at, :], reduce_buf[slot]) * slope[slot, at, :].astype(WIDE)
                grad = grad.astype(LOW)
                inner_grad[at, :] = grad
                total = total + jnp.sum(grad.astype(WIDE), axis=0, keepdims=True)
                acc[at, :] += dot_nt(grad, expand_buf[slot])
            for which, side in ((1 - member, 0), (member, half)):
                row = 8 + which * 2 + j // per_piece
                small[0, pl.ds(row, 1), own_columns(j)] = total[:, side : side + half]
            products(chunks + j, turned, inner_grad)

        phase("reduce", chunks, reduce_chunk)
        phase("expand", chunks, expand_chunk)
        finish(2 * chunks - 1)
        for k in (2 * chunks - 2, 2 * chunks - 1):
            send(k).wait_send()
        enc_near.wait()
        enc_far.wait()

    pl.run_scoped(
        feed_phase,
        pltpu.VMEM((rows, width), LOW),
        pltpu.VMEM((width, rows), LOW),
        pltpu.VMEM((width, rows), LOW),
        pltpu.VMEM((rows, width), LOW),
        pltpu.VMEM((2, rows, both), LOW),
        pltpu.VMEM((2, rows, both), LOW),
        pltpu.VMEM((rows, both), LOW),
        pltpu.VMEM((2, width, both), LOW),
        pltpu.VMEM((2, width, both), LOW),
        pltpu.VMEM((2, width, half), LOW),
        pltpu.VMEM((rows, width), LOW),
    )

    def merge_phase(normal, inverse, turned, near_ctx, far_ctx, merge, merge_far, grad_own, grad_far, merge_send):
        merge_columns = pl.ds(whole_ref.shape[2] - inner, inner)
        fetches = [
            fetch(normal_in, normal, 0),
            fetch(inverse_in, inverse, 1),
            fetch(context_in.at[rows_of(member)], near_ctx, 2),
            fetch(far_ctx_in, far_ctx, 3),
            fetch(whole_ref.at[0, :, merge_columns], merge, 4),
            fetch(far_ref.at[0, :, merge_columns], merge_far, 5),
        ]
        for copy in fetches:
            copy.start()
        for copy in fetches:
            copy.wait()

        def norm_tile(step):
            at = tile(step, short)
            grad = acc[at, :]
            unit = normal[at, :]
            add_sum(3, grad * unit)
            add_sum(4, grad)
            branch_grad = norm_back(grad * vectors_ref[3:4, :], unit, inverse[at, 0:1])
            branch_low = branch_grad.astype(LOW)
            add_sum(2, branch_low.astype(WIDE))
            acc[at, :] = branch_grad
            turned[:, at] = branch_grad.T.astype(LOW)
            grad_far[at, :] = dot_nn(branch_low, merge_far[...]).astype(LOW)
            grad_own[at, :] = dot_nn(branch_low, merge[...]).astype(LOW)

        phase("norm", rows // short, norm_tile)
        out_grad = other_core(grad_far, grad_ref.at[rows_of(member)], ctx_sem.at[0], ctx_sem.at[1])
        in_grad = pltpu.make_async_copy(grad_own, grad_ref.at[rows_of(member)], ctx_sem.at[2])
        out_grad.start()
        in_grad.start()
        out_merge = other_core(merge_send, merge_recv, merge_sem.at[0], merge_sem.at[1])

        def merge_step(which):
            @pl.when(which == 0)
            def _():
                for step in range(width // tall):
                    at = slice(step * tall, (step + 1) * tall)
                    merge_send[at, :] = dot_nn(turned[at, :], far_ctx[...]).astype(LOW)
                out_merge.start()

            @pl.when(which == 1)
            def _():
                out_merge.wait()
                for step in range(width // tall):
                    at = slice(step * tall, (step + 1) * tall)
                    grads[4][at, 0:inner] = (
                        dot_nn(turned[at, :], near_ctx[...]) + merge_recv[at, :].astype(WIDE)
                    ).astype(LOW)

        phase("merge", 2, merge_step)
        out_grad.wait()
        in_grad.wait()

    pl.run_scoped(
        merge_phase,
        pltpu.VMEM((rows, width), WIDE),
        pltpu.VMEM((rows, 128), WIDE),
        pltpu.VMEM((width, rows), LOW),
        pltpu.VMEM((rows, inner), LOW),
        pltpu.VMEM((rows, inner), LOW),
        pltpu.VMEM((width, inner), LOW),
        pltpu.VMEM((width, inner), LOW),
        pltpu.VMEM((rows, inner), LOW),
        pltpu.VMEM((rows, inner), LOW),
        pltpu.VMEM((width, inner), LOW),
    )
    def last_phase(mixed):
        def attend_phase(qkv, context, upper, kept, dots, key_turned, queries, uppers, query_sum, hidden_turned):
            def loads(pair, slot):
                columns = pl.ds(pl.multiple_of(pair * PAIR, PAIR), PAIR)
                return [
                    pltpu.make_async_copy(qkv_in.at[pair], qkv.at[slot], load_sem.at[slot, 0]),
                    pltpu.make_async_copy(
                        context_in.at[:, columns], context.at[slot], load_sem.at[slot, 1]
                    ),
                    pltpu.make_async_copy(
                        grad_ref.at[:, columns], upper.at[slot], load_sem.at[slot, 2]
                    ),
                ]

            blocks = ((0, LONGEST), (LONGEST, total_rows - LONGEST))
            per_pair = total_rows // TILE
            long_tiles = LONGEST // TILE

            def kept_copies(pair, number):
                slot = lax.rem(number, 2)
                tiles = []
                for source, offset, size in (
                    (long_in, 0, LONGEST),
                    (short_in, long_tiles, total_rows - LONGEST),
                ):
                    first = pl.multiple_of(lax.max(number - offset, 0) * TILE, TILE)
                    tiles.append(
                        pltpu.make_async_copy(
                            source.at[pair, :, pl.ds(lax.rem(first, size), TILE)],
                            kept.at[slot, :, :, pl.ds(0, size)],
                            kept_sem.at[slot],
                        )
                    )
                return tiles

            def kept_act(pair, number, act):
                tiles = kept_copies(pair, number)
                pl.when(number < long_tiles)(lambda: act(tiles[0]))
                pl.when(number >= long_tiles)(lambda: act(tiles[1]))

            def start(copy):
                copy.start()

            def wait(copy):
                copy.wait()

            for copy in loads(0, 0):
                copy.start()
            kept_act(0, jnp.int32(0), start)

            def hidden_tile(step, slot):
                return pltpu.make_async_copy(
                    hidden_turned_in.at[tile(step, tall), :],
                    hidden_turned.at[slot],
                    load_sem.at[slot, 3],
                )

            def project(second):
                grad, first = (grads[5], 0) if second else (grads[4], inner)
                span = (pairs // 2) * 3 * PAIR
                columns = slice(span if second else 0, span * 2 if second else span)
                hidden_tile(0, 0).start()
                for step in range(width // tall):
                    if step + 1 < width // tall:
                        hidden_tile(step + 1, (step + 1) % 2).start()
                    hidden_tile(step, step % 2).wait()
                    grad[step * tall : (step + 1) * tall, first : first + span] = dot_nn(
                        hidden_turned[step % 2], mixed[:, columns]
                    ).astype(LOW)

            def pair_body(pair):
                slot = lax.rem(pair, 2)
                for copy in loads(pair, slot):
                    copy.wait()

                @pl.when(pair + 1 < pairs)
                def _():
                    for copy in loads(pair + 1, 1 - slot):
                        copy.start()

                attend_back_open(
                    qkv.at[slot], context.at[slot], upper.at[slot], dots, key_turned, queries, uppers
                )
                base = pair * 3 * PAIR

                def columns(which):
                    return pl.ds(pl.multiple_of(base + which * PAIR, PAIR), PAIR)

                for begin, size in blocks:
                    block = slice(begin, begin + size)
                    query_sum[:, block] = jnp.zeros((PAIR, size), WIDE)

                    def key_tile(step, begin=begin, size=size):
                        number = begin // TILE + step
                        kept_act(pair, number, wait)
                        last = number + 1 == per_pair
                        after = jnp.where(last, 0, number + 1)

                        @pl.when(jnp.logical_not(last & (pair == pairs - 1)))
                        def _():
                            kept_act(pair + jnp.where(last, 1, 0), after, start)

                        at, key_sum, value_sum = attend_back_tile(
                            qkv.at[slot], lambda head: kept[lax.rem(number, 2), head, :, 0:size],
                            dots, key_turned, queries, uppers, query_sum, begin, size, step,
                        )
                        mixed[at, columns(1)] = key_sum.astype(LOW)
                        mixed[at, columns(2)] = value_sum.astype(LOW)

                    between = {}
                    for step in range(size // TILE):
                        number = begin // TILE + step
                        for act_pair in range(pairs):
                            for p, s in SCATTER_AT["attend"].get(act_pair * per_pair + number, ()):

                                def act(act_pair=act_pair, p=p, s=s):
                                    pl.when(pair == act_pair)(lambda: lines.stage(p, s))

                                between.setdefault(step, []).append(act)
                    looped(size // TILE, key_tile, between)
                    mixed[block, columns(0)] = (
                        (query_sum[:, block] * HEAD_DIM ** (-0.5)).T.astype(LOW)
                    )
                for which, row in ((0, 0), (2, 1)):
                    part = mixed[:, columns(which)].astype(WIDE)
                    spot = pl.multiple_of(member * inner + pair * PAIR, PAIR)
                    small[0, row : row + 1, pl.ds(spot, PAIR)] = jnp.sum(
                        part, axis=0, keepdims=True
                    )

            def project_stages(second):
                return [
                    functools.partial(project, second),
                    *[functools.partial(lines.stage, *st) for st in SCATTER_AT["project"][second]],
                ]

            looped(pairs, pair_body, {1: project_stages(0), 3: project_stages(1)})

        pl.run_scoped(
            attend_phase,
            pltpu.VMEM((2, total_rows, 3 * PAIR), LOW),
            pltpu.VMEM((2, total_rows, PAIR), LOW),
            pltpu.VMEM((2, total_rows, PAIR), LOW),
            pltpu.VMEM((2, 2, TILE, LONGEST), LOW),
            pltpu.VMEM((8, total_rows), WIDE),
            pltpu.VMEM((PAIR, total_rows), LOW),
            pltpu.VMEM((2, total_rows, PAIR), LOW),
            pltpu.VMEM((2, total_rows, PAIR), LOW),
            pltpu.VMEM((PAIR, total_rows), WIDE),
            pltpu.VMEM((2, tall, total_rows), LOW),
        )
        sums.step(0)

        def input_phase(weight, terms, leaving):
            fetches = [
                fetch(whole_ref.at[0, :, pl.ds(0, pairs * 3 * PAIR)], weight, 0),
            ]
            for copy in fetches:
                copy.start()
            for copy in fetches:
                copy.wait()

            def term_tile(step):
                at = tile(step, tall)
                total = dot_nt(mixed[at, :], weight[...])
                own = rows // tall
                mine = step // own == member

                @pl.when(mine)
                def _():
                    terms[at, :] = (total + acc[tile(lax.rem(step, own), tall), :]).astype(LOW)

                @pl.when(jnp.logical_not(mine))
                def _():
                    terms[at, :] = total.astype(LOW)

            phase("terms", total_rows // tall, term_tile)
            sums.step(1)

            def own_rows(which, step):
                places = places_of(which * rows + step * tall)
                return picked_rows(group.moved(places, group.own, group.first), terms)

            def far_tile(step):
                leaving[tile(step, tall), :] = own_rows(1 - member, step).astype(LOW)

            phase("far", rows // tall, far_tile)
            crossing = other_core(leaving, input_far, input_sem.at[0], input_sem.at[1])
            crossing.start()
            sums.step(2)

            def near_tile(step):
                acc[tile(step, tall), :] = own_rows(member, step)

            phase("near", rows // tall, near_tile)
            sums.step(3)
            crossing.wait()
            back = fetch(input_far, leaving, 2)
            back.start()
            back.wait()

            @pl.loop(0, rows // short)
            def _(step):
                at = tile(step, short)
                leaving[at, :] = (acc[at, :] + leaving[at, :].astype(WIDE)).astype(LOW)

            done = fetch(leaving, input_out, 2)
            done.start()
            done.wait()

        pl.run_scoped(
            input_phase,
            pltpu.VMEM((width, pairs * 3 * PAIR), LOW),
            pltpu.VMEM((total_rows, width), LOW),
            pltpu.VMEM((rows, width), LOW),
        )

    pl.run_scoped(last_phase, pltpu.VMEM((total_rows, pairs * 3 * PAIR), LOW))

    def end_phase(pair, encoded):
        fetches = [fetch(enc_pair.at[i], pair.at[rows_of(i)], i) for i in range(2)]
        for copy in fetches:
            copy.start()
        for copy in fetches:
            copy.wait()

        def encoded_tile(step):
            places = places_of(member * rows + step * tall)
            index = group.moved(places, group.dealt, group.first)
            encoded[tile(step, tall), :] = picked_rows(index, pair).astype(LOW)

        phase("encoded", rows // tall, encoded_tile)
        done = fetch(encoded, encoded_out, 2)
        done.start()
        for step in range(4, len(sums.partners) + 1):
            sums.step(step)
        small_out[...] = small[len(sums.partners)]
        for st in SCATTER_AT["end"]:
            lines.stage(*st)
        done.wait()

    pl.run_scoped(
        end_phase, pltpu.VMEM((total_rows, width), LOW), pltpu.VMEM((rows, width), LOW)
    )
    sums.sent()
    for p in range(len(grads)):
        lines.sent(p)


def finish_kernel(
    small_ref, vectors_ref, vectors_first, vectors_second, hidden_ref, hidden_first, hidden_second, *rest
):
    shards, (encoded_in, input_in), states_in, rest = rest[:6], rest[6:8], rest[8:20], rest[20:]
    encoded_out, input_out, vector_grad_ref, *rest = rest
    states_out, small_out, ins, outs = rest[:12], rest[12:18], rest[18:30], rest[30:42]
    state_sem, out_sem, pass_sem = rest[42:]
    width = vectors_ref.shape[1]
    inner = ins[3].shape[1]
    pairs = inner // PAIR
    span = shards[0].shape[1]
    loads = [pltpu.make_async_copy(states_in[i], ins[i], state_sem.at[i]) for i in range(12)]
    writes = [pltpu.make_async_copy(outs[i], states_out[i], out_sem.at[i]) for i in range(12)]
    passes = [
        pltpu.make_async_copy(encoded_in, encoded_out, pass_sem.at[0]),
        pltpu.make_async_copy(input_in, input_out, pass_sem.at[1]),
    ]
    for copy in [*reversed(loads), *passes]:
        copy.start()
    vector_grad_ref[...] = small_ref[0:8, :]
    states = vectors_ref[...], vectors_first[...], vectors_second[...]
    for i, value in enumerate(adamw_update(*states, small_ref[0:8, :], rate_vectors, 0.0)):
        small_out[i][...] = value
    for i in range(hidden_ref.shape[1] // width):
        columns = slice(i * width, (i + 1) * width)
        states = hidden_ref[:, columns], hidden_first[:, columns], hidden_second[:, columns]
        grad = small_ref[8 + i : 9 + i, :]
        for n, value in enumerate(adamw_update(*states, grad, rate_hidden, 0.0)):
            small_out[3 + n][:, columns] = value

    def update(matrix, lead, columns, grad, grad_columns):
        rate = (rate_project, rate_merge, rate_expand, rate_reduce)[matrix]

        @pl.loop(0, grad.shape[0] // 16)
        def _(step):
            at = pl.ds(pl.multiple_of(step * 16, 16), 16)
            old = [ins[3 * matrix + i][(*lead, at, columns)] for i in range(3)]
            new = adamw_update(*old, grad[at, grad_columns], rate, weight_decay)
            for i in range(3):
                outs[3 * matrix + i][(*lead, at, columns)] = new[i]

    for matrix in (3, 2, 1, 0):
        mine = slice(3 * matrix, 3 * matrix + 3)
        for copy in loads[mine]:
            copy.wait()
        if matrix >= 2:
            for i in range(2):
                columns = slice(i * span, (i + 1) * span)
                update(matrix, (), columns, shards[2 * (3 - matrix) + i], slice(0, span))
        elif matrix == 1:
            update(matrix, (), slice(0, inner), shards[4], slice(0, inner))
        else:
            for pair in range(pairs):
                piece, begin = (4, inner) if pair < pairs // 2 else (5, 0)
                for c in range(3):
                    at = begin + (3 * (pair % (pairs // 2)) + c) * PAIR
                    columns = slice(pair * PAIR, (pair + 1) * PAIR)
                    update(matrix, (c,), columns, shards[piece], slice(at, at + PAIR))
        for copy in writes[mine]:
            copy.start()
    for copy in [*writes, *passes]:
        copy.wait()


def finish(small, shards, rows_out, matrices, vectors, hidden):
    states = [one for matrix in matrices for one in matrix]
    shape, sem = jax.ShapeDtypeStruct, pltpu.SemaphoreType.DMA
    vmem, anywhere = pl.BlockSpec(memory_space=pltpu.VMEM), pl.BlockSpec(memory_space=pl.ANY)
    held = [pltpu.VMEM(one.shape, WIDE) for one in states]
    return pl.pallas_call(
        finish_kernel,
        in_specs=[*[vmem] * 13, *[anywhere] * 14],
        out_specs=[*[anywhere] * 2, vmem, *[anywhere] * 12, *[vmem] * 6],
        out_shape=[
            *[shape(one.shape, LOW) for one in rows_out],
            shape((8, small.shape[1]), WIDE),
            *[shape(one.shape, WIDE) for one in (*states, *vectors, *hidden)],
        ],
        scratch_shapes=[*held, *held, sem((12,)), sem((12,)), sem((2,))],
        compiler_params=pltpu.CompilerParams(vmem_limit_bytes=40 * MIB),
    )(small, *vectors, *hidden, *shards, *rows_out, *states)


def back(lengths, dealing, vectors, whole, far, kept, parts):
    qkv, hidden_turned, upstream, context, long, short, acc, *_ = kept
    rows, width = acc.shape
    total_rows, inner = context.shape
    depth, shard_rows = parts // 4, width // parts
    half, pair_span = 256, 3 * PAIR * (qkv.shape[0] // 2)
    piece_span = whole.shape[2] // 2
    spans = (*[piece_span] * 4, inner + pair_span, pair_span)
    classes = []
    for span in spans:
        third = max(128, span // 5 // 128 * 128)
        if (span - third) % 256:
            third += 128
        classes.append(((span - third) // 2, (span - third) // 2, third))
    shape, sem = jax.ShapeDtypeStruct, pltpu.SemaphoreType.DMA
    vmem, anywhere = pl.BlockSpec(memory_space=pltpu.VMEM), pl.BlockSpec(memory_space=pl.ANY)
    steps = 3 + depth.bit_length() - 1
    results = pl.pallas_call(
        functools.partial(back_kernel, depth),
        in_specs=[
            *[pl.BlockSpec(memory_space=pltpu.SMEM)] * 2,
            vmem,
            *[anywhere] * (2 + len(kept)),
        ],
        out_specs=[*[anywhere] * 2, *[vmem] * (1 + len(spans)), *[anywhere] * 3],
        out_shape=[
            shape((rows, width), LOW),
            shape((rows, width), LOW),
            shape((16, width), WIDE),
            *[shape((shard_rows, span), WIDE) for span in spans],
            shape((2, rows, width), LOW),
            shape((total_rows, inner), LOW),
            shape((rows, width), LOW),
        ],
        scratch_shapes=[
            pltpu.VMEM((rows, width), WIDE),
            pltpu.VMEM((2, width, half), LOW),
            pltpu.VMEM((width, inner), LOW),
            pltpu.VMEM((2 * steps + 1, 16, width), WIDE),
            *[pltpu.VMEM((width, span), LOW) for span in spans],
            *Scatter.scratch(depth, shard_rows, classes),
            sem((steps,)),
            sem((steps,)),
            sem((6,)),
            sem((2, 6)),
            sem((3,)),
            sem((2,)),
            sem((2,)),
            sem((2,)),
            sem((3,)),
            sem((2,)),
            sem((2,)),
            *Scatter.semaphores(depth, len(spans)),
        ],
        compiler_params=pltpu.CompilerParams(
            collective_id=1, has_side_effects=True, vmem_limit_bytes=63 * MIB
        ),
    )(lengths, dealing, vectors, whole, far, *kept)
    return results[:2], results[2], results[3 : 3 + len(spans)]


def by_kernels(tokens, cotangent, lengths, dealing, project, merge, expand, reduce, vectors, hidden, parts):
    hidden = tuple(one.reshape(1, -1) for one in hidden)
    matrices = (project, merge, expand, reduce)
    whole, far, *kept = front(
        lengths, dealing, *[one[0] for one in matrices], vectors[0], hidden[0], tokens, cotangent, parts
    )
    rows_out, small, shards = back(lengths, dealing, vectors[0], whole, far, kept, parts)
    results = finish(small, shards, rows_out, matrices, vectors, hidden)
    encoded, input_grad, vector_grad = results[:3]
    news = [results[3 + 3 * i : 6 + 3 * i] for i in range(6)]
    return (
        encoded,
        input_grad,
        *news[0],
        *[one.T for one in news[1]],
        *news[2],
        *[one.T for one in news[3]],
        *news[4],
        *[one.reshape(-1) for one in news[5]],
        vector_grad,
    )


def local(
    tokens,
    cotangent,
    lengths,
    dealing,
    project_weight,
    project_first,
    project_second,
    merge_weight,
    merge_first,
    merge_second,
    expand_weight,
    expand_first,
    expand_second,
    reduce_weight,
    reduce_first,
    reduce_second,
    vectors,
    vector_first,
    vector_second,
    hidden_bias,
    hidden_first,
    hidden_second,
):
    parts = lax.axis_size("dp")
    member = lax.axis_index("tensor")
    other = 1 - member
    half_rows, model_width = tokens.shape
    total_rows = 2 * half_rows
    width_half = project_weight.shape[2]
    pairs = width_half // PAIR
    hidden_half = expand_weight.shape[1]
    shard_rows = expand_weight.shape[0]
    own_begin = member * half_rows
    by_kernel = parts % 4 == 0 and (parts & (parts - 1)) == 0 and shard_rows % 16 == 0

    def swap(value):
        return lax.ppermute(value, "tensor", [(0, 1), (1, 0)])

    def own(value, size, which=member):
        return lax.dynamic_slice_in_dim(value, which * size, size, 0)

    if by_kernel:
        return by_kernels(
            tokens, cotangent, lengths, dealing,
            (project_weight, project_first, project_second),
            (merge_weight.T, merge_first.T, merge_second.T),
            (expand_weight, expand_first, expand_second),
            (reduce_weight.T, reduce_first.T, reduce_second.T),
            (vectors, vector_first, vector_second),
            (hidden_bias, hidden_first, hidden_second),
            parts,
        )

    segment, own_of, dealt_of, from_own, from_dealt = layout(lengths[0], dealing[0], total_rows)
    dealt_of = own(dealt_of, half_rows)
    short = segment[LONGEST:]
    score_bias = jnp.where(short[:, None] == short[None, :], 0.0, masked_score).astype(WIDE)

    def own_first(index):
        return lax.rem(index - own_begin + total_rows, total_rows)

    projections = (
        project_weight.reshape(3, shard_rows, pairs, PAIR)
        .transpose(1, 2, 0, 3)
        .reshape(shard_rows, 3 * width_half)
    )
    quarter = hidden_half // 2
    reduce_turned = reduce_weight.T
    shards = jnp.stack(
        [
            jnp.concatenate([projections, merge_weight.T], axis=1),
            jnp.concatenate([expand_weight[:, :quarter], reduce_turned[:, :quarter]], axis=1),
            jnp.concatenate([expand_weight[:, quarter:], reduce_turned[:, quarter:]], axis=1),
        ]
    ).astype(LOW)
    zeros_pair = jnp.zeros((pairs, PAIR), WIDE)
    bias_row = jnp.concatenate(
        [
            own(vectors[0], width_half).reshape(pairs, PAIR),
            zeros_pair,
            own(vectors[1], width_half).reshape(pairs, PAIR),
        ],
        axis=1,
    ).reshape(pairs, 1, 3 * PAIR)
    whole = lax.all_gather(shards, "dp", axis=1, tiled=True)
    far = swap(whole)
    token_pair = jnp.concatenate([tokens, swap(tokens)], axis=0)
    upper_pair = jnp.concatenate([cotangent, swap(cotangent)], axis=0)
    hidden = dot_nn(pick_rows(own_first(own_of), total_rows), token_pair).astype(LOW)
    upstream = dot_nn(pick_rows(own_first(dealt_of), total_rows), upper_pair).astype(LOW)
    qkv = jnp.einsum(
        "rd,dpc->prc",
        hidden,
        whole[0, :, : 3 * width_half].reshape(model_width, pairs, 3 * PAIR),
        preferred_element_type=WIDE,
    )
    qkv = (qkv + bias_row).astype(LOW)
    context, *kept = attend(qkv, score_bias)

    (
        encoded, branch_grad, context_grad, merge_grad, expand_grad, reduce_grad, sums, hidden_part_own, hidden_part_far,
    ) = feed_block(
        context,
        whole,
        far,
        own(hidden, half_rows),
        upstream,
        vectors,
        own(hidden_bias, hidden_half),
        own(hidden_bias, hidden_half, other),
    )
    encoded_pair = jnp.concatenate([encoded, swap(encoded)], axis=0)
    encoded_out = dot_nn(
        pick_rows(own_first(own(from_dealt, half_rows)), total_rows), encoded_pair
    ).astype(LOW)
    mixed_grads = attend_back(qkv, context, context_grad, *kept)
    mixed_sums = jnp.sum(mixed_grads.astype(WIDE), axis=1).reshape(pairs, 3, PAIR)
    mixed_grads = mixed_grads.transpose(1, 0, 2).reshape(total_rows, 3 * width_half)
    project_grad = dot_tn(hidden, mixed_grads)
    input_terms = dot_nt(mixed_grads, whole[0, :, : 3 * width_half])
    own_part = own(input_terms, half_rows) + branch_grad
    input_terms = lax.dynamic_update_slice_in_dim(input_terms, own_part, own_begin, 0).astype(LOW)
    input_far = swap(
        dot_nn(pick_rows(own(from_own, half_rows, other), total_rows), input_terms).astype(LOW)
    )
    input_grad = (
        dot_nn(pick_rows(own(from_own, half_rows), total_rows), input_terms)
        + input_far.astype(WIDE)
    ).astype(LOW)
    zeros_width = jnp.zeros((model_width,), WIDE)
    zeros_hidden = jnp.zeros_like(hidden_bias)
    hidden_total = lax.dynamic_update_slice_in_dim(
        lax.dynamic_update_slice_in_dim(
            zeros_hidden, hidden_part_own, member * hidden_half, 0
        ),
        hidden_part_far,
        other * hidden_half,
        0,
    )
    vector_rows = [
        lax.dynamic_update_slice_in_dim(
            zeros_width, mixed_sums[:, c].reshape(-1), member * width_half, 0
        )
        for c in (0, 2)
    ]
    small = jnp.concatenate(
        [
            jnp.stack(vector_rows),
            sums[2:],
            hidden_total.reshape(-1, model_width),
            jnp.zeros((4, model_width), WIDE),
        ],
        axis=0,
    )
    grads = [
        lax.psum_scatter(g.astype(LOW), "dp", scatter_dimension=0, tiled=True).astype(WIDE)
        for g in (project_grad, merge_grad, expand_grad, reduce_grad)
    ]
    small = lax.psum(small, ("dp", "tensor"))
    project_shard, merge_shard, expand_shard, reduce_shard = grads
    project_shard = (
        project_shard.reshape(shard_rows, pairs, 3, PAIR)
        .transpose(2, 0, 1, 3)
        .reshape(3, shard_rows, width_half)
    )
    vector_grad = small[:8]
    hidden_grad = small[8:12].reshape(-1)
    return (
        encoded_out,
        input_grad,
        *adamw_update(
            project_weight, project_first, project_second, project_shard, rate_project, weight_decay
        ),
        *adamw_update(
            merge_weight, merge_first, merge_second, merge_shard.T, rate_merge, weight_decay
        ),
        *adamw_update(
            expand_weight, expand_first, expand_second, expand_shard, rate_expand, weight_decay
        ),
        *adamw_update(
            reduce_weight, reduce_first, reduce_second, reduce_shard.T, rate_reduce, weight_decay
        ),
        *adamw_update(vectors, vector_first, vector_second, vector_grad, rate_vectors, 0.0),
        *adamw_update(hidden_bias, hidden_first, hidden_second, hidden_grad, rate_hidden, 0.0),
        vector_grad,
    )


def solution(mesh):
    sharded = (
        P("dp", None),
        P("dp", None),
        *[P(None, "dp", "tensor")] * 3,
        *[P("tensor", "dp")] * 3,
        *[P("dp", "tensor")] * 3,
        *[P("tensor", "dp")] * 3,
        *[P()] * 6,
    )
    rows = P(("dp", "tensor"), None)
    return jax.shard_map(
        local,
        mesh=mesh,
        in_specs=(rows, rows, *sharded),
        out_specs=(rows, rows, *sharded[2:], P()),
        check_vma=False,
    )
```

```python
import functools

import jax
import jax.numpy as jnp
from jax import lax
from jax.experimental import pallas as pl
from jax.experimental.pallas import tpu as pltpu
from jax.sharding import PartitionSpec as P

HEAD_DIM = 64
LONGEST = 1024
STEP = 10
PAIR = 2 * HEAD_DIM
TILE = 256
MIB = 1024 * 1024
MESH = pl.DeviceIdType.MESH
LOW = jnp.bfloat16
WIDE = jnp.float32

beta_one = 0.9
beta_two = 0.999
adam_epsilon = 1e-08
weight_decay = 0.01
norm_epsilon = 1e-05
masked_score = -1e30
rate_project = 0.03
rate_merge = 0.3
rate_expand = 0.03
rate_reduce = 0.015
rate_vectors = 0.4
rate_hidden = 0.1


def dot_nn(a, b):
    return jnp.dot(a, b, preferred_element_type=WIDE)


def dot_nt(a, b):
    return lax.dot_general(a, b, (((1,), (1,)), ((), ())), preferred_element_type=WIDE)


def dot_tn(a, b):
    return lax.dot_general(a, b, (((0,), (0,)), ((), ())), preferred_element_type=WIDE)


def layout(lengths_row, dealing_row, total_rows):
    slots = jnp.arange(lengths_row.shape[0], dtype=jnp.int32)
    places = jnp.arange(total_rows, dtype=jnp.int32)
    rank_of = jnp.sum(jnp.where(dealing_row[None, :] == slots[:, None], slots[None, :], 0), axis=1)
    own_start = jnp.cumsum(lengths_row) - lengths_row
    dealt_start = jnp.sum(
        jnp.where(rank_of[None, :] < rank_of[:, None], lengths_row[None, :], 0), axis=1
    )
    longest = lengths_row == LONGEST
    short = jnp.where(longest, 0, lengths_row)
    start = jnp.where(longest, 0, LONGEST + jnp.cumsum(short) - short)

    def inside(begin):
        return (places[:, None] >= begin[None, :]) & (
            places[:, None] < (begin + lengths_row)[None, :]
        )

    def moved(begin, end):
        return places + jnp.sum(jnp.where(inside(begin), (end - begin)[None, :], 0), axis=1)

    segment = jnp.sum(jnp.where(inside(start), slots[None, :], 0), axis=1)
    return (
        segment,
        moved(start, own_start),
        moved(start, dealt_start),
        moved(own_start, start),
        moved(dealt_start, start),
    )


def pick_rows(index, rows):
    places = jnp.arange(rows, dtype=jnp.int32)
    return (index[:, None] == places[None, :]).astype(LOW)


class Group:
    def __init__(self, lengths_ref, dealing_ref):
        count = lengths_ref.shape[1]
        self.lengths = [lengths_ref[0, s] for s in range(count)]
        order = [dealing_ref[0, i] for i in range(count)]
        rank = [sum(jnp.where(order[i] == s, i, 0) for i in range(count)) for s in range(count)]
        short = [jnp.where(length == LONGEST, 0, length) for length in self.lengths]
        self.own, self.dealt, self.first = [], [], []
        own = own_short = jnp.int32(0)
        for s in range(count):
            self.own.append(own)
            self.first.append(jnp.where(self.lengths[s] == LONGEST, 0, LONGEST + own_short))
            self.dealt.append(
                sum(jnp.where(rank[j] < rank[s], self.lengths[j], 0) for j in range(count))
            )
            own, own_short = own + self.lengths[s], own_short + short[s]

    def inside(self, places, begin, s):
        return (places >= begin[s]) & (places < begin[s] + self.lengths[s])

    def moved(self, places, begin, end):
        total = places
        for s in range(len(begin)):
            total = total + jnp.where(self.inside(places, begin, s), end[s] - begin[s], 0)
        return total

    def score_bias(self, count):
        sides = []
        for shape, axis in (((count, 1), 0), ((1, count), 1)):
            places = lax.broadcasted_iota(jnp.int32, shape, axis) + LONGEST
            segment = jnp.zeros_like(places)
            for s in range(len(self.first)):
                segment = segment + jnp.where(self.inside(places, self.first, s), s, 0)
            sides.append(segment)
        return jnp.where(sides[0] == sides[1], 0.0, masked_score).astype(WIDE)


def picked_rows(index, source):
    places = lax.broadcasted_iota(jnp.int32, (index.shape[0], source.shape[0]), 1)
    return dot_nn(jnp.where(index == places, 1.0, 0.0).astype(LOW), source[...])


def attend_tile(qkv_ref, pair, bias_ref, begin, size, step, context_ref, columns, total_ref):
    lane = lax.broadcasted_iota(jnp.int32, (1, PAIR), 1)
    scale = HEAD_DIM ** (-0.5)
    first = pl.multiple_of(begin + step * TILE, TILE)
    query = qkv_ref[pair, pl.ds(first, TILE), 0:PAIR]
    key = qkv_ref[pair, begin : begin + size, PAIR : 2 * PAIR]
    value = qkv_ref[pair, begin : begin + size, 2 * PAIR : 3 * PAIR]
    outcome = []
    for head in range(2):
        chosen = jnp.where(lane // HEAD_DIM == head, scale, 0.0).astype(LOW)
        scores = dot_nt(query * chosen, key)
        if begin:
            inner = pl.multiple_of(step * TILE, TILE)
            scores = scores + bias_ref[pl.ds(inner, TILE), :]
        top = jnp.max(scores, axis=1, keepdims=True)
        exponent = jnp.exp(scores - top)
        total = jnp.sum(exponent, axis=1, keepdims=True)
        outcome.append(dot_nn(exponent.astype(LOW), value) / total)
        log_total = jnp.broadcast_to(top + jnp.log(total), (TILE, PAIR))
        total_ref[pair, head : head + 1, pl.ds(first, TILE)] = log_total.T[0:1, :]
    context_ref[pl.ds(first, TILE), columns] = jnp.where(
        lane < HEAD_DIM, outcome[0], outcome[1]
    ).astype(LOW)


def attend_kernel(qkv_ref, bias_ref, context_ref, total_ref):
    rows = qkv_ref.shape[1]
    for begin, size in ((0, LONGEST), (LONGEST, rows - LONGEST)):

        @pl.loop(0, size // TILE)
        def _(step):
            attend_tile(
                qkv_ref, 0, bias_ref, begin, size, step, context_ref, slice(0, PAIR), total_ref
            )


def attend(qkv, bias):
    pairs, rows, width = qkv.shape
    return pl.pallas_call(
        attend_kernel,
        grid=(pairs,),
        in_specs=[
            pl.BlockSpec((1, rows, width), lambda p: (p, 0, 0)),
            pl.BlockSpec(bias.shape, lambda p: (0, 0)),
        ],
        out_specs=[
            pl.BlockSpec((rows, PAIR), lambda p: (0, p)),
            pl.BlockSpec((1, 8, rows), lambda p: (p, 0, 0)),
        ],
        out_shape=[
            jax.ShapeDtypeStruct((rows, pairs * PAIR), LOW),
            jax.ShapeDtypeStruct((pairs, 8, rows), WIDE),
        ],
        compiler_params=pltpu.CompilerParams(vmem_limit_bytes=48 * MIB),
    )(qkv, bias)


def attend_back_open(qkv_ref, context_ref, upper_ref, dots, key_turned, queries, uppers):
    lane = lax.broadcasted_iota(jnp.int32, (1, PAIR), 1)
    product = (upper_ref[...].astype(WIDE) * context_ref[...].astype(WIDE)).T
    for head in range(2):
        band = slice(head * HEAD_DIM, (head + 1) * HEAD_DIM)
        dots[head : head + 1, :] = jnp.sum(product[band, :], axis=0, keepdims=True)
        chosen = lane // HEAD_DIM == head
        queries[head] = qkv_ref[:, 0:PAIR] * jnp.where(chosen, HEAD_DIM ** (-0.5), 0.0).astype(LOW)
        uppers[head] = upper_ref[...] * jnp.where(chosen, 1.0, 0.0).astype(LOW)
    key_turned[...] = qkv_ref[:, PAIR : 2 * PAIR].astype(WIDE).T.astype(LOW)


def attend_back_tile(
    qkv_ref, bias_ref, total_ref, dots, key_turned, queries, uppers, query_sum, begin, size, step
):
    block = slice(begin, begin + size)
    first = pl.multiple_of(begin + step * TILE, TILE)
    key = qkv_ref[pl.ds(first, TILE), PAIR : 2 * PAIR]
    value = qkv_ref[pl.ds(first, TILE), 2 * PAIR : 3 * PAIR]
    key_sum = jnp.zeros((TILE, PAIR), WIDE)
    value_sum = jnp.zeros((TILE, PAIR), WIDE)
    scores = [dot_nt(key, queries[head, block, :]) for head in range(2)]
    weight_grads = [dot_nt(value, uppers[head, block, :]) for head in range(2)]
    for head in range(2):
        band = slice(head * HEAD_DIM, (head + 1) * HEAD_DIM)
        score = scores[head]
        if begin:
            inner = pl.multiple_of(step * TILE, TILE)
            score = score + bias_ref[pl.ds(inner, TILE), :]
        probability = jnp.exp(score - total_ref[head : head + 1, block])
        score_grads = probability * (weight_grads[head] - dots[head : head + 1, block])
        score_grads = score_grads.astype(LOW)
        value_sum = value_sum + dot_nn(probability.astype(LOW), uppers[head, block, :])
        key_sum = key_sum + dot_nn(score_grads, queries[head, block, :])
        query_sum[band, block] += dot_nn(key_turned[band, pl.ds(first, TILE)], score_grads)
    return pl.ds(first, TILE), key_sum, value_sum


def attend_back_kernel(
    qkv_ref, bias_ref, context_ref, grad_ref, total_ref, out_ref, dots, key_turned, queries, uppers, query_sum
):
    rows = qkv_ref.shape[1]
    qkv = qkv_ref.at[0]
    attend_back_open(qkv, context_ref, grad_ref, dots, key_turned, queries, uppers)
    for begin, size in ((0, LONGEST), (LONGEST, rows - LONGEST)):
        block = slice(begin, begin + size)
        query_sum[:, block] = jnp.zeros((PAIR, size), WIDE)

        @pl.loop(0, size // TILE)
        def _(step):
            at, key_sum, value_sum = attend_back_tile(
                qkv, bias_ref, total_ref.at[0], dots, key_turned, queries, uppers, query_sum, begin, size, step
            )
            out_ref[0, at, PAIR : 2 * PAIR] = key_sum.astype(LOW)
            out_ref[0, at, 2 * PAIR : 3 * PAIR] = value_sum.astype(LOW)

        out_ref[0, block, 0:PAIR] = (query_sum[:, block] * HEAD_DIM ** (-0.5)).T.astype(LOW)


def attend_back(qkv, bias, context, grad, totals):
    pairs, rows, width = qkv.shape
    return pl.pallas_call(
        attend_back_kernel,
        grid=(pairs,),
        in_specs=[
            pl.BlockSpec((1, rows, width), lambda p: (p, 0, 0)),
            pl.BlockSpec(bias.shape, lambda p: (0, 0)),
            pl.BlockSpec((rows, PAIR), lambda p: (0, p)),
            pl.BlockSpec((rows, PAIR), lambda p: (0, p)),
            pl.BlockSpec((1, 8, rows), lambda p: (p, 0, 0)),
        ],
        out_specs=pl.BlockSpec((1, rows, width), lambda p: (p, 0, 0)),
        out_shape=jax.ShapeDtypeStruct(qkv.shape, LOW),
        scratch_shapes=[
            pltpu.VMEM((8, rows), WIDE),
            pltpu.VMEM((PAIR, rows), LOW),
            pltpu.VMEM((2, rows, PAIR), LOW),
            pltpu.VMEM((2, rows, PAIR), LOW),
            pltpu.VMEM((PAIR, rows), WIDE),
        ],
        compiler_params=pltpu.CompilerParams(vmem_limit_bytes=48 * MIB),
    )(qkv, bias, context, grad, totals)


def place():
    me = lax.axis_index("dp")
    z, y, x = me // 4, (me // 2) % 2, me % 2
    return me, z, y, x


def line_slots(z, depth):
    slots = []
    for step in range(depth - 1):
        slots.append((z - 1 - step, z - 1 - step >= 0, 1))
        slots.append((z + 1 + step, z + 1 + step < depth, -1))
    return slots


def remote(source, target, send, receive, device):
    return pltpu.make_async_remote_copy(
        src_ref=source,
        dst_ref=target,
        send_sem=send,
        recv_sem=receive,
        device_id={"dp": device},
        device_id_type=MESH,
    )


def greet_line(me, z, y, x, depth, extra=()):
    barrier = pltpu.get_barrier_semaphore()
    for peer in (z * 4 + y * 2 + 1 - x, z * 4 + (1 - y) * 2 + x):
        pl.semaphore_signal(barrier, inc=1, device_id={"dp": peer}, device_id_type=MESH)

    @pl.when(z > 0)
    def _():
        pl.semaphore_signal(barrier, inc=1, device_id={"dp": me - 4}, device_id_type=MESH)

    @pl.when(z < depth - 1)
    def _():
        pl.semaphore_signal(barrier, inc=1, device_id={"dp": me + 4}, device_id_type=MESH)

    for peer in extra:
        pl.semaphore_signal(barrier, inc=1, device_id=peer, device_id_type=MESH)
    ends = jnp.where(z > 0, 1, 0) + jnp.where(z < depth - 1, 1, 0)
    pl.semaphore_wait(barrier, 2 + len(extra) + ends)


def other_core(source, target, send, receive):
    return pltpu.make_async_remote_copy(
        src_ref=source,
        dst_ref=target,
        send_sem=send,
        recv_sem=receive,
        device_id={"tensor": 1 - lax.axis_index("tensor")},
        device_id_type=MESH,
    )


class Gather:
    def __init__(self, depth, parts, whole, far, sems):
        self.whole, self.far = whole, far
        self.depth = depth
        self.me, self.z, self.y, self.x = place()
        self.x_peer = self.z * 4 + self.y * 2 + 1 - self.x
        self.y_peer = self.z * 4 + (1 - self.y) * 2 + self.x
        self.rows = whole.shape[1] // parts
        width = whole.shape[2]
        self.third = width // 4
        side = (width - self.third) // 2
        self.a, self.b = (0, side), (side, side)
        self.ab, self.c, self.all = (0, 2 * side), (2 * side, self.third), (0, width)
        (
            self.z_send, self.z_recv, self.zc_send, self.zc_recv, self.xa_send, self.xa_recv, self.yb_send, self.yb_recv,
            self.ya_send, self.ya_recv, self.xb_send, self.xb_recv, self.c_send, self.c_recv, self.far_send, self.far_recv,
        ) = sems
        self.slots = line_slots(self.z, depth)

    @staticmethod
    def semaphores(depth, pieces):
        sem = pltpu.SemaphoreType.DMA
        return [
            *[sem((pieces, depth + 1)), sem((pieces, depth))] * 2,
            *[sem((pieces, depth))] * 4,
            *[sem((pieces, depth, 2))] * 4,
            sem((pieces, 2)),
            sem((pieces, 2)),
            sem((pieces,)),
            sem((pieces,)),
        ]

    def block(self, zb, yb, xb):
        return zb * 4 + yb * 2 + xb

    def cut(self, ref, p, block, count, columns):
        first = pl.multiple_of(block * self.rows, self.rows)
        return ref.at[p, pl.ds(first, count * self.rows), pl.ds(*columns)]

    def copy(self, p, block, count, columns, send, receive, device):
        part = self.cut(self.whole, p, block, count, columns)
        return remote(part, part, send, receive, device)

    def forward(self, p, block, count, columns):
        if p == 0 and columns[0] + columns[1] <= self.c[0]:
            return
        if p == 0:
            columns = self.c
        other_core(
            self.cut(self.whole, p, block, count, columns),
            self.cut(self.far, p, block, count, columns),
            self.far_send.at[p],
            self.far_recv.at[p],
        ).start()

    def far_copy(self, p):
        columns = self.c if p == 0 else self.all
        part = self.far.at[p, :, pl.ds(*columns)]
        return other_core(part, part, self.far_send.at[p], self.far_recv.at[p])

    def z_copy(self, p, zb, way, back=False):
        block = self.block(zb, self.y, self.x)
        sem = self.depth if back else zb
        return self.copy(
            p, block, 1, self.ab, self.z_send.at[p, sem], self.z_recv.at[p, zb], self.me + 4 * way
        )

    def zc_copy(self, p, zb, way, back=False):
        sem = self.depth if back else zb
        return self.copy(
            p, zb * 4, 4, self.c, self.zc_send.at[p, sem], self.zc_recv.at[p, zb], self.me + 4 * way
        )

    def xa(self, p, zb, xb):
        block = self.block(zb, self.y, xb)
        return self.copy(
            p, block, 1, self.a, self.xa_send.at[p, zb], self.xa_recv.at[p, zb], self.x_peer
        )

    def yb(self, p, zb, yb):
        block = self.block(zb, yb, self.x)
        return self.copy(
            p, block, 1, self.b, self.yb_send.at[p, zb], self.yb_recv.at[p, zb], self.y_peer
        )

    def ya(self, p, zb, yb, xb):
        block = self.block(zb, yb, xb)
        return self.copy(
            p, block, 1, self.a, self.ya_send.at[p, zb, xb], self.ya_recv.at[p, zb, xb], self.y_peer
        )

    def xb(self, p, zb, yb, xb):
        block = self.block(zb, yb, xb)
        return self.copy(
            p, block, 1, self.b, self.xb_send.at[p, zb, yb], self.xb_recv.at[p, zb, yb], self.x_peer
        )

    def xc(self, p, xb):
        block = self.block(self.z, self.y, xb)
        return self.copy(
            p, block, 1, self.c, self.c_send.at[p, 0], self.c_recv.at[p, 0], self.x_peer
        )

    def yc(self, p, yb):
        block = self.block(self.z, yb, 0)
        return self.copy(
            p, block, 2, self.c, self.c_send.at[p, 1], self.c_recv.at[p, 1], self.y_peer
        )

    def both_ways(self, copy, act):
        @pl.when(self.z < self.depth - 1)
        def _():
            act(copy(self.z, 1))

        @pl.when(self.z > 0)
        def _():
            act(copy(self.z, -1, True))

    def spread(self, p, zb):
        self.xa(p, zb, self.x).start()
        self.yb(p, zb, self.y).start()
        self.ya(p, zb, self.y, self.x).start()
        self.xb(p, zb, self.y, self.x).start()

    def turn(self, p, zb):
        self.xa(p, zb, 1 - self.x).wait_recv()
        self.ya(p, zb, self.y, 1 - self.x).start()
        self.forward(p, self.block(zb, self.y, 1 - self.x), 1, self.a)
        self.yb(p, zb, 1 - self.y).wait_recv()
        self.xb(p, zb, 1 - self.y, self.x).start()
        self.forward(p, self.block(zb, 1 - self.y, self.x), 1, self.b)

    def at_step(self, step, act):
        for zb, valid, way in self.slots[2 * step : 2 * step + 2]:
            on = (self.z + way >= 0) & (self.z + way < self.depth)
            pl.when(valid)(functools.partial(act, zb, way, on))

    def arrive(self, p, step):
        def act(zb, way, on):
            self.z_copy(p, zb, way).wait_recv()
            pl.when(on)(lambda: self.z_copy(p, zb, way).start())
            self.spread(p, zb)
            self.forward(p, self.block(zb, self.y, self.x), 1, self.ab)

        self.at_step(step, act)

    def arrive_c(self, p, step):
        def act(zb, way, on):
            self.zc_copy(p, zb, way).wait_recv()
            pl.when(on)(lambda: self.zc_copy(p, zb, way).start())
            self.forward(p, zb * 4, 4, self.c)

        self.at_step(step, act)

    def stage(self, p, s):
        depth = self.depth
        if s == 0:
            self.both_ways(lambda *way: self.z_copy(p, *way), lambda copy: copy.start())
            self.xc(p, self.x).start()
            self.spread(p, self.z)
            self.forward(p, self.me, 1, self.all)
            return
        if s == 1:
            self.xc(p, 1 - self.x).wait_recv()
            self.yc(p, self.y).start()
            self.forward(p, self.block(self.z, self.y, 1 - self.x), 1, self.c)
        if s == 2:
            self.yc(p, 1 - self.y).wait_recv()
            self.both_ways(lambda *way: self.zc_copy(p, *way), lambda copy: copy.start())
            self.forward(p, self.block(self.z, 1 - self.y, 0), 2, self.c)
        if 1 <= s < depth:
            self.arrive(p, s - 1)
        if 3 <= s < depth + 2:
            self.arrive_c(p, s - 3)
        if s == 2:
            self.turn(p, self.z)
        if 3 <= s < depth + 2:
            self.at_step(s - 3, lambda zb, way, on: self.turn(p, zb))
        if s == depth + 2:
            for zb in range(depth):
                for other in range(2):
                    self.ya(p, zb, 1 - self.y, other).wait_recv()
                    self.forward(p, self.block(zb, 1 - self.y, other), 1, self.a)
                    self.xb(p, zb, other, 1 - self.x).wait_recv()
                    self.forward(p, self.block(zb, other, 1 - self.x), 1, self.b)

    def finish(self, p):
        def sent(copy):
            copy.wait_send()

        self.far_copy(p).wait_send()
        self.both_ways(lambda *way: self.z_copy(p, *way), sent)
        self.both_ways(lambda *way: self.zc_copy(p, *way), sent)
        for zb in range(self.depth):
            self.xa(p, zb, self.x).wait_send()
            self.yb(p, zb, self.y).wait_send()
            for other in range(2):
                self.ya(p, zb, self.y, other).wait_send()
                self.xb(p, zb, other, self.x).wait_send()
        self.xc(p, self.x).wait_send()
        self.yc(p, self.y).wait_send()

        def passed(zb, way, on):
            pl.when(on)(lambda: sent(self.z_copy(p, zb, way)))
            pl.when(on)(lambda: sent(self.zc_copy(p, zb, way)))

        for step in range(self.depth - 1):
            self.at_step(step, passed)


def looped(count, body, between):
    @pl.loop(0, count)
    def _(i):
        body(i)
        for step, acts in between.items():

            @pl.when(i == step)
            def _():
                for act in acts:
                    act()


GATHER_AT = {
    "hidden": {-1: [(0, 1)], 0: [(0, 2)], 3: [(0, 3), (0, 4)]},
    "upstream": {-1: [(1, 0)], 0: [(0, 5)], 1: [(2, 0)]},
    "project": {-1: [(0, 6)], 0: [(1, 1)]},
    "long": {-1: [(1, 2)], 2: [(2, 1)], 9: [(1, 3)], 11: [(2, 2)]},
    "short": {4: [(1, 4)]},
    "norm": {1: [(1, 5), (2, 3)]},
    "feed": {-1: [(1, 6)], 0: [(2, 4)], 1: [(2, 5)]},
    "last": {-1: [(2, 6)]},
}


def front_kernel(
    depth, lengths_ref, dealing_ref, project_ref, merge_ref, expand_ref, reduce_ref, vectors_ref, hidden_bias_ref,
    tokens_ref, cotangent_ref,
    whole_ref, far_ref, qkv_out, turned_out, upstream_out, context_out, total_out,
    acc_out, normal_out, inverse_out, low_turned_out, active_out, slope_out, far_context_out,
    shards, score_bias, token, upper, hidden, turned, upstream, weight, qkv, context, total,
    acc, normal, inverse, low, low_turned, active, slope, far_context, merge, merge_far, expand_buf, reduce_buf,
    local_sem, core_sem, out_sem, load_sem, chunk_sem, *sems,
):
    pieces = whole_ref.shape[0]
    half_rows, width = tokens_ref.shape
    rows = 2 * half_rows
    pairs = qkv.shape[0]
    inner = pairs * PAIR
    both = expand_buf.shape[2]
    half = both // 2
    hidden_half = expand_ref.shape[1]
    chunks = hidden_half // half
    per_piece = chunks // (pieces - 1)
    member = lax.axis_index("tensor")
    lines = Gather(depth, 4 * depth, whole_ref, far_ref, sems)
    me = lines.me
    tall, short = 2 * TILE, TILE // 2

    own = [
        pltpu.make_async_copy(
            shards.at[p], lines.cut(whole_ref, p, me, 1, lines.all), local_sem.at[p]
        )
        for p in range(pieces)
    ]
    own += [
        pltpu.make_async_copy(tokens_ref, token.at[member], local_sem.at[pieces]),
        pltpu.make_async_copy(cotangent_ref, upper.at[member], local_sem.at[pieces + 1]),
    ]
    for copy in own[pieces:]:
        copy.start()
    for pair in range(pairs):
        for c in range(3):
            first = (3 * pair + c) * PAIR
            shards[0, :, first : first + PAIR] = project_ref[
                c, :, pair * PAIR : (pair + 1) * PAIR
            ].astype(LOW)
    shards[0, :, 3 * inner :] = merge_ref[...].astype(LOW)
    quarter = hidden_half // (pieces - 1)
    for p in range(1, pieces):
        columns = slice((p - 1) * quarter, p * quarter)
        shards[p, :, 0:quarter] = expand_ref[:, columns].astype(LOW)
        shards[p, :, quarter:] = reduce_ref[:, columns].astype(LOW)
    for copy in own[:pieces]:
        copy.start()
    greet_line(me, lines.z, lines.y, lines.x, depth, [{"tensor": 1 - member}])
    crossing = [
        other_core(tokens_ref, token.at[member], core_sem.at[0, 0], core_sem.at[0, 1]),
        other_core(cotangent_ref, upper.at[member], core_sem.at[1, 0], core_sem.at[1, 1]),
    ]
    own[0].wait()
    lines.stage(0, 0)
    for copy in crossing:
        copy.start()
    group = Group(lengths_ref, dealing_ref)
    score_bias[...] = group.score_bias(rows - LONGEST)
    for copy in own[1:]:
        copy.wait()

    leaving = []

    def leave(source, target):
        copy = pltpu.make_async_copy(source, target, out_sem.at[len(leaving)])
        copy.start()
        leaving.append(copy)

    def phase(name, count, body):
        between = {
            step: [functools.partial(lines.stage, *stage) for stage in stages]
            for step, stages in GATHER_AT.get(name, {}).items()
        }
        for act in between.pop(-1, ()):
            act()
        looped(count, body, between)

    def places_of(first):
        return first + lax.broadcasted_iota(jnp.int32, (TILE, 1), 0)

    def picked(index, source):
        return picked_rows(index, source.at[0]) + picked_rows(index - half_rows, source.at[1])

    def tile(step, size=TILE):
        return pl.ds(pl.multiple_of(step * size, size), size)

    def hidden_tile(step):
        index = group.moved(places_of(step * TILE), group.first, group.own)
        rows_here = picked(index, token)
        hidden[tile(step), :] = rows_here.astype(LOW)
        turned[:, tile(step)] = rows_here.T.astype(LOW)

    def upstream_tile(step):
        places = places_of(member * half_rows + step * TILE)
        index = group.moved(places, group.first, group.dealt)
        upstream[tile(step), :] = picked(index, upper).astype(LOW)

    crossing[0].wait()
    phase("hidden", rows // TILE, hidden_tile)
    leave(turned, turned_out)
    crossing[1].wait()
    phase("upstream", half_rows // TILE, upstream_tile)
    leave(upstream, upstream_out)

    weight_copy = pltpu.make_async_copy(
        whole_ref.at[0, :, pl.ds(0, pairs * 3 * PAIR)], weight, local_sem.at[1]
    )

    def project_tile(i):
        @pl.when(i == 0)
        def _():
            weight_copy.start()
            weight_copy.wait()

        pair, step = i // (rows // tall), lax.rem(i, rows // tall)
        at = tile(step, tall)
        columns = pl.ds(pl.multiple_of(pair * 3 * PAIR, PAIR), 3 * PAIR)
        bias_columns = pl.ds(pl.multiple_of(member * inner + pair * PAIR, PAIR), PAIR)
        bias = jnp.concatenate(
            [
                vectors_ref[0:1, bias_columns],
                jnp.zeros((1, PAIR), WIDE),
                vectors_ref[1:2, bias_columns],
            ],
            axis=1,
        )
        qkv[pair, at, :] = (dot_nn(hidden[at, :], weight[:, columns]) + bias).astype(LOW)

    phase("project", pairs * rows // tall, project_tile)
    leave(qkv, qkv_out)

    def attend_step(begin, size):
        def step_of(i):
            pair, step = i // (size // TILE), lax.rem(i, size // TILE)
            columns = pl.ds(pl.multiple_of(pair * PAIR, PAIR), PAIR)
            attend_tile(qkv, pair, score_bias, begin, size, step, context, columns, total)

        return step_of

    phase("long", pairs * LONGEST // TILE, attend_step(0, LONGEST))
    phase("short", pairs * (rows - LONGEST) // TILE, attend_step(LONGEST, rows - LONGEST))
    leave(context, context_out)
    leave(total, total_out)

    own_first = member * half_rows
    other_rows = pl.ds(pl.multiple_of((1 - member) * half_rows, half_rows), half_rows)
    crossing = other_core(context.at[other_rows], far_context, core_sem.at[2, 0], core_sem.at[2, 1])
    crossing.start()
    lines.far_copy(0).wait_recv()
    merge_columns = pl.ds(whole_ref.shape[2] - inner, inner)
    fetches = [
        pltpu.make_async_copy(whole_ref.at[0, :, merge_columns], merge, local_sem.at[2]),
        pltpu.make_async_copy(far_ref.at[0, :, merge_columns], merge_far, local_sem.at[3]),
    ]
    for copy in fetches:
        copy.start()
    for copy in fetches:
        copy.wait()
    crossing.wait()
    leave(far_context, far_context_out)

    def norm_tile(step):
        at = tile(step, short)
        own_at = pl.ds(pl.multiple_of(own_first + step * short, short), short)
        branch = dot_nt(context[own_at, :], merge[...]) + dot_nt(far_context[at, :], merge_far[...])
        unit, scale = norm(hidden[own_at, :].astype(WIDE) + branch + vectors_ref[2:3, :])
        normed = unit * vectors_ref[3:4, :] + vectors_ref[4:5, :]
        normal[at, :] = unit
        inverse[at, :] = jnp.broadcast_to(scale, (short, 128))
        low[at, :] = normed.astype(LOW)
        low_turned[:, at] = normed.T.astype(LOW)
        acc[at, :] = normed + vectors_ref[5:6, :]

    phase("norm", half_rows // short, norm_tile)
    leave(normal, normal_out)
    leave(inverse, inverse_out)
    leave(low_turned, low_turned_out)

    def loads(j):
        slot, piece, at = lax.rem(j, 2), 1 + j // per_piece, lax.rem(j, per_piece) * half
        copies = []
        for kind, buf in enumerate((expand_buf, reduce_buf)):
            first = pl.multiple_of(at + kind * per_piece * half, half)
            for side, source in enumerate((far_ref, whole_ref)):
                copies.append(
                    pltpu.make_async_copy(
                        source.at[piece, :, pl.ds(first, half)],
                        buf.at[slot, :, pl.ds(side * half, half)],
                        load_sem.at[slot, kind, side],
                    )
                )
        return copies

    def results(j):
        slot = lax.rem(j, 2)
        return [
            pltpu.make_async_copy(active.at[slot], active_out.at[j], chunk_sem.at[slot, 0]),
            pltpu.make_async_copy(slope.at[slot], slope_out.at[j], chunk_sem.at[slot, 1]),
        ]

    def chunk_of(first_chunk):
        def chunk(i):
            j = first_chunk + i
            slot = lax.rem(j, 2)

            @pl.when(i == 0)
            def _():
                lines.far_copy(1 + first_chunk // per_piece).wait_recv()
                for copy in loads(j):
                    copy.start()

            for copy in loads(j):
                copy.wait()

            @pl.when(i + 1 < per_piece)
            def _():
                for copy in loads(j + 1):
                    copy.start()

            @pl.when(j >= 2)
            def _():
                for copy in results(j - 2):
                    copy.wait()

            biases = []
            for which in (1 - member, member):
                first = pl.multiple_of(which * hidden_half + j * half, half)
                biases.append(hidden_bias_ref[:, pl.ds(first, half)])
            bias = jnp.concatenate(biases, axis=1)
            for step in range(half_rows // TILE):
                at = slice(step * TILE, (step + 1) * TILE)
                value = dot_nn(low[at, :], expand_buf[slot]) + bias
                below, bell = normal_cells(value)
                held = (value * below).astype(LOW)
                active[slot, at, :] = held
                slope[slot, at, :] = (below + value * bell * 0.3989422804014327).astype(LOW)
                acc[at, :] += dot_nt(held, reduce_buf[slot])
            for copy in results(j):
                copy.start()

        return chunk

    phase("feed", per_piece, chunk_of(0))
    phase("last", per_piece, chunk_of(per_piece))
    leave(acc, acc_out)
    for p in range(pieces):
        lines.finish(p)
    for j in (chunks - 2, chunks - 1):
        for copy in results(j):
            copy.wait()
    for copy in leaving:
        copy.wait()


def front(lengths, dealing, project, merge, expand, reduce, vectors, hidden_bias, tokens, cotangent, parts):
    shard_rows, hidden_half = expand.shape
    pieces, columns = 3, hidden_half
    half_rows, width = tokens.shape
    rows, pairs, depth = 2 * half_rows, project.shape[2] // PAIR, parts // 4
    inner, half = pairs * PAIR, 256
    chunks, both = hidden_half // half, 2 * half
    shape, sem = jax.ShapeDtypeStruct, pltpu.SemaphoreType.DMA
    vmem, anywhere = pl.BlockSpec(memory_space=pltpu.VMEM), pl.BlockSpec(memory_space=pl.ANY)
    held = [
        ((pairs, rows, 3 * PAIR), LOW),
        ((width, rows), LOW),
        ((half_rows, width), LOW),
        ((rows, inner), LOW),
        ((pairs, 8, rows), WIDE),
        ((half_rows, width), WIDE),
        ((half_rows, width), WIDE),
        ((half_rows, 128), WIDE),
        ((width, half_rows), LOW),
        ((chunks, half_rows, both), LOW),
        ((chunks, half_rows, both), LOW),
        ((half_rows, inner), LOW),
    ]
    return pl.pallas_call(
        functools.partial(front_kernel, depth),
        in_specs=[*[pl.BlockSpec(memory_space=pltpu.SMEM)] * 2, *[vmem] * 6, *[anywhere] * 2],
        out_specs=[anywhere] * 14,
        out_shape=[
            shape((pieces, parts * shard_rows, columns), LOW),
            shape((pieces, parts * shard_rows, columns), LOW),
            *[shape(*one) for one in held],
        ],
        scratch_shapes=[
            pltpu.VMEM((pieces, shard_rows, columns), LOW),
            pltpu.VMEM((rows - LONGEST, rows - LONGEST), WIDE),
            pltpu.VMEM((2, half_rows, width), LOW),
            pltpu.VMEM((2, half_rows, width), LOW),
            pltpu.VMEM((rows, width), LOW),
            pltpu.VMEM((width, rows), LOW),
            pltpu.VMEM((half_rows, width), LOW),
            pltpu.VMEM((width, pairs * 3 * PAIR), LOW),
            pltpu.VMEM((pairs, rows, 3 * PAIR), LOW),
            pltpu.VMEM((rows, inner), LOW),
            pltpu.VMEM((pairs, 8, rows), WIDE),
            pltpu.VMEM((half_rows, width), WIDE),
            pltpu.VMEM((half_rows, width), WIDE),
            pltpu.VMEM((half_rows, 128), WIDE),
            pltpu.VMEM((half_rows, width), LOW),
            pltpu.VMEM((width, half_rows), LOW),
            pltpu.VMEM((2, half_rows, both), LOW),
            pltpu.VMEM((2, half_rows, both), LOW),
            pltpu.VMEM((half_rows, inner), LOW),
            pltpu.VMEM((width, inner), LOW),
            pltpu.VMEM((width, inner), LOW),
            pltpu.VMEM((2, width, both), LOW),
            pltpu.VMEM((2, width, both), LOW),
            sem((pieces + 2,)),
            sem((3, 2)),
            sem((10,)),
            sem((2, 2, 2)),
            sem((2, 2)),
            *Gather.semaphores(depth, pieces),
        ],
        compiler_params=pltpu.CompilerParams(
            collective_id=0, has_side_effects=True, vmem_limit_bytes=62 * MIB
        ),
    )(lengths, dealing, project, merge, expand, reduce, vectors, hidden_bias, tokens, cotangent)


def normal_cells(value):
    bell = jnp.exp2(value * value * (-0.5 * 1.4426950408889634))
    below = 1.0 + 0.39 * 0.7071067811865476 * jnp.abs(value)
    t = pl.reciprocal(below, approx=True)
    t = t * (2.0 - below * t)
    t = t * (2.0 - below * t)
    tail = 0.5 * -0.2275377237624147
    for factor in (
        0.8866668177122106,
        -0.6354042576077721,
        0.649562611731642,
        0.0913871257655044,
        0.23532542445435511,
    ):
        tail = tail * t + 0.5 * factor
    tail = tail * t * bell
    return jnp.where(value < 0.0, tail, 1.0 - tail), bell


def norm(values):
    center = values - jnp.mean(values, axis=1, keepdims=True)
    spread = jnp.mean(center * center, axis=1, keepdims=True)
    scale = lax.rsqrt(spread + norm_epsilon)
    return center * scale, scale


def norm_back(scaled, unit, scale):
    return scale * (
        scaled
        - jnp.mean(scaled, axis=1, keepdims=True)
        - unit * jnp.mean(scaled * unit, axis=1, keepdims=True)
    )


def feed_kernel(
    context_ref, merge_ref, merge_far_ref, whole_ref, far_ref, hidden_ref, upstream_ref, vectors_ref, bias_ref,
    encoded_ref, branch_ref, grad_ref, merge_grad_ref, expand_grad_ref, reduce_grad_ref, sums_ref, hidden_sums_ref,
    own_ctx, far_ctx, acc, normal, inverse, low, turned, late, late_turned, active, slope, inner_grad,
    expand_buf, reduce_buf, arrived, leaving, kept, done, grad_own, grad_far, merge_send, merge_recv,
    ctx_sem, load_sem, send_sem, recv_sem, out_sem, last_sem,
):
    rows = hidden_ref.shape[0]
    chunks, _, both = bias_ref.shape
    half = both // 2
    per_piece = whole_ref.shape[2] // (2 * half)
    member = lax.axis_index("tensor")
    peer = {"tensor": 1 - member}
    tall, short = 256, 128
    width = hidden_ref.shape[1]

    def across(source, target, send, receive):
        return pltpu.make_async_remote_copy(
            src_ref=source,
            dst_ref=target,
            send_sem=send,
            recv_sem=receive,
            device_id=peer,
            device_id_type=MESH,
        )

    def rows_of(which):
        return pl.ds(pl.multiple_of(which * rows, rows), rows)

    def tile(step, size):
        return pl.ds(pl.multiple_of(step * size, size), size)

    def loads(j, slot):
        piece, at = 1 + j // per_piece, lax.rem(j, per_piece) * half
        copies = []
        for kind, buf in enumerate((expand_buf, reduce_buf)):
            first = pl.multiple_of(at + kind * per_piece * half, half)
            for side, source in enumerate((far_ref, whole_ref)):
                copies.append(
                    pltpu.make_async_copy(
                        source.at[piece, :, pl.ds(first, half)],
                        buf.at[slot, :, pl.ds(side * half, half)],
                        load_sem.at[slot, kind, side],
                    )
                )
        return copies

    for copy in loads(0, 0):
        copy.start()
    barrier = pltpu.get_barrier_semaphore()
    pl.semaphore_signal(barrier, inc=1, device_id=peer, device_id_type=MESH)
    pl.semaphore_wait(barrier, 1)
    out_ctx = across(context_ref.at[rows_of(1 - member)], far_ctx, ctx_sem.at[0], ctx_sem.at[1])
    out_ctx.start()
    in_ctx = pltpu.make_async_copy(context_ref.at[rows_of(member)], own_ctx, ctx_sem.at[2])
    in_ctx.start()
    sums_ref[...] = jnp.zeros_like(sums_ref)
    in_ctx.wait()
    out_ctx.wait()

    def add_sum(row, values):
        sums_ref[row : row + 1, :] += jnp.sum(values, axis=0, keepdims=True)

    @pl.loop(0, rows // short)
    def _(step):
        at = tile(step, short)
        branch = dot_nt(own_ctx[at, :], merge_ref[...]) + dot_nt(far_ctx[at, :], merge_far_ref[...])
        unit, scale = norm(hidden_ref[at, :].astype(WIDE) + branch + vectors_ref[2:3, :])
        normed = unit * vectors_ref[3:4, :] + vectors_ref[4:5, :]
        normal[at, :] = unit
        inverse[at, :] = jnp.broadcast_to(scale, (short, 128))
        low[at, :] = normed.astype(LOW)
        turned[:, at] = normed.T.astype(LOW)
        acc[at, :] = normed + vectors_ref[5:6, :]

    @pl.loop(0, chunks)
    def _(j):
        slot = lax.rem(j, 2)
        for copy in loads(j, slot):
            copy.wait()

        @pl.when(j + 1 < chunks)
        def _():
            for copy in loads(j + 1, 1 - slot):
                copy.start()

        for step in range(rows // tall):
            at = slice(step * tall, (step + 1) * tall)
            inner = dot_nn(low[at, :], expand_buf[slot]) + bias_ref[j]
            below, bell = normal_cells(inner)
            held = (inner * below).astype(LOW)
            active[j, at, :] = held
            slope[j, at, :] = (below + inner * bell * 0.3989422804014327).astype(LOW)
            acc[at, :] += dot_nt(held, reduce_buf[slot])

    for copy in loads(0, 0):
        copy.start()

    @pl.loop(0, rows // short)
    def _(step):
        at = tile(step, short)
        unit, scale = norm(acc[at, :])
        encoded_ref[at, :] = (unit * vectors_ref[6:7, :] + vectors_ref[7:8, :]).astype(LOW)
        upper = upstream_ref[at, :].astype(WIDE)
        add_sum(6, upper * unit)
        add_sum(7, upper)
        grad = norm_back(upper * vectors_ref[6:7, :], unit, scale)
        grad_low = grad.astype(LOW)
        add_sum(5, grad_low.astype(WIDE))
        acc[at, :] = grad
        late[at, :] = grad_low
        late_turned[:, at] = grad.T.astype(LOW)

    def send(j, kind):
        return across(
            leaving.at[lax.rem(j, 2), kind],
            arrived.at[lax.rem(j, 4), kind],
            send_sem.at[lax.rem(j, 2), kind],
            recv_sem.at[lax.rem(j, 4), kind],
        )

    def store(j, kind):
        target = (expand_grad_ref, reduce_grad_ref)[kind]
        cols = pl.ds(pl.multiple_of(j * half, half), half)
        return pltpu.make_async_copy(
            done.at[lax.rem(j, 2), kind], target.at[:, cols], out_sem.at[lax.rem(j, 2), kind]
        )

    def finish(j):
        for kind in range(2):
            send(j, kind).wait_recv()

            @pl.when(j >= 2)
            def _():
                store(j - 2, kind).wait()

            @pl.loop(0, width // tall)
            def _(step):
                at = tile(step, tall)
                done[lax.rem(j, 2), kind, at, :] = (
                    kept[lax.rem(j, 2), kind, at, :]
                    + arrived[lax.rem(j, 4), kind, at, :].astype(WIDE)
                ).astype(LOW)

            store(j, kind).start()

    @pl.loop(0, chunks)
    def _(j):
        slot = lax.rem(j, 2)
        for copy in loads(j, slot):
            copy.wait()

        @pl.when(j + 1 < chunks)
        def _():
            for copy in loads(j + 1, 1 - slot):
                copy.start()

        total = jnp.zeros((1, both), WIDE)
        for step in range(rows // tall):
            at = slice(step * tall, (step + 1) * tall)
            grad = dot_nn(late[at, :], reduce_buf[slot]) * slope[j, at, :].astype(WIDE)
            grad = grad.astype(LOW)
            inner_grad[at, :] = grad
            total = total + jnp.sum(grad.astype(WIDE), axis=0, keepdims=True)
            acc[at, :] += dot_nt(grad, expand_buf[slot])
        hidden_sums_ref[j] = total

        @pl.when(j >= 2)
        def _():
            for kind in range(2):
                send(j - 2, kind).wait_send()

        for kind, (left, right) in enumerate(((turned, inner_grad), (late_turned, active.at[j]))):
            for step in range(width // tall):
                at = slice(step * tall, (step + 1) * tall)
                part = dot_nn(left[at, :], right[...])
                leaving[slot, kind, at, :] = part[:, 0:half].astype(LOW)
                kept[slot, kind, at, :] = part[:, half:both]
            send(j, kind).start()

        @pl.when(j >= 1)
        def _():
            finish(j - 1)

    @pl.loop(0, rows // short)
    def _(step):
        at = tile(step, short)
        grad = acc[at, :]
        unit = normal[at, :]
        add_sum(3, grad * unit)
        add_sum(4, grad)
        branch_grad = norm_back(grad * vectors_ref[3:4, :], unit, inverse[at, 0:1])
        branch_low = branch_grad.astype(LOW)
        add_sum(2, branch_low.astype(WIDE))
        branch_ref[at, :] = branch_grad
        turned[:, at] = branch_grad.T.astype(LOW)
        grad_far[at, :] = dot_nn(branch_low, merge_far_ref[...]).astype(LOW)
        grad_own[at, :] = dot_nn(branch_low, merge_ref[...]).astype(LOW)

    out_grad = across(grad_far, grad_ref.at[rows_of(member)], ctx_sem.at[0], ctx_sem.at[1])
    out_grad.start()
    in_grad = pltpu.make_async_copy(grad_own, grad_ref.at[rows_of(member)], ctx_sem.at[2])
    in_grad.start()
    for step in range(width // tall):
        at = slice(step * tall, (step + 1) * tall)
        merge_send[at, :] = dot_nn(turned[at, :], far_ctx[...]).astype(LOW)
    out_merge = across(merge_send, merge_recv, last_sem.at[0], last_sem.at[1])
    out_merge.start()
    finish(chunks - 1)
    for kind in range(2):
        send(chunks - 2, kind).wait_send()
        send(chunks - 1, kind).wait_send()
        store(chunks - 2, kind).wait()
        store(chunks - 1, kind).wait()
    out_merge.wait()
    for step in range(width // tall):
        at = slice(step * tall, (step + 1) * tall)
        merge_grad_ref[at, :] = (
            dot_nn(turned[at, :], own_ctx[...]) + merge_recv[at, :].astype(WIDE)
        ).astype(LOW)
    out_grad.wait()
    in_grad.wait()


def feed_block(context, whole, far, hidden_own, upstream, vectors, bias_own, bias_far):
    total_rows, inner = context.shape
    rows, width = hidden_own.shape
    hidden = bias_own.shape[0]
    merge, merge_far = whole[0, :, -inner:], far[0, :, -inner:]
    half = 256
    chunks = hidden // half
    both = 2 * half
    bias = jnp.concatenate(
        [bias_far.reshape(chunks, 1, half), bias_own.reshape(chunks, 1, half)], axis=2
    )
    vmem, anywhere = pl.BlockSpec(memory_space=pltpu.VMEM), pl.BlockSpec(memory_space=pl.ANY)
    sem = pltpu.SemaphoreType.DMA
    shape = jax.ShapeDtypeStruct
    *results, hidden_sums = pl.pallas_call(
        feed_kernel,
        in_specs=[anywhere, vmem, vmem, *[anywhere] * 2, *[vmem] * 4],
        out_specs=[vmem, vmem, anywhere, vmem, anywhere, anywhere, vmem, vmem],
        out_shape=[
            shape((rows, width), LOW),
            shape((rows, width), WIDE),
            shape((total_rows, inner), LOW),
            shape((width, inner), LOW),
            shape((width, hidden), LOW),
            shape((width, hidden), LOW),
            shape((8, width), WIDE),
            shape((chunks, 1, both), WIDE),
        ],
        scratch_shapes=[
            pltpu.VMEM((rows, inner), LOW),
            pltpu.VMEM((rows, inner), LOW),
            pltpu.VMEM((rows, width), WIDE),
            pltpu.VMEM((rows, width), WIDE),
            pltpu.VMEM((rows, 128), WIDE),
            pltpu.VMEM((rows, width), LOW),
            pltpu.VMEM((width, rows), LOW),
            pltpu.VMEM((rows, width), LOW),
            pltpu.VMEM((width, rows), LOW),
            pltpu.VMEM((chunks, rows, both), LOW),
            pltpu.VMEM((chunks, rows, both), LOW),
            pltpu.VMEM((rows, both), LOW),
            pltpu.VMEM((2, width, both), LOW),
            pltpu.VMEM((2, width, both), LOW),
            pltpu.VMEM((4, 2, width, half), LOW),
            pltpu.VMEM((2, 2, width, half), LOW),
            pltpu.VMEM((2, 2, width, half), WIDE),
            pltpu.VMEM((2, 2, width, half), LOW),
            pltpu.VMEM((rows, inner), LOW),
            pltpu.VMEM((rows, inner), LOW),
            pltpu.VMEM((width, inner), LOW),
            pltpu.VMEM((width, inner), LOW),
            sem((3,)),
            sem((2, 2, 2)),
            sem((2, 2)),
            sem((4, 2)),
            sem((2, 2)),
            sem((2,)),
        ],
        compiler_params=pltpu.CompilerParams(
            collective_id=2, has_side_effects=True, vmem_limit_bytes=60 * MIB
        ),
        cost_estimate=pl.CostEstimate(
            flops=12 * rows * width * 2 * hidden, bytes_accessed=8 * width * hidden * 4, transcendentals=0
        ),
    )(context, merge, merge_far, whole, far, hidden_own, upstream, vectors, bias)
    hidden_far = hidden_sums[:, 0, :half].reshape(-1)
    hidden_near = hidden_sums[:, 0, half:].reshape(-1)
    return (*results, hidden_near, hidden_far)


class Scatter:
    buffers = 8

    def __init__(self, depth, grads, shards, buffers, sems):
        self.depth, self.grads, self.shards = depth, grads, shards
        self.held = [buffers[8 * p : 8 * p + 8] for p in range(len(grads))]
        self.me, self.z, self.y, self.x = place()
        self.x_peer = self.z * 4 + self.y * 2 + 1 - self.x
        self.y_peer = self.z * 4 + (1 - self.y) * 2 + self.x
        self.rows = grads[0].shape[0] // (4 * depth)
        (
            self.a1_send, self.a1_recv, self.a2_send, self.a2_recv, self.b2_send, self.b2_recv, self.b1_send, self.b1_recv,
            self.z_send, self.z_recv, self.zc_send, self.zc_recv, self.c_send, self.c_recv,
        ) = sems

    @staticmethod
    def scratch(depth, rows, classes):
        found = []
        for a, b, c in classes:
            found += [
                pltpu.VMEM((depth, 2 * rows, a), LOW),
                pltpu.VMEM((depth, 2, rows, b), LOW),
                pltpu.VMEM((depth, rows, a), LOW),
                pltpu.VMEM((depth, rows, b), LOW),
                pltpu.VMEM((depth + 1, rows, a + b), LOW),
                pltpu.VMEM((depth + 1, 4 * rows, c), LOW),
                pltpu.VMEM((2 * rows, c), LOW),
                pltpu.VMEM((rows, c), LOW),
            ]
        return found

    @staticmethod
    def semaphores(depth, pieces):
        sem = pltpu.SemaphoreType.DMA
        return [
            *[sem((pieces, depth))] * 6,
            *[sem((pieces, depth, 2))] * 2,
            *[sem((pieces, depth)), sem((pieces, depth + 1))] * 2,
            sem((pieces, 2)),
            sem((pieces, 2)),
        ]

    def columns(self, p):
        a, b, c = (self.held[p][i].shape[-1] for i in (0, 1, 5))
        return pl.ds(0, a), pl.ds(a, b), pl.ds(a + b, c)

    def block(self, zb, yb, xb):
        return zb * 4 + yb * 2 + xb

    def span(self, block, count=1):
        return pl.ds(pl.multiple_of(block * self.rows, self.rows), count * self.rows)

    def add(self, put, count, *terms):
        chunk = min(count, 64)

        @pl.loop(0, count // chunk)
        def _(step):
            at = pl.multiple_of(step * chunk, chunk)
            parts = [term(at, chunk) for term in terms]
            if len(parts) > 2 or put.wide:
                parts = [part.astype(WIDE) for part in parts]
            total = parts[0]
            for part in parts[1:]:
                total = total + part
            put(at, chunk, total)

    def a1(self, p, zb):
        return remote(
            self.grads[p].at[self.span(self.block(zb, 1 - self.y, 0), 2), self.columns(p)[0]],
            self.held[p][0].at[zb],
            self.a1_send.at[p, zb],
            self.a1_recv.at[p, zb],
            self.y_peer,
        )

    def b1(self, p, zb, yb):
        return remote(
            self.grads[p].at[self.span(self.block(zb, yb, 1 - self.x)), self.columns(p)[1]],
            self.held[p][1].at[zb, yb],
            self.b1_send.at[p, zb, yb],
            self.b1_recv.at[p, zb, yb],
            self.x_peer,
        )

    def a2(self, p, zb):
        return remote(
            self.held[p][0].at[zb, self.span(1 - self.x)],
            self.held[p][2].at[zb],
            self.a2_send.at[p, zb],
            self.a2_recv.at[p, zb],
            self.x_peer,
        )

    def b2(self, p, zb):
        return remote(
            self.held[p][1].at[zb, 1 - self.y],
            self.held[p][3].at[zb],
            self.b2_send.at[p, zb],
            self.b2_recv.at[p, zb],
            self.y_peer,
        )

    def slot(self, zb, way):
        return zb if way > 0 else zb + (self.depth - zb) * jnp.where(zb == self.z - 1, 1, 0)

    def z_copy(self, p, zb, way):
        slot = self.slot(zb, way)
        return remote(
            self.held[p][4].at[zb],
            self.held[p][4].at[slot],
            self.z_send.at[p, zb],
            self.z_recv.at[p, slot],
            self.me + 4 * way,
        )

    def zc_copy(self, p, zb, way, first):
        slot = self.slot(zb, way)
        source = self.held[p][5].at[zb]
        if first:
            source = self.grads[p].at[self.span(zb * 4, 4), self.columns(p)[2]]
        return remote(
            source,
            self.held[p][5].at[slot],
            self.zc_send.at[p, zb],
            self.zc_recv.at[p, slot],
            self.me + 4 * way,
        )

    def arrived(self, ref, sem, slot):
        part = ref.at[slot]
        remote(part, part, sem, sem, self.me).wait_recv()

    def cy(self, p):
        return remote(
            self.held[p][5].at[self.z, self.span(2 * (1 - self.y), 2)],
            self.held[p][6],
            self.c_send.at[p, 0],
            self.c_recv.at[p, 0],
            self.y_peer,
        )

    def cx(self, p):
        return remote(
            self.held[p][5].at[self.z, self.span(2 * self.y + 1 - self.x)],
            self.held[p][7],
            self.c_send.at[p, 1],
            self.c_recv.at[p, 1],
            self.x_peer,
        )

    def grad(self, p, block, columns):
        def term(at, count):
            first = pl.multiple_of(block * self.rows + at, 16)
            return self.grads[p][pl.ds(first, count), columns]

        return term

    def part(self, ref, lead, block, columns=None):
        columns = slice(None) if columns is None else columns

        def term(at, count):
            first = pl.multiple_of(block * self.rows + at, 16)
            return ref[(*lead, pl.ds(first, count), columns)]

        return term

    def put(self, ref, lead, block, columns=None):
        columns = slice(None) if columns is None else columns

        def act(at, count, total):
            first = pl.multiple_of(block * self.rows + at, 16)
            ref[(*lead, pl.ds(first, count), columns)] = total.astype(ref.dtype)

        act.wide = ref.dtype == WIDE
        return act

    def open(self, p, zb):
        self.a1(p, zb).start()
        self.b1(p, zb, 0).start()
        self.b1(p, zb, 1).start()

    def first(self, p, zb):
        z, y, x = self.z, self.y, self.x
        a, b, _ = self.columns(p)
        r1a, r1b = self.held[p][0], self.held[p][1]
        self.a1(p, zb).wait_recv()
        self.add(
            self.put(r1a, (zb,), 1 - x),
            self.rows,
            self.part(r1a, (zb,), 1 - x),
            self.grad(p, self.block(zb, y, 1 - x), a),
        )
        self.a2(p, zb).start()
        self.b1(p, zb, 0).wait_recv()
        self.b1(p, zb, 1).wait_recv()
        self.add(
            self.put(r1b, (zb, 1 - y), 0),
            self.rows,
            self.part(r1b, (zb, 1 - y), 0),
            self.grad(p, self.block(zb, 1 - y, x), b),
        )
        self.b2(p, zb).start()

    def terms(self, p, zb):
        z, y, x = self.z, self.y, self.x
        a, b, _ = self.columns(p)
        r1a, r1b, r2a, r2b = self.held[p][:4]
        own = self.block(zb, y, x)
        return (
            [self.grad(p, own, a), self.part(r1a, (zb,), x), self.part(r2a, (zb,), 0)],
            [self.grad(p, own, b), self.part(r1b, (zb, y), 0), self.part(r2b, (zb,), 0)],
        )

    def pass_on(self, p, zb, way):
        a, b, _ = self.columns(p)
        rz = self.held[p][4]
        self.a2(p, zb).wait_recv()
        self.b2(p, zb).wait_recv()
        from_line = (self.z - way >= 0) & (self.z - way < self.depth)

        @pl.when(from_line)
        def _():
            self.arrived(rz, self.z_recv.at[p, zb], zb)
            for terms, columns in zip(self.terms(p, zb), (a, b), strict=True):
                self.add(
                    self.put(rz, (zb,), 0, columns),
                    self.rows,
                    *terms,
                    self.part(rz, (zb,), 0, columns),
                )

        @pl.when(jnp.logical_not(from_line))
        def _():
            for terms, columns in zip(self.terms(p, zb), (a, b), strict=True):
                self.add(self.put(rz, (zb,), 0, columns), self.rows, *terms)

        self.z_copy(p, zb, way).start()

    def pass_c(self, p, zb, way):
        c = self.columns(p)[2]
        rc = self.held[p][5]
        from_line = (self.z - way >= 0) & (self.z - way < self.depth)

        @pl.when(from_line)
        def _():
            self.arrived(rc, self.zc_recv.at[p, zb], zb)
            self.add(
                self.put(rc, (zb,), 0),
                4 * self.rows,
                self.part(rc, (zb,), 0),
                self.grad(p, zb * 4, c),
            )
            self.zc_copy(p, zb, way, False).start()

        @pl.when(jnp.logical_not(from_line))
        def _():
            self.zc_copy(p, zb, way, True).start()

    def own_c(self, p):
        z, depth = self.z, self.depth
        c = self.columns(p)[2]
        rc = self.held[p][5]
        grad = self.grad(p, z * 4, c)
        lower, upper = self.part(rc, (z,), 0), self.part(rc, (depth,), 0)
        put = self.put(rc, (z,), 0)

        @pl.when(z > 0)
        def _():
            self.arrived(rc, self.zc_recv.at[p, z], z)

        @pl.when(z < depth - 1)
        def _():
            self.arrived(rc, self.zc_recv.at[p, depth], depth)

        @pl.when((z > 0) & (z < depth - 1))
        def _():
            self.add(put, 4 * self.rows, grad, lower, upper)

        @pl.when(z == 0)
        def _():
            self.add(put, 4 * self.rows, grad, upper)

        @pl.when(z == depth - 1)
        def _():
            self.add(put, 4 * self.rows, grad, lower)

        self.cy(p).start()

    def turn_c(self, p):
        rc, rcy = self.held[p][5], self.held[p][6]
        self.cy(p).wait_recv()
        self.add(
            self.put(rc, (self.z,), 2 * self.y),
            2 * self.rows,
            self.part(rc, (self.z,), 2 * self.y),
            self.part(rcy, (), 0),
        )
        self.cx(p).start()

    def close(self, p):
        z, depth = self.z, self.depth
        a, b, c = self.columns(p)
        rz, rc, rcx = self.held[p][4], self.held[p][5], self.held[p][7]
        self.a2(p, z).wait_recv()
        self.b2(p, z).wait_recv()

        @pl.when(z > 0)
        def _():
            self.arrived(rz, self.z_recv.at[p, z], z)

        @pl.when(z < depth - 1)
        def _():
            self.arrived(rz, self.z_recv.at[p, depth], depth)

        def total(*slots):
            for terms, columns in zip(self.terms(p, z), (a, b), strict=True):
                lines = [self.part(rz, (slot,), 0, columns) for slot in slots]
                self.add(self.put(self.shards[p], (), 0, columns), self.rows, *terms, *lines)

        pl.when((z > 0) & (z < depth - 1))(lambda: total(z, depth))
        pl.when(z == 0)(lambda: total(depth))
        pl.when(z == depth - 1)(lambda: total(z))
        self.cx(p).wait_recv()
        self.add(
            self.put(self.shards[p], (), 0, c),
            self.rows,
            self.part(rc, (z,), 2 * self.y + self.x),
            self.part(rcx, (), 0),
        )

    def at_step(self, step, act):
        z, depth = self.z, self.depth
        if step < 0:
            act(z, 0)
            return
        for zb, valid, way in (
            (z + 1 + step, z + 1 + step < depth, 1),
            (z - 1 - step, z - 1 - step >= 0, -1),
        ):
            pl.when(valid)(functools.partial(act, zb, way))

    def stage(self, p, s):
        last = self.depth - 2

        def opened(step):
            self.at_step(step, lambda zb, way: self.open(p, zb))

        def added(step):
            self.at_step(step, lambda zb, way: self.first(p, zb))

        def passed(step):
            self.at_step(step, lambda zb, way: self.pass_on(p, zb, way))

        def passed_c(step):
            self.at_step(step, lambda zb, way: self.pass_c(p, zb, way))

        if s == 0:
            opened(last)
            opened(last - 1)
            passed_c(last)
            return
        if s <= last + 2:
            added(last + 1 - s)
        if last - 1 - s >= -1:
            opened(last - 1 - s)
        if last - s >= 0:
            passed_c(last - s)
        if s >= 2 and last + 2 - s >= 0:
            passed(last + 2 - s)
        if s == last + 1:
            self.own_c(p)
        if s == last + 2:
            self.turn_c(p)
        if s == last + 3:
            self.close(p)

    def sent(self, p):
        def line(zb, way):
            from_line = (self.z - way >= 0) & (self.z - way < self.depth)
            self.z_copy(p, zb, way).wait_send()
            pl.when(from_line)(lambda: self.zc_copy(p, zb, way, False).wait_send())
            pl.when(jnp.logical_not(from_line))(lambda: self.zc_copy(p, zb, way, True).wait_send())

        for zb in range(self.depth):
            self.a1(p, zb).wait_send()
            self.b1(p, zb, 0).wait_send()
            self.b1(p, zb, 1).wait_send()
            self.a2(p, zb).wait_send()
            self.b2(p, zb).wait_send()
        for step in range(self.depth - 1):
            self.at_step(step, line)
        self.cy(p).wait_send()
        self.cx(p).wait_send()


class SmallSum:
    def __init__(self, lines, buffer, send, recv):
        member = lax.axis_index("tensor")
        self.partners = [{"tensor": 1 - member}, {"dp": lines.x_peer}, {"dp": lines.y_peer}]
        for level in range(lines.depth.bit_length() - 1):
            reach = 1 << level
            way = 1 - 2 * ((lines.z // reach) % 2)
            self.partners.append({"dp": lines.me + 4 * reach * way})
        self.buffer, self.send, self.recv = buffer, send, recv

    def copy(self, step):
        return pltpu.make_async_remote_copy(
            src_ref=self.buffer.at[step],
            dst_ref=self.buffer.at[len(self.partners) + 1 + step],
            send_sem=self.send.at[step],
            recv_sem=self.recv.at[step],
            device_id=self.partners[step],
            device_id_type=MESH,
        )

    def step(self, step):
        if step:
            self.copy(step - 1).wait_recv()
            self.buffer[step] = self.buffer[step - 1] + self.buffer[len(self.partners) + step]
        if step < len(self.partners):
            self.copy(step).start()

    def sent(self):
        for step in range(len(self.partners)):
            self.copy(step).wait_send()


def adamw_update(master, moment, square, gradient, step_rate, decay_rate):
    moment_new = beta_one * moment + (1.0 - beta_one) * gradient
    square_new = beta_two * square + (1.0 - beta_two) * gradient * gradient
    moment_hat = moment_new / (1.0 - beta_one**STEP)
    square_hat = square_new / (1.0 - beta_two**STEP)
    master_new = master - step_rate * (
        moment_hat / (jnp.sqrt(square_hat) + adam_epsilon) + decay_rate * master
    )
    return (moment_new, square_new, master_new)


SCATTER_AT = {
    "reduce": {4: [(0, 0)]},
    "expand": {2: [(1, 0)], 4: [(2, 0), (0, 1), (1, 1)]},
    "norm": {-1: [(1, 2)], 1: [(2, 1)], 2: [(3, 0)], 3: [(0, 2)]},
    "attend": {1: [(2, 2), (3, 1)], 5: [(0, 3)], 8: [(2, 3)], 10: [(3, 2)], 13: [(3, 3), (4, 1)], 14: [(2, 4)], 19: [(1, 4)], 20: [(4, 2)], 22: [(3, 4)]},
    "project": {0: [(4, 0), (1, 3)], 1: [(5, 0), (1, 5)]},
    "terms": {1: [(5, 1)], 2: [(4, 3)]},
    "far": {-1: [(5, 2)], 0: [(0, 4), (2, 5)]},
    "near": {-1: [(5, 3), (3, 5)], 0: [(4, 4)]},
    "encoded": {-1: [(5, 4)], 1: [(0, 5)]},
    "end": [(5, 5), (4, 5)],
}


def back_kernel(
    depth, lengths_ref, dealing_ref, vectors_ref,
    whole_ref, far_ref, qkv_in, hidden_turned_in, upstream_in, context_in, totals_in,
    acc_in, normal_in, inverse_in, turned_in, active_in, slope_in, far_ctx_in, *rest,
):
    encoded_out, input_out, small_out, *rest = rest
    shards, rest = rest[:6], rest[6:]
    enc_pair, grad_ref, input_far, acc, arrived, merge_recv, small, score_bias, *rest = rest
    grads, rest = rest[:6], rest[6:]
    buffers, rest = rest[: 6 * Scatter.buffers], rest[6 * Scatter.buffers :]
    small_send, small_recv, in_sem, load_sem, ctx_sem, far_send, far_recv, merge_sem, enc_sem, input_sem, *sems = rest
    lines = Scatter(depth, grads, shards, buffers, sems)
    sums = SmallSum(lines, small, small_send, small_recv)
    group = Group(lengths_ref, dealing_ref)
    member = lax.axis_index("tensor")
    rows, width = acc.shape
    total_rows = 2 * rows
    chunks, _, both = active_in.shape
    half = both // 2
    per_piece = chunks // 2
    piece_span = grads[0].shape[1]
    pairs = qkv_in.shape[0]
    inner = pairs * PAIR
    tall, short = 256, 128

    def rows_of(which):
        return pl.ds(pl.multiple_of(which * rows, rows), rows)

    def tile(step, size):
        return pl.ds(pl.multiple_of(step * size, size), size)

    def fetch(source, target, sem):
        return pltpu.make_async_copy(source, target, in_sem.at[sem])

    def phase(name, count, body):
        between = {
            step: [functools.partial(lines.stage, *stage) for stage in stages]
            for step, stages in SCATTER_AT.get(name, {}).items()
        }
        for act in between.pop(-1, ()):
            act()
        looped(count, body, between)

    def places_of(first):
        return first + lax.broadcasted_iota(jnp.int32, (tall, 1), 0)

    def add_sum(row, values):
        small[0, row : row + 1, :] += jnp.sum(values, axis=0, keepdims=True)

    acc_copy = fetch(acc_in, acc, 0)
    acc_copy.start()
    greet_line(
        lines.me, lines.z, lines.y, lines.x, depth, [sums.partners[0], *sums.partners[3:]]
    )
    small[0] = jnp.zeros(small.shape[1:], WIDE)
    score_bias[...] = group.score_bias(total_rows - LONGEST)

    def feed_phase(late, late_turned, turned, upstream, active, slope, inner_grad, expand_buf, reduce_buf, leaving, encoded):
        def active_load(j):
            slot = lax.rem(j, 2)
            return [pltpu.make_async_copy(active_in.at[j], active.at[slot], load_sem.at[slot, 4])]

        def loads(j):
            slot = lax.rem(j, 2)
            piece, at = 1 + j // per_piece, lax.rem(j, per_piece) * half
            copies = [pltpu.make_async_copy(slope_in.at[j], slope.at[slot], load_sem.at[slot, 5])]
            for kind, buf in enumerate((expand_buf, reduce_buf)):
                first = pl.multiple_of(at + kind * per_piece * half, half)
                for side, source in enumerate((far_ref, whole_ref)):
                    copies.append(
                        pltpu.make_async_copy(
                            source.at[piece, :, pl.ds(first, half)],
                            buf.at[slot, :, pl.ds(side * half, half)],
                            load_sem.at[slot, 2 * kind + side],
                        )
                    )
            return copies

        def taken(j, load):
            for copy in load(j):
                copy.wait()

            @pl.when(j + 1 < chunks)
            def _():
                for copy in load(j + 1):
                    copy.start()

        fetches = [fetch(upstream_in, upstream, 1), fetch(turned_in, turned, 2)]
        for copy in fetches:
            copy.start()
        for copy in [*active_load(0), *loads(0)]:
            copy.start()
        acc_copy.wait()
        for copy in fetches:
            copy.wait()

        def late_tile(step):
            at = tile(step, short)
            unit, scale = norm(acc[at, :])
            encoded[at, :] = (unit * vectors_ref[6:7, :] + vectors_ref[7:8, :]).astype(LOW)
            upper = upstream[at, :].astype(WIDE)
            add_sum(6, upper * unit)
            add_sum(7, upper)
            grad = norm_back(upper * vectors_ref[6:7, :], unit, scale)
            grad_low = grad.astype(LOW)
            add_sum(5, grad_low.astype(WIDE))
            acc[at, :] = grad
            late[at, :] = grad_low
            late_turned[:, at] = grad.T.astype(LOW)

        looped(rows // short, late_tile, {})
        enc_near = pltpu.make_async_copy(encoded, enc_pair.at[member], enc_sem.at[2])
        enc_far = other_core(encoded, enc_pair.at[member], enc_sem.at[0], enc_sem.at[1])
        enc_near.start()
        enc_far.start()

        def send(k):
            slot = lax.rem(k, 2)
            return other_core(
                leaving.at[slot], arrived.at[slot], far_send.at[slot], far_recv.at[slot]
            )

        def own_columns(k):
            return pl.ds(pl.multiple_of(lax.rem(k, per_piece) * half, half), half)

        def in_piece(k, act):
            for piece in range(4):
                pl.when(k // per_piece == piece)(functools.partial(act, grads[piece]))

        def finish(k):
            send(k).wait_recv()

            def add(grad):
                @pl.loop(0, width // tall)
                def _(step):
                    at = tile(step, tall)
                    grad[at, own_columns(k)] += arrived[lax.rem(k, 2), at, :]

            in_piece(k, add)

        def products(k, left, right):
            @pl.when(k >= 2)
            def _():
                send(k - 2).wait_send()

            for step in range(width // tall):
                at = slice(step * tall, (step + 1) * tall)
                part = dot_nn(left[at, :], right[...])
                leaving[lax.rem(k, 2), at, :] = part[:, 0:half].astype(LOW)
                own = part[:, half:both].astype(LOW)

                def keep(grad, at=at, own=own):
                    grad[at, own_columns(k)] = own

                in_piece(k, keep)

            @pl.when(k >= 1)
            def _():
                finish(k - 1)

            send(k).start()

        def reduce_chunk(j):
            taken(j, active_load)
            products(j, late_turned, active.at[lax.rem(j, 2)])

        def expand_chunk(j):
            slot = lax.rem(j, 2)
            taken(j, loads)
            total = jnp.zeros((1, both), WIDE)
            for step in range(rows // tall):
                at = slice(step * tall, (step + 1) * tall)
                grad = dot_nn(late[at, :], reduce_buf[slot]) * slope[slot, at, :].astype(WIDE)
                grad = grad.astype(LOW)
                inner_grad[at, :] = grad
                total = total + jnp.sum(grad.astype(WIDE), axis=0, keepdims=True)
                acc[at, :] += dot_nt(grad, expand_buf[slot])
            for which, side in ((1 - member, 0), (member, half)):
                row = 8 + which * 2 + j // per_piece
                small[0, pl.ds(row, 1), own_columns(j)] = total[:, side : side + half]
            products(chunks + j, turned, inner_grad)

        phase("reduce", chunks, reduce_chunk)
        phase("expand", chunks, expand_chunk)
        finish(2 * chunks - 1)
        for k in (2 * chunks - 2, 2 * chunks - 1):
            send(k).wait_send()
        enc_near.wait()
        enc_far.wait()

    pl.run_scoped(
        feed_phase,
        pltpu.VMEM((rows, width), LOW),
        pltpu.VMEM((width, rows), LOW),
        pltpu.VMEM((width, rows), LOW),
        pltpu.VMEM((rows, width), LOW),
        pltpu.VMEM((2, rows, both), LOW),
        pltpu.VMEM((2, rows, both), LOW),
        pltpu.VMEM((rows, both), LOW),
        pltpu.VMEM((2, width, both), LOW),
        pltpu.VMEM((2, width, both), LOW),
        pltpu.VMEM((2, width, half), LOW),
        pltpu.VMEM((rows, width), LOW),
    )

    def merge_phase(normal, inverse, turned, near_ctx, far_ctx, merge, merge_far, grad_own, grad_far, merge_send):
        merge_columns = pl.ds(whole_ref.shape[2] - inner, inner)
        fetches = [
            fetch(normal_in, normal, 0),
            fetch(inverse_in, inverse, 1),
            fetch(context_in.at[rows_of(member)], near_ctx, 2),
            fetch(far_ctx_in, far_ctx, 3),
            fetch(whole_ref.at[0, :, merge_columns], merge, 4),
            fetch(far_ref.at[0, :, merge_columns], merge_far, 5),
        ]
        for copy in fetches:
            copy.start()
        for copy in fetches:
            copy.wait()

        def norm_tile(step):
            at = tile(step, short)
            grad = acc[at, :]
            unit = normal[at, :]
            add_sum(3, grad * unit)
            add_sum(4, grad)
            branch_grad = norm_back(grad * vectors_ref[3:4, :], unit, inverse[at, 0:1])
            branch_low = branch_grad.astype(LOW)
            add_sum(2, branch_low.astype(WIDE))
            acc[at, :] = branch_grad
            turned[:, at] = branch_grad.T.astype(LOW)
            grad_far[at, :] = dot_nn(branch_low, merge_far[...]).astype(LOW)
            grad_own[at, :] = dot_nn(branch_low, merge[...]).astype(LOW)

        phase("norm", rows // short, norm_tile)
        out_grad = other_core(grad_far, grad_ref.at[rows_of(member)], ctx_sem.at[0], ctx_sem.at[1])
        in_grad = pltpu.make_async_copy(grad_own, grad_ref.at[rows_of(member)], ctx_sem.at[2])
        out_grad.start()
        in_grad.start()
        out_merge = other_core(merge_send, merge_recv, merge_sem.at[0], merge_sem.at[1])

        def merge_step(which):
            @pl.when(which == 0)
            def _():
                for step in range(width // tall):
                    at = slice(step * tall, (step + 1) * tall)
                    merge_send[at, :] = dot_nn(turned[at, :], far_ctx[...]).astype(LOW)
                out_merge.start()

            @pl.when(which == 1)
            def _():
                out_merge.wait()
                for step in range(width // tall):
                    at = slice(step * tall, (step + 1) * tall)
                    grads[4][at, 0:inner] = (
                        dot_nn(turned[at, :], near_ctx[...]) + merge_recv[at, :].astype(WIDE)
                    ).astype(LOW)

        phase("merge", 2, merge_step)
        out_grad.wait()
        in_grad.wait()

    pl.run_scoped(
        merge_phase,
        pltpu.VMEM((rows, width), WIDE),
        pltpu.VMEM((rows, 128), WIDE),
        pltpu.VMEM((width, rows), LOW),
        pltpu.VMEM((rows, inner), LOW),
        pltpu.VMEM((rows, inner), LOW),
        pltpu.VMEM((width, inner), LOW),
        pltpu.VMEM((width, inner), LOW),
        pltpu.VMEM((rows, inner), LOW),
        pltpu.VMEM((rows, inner), LOW),
        pltpu.VMEM((width, inner), LOW),
    )
    def last_phase(mixed):
        def attend_phase(qkv, context, upper, totals, dots, key_turned, queries, uppers, query_sum, hidden_turned):
            def loads(pair, slot):
                columns = pl.ds(pl.multiple_of(pair * PAIR, PAIR), PAIR)
                return [
                    pltpu.make_async_copy(qkv_in.at[pair], qkv.at[slot], load_sem.at[slot, 0]),
                    pltpu.make_async_copy(
                        context_in.at[:, columns], context.at[slot], load_sem.at[slot, 1]
                    ),
                    pltpu.make_async_copy(
                        grad_ref.at[:, columns], upper.at[slot], load_sem.at[slot, 2]
                    ),
                ]

            fetches = [fetch(totals_in, totals, 0)]
            for copy in [*loads(0, 0), *fetches]:
                copy.start()
            for copy in fetches:
                copy.wait()
            blocks = ((0, LONGEST), (LONGEST, total_rows - LONGEST))
            per_pair = total_rows // TILE

            def hidden_tile(step, slot):
                return pltpu.make_async_copy(
                    hidden_turned_in.at[tile(step, tall), :],
                    hidden_turned.at[slot],
                    load_sem.at[slot, 3],
                )

            def project(second):
                grad, first = (grads[5], 0) if second else (grads[4], inner)
                span = (pairs // 2) * 3 * PAIR
                columns = slice(span if second else 0, span * 2 if second else span)
                hidden_tile(0, 0).start()
                for step in range(width // tall):
                    if step + 1 < width // tall:
                        hidden_tile(step + 1, (step + 1) % 2).start()
                    hidden_tile(step, step % 2).wait()
                    grad[step * tall : (step + 1) * tall, first : first + span] = dot_nn(
                        hidden_turned[step % 2], mixed[:, columns]
                    ).astype(LOW)

            def pair_body(pair):
                slot = lax.rem(pair, 2)
                for copy in loads(pair, slot):
                    copy.wait()

                @pl.when(pair + 1 < pairs)
                def _():
                    for copy in loads(pair + 1, 1 - slot):
                        copy.start()

                attend_back_open(
                    qkv.at[slot], context.at[slot], upper.at[slot], dots, key_turned, queries, uppers
                )
                base = pair * 3 * PAIR

                def columns(which):
                    return pl.ds(pl.multiple_of(base + which * PAIR, PAIR), PAIR)

                for begin, size in blocks:
                    block = slice(begin, begin + size)
                    query_sum[:, block] = jnp.zeros((PAIR, size), WIDE)

                    def key_tile(step, begin=begin, size=size):
                        at, key_sum, value_sum = attend_back_tile(
                            qkv.at[slot], score_bias, totals.at[pair], dots, key_turned, queries, uppers, query_sum,
                            begin, size, step,
                        )
                        mixed[at, columns(1)] = key_sum.astype(LOW)
                        mixed[at, columns(2)] = value_sum.astype(LOW)

                    between = {}
                    for step in range(size // TILE):
                        number = begin // TILE + step
                        for act_pair in range(pairs):
                            for p, s in SCATTER_AT["attend"].get(act_pair * per_pair + number, ()):

                                def act(act_pair=act_pair, p=p, s=s):
                                    pl.when(pair == act_pair)(lambda: lines.stage(p, s))

                                between.setdefault(step, []).append(act)
                    looped(size // TILE, key_tile, between)
                    mixed[block, columns(0)] = (
                        (query_sum[:, block] * HEAD_DIM ** (-0.5)).T.astype(LOW)
                    )
                for which, row in ((0, 0), (2, 1)):
                    part = mixed[:, columns(which)].astype(WIDE)
                    spot = pl.multiple_of(member * inner + pair * PAIR, PAIR)
                    small[0, row : row + 1, pl.ds(spot, PAIR)] = jnp.sum(
                        part, axis=0, keepdims=True
                    )

            def project_stages(second):
                return [
                    functools.partial(project, second),
                    *[functools.partial(lines.stage, *st) for st in SCATTER_AT["project"][second]],
                ]

            looped(pairs, pair_body, {1: project_stages(0), 3: project_stages(1)})

        pl.run_scoped(
            attend_phase,
            pltpu.VMEM((2, total_rows, 3 * PAIR), LOW),
            pltpu.VMEM((2, total_rows, PAIR), LOW),
            pltpu.VMEM((2, total_rows, PAIR), LOW),
            pltpu.VMEM(totals_in.shape, WIDE),
            pltpu.VMEM((8, total_rows), WIDE),
            pltpu.VMEM((PAIR, total_rows), LOW),
            pltpu.VMEM((2, total_rows, PAIR), LOW),
            pltpu.VMEM((2, total_rows, PAIR), LOW),
            pltpu.VMEM((PAIR, total_rows), WIDE),
            pltpu.VMEM((2, tall, total_rows), LOW),
        )
        sums.step(0)

        def input_phase(weight, terms, leaving):
            fetches = [
                fetch(whole_ref.at[0, :, pl.ds(0, pairs * 3 * PAIR)], weight, 0),
            ]
            for copy in fetches:
                copy.start()
            for copy in fetches:
                copy.wait()

            def term_tile(step):
                at = tile(step, tall)
                total = dot_nt(mixed[at, :], weight[...])
                own = rows // tall
                mine = step // own == member

                @pl.when(mine)
                def _():
                    terms[at, :] = (total + acc[tile(lax.rem(step, own), tall), :]).astype(LOW)

                @pl.when(jnp.logical_not(mine))
                def _():
                    terms[at, :] = total.astype(LOW)

            phase("terms", total_rows // tall, term_tile)
            sums.step(1)

            def own_rows(which, step):
                places = places_of(which * rows + step * tall)
                return picked_rows(group.moved(places, group.own, group.first), terms)

            def far_tile(step):
                leaving[tile(step, tall), :] = own_rows(1 - member, step).astype(LOW)

            phase("far", rows // tall, far_tile)
            crossing = other_core(leaving, input_far, input_sem.at[0], input_sem.at[1])
            crossing.start()
            sums.step(2)

            def near_tile(step):
                acc[tile(step, tall), :] = own_rows(member, step)

            phase("near", rows // tall, near_tile)
            sums.step(3)
            crossing.wait()
            back = fetch(input_far, leaving, 2)
            back.start()
            back.wait()

            @pl.loop(0, rows // short)
            def _(step):
                at = tile(step, short)
                leaving[at, :] = (acc[at, :] + leaving[at, :].astype(WIDE)).astype(LOW)

            done = fetch(leaving, input_out, 2)
            done.start()
            done.wait()

        pl.run_scoped(
            input_phase,
            pltpu.VMEM((width, pairs * 3 * PAIR), LOW),
            pltpu.VMEM((total_rows, width), LOW),
            pltpu.VMEM((rows, width), LOW),
        )

    pl.run_scoped(last_phase, pltpu.VMEM((total_rows, pairs * 3 * PAIR), LOW))

    def end_phase(pair, encoded):
        fetches = [fetch(enc_pair.at[i], pair.at[rows_of(i)], i) for i in range(2)]
        for copy in fetches:
            copy.start()
        for copy in fetches:
            copy.wait()

        def encoded_tile(step):
            places = places_of(member * rows + step * tall)
            index = group.moved(places, group.dealt, group.first)
            encoded[tile(step, tall), :] = picked_rows(index, pair).astype(LOW)

        phase("encoded", rows // tall, encoded_tile)
        done = fetch(encoded, encoded_out, 2)
        done.start()
        for step in range(4, len(sums.partners) + 1):
            sums.step(step)
        small_out[...] = small[len(sums.partners)]
        for st in SCATTER_AT["end"]:
            lines.stage(*st)
        done.wait()

    pl.run_scoped(
        end_phase, pltpu.VMEM((total_rows, width), LOW), pltpu.VMEM((rows, width), LOW)
    )
    sums.sent()
    for p in range(len(grads)):
        lines.sent(p)


def finish_kernel(
    small_ref, vectors_ref, vectors_first, vectors_second, hidden_ref, hidden_first, hidden_second, *rest
):
    shards, (encoded_in, input_in), states_in, rest = rest[:6], rest[6:8], rest[8:20], rest[20:]
    encoded_out, input_out, vector_grad_ref, *rest = rest
    states_out, small_out, ins, outs = rest[:12], rest[12:18], rest[18:30], rest[30:42]
    state_sem, out_sem, pass_sem = rest[42:]
    width = vectors_ref.shape[1]
    inner = ins[3].shape[1]
    pairs = inner // PAIR
    span = shards[0].shape[1]
    loads = [pltpu.make_async_copy(states_in[i], ins[i], state_sem.at[i]) for i in range(12)]
    writes = [pltpu.make_async_copy(outs[i], states_out[i], out_sem.at[i]) for i in range(12)]
    passes = [
        pltpu.make_async_copy(encoded_in, encoded_out, pass_sem.at[0]),
        pltpu.make_async_copy(input_in, input_out, pass_sem.at[1]),
    ]
    for copy in [*reversed(loads), *passes]:
        copy.start()
    vector_grad_ref[...] = small_ref[0:8, :]
    states = vectors_ref[...], vectors_first[...], vectors_second[...]
    for i, value in enumerate(adamw_update(*states, small_ref[0:8, :], rate_vectors, 0.0)):
        small_out[i][...] = value
    for i in range(hidden_ref.shape[1] // width):
        columns = slice(i * width, (i + 1) * width)
        states = hidden_ref[:, columns], hidden_first[:, columns], hidden_second[:, columns]
        grad = small_ref[8 + i : 9 + i, :]
        for n, value in enumerate(adamw_update(*states, grad, rate_hidden, 0.0)):
            small_out[3 + n][:, columns] = value

    def update(matrix, lead, columns, grad, grad_columns):
        rate = (rate_project, rate_merge, rate_expand, rate_reduce)[matrix]

        @pl.loop(0, grad.shape[0] // 16)
        def _(step):
            at = pl.ds(pl.multiple_of(step * 16, 16), 16)
            old = [ins[3 * matrix + i][(*lead, at, columns)] for i in range(3)]
            new = adamw_update(*old, grad[at, grad_columns], rate, weight_decay)
            for i in range(3):
                outs[3 * matrix + i][(*lead, at, columns)] = new[i]

    for matrix in (3, 2, 1, 0):
        mine = slice(3 * matrix, 3 * matrix + 3)
        for copy in loads[mine]:
            copy.wait()
        if matrix >= 2:
            for i in range(2):
                columns = slice(i * span, (i + 1) * span)
                update(matrix, (), columns, shards[2 * (3 - matrix) + i], slice(0, span))
        elif matrix == 1:
            update(matrix, (), slice(0, inner), shards[4], slice(0, inner))
        else:
            for pair in range(pairs):
                piece, begin = (4, inner) if pair < pairs // 2 else (5, 0)
                for c in range(3):
                    at = begin + (3 * (pair % (pairs // 2)) + c) * PAIR
                    columns = slice(pair * PAIR, (pair + 1) * PAIR)
                    update(matrix, (c,), columns, shards[piece], slice(at, at + PAIR))
        for copy in writes[mine]:
            copy.start()
    for copy in [*writes, *passes]:
        copy.wait()


def finish(small, shards, rows_out, matrices, vectors, hidden):
    states = [one for matrix in matrices for one in matrix]
    shape, sem = jax.ShapeDtypeStruct, pltpu.SemaphoreType.DMA
    vmem, anywhere = pl.BlockSpec(memory_space=pltpu.VMEM), pl.BlockSpec(memory_space=pl.ANY)
    held = [pltpu.VMEM(one.shape, WIDE) for one in states]
    return pl.pallas_call(
        finish_kernel,
        in_specs=[*[vmem] * 13, *[anywhere] * 14],
        out_specs=[*[anywhere] * 2, vmem, *[anywhere] * 12, *[vmem] * 6],
        out_shape=[
            *[shape(one.shape, LOW) for one in rows_out],
            shape((8, small.shape[1]), WIDE),
            *[shape(one.shape, WIDE) for one in (*states, *vectors, *hidden)],
        ],
        scratch_shapes=[*held, *held, sem((12,)), sem((12,)), sem((2,))],
        compiler_params=pltpu.CompilerParams(vmem_limit_bytes=63 * MIB),
    )(small, *vectors, *hidden, *shards, *rows_out, *states)


def back(lengths, dealing, vectors, whole, far, kept, parts):
    qkv, hidden_turned, upstream, context, totals, acc, *_ = kept
    rows, width = acc.shape
    total_rows, inner = context.shape
    depth, shard_rows = parts // 4, width // parts
    half, pair_span = 256, 3 * PAIR * (qkv.shape[0] // 2)
    piece_span = whole.shape[2] // 2
    spans = (*[piece_span] * 4, inner + pair_span, pair_span)
    classes = []
    for span in spans:
        third = max(128, span // 5 // 128 * 128)
        if (span - third) % 256:
            third += 128
        classes.append(((span - third) // 2, (span - third) // 2, third))
    shape, sem = jax.ShapeDtypeStruct, pltpu.SemaphoreType.DMA
    vmem, anywhere = pl.BlockSpec(memory_space=pltpu.VMEM), pl.BlockSpec(memory_space=pl.ANY)
    steps = 3 + depth.bit_length() - 1
    results = pl.pallas_call(
        functools.partial(back_kernel, depth),
        in_specs=[
            *[pl.BlockSpec(memory_space=pltpu.SMEM)] * 2,
            vmem,
            *[anywhere] * (2 + len(kept)),
        ],
        out_specs=[*[anywhere] * 2, *[vmem] * (1 + len(spans)), *[anywhere] * 3],
        out_shape=[
            shape((rows, width), LOW),
            shape((rows, width), LOW),
            shape((16, width), WIDE),
            *[shape((shard_rows, span), WIDE) for span in spans],
            shape((2, rows, width), LOW),
            shape((total_rows, inner), LOW),
            shape((rows, width), LOW),
        ],
        scratch_shapes=[
            pltpu.VMEM((rows, width), WIDE),
            pltpu.VMEM((2, width, half), LOW),
            pltpu.VMEM((width, inner), LOW),
            pltpu.VMEM((2 * steps + 1, 16, width), WIDE),
            pltpu.VMEM((total_rows - LONGEST, total_rows - LONGEST), WIDE),
            *[pltpu.VMEM((width, span), LOW) for span in spans],
            *Scatter.scratch(depth, shard_rows, classes),
            sem((steps,)),
            sem((steps,)),
            sem((6,)),
            sem((2, 6)),
            sem((3,)),
            sem((2,)),
            sem((2,)),
            sem((2,)),
            sem((3,)),
            sem((2,)),
            *Scatter.semaphores(depth, len(spans)),
        ],
        compiler_params=pltpu.CompilerParams(
            collective_id=1, has_side_effects=True, vmem_limit_bytes=63 * MIB
        ),
    )(lengths, dealing, vectors, whole, far, *kept)
    return results[:2], results[2], results[3 : 3 + len(spans)]


def by_kernels(tokens, cotangent, lengths, dealing, project, merge, expand, reduce, vectors, hidden, parts):
    hidden = tuple(one.reshape(1, -1) for one in hidden)
    matrices = (project, merge, expand, reduce)
    whole, far, *kept = front(
        lengths, dealing, *[one[0] for one in matrices], vectors[0], hidden[0], tokens, cotangent, parts
    )
    rows_out, small, shards = back(lengths, dealing, vectors[0], whole, far, kept, parts)
    results = finish(small, shards, rows_out, matrices, vectors, hidden)
    encoded, input_grad, vector_grad = results[:3]
    news = [results[3 + 3 * i : 6 + 3 * i] for i in range(6)]
    return (
        encoded,
        input_grad,
        *news[0],
        *[one.T for one in news[1]],
        *news[2],
        *[one.T for one in news[3]],
        *news[4],
        *[one.reshape(-1) for one in news[5]],
        vector_grad,
    )


def local(
    tokens,
    cotangent,
    lengths,
    dealing,
    project_weight,
    project_first,
    project_second,
    merge_weight,
    merge_first,
    merge_second,
    expand_weight,
    expand_first,
    expand_second,
    reduce_weight,
    reduce_first,
    reduce_second,
    vectors,
    vector_first,
    vector_second,
    hidden_bias,
    hidden_first,
    hidden_second,
):
    parts = lax.axis_size("dp")
    member = lax.axis_index("tensor")
    other = 1 - member
    half_rows, model_width = tokens.shape
    total_rows = 2 * half_rows
    width_half = project_weight.shape[2]
    pairs = width_half // PAIR
    hidden_half = expand_weight.shape[1]
    shard_rows = expand_weight.shape[0]
    own_begin = member * half_rows
    by_kernel = parts % 4 == 0 and (parts & (parts - 1)) == 0 and shard_rows % 16 == 0

    def swap(value):
        return lax.ppermute(value, "tensor", [(0, 1), (1, 0)])

    def own(value, size, which=member):
        return lax.dynamic_slice_in_dim(value, which * size, size, 0)

    if by_kernel:
        return by_kernels(
            tokens, cotangent, lengths, dealing,
            (project_weight, project_first, project_second),
            (merge_weight.T, merge_first.T, merge_second.T),
            (expand_weight, expand_first, expand_second),
            (reduce_weight.T, reduce_first.T, reduce_second.T),
            (vectors, vector_first, vector_second),
            (hidden_bias, hidden_first, hidden_second),
            parts,
        )

    segment, own_of, dealt_of, from_own, from_dealt = layout(lengths[0], dealing[0], total_rows)
    dealt_of = own(dealt_of, half_rows)
    short = segment[LONGEST:]
    score_bias = jnp.where(short[:, None] == short[None, :], 0.0, masked_score).astype(WIDE)

    def own_first(index):
        return lax.rem(index - own_begin + total_rows, total_rows)

    projections = (
        project_weight.reshape(3, shard_rows, pairs, PAIR)
        .transpose(1, 2, 0, 3)
        .reshape(shard_rows, 3 * width_half)
    )
    quarter = hidden_half // 2
    reduce_turned = reduce_weight.T
    shards = jnp.stack(
        [
            jnp.concatenate([projections, merge_weight.T], axis=1),
            jnp.concatenate([expand_weight[:, :quarter], reduce_turned[:, :quarter]], axis=1),
            jnp.concatenate([expand_weight[:, quarter:], reduce_turned[:, quarter:]], axis=1),
        ]
    ).astype(LOW)
    zeros_pair = jnp.zeros((pairs, PAIR), WIDE)
    bias_row = jnp.concatenate(
        [
            own(vectors[0], width_half).reshape(pairs, PAIR),
            zeros_pair,
            own(vectors[1], width_half).reshape(pairs, PAIR),
        ],
        axis=1,
    ).reshape(pairs, 1, 3 * PAIR)
    whole = lax.all_gather(shards, "dp", axis=1, tiled=True)
    far = swap(whole)
    token_pair = jnp.concatenate([tokens, swap(tokens)], axis=0)
    upper_pair = jnp.concatenate([cotangent, swap(cotangent)], axis=0)
    hidden = dot_nn(pick_rows(own_first(own_of), total_rows), token_pair).astype(LOW)
    upstream = dot_nn(pick_rows(own_first(dealt_of), total_rows), upper_pair).astype(LOW)
    qkv = jnp.einsum(
        "rd,dpc->prc",
        hidden,
        whole[0, :, : 3 * width_half].reshape(model_width, pairs, 3 * PAIR),
        preferred_element_type=WIDE,
    )
    qkv = (qkv + bias_row).astype(LOW)
    context, totals = attend(qkv, score_bias)

    (
        encoded, branch_grad, context_grad, merge_grad, expand_grad, reduce_grad, sums, hidden_part_own, hidden_part_far,
    ) = feed_block(
        context,
        whole,
        far,
        own(hidden, half_rows),
        upstream,
        vectors,
        own(hidden_bias, hidden_half),
        own(hidden_bias, hidden_half, other),
    )
    encoded_pair = jnp.concatenate([encoded, swap(encoded)], axis=0)
    encoded_out = dot_nn(
        pick_rows(own_first(own(from_dealt, half_rows)), total_rows), encoded_pair
    ).astype(LOW)
    mixed_grads = attend_back(qkv, score_bias, context, context_grad, totals)
    mixed_sums = jnp.sum(mixed_grads.astype(WIDE), axis=1).reshape(pairs, 3, PAIR)
    mixed_grads = mixed_grads.transpose(1, 0, 2).reshape(total_rows, 3 * width_half)
    project_grad = dot_tn(hidden, mixed_grads)
    input_terms = dot_nt(mixed_grads, whole[0, :, : 3 * width_half])
    own_part = own(input_terms, half_rows) + branch_grad
    input_terms = lax.dynamic_update_slice_in_dim(input_terms, own_part, own_begin, 0).astype(LOW)
    input_far = swap(
        dot_nn(pick_rows(own(from_own, half_rows, other), total_rows), input_terms).astype(LOW)
    )
    input_grad = (
        dot_nn(pick_rows(own(from_own, half_rows), total_rows), input_terms)
        + input_far.astype(WIDE)
    ).astype(LOW)
    zeros_width = jnp.zeros((model_width,), WIDE)
    zeros_hidden = jnp.zeros_like(hidden_bias)
    hidden_total = lax.dynamic_update_slice_in_dim(
        lax.dynamic_update_slice_in_dim(
            zeros_hidden, hidden_part_own, member * hidden_half, 0
        ),
        hidden_part_far,
        other * hidden_half,
        0,
    )
    vector_rows = [
        lax.dynamic_update_slice_in_dim(
            zeros_width, mixed_sums[:, c].reshape(-1), member * width_half, 0
        )
        for c in (0, 2)
    ]
    small = jnp.concatenate(
        [
            jnp.stack(vector_rows),
            sums[2:],
            hidden_total.reshape(-1, model_width),
            jnp.zeros((4, model_width), WIDE),
        ],
        axis=0,
    )
    grads = [
        lax.psum_scatter(g.astype(LOW), "dp", scatter_dimension=0, tiled=True).astype(WIDE)
        for g in (project_grad, merge_grad, expand_grad, reduce_grad)
    ]
    small = lax.psum(small, ("dp", "tensor"))
    project_shard, merge_shard, expand_shard, reduce_shard = grads
    project_shard = (
        project_shard.reshape(shard_rows, pairs, 3, PAIR)
        .transpose(2, 0, 1, 3)
        .reshape(3, shard_rows, width_half)
    )
    vector_grad = small[:8]
    hidden_grad = small[8:12].reshape(-1)
    return (
        encoded_out,
        input_grad,
        *adamw_update(
            project_weight, project_first, project_second, project_shard, rate_project, weight_decay
        ),
        *adamw_update(
            merge_weight, merge_first, merge_second, merge_shard.T, rate_merge, weight_decay
        ),
        *adamw_update(
            expand_weight, expand_first, expand_second, expand_shard, rate_expand, weight_decay
        ),
        *adamw_update(
            reduce_weight, reduce_first, reduce_second, reduce_shard.T, rate_reduce, weight_decay
        ),
        *adamw_update(vectors, vector_first, vector_second, vector_grad, rate_vectors, 0.0),
        *adamw_update(hidden_bias, hidden_first, hidden_second, hidden_grad, rate_hidden, 0.0),
        vector_grad,
    )


def solution(mesh):
    sharded = (
        P("dp", None),
        P("dp", None),
        *[P(None, "dp", "tensor")] * 3,
        *[P("tensor", "dp")] * 3,
        *[P("dp", "tensor")] * 3,
        *[P("tensor", "dp")] * 3,
        *[P()] * 6,
    )
    rows = P(("dp", "tensor"), None)
    return jax.shard_map(
        local,
        mesh=mesh,
        in_specs=(rows, rows, *sharded),
        out_specs=(rows, rows, *sharded[2:], P()),
        check_vma=False,
    )
```

```python
import functools

import jax
import jax.numpy as jnp
from jax import lax
from jax.experimental import pallas as pl
from jax.experimental.pallas import tpu as pltpu
from jax.sharding import PartitionSpec as P

HEAD_DIM = 64
LONGEST = 1024
STEP = 10
PAIR = 2 * HEAD_DIM
TILE = 256
MIB = 1024 * 1024
MESH = pl.DeviceIdType.MESH
LOW = jnp.bfloat16
WIDE = jnp.float32

beta_one = 0.9
beta_two = 0.999
adam_epsilon = 1e-08
weight_decay = 0.01
norm_epsilon = 1e-05
masked_score = -1e30
rate_project = 0.03
rate_merge = 0.3
rate_expand = 0.03
rate_reduce = 0.015
rate_vectors = 0.4
rate_hidden = 0.1


def dot_nn(a, b):
    return jnp.dot(a, b, preferred_element_type=WIDE)


def dot_nt(a, b):
    return lax.dot_general(a, b, (((1,), (1,)), ((), ())), preferred_element_type=WIDE)


def dot_tn(a, b):
    return lax.dot_general(a, b, (((0,), (0,)), ((), ())), preferred_element_type=WIDE)


def layout(lengths_row, dealing_row, total_rows):
    slots = jnp.arange(lengths_row.shape[0], dtype=jnp.int32)
    places = jnp.arange(total_rows, dtype=jnp.int32)
    rank_of = jnp.sum(jnp.where(dealing_row[None, :] == slots[:, None], slots[None, :], 0), axis=1)
    own_start = jnp.cumsum(lengths_row) - lengths_row
    dealt_start = jnp.sum(
        jnp.where(rank_of[None, :] < rank_of[:, None], lengths_row[None, :], 0), axis=1
    )
    longest = lengths_row == LONGEST
    short = jnp.where(longest, 0, lengths_row)
    start = jnp.where(longest, 0, LONGEST + jnp.cumsum(short) - short)

    def inside(begin):
        return (places[:, None] >= begin[None, :]) & (
            places[:, None] < (begin + lengths_row)[None, :]
        )

    def moved(begin, end):
        return places + jnp.sum(jnp.where(inside(begin), (end - begin)[None, :], 0), axis=1)

    segment = jnp.sum(jnp.where(inside(start), slots[None, :], 0), axis=1)
    return (
        segment,
        moved(start, own_start),
        moved(start, dealt_start),
        moved(own_start, start),
        moved(dealt_start, start),
    )


def pick_rows(index, rows):
    places = jnp.arange(rows, dtype=jnp.int32)
    return (index[:, None] == places[None, :]).astype(LOW)


class Group:
    def __init__(self, lengths_ref, dealing_ref):
        count = lengths_ref.shape[1]
        self.lengths = [lengths_ref[0, s] for s in range(count)]
        order = [dealing_ref[0, i] for i in range(count)]
        rank = [sum(jnp.where(order[i] == s, i, 0) for i in range(count)) for s in range(count)]
        short = [jnp.where(length == LONGEST, 0, length) for length in self.lengths]
        self.own, self.dealt, self.first = [], [], []
        own = own_short = jnp.int32(0)
        for s in range(count):
            self.own.append(own)
            self.first.append(jnp.where(self.lengths[s] == LONGEST, 0, LONGEST + own_short))
            self.dealt.append(
                sum(jnp.where(rank[j] < rank[s], self.lengths[j], 0) for j in range(count))
            )
            own, own_short = own + self.lengths[s], own_short + short[s]

    def inside(self, places, begin, s):
        return (places >= begin[s]) & (places < begin[s] + self.lengths[s])

    def moved(self, places, begin, end):
        total = places
        for s in range(len(begin)):
            total = total + jnp.where(self.inside(places, begin, s), end[s] - begin[s], 0)
        return total

    def score_bias(self, count):
        sides = []
        for shape, axis in (((count, 1), 0), ((1, count), 1)):
            places = lax.broadcasted_iota(jnp.int32, shape, axis) + LONGEST
            segment = jnp.zeros_like(places)
            for s in range(len(self.first)):
                segment = segment + jnp.where(self.inside(places, self.first, s), s, 0)
            sides.append(segment)
        return jnp.where(sides[0] == sides[1], 0.0, masked_score).astype(WIDE)


def picked_rows(index, source):
    places = lax.broadcasted_iota(jnp.int32, (index.shape[0], source.shape[0]), 1)
    return dot_nn(jnp.where(index == places, 1.0, 0.0).astype(LOW), source[...])


def attend_tile(qkv_ref, pair, bias_ref, begin, size, step, context_ref, columns, total_ref):
    lane = lax.broadcasted_iota(jnp.int32, (1, PAIR), 1)
    scale = HEAD_DIM ** (-0.5)
    first = pl.multiple_of(begin + step * TILE, TILE)
    query = qkv_ref[pair, pl.ds(first, TILE), 0:PAIR]
    key = qkv_ref[pair, begin : begin + size, PAIR : 2 * PAIR]
    value = qkv_ref[pair, begin : begin + size, 2 * PAIR : 3 * PAIR]
    outcome = []
    chosen = [jnp.where(lane // HEAD_DIM == head, scale, 0.0).astype(LOW) for head in range(2)]
    scores = [dot_nt(query * chosen[head], key) for head in range(2)]
    for head in range(2):
        score = scores[head]
        if begin:
            inner = pl.multiple_of(step * TILE, TILE)
            score = score + bias_ref[pl.ds(inner, TILE), :]
        top = jnp.max(score, axis=1, keepdims=True)
        exponent = jnp.exp(score - top)
        total = jnp.sum(exponent, axis=1, keepdims=True)
        outcome.append(dot_nn(exponent.astype(LOW), value) / total)
        log_total = jnp.broadcast_to(top + jnp.log(total), (TILE, PAIR))
        total_ref[pair, head : head + 1, pl.ds(first, TILE)] = log_total.T[0:1, :]
    context_ref[pl.ds(first, TILE), columns] = jnp.where(
        lane < HEAD_DIM, outcome[0], outcome[1]
    ).astype(LOW)


def attend_kernel(qkv_ref, bias_ref, context_ref, total_ref):
    rows = qkv_ref.shape[1]
    for begin, size in ((0, LONGEST), (LONGEST, rows - LONGEST)):

        @pl.loop(0, size // TILE)
        def _(step):
            attend_tile(
                qkv_ref, 0, bias_ref, begin, size, step, context_ref, slice(0, PAIR), total_ref
            )


def attend(qkv, bias):
    pairs, rows, width = qkv.shape
    return pl.pallas_call(
        attend_kernel,
        grid=(pairs,),
        in_specs=[
            pl.BlockSpec((1, rows, width), lambda p: (p, 0, 0)),
            pl.BlockSpec(bias.shape, lambda p: (0, 0)),
        ],
        out_specs=[
            pl.BlockSpec((rows, PAIR), lambda p: (0, p)),
            pl.BlockSpec((1, 8, rows), lambda p: (p, 0, 0)),
        ],
        out_shape=[
            jax.ShapeDtypeStruct((rows, pairs * PAIR), LOW),
            jax.ShapeDtypeStruct((pairs, 8, rows), WIDE),
        ],
        compiler_params=pltpu.CompilerParams(vmem_limit_bytes=48 * MIB),
    )(qkv, bias)


def attend_back_open(qkv_ref, context_ref, upper_ref, dots, key_turned, queries, uppers):
    lane = lax.broadcasted_iota(jnp.int32, (1, PAIR), 1)
    product = (upper_ref[...].astype(WIDE) * context_ref[...].astype(WIDE)).T
    for head in range(2):
        band = slice(head * HEAD_DIM, (head + 1) * HEAD_DIM)
        dots[head : head + 1, :] = jnp.sum(product[band, :], axis=0, keepdims=True)
        chosen = lane // HEAD_DIM == head
        queries[head] = qkv_ref[:, 0:PAIR] * jnp.where(chosen, HEAD_DIM ** (-0.5), 0.0).astype(LOW)
        uppers[head] = upper_ref[...] * jnp.where(chosen, 1.0, 0.0).astype(LOW)
    key_turned[...] = qkv_ref[:, PAIR : 2 * PAIR].astype(WIDE).T.astype(LOW)


def attend_back_tile(
    qkv_ref, bias_ref, total_ref, dots, key_turned, queries, uppers, query_sum, begin, size, step
):
    block = slice(begin, begin + size)
    first = pl.multiple_of(begin + step * TILE, TILE)
    key = qkv_ref[pl.ds(first, TILE), PAIR : 2 * PAIR]
    value = qkv_ref[pl.ds(first, TILE), 2 * PAIR : 3 * PAIR]
    key_sum = jnp.zeros((TILE, PAIR), WIDE)
    value_sum = jnp.zeros((TILE, PAIR), WIDE)
    scores = [dot_nt(key, queries[head, block, :]) for head in range(2)]
    weight_grads = [dot_nt(value, uppers[head, block, :]) for head in range(2)]
    for head in range(2):
        band = slice(head * HEAD_DIM, (head + 1) * HEAD_DIM)
        score = scores[head]
        if begin:
            inner = pl.multiple_of(step * TILE, TILE)
            score = score + bias_ref[pl.ds(inner, TILE), :]
        probability = jnp.exp(score - total_ref[head : head + 1, block])
        score_grads = probability * (weight_grads[head] - dots[head : head + 1, block])
        score_grads = score_grads.astype(LOW)
        value_sum = value_sum + dot_nn(probability.astype(LOW), uppers[head, block, :])
        key_sum = key_sum + dot_nn(score_grads, queries[head, block, :])
        query_sum[band, block] += dot_nn(key_turned[band, pl.ds(first, TILE)], score_grads)
    return pl.ds(first, TILE), key_sum, value_sum


def attend_back_kernel(
    qkv_ref, bias_ref, context_ref, grad_ref, total_ref, out_ref, dots, key_turned, queries, uppers, query_sum
):
    rows = qkv_ref.shape[1]
    qkv = qkv_ref.at[0]
    attend_back_open(qkv, context_ref, grad_ref, dots, key_turned, queries, uppers)
    for begin, size in ((0, LONGEST), (LONGEST, rows - LONGEST)):
        block = slice(begin, begin + size)
        query_sum[:, block] = jnp.zeros((PAIR, size), WIDE)

        @pl.loop(0, size // TILE)
        def _(step):
            at, key_sum, value_sum = attend_back_tile(
                qkv, bias_ref, total_ref.at[0], dots, key_turned, queries, uppers, query_sum, begin, size, step
            )
            out_ref[0, at, PAIR : 2 * PAIR] = key_sum.astype(LOW)
            out_ref[0, at, 2 * PAIR : 3 * PAIR] = value_sum.astype(LOW)

        out_ref[0, block, 0:PAIR] = (query_sum[:, block] * HEAD_DIM ** (-0.5)).T.astype(LOW)


def attend_back(qkv, bias, context, grad, totals):
    pairs, rows, width = qkv.shape
    return pl.pallas_call(
        attend_back_kernel,
        grid=(pairs,),
        in_specs=[
            pl.BlockSpec((1, rows, width), lambda p: (p, 0, 0)),
            pl.BlockSpec(bias.shape, lambda p: (0, 0)),
            pl.BlockSpec((rows, PAIR), lambda p: (0, p)),
            pl.BlockSpec((rows, PAIR), lambda p: (0, p)),
            pl.BlockSpec((1, 8, rows), lambda p: (p, 0, 0)),
        ],
        out_specs=pl.BlockSpec((1, rows, width), lambda p: (p, 0, 0)),
        out_shape=jax.ShapeDtypeStruct(qkv.shape, LOW),
        scratch_shapes=[
            pltpu.VMEM((8, rows), WIDE),
            pltpu.VMEM((PAIR, rows), LOW),
            pltpu.VMEM((2, rows, PAIR), LOW),
            pltpu.VMEM((2, rows, PAIR), LOW),
            pltpu.VMEM((PAIR, rows), WIDE),
        ],
        compiler_params=pltpu.CompilerParams(vmem_limit_bytes=48 * MIB),
    )(qkv, bias, context, grad, totals)


def place():
    me = lax.axis_index("dp")
    z, y, x = me // 4, (me // 2) % 2, me % 2
    return me, z, y, x


def line_slots(z, depth):
    slots = []
    for step in range(depth - 1):
        slots.append((z - 1 - step, z - 1 - step >= 0, 1))
        slots.append((z + 1 + step, z + 1 + step < depth, -1))
    return slots


def remote(source, target, send, receive, device):
    return pltpu.make_async_remote_copy(
        src_ref=source,
        dst_ref=target,
        send_sem=send,
        recv_sem=receive,
        device_id={"dp": device},
        device_id_type=MESH,
    )


def greet_line(me, z, y, x, depth, extra=()):
    barrier = pltpu.get_barrier_semaphore()
    for peer in (z * 4 + y * 2 + 1 - x, z * 4 + (1 - y) * 2 + x):
        pl.semaphore_signal(barrier, inc=1, device_id={"dp": peer}, device_id_type=MESH)

    @pl.when(z > 0)
    def _():
        pl.semaphore_signal(barrier, inc=1, device_id={"dp": me - 4}, device_id_type=MESH)

    @pl.when(z < depth - 1)
    def _():
        pl.semaphore_signal(barrier, inc=1, device_id={"dp": me + 4}, device_id_type=MESH)

    for peer in extra:
        pl.semaphore_signal(barrier, inc=1, device_id=peer, device_id_type=MESH)
    ends = jnp.where(z > 0, 1, 0) + jnp.where(z < depth - 1, 1, 0)
    pl.semaphore_wait(barrier, 2 + len(extra) + ends)


def other_core(source, target, send, receive):
    return pltpu.make_async_remote_copy(
        src_ref=source,
        dst_ref=target,
        send_sem=send,
        recv_sem=receive,
        device_id={"tensor": 1 - lax.axis_index("tensor")},
        device_id_type=MESH,
    )


class Gather:
    def __init__(self, depth, parts, whole, far, table, sems):
        self.whole, self.far = whole, far
        self.depth = depth
        self.me, self.z, self.y, self.x = place()
        self.x_peer = self.z * 4 + self.y * 2 + 1 - self.x
        self.y_peer = self.z * 4 + (1 - self.y) * 2 + self.x
        self.rows = whole.shape[1] // parts
        self.array = [array for array, *_ in table]
        self.a, self.b, self.ab, self.c, self.all = [], [], [], [], []
        for _, base, width, third in table:
            side = (width - third) // 2
            self.a.append((base, side))
            self.b.append((base + side, side))
            self.ab.append((base, 2 * side))
            self.c.append((base + 2 * side, third))
            self.all.append((base, width))
        (
            self.z_send, self.z_recv, self.zc_send, self.zc_recv, self.xa_send, self.xa_recv, self.yb_send, self.yb_recv,
            self.ya_send, self.ya_recv, self.xb_send, self.xb_recv, self.c_send, self.c_recv, self.far_send, self.far_recv,
        ) = sems
        self.slots = line_slots(self.z, depth)

    @staticmethod
    def semaphores(depth, pieces):
        sem = pltpu.SemaphoreType.DMA
        return [
            *[sem((pieces, depth + 1)), sem((pieces, depth))] * 2,
            *[sem((pieces, depth))] * 4,
            *[sem((pieces, depth, 2))] * 4,
            sem((pieces, 2)),
            sem((pieces, 2)),
            sem((pieces,)),
            sem((pieces,)),
        ]

    def block(self, zb, yb, xb):
        return zb * 4 + yb * 2 + xb

    def cut(self, ref, p, block, count, columns):
        first = pl.multiple_of(block * self.rows, self.rows)
        return ref.at[self.array[p], pl.ds(first, count * self.rows), pl.ds(*columns)]

    def copy(self, p, block, count, columns, send, receive, device):
        part = self.cut(self.whole, p, block, count, columns)
        return remote(part, part, send, receive, device)

    def forward(self, p, block, count, columns):
        if p == 0:
            return
        other_core(
            self.cut(self.whole, p, block, count, columns),
            self.cut(self.far, p, block, count, columns),
            self.far_send.at[p],
            self.far_recv.at[p],
        ).start()

    def far_copy(self, p):
        part = self.far.at[self.array[p], :, pl.ds(*self.all[p])]
        return other_core(part, part, self.far_send.at[p], self.far_recv.at[p])

    def z_copy(self, p, zb, way, back=False):
        block = self.block(zb, self.y, self.x)
        sem = self.depth if back else zb
        return self.copy(
            p, block, 1, self.ab[p], self.z_send.at[p, sem], self.z_recv.at[p, zb], self.me + 4 * way
        )

    def zc_copy(self, p, zb, way, back=False):
        sem = self.depth if back else zb
        return self.copy(
            p, zb * 4, 4, self.c[p], self.zc_send.at[p, sem], self.zc_recv.at[p, zb], self.me + 4 * way
        )

    def xa(self, p, zb, xb):
        block = self.block(zb, self.y, xb)
        return self.copy(
            p, block, 1, self.a[p], self.xa_send.at[p, zb], self.xa_recv.at[p, zb], self.x_peer
        )

    def yb(self, p, zb, yb):
        block = self.block(zb, yb, self.x)
        return self.copy(
            p, block, 1, self.b[p], self.yb_send.at[p, zb], self.yb_recv.at[p, zb], self.y_peer
        )

    def ya(self, p, zb, yb, xb):
        block = self.block(zb, yb, xb)
        return self.copy(
            p, block, 1, self.a[p], self.ya_send.at[p, zb, xb], self.ya_recv.at[p, zb, xb], self.y_peer
        )

    def xb(self, p, zb, yb, xb):
        block = self.block(zb, yb, xb)
        return self.copy(
            p, block, 1, self.b[p], self.xb_send.at[p, zb, yb], self.xb_recv.at[p, zb, yb], self.x_peer
        )

    def xc(self, p, xb):
        block = self.block(self.z, self.y, xb)
        return self.copy(
            p, block, 1, self.c[p], self.c_send.at[p, 0], self.c_recv.at[p, 0], self.x_peer
        )

    def yc(self, p, yb):
        block = self.block(self.z, yb, 0)
        return self.copy(
            p, block, 2, self.c[p], self.c_send.at[p, 1], self.c_recv.at[p, 1], self.y_peer
        )

    def both_ways(self, copy, act):
        @pl.when(self.z < self.depth - 1)
        def _():
            act(copy(self.z, 1))

        @pl.when(self.z > 0)
        def _():
            act(copy(self.z, -1, True))

    def spread(self, p, zb):
        self.xa(p, zb, self.x).start()
        self.yb(p, zb, self.y).start()
        self.ya(p, zb, self.y, self.x).start()
        self.xb(p, zb, self.y, self.x).start()

    def turn(self, p, zb):
        self.xa(p, zb, 1 - self.x).wait_recv()
        self.ya(p, zb, self.y, 1 - self.x).start()
        self.forward(p, self.block(zb, self.y, 1 - self.x), 1, self.a[p])
        self.yb(p, zb, 1 - self.y).wait_recv()
        self.xb(p, zb, 1 - self.y, self.x).start()
        self.forward(p, self.block(zb, 1 - self.y, self.x), 1, self.b[p])

    def at_step(self, step, act):
        for zb, valid, way in self.slots[2 * step : 2 * step + 2]:
            on = (self.z + way >= 0) & (self.z + way < self.depth)
            pl.when(valid)(functools.partial(act, zb, way, on))

    def arrive(self, p, step):
        def act(zb, way, on):
            self.z_copy(p, zb, way).wait_recv()
            pl.when(on)(lambda: self.z_copy(p, zb, way).start())
            self.spread(p, zb)
            self.forward(p, self.block(zb, self.y, self.x), 1, self.ab[p])

        self.at_step(step, act)

    def arrive_c(self, p, step):
        def act(zb, way, on):
            self.zc_copy(p, zb, way).wait_recv()
            pl.when(on)(lambda: self.zc_copy(p, zb, way).start())
            self.forward(p, zb * 4, 4, self.c[p])

        self.at_step(step, act)

    def stage(self, p, s):
        depth = self.depth
        if s == 0:
            self.both_ways(lambda *way: self.z_copy(p, *way), lambda copy: copy.start())
            self.xc(p, self.x).start()
            self.spread(p, self.z)
            self.forward(p, self.me, 1, self.all[p])
            return
        if s == 1:
            self.xc(p, 1 - self.x).wait_recv()
            self.yc(p, self.y).start()
            self.forward(p, self.block(self.z, self.y, 1 - self.x), 1, self.c[p])
        if s == 2:
            self.yc(p, 1 - self.y).wait_recv()
            self.both_ways(lambda *way: self.zc_copy(p, *way), lambda copy: copy.start())
            self.forward(p, self.block(self.z, 1 - self.y, 0), 2, self.c[p])
        if 1 <= s < depth:
            self.arrive(p, s - 1)
        if 3 <= s < depth + 2:
            self.arrive_c(p, s - 3)
        if s == 2:
            self.turn(p, self.z)
        if 3 <= s < depth + 2:
            self.at_step(s - 3, lambda zb, way, on: self.turn(p, zb))
        if s == depth + 2:
            for zb in range(depth):
                for other in range(2):
                    self.ya(p, zb, 1 - self.y, other).wait_recv()
                    self.forward(p, self.block(zb, 1 - self.y, other), 1, self.a[p])
                    self.xb(p, zb, other, 1 - self.x).wait_recv()
                    self.forward(p, self.block(zb, other, 1 - self.x), 1, self.b[p])

    def finish(self, p):
        def sent(copy):
            copy.wait_send()

        if p:
            self.far_copy(p).wait_send()
        self.both_ways(lambda *way: self.z_copy(p, *way), sent)
        self.both_ways(lambda *way: self.zc_copy(p, *way), sent)
        for zb in range(self.depth):
            self.xa(p, zb, self.x).wait_send()
            self.yb(p, zb, self.y).wait_send()
            for other in range(2):
                self.ya(p, zb, self.y, other).wait_send()
                self.xb(p, zb, other, self.x).wait_send()
        self.xc(p, self.x).wait_send()
        self.yc(p, self.y).wait_send()

        def passed(zb, way, on):
            pl.when(on)(lambda: sent(self.z_copy(p, zb, way)))
            pl.when(on)(lambda: sent(self.zc_copy(p, zb, way)))

        for step in range(self.depth - 1):
            self.at_step(step, passed)


def looped(count, body, between):
    @pl.loop(0, count)
    def _(i):
        body(i)
        for step, acts in between.items():

            @pl.when(i == step)
            def _():
                for act in acts:
                    act()


GATHER_AT = {
    "hidden": {0: [(2, 0), (1, 0)], 1: [(0, 1), (0, 2), (0, 3)], 3: [(0, 4)], 4: [(0, 5), (1, 1)]},
    "upstream": {-1: [(2, 1)], 1: [(3, 0)]},
    "project": {-1: [(4, 0), (0, 6)], 1: [(1, 2)], 5: [(2, 2)]},
    "long": {2: [(3, 1), (1, 3)], 7: [(2, 3)], 9: [(1, 4)], 14: [(2, 4)]},
    "short": {2: [(1, 5)], 3: [(3, 2)], 5: [(4, 1)]},
    "norm": {-1: [(1, 6)], 1: [(2, 5)], 3: [(3, 3)]},
    "feed": {-1: [(4, 2), (2, 6)], 0: [(3, 4)], 1: [(4, 3)], 2: [(3, 5)]},
    "last": {-1: [(3, 6), (4, 4)], 0: [(4, 5)]},
    "tail": {-1: [(4, 6)]},
}


def piece_table(width, inner):
    third = width // 8
    return (
        (0, 0, 3 * inner, third),
        (0, 3 * inner, inner, third),
        (1, 0, width, 2 * third),
        (2, 0, width // 2, third),
        (2, width // 2, width // 2, third),
    )


def chunk_columns(j, per_piece, half):
    array, at = 1 + j // per_piece, j % per_piece
    pair = per_piece // 2
    quarter = (at // pair) * per_piece * half + (at % pair) * half
    if isinstance(j, int):
        split = array > 1
        return array, quarter if split else at * half, (
            quarter + pair * half if split else (per_piece + at) * half
        )
    split = array > 1
    first = jnp.where(split, quarter, at * half)
    return array, first, first + jnp.where(split, pair, per_piece) * half


def front_kernel(
    depth, lengths_ref, dealing_ref, project_ref, merge_ref, expand_ref, reduce_ref, vectors_ref, hidden_bias_ref,
    tokens_ref, cotangent_ref,
    whole_out, far_ref, qkv_out, turned_out, upstream_out, context_out, total_out,
    acc_out, normal_out, inverse_out, low_turned_out, active_out, slope_out, far_context_out,
    whole, score_bias, token, upper, hidden, turned, upstream, qkv, context, total,
    acc, normal, inverse, low, low_turned, active, slope, far_context, merge_far, expand_buf, reduce_buf,
    local_sem, core_sem, out_sem, load_sem, chunk_sem, *sems,
):
    arrays = whole.shape[0]
    half_rows, width = tokens_ref.shape
    rows = 2 * half_rows
    pairs = qkv.shape[0]
    inner = pairs * PAIR
    both = expand_buf.shape[2]
    half = both // 2
    hidden_half = expand_ref.shape[1]
    chunks = hidden_half // half
    per_piece = chunks // (arrays - 1)
    member = lax.axis_index("tensor")
    table = piece_table(whole.shape[2], inner)
    pieces = len(table)
    lines = Gather(depth, 4 * depth, whole, far_ref, table, sems)
    me = lines.me
    tall, short = 2 * TILE, TILE // 2

    own = [
        pltpu.make_async_copy(tokens_ref, token.at[member], local_sem.at[0]),
        pltpu.make_async_copy(cotangent_ref, upper.at[member], local_sem.at[1]),
    ]
    for copy in own:
        copy.start()
    mine = pl.ds(pl.multiple_of(me * lines.rows, lines.rows), lines.rows)
    for pair in range(pairs):
        for c in range(3):
            first = (3 * pair + c) * PAIR
            whole[0, mine, first : first + PAIR] = project_ref[
                c, :, pair * PAIR : (pair + 1) * PAIR
            ].astype(LOW)
    whole[0, mine, 3 * inner :] = merge_ref[...].astype(LOW)
    for j in range(chunks):
        array, first, second = chunk_columns(j, per_piece, half)
        columns = slice(j * half, (j + 1) * half)
        whole[array, mine, first : first + half] = expand_ref[:, columns].astype(LOW)
        whole[array, mine, second : second + half] = reduce_ref[:, columns].astype(LOW)
    greet_line(me, lines.z, lines.y, lines.x, depth, [{"tensor": 1 - member}])
    crossing = [
        other_core(tokens_ref, token.at[member], core_sem.at[0, 0], core_sem.at[0, 1]),
        other_core(cotangent_ref, upper.at[member], core_sem.at[1, 0], core_sem.at[1, 1]),
    ]
    lines.stage(0, 0)
    for copy in crossing:
        copy.start()
    group = Group(lengths_ref, dealing_ref)
    score_bias[...] = group.score_bias(rows - LONGEST)
    for copy in own:
        copy.wait()

    leaving = []

    def leave(source, target):
        copy = pltpu.make_async_copy(source, target, out_sem.at[len(leaving)])
        copy.start()
        leaving.append(copy)

    def before(name):
        for stage in GATHER_AT.get(name, {}).get(-1, ()):
            lines.stage(*stage)

    def phase(name, count, body):
        between = {
            step: [functools.partial(lines.stage, *stage) for stage in stages]
            for step, stages in GATHER_AT.get(name, {}).items()
            if step >= 0
        }
        looped(count, body, between)

    def places_of(first):
        return first + lax.broadcasted_iota(jnp.int32, (TILE, 1), 0)

    def picked(index, source):
        return picked_rows(index, source.at[0]) + picked_rows(index - half_rows, source.at[1])

    def tile(step, size=TILE):
        return pl.ds(pl.multiple_of(step * size, size), size)

    def hidden_tile(step):
        index = group.moved(places_of(step * TILE), group.first, group.own)
        rows_here = picked(index, token)
        hidden[tile(step), :] = rows_here.astype(LOW)
        turned[:, tile(step)] = rows_here.T.astype(LOW)

    def upstream_tile(step):
        places = places_of(member * half_rows + step * TILE)
        index = group.moved(places, group.first, group.dealt)
        upstream[tile(step), :] = picked(index, upper).astype(LOW)

    crossing[0].wait()
    before("hidden")
    phase("hidden", rows // TILE, hidden_tile)
    leave(turned, turned_out)
    crossing[1].wait()
    before("upstream")
    phase("upstream", half_rows // TILE, upstream_tile)
    leave(upstream, upstream_out)

    def project_tile(i):
        pair, step = i // (rows // tall), lax.rem(i, rows // tall)
        at = tile(step, tall)
        columns = pl.ds(pl.multiple_of(pair * 3 * PAIR, PAIR), 3 * PAIR)
        bias_columns = pl.ds(pl.multiple_of(member * inner + pair * PAIR, PAIR), PAIR)
        bias = jnp.concatenate(
            [
                vectors_ref[0:1, bias_columns],
                jnp.zeros((1, PAIR), WIDE),
                vectors_ref[1:2, bias_columns],
            ],
            axis=1,
        )
        qkv[pair, at, :] = (dot_nn(hidden[at, :], whole[0, :, columns]) + bias).astype(LOW)

    before("project")
    phase("project", pairs * rows // tall, project_tile)
    leave(qkv, qkv_out)

    def attend_step(begin, size):
        def step_of(i):
            pair, step = i // (size // TILE), lax.rem(i, size // TILE)
            columns = pl.ds(pl.multiple_of(pair * PAIR, PAIR), PAIR)
            attend_tile(qkv, pair, score_bias, begin, size, step, context, columns, total)

        return step_of

    before("long")
    phase("long", pairs * LONGEST // TILE, attend_step(0, LONGEST))
    before("short")
    phase("short", pairs * (rows - LONGEST) // TILE, attend_step(LONGEST, rows - LONGEST))
    leave(context, context_out)
    leave(total, total_out)

    own_first = member * half_rows
    other_rows = pl.ds(pl.multiple_of((1 - member) * half_rows, half_rows), half_rows)
    crossing = other_core(context.at[other_rows], far_context, core_sem.at[2, 0], core_sem.at[2, 1])
    crossing.start()
    before("norm")
    lines.far_copy(1).wait_recv()
    merge_columns = pl.ds(whole.shape[2] - inner, inner)
    merge_copy = pltpu.make_async_copy(
        far_ref.at[0, :, merge_columns], merge_far, local_sem.at[2]
    )
    merge_copy.start()
    merge_copy.wait()
    crossing.wait()
    leave(far_context, far_context_out)

    def norm_tile(step):
        at = tile(step, short)
        own_at = pl.ds(pl.multiple_of(own_first + step * short, short), short)
        branch = dot_nt(context[own_at, :], whole[0, :, merge_columns])
        branch = branch + dot_nt(far_context[at, :], merge_far[...])
        unit, scale = norm(hidden[own_at, :].astype(WIDE) + branch + vectors_ref[2:3, :])
        normed = unit * vectors_ref[3:4, :] + vectors_ref[4:5, :]
        normal[at, :] = unit
        inverse[at, :] = jnp.broadcast_to(scale, (short, 128))
        low[at, :] = normed.astype(LOW)
        low_turned[:, at] = normed.T.astype(LOW)
        acc[at, :] = normed + vectors_ref[5:6, :]

    phase("norm", half_rows // short, norm_tile)
    leave(whole.at[0], whole_out.at[0])
    leave(normal, normal_out)
    leave(inverse, inverse_out)
    leave(low_turned, low_turned_out)

    def loads(j):
        slot = lax.rem(j, 2)
        array, *firsts = chunk_columns(j, per_piece, half)
        copies = []
        for kind, buf in enumerate((expand_buf, reduce_buf)):
            first = pl.multiple_of(firsts[kind], half)
            for side, source in enumerate((far_ref, whole)):
                copies.append(
                    pltpu.make_async_copy(
                        source.at[array, :, pl.ds(first, half)],
                        buf.at[slot, :, pl.ds(side * half, half)],
                        load_sem.at[slot, kind, side],
                    )
                )
        return copies

    def results(j):
        slot = lax.rem(j, 2)
        return [
            pltpu.make_async_copy(active.at[slot], active_out.at[j], chunk_sem.at[slot, 0]),
            pltpu.make_async_copy(slope.at[slot], slope_out.at[j], chunk_sem.at[slot, 1]),
        ]

    def chunk_of(piece, first_chunk, count):
        def chunk(i):
            j = first_chunk + i
            slot = lax.rem(j, 2)

            @pl.when(i == 0)
            def _():
                lines.far_copy(piece).wait_recv()
                for copy in loads(j):
                    copy.start()

            for copy in loads(j):
                copy.wait()

            @pl.when(i + 1 < count)
            def _():
                for copy in loads(j + 1):
                    copy.start()

            @pl.when(j >= 2)
            def _():
                for copy in results(j - 2):
                    copy.wait()

            biases = []
            for which in (1 - member, member):
                first = pl.multiple_of(which * hidden_half + j * half, half)
                biases.append(hidden_bias_ref[:, pl.ds(first, half)])
            bias = jnp.concatenate(biases, axis=1)
            for step in range(half_rows // TILE):
                at = slice(step * TILE, (step + 1) * TILE)
                value = dot_nn(low[at, :], expand_buf[slot]) + bias
                below, bell = normal_cells(value)
                held = (value * below).astype(LOW)
                active[slot, at, :] = held
                slope[slot, at, :] = (below + value * bell * 0.3989422804014327).astype(LOW)
                acc[at, :] += dot_nt(held, reduce_buf[slot])
            for copy in results(j):
                copy.start()

        return chunk

    first_chunk = 0
    for piece, name in ((2, "feed"), (3, "last"), (4, "tail")):
        count = chunks * table[piece][2] // (2 * hidden_half)
        before(name)
        phase(name, count, chunk_of(piece, first_chunk, count))
        columns = pl.ds(*lines.all[piece])
        leave(
            whole.at[lines.array[piece], :, columns],
            whole_out.at[lines.array[piece], :, columns],
        )
        first_chunk += count
    leave(acc, acc_out)
    for p in range(pieces):
        lines.finish(p)
    for j in (chunks - 2, chunks - 1):
        for copy in results(j):
            copy.wait()
    for copy in leaving:
        copy.wait()


def front(lengths, dealing, project, merge, expand, reduce, vectors, hidden_bias, tokens, cotangent, parts):
    shard_rows, hidden_half = expand.shape
    arrays, columns = 3, hidden_half
    half_rows, width = tokens.shape
    rows, pairs, depth = 2 * half_rows, project.shape[2] // PAIR, parts // 4
    inner, half = pairs * PAIR, 256
    pieces = len(piece_table(columns, inner))
    chunks, both = hidden_half // half, 2 * half
    shape, sem = jax.ShapeDtypeStruct, pltpu.SemaphoreType.DMA
    vmem, anywhere = pl.BlockSpec(memory_space=pltpu.VMEM), pl.BlockSpec(memory_space=pl.ANY)
    held = [
        ((pairs, rows, 3 * PAIR), LOW),
        ((width, rows), LOW),
        ((half_rows, width), LOW),
        ((rows, inner), LOW),
        ((pairs, 8, rows), WIDE),
        ((half_rows, width), WIDE),
        ((half_rows, width), WIDE),
        ((half_rows, 128), WIDE),
        ((width, half_rows), LOW),
        ((chunks, half_rows, both), LOW),
        ((chunks, half_rows, both), LOW),
        ((half_rows, inner), LOW),
    ]
    return pl.pallas_call(
        functools.partial(front_kernel, depth),
        in_specs=[*[pl.BlockSpec(memory_space=pltpu.SMEM)] * 2, *[vmem] * 6, *[anywhere] * 2],
        out_specs=[anywhere] * 14,
        out_shape=[
            shape((arrays, parts * shard_rows, columns), LOW),
            shape((arrays, parts * shard_rows, columns), LOW),
            *[shape(*one) for one in held],
        ],
        scratch_shapes=[
            pltpu.VMEM((arrays, parts * shard_rows, columns), LOW),
            pltpu.VMEM((rows - LONGEST, rows - LONGEST), WIDE),
            pltpu.VMEM((2, half_rows, width), LOW),
            pltpu.VMEM((2, half_rows, width), LOW),
            pltpu.VMEM((rows, width), LOW),
            pltpu.VMEM((width, rows), LOW),
            pltpu.VMEM((half_rows, width), LOW),
            pltpu.VMEM((pairs, rows, 3 * PAIR), LOW),
            pltpu.VMEM((rows, inner), LOW),
            pltpu.VMEM((pairs, 8, rows), WIDE),
            pltpu.VMEM((half_rows, width), WIDE),
            pltpu.VMEM((half_rows, width), WIDE),
            pltpu.VMEM((half_rows, 128), WIDE),
            pltpu.VMEM((half_rows, width), LOW),
            pltpu.VMEM((width, half_rows), LOW),
            pltpu.VMEM((2, half_rows, both), LOW),
            pltpu.VMEM((2, half_rows, both), LOW),
            pltpu.VMEM((half_rows, inner), LOW),
            pltpu.VMEM((width, inner), LOW),
            pltpu.VMEM((2, width, both), LOW),
            pltpu.VMEM((2, width, both), LOW),
            sem((3,)),
            sem((3, 2)),
            sem((16,)),
            sem((2, 2, 2)),
            sem((2, 2)),
            *Gather.semaphores(depth, pieces),
        ],
        compiler_params=pltpu.CompilerParams(
            collective_id=0, has_side_effects=True, vmem_limit_bytes=63 * MIB
        ),
    )(lengths, dealing, project, merge, expand, reduce, vectors, hidden_bias, tokens, cotangent)


def normal_cells(value):
    bell = jnp.exp2(value * value * (-0.5 * 1.4426950408889634))
    below = 1.0 + 0.39 * 0.7071067811865476 * jnp.abs(value)
    t = pl.reciprocal(below, approx=True)
    t = t * (2.0 - below * t)
    t = t * (2.0 - below * t)
    tail = 0.5 * -0.2275377237624147
    for factor in (
        0.8866668177122106,
        -0.6354042576077721,
        0.649562611731642,
        0.0913871257655044,
        0.23532542445435511,
    ):
        tail = tail * t + 0.5 * factor
    tail = tail * t * bell
    return jnp.where(value < 0.0, tail, 1.0 - tail), bell


def norm(values):
    center = values - jnp.mean(values, axis=1, keepdims=True)
    spread = jnp.mean(center * center, axis=1, keepdims=True)
    scale = lax.rsqrt(spread + norm_epsilon)
    return center * scale, scale


def norm_back(scaled, unit, scale):
    return scale * (
        scaled
        - jnp.mean(scaled, axis=1, keepdims=True)
        - unit * jnp.mean(scaled * unit, axis=1, keepdims=True)
    )


def feed_kernel(
    context_ref, merge_ref, merge_far_ref, whole_ref, far_ref, hidden_ref, upstream_ref, vectors_ref, bias_ref,
    encoded_ref, branch_ref, grad_ref, merge_grad_ref, expand_grad_ref, reduce_grad_ref, sums_ref, hidden_sums_ref,
    own_ctx, far_ctx, acc, normal, inverse, low, turned, late, late_turned, active, slope, inner_grad,
    expand_buf, reduce_buf, arrived, leaving, kept, done, grad_own, grad_far, merge_send, merge_recv,
    ctx_sem, load_sem, send_sem, recv_sem, out_sem, last_sem,
):
    rows = hidden_ref.shape[0]
    chunks, _, both = bias_ref.shape
    half = both // 2
    per_piece = whole_ref.shape[2] // (2 * half)
    member = lax.axis_index("tensor")
    peer = {"tensor": 1 - member}
    tall, short = 256, 128
    width = hidden_ref.shape[1]

    def across(source, target, send, receive):
        return pltpu.make_async_remote_copy(
            src_ref=source,
            dst_ref=target,
            send_sem=send,
            recv_sem=receive,
            device_id=peer,
            device_id_type=MESH,
        )

    def rows_of(which):
        return pl.ds(pl.multiple_of(which * rows, rows), rows)

    def tile(step, size):
        return pl.ds(pl.multiple_of(step * size, size), size)

    def loads(j, slot):
        piece, at = 1 + j // per_piece, lax.rem(j, per_piece) * half
        copies = []
        for kind, buf in enumerate((expand_buf, reduce_buf)):
            first = pl.multiple_of(at + kind * per_piece * half, half)
            for side, source in enumerate((far_ref, whole_ref)):
                copies.append(
                    pltpu.make_async_copy(
                        source.at[piece, :, pl.ds(first, half)],
                        buf.at[slot, :, pl.ds(side * half, half)],
                        load_sem.at[slot, kind, side],
                    )
                )
        return copies

    for copy in loads(0, 0):
        copy.start()
    barrier = pltpu.get_barrier_semaphore()
    pl.semaphore_signal(barrier, inc=1, device_id=peer, device_id_type=MESH)
    pl.semaphore_wait(barrier, 1)
    out_ctx = across(context_ref.at[rows_of(1 - member)], far_ctx, ctx_sem.at[0], ctx_sem.at[1])
    out_ctx.start()
    in_ctx = pltpu.make_async_copy(context_ref.at[rows_of(member)], own_ctx, ctx_sem.at[2])
    in_ctx.start()
    sums_ref[...] = jnp.zeros_like(sums_ref)
    in_ctx.wait()
    out_ctx.wait()

    def add_sum(row, values):
        sums_ref[row : row + 1, :] += jnp.sum(values, axis=0, keepdims=True)

    @pl.loop(0, rows // short)
    def _(step):
        at = tile(step, short)
        branch = dot_nt(own_ctx[at, :], merge_ref[...]) + dot_nt(far_ctx[at, :], merge_far_ref[...])
        unit, scale = norm(hidden_ref[at, :].astype(WIDE) + branch + vectors_ref[2:3, :])
        normed = unit * vectors_ref[3:4, :] + vectors_ref[4:5, :]
        normal[at, :] = unit
        inverse[at, :] = jnp.broadcast_to(scale, (short, 128))
        low[at, :] = normed.astype(LOW)
        turned[:, at] = normed.T.astype(LOW)
        acc[at, :] = normed + vectors_ref[5:6, :]

    @pl.loop(0, chunks)
    def _(j):
        slot = lax.rem(j, 2)
        for copy in loads(j, slot):
            copy.wait()

        @pl.when(j + 1 < chunks)
        def _():
            for copy in loads(j + 1, 1 - slot):
                copy.start()

        for step in range(rows // tall):
            at = slice(step * tall, (step + 1) * tall)
            inner = dot_nn(low[at, :], expand_buf[slot]) + bias_ref[j]
            below, bell = normal_cells(inner)
            held = (inner * below).astype(LOW)
            active[j, at, :] = held
            slope[j, at, :] = (below + inner * bell * 0.3989422804014327).astype(LOW)
            acc[at, :] += dot_nt(held, reduce_buf[slot])

    for copy in loads(0, 0):
        copy.start()

    @pl.loop(0, rows // short)
    def _(step):
        at = tile(step, short)
        unit, scale = norm(acc[at, :])
        encoded_ref[at, :] = (unit * vectors_ref[6:7, :] + vectors_ref[7:8, :]).astype(LOW)
        upper = upstream_ref[at, :].astype(WIDE)
        add_sum(6, upper * unit)
        add_sum(7, upper)
        grad = norm_back(upper * vectors_ref[6:7, :], unit, scale)
        grad_low = grad.astype(LOW)
        add_sum(5, grad_low.astype(WIDE))
        acc[at, :] = grad
        late[at, :] = grad_low
        late_turned[:, at] = grad.T.astype(LOW)

    def send(j, kind):
        return across(
            leaving.at[lax.rem(j, 2), kind],
            arrived.at[lax.rem(j, 4), kind],
            send_sem.at[lax.rem(j, 2), kind],
            recv_sem.at[lax.rem(j, 4), kind],
        )

    def store(j, kind):
        target = (expand_grad_ref, reduce_grad_ref)[kind]
        cols = pl.ds(pl.multiple_of(j * half, half), half)
        return pltpu.make_async_copy(
            done.at[lax.rem(j, 2), kind], target.at[:, cols], out_sem.at[lax.rem(j, 2), kind]
        )

    def finish(j):
        for kind in range(2):
            send(j, kind).wait_recv()

            @pl.when(j >= 2)
            def _():
                store(j - 2, kind).wait()

            @pl.loop(0, width // tall)
            def _(step):
                at = tile(step, tall)
                done[lax.rem(j, 2), kind, at, :] = (
                    kept[lax.rem(j, 2), kind, at, :]
                    + arrived[lax.rem(j, 4), kind, at, :].astype(WIDE)
                ).astype(LOW)

            store(j, kind).start()

    @pl.loop(0, chunks)
    def _(j):
        slot = lax.rem(j, 2)
        for copy in loads(j, slot):
            copy.wait()

        @pl.when(j + 1 < chunks)
        def _():
            for copy in loads(j + 1, 1 - slot):
                copy.start()

        total = jnp.zeros((1, both), WIDE)
        for step in range(rows // tall):
            at = slice(step * tall, (step + 1) * tall)
            grad = dot_nn(late[at, :], reduce_buf[slot]) * slope[j, at, :].astype(WIDE)
            grad = grad.astype(LOW)
            inner_grad[at, :] = grad
            total = total + jnp.sum(grad.astype(WIDE), axis=0, keepdims=True)
            acc[at, :] += dot_nt(grad, expand_buf[slot])
        hidden_sums_ref[j] = total

        @pl.when(j >= 2)
        def _():
            for kind in range(2):
                send(j - 2, kind).wait_send()

        for kind, (left, right) in enumerate(((turned, inner_grad), (late_turned, active.at[j]))):
            for step in range(width // tall):
                at = slice(step * tall, (step + 1) * tall)
                part = dot_nn(left[at, :], right[...])
                leaving[slot, kind, at, :] = part[:, 0:half].astype(LOW)
                kept[slot, kind, at, :] = part[:, half:both]
            send(j, kind).start()

        @pl.when(j >= 1)
        def _():
            finish(j - 1)

    @pl.loop(0, rows // short)
    def _(step):
        at = tile(step, short)
        grad = acc[at, :]
        unit = normal[at, :]
        add_sum(3, grad * unit)
        add_sum(4, grad)
        branch_grad = norm_back(grad * vectors_ref[3:4, :], unit, inverse[at, 0:1])
        branch_low = branch_grad.astype(LOW)
        add_sum(2, branch_low.astype(WIDE))
        branch_ref[at, :] = branch_grad
        turned[:, at] = branch_grad.T.astype(LOW)
        grad_far[at, :] = dot_nn(branch_low, merge_far_ref[...]).astype(LOW)
        grad_own[at, :] = dot_nn(branch_low, merge_ref[...]).astype(LOW)

    out_grad = across(grad_far, grad_ref.at[rows_of(member)], ctx_sem.at[0], ctx_sem.at[1])
    out_grad.start()
    in_grad = pltpu.make_async_copy(grad_own, grad_ref.at[rows_of(member)], ctx_sem.at[2])
    in_grad.start()
    for step in range(width // tall):
        at = slice(step * tall, (step + 1) * tall)
        merge_send[at, :] = dot_nn(turned[at, :], far_ctx[...]).astype(LOW)
    out_merge = across(merge_send, merge_recv, last_sem.at[0], last_sem.at[1])
    out_merge.start()
    finish(chunks - 1)
    for kind in range(2):
        send(chunks - 2, kind).wait_send()
        send(chunks - 1, kind).wait_send()
        store(chunks - 2, kind).wait()
        store(chunks - 1, kind).wait()
    out_merge.wait()
    for step in range(width // tall):
        at = slice(step * tall, (step + 1) * tall)
        merge_grad_ref[at, :] = (
            dot_nn(turned[at, :], own_ctx[...]) + merge_recv[at, :].astype(WIDE)
        ).astype(LOW)
    out_grad.wait()
    in_grad.wait()


def feed_block(context, whole, far, hidden_own, upstream, vectors, bias_own, bias_far):
    total_rows, inner = context.shape
    rows, width = hidden_own.shape
    hidden = bias_own.shape[0]
    merge, merge_far = whole[0, :, -inner:], far[0, :, -inner:]
    half = 256
    chunks = hidden // half
    both = 2 * half
    bias = jnp.concatenate(
        [bias_far.reshape(chunks, 1, half), bias_own.reshape(chunks, 1, half)], axis=2
    )
    vmem, anywhere = pl.BlockSpec(memory_space=pltpu.VMEM), pl.BlockSpec(memory_space=pl.ANY)
    sem = pltpu.SemaphoreType.DMA
    shape = jax.ShapeDtypeStruct
    *results, hidden_sums = pl.pallas_call(
        feed_kernel,
        in_specs=[anywhere, vmem, vmem, *[anywhere] * 2, *[vmem] * 4],
        out_specs=[vmem, vmem, anywhere, vmem, anywhere, anywhere, vmem, vmem],
        out_shape=[
            shape((rows, width), LOW),
            shape((rows, width), WIDE),
            shape((total_rows, inner), LOW),
            shape((width, inner), LOW),
            shape((width, hidden), LOW),
            shape((width, hidden), LOW),
            shape((8, width), WIDE),
            shape((chunks, 1, both), WIDE),
        ],
        scratch_shapes=[
            pltpu.VMEM((rows, inner), LOW),
            pltpu.VMEM((rows, inner), LOW),
            pltpu.VMEM((rows, width), WIDE),
            pltpu.VMEM((rows, width), WIDE),
            pltpu.VMEM((rows, 128), WIDE),
            pltpu.VMEM((rows, width), LOW),
            pltpu.VMEM((width, rows), LOW),
            pltpu.VMEM((rows, width), LOW),
            pltpu.VMEM((width, rows), LOW),
            pltpu.VMEM((chunks, rows, both), LOW),
            pltpu.VMEM((chunks, rows, both), LOW),
            pltpu.VMEM((rows, both), LOW),
            pltpu.VMEM((2, width, both), LOW),
            pltpu.VMEM((2, width, both), LOW),
            pltpu.VMEM((4, 2, width, half), LOW),
            pltpu.VMEM((2, 2, width, half), LOW),
            pltpu.VMEM((2, 2, width, half), WIDE),
            pltpu.VMEM((2, 2, width, half), LOW),
            pltpu.VMEM((rows, inner), LOW),
            pltpu.VMEM((rows, inner), LOW),
            pltpu.VMEM((width, inner), LOW),
            pltpu.VMEM((width, inner), LOW),
            sem((3,)),
            sem((2, 2, 2)),
            sem((2, 2)),
            sem((4, 2)),
            sem((2, 2)),
            sem((2,)),
        ],
        compiler_params=pltpu.CompilerParams(
            collective_id=2, has_side_effects=True, vmem_limit_bytes=60 * MIB
        ),
        cost_estimate=pl.CostEstimate(
            flops=12 * rows * width * 2 * hidden, bytes_accessed=8 * width * hidden * 4, transcendentals=0
        ),
    )(context, merge, merge_far, whole, far, hidden_own, upstream, vectors, bias)
    hidden_far = hidden_sums[:, 0, :half].reshape(-1)
    hidden_near = hidden_sums[:, 0, half:].reshape(-1)
    return (*results, hidden_near, hidden_far)


class Scatter:
    buffers = 8

    def __init__(self, depth, grads, shards, buffers, sems):
        self.depth, self.grads, self.shards = depth, grads, shards
        self.held = [buffers[8 * p : 8 * p + 8] for p in range(len(grads))]
        self.me, self.z, self.y, self.x = place()
        self.x_peer = self.z * 4 + self.y * 2 + 1 - self.x
        self.y_peer = self.z * 4 + (1 - self.y) * 2 + self.x
        self.rows = grads[0].shape[0] // (4 * depth)
        (
            self.a1_send, self.a1_recv, self.a2_send, self.a2_recv, self.b2_send, self.b2_recv, self.b1_send, self.b1_recv,
            self.z_send, self.z_recv, self.zc_send, self.zc_recv, self.c_send, self.c_recv,
        ) = sems

    @staticmethod
    def scratch(depth, rows, classes):
        found = []
        for a, b, c in classes:
            found += [
                pltpu.VMEM((depth, 2 * rows, a), LOW),
                pltpu.VMEM((depth, 2, rows, b), LOW),
                pltpu.VMEM((depth, rows, a), LOW),
                pltpu.VMEM((depth, rows, b), LOW),
                pltpu.VMEM((depth + 1, rows, a + b), LOW),
                pltpu.VMEM((depth + 1, 4 * rows, c), LOW),
                pltpu.VMEM((2 * rows, c), LOW),
                pltpu.VMEM((rows, c), LOW),
            ]
        return found

    @staticmethod
    def semaphores(depth, pieces):
        sem = pltpu.SemaphoreType.DMA
        return [
            *[sem((pieces, depth))] * 6,
            *[sem((pieces, depth, 2))] * 2,
            *[sem((pieces, depth)), sem((pieces, depth + 1))] * 2,
            sem((pieces, 2)),
            sem((pieces, 2)),
        ]

    def columns(self, p):
        a, b, c = (self.held[p][i].shape[-1] for i in (0, 1, 5))
        return pl.ds(0, a), pl.ds(a, b), pl.ds(a + b, c)

    def block(self, zb, yb, xb):
        return zb * 4 + yb * 2 + xb

    def span(self, block, count=1):
        return pl.ds(pl.multiple_of(block * self.rows, self.rows), count * self.rows)

    def add(self, put, count, *terms):
        chunk = min(count, 64)

        @pl.loop(0, count // chunk)
        def _(step):
            at = pl.multiple_of(step * chunk, chunk)
            parts = [term(at, chunk) for term in terms]
            if len(parts) > 2 or put.wide:
                parts = [part.astype(WIDE) for part in parts]
            total = parts[0]
            for part in parts[1:]:
                total = total + part
            put(at, chunk, total)

    def a1(self, p, zb):
        return remote(
            self.grads[p].at[self.span(self.block(zb, 1 - self.y, 0), 2), self.columns(p)[0]],
            self.held[p][0].at[zb],
            self.a1_send.at[p, zb],
            self.a1_recv.at[p, zb],
            self.y_peer,
        )

    def b1(self, p, zb, yb):
        return remote(
            self.grads[p].at[self.span(self.block(zb, yb, 1 - self.x)), self.columns(p)[1]],
            self.held[p][1].at[zb, yb],
            self.b1_send.at[p, zb, yb],
            self.b1_recv.at[p, zb, yb],
            self.x_peer,
        )

    def a2(self, p, zb):
        return remote(
            self.held[p][0].at[zb, self.span(1 - self.x)],
            self.held[p][2].at[zb],
            self.a2_send.at[p, zb],
            self.a2_recv.at[p, zb],
            self.x_peer,
        )

    def b2(self, p, zb):
        return remote(
            self.held[p][1].at[zb, 1 - self.y],
            self.held[p][3].at[zb],
            self.b2_send.at[p, zb],
            self.b2_recv.at[p, zb],
            self.y_peer,
        )

    def slot(self, zb, way):
        return zb if way > 0 else zb + (self.depth - zb) * jnp.where(zb == self.z - 1, 1, 0)

    def z_copy(self, p, zb, way):
        slot = self.slot(zb, way)
        return remote(
            self.held[p][4].at[zb],
            self.held[p][4].at[slot],
            self.z_send.at[p, zb],
            self.z_recv.at[p, slot],
            self.me + 4 * way,
        )

    def zc_copy(self, p, zb, way, first):
        slot = self.slot(zb, way)
        source = self.held[p][5].at[zb]
        if first:
            source = self.grads[p].at[self.span(zb * 4, 4), self.columns(p)[2]]
        return remote(
            source,
            self.held[p][5].at[slot],
            self.zc_send.at[p, zb],
            self.zc_recv.at[p, slot],
            self.me + 4 * way,
        )

    def arrived(self, ref, sem, slot):
        part = ref.at[slot]
        remote(part, part, sem, sem, self.me).wait_recv()

    def cy(self, p):
        return remote(
            self.held[p][5].at[self.z, self.span(2 * (1 - self.y), 2)],
            self.held[p][6],
            self.c_send.at[p, 0],
            self.c_recv.at[p, 0],
            self.y_peer,
        )

    def cx(self, p):
        return remote(
            self.held[p][5].at[self.z, self.span(2 * self.y + 1 - self.x)],
            self.held[p][7],
            self.c_send.at[p, 1],
            self.c_recv.at[p, 1],
            self.x_peer,
        )

    def grad(self, p, block, columns):
        def term(at, count):
            first = pl.multiple_of(block * self.rows + at, 16)
            return self.grads[p][pl.ds(first, count), columns]

        return term

    def part(self, ref, lead, block, columns=None):
        columns = slice(None) if columns is None else columns

        def term(at, count):
            first = pl.multiple_of(block * self.rows + at, 16)
            return ref[(*lead, pl.ds(first, count), columns)]

        return term

    def put(self, ref, lead, block, columns=None):
        columns = slice(None) if columns is None else columns

        def act(at, count, total):
            first = pl.multiple_of(block * self.rows + at, 16)
            ref[(*lead, pl.ds(first, count), columns)] = total.astype(ref.dtype)

        act.wide = ref.dtype == WIDE
        return act

    def open(self, p, zb):
        self.a1(p, zb).start()
        self.b1(p, zb, 0).start()
        self.b1(p, zb, 1).start()

    def first(self, p, zb):
        z, y, x = self.z, self.y, self.x
        a, b, _ = self.columns(p)
        r1a, r1b = self.held[p][0], self.held[p][1]
        self.a1(p, zb).wait_recv()
        self.add(
            self.put(r1a, (zb,), 1 - x),
            self.rows,
            self.part(r1a, (zb,), 1 - x),
            self.grad(p, self.block(zb, y, 1 - x), a),
        )
        self.a2(p, zb).start()
        self.b1(p, zb, 0).wait_recv()
        self.b1(p, zb, 1).wait_recv()
        self.add(
            self.put(r1b, (zb, 1 - y), 0),
            self.rows,
            self.part(r1b, (zb, 1 - y), 0),
            self.grad(p, self.block(zb, 1 - y, x), b),
        )
        self.b2(p, zb).start()

    def terms(self, p, zb):
        z, y, x = self.z, self.y, self.x
        a, b, _ = self.columns(p)
        r1a, r1b, r2a, r2b = self.held[p][:4]
        own = self.block(zb, y, x)
        return (
            [self.grad(p, own, a), self.part(r1a, (zb,), x), self.part(r2a, (zb,), 0)],
            [self.grad(p, own, b), self.part(r1b, (zb, y), 0), self.part(r2b, (zb,), 0)],
        )

    def pass_on(self, p, zb, way):
        a, b, _ = self.columns(p)
        rz = self.held[p][4]
        self.a2(p, zb).wait_recv()
        self.b2(p, zb).wait_recv()
        from_line = (self.z - way >= 0) & (self.z - way < self.depth)

        @pl.when(from_line)
        def _():
            self.arrived(rz, self.z_recv.at[p, zb], zb)
            for terms, columns in zip(self.terms(p, zb), (a, b), strict=True):
                self.add(
                    self.put(rz, (zb,), 0, columns),
                    self.rows,
                    *terms,
                    self.part(rz, (zb,), 0, columns),
                )

        @pl.when(jnp.logical_not(from_line))
        def _():
            for terms, columns in zip(self.terms(p, zb), (a, b), strict=True):
                self.add(self.put(rz, (zb,), 0, columns), self.rows, *terms)

        self.z_copy(p, zb, way).start()

    def pass_c(self, p, zb, way):
        c = self.columns(p)[2]
        rc = self.held[p][5]
        from_line = (self.z - way >= 0) & (self.z - way < self.depth)

        @pl.when(from_line)
        def _():
            self.arrived(rc, self.zc_recv.at[p, zb], zb)
            self.add(
                self.put(rc, (zb,), 0),
                4 * self.rows,
                self.part(rc, (zb,), 0),
                self.grad(p, zb * 4, c),
            )
            self.zc_copy(p, zb, way, False).start()

        @pl.when(jnp.logical_not(from_line))
        def _():
            self.zc_copy(p, zb, way, True).start()

    def own_c(self, p):
        z, depth = self.z, self.depth
        c = self.columns(p)[2]
        rc = self.held[p][5]
        grad = self.grad(p, z * 4, c)
        lower, upper = self.part(rc, (z,), 0), self.part(rc, (depth,), 0)
        put = self.put(rc, (z,), 0)

        @pl.when(z > 0)
        def _():
            self.arrived(rc, self.zc_recv.at[p, z], z)

        @pl.when(z < depth - 1)
        def _():
            self.arrived(rc, self.zc_recv.at[p, depth], depth)

        @pl.when((z > 0) & (z < depth - 1))
        def _():
            self.add(put, 4 * self.rows, grad, lower, upper)

        @pl.when(z == 0)
        def _():
            self.add(put, 4 * self.rows, grad, upper)

        @pl.when(z == depth - 1)
        def _():
            self.add(put, 4 * self.rows, grad, lower)

        self.cy(p).start()

    def turn_c(self, p):
        rc, rcy = self.held[p][5], self.held[p][6]
        self.cy(p).wait_recv()
        self.add(
            self.put(rc, (self.z,), 2 * self.y),
            2 * self.rows,
            self.part(rc, (self.z,), 2 * self.y),
            self.part(rcy, (), 0),
        )
        self.cx(p).start()

    def close(self, p):
        z, depth = self.z, self.depth
        a, b, c = self.columns(p)
        rz, rc, rcx = self.held[p][4], self.held[p][5], self.held[p][7]
        self.a2(p, z).wait_recv()
        self.b2(p, z).wait_recv()

        @pl.when(z > 0)
        def _():
            self.arrived(rz, self.z_recv.at[p, z], z)

        @pl.when(z < depth - 1)
        def _():
            self.arrived(rz, self.z_recv.at[p, depth], depth)

        def total(*slots):
            for terms, columns in zip(self.terms(p, z), (a, b), strict=True):
                lines = [self.part(rz, (slot,), 0, columns) for slot in slots]
                self.add(self.put(self.shards[p], (), 0, columns), self.rows, *terms, *lines)

        pl.when((z > 0) & (z < depth - 1))(lambda: total(z, depth))
        pl.when(z == 0)(lambda: total(depth))
        pl.when(z == depth - 1)(lambda: total(z))
        self.cx(p).wait_recv()
        self.add(
            self.put(self.shards[p], (), 0, c),
            self.rows,
            self.part(rc, (z,), 2 * self.y + self.x),
            self.part(rcx, (), 0),
        )

    def at_step(self, step, act):
        z, depth = self.z, self.depth
        if step < 0:
            act(z, 0)
            return
        for zb, valid, way in (
            (z + 1 + step, z + 1 + step < depth, 1),
            (z - 1 - step, z - 1 - step >= 0, -1),
        ):
            pl.when(valid)(functools.partial(act, zb, way))

    def stage(self, p, s):
        last = self.depth - 2

        def opened(step):
            self.at_step(step, lambda zb, way: self.open(p, zb))

        def added(step):
            self.at_step(step, lambda zb, way: self.first(p, zb))

        def passed(step):
            self.at_step(step, lambda zb, way: self.pass_on(p, zb, way))

        def passed_c(step):
            self.at_step(step, lambda zb, way: self.pass_c(p, zb, way))

        if s == 0:
            opened(last)
            opened(last - 1)
            passed_c(last)
            return
        if s <= last + 2:
            added(last + 1 - s)
        if last - 1 - s >= -1:
            opened(last - 1 - s)
        if last - s >= 0:
            passed_c(last - s)
        if s >= 2 and last + 2 - s >= 0:
            passed(last + 2 - s)
        if s == last + 1:
            self.own_c(p)
        if s == last + 2:
            self.turn_c(p)
        if s == last + 3:
            self.close(p)

    def sent(self, p):
        def line(zb, way):
            from_line = (self.z - way >= 0) & (self.z - way < self.depth)
            self.z_copy(p, zb, way).wait_send()
            pl.when(from_line)(lambda: self.zc_copy(p, zb, way, False).wait_send())
            pl.when(jnp.logical_not(from_line))(lambda: self.zc_copy(p, zb, way, True).wait_send())

        for zb in range(self.depth):
            self.a1(p, zb).wait_send()
            self.b1(p, zb, 0).wait_send()
            self.b1(p, zb, 1).wait_send()
            self.a2(p, zb).wait_send()
            self.b2(p, zb).wait_send()
        for step in range(self.depth - 1):
            self.at_step(step, line)
        self.cy(p).wait_send()
        self.cx(p).wait_send()


class SmallSum:
    def __init__(self, lines, buffer, send, recv):
        member = lax.axis_index("tensor")
        self.partners = [{"tensor": 1 - member}, {"dp": lines.x_peer}, {"dp": lines.y_peer}]
        for level in range(lines.depth.bit_length() - 1):
            reach = 1 << level
            way = 1 - 2 * ((lines.z // reach) % 2)
            self.partners.append({"dp": lines.me + 4 * reach * way})
        self.buffer, self.send, self.recv = buffer, send, recv

    def copy(self, step):
        return pltpu.make_async_remote_copy(
            src_ref=self.buffer.at[step],
            dst_ref=self.buffer.at[len(self.partners) + 1 + step],
            send_sem=self.send.at[step],
            recv_sem=self.recv.at[step],
            device_id=self.partners[step],
            device_id_type=MESH,
        )

    def step(self, step):
        if step:
            self.copy(step - 1).wait_recv()
            self.buffer[step] = self.buffer[step - 1] + self.buffer[len(self.partners) + step]
        if step < len(self.partners):
            self.copy(step).start()

    def sent(self):
        for step in range(len(self.partners)):
            self.copy(step).wait_send()


def adamw_update(master, moment, square, gradient, step_rate, decay_rate):
    moment_new = beta_one * moment + (1.0 - beta_one) * gradient
    square_new = beta_two * square + (1.0 - beta_two) * gradient * gradient
    moment_hat = moment_new / (1.0 - beta_one**STEP)
    square_hat = square_new / (1.0 - beta_two**STEP)
    master_new = master - step_rate * (
        moment_hat / (jnp.sqrt(square_hat) + adam_epsilon) + decay_rate * master
    )
    return (moment_new, square_new, master_new)


SCATTER_AT = {
    "reduce": {4: [(0, 0)]},
    "expand": {2: [(1, 0)], 4: [(2, 0), (0, 1), (1, 1)]},
    "norm": {-1: [(1, 2)], 1: [(2, 1)], 2: [(3, 0)], 3: [(0, 2)]},
    "attend": {1: [(2, 2), (3, 1)], 5: [(0, 3)], 8: [(2, 3)], 10: [(3, 2)], 13: [(3, 3), (4, 1)], 14: [(2, 4)], 19: [(1, 4)], 20: [(4, 2)], 22: [(3, 4)]},
    "project": {0: [(4, 0), (1, 3)], 1: [(5, 0), (1, 5)]},
    "terms": {1: [(5, 1)], 2: [(4, 3)]},
    "far": {-1: [(5, 2)], 0: [(0, 4), (2, 5)]},
    "near": {-1: [(5, 3), (3, 5)], 0: [(4, 4)]},
    "encoded": {-1: [(5, 4)], 1: [(0, 5)]},
    "end": [(5, 5), (4, 5)],
}


def back_kernel(
    depth, lengths_ref, dealing_ref, vectors_ref,
    whole_ref, far_ref, qkv_in, hidden_turned_in, upstream_in, context_in, totals_in,
    acc_in, normal_in, inverse_in, turned_in, active_in, slope_in, far_ctx_in, *rest,
):
    encoded_out, input_out, small_out, *rest = rest
    shards, rest = rest[:6], rest[6:]
    enc_pair, grad_ref, input_far, acc, arrived, merge_recv, small, score_bias, *rest = rest
    grads, rest = rest[:6], rest[6:]
    buffers, rest = rest[: 6 * Scatter.buffers], rest[6 * Scatter.buffers :]
    small_send, small_recv, in_sem, load_sem, ctx_sem, far_send, far_recv, merge_sem, enc_sem, input_sem, *sems = rest
    lines = Scatter(depth, grads, shards, buffers, sems)
    sums = SmallSum(lines, small, small_send, small_recv)
    group = Group(lengths_ref, dealing_ref)
    member = lax.axis_index("tensor")
    rows, width = acc.shape
    total_rows = 2 * rows
    chunks, _, both = active_in.shape
    half = both // 2
    per_piece = chunks // 2
    piece_span = grads[0].shape[1]
    pairs = qkv_in.shape[0]
    inner = pairs * PAIR
    tall, short = 256, 128

    def rows_of(which):
        return pl.ds(pl.multiple_of(which * rows, rows), rows)

    def tile(step, size):
        return pl.ds(pl.multiple_of(step * size, size), size)

    def fetch(source, target, sem):
        return pltpu.make_async_copy(source, target, in_sem.at[sem])

    def phase(name, count, body):
        between = {
            step: [functools.partial(lines.stage, *stage) for stage in stages]
            for step, stages in SCATTER_AT.get(name, {}).items()
        }
        for act in between.pop(-1, ()):
            act()
        looped(count, body, between)

    def places_of(first):
        return first + lax.broadcasted_iota(jnp.int32, (tall, 1), 0)

    def add_sum(row, values):
        small[0, row : row + 1, :] += jnp.sum(values, axis=0, keepdims=True)

    acc_copy = fetch(acc_in, acc, 0)
    acc_copy.start()
    greet_line(
        lines.me, lines.z, lines.y, lines.x, depth, [sums.partners[0], *sums.partners[3:]]
    )
    small[0] = jnp.zeros(small.shape[1:], WIDE)
    score_bias[...] = group.score_bias(total_rows - LONGEST)

    def feed_phase(late, late_turned, turned, upstream, active, slope, inner_grad, expand_buf, reduce_buf, leaving, encoded):
        def active_load(j):
            slot = lax.rem(j, 2)
            return [pltpu.make_async_copy(active_in.at[j], active.at[slot], load_sem.at[slot, 4])]

        def loads(j):
            slot = lax.rem(j, 2)
            array, *firsts = chunk_columns(j, per_piece, half)
            copies = [pltpu.make_async_copy(slope_in.at[j], slope.at[slot], load_sem.at[slot, 5])]
            for kind, buf in enumerate((expand_buf, reduce_buf)):
                first = pl.multiple_of(firsts[kind], half)
                for side, source in enumerate((far_ref, whole_ref)):
                    copies.append(
                        pltpu.make_async_copy(
                            source.at[array, :, pl.ds(first, half)],
                            buf.at[slot, :, pl.ds(side * half, half)],
                            load_sem.at[slot, 2 * kind + side],
                        )
                    )
            return copies

        def taken(j, load):
            for copy in load(j):
                copy.wait()

            @pl.when(j + 1 < chunks)
            def _():
                for copy in load(j + 1):
                    copy.start()

        fetches = [fetch(upstream_in, upstream, 1), fetch(turned_in, turned, 2)]
        for copy in fetches:
            copy.start()
        for copy in [*active_load(0), *loads(0)]:
            copy.start()
        acc_copy.wait()
        for copy in fetches:
            copy.wait()

        def late_tile(step):
            at = tile(step, short)
            unit, scale = norm(acc[at, :])
            encoded[at, :] = (unit * vectors_ref[6:7, :] + vectors_ref[7:8, :]).astype(LOW)
            upper = upstream[at, :].astype(WIDE)
            add_sum(6, upper * unit)
            add_sum(7, upper)
            grad = norm_back(upper * vectors_ref[6:7, :], unit, scale)
            grad_low = grad.astype(LOW)
            add_sum(5, grad_low.astype(WIDE))
            acc[at, :] = grad
            late[at, :] = grad_low
            late_turned[:, at] = grad.T.astype(LOW)

        looped(rows // short, late_tile, {})
        enc_near = pltpu.make_async_copy(encoded, enc_pair.at[member], enc_sem.at[2])
        enc_far = other_core(encoded, enc_pair.at[member], enc_sem.at[0], enc_sem.at[1])
        enc_near.start()
        enc_far.start()

        def send(k):
            slot = lax.rem(k, 2)
            return other_core(
                leaving.at[slot], arrived.at[slot], far_send.at[slot], far_recv.at[slot]
            )

        def own_columns(k):
            return pl.ds(pl.multiple_of(lax.rem(k, per_piece) * half, half), half)

        def in_piece(k, act):
            for piece in range(4):
                pl.when(k // per_piece == piece)(functools.partial(act, grads[piece]))

        def finish(k):
            send(k).wait_recv()

            def add(grad):
                @pl.loop(0, width // tall)
                def _(step):
                    at = tile(step, tall)
                    grad[at, own_columns(k)] += arrived[lax.rem(k, 2), at, :]

            in_piece(k, add)

        def products(k, left, right):
            @pl.when(k >= 2)
            def _():
                send(k - 2).wait_send()

            for step in range(width // tall):
                at = slice(step * tall, (step + 1) * tall)
                part = dot_nn(left[at, :], right[...])
                leaving[lax.rem(k, 2), at, :] = part[:, 0:half].astype(LOW)
                own = part[:, half:both].astype(LOW)

                def keep(grad, at=at, own=own):
                    grad[at, own_columns(k)] = own

                in_piece(k, keep)

            @pl.when(k >= 1)
            def _():
                finish(k - 1)

            send(k).start()

        def reduce_chunk(j):
            taken(j, active_load)
            products(j, late_turned, active.at[lax.rem(j, 2)])

        def expand_chunk(j):
            slot = lax.rem(j, 2)
            taken(j, loads)
            total = jnp.zeros((1, both), WIDE)
            for step in range(rows // tall):
                at = slice(step * tall, (step + 1) * tall)
                grad = dot_nn(late[at, :], reduce_buf[slot]) * slope[slot, at, :].astype(WIDE)
                grad = grad.astype(LOW)
                inner_grad[at, :] = grad
                total = total + jnp.sum(grad.astype(WIDE), axis=0, keepdims=True)
                acc[at, :] += dot_nt(grad, expand_buf[slot])
            for which, side in ((1 - member, 0), (member, half)):
                row = 8 + which * 2 + j // per_piece
                small[0, pl.ds(row, 1), own_columns(j)] = total[:, side : side + half]
            products(chunks + j, turned, inner_grad)

        phase("reduce", chunks, reduce_chunk)
        phase("expand", chunks, expand_chunk)
        finish(2 * chunks - 1)
        for k in (2 * chunks - 2, 2 * chunks - 1):
            send(k).wait_send()
        enc_near.wait()
        enc_far.wait()

    pl.run_scoped(
        feed_phase,
        pltpu.VMEM((rows, width), LOW),
        pltpu.VMEM((width, rows), LOW),
        pltpu.VMEM((width, rows), LOW),
        pltpu.VMEM((rows, width), LOW),
        pltpu.VMEM((2, rows, both), LOW),
        pltpu.VMEM((2, rows, both), LOW),
        pltpu.VMEM((rows, both), LOW),
        pltpu.VMEM((2, width, both), LOW),
        pltpu.VMEM((2, width, both), LOW),
        pltpu.VMEM((2, width, half), LOW),
        pltpu.VMEM((rows, width), LOW),
    )

    def merge_phase(normal, inverse, turned, near_ctx, far_ctx, merge, merge_far, grad_own, grad_far, merge_send):
        merge_columns = pl.ds(whole_ref.shape[2] - inner, inner)
        fetches = [
            fetch(normal_in, normal, 0),
            fetch(inverse_in, inverse, 1),
            fetch(context_in.at[rows_of(member)], near_ctx, 2),
            fetch(far_ctx_in, far_ctx, 3),
            fetch(whole_ref.at[0, :, merge_columns], merge, 4),
            fetch(far_ref.at[0, :, merge_columns], merge_far, 5),
        ]
        for copy in fetches:
            copy.start()
        for copy in fetches:
            copy.wait()

        def norm_tile(step):
            at = tile(step, short)
            grad = acc[at, :]
            unit = normal[at, :]
            add_sum(3, grad * unit)
            add_sum(4, grad)
            branch_grad = norm_back(grad * vectors_ref[3:4, :], unit, inverse[at, 0:1])
            branch_low = branch_grad.astype(LOW)
            add_sum(2, branch_low.astype(WIDE))
            acc[at, :] = branch_grad
            turned[:, at] = branch_grad.T.astype(LOW)
            grad_far[at, :] = dot_nn(branch_low, merge_far[...]).astype(LOW)
            grad_own[at, :] = dot_nn(branch_low, merge[...]).astype(LOW)

        phase("norm", rows // short, norm_tile)
        out_grad = other_core(grad_far, grad_ref.at[rows_of(member)], ctx_sem.at[0], ctx_sem.at[1])
        in_grad = pltpu.make_async_copy(grad_own, grad_ref.at[rows_of(member)], ctx_sem.at[2])
        out_grad.start()
        in_grad.start()
        out_merge = other_core(merge_send, merge_recv, merge_sem.at[0], merge_sem.at[1])

        def merge_step(which):
            @pl.when(which == 0)
            def _():
                for step in range(width // tall):
                    at = slice(step * tall, (step + 1) * tall)
                    merge_send[at, :] = dot_nn(turned[at, :], far_ctx[...]).astype(LOW)
                out_merge.start()

            @pl.when(which == 1)
            def _():
                out_merge.wait()
                for step in range(width // tall):
                    at = slice(step * tall, (step + 1) * tall)
                    grads[4][at, 0:inner] = (
                        dot_nn(turned[at, :], near_ctx[...]) + merge_recv[at, :].astype(WIDE)
                    ).astype(LOW)

        phase("merge", 2, merge_step)
        out_grad.wait()
        in_grad.wait()

    pl.run_scoped(
        merge_phase,
        pltpu.VMEM((rows, width), WIDE),
        pltpu.VMEM((rows, 128), WIDE),
        pltpu.VMEM((width, rows), LOW),
        pltpu.VMEM((rows, inner), LOW),
        pltpu.VMEM((rows, inner), LOW),
        pltpu.VMEM((width, inner), LOW),
        pltpu.VMEM((width, inner), LOW),
        pltpu.VMEM((rows, inner), LOW),
        pltpu.VMEM((rows, inner), LOW),
        pltpu.VMEM((width, inner), LOW),
    )
    def last_phase(mixed):
        def attend_phase(qkv, context, upper, totals, dots, key_turned, queries, uppers, query_sum, hidden_turned):
            def loads(pair, slot):
                columns = pl.ds(pl.multiple_of(pair * PAIR, PAIR), PAIR)
                return [
                    pltpu.make_async_copy(qkv_in.at[pair], qkv.at[slot], load_sem.at[slot, 0]),
                    pltpu.make_async_copy(
                        context_in.at[:, columns], context.at[slot], load_sem.at[slot, 1]
                    ),
                    pltpu.make_async_copy(
                        grad_ref.at[:, columns], upper.at[slot], load_sem.at[slot, 2]
                    ),
                ]

            fetches = [fetch(totals_in, totals, 0)]
            for copy in [*loads(0, 0), *fetches]:
                copy.start()
            for copy in fetches:
                copy.wait()
            blocks = ((0, LONGEST), (LONGEST, total_rows - LONGEST))
            per_pair = total_rows // TILE

            def hidden_tile(step, slot):
                return pltpu.make_async_copy(
                    hidden_turned_in.at[tile(step, tall), :],
                    hidden_turned.at[slot],
                    load_sem.at[slot, 3],
                )

            def project(second):
                grad, first = (grads[5], 0) if second else (grads[4], inner)
                span = (pairs // 2) * 3 * PAIR
                columns = slice(span if second else 0, span * 2 if second else span)
                hidden_tile(0, 0).start()
                for step in range(width // tall):
                    if step + 1 < width // tall:
                        hidden_tile(step + 1, (step + 1) % 2).start()
                    hidden_tile(step, step % 2).wait()
                    grad[step * tall : (step + 1) * tall, first : first + span] = dot_nn(
                        hidden_turned[step % 2], mixed[:, columns]
                    ).astype(LOW)

            def pair_body(pair):
                slot = lax.rem(pair, 2)
                for copy in loads(pair, slot):
                    copy.wait()

                @pl.when(pair + 1 < pairs)
                def _():
                    for copy in loads(pair + 1, 1 - slot):
                        copy.start()

                attend_back_open(
                    qkv.at[slot], context.at[slot], upper.at[slot], dots, key_turned, queries, uppers
                )
                base = pair * 3 * PAIR

                def columns(which):
                    return pl.ds(pl.multiple_of(base + which * PAIR, PAIR), PAIR)

                for begin, size in blocks:
                    block = slice(begin, begin + size)
                    query_sum[:, block] = jnp.zeros((PAIR, size), WIDE)

                    def key_tile(step, begin=begin, size=size):
                        at, key_sum, value_sum = attend_back_tile(
                            qkv.at[slot], score_bias, totals.at[pair], dots, key_turned, queries, uppers, query_sum,
                            begin, size, step,
                        )
                        mixed[at, columns(1)] = key_sum.astype(LOW)
                        mixed[at, columns(2)] = value_sum.astype(LOW)

                    between = {}
                    for step in range(size // TILE):
                        number = begin // TILE + step
                        for act_pair in range(pairs):
                            for p, s in SCATTER_AT["attend"].get(act_pair * per_pair + number, ()):

                                def act(act_pair=act_pair, p=p, s=s):
                                    pl.when(pair == act_pair)(lambda: lines.stage(p, s))

                                between.setdefault(step, []).append(act)
                    looped(size // TILE, key_tile, between)
                    mixed[block, columns(0)] = (
                        (query_sum[:, block] * HEAD_DIM ** (-0.5)).T.astype(LOW)
                    )
                for which, row in ((0, 0), (2, 1)):
                    part = mixed[:, columns(which)].astype(WIDE)
                    spot = pl.multiple_of(member * inner + pair * PAIR, PAIR)
                    small[0, row : row + 1, pl.ds(spot, PAIR)] = jnp.sum(
                        part, axis=0, keepdims=True
                    )

            def project_stages(second):
                return [
                    functools.partial(project, second),
                    *[functools.partial(lines.stage, *st) for st in SCATTER_AT["project"][second]],
                ]

            looped(pairs, pair_body, {1: project_stages(0), 3: project_stages(1)})

        pl.run_scoped(
            attend_phase,
            pltpu.VMEM((2, total_rows, 3 * PAIR), LOW),
            pltpu.VMEM((2, total_rows, PAIR), LOW),
            pltpu.VMEM((2, total_rows, PAIR), LOW),
            pltpu.VMEM(totals_in.shape, WIDE),
            pltpu.VMEM((8, total_rows), WIDE),
            pltpu.VMEM((PAIR, total_rows), LOW),
            pltpu.VMEM((2, total_rows, PAIR), LOW),
            pltpu.VMEM((2, total_rows, PAIR), LOW),
            pltpu.VMEM((PAIR, total_rows), WIDE),
            pltpu.VMEM((2, tall, total_rows), LOW),
        )
        sums.step(0)

        def input_phase(weight, terms, leaving):
            fetches = [
                fetch(whole_ref.at[0, :, pl.ds(0, pairs * 3 * PAIR)], weight, 0),
            ]
            for copy in fetches:
                copy.start()
            for copy in fetches:
                copy.wait()

            def term_tile(step):
                at = tile(step, tall)
                total = dot_nt(mixed[at, :], weight[...])
                own = rows // tall
                mine = step // own == member

                @pl.when(mine)
                def _():
                    terms[at, :] = (total + acc[tile(lax.rem(step, own), tall), :]).astype(LOW)

                @pl.when(jnp.logical_not(mine))
                def _():
                    terms[at, :] = total.astype(LOW)

            phase("terms", total_rows // tall, term_tile)
            sums.step(1)

            def own_rows(which, step):
                places = places_of(which * rows + step * tall)
                return picked_rows(group.moved(places, group.own, group.first), terms)

            def far_tile(step):
                leaving[tile(step, tall), :] = own_rows(1 - member, step).astype(LOW)

            phase("far", rows // tall, far_tile)
            crossing = other_core(leaving, input_far, input_sem.at[0], input_sem.at[1])
            crossing.start()
            sums.step(2)

            def near_tile(step):
                acc[tile(step, tall), :] = own_rows(member, step)

            phase("near", rows // tall, near_tile)
            sums.step(3)
            crossing.wait()
            back = fetch(input_far, leaving, 2)
            back.start()
            back.wait()

            @pl.loop(0, rows // short)
            def _(step):
                at = tile(step, short)
                leaving[at, :] = (acc[at, :] + leaving[at, :].astype(WIDE)).astype(LOW)

            done = fetch(leaving, input_out, 2)
            done.start()
            done.wait()

        pl.run_scoped(
            input_phase,
            pltpu.VMEM((width, pairs * 3 * PAIR), LOW),
            pltpu.VMEM((total_rows, width), LOW),
            pltpu.VMEM((rows, width), LOW),
        )

    pl.run_scoped(last_phase, pltpu.VMEM((total_rows, pairs * 3 * PAIR), LOW))

    def end_phase(pair, encoded):
        fetches = [fetch(enc_pair.at[i], pair.at[rows_of(i)], i) for i in range(2)]
        for copy in fetches:
            copy.start()
        for copy in fetches:
            copy.wait()

        def encoded_tile(step):
            places = places_of(member * rows + step * tall)
            index = group.moved(places, group.dealt, group.first)
            encoded[tile(step, tall), :] = picked_rows(index, pair).astype(LOW)

        phase("encoded", rows // tall, encoded_tile)
        done = fetch(encoded, encoded_out, 2)
        done.start()
        for step in range(4, len(sums.partners) + 1):
            sums.step(step)
        small_out[...] = small[len(sums.partners)]
        for st in SCATTER_AT["end"]:
            lines.stage(*st)
        done.wait()

    pl.run_scoped(
        end_phase, pltpu.VMEM((total_rows, width), LOW), pltpu.VMEM((rows, width), LOW)
    )
    sums.sent()
    for p in range(len(grads)):
        lines.sent(p)


def finish_kernel(
    small_ref, vectors_ref, vectors_first, vectors_second, hidden_ref, hidden_first, hidden_second, *rest
):
    shards, (encoded_in, input_in), states_in, rest = rest[:6], rest[6:8], rest[8:20], rest[20:]
    encoded_out, input_out, vector_grad_ref, *rest = rest
    states_out, small_out, ins, outs = rest[:12], rest[12:18], rest[18:30], rest[30:42]
    held, state_sem, out_sem, pass_sem = rest[42:]
    width = vectors_ref.shape[1]
    inner = ins[3].shape[1]
    pairs = inner // PAIR
    span = shards[0].shape[1]
    loads = [pltpu.make_async_copy(states_in[i], ins[i], state_sem.at[i]) for i in range(12)]
    writes = [pltpu.make_async_copy(outs[i], states_out[i], out_sem.at[i]) for i in range(12)]
    rows_in = [
        pltpu.make_async_copy(one, held.at[i], pass_sem.at[0, i])
        for i, one in enumerate((encoded_in, input_in))
    ]
    passes = [
        pltpu.make_async_copy(held.at[i], one, pass_sem.at[1, i])
        for i, one in enumerate((encoded_out, input_out))
    ]
    for copy in [*rows_in, *reversed(loads)]:
        copy.start()
    vector_grad_ref[...] = small_ref[0:8, :]
    states = vectors_ref[...], vectors_first[...], vectors_second[...]
    for i, value in enumerate(adamw_update(*states, small_ref[0:8, :], rate_vectors, 0.0)):
        small_out[i][...] = value
    for i in range(hidden_ref.shape[1] // width):
        columns = slice(i * width, (i + 1) * width)
        states = hidden_ref[:, columns], hidden_first[:, columns], hidden_second[:, columns]
        grad = small_ref[8 + i : 9 + i, :]
        for n, value in enumerate(adamw_update(*states, grad, rate_hidden, 0.0)):
            small_out[3 + n][:, columns] = value

    def update(matrix, lead, columns, grad, grad_columns):
        rate = (rate_project, rate_merge, rate_expand, rate_reduce)[matrix]

        @pl.loop(0, grad.shape[0] // 16)
        def _(step):
            at = pl.ds(pl.multiple_of(step * 16, 16), 16)
            old = [ins[3 * matrix + i][(*lead, at, columns)] for i in range(3)]
            new = adamw_update(*old, grad[at, grad_columns], rate, weight_decay)
            for i in range(3):
                outs[3 * matrix + i][(*lead, at, columns)] = new[i]

    for matrix in (3, 2, 1, 0):
        mine = slice(3 * matrix, 3 * matrix + 3)
        for copy in loads[mine]:
            copy.wait()
        if matrix >= 2:
            for i in range(2):
                columns = slice(i * span, (i + 1) * span)
                update(matrix, (), columns, shards[2 * (3 - matrix) + i], slice(0, span))
        elif matrix == 1:
            update(matrix, (), slice(0, inner), shards[4], slice(0, inner))
        else:
            for pair in range(pairs):
                piece, begin = (4, inner) if pair < pairs // 2 else (5, 0)
                for c in range(3):
                    at = begin + (3 * (pair % (pairs // 2)) + c) * PAIR
                    columns = slice(pair * PAIR, (pair + 1) * PAIR)
                    update(matrix, (c,), columns, shards[piece], slice(at, at + PAIR))
        for copy in writes[mine]:
            copy.start()
        if matrix == 3:
            for copy in rows_in:
                copy.wait()
            for copy in passes:
                copy.start()
    for copy in [*writes, *passes]:
        copy.wait()


def finish(small, shards, rows_out, matrices, vectors, hidden):
    states = [one for matrix in matrices for one in matrix]
    shape, sem = jax.ShapeDtypeStruct, pltpu.SemaphoreType.DMA
    vmem, anywhere = pl.BlockSpec(memory_space=pltpu.VMEM), pl.BlockSpec(memory_space=pl.ANY)
    held = [pltpu.VMEM(one.shape, WIDE) for one in states]
    return pl.pallas_call(
        finish_kernel,
        in_specs=[*[vmem] * 13, *[anywhere] * 14],
        out_specs=[*[anywhere] * 2, vmem, *[anywhere] * 12, *[vmem] * 6],
        out_shape=[
            *[shape(one.shape, LOW) for one in rows_out],
            shape((8, small.shape[1]), WIDE),
            *[shape(one.shape, WIDE) for one in (*states, *vectors, *hidden)],
        ],
        scratch_shapes=[
            *held,
            *held,
            pltpu.VMEM((2, *rows_out[0].shape), LOW),
            sem((12,)),
            sem((12,)),
            sem((2, 2)),
        ],
        compiler_params=pltpu.CompilerParams(vmem_limit_bytes=63 * MIB),
    )(small, *vectors, *hidden, *shards, *rows_out, *states)


def back(lengths, dealing, vectors, whole, far, kept, parts):
    qkv, hidden_turned, upstream, context, totals, acc, *_ = kept
    rows, width = acc.shape
    total_rows, inner = context.shape
    depth, shard_rows = parts // 4, width // parts
    half, pair_span = 256, 3 * PAIR * (qkv.shape[0] // 2)
    piece_span = whole.shape[2] // 2
    spans = (*[piece_span] * 4, inner + pair_span, pair_span)
    classes = []
    for span in spans:
        third = max(128, span // 5 // 128 * 128)
        if (span - third) % 256:
            third += 128
        classes.append(((span - third) // 2, (span - third) // 2, third))
    shape, sem = jax.ShapeDtypeStruct, pltpu.SemaphoreType.DMA
    vmem, anywhere = pl.BlockSpec(memory_space=pltpu.VMEM), pl.BlockSpec(memory_space=pl.ANY)
    steps = 3 + depth.bit_length() - 1
    results = pl.pallas_call(
        functools.partial(back_kernel, depth),
        in_specs=[
            *[pl.BlockSpec(memory_space=pltpu.SMEM)] * 2,
            vmem,
            *[anywhere] * (2 + len(kept)),
        ],
        out_specs=[*[anywhere] * 2, *[vmem] * (1 + len(spans)), *[anywhere] * 3],
        out_shape=[
            shape((rows, width), LOW),
            shape((rows, width), LOW),
            shape((16, width), WIDE),
            *[shape((shard_rows, span), WIDE) for span in spans],
            shape((2, rows, width), LOW),
            shape((total_rows, inner), LOW),
            shape((rows, width), LOW),
        ],
        scratch_shapes=[
            pltpu.VMEM((rows, width), WIDE),
            pltpu.VMEM((2, width, half), LOW),
            pltpu.VMEM((width, inner), LOW),
            pltpu.VMEM((2 * steps + 1, 16, width), WIDE),
            pltpu.VMEM((total_rows - LONGEST, total_rows - LONGEST), WIDE),
            *[pltpu.VMEM((width, span), LOW) for span in spans],
            *Scatter.scratch(depth, shard_rows, classes),
            sem((steps,)),
            sem((steps,)),
            sem((6,)),
            sem((2, 6)),
            sem((3,)),
            sem((2,)),
            sem((2,)),
            sem((2,)),
            sem((3,)),
            sem((2,)),
            *Scatter.semaphores(depth, len(spans)),
        ],
        compiler_params=pltpu.CompilerParams(
            collective_id=1, has_side_effects=True, vmem_limit_bytes=63 * MIB
        ),
    )(lengths, dealing, vectors, whole, far, *kept)
    return results[:2], results[2], results[3 : 3 + len(spans)]


def by_kernels(tokens, cotangent, lengths, dealing, project, merge, expand, reduce, vectors, hidden, parts):
    hidden = tuple(one.reshape(1, -1) for one in hidden)
    matrices = (project, merge, expand, reduce)
    whole, far, *kept = front(
        lengths, dealing, *[one[0] for one in matrices], vectors[0], hidden[0], tokens, cotangent, parts
    )
    rows_out, small, shards = back(lengths, dealing, vectors[0], whole, far, kept, parts)
    results = finish(small, shards, rows_out, matrices, vectors, hidden)
    encoded, input_grad, vector_grad = results[:3]
    news = [results[3 + 3 * i : 6 + 3 * i] for i in range(6)]
    return (
        encoded,
        input_grad,
        *news[0],
        *[one.T for one in news[1]],
        *news[2],
        *[one.T for one in news[3]],
        *news[4],
        *[one.reshape(-1) for one in news[5]],
        vector_grad,
    )


def local(
    tokens,
    cotangent,
    lengths,
    dealing,
    project_weight,
    project_first,
    project_second,
    merge_weight,
    merge_first,
    merge_second,
    expand_weight,
    expand_first,
    expand_second,
    reduce_weight,
    reduce_first,
    reduce_second,
    vectors,
    vector_first,
    vector_second,
    hidden_bias,
    hidden_first,
    hidden_second,
):
    parts = lax.axis_size("dp")
    member = lax.axis_index("tensor")
    other = 1 - member
    half_rows, model_width = tokens.shape
    total_rows = 2 * half_rows
    width_half = project_weight.shape[2]
    pairs = width_half // PAIR
    hidden_half = expand_weight.shape[1]
    shard_rows = expand_weight.shape[0]
    own_begin = member * half_rows
    by_kernel = parts % 4 == 0 and (parts & (parts - 1)) == 0 and shard_rows % 16 == 0

    def swap(value):
        return lax.ppermute(value, "tensor", [(0, 1), (1, 0)])

    def own(value, size, which=member):
        return lax.dynamic_slice_in_dim(value, which * size, size, 0)

    if by_kernel:
        return by_kernels(
            tokens, cotangent, lengths, dealing,
            (project_weight, project_first, project_second),
            (merge_weight.T, merge_first.T, merge_second.T),
            (expand_weight, expand_first, expand_second),
            (reduce_weight.T, reduce_first.T, reduce_second.T),
            (vectors, vector_first, vector_second),
            (hidden_bias, hidden_first, hidden_second),
            parts,
        )

    segment, own_of, dealt_of, from_own, from_dealt = layout(lengths[0], dealing[0], total_rows)
    dealt_of = own(dealt_of, half_rows)
    short = segment[LONGEST:]
    score_bias = jnp.where(short[:, None] == short[None, :], 0.0, masked_score).astype(WIDE)

    def own_first(index):
        return lax.rem(index - own_begin + total_rows, total_rows)

    projections = (
        project_weight.reshape(3, shard_rows, pairs, PAIR)
        .transpose(1, 2, 0, 3)
        .reshape(shard_rows, 3 * width_half)
    )
    quarter = hidden_half // 2
    reduce_turned = reduce_weight.T
    shards = jnp.stack(
        [
            jnp.concatenate([projections, merge_weight.T], axis=1),
            jnp.concatenate([expand_weight[:, :quarter], reduce_turned[:, :quarter]], axis=1),
            jnp.concatenate([expand_weight[:, quarter:], reduce_turned[:, quarter:]], axis=1),
        ]
    ).astype(LOW)
    zeros_pair = jnp.zeros((pairs, PAIR), WIDE)
    bias_row = jnp.concatenate(
        [
            own(vectors[0], width_half).reshape(pairs, PAIR),
            zeros_pair,
            own(vectors[1], width_half).reshape(pairs, PAIR),
        ],
        axis=1,
    ).reshape(pairs, 1, 3 * PAIR)
    whole = lax.all_gather(shards, "dp", axis=1, tiled=True)
    far = swap(whole)
    token_pair = jnp.concatenate([tokens, swap(tokens)], axis=0)
    upper_pair = jnp.concatenate([cotangent, swap(cotangent)], axis=0)
    hidden = dot_nn(pick_rows(own_first(own_of), total_rows), token_pair).astype(LOW)
    upstream = dot_nn(pick_rows(own_first(dealt_of), total_rows), upper_pair).astype(LOW)
    qkv = jnp.einsum(
        "rd,dpc->prc",
        hidden,
        whole[0, :, : 3 * width_half].reshape(model_width, pairs, 3 * PAIR),
        preferred_element_type=WIDE,
    )
    qkv = (qkv + bias_row).astype(LOW)
    context, totals = attend(qkv, score_bias)

    (
        encoded, branch_grad, context_grad, merge_grad, expand_grad, reduce_grad, sums, hidden_part_own, hidden_part_far,
    ) = feed_block(
        context,
        whole,
        far,
        own(hidden, half_rows),
        upstream,
        vectors,
        own(hidden_bias, hidden_half),
        own(hidden_bias, hidden_half, other),
    )
    encoded_pair = jnp.concatenate([encoded, swap(encoded)], axis=0)
    encoded_out = dot_nn(
        pick_rows(own_first(own(from_dealt, half_rows)), total_rows), encoded_pair
    ).astype(LOW)
    mixed_grads = attend_back(qkv, score_bias, context, context_grad, totals)
    mixed_sums = jnp.sum(mixed_grads.astype(WIDE), axis=1).reshape(pairs, 3, PAIR)
    mixed_grads = mixed_grads.transpose(1, 0, 2).reshape(total_rows, 3 * width_half)
    project_grad = dot_tn(hidden, mixed_grads)
    input_terms = dot_nt(mixed_grads, whole[0, :, : 3 * width_half])
    own_part = own(input_terms, half_rows) + branch_grad
    input_terms = lax.dynamic_update_slice_in_dim(input_terms, own_part, own_begin, 0).astype(LOW)
    input_far = swap(
        dot_nn(pick_rows(own(from_own, half_rows, other), total_rows), input_terms).astype(LOW)
    )
    input_grad = (
        dot_nn(pick_rows(own(from_own, half_rows), total_rows), input_terms)
        + input_far.astype(WIDE)
    ).astype(LOW)
    zeros_width = jnp.zeros((model_width,), WIDE)
    zeros_hidden = jnp.zeros_like(hidden_bias)
    hidden_total = lax.dynamic_update_slice_in_dim(
        lax.dynamic_update_slice_in_dim(
            zeros_hidden, hidden_part_own, member * hidden_half, 0
        ),
        hidden_part_far,
        other * hidden_half,
        0,
    )
    vector_rows = [
        lax.dynamic_update_slice_in_dim(
            zeros_width, mixed_sums[:, c].reshape(-1), member * width_half, 0
        )
        for c in (0, 2)
    ]
    small = jnp.concatenate(
        [
            jnp.stack(vector_rows),
            sums[2:],
            hidden_total.reshape(-1, model_width),
            jnp.zeros((4, model_width), WIDE),
        ],
        axis=0,
    )
    grads = [
        lax.psum_scatter(g.astype(LOW), "dp", scatter_dimension=0, tiled=True).astype(WIDE)
        for g in (project_grad, merge_grad, expand_grad, reduce_grad)
    ]
    small = lax.psum(small, ("dp", "tensor"))
    project_shard, merge_shard, expand_shard, reduce_shard = grads
    project_shard = (
        project_shard.reshape(shard_rows, pairs, 3, PAIR)
        .transpose(2, 0, 1, 3)
        .reshape(3, shard_rows, width_half)
    )
    vector_grad = small[:8]
    hidden_grad = small[8:12].reshape(-1)
    return (
        encoded_out,
        input_grad,
        *adamw_update(
            project_weight, project_first, project_second, project_shard, rate_project, weight_decay
        ),
        *adamw_update(
            merge_weight, merge_first, merge_second, merge_shard.T, rate_merge, weight_decay
        ),
        *adamw_update(
            expand_weight, expand_first, expand_second, expand_shard, rate_expand, weight_decay
        ),
        *adamw_update(
            reduce_weight, reduce_first, reduce_second, reduce_shard.T, rate_reduce, weight_decay
        ),
        *adamw_update(vectors, vector_first, vector_second, vector_grad, rate_vectors, 0.0),
        *adamw_update(hidden_bias, hidden_first, hidden_second, hidden_grad, rate_hidden, 0.0),
        vector_grad,
    )


def solution(mesh):
    sharded = (
        P("dp", None),
        P("dp", None),
        *[P(None, "dp", "tensor")] * 3,
        *[P("tensor", "dp")] * 3,
        *[P("dp", "tensor")] * 3,
        *[P("tensor", "dp")] * 3,
        *[P()] * 6,
    )
    rows = P(("dp", "tensor"), None)
    return jax.shard_map(
        local,
        mesh=mesh,
        in_specs=(rows, rows, *sharded),
        out_specs=(rows, rows, *sharded[2:], P()),
        check_vma=False,
    )
```

```python
import functools

import jax
import jax.numpy as jnp
from jax import lax
from jax.experimental import pallas as pl
from jax.experimental.pallas import tpu as pltpu
from jax.sharding import PartitionSpec as P

HEAD_DIM = 64
LONGEST = 1024
STEP = 10
PAIR = 2 * HEAD_DIM
TILE = 256
MIB = 1024 * 1024
MESH = pl.DeviceIdType.MESH
LOW = jnp.bfloat16
WIDE = jnp.float32

beta_one = 0.9
beta_two = 0.999
adam_epsilon = 1e-08
weight_decay = 0.01
norm_epsilon = 1e-05
masked_score = -1e30
rate_project = 0.03
rate_merge = 0.3
rate_expand = 0.03
rate_reduce = 0.015
rate_vectors = 0.4
rate_hidden = 0.1


def dot_nn(a, b):
    return jnp.dot(a, b, preferred_element_type=WIDE)


def dot_nt(a, b):
    return lax.dot_general(a, b, (((1,), (1,)), ((), ())), preferred_element_type=WIDE)


def dot_tn(a, b):
    return lax.dot_general(a, b, (((0,), (0,)), ((), ())), preferred_element_type=WIDE)


def layout(lengths_row, dealing_row, total_rows):
    slots = jnp.arange(lengths_row.shape[0], dtype=jnp.int32)
    places = jnp.arange(total_rows, dtype=jnp.int32)
    rank_of = jnp.sum(jnp.where(dealing_row[None, :] == slots[:, None], slots[None, :], 0), axis=1)
    own_start = jnp.cumsum(lengths_row) - lengths_row
    dealt_start = jnp.sum(
        jnp.where(rank_of[None, :] < rank_of[:, None], lengths_row[None, :], 0), axis=1
    )
    longest = lengths_row == LONGEST
    short = jnp.where(longest, 0, lengths_row)
    start = jnp.where(longest, 0, LONGEST + jnp.cumsum(short) - short)

    def inside(begin):
        return (places[:, None] >= begin[None, :]) & (
            places[:, None] < (begin + lengths_row)[None, :]
        )

    def moved(begin, end):
        return places + jnp.sum(jnp.where(inside(begin), (end - begin)[None, :], 0), axis=1)

    segment = jnp.sum(jnp.where(inside(start), slots[None, :], 0), axis=1)
    return (
        segment,
        moved(start, own_start),
        moved(start, dealt_start),
        moved(own_start, start),
        moved(dealt_start, start),
    )


def pick_rows(index, rows):
    places = jnp.arange(rows, dtype=jnp.int32)
    return (index[:, None] == places[None, :]).astype(LOW)


class Group:
    def __init__(self, lengths_ref, dealing_ref):
        count = lengths_ref.shape[1]
        self.lengths = [lengths_ref[0, s] for s in range(count)]
        order = [dealing_ref[0, i] for i in range(count)]
        rank = [sum(jnp.where(order[i] == s, i, 0) for i in range(count)) for s in range(count)]
        short = [jnp.where(length == LONGEST, 0, length) for length in self.lengths]
        self.own, self.dealt, self.first = [], [], []
        own = own_short = jnp.int32(0)
        for s in range(count):
            self.own.append(own)
            self.first.append(jnp.where(self.lengths[s] == LONGEST, 0, LONGEST + own_short))
            self.dealt.append(
                sum(jnp.where(rank[j] < rank[s], self.lengths[j], 0) for j in range(count))
            )
            own, own_short = own + self.lengths[s], own_short + short[s]

    def inside(self, places, begin, s):
        return (places >= begin[s]) & (places < begin[s] + self.lengths[s])

    def moved(self, places, begin, end):
        total = places
        for s in range(len(begin)):
            total = total + jnp.where(self.inside(places, begin, s), end[s] - begin[s], 0)
        return total

    def score_bias(self, count):
        sides = []
        for shape, axis in (((count, 1), 0), ((1, count), 1)):
            places = lax.broadcasted_iota(jnp.int32, shape, axis) + LONGEST
            segment = jnp.zeros_like(places)
            for s in range(len(self.first)):
                segment = segment + jnp.where(self.inside(places, self.first, s), s, 0)
            sides.append(segment)
        return jnp.where(sides[0] == sides[1], 0.0, masked_score).astype(WIDE)


def picked_rows(index, source):
    places = lax.broadcasted_iota(jnp.int32, (index.shape[0], source.shape[0]), 1)
    return dot_nn(jnp.where(index == places, 1.0, 0.0).astype(LOW), source[...])


def attend_tile(qkv_ref, pair, bias_ref, begin, size, step, context_ref, columns, total_ref):
    lane = lax.broadcasted_iota(jnp.int32, (1, PAIR), 1)
    scale = HEAD_DIM ** (-0.5)
    first = pl.multiple_of(begin + step * TILE, TILE)
    query = qkv_ref[pair, pl.ds(first, TILE), 0:PAIR]
    key = qkv_ref[pair, begin : begin + size, PAIR : 2 * PAIR]
    value = qkv_ref[pair, begin : begin + size, 2 * PAIR : 3 * PAIR]
    outcome = []
    chosen = [jnp.where(lane // HEAD_DIM == head, scale, 0.0).astype(LOW) for head in range(2)]
    scores = [dot_nt(query * chosen[head], key) for head in range(2)]
    for head in range(2):
        score = scores[head]
        if begin:
            inner = pl.multiple_of(step * TILE, TILE)
            score = score + bias_ref[pl.ds(inner, TILE), :]
        top = jnp.max(score, axis=1, keepdims=True)
        exponent = jnp.exp(score - top)
        total = jnp.sum(exponent, axis=1, keepdims=True)
        outcome.append(dot_nn(exponent.astype(LOW), value) / total)
        log_total = jnp.broadcast_to(top + jnp.log(total), (TILE, PAIR))
        total_ref[pair, head : head + 1, pl.ds(first, TILE)] = log_total.T[0:1, :]
    context_ref[pl.ds(first, TILE), columns] = jnp.where(
        lane < HEAD_DIM, outcome[0], outcome[1]
    ).astype(LOW)


def attend_kernel(qkv_ref, bias_ref, context_ref, total_ref):
    rows = qkv_ref.shape[1]
    for begin, size in ((0, LONGEST), (LONGEST, rows - LONGEST)):

        @pl.loop(0, size // TILE)
        def _(step):
            attend_tile(
                qkv_ref, 0, bias_ref, begin, size, step, context_ref, slice(0, PAIR), total_ref
            )


def attend(qkv, bias):
    pairs, rows, width = qkv.shape
    return pl.pallas_call(
        attend_kernel,
        grid=(pairs,),
        in_specs=[
            pl.BlockSpec((1, rows, width), lambda p: (p, 0, 0)),
            pl.BlockSpec(bias.shape, lambda p: (0, 0)),
        ],
        out_specs=[
            pl.BlockSpec((rows, PAIR), lambda p: (0, p)),
            pl.BlockSpec((1, 8, rows), lambda p: (p, 0, 0)),
        ],
        out_shape=[
            jax.ShapeDtypeStruct((rows, pairs * PAIR), LOW),
            jax.ShapeDtypeStruct((pairs, 8, rows), WIDE),
        ],
        compiler_params=pltpu.CompilerParams(vmem_limit_bytes=48 * MIB),
    )(qkv, bias)


def attend_back_open(qkv_ref, context_ref, upper_ref, dots, key_turned, queries, uppers):
    lane = lax.broadcasted_iota(jnp.int32, (1, PAIR), 1)
    product = (upper_ref[...].astype(WIDE) * context_ref[...].astype(WIDE)).T
    for head in range(2):
        band = slice(head * HEAD_DIM, (head + 1) * HEAD_DIM)
        dots[head : head + 1, :] = jnp.sum(product[band, :], axis=0, keepdims=True)
        chosen = lane // HEAD_DIM == head
        queries[head] = qkv_ref[:, 0:PAIR] * jnp.where(chosen, HEAD_DIM ** (-0.5), 0.0).astype(LOW)
        uppers[head] = upper_ref[...] * jnp.where(chosen, 1.0, 0.0).astype(LOW)
    key_turned[...] = qkv_ref[:, PAIR : 2 * PAIR].astype(WIDE).T.astype(LOW)


def attend_back_tile(
    qkv_ref, bias_ref, total_ref, dots, key_turned, queries, uppers, query_sum, begin, size, step
):
    block = slice(begin, begin + size)
    first = pl.multiple_of(begin + step * TILE, TILE)
    key = qkv_ref[pl.ds(first, TILE), PAIR : 2 * PAIR]
    value = qkv_ref[pl.ds(first, TILE), 2 * PAIR : 3 * PAIR]
    key_sum = jnp.zeros((TILE, PAIR), WIDE)
    value_sum = jnp.zeros((TILE, PAIR), WIDE)
    scores = [dot_nt(key, queries[head, block, :]) for head in range(2)]
    weight_grads = [dot_nt(value, uppers[head, block, :]) for head in range(2)]
    for head in range(2):
        band = slice(head * HEAD_DIM, (head + 1) * HEAD_DIM)
        score = scores[head]
        if begin:
            inner = pl.multiple_of(step * TILE, TILE)
            score = score + bias_ref[pl.ds(inner, TILE), :]
        probability = jnp.exp(score - total_ref[head : head + 1, block])
        score_grads = probability * (weight_grads[head] - dots[head : head + 1, block])
        score_grads = score_grads.astype(LOW)
        value_sum = value_sum + dot_nn(probability.astype(LOW), uppers[head, block, :])
        key_sum = key_sum + dot_nn(score_grads, queries[head, block, :])
        query_sum[band, block] += dot_nn(key_turned[band, pl.ds(first, TILE)], score_grads)
    return pl.ds(first, TILE), key_sum, value_sum


def attend_back_kernel(
    qkv_ref, bias_ref, context_ref, grad_ref, total_ref, out_ref, dots, key_turned, queries, uppers, query_sum
):
    rows = qkv_ref.shape[1]
    qkv = qkv_ref.at[0]
    attend_back_open(qkv, context_ref, grad_ref, dots, key_turned, queries, uppers)
    for begin, size in ((0, LONGEST), (LONGEST, rows - LONGEST)):
        block = slice(begin, begin + size)
        query_sum[:, block] = jnp.zeros((PAIR, size), WIDE)

        @pl.loop(0, size // TILE)
        def _(step):
            at, key_sum, value_sum = attend_back_tile(
                qkv, bias_ref, total_ref.at[0], dots, key_turned, queries, uppers, query_sum, begin, size, step
            )
            out_ref[0, at, PAIR : 2 * PAIR] = key_sum.astype(LOW)
            out_ref[0, at, 2 * PAIR : 3 * PAIR] = value_sum.astype(LOW)

        out_ref[0, block, 0:PAIR] = (query_sum[:, block] * HEAD_DIM ** (-0.5)).T.astype(LOW)


def attend_back(qkv, bias, context, grad, totals):
    pairs, rows, width = qkv.shape
    return pl.pallas_call(
        attend_back_kernel,
        grid=(pairs,),
        in_specs=[
            pl.BlockSpec((1, rows, width), lambda p: (p, 0, 0)),
            pl.BlockSpec(bias.shape, lambda p: (0, 0)),
            pl.BlockSpec((rows, PAIR), lambda p: (0, p)),
            pl.BlockSpec((rows, PAIR), lambda p: (0, p)),
            pl.BlockSpec((1, 8, rows), lambda p: (p, 0, 0)),
        ],
        out_specs=pl.BlockSpec((1, rows, width), lambda p: (p, 0, 0)),
        out_shape=jax.ShapeDtypeStruct(qkv.shape, LOW),
        scratch_shapes=[
            pltpu.VMEM((8, rows), WIDE),
            pltpu.VMEM((PAIR, rows), LOW),
            pltpu.VMEM((2, rows, PAIR), LOW),
            pltpu.VMEM((2, rows, PAIR), LOW),
            pltpu.VMEM((PAIR, rows), WIDE),
        ],
        compiler_params=pltpu.CompilerParams(vmem_limit_bytes=48 * MIB),
    )(qkv, bias, context, grad, totals)


def place():
    me = lax.axis_index("dp")
    z, y, x = me // 4, (me // 2) % 2, me % 2
    return me, z, y, x


def line_slots(z, depth):
    slots = []
    for step in range(depth - 1):
        slots.append((z - 1 - step, z - 1 - step >= 0, 1))
        slots.append((z + 1 + step, z + 1 + step < depth, -1))
    return slots


def remote(source, target, send, receive, device):
    return pltpu.make_async_remote_copy(
        src_ref=source,
        dst_ref=target,
        send_sem=send,
        recv_sem=receive,
        device_id={"dp": device},
        device_id_type=MESH,
    )


def greet_line(me, z, y, x, depth, extra=()):
    barrier = pltpu.get_barrier_semaphore()
    for peer in (z * 4 + y * 2 + 1 - x, z * 4 + (1 - y) * 2 + x):
        pl.semaphore_signal(barrier, inc=1, device_id={"dp": peer}, device_id_type=MESH)

    @pl.when(z > 0)
    def _():
        pl.semaphore_signal(barrier, inc=1, device_id={"dp": me - 4}, device_id_type=MESH)

    @pl.when(z < depth - 1)
    def _():
        pl.semaphore_signal(barrier, inc=1, device_id={"dp": me + 4}, device_id_type=MESH)

    for peer in extra:
        pl.semaphore_signal(barrier, inc=1, device_id=peer, device_id_type=MESH)
    ends = jnp.where(z > 0, 1, 0) + jnp.where(z < depth - 1, 1, 0)
    pl.semaphore_wait(barrier, 2 + len(extra) + ends)


def other_core(source, target, send, receive):
    return pltpu.make_async_remote_copy(
        src_ref=source,
        dst_ref=target,
        send_sem=send,
        recv_sem=receive,
        device_id={"tensor": 1 - lax.axis_index("tensor")},
        device_id_type=MESH,
    )


class Gather:
    def __init__(self, depth, parts, whole, far, table, sems):
        self.whole, self.far = whole, far
        self.depth = depth
        self.me, self.z, self.y, self.x = place()
        self.x_peer = self.z * 4 + self.y * 2 + 1 - self.x
        self.y_peer = self.z * 4 + (1 - self.y) * 2 + self.x
        self.rows = whole.shape[1] // parts
        self.array = [array for array, *_ in table]
        self.a, self.b, self.ab, self.c, self.all = [], [], [], [], []
        for _, base, width, third in table:
            side = (width - third) // 2
            self.a.append((base, side))
            self.b.append((base + side, side))
            self.ab.append((base, 2 * side))
            self.c.append((base + 2 * side, third))
            self.all.append((base, width))
        (
            self.z_send, self.z_recv, self.zc_send, self.zc_recv, self.xa_send, self.xa_recv, self.yb_send, self.yb_recv,
            self.ya_send, self.ya_recv, self.xb_send, self.xb_recv, self.c_send, self.c_recv, self.far_send, self.far_recv,
        ) = sems
        self.slots = line_slots(self.z, depth)

    @staticmethod
    def semaphores(depth, pieces):
        sem = pltpu.SemaphoreType.DMA
        return [
            *[sem((pieces, depth + 1)), sem((pieces, depth))] * 2,
            *[sem((pieces, depth))] * 4,
            *[sem((pieces, depth, 2))] * 4,
            sem((pieces, 2)),
            sem((pieces, 2)),
            sem((pieces,)),
            sem((pieces,)),
        ]

    def block(self, zb, yb, xb):
        return zb * 4 + yb * 2 + xb

    def cut(self, ref, p, block, count, columns):
        first = pl.multiple_of(block * self.rows, self.rows)
        return ref.at[self.array[p], pl.ds(first, count * self.rows), pl.ds(*columns)]

    def copy(self, p, block, count, columns, send, receive, device):
        part = self.cut(self.whole, p, block, count, columns)
        return remote(part, part, send, receive, device)

    def forward(self, p, block, count, columns):
        if p == 0:
            return
        other_core(
            self.cut(self.whole, p, block, count, columns),
            self.cut(self.far, p, block, count, columns),
            self.far_send.at[p],
            self.far_recv.at[p],
        ).start()

    def far_copy(self, p):
        part = self.far.at[self.array[p], :, pl.ds(*self.all[p])]
        return other_core(part, part, self.far_send.at[p], self.far_recv.at[p])

    def z_copy(self, p, zb, way, back=False):
        block = self.block(zb, self.y, self.x)
        sem = self.depth if back else zb
        return self.copy(
            p, block, 1, self.ab[p], self.z_send.at[p, sem], self.z_recv.at[p, zb], self.me + 4 * way
        )

    def zc_copy(self, p, zb, way, back=False):
        sem = self.depth if back else zb
        return self.copy(
            p, zb * 4, 4, self.c[p], self.zc_send.at[p, sem], self.zc_recv.at[p, zb], self.me + 4 * way
        )

    def xa(self, p, zb, xb):
        block = self.block(zb, self.y, xb)
        return self.copy(
            p, block, 1, self.a[p], self.xa_send.at[p, zb], self.xa_recv.at[p, zb], self.x_peer
        )

    def yb(self, p, zb, yb):
        block = self.block(zb, yb, self.x)
        return self.copy(
            p, block, 1, self.b[p], self.yb_send.at[p, zb], self.yb_recv.at[p, zb], self.y_peer
        )

    def ya(self, p, zb, yb, xb):
        block = self.block(zb, yb, xb)
        return self.copy(
            p, block, 1, self.a[p], self.ya_send.at[p, zb, xb], self.ya_recv.at[p, zb, xb], self.y_peer
        )

    def xb(self, p, zb, yb, xb):
        block = self.block(zb, yb, xb)
        return self.copy(
            p, block, 1, self.b[p], self.xb_send.at[p, zb, yb], self.xb_recv.at[p, zb, yb], self.x_peer
        )

    def xc(self, p, xb):
        block = self.block(self.z, self.y, xb)
        return self.copy(
            p, block, 1, self.c[p], self.c_send.at[p, 0], self.c_recv.at[p, 0], self.x_peer
        )

    def yc(self, p, yb):
        block = self.block(self.z, yb, 0)
        return self.copy(
            p, block, 2, self.c[p], self.c_send.at[p, 1], self.c_recv.at[p, 1], self.y_peer
        )

    def both_ways(self, copy, act):
        @pl.when(self.z < self.depth - 1)
        def _():
            act(copy(self.z, 1))

        @pl.when(self.z > 0)
        def _():
            act(copy(self.z, -1, True))

    def spread(self, p, zb):
        self.xa(p, zb, self.x).start()
        self.yb(p, zb, self.y).start()
        self.ya(p, zb, self.y, self.x).start()
        self.xb(p, zb, self.y, self.x).start()

    def turn(self, p, zb):
        self.xa(p, zb, 1 - self.x).wait_recv()
        self.ya(p, zb, self.y, 1 - self.x).start()
        self.forward(p, self.block(zb, self.y, 1 - self.x), 1, self.a[p])
        self.yb(p, zb, 1 - self.y).wait_recv()
        self.xb(p, zb, 1 - self.y, self.x).start()
        self.forward(p, self.block(zb, 1 - self.y, self.x), 1, self.b[p])

    def at_step(self, step, act):
        for zb, valid, way in self.slots[2 * step : 2 * step + 2]:
            on = (self.z + way >= 0) & (self.z + way < self.depth)
            pl.when(valid)(functools.partial(act, zb, way, on))

    def arrive(self, p, step):
        def act(zb, way, on):
            self.z_copy(p, zb, way).wait_recv()
            pl.when(on)(lambda: self.z_copy(p, zb, way).start())
            self.spread(p, zb)
            self.forward(p, self.block(zb, self.y, self.x), 1, self.ab[p])

        self.at_step(step, act)

    def arrive_c(self, p, step):
        def act(zb, way, on):
            self.zc_copy(p, zb, way).wait_recv()
            pl.when(on)(lambda: self.zc_copy(p, zb, way).start())
            self.forward(p, zb * 4, 4, self.c[p])

        self.at_step(step, act)

    def stage(self, p, s):
        depth = self.depth
        if s == 0:
            self.both_ways(lambda *way: self.z_copy(p, *way), lambda copy: copy.start())
            self.xc(p, self.x).start()
            self.spread(p, self.z)
            self.forward(p, self.me, 1, self.all[p])
            return
        if s == 1:
            self.xc(p, 1 - self.x).wait_recv()
            self.yc(p, self.y).start()
            self.forward(p, self.block(self.z, self.y, 1 - self.x), 1, self.c[p])
        if s == 2:
            self.yc(p, 1 - self.y).wait_recv()
            self.both_ways(lambda *way: self.zc_copy(p, *way), lambda copy: copy.start())
            self.forward(p, self.block(self.z, 1 - self.y, 0), 2, self.c[p])
        if 1 <= s < depth:
            self.arrive(p, s - 1)
        if 3 <= s < depth + 2:
            self.arrive_c(p, s - 3)
        if s == 2:
            self.turn(p, self.z)
        if 3 <= s < depth + 2:
            self.at_step(s - 3, lambda zb, way, on: self.turn(p, zb))
        if s == depth + 2:
            for zb in range(depth):
                for other in range(2):
                    self.ya(p, zb, 1 - self.y, other).wait_recv()
                    self.forward(p, self.block(zb, 1 - self.y, other), 1, self.a[p])
                    self.xb(p, zb, other, 1 - self.x).wait_recv()
                    self.forward(p, self.block(zb, other, 1 - self.x), 1, self.b[p])

    def finish(self, p):
        def sent(copy):
            copy.wait_send()

        if p:
            self.far_copy(p).wait_send()
        self.both_ways(lambda *way: self.z_copy(p, *way), sent)
        self.both_ways(lambda *way: self.zc_copy(p, *way), sent)
        for zb in range(self.depth):
            self.xa(p, zb, self.x).wait_send()
            self.yb(p, zb, self.y).wait_send()
            for other in range(2):
                self.ya(p, zb, self.y, other).wait_send()
                self.xb(p, zb, other, self.x).wait_send()
        self.xc(p, self.x).wait_send()
        self.yc(p, self.y).wait_send()

        def passed(zb, way, on):
            pl.when(on)(lambda: sent(self.z_copy(p, zb, way)))
            pl.when(on)(lambda: sent(self.zc_copy(p, zb, way)))

        for step in range(self.depth - 1):
            self.at_step(step, passed)


def looped(count, body, between):
    @pl.loop(0, count)
    def _(i):
        body(i)
        for step, acts in between.items():

            @pl.when(i == step)
            def _():
                for act in acts:
                    act()


GATHER_AT = {
    "hidden": {0: [(2, 0), (1, 0)], 1: [(0, 1), (0, 2), (0, 3)], 3: [(0, 4)], 4: [(0, 5), (1, 1)]},
    "upstream": {-1: [(2, 1)], 1: [(3, 0)]},
    "project": {-1: [(4, 0), (0, 6)], 1: [(1, 2)], 5: [(2, 2)]},
    "long": {2: [(3, 1), (1, 3)], 7: [(2, 3)], 9: [(1, 4)], 14: [(2, 4)]},
    "short": {2: [(1, 5)], 3: [(3, 2)], 5: [(4, 1)]},
    "norm": {-1: [(1, 6)], 1: [(2, 5)], 3: [(3, 3)]},
    "feed": {-1: [(4, 2), (2, 6)], 0: [(3, 4)], 1: [(4, 3)], 2: [(3, 5)]},
    "last": {-1: [(3, 6), (4, 4)], 0: [(4, 5)]},
    "tail": {-1: [(4, 6)]},
}


def piece_table(width, inner):
    third = width // 8
    return (
        (0, 0, 3 * inner, third),
        (0, 3 * inner, inner, third),
        (1, 0, width, 2 * third),
        (2, 0, width // 2, third),
        (2, width // 2, width // 2, third),
    )


def chunk_columns(j, per_piece, half):
    array, at = 1 + j // per_piece, j % per_piece
    pair = per_piece // 2
    quarter = (at // pair) * per_piece * half + (at % pair) * half
    if isinstance(j, int):
        split = array > 1
        return array, quarter if split else at * half, (
            quarter + pair * half if split else (per_piece + at) * half
        )
    split = array > 1
    first = jnp.where(split, quarter, at * half)
    return array, first, first + jnp.where(split, pair, per_piece) * half


def front_kernel(
    depth, lengths_ref, dealing_ref, project_ref, merge_ref, expand_ref, reduce_ref, vectors_ref, hidden_bias_ref,
    tokens_ref, cotangent_ref,
    whole_out, far_ref, qkv_out, turned_out, upstream_out, context_out, total_out,
    acc_out, normal_out, inverse_out, low_turned_out, active_out, slope_out, far_context_out,
    whole, score_bias, token, upper, hidden, turned, upstream, qkv, context, total,
    acc, normal, inverse, low, low_turned, active, slope, far_context, merge_far, expand_buf, reduce_buf,
    local_sem, core_sem, out_sem, load_sem, chunk_sem, *sems,
):
    arrays = whole.shape[0]
    half_rows, width = tokens_ref.shape
    rows = 2 * half_rows
    pairs = qkv.shape[0]
    inner = pairs * PAIR
    both = expand_buf.shape[2]
    half = both // 2
    hidden_half = expand_ref.shape[1]
    chunks = hidden_half // half
    per_piece = chunks // (arrays - 1)
    member = lax.axis_index("tensor")
    table = piece_table(whole.shape[2], inner)
    pieces = len(table)
    lines = Gather(depth, 4 * depth, whole, far_ref, table, sems)
    me = lines.me
    tall, short = 2 * TILE, TILE // 2

    own = [
        pltpu.make_async_copy(tokens_ref, token.at[member], local_sem.at[0]),
        pltpu.make_async_copy(cotangent_ref, upper.at[member], local_sem.at[1]),
    ]
    for copy in own:
        copy.start()
    mine = pl.ds(pl.multiple_of(me * lines.rows, lines.rows), lines.rows)
    for pair in range(pairs):
        for c in range(3):
            first = (3 * pair + c) * PAIR
            whole[0, mine, first : first + PAIR] = project_ref[
                c, :, pair * PAIR : (pair + 1) * PAIR
            ].astype(LOW)
    whole[0, mine, 3 * inner :] = merge_ref[...].astype(LOW)
    for j in range(chunks):
        array, first, second = chunk_columns(j, per_piece, half)
        columns = slice(j * half, (j + 1) * half)
        whole[array, mine, first : first + half] = expand_ref[:, columns].astype(LOW)
        whole[array, mine, second : second + half] = reduce_ref[:, columns].astype(LOW)
    greet_line(me, lines.z, lines.y, lines.x, depth, [{"tensor": 1 - member}])
    crossing = [
        other_core(tokens_ref, token.at[member], core_sem.at[0, 0], core_sem.at[0, 1]),
        other_core(cotangent_ref, upper.at[member], core_sem.at[1, 0], core_sem.at[1, 1]),
    ]
    lines.stage(0, 0)
    for copy in crossing:
        copy.start()
    group = Group(lengths_ref, dealing_ref)
    score_bias[...] = group.score_bias(rows - LONGEST)
    for copy in own:
        copy.wait()

    leaving = []

    def leave(source, target):
        copy = pltpu.make_async_copy(source, target, out_sem.at[len(leaving)])
        copy.start()
        leaving.append(copy)

    def before(name):
        for stage in GATHER_AT.get(name, {}).get(-1, ()):
            lines.stage(*stage)

    def phase(name, count, body):
        between = {
            step: [functools.partial(lines.stage, *stage) for stage in stages]
            for step, stages in GATHER_AT.get(name, {}).items()
            if step >= 0
        }
        looped(count, body, between)

    def places_of(first):
        return first + lax.broadcasted_iota(jnp.int32, (TILE, 1), 0)

    def picked(index, source):
        return picked_rows(index, source.at[0]) + picked_rows(index - half_rows, source.at[1])

    def tile(step, size=TILE):
        return pl.ds(pl.multiple_of(step * size, size), size)

    def hidden_tile(step):
        index = group.moved(places_of(step * TILE), group.first, group.own)
        rows_here = picked(index, token)
        hidden[tile(step), :] = rows_here.astype(LOW)
        turned[:, tile(step)] = rows_here.T.astype(LOW)

    def upstream_tile(step):
        places = places_of(member * half_rows + step * TILE)
        index = group.moved(places, group.first, group.dealt)
        upstream[tile(step), :] = picked(index, upper).astype(LOW)

    crossing[0].wait()
    before("hidden")
    phase("hidden", rows // TILE, hidden_tile)
    leave(turned, turned_out)
    crossing[1].wait()
    before("upstream")
    phase("upstream", half_rows // TILE, upstream_tile)
    leave(upstream, upstream_out)

    def project_tile(i):
        pair, step = i // (rows // tall), lax.rem(i, rows // tall)
        at = tile(step, tall)
        columns = pl.ds(pl.multiple_of(pair * 3 * PAIR, PAIR), 3 * PAIR)
        bias_columns = pl.ds(pl.multiple_of(member * inner + pair * PAIR, PAIR), PAIR)
        bias = jnp.concatenate(
            [
                vectors_ref[0:1, bias_columns],
                jnp.zeros((1, PAIR), WIDE),
                vectors_ref[1:2, bias_columns],
            ],
            axis=1,
        )
        qkv[pair, at, :] = (dot_nn(hidden[at, :], whole[0, :, columns]) + bias).astype(LOW)

    before("project")
    phase("project", pairs * rows // tall, project_tile)
    leave(qkv, qkv_out)

    def attend_step(begin, size):
        def step_of(i):
            pair, step = i // (size // TILE), lax.rem(i, size // TILE)
            columns = pl.ds(pl.multiple_of(pair * PAIR, PAIR), PAIR)
            attend_tile(qkv, pair, score_bias, begin, size, step, context, columns, total)

        return step_of

    before("long")
    phase("long", pairs * LONGEST // TILE, attend_step(0, LONGEST))
    before("short")
    phase("short", pairs * (rows - LONGEST) // TILE, attend_step(LONGEST, rows - LONGEST))
    leave(context, context_out)
    leave(total, total_out)

    own_first = member * half_rows
    other_rows = pl.ds(pl.multiple_of((1 - member) * half_rows, half_rows), half_rows)
    crossing = other_core(context.at[other_rows], far_context, core_sem.at[2, 0], core_sem.at[2, 1])
    crossing.start()
    before("norm")
    lines.far_copy(1).wait_recv()
    merge_columns = pl.ds(whole.shape[2] - inner, inner)
    merge_copy = pltpu.make_async_copy(
        far_ref.at[0, :, merge_columns], merge_far, local_sem.at[2]
    )
    merge_copy.start()
    merge_copy.wait()
    crossing.wait()
    leave(far_context, far_context_out)

    def norm_tile(step):
        at = tile(step, short)
        own_at = pl.ds(pl.multiple_of(own_first + step * short, short), short)
        branch = dot_nt(context[own_at, :], whole[0, :, merge_columns])
        branch = branch + dot_nt(far_context[at, :], merge_far[...])
        unit, scale = norm(hidden[own_at, :].astype(WIDE) + branch + vectors_ref[2:3, :])
        normed = unit * vectors_ref[3:4, :] + vectors_ref[4:5, :]
        normal[at, :] = unit
        inverse[at, :] = jnp.broadcast_to(scale, (short, 128))
        low[at, :] = normed.astype(LOW)
        low_turned[:, at] = normed.T.astype(LOW)
        acc[at, :] = normed + vectors_ref[5:6, :]

    phase("norm", half_rows // short, norm_tile)
    leave(whole.at[0], whole_out.at[0])
    leave(normal, normal_out)
    leave(inverse, inverse_out)
    leave(low_turned, low_turned_out)

    def loads(j):
        slot = lax.rem(j, 2)
        array, *firsts = chunk_columns(j, per_piece, half)
        copies = []
        for kind, buf in enumerate((expand_buf, reduce_buf)):
            first = pl.multiple_of(firsts[kind], half)
            for side, source in enumerate((far_ref, whole)):
                copies.append(
                    pltpu.make_async_copy(
                        source.at[array, :, pl.ds(first, half)],
                        buf.at[slot, :, pl.ds(side * half, half)],
                        load_sem.at[slot, kind, side],
                    )
                )
        return copies

    def results(j):
        slot = lax.rem(j, 2)
        return [
            pltpu.make_async_copy(active.at[slot], active_out.at[j], chunk_sem.at[slot, 0]),
            pltpu.make_async_copy(slope.at[slot], slope_out.at[j], chunk_sem.at[slot, 1]),
        ]

    def chunk_of(piece, first_chunk, count):
        def chunk(i):
            j = first_chunk + i
            slot = lax.rem(j, 2)

            @pl.when(i == 0)
            def _():
                lines.far_copy(piece).wait_recv()
                for copy in loads(j):
                    copy.start()

            for copy in loads(j):
                copy.wait()

            @pl.when(i + 1 < count)
            def _():
                for copy in loads(j + 1):
                    copy.start()

            @pl.when(j >= 2)
            def _():
                for copy in results(j - 2):
                    copy.wait()

            biases = []
            for which in (1 - member, member):
                first = pl.multiple_of(which * hidden_half + j * half, half)
                biases.append(hidden_bias_ref[:, pl.ds(first, half)])
            bias = jnp.concatenate(biases, axis=1)
            tiles = [slice(step * TILE, (step + 1) * TILE) for step in range(half_rows // TILE)]
            parts = [dot_nn(low[at, :], expand_buf[slot]) for at in tiles]
            for at, part in zip(tiles, parts, strict=True):
                value = part + bias
                below, bell = normal_cells(value)
                held = (value * below).astype(LOW)
                active[slot, at, :] = held
                slope[slot, at, :] = (below + value * bell * 0.3989422804014327).astype(LOW)
                acc[at, :] += dot_nt(held, reduce_buf[slot])
            for copy in results(j):
                copy.start()

        return chunk

    first_chunk = 0
    for piece, name in ((2, "feed"), (3, "last"), (4, "tail")):
        count = chunks * table[piece][2] // (2 * hidden_half)
        before(name)
        phase(name, count, chunk_of(piece, first_chunk, count))
        columns = pl.ds(*lines.all[piece])
        leave(
            whole.at[lines.array[piece], :, columns],
            whole_out.at[lines.array[piece], :, columns],
        )
        first_chunk += count
    leave(acc, acc_out)
    for p in range(pieces):
        lines.finish(p)
    for j in (chunks - 2, chunks - 1):
        for copy in results(j):
            copy.wait()
    for copy in leaving:
        copy.wait()


def front(lengths, dealing, project, merge, expand, reduce, vectors, hidden_bias, tokens, cotangent, parts):
    shard_rows, hidden_half = expand.shape
    arrays, columns = 3, hidden_half
    half_rows, width = tokens.shape
    rows, pairs, depth = 2 * half_rows, project.shape[2] // PAIR, parts // 4
    inner, half = pairs * PAIR, 256
    pieces = len(piece_table(columns, inner))
    chunks, both = hidden_half // half, 2 * half
    shape, sem = jax.ShapeDtypeStruct, pltpu.SemaphoreType.DMA
    vmem, anywhere = pl.BlockSpec(memory_space=pltpu.VMEM), pl.BlockSpec(memory_space=pl.ANY)
    held = [
        ((pairs, rows, 3 * PAIR), LOW),
        ((width, rows), LOW),
        ((half_rows, width), LOW),
        ((rows, inner), LOW),
        ((pairs, 8, rows), WIDE),
        ((half_rows, width), WIDE),
        ((half_rows, width), WIDE),
        ((half_rows, 128), WIDE),
        ((width, half_rows), LOW),
        ((chunks, half_rows, both), LOW),
        ((chunks, half_rows, both), LOW),
        ((half_rows, inner), LOW),
    ]
    return pl.pallas_call(
        functools.partial(front_kernel, depth),
        in_specs=[*[pl.BlockSpec(memory_space=pltpu.SMEM)] * 2, *[vmem] * 6, *[anywhere] * 2],
        out_specs=[anywhere] * 14,
        out_shape=[
            shape((arrays, parts * shard_rows, columns), LOW),
            shape((arrays, parts * shard_rows, columns), LOW),
            *[shape(*one) for one in held],
        ],
        scratch_shapes=[
            pltpu.VMEM((arrays, parts * shard_rows, columns), LOW),
            pltpu.VMEM((rows - LONGEST, rows - LONGEST), WIDE),
            pltpu.VMEM((2, half_rows, width), LOW),
            pltpu.VMEM((2, half_rows, width), LOW),
            pltpu.VMEM((rows, width), LOW),
            pltpu.VMEM((width, rows), LOW),
            pltpu.VMEM((half_rows, width), LOW),
            pltpu.VMEM((pairs, rows, 3 * PAIR), LOW),
            pltpu.VMEM((rows, inner), LOW),
            pltpu.VMEM((pairs, 8, rows), WIDE),
            pltpu.VMEM((half_rows, width), WIDE),
            pltpu.VMEM((half_rows, width), WIDE),
            pltpu.VMEM((half_rows, 128), WIDE),
            pltpu.VMEM((half_rows, width), LOW),
            pltpu.VMEM((width, half_rows), LOW),
            pltpu.VMEM((2, half_rows, both), LOW),
            pltpu.VMEM((2, half_rows, both), LOW),
            pltpu.VMEM((half_rows, inner), LOW),
            pltpu.VMEM((width, inner), LOW),
            pltpu.VMEM((2, width, both), LOW),
            pltpu.VMEM((2, width, both), LOW),
            sem((3,)),
            sem((3, 2)),
            sem((16,)),
            sem((2, 2, 2)),
            sem((2, 2)),
            *Gather.semaphores(depth, pieces),
        ],
        compiler_params=pltpu.CompilerParams(
            collective_id=0, has_side_effects=True, vmem_limit_bytes=63 * MIB
        ),
    )(lengths, dealing, project, merge, expand, reduce, vectors, hidden_bias, tokens, cotangent)


def normal_cells(value):
    bell = jnp.exp2(value * value * (-0.5 * 1.4426950408889634))
    below = 1.0 + 0.39 * 0.7071067811865476 * jnp.abs(value)
    t = pl.reciprocal(below, approx=True)
    t = t * (2.0 - below * t)
    t = t * (2.0 - below * t)
    tail = 0.5 * -0.2275377237624147
    for factor in (
        0.8866668177122106,
        -0.6354042576077721,
        0.649562611731642,
        0.0913871257655044,
        0.23532542445435511,
    ):
        tail = tail * t + 0.5 * factor
    tail = tail * t * bell
    return jnp.where(value < 0.0, tail, 1.0 - tail), bell


def norm(values):
    center = values - jnp.mean(values, axis=1, keepdims=True)
    spread = jnp.mean(center * center, axis=1, keepdims=True)
    scale = lax.rsqrt(spread + norm_epsilon)
    return center * scale, scale


def norm_back(scaled, unit, scale):
    return scale * (
        scaled
        - jnp.mean(scaled, axis=1, keepdims=True)
        - unit * jnp.mean(scaled * unit, axis=1, keepdims=True)
    )


def feed_kernel(
    context_ref, merge_ref, merge_far_ref, whole_ref, far_ref, hidden_ref, upstream_ref, vectors_ref, bias_ref,
    encoded_ref, branch_ref, grad_ref, merge_grad_ref, expand_grad_ref, reduce_grad_ref, sums_ref, hidden_sums_ref,
    own_ctx, far_ctx, acc, normal, inverse, low, turned, late, late_turned, active, slope, inner_grad,
    expand_buf, reduce_buf, arrived, leaving, kept, done, grad_own, grad_far, merge_send, merge_recv,
    ctx_sem, load_sem, send_sem, recv_sem, out_sem, last_sem,
):
    rows = hidden_ref.shape[0]
    chunks, _, both = bias_ref.shape
    half = both // 2
    per_piece = whole_ref.shape[2] // (2 * half)
    member = lax.axis_index("tensor")
    peer = {"tensor": 1 - member}
    tall, short = 256, 128
    width = hidden_ref.shape[1]

    def across(source, target, send, receive):
        return pltpu.make_async_remote_copy(
            src_ref=source,
            dst_ref=target,
            send_sem=send,
            recv_sem=receive,
            device_id=peer,
            device_id_type=MESH,
        )

    def rows_of(which):
        return pl.ds(pl.multiple_of(which * rows, rows), rows)

    def tile(step, size):
        return pl.ds(pl.multiple_of(step * size, size), size)

    def loads(j, slot):
        piece, at = 1 + j // per_piece, lax.rem(j, per_piece) * half
        copies = []
        for kind, buf in enumerate((expand_buf, reduce_buf)):
            first = pl.multiple_of(at + kind * per_piece * half, half)
            for side, source in enumerate((far_ref, whole_ref)):
                copies.append(
                    pltpu.make_async_copy(
                        source.at[piece, :, pl.ds(first, half)],
                        buf.at[slot, :, pl.ds(side * half, half)],
                        load_sem.at[slot, kind, side],
                    )
                )
        return copies

    for copy in loads(0, 0):
        copy.start()
    barrier = pltpu.get_barrier_semaphore()
    pl.semaphore_signal(barrier, inc=1, device_id=peer, device_id_type=MESH)
    pl.semaphore_wait(barrier, 1)
    out_ctx = across(context_ref.at[rows_of(1 - member)], far_ctx, ctx_sem.at[0], ctx_sem.at[1])
    out_ctx.start()
    in_ctx = pltpu.make_async_copy(context_ref.at[rows_of(member)], own_ctx, ctx_sem.at[2])
    in_ctx.start()
    sums_ref[...] = jnp.zeros_like(sums_ref)
    in_ctx.wait()
    out_ctx.wait()

    def add_sum(row, values):
        sums_ref[row : row + 1, :] += jnp.sum(values, axis=0, keepdims=True)

    @pl.loop(0, rows // short)
    def _(step):
        at = tile(step, short)
        branch = dot_nt(own_ctx[at, :], merge_ref[...]) + dot_nt(far_ctx[at, :], merge_far_ref[...])
        unit, scale = norm(hidden_ref[at, :].astype(WIDE) + branch + vectors_ref[2:3, :])
        normed = unit * vectors_ref[3:4, :] + vectors_ref[4:5, :]
        normal[at, :] = unit
        inverse[at, :] = jnp.broadcast_to(scale, (short, 128))
        low[at, :] = normed.astype(LOW)
        turned[:, at] = normed.T.astype(LOW)
        acc[at, :] = normed + vectors_ref[5:6, :]

    @pl.loop(0, chunks)
    def _(j):
        slot = lax.rem(j, 2)
        for copy in loads(j, slot):
            copy.wait()

        @pl.when(j + 1 < chunks)
        def _():
            for copy in loads(j + 1, 1 - slot):
                copy.start()

        for step in range(rows // tall):
            at = slice(step * tall, (step + 1) * tall)
            inner = dot_nn(low[at, :], expand_buf[slot]) + bias_ref[j]
            below, bell = normal_cells(inner)
            held = (inner * below).astype(LOW)
            active[j, at, :] = held
            slope[j, at, :] = (below + inner * bell * 0.3989422804014327).astype(LOW)
            acc[at, :] += dot_nt(held, reduce_buf[slot])

    for copy in loads(0, 0):
        copy.start()

    @pl.loop(0, rows // short)
    def _(step):
        at = tile(step, short)
        unit, scale = norm(acc[at, :])
        encoded_ref[at, :] = (unit * vectors_ref[6:7, :] + vectors_ref[7:8, :]).astype(LOW)
        upper = upstream_ref[at, :].astype(WIDE)
        add_sum(6, upper * unit)
        add_sum(7, upper)
        grad = norm_back(upper * vectors_ref[6:7, :], unit, scale)
        grad_low = grad.astype(LOW)
        add_sum(5, grad_low.astype(WIDE))
        acc[at, :] = grad
        late[at, :] = grad_low
        late_turned[:, at] = grad.T.astype(LOW)

    def send(j, kind):
        return across(
            leaving.at[lax.rem(j, 2), kind],
            arrived.at[lax.rem(j, 4), kind],
            send_sem.at[lax.rem(j, 2), kind],
            recv_sem.at[lax.rem(j, 4), kind],
        )

    def store(j, kind):
        target = (expand_grad_ref, reduce_grad_ref)[kind]
        cols = pl.ds(pl.multiple_of(j * half, half), half)
        return pltpu.make_async_copy(
            done.at[lax.rem(j, 2), kind], target.at[:, cols], out_sem.at[lax.rem(j, 2), kind]
        )

    def finish(j):
        for kind in range(2):
            send(j, kind).wait_recv()

            @pl.when(j >= 2)
            def _():
                store(j - 2, kind).wait()

            @pl.loop(0, width // tall)
            def _(step):
                at = tile(step, tall)
                done[lax.rem(j, 2), kind, at, :] = (
                    kept[lax.rem(j, 2), kind, at, :]
                    + arrived[lax.rem(j, 4), kind, at, :].astype(WIDE)
                ).astype(LOW)

            store(j, kind).start()

    @pl.loop(0, chunks)
    def _(j):
        slot = lax.rem(j, 2)
        for copy in loads(j, slot):
            copy.wait()

        @pl.when(j + 1 < chunks)
        def _():
            for copy in loads(j + 1, 1 - slot):
                copy.start()

        total = jnp.zeros((1, both), WIDE)
        for step in range(rows // tall):
            at = slice(step * tall, (step + 1) * tall)
            grad = dot_nn(late[at, :], reduce_buf[slot]) * slope[j, at, :].astype(WIDE)
            grad = grad.astype(LOW)
            inner_grad[at, :] = grad
            total = total + jnp.sum(grad.astype(WIDE), axis=0, keepdims=True)
            acc[at, :] += dot_nt(grad, expand_buf[slot])
        hidden_sums_ref[j] = total

        @pl.when(j >= 2)
        def _():
            for kind in range(2):
                send(j - 2, kind).wait_send()

        for kind, (left, right) in enumerate(((turned, inner_grad), (late_turned, active.at[j]))):
            for step in range(width // tall):
                at = slice(step * tall, (step + 1) * tall)
                part = dot_nn(left[at, :], right[...])
                leaving[slot, kind, at, :] = part[:, 0:half].astype(LOW)
                kept[slot, kind, at, :] = part[:, half:both]
            send(j, kind).start()

        @pl.when(j >= 1)
        def _():
            finish(j - 1)

    @pl.loop(0, rows // short)
    def _(step):
        at = tile(step, short)
        grad = acc[at, :]
        unit = normal[at, :]
        add_sum(3, grad * unit)
        add_sum(4, grad)
        branch_grad = norm_back(grad * vectors_ref[3:4, :], unit, inverse[at, 0:1])
        branch_low = branch_grad.astype(LOW)
        add_sum(2, branch_low.astype(WIDE))
        branch_ref[at, :] = branch_grad
        turned[:, at] = branch_grad.T.astype(LOW)
        grad_far[at, :] = dot_nn(branch_low, merge_far_ref[...]).astype(LOW)
        grad_own[at, :] = dot_nn(branch_low, merge_ref[...]).astype(LOW)

    out_grad = across(grad_far, grad_ref.at[rows_of(member)], ctx_sem.at[0], ctx_sem.at[1])
    out_grad.start()
    in_grad = pltpu.make_async_copy(grad_own, grad_ref.at[rows_of(member)], ctx_sem.at[2])
    in_grad.start()
    for step in range(width // tall):
        at = slice(step * tall, (step + 1) * tall)
        merge_send[at, :] = dot_nn(turned[at, :], far_ctx[...]).astype(LOW)
    out_merge = across(merge_send, merge_recv, last_sem.at[0], last_sem.at[1])
    out_merge.start()
    finish(chunks - 1)
    for kind in range(2):
        send(chunks - 2, kind).wait_send()
        send(chunks - 1, kind).wait_send()
        store(chunks - 2, kind).wait()
        store(chunks - 1, kind).wait()
    out_merge.wait()
    for step in range(width // tall):
        at = slice(step * tall, (step + 1) * tall)
        merge_grad_ref[at, :] = (
            dot_nn(turned[at, :], own_ctx[...]) + merge_recv[at, :].astype(WIDE)
        ).astype(LOW)
    out_grad.wait()
    in_grad.wait()


def feed_block(context, whole, far, hidden_own, upstream, vectors, bias_own, bias_far):
    total_rows, inner = context.shape
    rows, width = hidden_own.shape
    hidden = bias_own.shape[0]
    merge, merge_far = whole[0, :, -inner:], far[0, :, -inner:]
    half = 256
    chunks = hidden // half
    both = 2 * half
    bias = jnp.concatenate(
        [bias_far.reshape(chunks, 1, half), bias_own.reshape(chunks, 1, half)], axis=2
    )
    vmem, anywhere = pl.BlockSpec(memory_space=pltpu.VMEM), pl.BlockSpec(memory_space=pl.ANY)
    sem = pltpu.SemaphoreType.DMA
    shape = jax.ShapeDtypeStruct
    *results, hidden_sums = pl.pallas_call(
        feed_kernel,
        in_specs=[anywhere, vmem, vmem, *[anywhere] * 2, *[vmem] * 4],
        out_specs=[vmem, vmem, anywhere, vmem, anywhere, anywhere, vmem, vmem],
        out_shape=[
            shape((rows, width), LOW),
            shape((rows, width), WIDE),
            shape((total_rows, inner), LOW),
            shape((width, inner), LOW),
            shape((width, hidden), LOW),
            shape((width, hidden), LOW),
            shape((8, width), WIDE),
            shape((chunks, 1, both), WIDE),
        ],
        scratch_shapes=[
            pltpu.VMEM((rows, inner), LOW),
            pltpu.VMEM((rows, inner), LOW),
            pltpu.VMEM((rows, width), WIDE),
            pltpu.VMEM((rows, width), WIDE),
            pltpu.VMEM((rows, 128), WIDE),
            pltpu.VMEM((rows, width), LOW),
            pltpu.VMEM((width, rows), LOW),
            pltpu.VMEM((rows, width), LOW),
            pltpu.VMEM((width, rows), LOW),
            pltpu.VMEM((chunks, rows, both), LOW),
            pltpu.VMEM((chunks, rows, both), LOW),
            pltpu.VMEM((rows, both), LOW),
            pltpu.VMEM((2, width, both), LOW),
            pltpu.VMEM((2, width, both), LOW),
            pltpu.VMEM((4, 2, width, half), LOW),
            pltpu.VMEM((2, 2, width, half), LOW),
            pltpu.VMEM((2, 2, width, half), WIDE),
            pltpu.VMEM((2, 2, width, half), LOW),
            pltpu.VMEM((rows, inner), LOW),
            pltpu.VMEM((rows, inner), LOW),
            pltpu.VMEM((width, inner), LOW),
            pltpu.VMEM((width, inner), LOW),
            sem((3,)),
            sem((2, 2, 2)),
            sem((2, 2)),
            sem((4, 2)),
            sem((2, 2)),
            sem((2,)),
        ],
        compiler_params=pltpu.CompilerParams(
            collective_id=2, has_side_effects=True, vmem_limit_bytes=60 * MIB
        ),
        cost_estimate=pl.CostEstimate(
            flops=12 * rows * width * 2 * hidden, bytes_accessed=8 * width * hidden * 4, transcendentals=0
        ),
    )(context, merge, merge_far, whole, far, hidden_own, upstream, vectors, bias)
    hidden_far = hidden_sums[:, 0, :half].reshape(-1)
    hidden_near = hidden_sums[:, 0, half:].reshape(-1)
    return (*results, hidden_near, hidden_far)


class Scatter:
    buffers = 8

    def __init__(self, depth, grads, shards, buffers, sems):
        self.depth, self.grads, self.shards = depth, grads, shards
        self.held = [buffers[8 * p : 8 * p + 8] for p in range(len(grads))]
        self.me, self.z, self.y, self.x = place()
        self.x_peer = self.z * 4 + self.y * 2 + 1 - self.x
        self.y_peer = self.z * 4 + (1 - self.y) * 2 + self.x
        self.rows = grads[0].shape[0] // (4 * depth)
        (
            self.a1_send, self.a1_recv, self.a2_send, self.a2_recv, self.b2_send, self.b2_recv, self.b1_send, self.b1_recv,
            self.z_send, self.z_recv, self.zc_send, self.zc_recv, self.c_send, self.c_recv,
        ) = sems

    @staticmethod
    def scratch(depth, rows, classes):
        found = []
        for a, b, c in classes:
            found += [
                pltpu.VMEM((depth, 2 * rows, a), LOW),
                pltpu.VMEM((depth, 2, rows, b), LOW),
                pltpu.VMEM((depth, rows, a), LOW),
                pltpu.VMEM((depth, rows, b), LOW),
                pltpu.VMEM((depth + 1, rows, a + b), LOW),
                pltpu.VMEM((depth + 1, 4 * rows, c), LOW),
                pltpu.VMEM((2 * rows, c), LOW),
                pltpu.VMEM((rows, c), LOW),
            ]
        return found

    @staticmethod
    def semaphores(depth, pieces):
        sem = pltpu.SemaphoreType.DMA
        return [
            *[sem((pieces, depth))] * 6,
            *[sem((pieces, depth, 2))] * 2,
            *[sem((pieces, depth)), sem((pieces, depth + 1))] * 2,
            sem((pieces, 2)),
            sem((pieces, 2)),
        ]

    def columns(self, p):
        a, b, c = (self.held[p][i].shape[-1] for i in (0, 1, 5))
        return pl.ds(0, a), pl.ds(a, b), pl.ds(a + b, c)

    def block(self, zb, yb, xb):
        return zb * 4 + yb * 2 + xb

    def span(self, block, count=1):
        return pl.ds(pl.multiple_of(block * self.rows, self.rows), count * self.rows)

    def add(self, put, count, *terms):
        chunk = min(count, 64)

        @pl.loop(0, count // chunk)
        def _(step):
            at = pl.multiple_of(step * chunk, chunk)
            parts = [term(at, chunk) for term in terms]
            if len(parts) > 2 or put.wide:
                parts = [part.astype(WIDE) for part in parts]
            total = parts[0]
            for part in parts[1:]:
                total = total + part
            put(at, chunk, total)

    def a1(self, p, zb):
        return remote(
            self.grads[p].at[self.span(self.block(zb, 1 - self.y, 0), 2), self.columns(p)[0]],
            self.held[p][0].at[zb],
            self.a1_send.at[p, zb],
            self.a1_recv.at[p, zb],
            self.y_peer,
        )

    def b1(self, p, zb, yb):
        return remote(
            self.grads[p].at[self.span(self.block(zb, yb, 1 - self.x)), self.columns(p)[1]],
            self.held[p][1].at[zb, yb],
            self.b1_send.at[p, zb, yb],
            self.b1_recv.at[p, zb, yb],
            self.x_peer,
        )

    def a2(self, p, zb):
        return remote(
            self.held[p][0].at[zb, self.span(1 - self.x)],
            self.held[p][2].at[zb],
            self.a2_send.at[p, zb],
            self.a2_recv.at[p, zb],
            self.x_peer,
        )

    def b2(self, p, zb):
        return remote(
            self.held[p][1].at[zb, 1 - self.y],
            self.held[p][3].at[zb],
            self.b2_send.at[p, zb],
            self.b2_recv.at[p, zb],
            self.y_peer,
        )

    def slot(self, zb, way):
        return zb if way > 0 else zb + (self.depth - zb) * jnp.where(zb == self.z - 1, 1, 0)

    def z_copy(self, p, zb, way):
        slot = self.slot(zb, way)
        return remote(
            self.held[p][4].at[zb],
            self.held[p][4].at[slot],
            self.z_send.at[p, zb],
            self.z_recv.at[p, slot],
            self.me + 4 * way,
        )

    def zc_copy(self, p, zb, way, first):
        slot = self.slot(zb, way)
        source = self.held[p][5].at[zb]
        if first:
            source = self.grads[p].at[self.span(zb * 4, 4), self.columns(p)[2]]
        return remote(
            source,
            self.held[p][5].at[slot],
            self.zc_send.at[p, zb],
            self.zc_recv.at[p, slot],
            self.me + 4 * way,
        )

    def arrived(self, ref, sem, slot):
        part = ref.at[slot]
        remote(part, part, sem, sem, self.me).wait_recv()

    def cy(self, p):
        return remote(
            self.held[p][5].at[self.z, self.span(2 * (1 - self.y), 2)],
            self.held[p][6],
            self.c_send.at[p, 0],
            self.c_recv.at[p, 0],
            self.y_peer,
        )

    def cx(self, p):
        return remote(
            self.held[p][5].at[self.z, self.span(2 * self.y + 1 - self.x)],
            self.held[p][7],
            self.c_send.at[p, 1],
            self.c_recv.at[p, 1],
            self.x_peer,
        )

    def grad(self, p, block, columns):
        def term(at, count):
            first = pl.multiple_of(block * self.rows + at, 16)
            return self.grads[p][pl.ds(first, count), columns]

        return term

    def part(self, ref, lead, block, columns=None):
        columns = slice(None) if columns is None else columns

        def term(at, count):
            first = pl.multiple_of(block * self.rows + at, 16)
            return ref[(*lead, pl.ds(first, count), columns)]

        return term

    def put(self, ref, lead, block, columns=None):
        columns = slice(None) if columns is None else columns

        def act(at, count, total):
            first = pl.multiple_of(block * self.rows + at, 16)
            ref[(*lead, pl.ds(first, count), columns)] = total.astype(ref.dtype)

        act.wide = ref.dtype == WIDE
        return act

    def open(self, p, zb):
        self.a1(p, zb).start()
        self.b1(p, zb, 0).start()
        self.b1(p, zb, 1).start()

    def first(self, p, zb):
        z, y, x = self.z, self.y, self.x
        a, b, _ = self.columns(p)
        r1a, r1b = self.held[p][0], self.held[p][1]
        self.a1(p, zb).wait_recv()
        self.add(
            self.put(r1a, (zb,), 1 - x),
            self.rows,
            self.part(r1a, (zb,), 1 - x),
            self.grad(p, self.block(zb, y, 1 - x), a),
        )
        self.a2(p, zb).start()
        self.b1(p, zb, 0).wait_recv()
        self.b1(p, zb, 1).wait_recv()
        self.add(
            self.put(r1b, (zb, 1 - y), 0),
            self.rows,
            self.part(r1b, (zb, 1 - y), 0),
            self.grad(p, self.block(zb, 1 - y, x), b),
        )
        self.b2(p, zb).start()

    def terms(self, p, zb):
        z, y, x = self.z, self.y, self.x
        a, b, _ = self.columns(p)
        r1a, r1b, r2a, r2b = self.held[p][:4]
        own = self.block(zb, y, x)
        return (
            [self.grad(p, own, a), self.part(r1a, (zb,), x), self.part(r2a, (zb,), 0)],
            [self.grad(p, own, b), self.part(r1b, (zb, y), 0), self.part(r2b, (zb,), 0)],
        )

    def pass_on(self, p, zb, way):
        a, b, _ = self.columns(p)
        rz = self.held[p][4]
        self.a2(p, zb).wait_recv()
        self.b2(p, zb).wait_recv()
        from_line = (self.z - way >= 0) & (self.z - way < self.depth)

        @pl.when(from_line)
        def _():
            self.arrived(rz, self.z_recv.at[p, zb], zb)
            for terms, columns in zip(self.terms(p, zb), (a, b), strict=True):
                self.add(
                    self.put(rz, (zb,), 0, columns),
                    self.rows,
                    *terms,
                    self.part(rz, (zb,), 0, columns),
                )

        @pl.when(jnp.logical_not(from_line))
        def _():
            for terms, columns in zip(self.terms(p, zb), (a, b), strict=True):
                self.add(self.put(rz, (zb,), 0, columns), self.rows, *terms)

        self.z_copy(p, zb, way).start()

    def pass_c(self, p, zb, way):
        c = self.columns(p)[2]
        rc = self.held[p][5]
        from_line = (self.z - way >= 0) & (self.z - way < self.depth)

        @pl.when(from_line)
        def _():
            self.arrived(rc, self.zc_recv.at[p, zb], zb)
            self.add(
                self.put(rc, (zb,), 0),
                4 * self.rows,
                self.part(rc, (zb,), 0),
                self.grad(p, zb * 4, c),
            )
            self.zc_copy(p, zb, way, False).start()

        @pl.when(jnp.logical_not(from_line))
        def _():
            self.zc_copy(p, zb, way, True).start()

    def own_c(self, p):
        z, depth = self.z, self.depth
        c = self.columns(p)[2]
        rc = self.held[p][5]
        grad = self.grad(p, z * 4, c)
        lower, upper = self.part(rc, (z,), 0), self.part(rc, (depth,), 0)
        put = self.put(rc, (z,), 0)

        @pl.when(z > 0)
        def _():
            self.arrived(rc, self.zc_recv.at[p, z], z)

        @pl.when(z < depth - 1)
        def _():
            self.arrived(rc, self.zc_recv.at[p, depth], depth)

        @pl.when((z > 0) & (z < depth - 1))
        def _():
            self.add(put, 4 * self.rows, grad, lower, upper)

        @pl.when(z == 0)
        def _():
            self.add(put, 4 * self.rows, grad, upper)

        @pl.when(z == depth - 1)
        def _():
            self.add(put, 4 * self.rows, grad, lower)

        self.cy(p).start()

    def turn_c(self, p):
        rc, rcy = self.held[p][5], self.held[p][6]
        self.cy(p).wait_recv()
        self.add(
            self.put(rc, (self.z,), 2 * self.y),
            2 * self.rows,
            self.part(rc, (self.z,), 2 * self.y),
            self.part(rcy, (), 0),
        )
        self.cx(p).start()

    def close(self, p):
        z, depth = self.z, self.depth
        a, b, c = self.columns(p)
        rz, rc, rcx = self.held[p][4], self.held[p][5], self.held[p][7]
        self.a2(p, z).wait_recv()
        self.b2(p, z).wait_recv()

        @pl.when(z > 0)
        def _():
            self.arrived(rz, self.z_recv.at[p, z], z)

        @pl.when(z < depth - 1)
        def _():
            self.arrived(rz, self.z_recv.at[p, depth], depth)

        def total(*slots):
            for terms, columns in zip(self.terms(p, z), (a, b), strict=True):
                lines = [self.part(rz, (slot,), 0, columns) for slot in slots]
                self.add(self.put(self.shards[p], (), 0, columns), self.rows, *terms, *lines)

        pl.when((z > 0) & (z < depth - 1))(lambda: total(z, depth))
        pl.when(z == 0)(lambda: total(depth))
        pl.when(z == depth - 1)(lambda: total(z))
        self.cx(p).wait_recv()
        self.add(
            self.put(self.shards[p], (), 0, c),
            self.rows,
            self.part(rc, (z,), 2 * self.y + self.x),
            self.part(rcx, (), 0),
        )

    def at_step(self, step, act):
        z, depth = self.z, self.depth
        if step < 0:
            act(z, 0)
            return
        for zb, valid, way in (
            (z + 1 + step, z + 1 + step < depth, 1),
            (z - 1 - step, z - 1 - step >= 0, -1),
        ):
            pl.when(valid)(functools.partial(act, zb, way))

    def stage(self, p, s):
        last = self.depth - 2

        def opened(step):
            self.at_step(step, lambda zb, way: self.open(p, zb))

        def added(step):
            self.at_step(step, lambda zb, way: self.first(p, zb))

        def passed(step):
            self.at_step(step, lambda zb, way: self.pass_on(p, zb, way))

        def passed_c(step):
            self.at_step(step, lambda zb, way: self.pass_c(p, zb, way))

        if s == 0:
            opened(last)
            opened(last - 1)
            passed_c(last)
            return
        if s <= last + 2:
            added(last + 1 - s)
        if last - 1 - s >= -1:
            opened(last - 1 - s)
        if last - s >= 0:
            passed_c(last - s)
        if s >= 2 and last + 2 - s >= 0:
            passed(last + 2 - s)
        if s == last + 1:
            self.own_c(p)
        if s == last + 2:
            self.turn_c(p)
        if s == last + 3:
            self.close(p)

    def sent(self, p):
        def line(zb, way):
            from_line = (self.z - way >= 0) & (self.z - way < self.depth)
            self.z_copy(p, zb, way).wait_send()
            pl.when(from_line)(lambda: self.zc_copy(p, zb, way, False).wait_send())
            pl.when(jnp.logical_not(from_line))(lambda: self.zc_copy(p, zb, way, True).wait_send())

        for zb in range(self.depth):
            self.a1(p, zb).wait_send()
            self.b1(p, zb, 0).wait_send()
            self.b1(p, zb, 1).wait_send()
            self.a2(p, zb).wait_send()
            self.b2(p, zb).wait_send()
        for step in range(self.depth - 1):
            self.at_step(step, line)
        self.cy(p).wait_send()
        self.cx(p).wait_send()


class SmallSum:
    def __init__(self, lines, buffer, send, recv):
        member = lax.axis_index("tensor")
        self.partners = [{"tensor": 1 - member}, {"dp": lines.x_peer}, {"dp": lines.y_peer}]
        for level in range(lines.depth.bit_length() - 1):
            reach = 1 << level
            way = 1 - 2 * ((lines.z // reach) % 2)
            self.partners.append({"dp": lines.me + 4 * reach * way})
        self.buffer, self.send, self.recv = buffer, send, recv

    def copy(self, step):
        return pltpu.make_async_remote_copy(
            src_ref=self.buffer.at[step],
            dst_ref=self.buffer.at[len(self.partners) + 1 + step],
            send_sem=self.send.at[step],
            recv_sem=self.recv.at[step],
            device_id=self.partners[step],
            device_id_type=MESH,
        )

    def step(self, step):
        if step:
            self.copy(step - 1).wait_recv()
            self.buffer[step] = self.buffer[step - 1] + self.buffer[len(self.partners) + step]
        if step < len(self.partners):
            self.copy(step).start()

    def sent(self):
        for step in range(len(self.partners)):
            self.copy(step).wait_send()


def adamw_update(master, moment, square, gradient, step_rate, decay_rate):
    moment_new = beta_one * moment + (1.0 - beta_one) * gradient
    square_new = beta_two * square + (1.0 - beta_two) * gradient * gradient
    moment_hat = moment_new * (1.0 / (1.0 - beta_one**STEP))
    square_hat = square_new * (1.0 / (1.0 - beta_two**STEP))
    master_new = master - step_rate * (
        moment_hat / (jnp.sqrt(square_hat) + adam_epsilon) + decay_rate * master
    )
    return (moment_new, square_new, master_new)


SCATTER_AT = {
    "reduce": {4: [(0, 0)]},
    "expand": {2: [(1, 0)], 4: [(2, 0), (0, 1), (1, 1)]},
    "norm": {-1: [(1, 2)], 1: [(2, 1)], 2: [(3, 0)], 3: [(0, 2)]},
    "attend": {1: [(2, 2), (3, 1)], 5: [(0, 3)], 8: [(2, 3)], 10: [(3, 2)], 13: [(3, 3), (4, 1)], 14: [(2, 4)], 19: [(1, 4)], 20: [(4, 2)], 22: [(3, 4)]},
    "project": {0: [(4, 0), (1, 3)], 1: [(5, 0), (1, 5)]},
    "terms": {1: [(5, 1)], 2: [(4, 3)]},
    "far": {-1: [(5, 2)], 0: [(0, 4), (2, 5)]},
    "near": {-1: [(5, 3), (3, 5)], 0: [(4, 4)]},
    "encoded": {-1: [(5, 4)], 1: [(0, 5)]},
    "end": [(5, 5), (4, 5)],
}


def back_kernel(
    depth, lengths_ref, dealing_ref, vectors_ref,
    whole_ref, far_ref, qkv_in, hidden_turned_in, upstream_in, context_in, totals_in,
    acc_in, normal_in, inverse_in, turned_in, active_in, slope_in, far_ctx_in, *rest,
):
    encoded_out, input_out, small_out, *rest = rest
    shards, rest = rest[:6], rest[6:]
    enc_pair, grad_ref, input_far, acc, arrived, merge_recv, small, score_bias, *rest = rest
    chunk_grads, *rest = rest
    grads, rest = [*[chunk_grads.at[p] for p in range(4)], *rest[:2]], rest[2:]
    buffers, rest = rest[: 6 * Scatter.buffers], rest[6 * Scatter.buffers :]
    small_send, small_recv, in_sem, load_sem, ctx_sem, far_send, far_recv, merge_sem, enc_sem, input_sem, *sems = rest
    lines = Scatter(depth, grads, shards, buffers, sems)
    sums = SmallSum(lines, small, small_send, small_recv)
    group = Group(lengths_ref, dealing_ref)
    member = lax.axis_index("tensor")
    rows, width = acc.shape
    total_rows = 2 * rows
    chunks, _, both = active_in.shape
    half = both // 2
    per_piece = chunks // 2
    piece_span = grads[0].shape[1]
    pairs = qkv_in.shape[0]
    inner = pairs * PAIR
    tall, short = 256, 128

    def rows_of(which):
        return pl.ds(pl.multiple_of(which * rows, rows), rows)

    def tile(step, size):
        return pl.ds(pl.multiple_of(step * size, size), size)

    def fetch(source, target, sem):
        return pltpu.make_async_copy(source, target, in_sem.at[sem])

    def phase(name, count, body):
        between = {
            step: [functools.partial(lines.stage, *stage) for stage in stages]
            for step, stages in SCATTER_AT.get(name, {}).items()
        }
        for act in between.pop(-1, ()):
            act()
        looped(count, body, between)

    def places_of(first):
        return first + lax.broadcasted_iota(jnp.int32, (tall, 1), 0)

    def add_sum(row, values):
        small[0, row : row + 1, :] += jnp.sum(values, axis=0, keepdims=True)

    def feed_phase(later, late, late_turned, turned, upstream, active, slope, inner_grad, expand_buf, reduce_buf, leaving):
        def active_load(j):
            slot = lax.rem(j, 2)
            return [pltpu.make_async_copy(active_in.at[j], active.at[slot], load_sem.at[slot, 4])]

        def loads(j):
            slot = lax.rem(j, 2)
            array, *firsts = chunk_columns(j, per_piece, half)
            copies = [pltpu.make_async_copy(slope_in.at[j], slope.at[slot], load_sem.at[slot, 5])]
            for kind, buf in enumerate((expand_buf, reduce_buf)):
                first = pl.multiple_of(firsts[kind], half)
                for side, source in enumerate((far_ref, whole_ref)):
                    copies.append(
                        pltpu.make_async_copy(
                            source.at[array, :, pl.ds(first, half)],
                            buf.at[slot, :, pl.ds(side * half, half)],
                            load_sem.at[slot, 2 * kind + side],
                        )
                    )
            return copies

        def taken(j, load):
            for copy in load(j):
                copy.wait()

            @pl.when(j + 1 < chunks)
            def _():
                for copy in load(j + 1):
                    copy.start()

        acc_copy = fetch(acc_in, acc, 0)
        acc_copy.start()
        fetches = [fetch(upstream_in, upstream, 1), fetch(turned_in, turned, 2)]
        for copy in fetches:
            copy.start()
        for copy in [*active_load(0), *loads(0)]:
            copy.start()
        greet_line(
            lines.me, lines.z, lines.y, lines.x, depth, [sums.partners[0], *sums.partners[3:]]
        )
        for copy in later:
            copy.start()
        small[0] = jnp.zeros(small.shape[1:], WIDE)
        score_bias[...] = group.score_bias(total_rows - LONGEST)
        acc_copy.wait()
        for copy in fetches:
            copy.wait()

        def late_tile(step):
            at = tile(step, short)
            unit, scale = norm(acc[at, :])
            upper = upstream[at, :].astype(WIDE)
            upstream[at, :] = (unit * vectors_ref[6:7, :] + vectors_ref[7:8, :]).astype(LOW)
            add_sum(6, upper * unit)
            add_sum(7, upper)
            grad = norm_back(upper * vectors_ref[6:7, :], unit, scale)
            grad_low = grad.astype(LOW)
            add_sum(5, grad_low.astype(WIDE))
            acc[at, :] = grad
            late[at, :] = grad_low
            late_turned[:, at] = grad.T.astype(LOW)

        looped(rows // short, late_tile, {})
        enc_near = pltpu.make_async_copy(upstream, enc_pair.at[member], enc_sem.at[2])
        enc_far = other_core(upstream, enc_pair.at[member], enc_sem.at[0], enc_sem.at[1])
        enc_near.start()
        enc_far.start()

        def send(k):
            slot = lax.rem(k, 2)
            return other_core(
                leaving.at[slot], arrived.at[slot], far_send.at[slot], far_recv.at[slot]
            )

        def own_columns(k):
            return pl.ds(pl.multiple_of(lax.rem(k, per_piece) * half, half), half)

        def finish(k):
            piece, slot = k // per_piece, lax.rem(k, 2)
            send(k).wait_recv()

            @pl.loop(0, width // tall)
            def _(step):
                at = tile(step, tall)
                chunk_grads[piece, at, own_columns(k)] += arrived[slot, at, :]

        def products(k, left, right):
            piece, slot = k // per_piece, lax.rem(k, 2)

            @pl.when(k >= 2)
            def _():
                send(k - 2).wait_send()

            parts = [
                dot_nn(left[step * tall : (step + 1) * tall, :], right[...])
                for step in range(width // tall)
            ]
            for step, part in enumerate(parts):
                at = slice(step * tall, (step + 1) * tall)
                leaving[slot, at, :] = part[:, 0:half].astype(LOW)
                chunk_grads[piece, at, own_columns(k)] = part[:, half:both].astype(LOW)

            @pl.when(k >= 1)
            def _():
                finish(k - 1)

            send(k).start()

        def reduce_chunk(j):
            taken(j, active_load)
            products(j, late_turned, active.at[lax.rem(j, 2)])

        def expand_chunk(j):
            slot = lax.rem(j, 2)
            taken(j, loads)
            total = jnp.zeros((1, both), WIDE)
            tiles = [slice(step * tall, (step + 1) * tall) for step in range(rows // tall)]
            parts = [dot_nn(late[at, :], reduce_buf[slot]) for at in tiles]
            for at, part in zip(tiles, parts, strict=True):
                grad = (part * slope[slot, at, :].astype(WIDE)).astype(LOW)
                inner_grad[at, :] = grad
                total = total + jnp.sum(grad.astype(WIDE), axis=0, keepdims=True)
                acc[at, :] += dot_nt(grad, expand_buf[slot])
            for which, side in ((1 - member, 0), (member, half)):
                row = 8 + which * 2 + j // per_piece
                small[0, pl.ds(row, 1), own_columns(j)] = total[:, side : side + half]
            products(chunks + j, turned, inner_grad)

        phase("reduce", chunks, reduce_chunk)
        phase("expand", chunks, expand_chunk)
        finish(2 * chunks - 1)
        for k in (2 * chunks - 2, 2 * chunks - 1):
            send(k).wait_send()
        enc_near.wait()
        enc_far.wait()

    def merge_phase(normal, inverse, near_ctx, far_ctx, merge, merge_far, fetches, turned, grad_own, grad_far, merge_send):
        for copy in fetches:
            copy.wait()

        def norm_tile(step):
            at = tile(step, short)
            grad = acc[at, :]
            unit = normal[at, :]
            add_sum(3, grad * unit)
            add_sum(4, grad)
            branch_grad = norm_back(grad * vectors_ref[3:4, :], unit, inverse[at, 0:1])
            branch_low = branch_grad.astype(LOW)
            add_sum(2, branch_low.astype(WIDE))
            acc[at, :] = branch_grad
            turned[:, at] = branch_grad.T.astype(LOW)
            grad_far[at, :] = dot_nn(branch_low, merge_far[...]).astype(LOW)
            grad_own[at, :] = dot_nn(branch_low, merge[...]).astype(LOW)

        phase("norm", rows // short, norm_tile)
        out_grad = other_core(grad_far, grad_ref.at[rows_of(member)], ctx_sem.at[0], ctx_sem.at[1])
        in_grad = pltpu.make_async_copy(grad_own, grad_ref.at[rows_of(member)], ctx_sem.at[2])
        out_grad.start()
        in_grad.start()
        out_merge = other_core(merge_send, merge_recv, merge_sem.at[0], merge_sem.at[1])

        def merge_step(which):
            @pl.when(which == 0)
            def _():
                for step in range(width // tall):
                    at = slice(step * tall, (step + 1) * tall)
                    merge_send[at, :] = dot_nn(turned[at, :], far_ctx[...]).astype(LOW)
                out_merge.start()

            @pl.when(which == 1)
            def _():
                out_merge.wait()
                for step in range(width // tall):
                    at = slice(step * tall, (step + 1) * tall)
                    grads[4][at, 0:inner] = (
                        dot_nn(turned[at, :], near_ctx[...]) + merge_recv[at, :].astype(WIDE)
                    ).astype(LOW)

        phase("merge", 2, merge_step)
        out_grad.wait()
        in_grad.wait()

    def early_phase(normal, inverse, near_ctx, far_ctx, merge, merge_far):
        merge_columns = pl.ds(whole_ref.shape[2] - inner, inner)
        fetches = [
            fetch(normal_in, normal, 3),
            fetch(inverse_in, inverse, 4),
            fetch(context_in.at[rows_of(member)], near_ctx, 5),
            fetch(far_ctx_in, far_ctx, 6),
            fetch(whole_ref.at[0, :, merge_columns], merge, 7),
            fetch(far_ref.at[0, :, merge_columns], merge_far, 8),
        ]
        pl.run_scoped(
            functools.partial(feed_phase, fetches),
            pltpu.VMEM((rows, width), LOW),
            pltpu.VMEM((width, rows), LOW),
            pltpu.VMEM((width, rows), LOW),
            pltpu.VMEM((rows, width), LOW),
            pltpu.VMEM((2, rows, both), LOW),
            pltpu.VMEM((2, rows, both), LOW),
            pltpu.VMEM((rows, both), LOW),
            pltpu.VMEM((2, width, both), LOW),
            pltpu.VMEM((2, width, both), LOW),
            pltpu.VMEM((2, width, half), LOW),
        )
        pl.run_scoped(
            functools.partial(
                merge_phase, normal, inverse, near_ctx, far_ctx, merge, merge_far, fetches
            ),
            pltpu.VMEM((width, rows), LOW),
            pltpu.VMEM((rows, inner), LOW),
            pltpu.VMEM((rows, inner), LOW),
            pltpu.VMEM((width, inner), LOW),
        )

    pl.run_scoped(
        early_phase,
        pltpu.VMEM((rows, width), WIDE),
        pltpu.VMEM((rows, 128), WIDE),
        pltpu.VMEM((rows, inner), LOW),
        pltpu.VMEM((rows, inner), LOW),
        pltpu.VMEM((width, inner), LOW),
        pltpu.VMEM((width, inner), LOW),
    )

    def last_phase(mixed):
        def attend_phase(qkv, context, upper, totals, dots, key_turned, queries, uppers, query_sum, hidden_turned):
            def loads(pair, slot):
                columns = pl.ds(pl.multiple_of(pair * PAIR, PAIR), PAIR)
                return [
                    pltpu.make_async_copy(qkv_in.at[pair], qkv.at[slot], load_sem.at[slot, 0]),
                    pltpu.make_async_copy(
                        context_in.at[:, columns], context.at[slot], load_sem.at[slot, 1]
                    ),
                    pltpu.make_async_copy(
                        grad_ref.at[:, columns], upper.at[slot], load_sem.at[slot, 2]
                    ),
                ]

            fetches = [fetch(totals_in, totals, 0)]
            for copy in [*loads(0, 0), *fetches]:
                copy.start()
            for copy in fetches:
                copy.wait()
            blocks = ((0, LONGEST), (LONGEST, total_rows - LONGEST))
            per_pair = total_rows // TILE

            def hidden_tile(step, slot):
                return pltpu.make_async_copy(
                    hidden_turned_in.at[tile(step, tall), :],
                    hidden_turned.at[slot],
                    load_sem.at[slot, 3],
                )

            def project(second):
                grad, first = (grads[5], 0) if second else (grads[4], inner)
                span = (pairs // 2) * 3 * PAIR
                columns = slice(span if second else 0, span * 2 if second else span)
                hidden_tile(0, 0).start()
                for step in range(width // tall):
                    if step + 1 < width // tall:
                        hidden_tile(step + 1, (step + 1) % 2).start()
                    hidden_tile(step, step % 2).wait()
                    grad[step * tall : (step + 1) * tall, first : first + span] = dot_nn(
                        hidden_turned[step % 2], mixed[:, columns]
                    ).astype(LOW)

            def pair_body(pair):
                slot = lax.rem(pair, 2)
                for copy in loads(pair, slot):
                    copy.wait()

                @pl.when(pair + 1 < pairs)
                def _():
                    for copy in loads(pair + 1, 1 - slot):
                        copy.start()

                attend_back_open(
                    qkv.at[slot], context.at[slot], upper.at[slot], dots, key_turned, queries, uppers
                )
                base = pair * 3 * PAIR

                def columns(which):
                    return pl.ds(pl.multiple_of(base + which * PAIR, PAIR), PAIR)

                for begin, size in blocks:
                    block = slice(begin, begin + size)
                    query_sum[:, block] = jnp.zeros((PAIR, size), WIDE)

                    def key_tile(step, begin=begin, size=size):
                        at, key_sum, value_sum = attend_back_tile(
                            qkv.at[slot], score_bias, totals.at[pair], dots, key_turned, queries, uppers, query_sum,
                            begin, size, step,
                        )
                        mixed[at, columns(1)] = key_sum.astype(LOW)
                        mixed[at, columns(2)] = value_sum.astype(LOW)

                    between = {}
                    for step in range(size // TILE):
                        number = begin // TILE + step
                        for act_pair in range(pairs):
                            for p, s in SCATTER_AT["attend"].get(act_pair * per_pair + number, ()):

                                def act(act_pair=act_pair, p=p, s=s):
                                    pl.when(pair == act_pair)(lambda: lines.stage(p, s))

                                between.setdefault(step, []).append(act)
                    looped(size // TILE, key_tile, between)
                    mixed[block, columns(0)] = (
                        (query_sum[:, block] * HEAD_DIM ** (-0.5)).T.astype(LOW)
                    )
                for which, row in ((0, 0), (2, 1)):
                    part = mixed[:, columns(which)].astype(WIDE)
                    spot = pl.multiple_of(member * inner + pair * PAIR, PAIR)
                    small[0, row : row + 1, pl.ds(spot, PAIR)] = jnp.sum(
                        part, axis=0, keepdims=True
                    )

            def project_stages(second):
                return [
                    functools.partial(project, second),
                    *[functools.partial(lines.stage, *st) for st in SCATTER_AT["project"][second]],
                ]

            looped(pairs, pair_body, {1: project_stages(0), 3: project_stages(1)})

        pl.run_scoped(
            attend_phase,
            pltpu.VMEM((2, total_rows, 3 * PAIR), LOW),
            pltpu.VMEM((2, total_rows, PAIR), LOW),
            pltpu.VMEM((2, total_rows, PAIR), LOW),
            pltpu.VMEM(totals_in.shape, WIDE),
            pltpu.VMEM((8, total_rows), WIDE),
            pltpu.VMEM((PAIR, total_rows), LOW),
            pltpu.VMEM((2, total_rows, PAIR), LOW),
            pltpu.VMEM((2, total_rows, PAIR), LOW),
            pltpu.VMEM((PAIR, total_rows), WIDE),
            pltpu.VMEM((2, tall, total_rows), LOW),
        )
        sums.step(0)

        def input_phase(weight, terms, leaving, pair):
            weight_copy = fetch(whole_ref.at[0, :, pl.ds(0, pairs * 3 * PAIR)], weight, 0)
            weight_copy.start()
            pair_copies = [fetch(enc_pair.at[i], pair.at[rows_of(i)], 3 + i) for i in range(2)]
            for copy in pair_copies:
                copy.start()
            weight_copy.wait()

            def term_tile(step):
                at = tile(step, tall)
                total = dot_nt(mixed[at, :], weight[...])
                own = rows // tall
                mine = step // own == member

                @pl.when(mine)
                def _():
                    terms[at, :] = (total + acc[tile(lax.rem(step, own), tall), :]).astype(LOW)

                @pl.when(jnp.logical_not(mine))
                def _():
                    terms[at, :] = total.astype(LOW)

            phase("terms", total_rows // tall, term_tile)
            sums.step(1)

            def own_rows(which, step):
                places = places_of(which * rows + step * tall)
                return picked_rows(group.moved(places, group.own, group.first), terms)

            def far_tile(step):
                leaving[tile(step, tall), :] = own_rows(1 - member, step).astype(LOW)

            phase("far", rows // tall, far_tile)
            crossing = other_core(leaving, input_far, input_sem.at[0], input_sem.at[1])
            crossing.start()
            sums.step(2)

            def near_tile(step):
                acc[tile(step, tall), :] = own_rows(member, step)

            phase("near", rows // tall, near_tile)
            sums.step(3)
            crossing.wait()
            back = fetch(input_far, leaving, 2)
            back.start()
            back.wait()

            @pl.loop(0, rows // short)
            def _(step):
                at = tile(step, short)
                leaving[at, :] = (acc[at, :] + leaving[at, :].astype(WIDE)).astype(LOW)

            done = fetch(leaving, input_out, 2)
            done.start()
            for copy in pair_copies:
                copy.wait()

            def encoded_tile(step):
                places = places_of(member * rows + step * tall)
                index = group.moved(places, group.dealt, group.first)
                terms[tile(step, tall), :] = picked_rows(index, pair).astype(LOW)

            phase("encoded", rows // tall, encoded_tile)
            done.wait()
            done = fetch(terms.at[pl.ds(0, rows)], encoded_out, 2)
            done.start()
            done.wait()

        pl.run_scoped(
            input_phase,
            pltpu.VMEM((width, pairs * 3 * PAIR), LOW),
            pltpu.VMEM((total_rows, width), LOW),
            pltpu.VMEM((rows, width), LOW),
            pltpu.VMEM((total_rows, width), LOW),
        )

    pl.run_scoped(last_phase, pltpu.VMEM((total_rows, pairs * 3 * PAIR), LOW))

    for step in range(4, len(sums.partners) + 1):
        sums.step(step)
    small_out[...] = small[len(sums.partners)]
    for st in SCATTER_AT["end"]:
        lines.stage(*st)
    sums.sent()
    for p in range(len(grads)):
        lines.sent(p)


def finish_kernel(
    small_ref, vectors_ref, vectors_first, vectors_second, hidden_ref, hidden_first, hidden_second, *rest
):
    shards, (encoded_in, input_in), states_in, rest = rest[:6], rest[6:8], rest[8:20], rest[20:]
    encoded_out, input_out, vector_grad_ref, *rest = rest
    states_out, small_out, ins, outs = rest[:12], rest[12:18], rest[18:30], rest[30:42]
    held, state_sem, out_sem, pass_sem = rest[42:]
    width = vectors_ref.shape[1]
    inner = ins[3].shape[1]
    pairs = inner // PAIR
    span = shards[0].shape[1]
    loads = [pltpu.make_async_copy(states_in[i], ins[i], state_sem.at[i]) for i in range(12)]
    writes = [pltpu.make_async_copy(outs[i], states_out[i], out_sem.at[i]) for i in range(12)]
    rows_in = [
        pltpu.make_async_copy(one, held.at[i], pass_sem.at[0, i])
        for i, one in enumerate((encoded_in, input_in))
    ]
    passes = [
        pltpu.make_async_copy(held.at[i], one, pass_sem.at[1, i])
        for i, one in enumerate((encoded_out, input_out))
    ]
    for copy in [*rows_in, *reversed(loads)]:
        copy.start()
    vector_grad_ref[...] = small_ref[0:8, :]
    states = vectors_ref[...], vectors_first[...], vectors_second[...]
    for i, value in enumerate(adamw_update(*states, small_ref[0:8, :], rate_vectors, 0.0)):
        small_out[i][...] = value
    for i in range(hidden_ref.shape[1] // width):
        columns = slice(i * width, (i + 1) * width)
        states = hidden_ref[:, columns], hidden_first[:, columns], hidden_second[:, columns]
        grad = small_ref[8 + i : 9 + i, :]
        for n, value in enumerate(adamw_update(*states, grad, rate_hidden, 0.0)):
            small_out[3 + n][:, columns] = value

    def update(matrix, lead, columns, grad, grad_columns):
        rate = (rate_project, rate_merge, rate_expand, rate_reduce)[matrix]

        @pl.loop(0, grad.shape[0] // 16)
        def _(step):
            at = pl.ds(pl.multiple_of(step * 16, 16), 16)
            old = [ins[3 * matrix + i][(*lead, at, columns)] for i in range(3)]
            new = adamw_update(*old, grad[at, grad_columns], rate, weight_decay)
            for i in range(3):
                outs[3 * matrix + i][(*lead, at, columns)] = new[i]

    for matrix in (3, 2, 1, 0):
        mine = slice(3 * matrix, 3 * matrix + 3)
        for copy in loads[mine]:
            copy.wait()
        if matrix >= 2:
            for i in range(2):
                columns = slice(i * span, (i + 1) * span)
                update(matrix, (), columns, shards[2 * (3 - matrix) + i], slice(0, span))
        elif matrix == 1:
            update(matrix, (), slice(0, inner), shards[4], slice(0, inner))
        else:
            for pair in range(pairs):
                piece, begin = (4, inner) if pair < pairs // 2 else (5, 0)
                for c in range(3):
                    at = begin + (3 * (pair % (pairs // 2)) + c) * PAIR
                    columns = slice(pair * PAIR, (pair + 1) * PAIR)
                    update(matrix, (c,), columns, shards[piece], slice(at, at + PAIR))
        for copy in writes[mine]:
            copy.start()
        if matrix == 3:
            for copy in rows_in:
                copy.wait()
            for copy in passes:
                copy.start()
    for copy in [*writes, *passes]:
        copy.wait()


def finish(small, shards, rows_out, matrices, vectors, hidden):
    states = [one for matrix in matrices for one in matrix]
    shape, sem = jax.ShapeDtypeStruct, pltpu.SemaphoreType.DMA
    vmem, anywhere = pl.BlockSpec(memory_space=pltpu.VMEM), pl.BlockSpec(memory_space=pl.ANY)
    held = [pltpu.VMEM(one.shape, WIDE) for one in states]
    return pl.pallas_call(
        finish_kernel,
        in_specs=[*[vmem] * 13, *[anywhere] * 14],
        out_specs=[*[anywhere] * 2, vmem, *[anywhere] * 12, *[vmem] * 6],
        out_shape=[
            *[shape(one.shape, LOW) for one in rows_out],
            shape((8, small.shape[1]), WIDE),
            *[shape(one.shape, WIDE) for one in (*states, *vectors, *hidden)],
        ],
        scratch_shapes=[
            *held,
            *held,
            pltpu.VMEM((2, *rows_out[0].shape), LOW),
            sem((12,)),
            sem((12,)),
            sem((2, 2)),
        ],
        compiler_params=pltpu.CompilerParams(vmem_limit_bytes=63 * MIB),
    )(small, *vectors, *hidden, *shards, *rows_out, *states)


def back(lengths, dealing, vectors, whole, far, kept, parts):
    qkv, hidden_turned, upstream, context, totals, acc, *_ = kept
    rows, width = acc.shape
    total_rows, inner = context.shape
    depth, shard_rows = parts // 4, width // parts
    half, pair_span = 256, 3 * PAIR * (qkv.shape[0] // 2)
    piece_span = whole.shape[2] // 2
    spans = (*[piece_span] * 4, inner + pair_span, pair_span)
    classes = []
    for span in spans:
        third = max(128, span // 5 // 128 * 128)
        if (span - third) % 256:
            third += 128
        classes.append(((span - third) // 2, (span - third) // 2, third))
    shape, sem = jax.ShapeDtypeStruct, pltpu.SemaphoreType.DMA
    vmem, anywhere = pl.BlockSpec(memory_space=pltpu.VMEM), pl.BlockSpec(memory_space=pl.ANY)
    steps = 3 + depth.bit_length() - 1
    results = pl.pallas_call(
        functools.partial(back_kernel, depth),
        in_specs=[
            *[pl.BlockSpec(memory_space=pltpu.SMEM)] * 2,
            vmem,
            *[anywhere] * (2 + len(kept)),
        ],
        out_specs=[*[anywhere] * 2, *[vmem] * (1 + len(spans)), *[anywhere] * 3],
        out_shape=[
            shape((rows, width), LOW),
            shape((rows, width), LOW),
            shape((16, width), WIDE),
            *[shape((shard_rows, span), WIDE) for span in spans],
            shape((2, rows, width), LOW),
            shape((total_rows, inner), LOW),
            shape((rows, width), LOW),
        ],
        scratch_shapes=[
            pltpu.VMEM((rows, width), WIDE),
            pltpu.VMEM((2, width, half), LOW),
            pltpu.VMEM((width, inner), LOW),
            pltpu.VMEM((2 * steps + 1, 16, width), WIDE),
            pltpu.VMEM((total_rows - LONGEST, total_rows - LONGEST), WIDE),
            pltpu.VMEM((4, width, piece_span), LOW),
            *[pltpu.VMEM((width, span), LOW) for span in spans[4:]],
            *Scatter.scratch(depth, shard_rows, classes),
            sem((steps,)),
            sem((steps,)),
            sem((9,)),
            sem((2, 6)),
            sem((3,)),
            sem((2,)),
            sem((2,)),
            sem((2,)),
            sem((3,)),
            sem((2,)),
            *Scatter.semaphores(depth, len(spans)),
        ],
        compiler_params=pltpu.CompilerParams(
            collective_id=1, has_side_effects=True, vmem_limit_bytes=63 * MIB
        ),
    )(lengths, dealing, vectors, whole, far, *kept)
    return results[:2], results[2], results[3 : 3 + len(spans)]


def by_kernels(tokens, cotangent, lengths, dealing, project, merge, expand, reduce, vectors, hidden, parts):
    hidden = tuple(one.reshape(1, -1) for one in hidden)
    matrices = (project, merge, expand, reduce)
    whole, far, *kept = front(
        lengths, dealing, *[one[0] for one in matrices], vectors[0], hidden[0], tokens, cotangent, parts
    )
    rows_out, small, shards = back(lengths, dealing, vectors[0], whole, far, kept, parts)
    results = finish(small, shards, rows_out, matrices, vectors, hidden)
    encoded, input_grad, vector_grad = results[:3]
    news = [results[3 + 3 * i : 6 + 3 * i] for i in range(6)]
    return (
        encoded,
        input_grad,
        *news[0],
        *[one.T for one in news[1]],
        *news[2],
        *[one.T for one in news[3]],
        *news[4],
        *[one.reshape(-1) for one in news[5]],
        vector_grad,
    )


def local(
    tokens,
    cotangent,
    lengths,
    dealing,
    project_weight,
    project_first,
    project_second,
    merge_weight,
    merge_first,
    merge_second,
    expand_weight,
    expand_first,
    expand_second,
    reduce_weight,
    reduce_first,
    reduce_second,
    vectors,
    vector_first,
    vector_second,
    hidden_bias,
    hidden_first,
    hidden_second,
):
    parts = lax.axis_size("dp")
    member = lax.axis_index("tensor")
    other = 1 - member
    half_rows, model_width = tokens.shape
    total_rows = 2 * half_rows
    width_half = project_weight.shape[2]
    pairs = width_half // PAIR
    hidden_half = expand_weight.shape[1]
    shard_rows = expand_weight.shape[0]
    own_begin = member * half_rows
    by_kernel = parts % 4 == 0 and (parts & (parts - 1)) == 0 and shard_rows % 16 == 0

    def swap(value):
        return lax.ppermute(value, "tensor", [(0, 1), (1, 0)])

    def own(value, size, which=member):
        return lax.dynamic_slice_in_dim(value, which * size, size, 0)

    if by_kernel:
        return by_kernels(
            tokens, cotangent, lengths, dealing,
            (project_weight, project_first, project_second),
            (merge_weight.T, merge_first.T, merge_second.T),
            (expand_weight, expand_first, expand_second),
            (reduce_weight.T, reduce_first.T, reduce_second.T),
            (vectors, vector_first, vector_second),
            (hidden_bias, hidden_first, hidden_second),
            parts,
        )

    segment, own_of, dealt_of, from_own, from_dealt = layout(lengths[0], dealing[0], total_rows)
    dealt_of = own(dealt_of, half_rows)
    short = segment[LONGEST:]
    score_bias = jnp.where(short[:, None] == short[None, :], 0.0, masked_score).astype(WIDE)

    def own_first(index):
        return lax.rem(index - own_begin + total_rows, total_rows)

    projections = (
        project_weight.reshape(3, shard_rows, pairs, PAIR)
        .transpose(1, 2, 0, 3)
        .reshape(shard_rows, 3 * width_half)
    )
    quarter = hidden_half // 2
    reduce_turned = reduce_weight.T
    shards = jnp.stack(
        [
            jnp.concatenate([projections, merge_weight.T], axis=1),
            jnp.concatenate([expand_weight[:, :quarter], reduce_turned[:, :quarter]], axis=1),
            jnp.concatenate([expand_weight[:, quarter:], reduce_turned[:, quarter:]], axis=1),
        ]
    ).astype(LOW)
    zeros_pair = jnp.zeros((pairs, PAIR), WIDE)
    bias_row = jnp.concatenate(
        [
            own(vectors[0], width_half).reshape(pairs, PAIR),
            zeros_pair,
            own(vectors[1], width_half).reshape(pairs, PAIR),
        ],
        axis=1,
    ).reshape(pairs, 1, 3 * PAIR)
    whole = lax.all_gather(shards, "dp", axis=1, tiled=True)
    far = swap(whole)
    token_pair = jnp.concatenate([tokens, swap(tokens)], axis=0)
    upper_pair = jnp.concatenate([cotangent, swap(cotangent)], axis=0)
    hidden = dot_nn(pick_rows(own_first(own_of), total_rows), token_pair).astype(LOW)
    upstream = dot_nn(pick_rows(own_first(dealt_of), total_rows), upper_pair).astype(LOW)
    qkv = jnp.einsum(
        "rd,dpc->prc",
        hidden,
        whole[0, :, : 3 * width_half].reshape(model_width, pairs, 3 * PAIR),
        preferred_element_type=WIDE,
    )
    qkv = (qkv + bias_row).astype(LOW)
    context, totals = attend(qkv, score_bias)

    (
        encoded, branch_grad, context_grad, merge_grad, expand_grad, reduce_grad, sums, hidden_part_own, hidden_part_far,
    ) = feed_block(
        context,
        whole,
        far,
        own(hidden, half_rows),
        upstream,
        vectors,
        own(hidden_bias, hidden_half),
        own(hidden_bias, hidden_half, other),
    )
    encoded_pair = jnp.concatenate([encoded, swap(encoded)], axis=0)
    encoded_out = dot_nn(
        pick_rows(own_first(own(from_dealt, half_rows)), total_rows), encoded_pair
    ).astype(LOW)
    mixed_grads = attend_back(qkv, score_bias, context, context_grad, totals)
    mixed_sums = jnp.sum(mixed_grads.astype(WIDE), axis=1).reshape(pairs, 3, PAIR)
    mixed_grads = mixed_grads.transpose(1, 0, 2).reshape(total_rows, 3 * width_half)
    project_grad = dot_tn(hidden, mixed_grads)
    input_terms = dot_nt(mixed_grads, whole[0, :, : 3 * width_half])
    own_part = own(input_terms, half_rows) + branch_grad
    input_terms = lax.dynamic_update_slice_in_dim(input_terms, own_part, own_begin, 0).astype(LOW)
    input_far = swap(
        dot_nn(pick_rows(own(from_own, half_rows, other), total_rows), input_terms).astype(LOW)
    )
    input_grad = (
        dot_nn(pick_rows(own(from_own, half_rows), total_rows), input_terms)
        + input_far.astype(WIDE)
    ).astype(LOW)
    zeros_width = jnp.zeros((model_width,), WIDE)
    zeros_hidden = jnp.zeros_like(hidden_bias)
    hidden_total = lax.dynamic_update_slice_in_dim(
        lax.dynamic_update_slice_in_dim(
            zeros_hidden, hidden_part_own, member * hidden_half, 0
        ),
        hidden_part_far,
        other * hidden_half,
        0,
    )
    vector_rows = [
        lax.dynamic_update_slice_in_dim(
            zeros_width, mixed_sums[:, c].reshape(-1), member * width_half, 0
        )
        for c in (0, 2)
    ]
    small = jnp.concatenate(
        [
            jnp.stack(vector_rows),
            sums[2:],
            hidden_total.reshape(-1, model_width),
            jnp.zeros((4, model_width), WIDE),
        ],
        axis=0,
    )
    grads = [
        lax.psum_scatter(g.astype(LOW), "dp", scatter_dimension=0, tiled=True).astype(WIDE)
        for g in (project_grad, merge_grad, expand_grad, reduce_grad)
    ]
    small = lax.psum(small, ("dp", "tensor"))
    project_shard, merge_shard, expand_shard, reduce_shard = grads
    project_shard = (
        project_shard.reshape(shard_rows, pairs, 3, PAIR)
        .transpose(2, 0, 1, 3)
        .reshape(3, shard_rows, width_half)
    )
    vector_grad = small[:8]
    hidden_grad = small[8:12].reshape(-1)
    return (
        encoded_out,
        input_grad,
        *adamw_update(
            project_weight, project_first, project_second, project_shard, rate_project, weight_decay
        ),
        *adamw_update(
            merge_weight, merge_first, merge_second, merge_shard.T, rate_merge, weight_decay
        ),
        *adamw_update(
            expand_weight, expand_first, expand_second, expand_shard, rate_expand, weight_decay
        ),
        *adamw_update(
            reduce_weight, reduce_first, reduce_second, reduce_shard.T, rate_reduce, weight_decay
        ),
        *adamw_update(vectors, vector_first, vector_second, vector_grad, rate_vectors, 0.0),
        *adamw_update(hidden_bias, hidden_first, hidden_second, hidden_grad, rate_hidden, 0.0),
        vector_grad,
    )


def solution(mesh):
    sharded = (
        P("dp", None),
        P("dp", None),
        *[P(None, "dp", "tensor")] * 3,
        *[P("tensor", "dp")] * 3,
        *[P("dp", "tensor")] * 3,
        *[P("tensor", "dp")] * 3,
        *[P()] * 6,
    )
    rows = P(("dp", "tensor"), None)
    return jax.shard_map(
        local,
        mesh=mesh,
        in_specs=(rows, rows, *sharded),
        out_specs=(rows, rows, *sharded[2:], P()),
        check_vma=False,
    )
```

```python
import functools

import jax
import jax.numpy as jnp
from jax import lax
from jax.experimental import pallas as pl
from jax.experimental.pallas import tpu as pltpu
from jax.sharding import PartitionSpec as P

HEAD_DIM = 64
LONGEST = 1024
STEP = 10
PAIR = 2 * HEAD_DIM
TILE = 256
MIB = 1024 * 1024
MESH = pl.DeviceIdType.MESH
LOW = jnp.bfloat16
WIDE = jnp.float32

beta_one = 0.9
beta_two = 0.999
adam_epsilon = 1e-08
weight_decay = 0.01
norm_epsilon = 1e-05
masked_score = -1e30
rate_project = 0.03
rate_merge = 0.3
rate_expand = 0.03
rate_reduce = 0.015
rate_vectors = 0.4
rate_hidden = 0.1


def dot_nn(a, b):
    return jnp.dot(a, b, preferred_element_type=WIDE)


def dot_nt(a, b):
    return lax.dot_general(a, b, (((1,), (1,)), ((), ())), preferred_element_type=WIDE)


def dot_tn(a, b):
    return lax.dot_general(a, b, (((0,), (0,)), ((), ())), preferred_element_type=WIDE)


def layout(lengths_row, dealing_row, total_rows):
    slots = jnp.arange(lengths_row.shape[0], dtype=jnp.int32)
    places = jnp.arange(total_rows, dtype=jnp.int32)
    rank_of = jnp.sum(jnp.where(dealing_row[None, :] == slots[:, None], slots[None, :], 0), axis=1)
    own_start = jnp.cumsum(lengths_row) - lengths_row
    dealt_start = jnp.sum(
        jnp.where(rank_of[None, :] < rank_of[:, None], lengths_row[None, :], 0), axis=1
    )
    longest = lengths_row == LONGEST
    short = jnp.where(longest, 0, lengths_row)
    start = jnp.where(longest, 0, LONGEST + jnp.cumsum(short) - short)

    def inside(begin):
        return (places[:, None] >= begin[None, :]) & (
            places[:, None] < (begin + lengths_row)[None, :]
        )

    def moved(begin, end):
        return places + jnp.sum(jnp.where(inside(begin), (end - begin)[None, :], 0), axis=1)

    segment = jnp.sum(jnp.where(inside(start), slots[None, :], 0), axis=1)
    return (
        segment,
        moved(start, own_start),
        moved(start, dealt_start),
        moved(own_start, start),
        moved(dealt_start, start),
    )


def pick_rows(index, rows):
    places = jnp.arange(rows, dtype=jnp.int32)
    return (index[:, None] == places[None, :]).astype(LOW)


class Group:
    def __init__(self, lengths_ref, dealing_ref):
        count = lengths_ref.shape[1]
        self.lengths = [lengths_ref[0, s] for s in range(count)]
        order = [dealing_ref[0, i] for i in range(count)]
        rank = [sum(jnp.where(order[i] == s, i, 0) for i in range(count)) for s in range(count)]
        short = [jnp.where(length == LONGEST, 0, length) for length in self.lengths]
        self.own, self.dealt, self.first = [], [], []
        own = own_short = jnp.int32(0)
        for s in range(count):
            self.own.append(own)
            self.first.append(jnp.where(self.lengths[s] == LONGEST, 0, LONGEST + own_short))
            self.dealt.append(
                sum(jnp.where(rank[j] < rank[s], self.lengths[j], 0) for j in range(count))
            )
            own, own_short = own + self.lengths[s], own_short + short[s]

    def inside(self, places, begin, s):
        return (places >= begin[s]) & (places < begin[s] + self.lengths[s])

    def moved(self, places, begin, end):
        total = places
        for s in range(len(begin)):
            total = total + jnp.where(self.inside(places, begin, s), end[s] - begin[s], 0)
        return total

    def score_bias(self, count):
        sides = []
        for shape, axis in (((count, 1), 0), ((1, count), 1)):
            places = lax.broadcasted_iota(jnp.int32, shape, axis) + LONGEST
            segment = jnp.zeros_like(places)
            for s in range(len(self.first)):
                segment = segment + jnp.where(self.inside(places, self.first, s), s, 0)
            sides.append(segment)
        return jnp.where(sides[0] == sides[1], 0.0, masked_score).astype(WIDE)


def picked_rows(index, source):
    places = lax.broadcasted_iota(jnp.int32, (index.shape[0], source.shape[0]), 1)
    return dot_nn(jnp.where(index == places, 1.0, 0.0).astype(LOW), source[...])


def attend_tile(qkv_ref, pair, bias_ref, begin, size, step, context_ref, columns, total_ref):
    lane = lax.broadcasted_iota(jnp.int32, (1, PAIR), 1)
    scale = HEAD_DIM ** (-0.5)
    first = pl.multiple_of(begin + step * TILE, TILE)
    query = qkv_ref[pair, pl.ds(first, TILE), 0:PAIR]
    key = qkv_ref[pair, begin : begin + size, PAIR : 2 * PAIR]
    value = qkv_ref[pair, begin : begin + size, 2 * PAIR : 3 * PAIR]
    outcome = []
    chosen = [jnp.where(lane // HEAD_DIM == head, scale, 0.0).astype(LOW) for head in range(2)]
    scores = [dot_nt(query * chosen[head], key) for head in range(2)]
    for head in range(2):
        score = scores[head]
        if begin:
            inner = pl.multiple_of(step * TILE, TILE)
            score = score + bias_ref[pl.ds(inner, TILE), :]
        top = jnp.max(score, axis=1, keepdims=True)
        exponent = jnp.exp(score - top)
        total = jnp.sum(exponent, axis=1, keepdims=True)
        outcome.append(dot_nn(exponent.astype(LOW), value) / total)
        log_total = jnp.broadcast_to(top + jnp.log(total), (TILE, PAIR))
        total_ref[pair, head : head + 1, pl.ds(first, TILE)] = log_total.T[0:1, :]
    context_ref[pl.ds(first, TILE), columns] = jnp.where(
        lane < HEAD_DIM, outcome[0], outcome[1]
    ).astype(LOW)


def attend_kernel(qkv_ref, bias_ref, context_ref, total_ref):
    rows = qkv_ref.shape[1]
    for begin, size in ((0, LONGEST), (LONGEST, rows - LONGEST)):

        @pl.loop(0, size // TILE)
        def _(step):
            attend_tile(
                qkv_ref, 0, bias_ref, begin, size, step, context_ref, slice(0, PAIR), total_ref
            )


def attend(qkv, bias):
    pairs, rows, width = qkv.shape
    return pl.pallas_call(
        attend_kernel,
        grid=(pairs,),
        in_specs=[
            pl.BlockSpec((1, rows, width), lambda p: (p, 0, 0)),
            pl.BlockSpec(bias.shape, lambda p: (0, 0)),
        ],
        out_specs=[
            pl.BlockSpec((rows, PAIR), lambda p: (0, p)),
            pl.BlockSpec((1, 8, rows), lambda p: (p, 0, 0)),
        ],
        out_shape=[
            jax.ShapeDtypeStruct((rows, pairs * PAIR), LOW),
            jax.ShapeDtypeStruct((pairs, 8, rows), WIDE),
        ],
        compiler_params=pltpu.CompilerParams(vmem_limit_bytes=48 * MIB),
    )(qkv, bias)


def attend_back_open(qkv_ref, context_ref, upper_ref, dots, key_turned, queries, uppers):
    lane = lax.broadcasted_iota(jnp.int32, (1, PAIR), 1)
    product = (upper_ref[...].astype(WIDE) * context_ref[...].astype(WIDE)).T
    for head in range(2):
        band = slice(head * HEAD_DIM, (head + 1) * HEAD_DIM)
        dots[head : head + 1, :] = jnp.sum(product[band, :], axis=0, keepdims=True)
        chosen = lane // HEAD_DIM == head
        queries[head] = qkv_ref[:, 0:PAIR] * jnp.where(chosen, HEAD_DIM ** (-0.5), 0.0).astype(LOW)
        uppers[head] = upper_ref[...] * jnp.where(chosen, 1.0, 0.0).astype(LOW)
    key_turned[...] = qkv_ref[:, PAIR : 2 * PAIR].astype(WIDE).T.astype(LOW)


def attend_back_tile(
    qkv_ref, bias_ref, total_ref, dots, key_turned, queries, uppers, query_sum, begin, size, step
):
    block = slice(begin, begin + size)
    first = pl.multiple_of(begin + step * TILE, TILE)
    key = qkv_ref[pl.ds(first, TILE), PAIR : 2 * PAIR]
    value = qkv_ref[pl.ds(first, TILE), 2 * PAIR : 3 * PAIR]
    key_sum = jnp.zeros((TILE, PAIR), WIDE)
    value_sum = jnp.zeros((TILE, PAIR), WIDE)
    scores = [dot_nt(key, queries[head, block, :]) for head in range(2)]
    weight_grads = [dot_nt(value, uppers[head, block, :]) for head in range(2)]
    for head in range(2):
        band = slice(head * HEAD_DIM, (head + 1) * HEAD_DIM)
        score = scores[head]
        if begin:
            inner = pl.multiple_of(step * TILE, TILE)
            score = score + bias_ref[pl.ds(inner, TILE), :]
        probability = jnp.exp(score - total_ref[head : head + 1, block])
        score_grads = probability * (weight_grads[head] - dots[head : head + 1, block])
        score_grads = score_grads.astype(LOW)
        value_sum = value_sum + dot_nn(probability.astype(LOW), uppers[head, block, :])
        key_sum = key_sum + dot_nn(score_grads, queries[head, block, :])
        query_sum[band, block] += dot_nn(key_turned[band, pl.ds(first, TILE)], score_grads)
    return pl.ds(first, TILE), key_sum, value_sum


def attend_back_kernel(
    qkv_ref, bias_ref, context_ref, grad_ref, total_ref, out_ref, dots, key_turned, queries, uppers, query_sum
):
    rows = qkv_ref.shape[1]
    qkv = qkv_ref.at[0]
    attend_back_open(qkv, context_ref, grad_ref, dots, key_turned, queries, uppers)
    for begin, size in ((0, LONGEST), (LONGEST, rows - LONGEST)):
        block = slice(begin, begin + size)
        query_sum[:, block] = jnp.zeros((PAIR, size), WIDE)

        @pl.loop(0, size // TILE)
        def _(step):
            at, key_sum, value_sum = attend_back_tile(
                qkv, bias_ref, total_ref.at[0], dots, key_turned, queries, uppers, query_sum, begin, size, step
            )
            out_ref[0, at, PAIR : 2 * PAIR] = key_sum.astype(LOW)
            out_ref[0, at, 2 * PAIR : 3 * PAIR] = value_sum.astype(LOW)

        out_ref[0, block, 0:PAIR] = (query_sum[:, block] * HEAD_DIM ** (-0.5)).T.astype(LOW)


def attend_back(qkv, bias, context, grad, totals):
    pairs, rows, width = qkv.shape
    return pl.pallas_call(
        attend_back_kernel,
        grid=(pairs,),
        in_specs=[
            pl.BlockSpec((1, rows, width), lambda p: (p, 0, 0)),
            pl.BlockSpec(bias.shape, lambda p: (0, 0)),
            pl.BlockSpec((rows, PAIR), lambda p: (0, p)),
            pl.BlockSpec((rows, PAIR), lambda p: (0, p)),
            pl.BlockSpec((1, 8, rows), lambda p: (p, 0, 0)),
        ],
        out_specs=pl.BlockSpec((1, rows, width), lambda p: (p, 0, 0)),
        out_shape=jax.ShapeDtypeStruct(qkv.shape, LOW),
        scratch_shapes=[
            pltpu.VMEM((8, rows), WIDE),
            pltpu.VMEM((PAIR, rows), LOW),
            pltpu.VMEM((2, rows, PAIR), LOW),
            pltpu.VMEM((2, rows, PAIR), LOW),
            pltpu.VMEM((PAIR, rows), WIDE),
        ],
        compiler_params=pltpu.CompilerParams(vmem_limit_bytes=48 * MIB),
    )(qkv, bias, context, grad, totals)


def place():
    me = lax.axis_index("dp")
    z, y, x = me // 4, (me // 2) % 2, me % 2
    return me, z, y, x


def line_slots(z, depth):
    slots = []
    for step in range(depth - 1):
        slots.append((z - 1 - step, z - 1 - step >= 0, 1))
        slots.append((z + 1 + step, z + 1 + step < depth, -1))
    return slots


def remote(source, target, send, receive, device):
    return pltpu.make_async_remote_copy(
        src_ref=source,
        dst_ref=target,
        send_sem=send,
        recv_sem=receive,
        device_id={"dp": device},
        device_id_type=MESH,
    )


def greet_line(me, z, y, x, depth, extra=()):
    barrier = pltpu.get_barrier_semaphore()
    for peer in (z * 4 + y * 2 + 1 - x, z * 4 + (1 - y) * 2 + x):
        pl.semaphore_signal(barrier, inc=1, device_id={"dp": peer}, device_id_type=MESH)

    @pl.when(z > 0)
    def _():
        pl.semaphore_signal(barrier, inc=1, device_id={"dp": me - 4}, device_id_type=MESH)

    @pl.when(z < depth - 1)
    def _():
        pl.semaphore_signal(barrier, inc=1, device_id={"dp": me + 4}, device_id_type=MESH)

    for peer in extra:
        pl.semaphore_signal(barrier, inc=1, device_id=peer, device_id_type=MESH)
    ends = jnp.where(z > 0, 1, 0) + jnp.where(z < depth - 1, 1, 0)
    pl.semaphore_wait(barrier, 2 + len(extra) + ends)


def other_core(source, target, send, receive):
    return pltpu.make_async_remote_copy(
        src_ref=source,
        dst_ref=target,
        send_sem=send,
        recv_sem=receive,
        device_id={"tensor": 1 - lax.axis_index("tensor")},
        device_id_type=MESH,
    )


class Gather:
    def __init__(self, depth, parts, whole, far, table, sems):
        self.whole, self.far = whole, far
        self.depth = depth
        self.me, self.z, self.y, self.x = place()
        self.x_peer = self.z * 4 + self.y * 2 + 1 - self.x
        self.y_peer = self.z * 4 + (1 - self.y) * 2 + self.x
        self.rows = whole.shape[1] // parts
        self.array = [array for array, *_ in table]
        self.a, self.b, self.ab, self.c, self.all = [], [], [], [], []
        for _, base, width, third in table:
            side = (width - third) // 2
            self.a.append((base, side))
            self.b.append((base + side, side))
            self.ab.append((base, 2 * side))
            self.c.append((base + 2 * side, third))
            self.all.append((base, width))
        (
            self.z_send, self.z_recv, self.zc_send, self.zc_recv, self.xa_send, self.xa_recv, self.yb_send, self.yb_recv,
            self.ya_send, self.ya_recv, self.xb_send, self.xb_recv, self.c_send, self.c_recv, self.far_send, self.far_recv,
        ) = sems
        self.slots = line_slots(self.z, depth)

    @staticmethod
    def semaphores(depth, pieces):
        sem = pltpu.SemaphoreType.DMA
        return [
            *[sem((pieces, depth + 1)), sem((pieces, depth))] * 2,
            *[sem((pieces, depth))] * 4,
            *[sem((pieces, depth, 2))] * 4,
            sem((pieces, 2)),
            sem((pieces, 2)),
            sem((pieces,)),
            sem((pieces,)),
        ]

    def block(self, zb, yb, xb):
        return zb * 4 + yb * 2 + xb

    def cut(self, ref, p, block, count, columns):
        first = pl.multiple_of(block * self.rows, self.rows)
        return ref.at[self.array[p], pl.ds(first, count * self.rows), pl.ds(*columns)]

    def copy(self, p, block, count, columns, send, receive, device):
        part = self.cut(self.whole, p, block, count, columns)
        return remote(part, part, send, receive, device)

    def forward(self, p, block, count, columns):
        if p == 0:
            return
        other_core(
            self.cut(self.whole, p, block, count, columns),
            self.cut(self.far, p, block, count, columns),
            self.far_send.at[p],
            self.far_recv.at[p],
        ).start()

    def far_copy(self, p):
        part = self.far.at[self.array[p], :, pl.ds(*self.all[p])]
        return other_core(part, part, self.far_send.at[p], self.far_recv.at[p])

    def z_copy(self, p, zb, way, back=False):
        block = self.block(zb, self.y, self.x)
        sem = self.depth if back else zb
        return self.copy(
            p, block, 1, self.ab[p], self.z_send.at[p, sem], self.z_recv.at[p, zb], self.me + 4 * way
        )

    def zc_copy(self, p, zb, way, back=False):
        sem = self.depth if back else zb
        return self.copy(
            p, zb * 4, 4, self.c[p], self.zc_send.at[p, sem], self.zc_recv.at[p, zb], self.me + 4 * way
        )

    def xa(self, p, zb, xb):
        block = self.block(zb, self.y, xb)
        return self.copy(
            p, block, 1, self.a[p], self.xa_send.at[p, zb], self.xa_recv.at[p, zb], self.x_peer
        )

    def yb(self, p, zb, yb):
        block = self.block(zb, yb, self.x)
        return self.copy(
            p, block, 1, self.b[p], self.yb_send.at[p, zb], self.yb_recv.at[p, zb], self.y_peer
        )

    def ya(self, p, zb, yb, xb):
        block = self.block(zb, yb, xb)
        return self.copy(
            p, block, 1, self.a[p], self.ya_send.at[p, zb, xb], self.ya_recv.at[p, zb, xb], self.y_peer
        )

    def xb(self, p, zb, yb, xb):
        block = self.block(zb, yb, xb)
        return self.copy(
            p, block, 1, self.b[p], self.xb_send.at[p, zb, yb], self.xb_recv.at[p, zb, yb], self.x_peer
        )

    def xc(self, p, xb):
        block = self.block(self.z, self.y, xb)
        return self.copy(
            p, block, 1, self.c[p], self.c_send.at[p, 0], self.c_recv.at[p, 0], self.x_peer
        )

    def yc(self, p, yb):
        block = self.block(self.z, yb, 0)
        return self.copy(
            p, block, 2, self.c[p], self.c_send.at[p, 1], self.c_recv.at[p, 1], self.y_peer
        )

    def both_ways(self, copy, act):
        @pl.when(self.z < self.depth - 1)
        def _():
            act(copy(self.z, 1))

        @pl.when(self.z > 0)
        def _():
            act(copy(self.z, -1, True))

    def spread(self, p, zb):
        self.xa(p, zb, self.x).start()
        self.yb(p, zb, self.y).start()
        self.ya(p, zb, self.y, self.x).start()
        self.xb(p, zb, self.y, self.x).start()

    def turn(self, p, zb):
        self.xa(p, zb, 1 - self.x).wait_recv()
        self.ya(p, zb, self.y, 1 - self.x).start()
        self.forward(p, self.block(zb, self.y, 1 - self.x), 1, self.a[p])
        self.yb(p, zb, 1 - self.y).wait_recv()
        self.xb(p, zb, 1 - self.y, self.x).start()
        self.forward(p, self.block(zb, 1 - self.y, self.x), 1, self.b[p])

    def at_step(self, step, act):
        for zb, valid, way in self.slots[2 * step : 2 * step + 2]:
            on = (self.z + way >= 0) & (self.z + way < self.depth)
            pl.when(valid)(functools.partial(act, zb, way, on))

    def arrive(self, p, step):
        def act(zb, way, on):
            self.z_copy(p, zb, way).wait_recv()
            pl.when(on)(lambda: self.z_copy(p, zb, way).start())
            self.spread(p, zb)
            self.forward(p, self.block(zb, self.y, self.x), 1, self.ab[p])

        self.at_step(step, act)

    def arrive_c(self, p, step):
        def act(zb, way, on):
            self.zc_copy(p, zb, way).wait_recv()
            pl.when(on)(lambda: self.zc_copy(p, zb, way).start())
            self.forward(p, zb * 4, 4, self.c[p])

        self.at_step(step, act)

    def stage(self, p, s):
        depth = self.depth
        if s == 0:
            self.both_ways(lambda *way: self.z_copy(p, *way), lambda copy: copy.start())
            self.xc(p, self.x).start()
            self.spread(p, self.z)
            self.forward(p, self.me, 1, self.all[p])
            return
        if s == 1:
            self.xc(p, 1 - self.x).wait_recv()
            self.yc(p, self.y).start()
            self.forward(p, self.block(self.z, self.y, 1 - self.x), 1, self.c[p])
        if s == 2:
            self.yc(p, 1 - self.y).wait_recv()
            self.both_ways(lambda *way: self.zc_copy(p, *way), lambda copy: copy.start())
            self.forward(p, self.block(self.z, 1 - self.y, 0), 2, self.c[p])
        if 1 <= s < depth:
            self.arrive(p, s - 1)
        if 3 <= s < depth + 2:
            self.arrive_c(p, s - 3)
        if s == 2:
            self.turn(p, self.z)
        if 3 <= s < depth + 2:
            self.at_step(s - 3, lambda zb, way, on: self.turn(p, zb))
        if s == depth + 2:
            for zb in range(depth):
                for other in range(2):
                    self.ya(p, zb, 1 - self.y, other).wait_recv()
                    self.forward(p, self.block(zb, 1 - self.y, other), 1, self.a[p])
                    self.xb(p, zb, other, 1 - self.x).wait_recv()
                    self.forward(p, self.block(zb, other, 1 - self.x), 1, self.b[p])

    def finish(self, p):
        def sent(copy):
            copy.wait_send()

        if p:
            self.far_copy(p).wait_send()
        self.both_ways(lambda *way: self.z_copy(p, *way), sent)
        self.both_ways(lambda *way: self.zc_copy(p, *way), sent)
        for zb in range(self.depth):
            self.xa(p, zb, self.x).wait_send()
            self.yb(p, zb, self.y).wait_send()
            for other in range(2):
                self.ya(p, zb, self.y, other).wait_send()
                self.xb(p, zb, other, self.x).wait_send()
        self.xc(p, self.x).wait_send()
        self.yc(p, self.y).wait_send()

        def passed(zb, way, on):
            pl.when(on)(lambda: sent(self.z_copy(p, zb, way)))
            pl.when(on)(lambda: sent(self.zc_copy(p, zb, way)))

        for step in range(self.depth - 1):
            self.at_step(step, passed)


def looped(count, body, between):
    @pl.loop(0, count)
    def _(i):
        body(i)
        for step, acts in between.items():

            @pl.when(i == step)
            def _():
                for act in acts:
                    act()


GATHER_AT = {
    "hidden": {0: [(2, 0), (1, 0)], 1: [(0, 1), (0, 2), (0, 3)], 3: [(0, 4)], 4: [(0, 5), (1, 1)]},
    "upstream": {-1: [(2, 1)], 1: [(3, 0)]},
    "project": {-1: [(4, 0), (0, 6)], 1: [(1, 2)], 5: [(2, 2)]},
    "long": {2: [(3, 1), (1, 3)], 7: [(2, 3)], 9: [(1, 4)], 14: [(2, 4)]},
    "short": {2: [(1, 5)], 3: [(3, 2)], 5: [(4, 1)]},
    "norm": {-1: [(1, 6)], 1: [(2, 5)], 3: [(3, 3)]},
    "feed": {-1: [(4, 2), (2, 6)], 0: [(3, 4)], 1: [(4, 3)], 2: [(3, 5)]},
    "last": {-1: [(3, 6), (4, 4)], 0: [(4, 5)]},
    "tail": {-1: [(4, 6)]},
}


def piece_table(width, inner):
    third = width // 8
    return (
        (0, 0, 3 * inner, third),
        (0, 3 * inner, inner, third),
        (1, 0, width, 2 * third),
        (2, 0, width // 2, third),
        (2, width // 2, width // 2, third),
    )


def chunk_columns(j, per_piece, half):
    array, at = 1 + j // per_piece, j % per_piece
    pair = per_piece // 2
    quarter = (at // pair) * per_piece * half + (at % pair) * half
    if isinstance(j, int):
        split = array > 1
        return array, quarter if split else at * half, (
            quarter + pair * half if split else (per_piece + at) * half
        )
    split = array > 1
    first = jnp.where(split, quarter, at * half)
    return array, first, first + jnp.where(split, pair, per_piece) * half


def front_kernel(
    depth, lengths_ref, dealing_ref, project_in, merge_in, expand_in, reduce_in, vectors_in, hidden_bias_in,
    tokens_ref, cotangent_ref,
    whole_out, far_ref, qkv_out, turned_out, upstream_out, context_out, total_out,
    acc_out, normal_out, inverse_out, low_turned_out, active_out, slope_out, far_context_out,
    project_ref, merge_ref, expand_ref, reduce_ref, vectors_ref, hidden_bias_ref,
    whole, score_bias, token, upper, hidden, turned, upstream, qkv, context, total,
    acc, normal, inverse, low, low_turned, active, slope, far_context, merge_far, expand_buf, reduce_buf,
    local_sem, core_sem, out_sem, load_sem, chunk_sem, weight_sem, *sems,
):
    arrays = whole.shape[0]
    half_rows, width = tokens_ref.shape
    rows = 2 * half_rows
    pairs = qkv.shape[0]
    inner = pairs * PAIR
    both = expand_buf.shape[2]
    half = both // 2
    hidden_half = expand_ref.shape[1]
    chunks = hidden_half // half
    per_piece = chunks // (arrays - 1)
    member = lax.axis_index("tensor")
    table = piece_table(whole.shape[2], inner)
    pieces = len(table)
    lines = Gather(depth, 4 * depth, whole, far_ref, table, sems)
    me = lines.me
    tall, short = 2 * TILE, TILE // 2

    weights = [
        pltpu.make_async_copy(source, target, weight_sem.at[i])
        for i, (source, target) in enumerate(
            (
                (project_in, project_ref),
                (merge_in, merge_ref),
                (expand_in, expand_ref),
                (reduce_in, reduce_ref),
                (vectors_in, vectors_ref),
                (hidden_bias_in, hidden_bias_ref),
            )
        )
    ]
    for copy in weights:
        copy.start()
    own = [
        pltpu.make_async_copy(tokens_ref, token.at[member], local_sem.at[0]),
        pltpu.make_async_copy(cotangent_ref, upper.at[member], local_sem.at[1]),
    ]
    for copy in own:
        copy.start()
    for copy in weights:
        copy.wait()
    mine = pl.ds(pl.multiple_of(me * lines.rows, lines.rows), lines.rows)
    for pair in range(pairs):
        for c in range(3):
            first = (3 * pair + c) * PAIR
            whole[0, mine, first : first + PAIR] = project_ref[
                c, :, pair * PAIR : (pair + 1) * PAIR
            ].astype(LOW)
    whole[0, mine, 3 * inner :] = merge_ref[...].astype(LOW)
    for j in range(chunks):
        array, first, second = chunk_columns(j, per_piece, half)
        columns = slice(j * half, (j + 1) * half)
        whole[array, mine, first : first + half] = expand_ref[:, columns].astype(LOW)
        whole[array, mine, second : second + half] = reduce_ref[:, columns].astype(LOW)
    greet_line(me, lines.z, lines.y, lines.x, depth, [{"tensor": 1 - member}])
    crossing = [
        other_core(tokens_ref, token.at[member], core_sem.at[0, 0], core_sem.at[0, 1]),
        other_core(cotangent_ref, upper.at[member], core_sem.at[1, 0], core_sem.at[1, 1]),
    ]
    lines.stage(0, 0)
    for copy in crossing:
        copy.start()
    group = Group(lengths_ref, dealing_ref)
    score_bias[...] = group.score_bias(rows - LONGEST)
    for copy in own:
        copy.wait()

    leaving = []

    def leave(source, target):
        copy = pltpu.make_async_copy(source, target, out_sem.at[len(leaving)])
        copy.start()
        leaving.append(copy)

    def before(name):
        for stage in GATHER_AT.get(name, {}).get(-1, ()):
            lines.stage(*stage)

    def phase(name, count, body):
        between = {
            step: [functools.partial(lines.stage, *stage) for stage in stages]
            for step, stages in GATHER_AT.get(name, {}).items()
            if step >= 0
        }
        looped(count, body, between)

    def places_of(first):
        return first + lax.broadcasted_iota(jnp.int32, (TILE, 1), 0)

    def picked(index, source):
        return picked_rows(index, source.at[0]) + picked_rows(index - half_rows, source.at[1])

    def tile(step, size=TILE):
        return pl.ds(pl.multiple_of(step * size, size), size)

    def hidden_tile(step):
        index = group.moved(places_of(step * TILE), group.first, group.own)
        rows_here = picked(index, token)
        hidden[tile(step), :] = rows_here.astype(LOW)
        turned[:, tile(step)] = rows_here.T.astype(LOW)

    def upstream_tile(step):
        places = places_of(member * half_rows + step * TILE)
        index = group.moved(places, group.first, group.dealt)
        upstream[tile(step), :] = picked(index, upper).astype(LOW)

    crossing[0].wait()
    before("hidden")
    phase("hidden", rows // TILE, hidden_tile)
    leave(turned, turned_out)
    crossing[1].wait()
    before("upstream")
    phase("upstream", half_rows // TILE, upstream_tile)
    leave(upstream, upstream_out)

    def project_tile(i):
        pair, step = i // (rows // tall), lax.rem(i, rows // tall)
        at = tile(step, tall)
        columns = pl.ds(pl.multiple_of(pair * 3 * PAIR, PAIR), 3 * PAIR)
        bias_columns = pl.ds(pl.multiple_of(member * inner + pair * PAIR, PAIR), PAIR)
        bias = jnp.concatenate(
            [
                vectors_ref[0:1, bias_columns],
                jnp.zeros((1, PAIR), WIDE),
                vectors_ref[1:2, bias_columns],
            ],
            axis=1,
        )
        qkv[pair, at, :] = (dot_nn(hidden[at, :], whole[0, :, columns]) + bias).astype(LOW)

    before("project")
    phase("project", pairs * rows // tall, project_tile)
    leave(qkv, qkv_out)

    def attend_step(begin, size):
        def step_of(i):
            pair, step = i // (size // TILE), lax.rem(i, size // TILE)
            columns = pl.ds(pl.multiple_of(pair * PAIR, PAIR), PAIR)
            attend_tile(qkv, pair, score_bias, begin, size, step, context, columns, total)

        return step_of

    before("long")
    phase("long", pairs * LONGEST // TILE, attend_step(0, LONGEST))
    before("short")
    phase("short", pairs * (rows - LONGEST) // TILE, attend_step(LONGEST, rows - LONGEST))
    leave(context, context_out)
    leave(total, total_out)

    own_first = member * half_rows
    other_rows = pl.ds(pl.multiple_of((1 - member) * half_rows, half_rows), half_rows)
    crossing = other_core(context.at[other_rows], far_context, core_sem.at[2, 0], core_sem.at[2, 1])
    crossing.start()
    before("norm")
    lines.far_copy(1).wait_recv()
    merge_columns = pl.ds(whole.shape[2] - inner, inner)
    merge_copy = pltpu.make_async_copy(
        far_ref.at[0, :, merge_columns], merge_far, local_sem.at[2]
    )
    merge_copy.start()
    merge_copy.wait()
    crossing.wait()
    leave(far_context, far_context_out)

    def norm_tile(step):
        at = tile(step, short)
        own_at = pl.ds(pl.multiple_of(own_first + step * short, short), short)
        branch = dot_nt(context[own_at, :], whole[0, :, merge_columns])
        branch = branch + dot_nt(far_context[at, :], merge_far[...])
        unit, scale = norm(hidden[own_at, :].astype(WIDE) + branch + vectors_ref[2:3, :])
        normed = unit * vectors_ref[3:4, :] + vectors_ref[4:5, :]
        normal[at, :] = unit
        inverse[at, :] = jnp.broadcast_to(scale, (short, 128))
        low[at, :] = normed.astype(LOW)
        low_turned[:, at] = normed.T.astype(LOW)
        acc[at, :] = normed + vectors_ref[5:6, :]

    phase("norm", half_rows // short, norm_tile)
    leave(whole.at[0], whole_out.at[0])
    leave(normal, normal_out)
    leave(inverse, inverse_out)
    leave(low_turned, low_turned_out)

    def loads(j):
        slot = lax.rem(j, 2)
        array, *firsts = chunk_columns(j, per_piece, half)
        copies = []
        for kind, buf in enumerate((expand_buf, reduce_buf)):
            first = pl.multiple_of(firsts[kind], half)
            for side, source in enumerate((far_ref, whole)):
                copies.append(
                    pltpu.make_async_copy(
                        source.at[array, :, pl.ds(first, half)],
                        buf.at[slot, :, pl.ds(side * half, half)],
                        load_sem.at[slot, kind, side],
                    )
                )
        return copies

    def results(j):
        slot = lax.rem(j, 2)
        return [
            pltpu.make_async_copy(active.at[slot], active_out.at[j], chunk_sem.at[slot, 0]),
            pltpu.make_async_copy(slope.at[slot], slope_out.at[j], chunk_sem.at[slot, 1]),
        ]

    def chunk_of(piece, first_chunk, count):
        def chunk(i):
            j = first_chunk + i
            slot = lax.rem(j, 2)

            @pl.when(i == 0)
            def _():
                lines.far_copy(piece).wait_recv()
                for copy in loads(j):
                    copy.start()

            for copy in loads(j):
                copy.wait()

            @pl.when(i + 1 < count)
            def _():
                for copy in loads(j + 1):
                    copy.start()

            @pl.when(j >= 2)
            def _():
                for copy in results(j - 2):
                    copy.wait()

            biases = []
            for which in (1 - member, member):
                first = pl.multiple_of(which * hidden_half + j * half, half)
                biases.append(hidden_bias_ref[:, pl.ds(first, half)])
            bias = jnp.concatenate(biases, axis=1)
            tiles = [slice(step * TILE, (step + 1) * TILE) for step in range(half_rows // TILE)]
            parts = [dot_nn(low[at, :], expand_buf[slot]) for at in tiles]
            for at, part in zip(tiles, parts, strict=True):
                value = part + bias
                below, bell = normal_cells(value)
                held = (value * below).astype(LOW)
                active[slot, at, :] = held
                slope[slot, at, :] = (below + value * bell * 0.3989422804014327).astype(LOW)
                acc[at, :] += dot_nt(held, reduce_buf[slot])
            for copy in results(j):
                copy.start()

        return chunk

    first_chunk = 0
    for piece, name in ((2, "feed"), (3, "last"), (4, "tail")):
        count = chunks * table[piece][2] // (2 * hidden_half)
        before(name)
        phase(name, count, chunk_of(piece, first_chunk, count))
        columns = pl.ds(*lines.all[piece])
        leave(
            whole.at[lines.array[piece], :, columns],
            whole_out.at[lines.array[piece], :, columns],
        )
        first_chunk += count
    leave(acc, acc_out)
    for p in range(pieces):
        lines.finish(p)
    for j in (chunks - 2, chunks - 1):
        for copy in results(j):
            copy.wait()
    for copy in leaving:
        copy.wait()


def front(lengths, dealing, project, merge, expand, reduce, vectors, hidden_bias, tokens, cotangent, parts):
    shard_rows, hidden_half = expand.shape
    arrays, columns = 3, hidden_half
    half_rows, width = tokens.shape
    rows, pairs, depth = 2 * half_rows, project.shape[2] // PAIR, parts // 4
    inner, half = pairs * PAIR, 256
    pieces = len(piece_table(columns, inner))
    chunks, both = hidden_half // half, 2 * half
    shape, sem = jax.ShapeDtypeStruct, pltpu.SemaphoreType.DMA
    anywhere = pl.BlockSpec(memory_space=pl.ANY)
    held = [
        ((pairs, rows, 3 * PAIR), LOW),
        ((width, rows), LOW),
        ((half_rows, width), LOW),
        ((rows, inner), LOW),
        ((pairs, 8, rows), WIDE),
        ((half_rows, width), WIDE),
        ((half_rows, width), WIDE),
        ((half_rows, 128), WIDE),
        ((width, half_rows), LOW),
        ((chunks, half_rows, both), LOW),
        ((chunks, half_rows, both), LOW),
        ((half_rows, inner), LOW),
    ]
    return pl.pallas_call(
        functools.partial(front_kernel, depth),
        in_specs=[*[pl.BlockSpec(memory_space=pltpu.SMEM)] * 2, *[anywhere] * 8],
        out_specs=[anywhere] * 14,
        out_shape=[
            shape((arrays, parts * shard_rows, columns), LOW),
            shape((arrays, parts * shard_rows, columns), LOW),
            *[shape(*one) for one in held],
        ],
        scratch_shapes=[
            *[
                pltpu.VMEM(one.shape, WIDE)
                for one in (project, merge, expand, reduce, vectors, hidden_bias)
            ],
            pltpu.VMEM((arrays, parts * shard_rows, columns), LOW),
            pltpu.VMEM((rows - LONGEST, rows - LONGEST), WIDE),
            pltpu.VMEM((2, half_rows, width), LOW),
            pltpu.VMEM((2, half_rows, width), LOW),
            pltpu.VMEM((rows, width), LOW),
            pltpu.VMEM((width, rows), LOW),
            pltpu.VMEM((half_rows, width), LOW),
            pltpu.VMEM((pairs, rows, 3 * PAIR), LOW),
            pltpu.VMEM((rows, inner), LOW),
            pltpu.VMEM((pairs, 8, rows), WIDE),
            pltpu.VMEM((half_rows, width), WIDE),
            pltpu.VMEM((half_rows, width), WIDE),
            pltpu.VMEM((half_rows, 128), WIDE),
            pltpu.VMEM((half_rows, width), LOW),
            pltpu.VMEM((width, half_rows), LOW),
            pltpu.VMEM((2, half_rows, both), LOW),
            pltpu.VMEM((2, half_rows, both), LOW),
            pltpu.VMEM((half_rows, inner), LOW),
            pltpu.VMEM((width, inner), LOW),
            pltpu.VMEM((2, width, both), LOW),
            pltpu.VMEM((2, width, both), LOW),
            sem((3,)),
            sem((3, 2)),
            sem((16,)),
            sem((2, 2, 2)),
            sem((2, 2)),
            sem((6,)),
            *Gather.semaphores(depth, pieces),
        ],
        compiler_params=pltpu.CompilerParams(
            collective_id=0, has_side_effects=True, vmem_limit_bytes=63 * MIB
        ),
    )(lengths, dealing, project, merge, expand, reduce, vectors, hidden_bias, tokens, cotangent)


def normal_cells(value):
    bell = jnp.exp2(value * value * (-0.5 * 1.4426950408889634))
    below = 1.0 + 0.39 * 0.7071067811865476 * jnp.abs(value)
    t = pl.reciprocal(below, approx=True)
    t = t * (2.0 - below * t)
    t = t * (2.0 - below * t)
    tail = 0.5 * -0.2275377237624147
    for factor in (
        0.8866668177122106,
        -0.6354042576077721,
        0.649562611731642,
        0.0913871257655044,
        0.23532542445435511,
    ):
        tail = tail * t + 0.5 * factor
    tail = tail * t * bell
    return jnp.where(value < 0.0, tail, 1.0 - tail), bell


def norm(values):
    center = values - jnp.mean(values, axis=1, keepdims=True)
    spread = jnp.mean(center * center, axis=1, keepdims=True)
    scale = lax.rsqrt(spread + norm_epsilon)
    return center * scale, scale


def norm_back(scaled, unit, scale):
    return scale * (
        scaled
        - jnp.mean(scaled, axis=1, keepdims=True)
        - unit * jnp.mean(scaled * unit, axis=1, keepdims=True)
    )


def feed_kernel(
    context_ref, merge_ref, merge_far_ref, whole_ref, far_ref, hidden_ref, upstream_ref, vectors_ref, bias_ref,
    encoded_ref, branch_ref, grad_ref, merge_grad_ref, expand_grad_ref, reduce_grad_ref, sums_ref, hidden_sums_ref,
    own_ctx, far_ctx, acc, normal, inverse, low, turned, late, late_turned, active, slope, inner_grad,
    expand_buf, reduce_buf, arrived, leaving, kept, done, grad_own, grad_far, merge_send, merge_recv,
    ctx_sem, load_sem, send_sem, recv_sem, out_sem, last_sem,
):
    rows = hidden_ref.shape[0]
    chunks, _, both = bias_ref.shape
    half = both // 2
    per_piece = whole_ref.shape[2] // (2 * half)
    member = lax.axis_index("tensor")
    peer = {"tensor": 1 - member}
    tall, short = 256, 128
    width = hidden_ref.shape[1]

    def across(source, target, send, receive):
        return pltpu.make_async_remote_copy(
            src_ref=source,
            dst_ref=target,
            send_sem=send,
            recv_sem=receive,
            device_id=peer,
            device_id_type=MESH,
        )

    def rows_of(which):
        return pl.ds(pl.multiple_of(which * rows, rows), rows)

    def tile(step, size):
        return pl.ds(pl.multiple_of(step * size, size), size)

    def loads(j, slot):
        piece, at = 1 + j // per_piece, lax.rem(j, per_piece) * half
        copies = []
        for kind, buf in enumerate((expand_buf, reduce_buf)):
            first = pl.multiple_of(at + kind * per_piece * half, half)
            for side, source in enumerate((far_ref, whole_ref)):
                copies.append(
                    pltpu.make_async_copy(
                        source.at[piece, :, pl.ds(first, half)],
                        buf.at[slot, :, pl.ds(side * half, half)],
                        load_sem.at[slot, kind, side],
                    )
                )
        return copies

    for copy in loads(0, 0):
        copy.start()
    barrier = pltpu.get_barrier_semaphore()
    pl.semaphore_signal(barrier, inc=1, device_id=peer, device_id_type=MESH)
    pl.semaphore_wait(barrier, 1)
    out_ctx = across(context_ref.at[rows_of(1 - member)], far_ctx, ctx_sem.at[0], ctx_sem.at[1])
    out_ctx.start()
    in_ctx = pltpu.make_async_copy(context_ref.at[rows_of(member)], own_ctx, ctx_sem.at[2])
    in_ctx.start()
    sums_ref[...] = jnp.zeros_like(sums_ref)
    in_ctx.wait()
    out_ctx.wait()

    def add_sum(row, values):
        sums_ref[row : row + 1, :] += jnp.sum(values, axis=0, keepdims=True)

    @pl.loop(0, rows // short)
    def _(step):
        at = tile(step, short)
        branch = dot_nt(own_ctx[at, :], merge_ref[...]) + dot_nt(far_ctx[at, :], merge_far_ref[...])
        unit, scale = norm(hidden_ref[at, :].astype(WIDE) + branch + vectors_ref[2:3, :])
        normed = unit * vectors_ref[3:4, :] + vectors_ref[4:5, :]
        normal[at, :] = unit
        inverse[at, :] = jnp.broadcast_to(scale, (short, 128))
        low[at, :] = normed.astype(LOW)
        turned[:, at] = normed.T.astype(LOW)
        acc[at, :] = normed + vectors_ref[5:6, :]

    @pl.loop(0, chunks)
    def _(j):
        slot = lax.rem(j, 2)
        for copy in loads(j, slot):
            copy.wait()

        @pl.when(j + 1 < chunks)
        def _():
            for copy in loads(j + 1, 1 - slot):
                copy.start()

        for step in range(rows // tall):
            at = slice(step * tall, (step + 1) * tall)
            inner = dot_nn(low[at, :], expand_buf[slot]) + bias_ref[j]
            below, bell = normal_cells(inner)
            held = (inner * below).astype(LOW)
            active[j, at, :] = held
            slope[j, at, :] = (below + inner * bell * 0.3989422804014327).astype(LOW)
            acc[at, :] += dot_nt(held, reduce_buf[slot])

    for copy in loads(0, 0):
        copy.start()

    @pl.loop(0, rows // short)
    def _(step):
        at = tile(step, short)
        unit, scale = norm(acc[at, :])
        encoded_ref[at, :] = (unit * vectors_ref[6:7, :] + vectors_ref[7:8, :]).astype(LOW)
        upper = upstream_ref[at, :].astype(WIDE)
        add_sum(6, upper * unit)
        add_sum(7, upper)
        grad = norm_back(upper * vectors_ref[6:7, :], unit, scale)
        grad_low = grad.astype(LOW)
        add_sum(5, grad_low.astype(WIDE))
        acc[at, :] = grad
        late[at, :] = grad_low
        late_turned[:, at] = grad.T.astype(LOW)

    def send(j, kind):
        return across(
            leaving.at[lax.rem(j, 2), kind],
            arrived.at[lax.rem(j, 4), kind],
            send_sem.at[lax.rem(j, 2), kind],
            recv_sem.at[lax.rem(j, 4), kind],
        )

    def store(j, kind):
        target = (expand_grad_ref, reduce_grad_ref)[kind]
        cols = pl.ds(pl.multiple_of(j * half, half), half)
        return pltpu.make_async_copy(
            done.at[lax.rem(j, 2), kind], target.at[:, cols], out_sem.at[lax.rem(j, 2), kind]
        )

    def finish(j):
        for kind in range(2):
            send(j, kind).wait_recv()

            @pl.when(j >= 2)
            def _():
                store(j - 2, kind).wait()

            @pl.loop(0, width // tall)
            def _(step):
                at = tile(step, tall)
                done[lax.rem(j, 2), kind, at, :] = (
                    kept[lax.rem(j, 2), kind, at, :]
                    + arrived[lax.rem(j, 4), kind, at, :].astype(WIDE)
                ).astype(LOW)

            store(j, kind).start()

    @pl.loop(0, chunks)
    def _(j):
        slot = lax.rem(j, 2)
        for copy in loads(j, slot):
            copy.wait()

        @pl.when(j + 1 < chunks)
        def _():
            for copy in loads(j + 1, 1 - slot):
                copy.start()

        total = jnp.zeros((1, both), WIDE)
        for step in range(rows // tall):
            at = slice(step * tall, (step + 1) * tall)
            grad = dot_nn(late[at, :], reduce_buf[slot]) * slope[j, at, :].astype(WIDE)
            grad = grad.astype(LOW)
            inner_grad[at, :] = grad
            total = total + jnp.sum(grad.astype(WIDE), axis=0, keepdims=True)
            acc[at, :] += dot_nt(grad, expand_buf[slot])
        hidden_sums_ref[j] = total

        @pl.when(j >= 2)
        def _():
            for kind in range(2):
                send(j - 2, kind).wait_send()

        for kind, (left, right) in enumerate(((turned, inner_grad), (late_turned, active.at[j]))):
            for step in range(width // tall):
                at = slice(step * tall, (step + 1) * tall)
                part = dot_nn(left[at, :], right[...])
                leaving[slot, kind, at, :] = part[:, 0:half].astype(LOW)
                kept[slot, kind, at, :] = part[:, half:both]
            send(j, kind).start()

        @pl.when(j >= 1)
        def _():
            finish(j - 1)

    @pl.loop(0, rows // short)
    def _(step):
        at = tile(step, short)
        grad = acc[at, :]
        unit = normal[at, :]
        add_sum(3, grad * unit)
        add_sum(4, grad)
        branch_grad = norm_back(grad * vectors_ref[3:4, :], unit, inverse[at, 0:1])
        branch_low = branch_grad.astype(LOW)
        add_sum(2, branch_low.astype(WIDE))
        branch_ref[at, :] = branch_grad
        turned[:, at] = branch_grad.T.astype(LOW)
        grad_far[at, :] = dot_nn(branch_low, merge_far_ref[...]).astype(LOW)
        grad_own[at, :] = dot_nn(branch_low, merge_ref[...]).astype(LOW)

    out_grad = across(grad_far, grad_ref.at[rows_of(member)], ctx_sem.at[0], ctx_sem.at[1])
    out_grad.start()
    in_grad = pltpu.make_async_copy(grad_own, grad_ref.at[rows_of(member)], ctx_sem.at[2])
    in_grad.start()
    for step in range(width // tall):
        at = slice(step * tall, (step + 1) * tall)
        merge_send[at, :] = dot_nn(turned[at, :], far_ctx[...]).astype(LOW)
    out_merge = across(merge_send, merge_recv, last_sem.at[0], last_sem.at[1])
    out_merge.start()
    finish(chunks - 1)
    for kind in range(2):
        send(chunks - 2, kind).wait_send()
        send(chunks - 1, kind).wait_send()
        store(chunks - 2, kind).wait()
        store(chunks - 1, kind).wait()
    out_merge.wait()
    for step in range(width // tall):
        at = slice(step * tall, (step + 1) * tall)
        merge_grad_ref[at, :] = (
            dot_nn(turned[at, :], own_ctx[...]) + merge_recv[at, :].astype(WIDE)
        ).astype(LOW)
    out_grad.wait()
    in_grad.wait()


def feed_block(context, whole, far, hidden_own, upstream, vectors, bias_own, bias_far):
    total_rows, inner = context.shape
    rows, width = hidden_own.shape
    hidden = bias_own.shape[0]
    merge, merge_far = whole[0, :, -inner:], far[0, :, -inner:]
    half = 256
    chunks = hidden // half
    both = 2 * half
    bias = jnp.concatenate(
        [bias_far.reshape(chunks, 1, half), bias_own.reshape(chunks, 1, half)], axis=2
    )
    vmem, anywhere = pl.BlockSpec(memory_space=pltpu.VMEM), pl.BlockSpec(memory_space=pl.ANY)
    sem = pltpu.SemaphoreType.DMA
    shape = jax.ShapeDtypeStruct
    *results, hidden_sums = pl.pallas_call(
        feed_kernel,
        in_specs=[anywhere, vmem, vmem, *[anywhere] * 2, *[vmem] * 4],
        out_specs=[vmem, vmem, anywhere, vmem, anywhere, anywhere, vmem, vmem],
        out_shape=[
            shape((rows, width), LOW),
            shape((rows, width), WIDE),
            shape((total_rows, inner), LOW),
            shape((width, inner), LOW),
            shape((width, hidden), LOW),
            shape((width, hidden), LOW),
            shape((8, width), WIDE),
            shape((chunks, 1, both), WIDE),
        ],
        scratch_shapes=[
            pltpu.VMEM((rows, inner), LOW),
            pltpu.VMEM((rows, inner), LOW),
            pltpu.VMEM((rows, width), WIDE),
            pltpu.VMEM((rows, width), WIDE),
            pltpu.VMEM((rows, 128), WIDE),
            pltpu.VMEM((rows, width), LOW),
            pltpu.VMEM((width, rows), LOW),
            pltpu.VMEM((rows, width), LOW),
            pltpu.VMEM((width, rows), LOW),
            pltpu.VMEM((chunks, rows, both), LOW),
            pltpu.VMEM((chunks, rows, both), LOW),
            pltpu.VMEM((rows, both), LOW),
            pltpu.VMEM((2, width, both), LOW),
            pltpu.VMEM((2, width, both), LOW),
            pltpu.VMEM((4, 2, width, half), LOW),
            pltpu.VMEM((2, 2, width, half), LOW),
            pltpu.VMEM((2, 2, width, half), WIDE),
            pltpu.VMEM((2, 2, width, half), LOW),
            pltpu.VMEM((rows, inner), LOW),
            pltpu.VMEM((rows, inner), LOW),
            pltpu.VMEM((width, inner), LOW),
            pltpu.VMEM((width, inner), LOW),
            sem((3,)),
            sem((2, 2, 2)),
            sem((2, 2)),
            sem((4, 2)),
            sem((2, 2)),
            sem((2,)),
        ],
        compiler_params=pltpu.CompilerParams(
            collective_id=2, has_side_effects=True, vmem_limit_bytes=60 * MIB
        ),
        cost_estimate=pl.CostEstimate(
            flops=12 * rows * width * 2 * hidden, bytes_accessed=8 * width * hidden * 4, transcendentals=0
        ),
    )(context, merge, merge_far, whole, far, hidden_own, upstream, vectors, bias)
    hidden_far = hidden_sums[:, 0, :half].reshape(-1)
    hidden_near = hidden_sums[:, 0, half:].reshape(-1)
    return (*results, hidden_near, hidden_far)


class Scatter:
    buffers = 8

    def __init__(self, depth, grads, shards, targets, buffers, sems):
        self.depth, self.grads, self.shards, self.targets = depth, grads, shards, targets
        self.held = [buffers[8 * p : 8 * p + 8] for p in range(len(grads))]
        self.me, self.z, self.y, self.x = place()
        self.x_peer = self.z * 4 + self.y * 2 + 1 - self.x
        self.y_peer = self.z * 4 + (1 - self.y) * 2 + self.x
        self.rows = grads[0].shape[0] // (4 * depth)
        (
            self.a1_send, self.a1_recv, self.a2_send, self.a2_recv, self.b2_send, self.b2_recv, self.b1_send, self.b1_recv,
            self.z_send, self.z_recv, self.zc_send, self.zc_recv, self.c_send, self.c_recv, self.out_sem,
        ) = sems

    @staticmethod
    def scratch(depth, rows, classes):
        found = []
        for a, b, c in classes:
            found += [
                pltpu.VMEM((depth, 2 * rows, a), LOW),
                pltpu.VMEM((depth, 2, rows, b), LOW),
                pltpu.VMEM((depth, rows, a), LOW),
                pltpu.VMEM((depth, rows, b), LOW),
                pltpu.VMEM((depth + 1, rows, a + b), LOW),
                pltpu.VMEM((depth + 1, 4 * rows, c), LOW),
                pltpu.VMEM((2 * rows, c), LOW),
                pltpu.VMEM((rows, c), LOW),
            ]
        return found

    @staticmethod
    def semaphores(depth, pieces):
        sem = pltpu.SemaphoreType.DMA
        return [
            *[sem((pieces, depth))] * 6,
            *[sem((pieces, depth, 2))] * 2,
            *[sem((pieces, depth)), sem((pieces, depth + 1))] * 2,
            sem((pieces, 2)),
            sem((pieces, 2)),
            sem((pieces,)),
        ]

    def done(self, p):
        return pltpu.make_async_copy(self.shards[p], self.targets[p], self.out_sem.at[p])

    def columns(self, p):
        a, b, c = (self.held[p][i].shape[-1] for i in (0, 1, 5))
        return pl.ds(0, a), pl.ds(a, b), pl.ds(a + b, c)

    def block(self, zb, yb, xb):
        return zb * 4 + yb * 2 + xb

    def span(self, block, count=1):
        return pl.ds(pl.multiple_of(block * self.rows, self.rows), count * self.rows)

    def add(self, put, count, *terms):
        chunk = min(count, 64)

        @pl.loop(0, count // chunk)
        def _(step):
            at = pl.multiple_of(step * chunk, chunk)
            parts = [term(at, chunk) for term in terms]
            if len(parts) > 2 or put.wide:
                parts = [part.astype(WIDE) for part in parts]
            total = parts[0]
            for part in parts[1:]:
                total = total + part
            put(at, chunk, total)

    def a1(self, p, zb):
        return remote(
            self.grads[p].at[self.span(self.block(zb, 1 - self.y, 0), 2), self.columns(p)[0]],
            self.held[p][0].at[zb],
            self.a1_send.at[p, zb],
            self.a1_recv.at[p, zb],
            self.y_peer,
        )

    def b1(self, p, zb, yb):
        return remote(
            self.grads[p].at[self.span(self.block(zb, yb, 1 - self.x)), self.columns(p)[1]],
            self.held[p][1].at[zb, yb],
            self.b1_send.at[p, zb, yb],
            self.b1_recv.at[p, zb, yb],
            self.x_peer,
        )

    def a2(self, p, zb):
        return remote(
            self.held[p][0].at[zb, self.span(1 - self.x)],
            self.held[p][2].at[zb],
            self.a2_send.at[p, zb],
            self.a2_recv.at[p, zb],
            self.x_peer,
        )

    def b2(self, p, zb):
        return remote(
            self.held[p][1].at[zb, 1 - self.y],
            self.held[p][3].at[zb],
            self.b2_send.at[p, zb],
            self.b2_recv.at[p, zb],
            self.y_peer,
        )

    def slot(self, zb, way):
        return zb if way > 0 else zb + (self.depth - zb) * jnp.where(zb == self.z - 1, 1, 0)

    def z_copy(self, p, zb, way):
        slot = self.slot(zb, way)
        return remote(
            self.held[p][4].at[zb],
            self.held[p][4].at[slot],
            self.z_send.at[p, zb],
            self.z_recv.at[p, slot],
            self.me + 4 * way,
        )

    def zc_copy(self, p, zb, way, first):
        slot = self.slot(zb, way)
        source = self.held[p][5].at[zb]
        if first:
            source = self.grads[p].at[self.span(zb * 4, 4), self.columns(p)[2]]
        return remote(
            source,
            self.held[p][5].at[slot],
            self.zc_send.at[p, zb],
            self.zc_recv.at[p, slot],
            self.me + 4 * way,
        )

    def arrived(self, ref, sem, slot):
        part = ref.at[slot]
        remote(part, part, sem, sem, self.me).wait_recv()

    def cy(self, p):
        return remote(
            self.held[p][5].at[self.z, self.span(2 * (1 - self.y), 2)],
            self.held[p][6],
            self.c_send.at[p, 0],
            self.c_recv.at[p, 0],
            self.y_peer,
        )

    def cx(self, p):
        return remote(
            self.held[p][5].at[self.z, self.span(2 * self.y + 1 - self.x)],
            self.held[p][7],
            self.c_send.at[p, 1],
            self.c_recv.at[p, 1],
            self.x_peer,
        )

    def grad(self, p, block, columns):
        def term(at, count):
            first = pl.multiple_of(block * self.rows + at, 16)
            return self.grads[p][pl.ds(first, count), columns]

        return term

    def part(self, ref, lead, block, columns=None):
        columns = slice(None) if columns is None else columns

        def term(at, count):
            first = pl.multiple_of(block * self.rows + at, 16)
            return ref[(*lead, pl.ds(first, count), columns)]

        return term

    def put(self, ref, lead, block, columns=None):
        columns = slice(None) if columns is None else columns

        def act(at, count, total):
            first = pl.multiple_of(block * self.rows + at, 16)
            ref[(*lead, pl.ds(first, count), columns)] = total.astype(ref.dtype)

        act.wide = ref.dtype == WIDE
        return act

    def open(self, p, zb):
        self.a1(p, zb).start()
        self.b1(p, zb, 0).start()
        self.b1(p, zb, 1).start()

    def first(self, p, zb):
        z, y, x = self.z, self.y, self.x
        a, b, _ = self.columns(p)
        r1a, r1b = self.held[p][0], self.held[p][1]
        self.a1(p, zb).wait_recv()
        self.add(
            self.put(r1a, (zb,), 1 - x),
            self.rows,
            self.part(r1a, (zb,), 1 - x),
            self.grad(p, self.block(zb, y, 1 - x), a),
        )
        self.a2(p, zb).start()
        self.b1(p, zb, 0).wait_recv()
        self.b1(p, zb, 1).wait_recv()
        self.add(
            self.put(r1b, (zb, 1 - y), 0),
            self.rows,
            self.part(r1b, (zb, 1 - y), 0),
            self.grad(p, self.block(zb, 1 - y, x), b),
        )
        self.b2(p, zb).start()

    def terms(self, p, zb):
        z, y, x = self.z, self.y, self.x
        a, b, _ = self.columns(p)
        r1a, r1b, r2a, r2b = self.held[p][:4]
        own = self.block(zb, y, x)
        return (
            [self.grad(p, own, a), self.part(r1a, (zb,), x), self.part(r2a, (zb,), 0)],
            [self.grad(p, own, b), self.part(r1b, (zb, y), 0), self.part(r2b, (zb,), 0)],
        )

    def pass_on(self, p, zb, way):
        a, b, _ = self.columns(p)
        rz = self.held[p][4]
        self.a2(p, zb).wait_recv()
        self.b2(p, zb).wait_recv()
        from_line = (self.z - way >= 0) & (self.z - way < self.depth)

        @pl.when(from_line)
        def _():
            self.arrived(rz, self.z_recv.at[p, zb], zb)
            for terms, columns in zip(self.terms(p, zb), (a, b), strict=True):
                self.add(
                    self.put(rz, (zb,), 0, columns),
                    self.rows,
                    *terms,
                    self.part(rz, (zb,), 0, columns),
                )

        @pl.when(jnp.logical_not(from_line))
        def _():
            for terms, columns in zip(self.terms(p, zb), (a, b), strict=True):
                self.add(self.put(rz, (zb,), 0, columns), self.rows, *terms)

        self.z_copy(p, zb, way).start()

    def pass_c(self, p, zb, way):
        c = self.columns(p)[2]
        rc = self.held[p][5]
        from_line = (self.z - way >= 0) & (self.z - way < self.depth)

        @pl.when(from_line)
        def _():
            self.arrived(rc, self.zc_recv.at[p, zb], zb)
            self.add(
                self.put(rc, (zb,), 0),
                4 * self.rows,
                self.part(rc, (zb,), 0),
                self.grad(p, zb * 4, c),
            )
            self.zc_copy(p, zb, way, False).start()

        @pl.when(jnp.logical_not(from_line))
        def _():
            self.zc_copy(p, zb, way, True).start()

    def own_c(self, p):
        z, depth = self.z, self.depth
        c = self.columns(p)[2]
        rc = self.held[p][5]
        grad = self.grad(p, z * 4, c)
        lower, upper = self.part(rc, (z,), 0), self.part(rc, (depth,), 0)
        put = self.put(rc, (z,), 0)

        @pl.when(z > 0)
        def _():
            self.arrived(rc, self.zc_recv.at[p, z], z)

        @pl.when(z < depth - 1)
        def _():
            self.arrived(rc, self.zc_recv.at[p, depth], depth)

        @pl.when((z > 0) & (z < depth - 1))
        def _():
            self.add(put, 4 * self.rows, grad, lower, upper)

        @pl.when(z == 0)
        def _():
            self.add(put, 4 * self.rows, grad, upper)

        @pl.when(z == depth - 1)
        def _():
            self.add(put, 4 * self.rows, grad, lower)

        self.cy(p).start()

    def turn_c(self, p):
        rc, rcy = self.held[p][5], self.held[p][6]
        self.cy(p).wait_recv()
        self.add(
            self.put(rc, (self.z,), 2 * self.y),
            2 * self.rows,
            self.part(rc, (self.z,), 2 * self.y),
            self.part(rcy, (), 0),
        )
        self.cx(p).start()

    def close(self, p):
        z, depth = self.z, self.depth
        a, b, c = self.columns(p)
        rz, rc, rcx = self.held[p][4], self.held[p][5], self.held[p][7]
        self.a2(p, z).wait_recv()
        self.b2(p, z).wait_recv()

        @pl.when(z > 0)
        def _():
            self.arrived(rz, self.z_recv.at[p, z], z)

        @pl.when(z < depth - 1)
        def _():
            self.arrived(rz, self.z_recv.at[p, depth], depth)

        def total(*slots):
            for terms, columns in zip(self.terms(p, z), (a, b), strict=True):
                lines = [self.part(rz, (slot,), 0, columns) for slot in slots]
                self.add(self.put(self.shards[p], (), 0, columns), self.rows, *terms, *lines)

        pl.when((z > 0) & (z < depth - 1))(lambda: total(z, depth))
        pl.when(z == 0)(lambda: total(depth))
        pl.when(z == depth - 1)(lambda: total(z))
        self.cx(p).wait_recv()
        self.add(
            self.put(self.shards[p], (), 0, c),
            self.rows,
            self.part(rc, (z,), 2 * self.y + self.x),
            self.part(rcx, (), 0),
        )
        self.done(p).start()

    def at_step(self, step, act):
        z, depth = self.z, self.depth
        if step < 0:
            act(z, 0)
            return
        for zb, valid, way in (
            (z + 1 + step, z + 1 + step < depth, 1),
            (z - 1 - step, z - 1 - step >= 0, -1),
        ):
            pl.when(valid)(functools.partial(act, zb, way))

    def stage(self, p, s):
        last = self.depth - 2

        def opened(step):
            self.at_step(step, lambda zb, way: self.open(p, zb))

        def added(step):
            self.at_step(step, lambda zb, way: self.first(p, zb))

        def passed(step):
            self.at_step(step, lambda zb, way: self.pass_on(p, zb, way))

        def passed_c(step):
            self.at_step(step, lambda zb, way: self.pass_c(p, zb, way))

        if s == 0:
            opened(last)
            opened(last - 1)
            passed_c(last)
            return
        if s <= last + 2:
            added(last + 1 - s)
        if last - 1 - s >= -1:
            opened(last - 1 - s)
        if last - s >= 0:
            passed_c(last - s)
        if s >= 2 and last + 2 - s >= 0:
            passed(last + 2 - s)
        if s == last + 1:
            self.own_c(p)
        if s == last + 2:
            self.turn_c(p)
        if s == last + 3:
            self.close(p)

    def sent(self, p):
        def line(zb, way):
            from_line = (self.z - way >= 0) & (self.z - way < self.depth)
            self.z_copy(p, zb, way).wait_send()
            pl.when(from_line)(lambda: self.zc_copy(p, zb, way, False).wait_send())
            pl.when(jnp.logical_not(from_line))(lambda: self.zc_copy(p, zb, way, True).wait_send())

        for zb in range(self.depth):
            self.a1(p, zb).wait_send()
            self.b1(p, zb, 0).wait_send()
            self.b1(p, zb, 1).wait_send()
            self.a2(p, zb).wait_send()
            self.b2(p, zb).wait_send()
        for step in range(self.depth - 1):
            self.at_step(step, line)
        self.cy(p).wait_send()
        self.cx(p).wait_send()
        self.done(p).wait()


class SmallSum:
    def __init__(self, lines, buffer, send, recv):
        member = lax.axis_index("tensor")
        self.partners = [{"tensor": 1 - member}, {"dp": lines.x_peer}, {"dp": lines.y_peer}]
        for level in range(lines.depth.bit_length() - 1):
            reach = 1 << level
            way = 1 - 2 * ((lines.z // reach) % 2)
            self.partners.append({"dp": lines.me + 4 * reach * way})
        self.buffer, self.send, self.recv = buffer, send, recv

    def copy(self, step):
        return pltpu.make_async_remote_copy(
            src_ref=self.buffer.at[step],
            dst_ref=self.buffer.at[len(self.partners) + 1 + step],
            send_sem=self.send.at[step],
            recv_sem=self.recv.at[step],
            device_id=self.partners[step],
            device_id_type=MESH,
        )

    def step(self, step):
        if step:
            self.copy(step - 1).wait_recv()
            self.buffer[step] = self.buffer[step - 1] + self.buffer[len(self.partners) + step]
        if step < len(self.partners):
            self.copy(step).start()

    def sent(self):
        for step in range(len(self.partners)):
            self.copy(step).wait_send()


def adamw_update(master, moment, square, gradient, step_rate, decay_rate):
    moment_new = beta_one * moment + (1.0 - beta_one) * gradient
    square_new = beta_two * square + (1.0 - beta_two) * gradient * gradient
    moment_hat = moment_new * (1.0 / (1.0 - beta_one**STEP))
    square_hat = square_new * (1.0 / (1.0 - beta_two**STEP))
    master_new = master - step_rate * (
        moment_hat / (jnp.sqrt(square_hat) + adam_epsilon) + decay_rate * master
    )
    return (moment_new, square_new, master_new)


SCATTER_AT = {
    "reduce": {5: [(0, 0)]},
    "expand": {0: [(0, 1)], 1: [(1, 0)], 5: [(2, 0)], 6: [(0, 2)]},
    "norm": {0: [(1, 1)], 3: [(2, 1)], 4: [(3, 0)]},
    "merge": {1: [(1, 2)]},
    "attend": {1: [(3, 1)], 3: [(0, 3)], 6: [(2, 2)], 7: [(3, 2)], 11: [(2, 3)], 13: [(2, 4)], 14: [(4, 1)], 18: [(3, 4)], 21: [(4, 2)]},
    "project": {0: [(4, 0), (3, 3), (1, 3)], 1: [(5, 0)]},
    "terms": {0: [(4, 3)], 1: [(5, 1)], 2: [(3, 5)], 4: [(0, 4)]},
    "far": {-1: [(5, 2)], 0: [(4, 4)]},
    "near": {0: [(5, 3), (1, 4)]},
    "encoded": {0: [(5, 4), (4, 5)]},
    "end": [(0, 5), (2, 5), (1, 5), (5, 5)],
}


def back_kernel(
    depth, lengths_ref, dealing_ref, vectors_ref,
    whole_ref, far_ref, qkv_in, hidden_turned_in, upstream_in, context_in, totals_in,
    acc_in, normal_in, inverse_in, turned_in, active_in, slope_in, far_ctx_in, *rest,
):
    encoded_out, input_out, small_out, *rest = rest
    targets, rest = rest[:6], rest[6:]
    enc_pair, grad_ref, input_far, acc, arrived, merge_recv, small, score_bias, *rest = rest
    chunk_grads, *rest = rest
    grads, rest = [*[chunk_grads.at[p] for p in range(4)], *rest[:2]], rest[2:]
    shards, rest = rest[:6], rest[6:]
    buffers, rest = rest[: 6 * Scatter.buffers], rest[6 * Scatter.buffers :]
    small_send, small_recv, in_sem, load_sem, ctx_sem, far_send, far_recv, merge_sem, enc_sem, input_sem, *sems = rest
    lines = Scatter(depth, grads, shards, targets, buffers, sems)
    sums = SmallSum(lines, small, small_send, small_recv)
    group = Group(lengths_ref, dealing_ref)
    member = lax.axis_index("tensor")
    rows, width = acc.shape
    total_rows = 2 * rows
    chunks, _, both = active_in.shape
    half = both // 2
    per_piece = chunks // 2
    piece_span = grads[0].shape[1]
    pairs = qkv_in.shape[0]
    inner = pairs * PAIR
    tall, short = 256, 128

    def rows_of(which):
        return pl.ds(pl.multiple_of(which * rows, rows), rows)

    def tile(step, size):
        return pl.ds(pl.multiple_of(step * size, size), size)

    def fetch(source, target, sem):
        return pltpu.make_async_copy(source, target, in_sem.at[sem])

    def phase(name, count, body):
        between = {
            step: [functools.partial(lines.stage, *stage) for stage in stages]
            for step, stages in SCATTER_AT.get(name, {}).items()
        }
        for act in between.pop(-1, ()):
            act()
        looped(count, body, between)

    def places_of(first):
        return first + lax.broadcasted_iota(jnp.int32, (tall, 1), 0)

    def add_sum(row, values):
        small[0, row : row + 1, :] += jnp.sum(values, axis=0, keepdims=True)

    def feed_phase(later, late, late_turned, turned, upstream, active, slope, inner_grad, expand_buf, reduce_buf, leaving):
        def active_load(j):
            slot = lax.rem(j, 2)
            return [pltpu.make_async_copy(active_in.at[j], active.at[slot], load_sem.at[slot, 4])]

        def loads(j):
            slot = lax.rem(j, 2)
            array, *firsts = chunk_columns(j, per_piece, half)
            copies = [pltpu.make_async_copy(slope_in.at[j], slope.at[slot], load_sem.at[slot, 5])]
            for kind, buf in enumerate((expand_buf, reduce_buf)):
                first = pl.multiple_of(firsts[kind], half)
                for side, source in enumerate((far_ref, whole_ref)):
                    copies.append(
                        pltpu.make_async_copy(
                            source.at[array, :, pl.ds(first, half)],
                            buf.at[slot, :, pl.ds(side * half, half)],
                            load_sem.at[slot, 2 * kind + side],
                        )
                    )
            return copies

        def taken(j, load):
            for copy in load(j):
                copy.wait()

            @pl.when(j + 1 < chunks)
            def _():
                for copy in load(j + 1):
                    copy.start()

        acc_copy = fetch(acc_in, acc, 0)
        acc_copy.start()
        fetches = [fetch(upstream_in, upstream, 1), fetch(turned_in, turned, 2)]
        for copy in fetches:
            copy.start()
        for copy in [*active_load(0), *loads(0)]:
            copy.start()
        greet_line(
            lines.me, lines.z, lines.y, lines.x, depth, [sums.partners[0], *sums.partners[3:]]
        )
        for copy in later:
            copy.start()
        small[0] = jnp.zeros(small.shape[1:], WIDE)
        score_bias[...] = group.score_bias(total_rows - LONGEST)
        acc_copy.wait()
        for copy in fetches:
            copy.wait()

        def late_tile(step):
            at = tile(step, short)
            unit, scale = norm(acc[at, :])
            upper = upstream[at, :].astype(WIDE)
            upstream[at, :] = (unit * vectors_ref[6:7, :] + vectors_ref[7:8, :]).astype(LOW)
            add_sum(6, upper * unit)
            add_sum(7, upper)
            grad = norm_back(upper * vectors_ref[6:7, :], unit, scale)
            grad_low = grad.astype(LOW)
            add_sum(5, grad_low.astype(WIDE))
            acc[at, :] = grad
            late[at, :] = grad_low
            late_turned[:, at] = grad.T.astype(LOW)

        looped(rows // short, late_tile, {})
        enc_near = pltpu.make_async_copy(upstream, enc_pair.at[member], enc_sem.at[2])
        enc_far = other_core(upstream, enc_pair.at[member], enc_sem.at[0], enc_sem.at[1])
        enc_near.start()
        enc_far.start()

        def send(k):
            slot = lax.rem(k, 2)
            return other_core(
                leaving.at[slot], arrived.at[slot], far_send.at[slot], far_recv.at[slot]
            )

        def own_columns(k):
            return pl.ds(pl.multiple_of(lax.rem(k, per_piece) * half, half), half)

        def finish(k):
            piece, slot = k // per_piece, lax.rem(k, 2)
            send(k).wait_recv()

            @pl.loop(0, width // tall)
            def _(step):
                at = tile(step, tall)
                chunk_grads[piece, at, own_columns(k)] += arrived[slot, at, :]

        def products(k, left, right):
            piece, slot = k // per_piece, lax.rem(k, 2)

            @pl.when(k >= 2)
            def _():
                send(k - 2).wait_send()

            parts = [
                dot_nn(left[step * tall : (step + 1) * tall, :], right[...])
                for step in range(width // tall)
            ]
            for step, part in enumerate(parts):
                at = slice(step * tall, (step + 1) * tall)
                leaving[slot, at, :] = part[:, 0:half].astype(LOW)
                chunk_grads[piece, at, own_columns(k)] = part[:, half:both].astype(LOW)

            @pl.when(k >= 1)
            def _():
                finish(k - 1)

            send(k).start()

        def reduce_chunk(j):
            taken(j, active_load)
            products(j, late_turned, active.at[lax.rem(j, 2)])

        def expand_chunk(j):
            slot = lax.rem(j, 2)
            taken(j, loads)
            total = jnp.zeros((1, both), WIDE)
            tiles = [slice(step * tall, (step + 1) * tall) for step in range(rows // tall)]
            parts = [dot_nn(late[at, :], reduce_buf[slot]) for at in tiles]
            for at, part in zip(tiles, parts, strict=True):
                grad = (part * slope[slot, at, :].astype(WIDE)).astype(LOW)
                inner_grad[at, :] = grad
                total = total + jnp.sum(grad.astype(WIDE), axis=0, keepdims=True)
                acc[at, :] += dot_nt(grad, expand_buf[slot])
            for which, side in ((1 - member, 0), (member, half)):
                row = 8 + which * 2 + j // per_piece
                small[0, pl.ds(row, 1), own_columns(j)] = total[:, side : side + half]
            products(chunks + j, turned, inner_grad)

        phase("reduce", chunks, reduce_chunk)
        phase("expand", chunks, expand_chunk)
        finish(2 * chunks - 1)
        for k in (2 * chunks - 2, 2 * chunks - 1):
            send(k).wait_send()
        enc_near.wait()
        enc_far.wait()

    def merge_phase(normal, inverse, near_ctx, far_ctx, merge, merge_far, fetches, turned, grad_own, grad_far, merge_send):
        for copy in fetches:
            copy.wait()

        def norm_tile(step):
            at = tile(step, short)
            grad = acc[at, :]
            unit = normal[at, :]
            add_sum(3, grad * unit)
            add_sum(4, grad)
            branch_grad = norm_back(grad * vectors_ref[3:4, :], unit, inverse[at, 0:1])
            branch_low = branch_grad.astype(LOW)
            add_sum(2, branch_low.astype(WIDE))
            acc[at, :] = branch_grad
            turned[:, at] = branch_grad.T.astype(LOW)
            grad_far[at, :] = dot_nn(branch_low, merge_far[...]).astype(LOW)
            grad_own[at, :] = dot_nn(branch_low, merge[...]).astype(LOW)

        phase("norm", rows // short, norm_tile)
        out_grad = other_core(grad_far, grad_ref.at[rows_of(member)], ctx_sem.at[0], ctx_sem.at[1])
        in_grad = pltpu.make_async_copy(grad_own, grad_ref.at[rows_of(member)], ctx_sem.at[2])
        out_grad.start()
        in_grad.start()
        out_merge = other_core(merge_send, merge_recv, merge_sem.at[0], merge_sem.at[1])

        def merge_step(which):
            @pl.when(which == 0)
            def _():
                for step in range(width // tall):
                    at = slice(step * tall, (step + 1) * tall)
                    merge_send[at, :] = dot_nn(turned[at, :], far_ctx[...]).astype(LOW)
                out_merge.start()

            @pl.when(which == 1)
            def _():
                out_merge.wait()
                for step in range(width // tall):
                    at = slice(step * tall, (step + 1) * tall)
                    grads[4][at, 0:inner] = (
                        dot_nn(turned[at, :], near_ctx[...]) + merge_recv[at, :].astype(WIDE)
                    ).astype(LOW)

        phase("merge", 2, merge_step)
        out_grad.wait()
        in_grad.wait()

    def early_phase(normal, inverse, near_ctx, far_ctx, merge, merge_far):
        merge_columns = pl.ds(whole_ref.shape[2] - inner, inner)
        fetches = [
            fetch(normal_in, normal, 3),
            fetch(inverse_in, inverse, 4),
            fetch(context_in.at[rows_of(member)], near_ctx, 5),
            fetch(far_ctx_in, far_ctx, 6),
            fetch(whole_ref.at[0, :, merge_columns], merge, 7),
            fetch(far_ref.at[0, :, merge_columns], merge_far, 8),
        ]
        pl.run_scoped(
            functools.partial(feed_phase, fetches),
            pltpu.VMEM((rows, width), LOW),
            pltpu.VMEM((width, rows), LOW),
            pltpu.VMEM((width, rows), LOW),
            pltpu.VMEM((rows, width), LOW),
            pltpu.VMEM((2, rows, both), LOW),
            pltpu.VMEM((2, rows, both), LOW),
            pltpu.VMEM((rows, both), LOW),
            pltpu.VMEM((2, width, both), LOW),
            pltpu.VMEM((2, width, both), LOW),
            pltpu.VMEM((2, width, half), LOW),
        )
        pl.run_scoped(
            functools.partial(
                merge_phase, normal, inverse, near_ctx, far_ctx, merge, merge_far, fetches
            ),
            pltpu.VMEM((width, rows), LOW),
            pltpu.VMEM((rows, inner), LOW),
            pltpu.VMEM((rows, inner), LOW),
            pltpu.VMEM((width, inner), LOW),
        )

    pl.run_scoped(
        early_phase,
        pltpu.VMEM((rows, width), WIDE),
        pltpu.VMEM((rows, 128), WIDE),
        pltpu.VMEM((rows, inner), LOW),
        pltpu.VMEM((rows, inner), LOW),
        pltpu.VMEM((width, inner), LOW),
        pltpu.VMEM((width, inner), LOW),
    )

    def last_phase(mixed):
        def attend_phase(qkv, context, upper, totals, dots, key_turned, queries, uppers, query_sum, hidden_turned):
            def loads(pair, slot):
                columns = pl.ds(pl.multiple_of(pair * PAIR, PAIR), PAIR)
                return [
                    pltpu.make_async_copy(qkv_in.at[pair], qkv.at[slot], load_sem.at[slot, 0]),
                    pltpu.make_async_copy(
                        context_in.at[:, columns], context.at[slot], load_sem.at[slot, 1]
                    ),
                    pltpu.make_async_copy(
                        grad_ref.at[:, columns], upper.at[slot], load_sem.at[slot, 2]
                    ),
                ]

            fetches = [fetch(totals_in, totals, 0)]
            for copy in [*loads(0, 0), *fetches]:
                copy.start()
            for copy in fetches:
                copy.wait()
            blocks = ((0, LONGEST), (LONGEST, total_rows - LONGEST))
            per_pair = total_rows // TILE

            def hidden_tile(step, slot):
                return pltpu.make_async_copy(
                    hidden_turned_in.at[tile(step, tall), :],
                    hidden_turned.at[slot],
                    load_sem.at[slot, 3],
                )

            def project(second):
                grad, first = (grads[5], 0) if second else (grads[4], inner)
                span = (pairs // 2) * 3 * PAIR
                columns = slice(span if second else 0, span * 2 if second else span)
                hidden_tile(0, 0).start()
                for step in range(width // tall):
                    if step + 1 < width // tall:
                        hidden_tile(step + 1, (step + 1) % 2).start()
                    hidden_tile(step, step % 2).wait()
                    grad[step * tall : (step + 1) * tall, first : first + span] = dot_nn(
                        hidden_turned[step % 2], mixed[:, columns]
                    ).astype(LOW)

            def pair_body(pair):
                slot = lax.rem(pair, 2)
                for copy in loads(pair, slot):
                    copy.wait()

                @pl.when(pair + 1 < pairs)
                def _():
                    for copy in loads(pair + 1, 1 - slot):
                        copy.start()

                attend_back_open(
                    qkv.at[slot], context.at[slot], upper.at[slot], dots, key_turned, queries, uppers
                )
                base = pair * 3 * PAIR

                def columns(which):
                    return pl.ds(pl.multiple_of(base + which * PAIR, PAIR), PAIR)

                for begin, size in blocks:
                    block = slice(begin, begin + size)
                    query_sum[:, block] = jnp.zeros((PAIR, size), WIDE)

                    def key_tile(step, begin=begin, size=size):
                        at, key_sum, value_sum = attend_back_tile(
                            qkv.at[slot], score_bias, totals.at[pair], dots, key_turned, queries, uppers, query_sum,
                            begin, size, step,
                        )
                        mixed[at, columns(1)] = key_sum.astype(LOW)
                        mixed[at, columns(2)] = value_sum.astype(LOW)

                    between = {}
                    for step in range(size // TILE):
                        number = begin // TILE + step
                        for act_pair in range(pairs):
                            for p, s in SCATTER_AT["attend"].get(act_pair * per_pair + number, ()):

                                def act(act_pair=act_pair, p=p, s=s):
                                    pl.when(pair == act_pair)(lambda: lines.stage(p, s))

                                between.setdefault(step, []).append(act)
                    looped(size // TILE, key_tile, between)
                    mixed[block, columns(0)] = (
                        (query_sum[:, block] * HEAD_DIM ** (-0.5)).T.astype(LOW)
                    )
                for which, row in ((0, 0), (2, 1)):
                    part = mixed[:, columns(which)].astype(WIDE)
                    spot = pl.multiple_of(member * inner + pair * PAIR, PAIR)
                    small[0, row : row + 1, pl.ds(spot, PAIR)] = jnp.sum(
                        part, axis=0, keepdims=True
                    )

            def project_stages(second):
                return [
                    functools.partial(project, second),
                    *[functools.partial(lines.stage, *st) for st in SCATTER_AT["project"][second]],
                ]

            looped(pairs, pair_body, {1: project_stages(0), 3: project_stages(1)})

        pl.run_scoped(
            attend_phase,
            pltpu.VMEM((2, total_rows, 3 * PAIR), LOW),
            pltpu.VMEM((2, total_rows, PAIR), LOW),
            pltpu.VMEM((2, total_rows, PAIR), LOW),
            pltpu.VMEM(totals_in.shape, WIDE),
            pltpu.VMEM((8, total_rows), WIDE),
            pltpu.VMEM((PAIR, total_rows), LOW),
            pltpu.VMEM((2, total_rows, PAIR), LOW),
            pltpu.VMEM((2, total_rows, PAIR), LOW),
            pltpu.VMEM((PAIR, total_rows), WIDE),
            pltpu.VMEM((2, tall, total_rows), LOW),
        )
        sums.step(0)

        def input_phase(weight, terms, leaving, pair):
            weight_copy = fetch(whole_ref.at[0, :, pl.ds(0, pairs * 3 * PAIR)], weight, 0)
            weight_copy.start()
            pair_copies = [fetch(enc_pair.at[i], pair.at[rows_of(i)], 3 + i) for i in range(2)]
            for copy in pair_copies:
                copy.start()
            weight_copy.wait()

            def term_tile(step):
                at = tile(step, tall)
                total = dot_nt(mixed[at, :], weight[...])
                own = rows // tall
                mine = step // own == member

                @pl.when(mine)
                def _():
                    terms[at, :] = (total + acc[tile(lax.rem(step, own), tall), :]).astype(LOW)

                @pl.when(jnp.logical_not(mine))
                def _():
                    terms[at, :] = total.astype(LOW)

            phase("terms", total_rows // tall, term_tile)
            sums.step(1)

            def own_rows(which, step):
                places = places_of(which * rows + step * tall)
                return picked_rows(group.moved(places, group.own, group.first), terms)

            def far_tile(step):
                leaving[tile(step, tall), :] = own_rows(1 - member, step).astype(LOW)

            phase("far", rows // tall, far_tile)
            crossing = other_core(leaving, input_far, input_sem.at[0], input_sem.at[1])
            crossing.start()
            sums.step(2)

            def near_tile(step):
                acc[tile(step, tall), :] = own_rows(member, step)

            phase("near", rows // tall, near_tile)
            sums.step(3)
            crossing.wait()
            back = fetch(input_far, leaving, 2)
            back.start()
            back.wait()

            @pl.loop(0, rows // short)
            def _(step):
                at = tile(step, short)
                leaving[at, :] = (acc[at, :] + leaving[at, :].astype(WIDE)).astype(LOW)

            done = fetch(leaving, input_out, 2)
            done.start()
            for copy in pair_copies:
                copy.wait()

            def encoded_tile(step):
                places = places_of(member * rows + step * tall)
                index = group.moved(places, group.dealt, group.first)
                terms[tile(step, tall), :] = picked_rows(index, pair).astype(LOW)

            phase("encoded", rows // tall, encoded_tile)
            done.wait()
            done = fetch(terms.at[pl.ds(0, rows)], encoded_out, 2)
            done.start()
            done.wait()

        pl.run_scoped(
            input_phase,
            pltpu.VMEM((width, pairs * 3 * PAIR), LOW),
            pltpu.VMEM((total_rows, width), LOW),
            pltpu.VMEM((rows, width), LOW),
            pltpu.VMEM((total_rows, width), LOW),
        )

    pl.run_scoped(last_phase, pltpu.VMEM((total_rows, pairs * 3 * PAIR), LOW))

    for step in range(4, len(sums.partners) + 1):
        sums.step(step)
    small_out[...] = small[len(sums.partners)]
    for st in SCATTER_AT["end"]:
        lines.stage(*st)
    sums.sent()
    for p in range(len(grads)):
        lines.sent(p)


def finish_kernel(*refs):
    sources, refs = refs[:27], refs[27:]
    targets, refs = refs[:21], refs[21:]
    held, made, (in_sem, out_sem) = refs[:27], refs[27:46], refs[46:]
    loads = [pltpu.make_async_copy(sources[i], held[i], in_sem.at[i]) for i in range(27)]
    for copy in loads:
        copy.start()
    small_ref, *smalls = held[:7]
    vectors_ref, vectors_first, vectors_second, hidden_ref, hidden_first, hidden_second = smalls
    shards, ins, rows_held = held[7:13], held[13:25], held[25:]
    vector_grad_ref, *rest = made
    outs, small_out = rest[:12], rest[12:]
    results = [*rows_held, *made]
    writes = [pltpu.make_async_copy(results[i], targets[i], out_sem.at[i]) for i in range(21)]
    for copy in loads[:7]:
        copy.wait()
    width = vectors_ref.shape[1]
    inner = ins[3].shape[1]
    pairs = inner // PAIR
    span = shards[0].shape[1]
    vector_grad_ref[...] = small_ref[0:8, :]
    states = vectors_ref[...], vectors_first[...], vectors_second[...]
    for i, value in enumerate(adamw_update(*states, small_ref[0:8, :], rate_vectors, 0.0)):
        small_out[i][...] = value
    for i in range(hidden_ref.shape[1] // width):
        columns = slice(i * width, (i + 1) * width)
        states = hidden_ref[:, columns], hidden_first[:, columns], hidden_second[:, columns]
        grad = small_ref[8 + i : 9 + i, :]
        for n, value in enumerate(adamw_update(*states, grad, rate_hidden, 0.0)):
            small_out[3 + n][:, columns] = value

    def update(matrix, lead, columns, grad, grad_columns):
        rate = (rate_project, rate_merge, rate_expand, rate_reduce)[matrix]

        @pl.loop(0, grad.shape[0] // 16)
        def _(step):
            at = pl.ds(pl.multiple_of(step * 16, 16), 16)
            old = [ins[3 * matrix + i][(*lead, at, columns)] for i in range(3)]
            new = adamw_update(*old, grad[at, grad_columns], rate, weight_decay)
            for i in range(3):
                outs[3 * matrix + i][(*lead, at, columns)] = new[i]

    for i in (2, *range(15, 21)):
        writes[i].start()
    for copy in loads[7:13]:
        copy.wait()
    for matrix in (3, 2, 1, 0):
        for copy in loads[13 + 3 * matrix : 16 + 3 * matrix]:
            copy.wait()
        if matrix >= 2:
            for i in range(2):
                columns = slice(i * span, (i + 1) * span)
                update(matrix, (), columns, shards[2 * (3 - matrix) + i], slice(0, span))
        elif matrix == 1:
            update(matrix, (), slice(0, inner), shards[4], slice(0, inner))
        else:
            for pair in range(pairs):
                piece, begin = (4, inner) if pair < pairs // 2 else (5, 0)
                for c in range(3):
                    at = begin + (3 * (pair % (pairs // 2)) + c) * PAIR
                    columns = slice(pair * PAIR, (pair + 1) * PAIR)
                    update(matrix, (c,), columns, shards[piece], slice(at, at + PAIR))
        for copy in writes[3 + 3 * matrix : 6 + 3 * matrix]:
            copy.start()
        if matrix == 3:
            for copy in loads[25:]:
                copy.wait()
            for copy in writes[:2]:
                copy.start()
    for copy in writes:
        copy.wait()


def finish(small, shards, rows_out, matrices, vectors, hidden):
    states = [one for matrix in matrices for one in matrix]
    operands = [small, *vectors, *hidden, *shards, *states, *rows_out]
    shape, sem = jax.ShapeDtypeStruct, pltpu.SemaphoreType.DMA
    results = [
        *[shape(one.shape, LOW) for one in rows_out],
        shape((8, small.shape[1]), WIDE),
        *[shape(one.shape, WIDE) for one in (*states, *vectors, *hidden)],
    ]
    anywhere = pl.BlockSpec(memory_space=pl.ANY)
    return pl.pallas_call(
        finish_kernel,
        in_specs=[anywhere] * len(operands),
        out_specs=[anywhere] * len(results),
        out_shape=results,
        scratch_shapes=[
            *[pltpu.VMEM(one.shape, one.dtype) for one in operands],
            *[pltpu.VMEM(one.shape, one.dtype) for one in results[2:]],
            sem((len(operands),)),
            sem((len(results),)),
        ],
        compiler_params=pltpu.CompilerParams(vmem_limit_bytes=63 * MIB),
    )(*operands)


def back(lengths, dealing, vectors, whole, far, kept, parts):
    qkv, hidden_turned, upstream, context, totals, acc, *_ = kept
    rows, width = acc.shape
    total_rows, inner = context.shape
    depth, shard_rows = parts // 4, width // parts
    half, pair_span = 256, 3 * PAIR * (qkv.shape[0] // 2)
    piece_span = whole.shape[2] // 2
    spans = (*[piece_span] * 4, inner + pair_span, pair_span)
    classes = []
    for span in spans:
        third = max(128, span // 5 // 128 * 128)
        if (span - third) % 256:
            third += 128
        classes.append(((span - third) // 2, (span - third) // 2, third))
    shape, sem = jax.ShapeDtypeStruct, pltpu.SemaphoreType.DMA
    vmem, anywhere = pl.BlockSpec(memory_space=pltpu.VMEM), pl.BlockSpec(memory_space=pl.ANY)
    steps = 3 + depth.bit_length() - 1
    results = pl.pallas_call(
        functools.partial(back_kernel, depth),
        in_specs=[
            *[pl.BlockSpec(memory_space=pltpu.SMEM)] * 2,
            vmem,
            *[anywhere] * (2 + len(kept)),
        ],
        out_specs=[*[anywhere] * 2, vmem, *[anywhere] * (len(spans) + 3)],
        out_shape=[
            shape((rows, width), LOW),
            shape((rows, width), LOW),
            shape((16, width), WIDE),
            *[shape((shard_rows, span), WIDE) for span in spans],
            shape((2, rows, width), LOW),
            shape((total_rows, inner), LOW),
            shape((rows, width), LOW),
        ],
        scratch_shapes=[
            pltpu.VMEM((rows, width), WIDE),
            pltpu.VMEM((2, width, half), LOW),
            pltpu.VMEM((width, inner), LOW),
            pltpu.VMEM((2 * steps + 1, 16, width), WIDE),
            pltpu.VMEM((total_rows - LONGEST, total_rows - LONGEST), WIDE),
            pltpu.VMEM((4, width, piece_span), LOW),
            *[pltpu.VMEM((width, span), LOW) for span in spans[4:]],
            *[pltpu.VMEM((shard_rows, span), WIDE) for span in spans],
            *Scatter.scratch(depth, shard_rows, classes),
            sem((steps,)),
            sem((steps,)),
            sem((9,)),
            sem((2, 6)),
            sem((3,)),
            sem((2,)),
            sem((2,)),
            sem((2,)),
            sem((3,)),
            sem((2,)),
            *Scatter.semaphores(depth, len(spans)),
        ],
        compiler_params=pltpu.CompilerParams(
            collective_id=1, has_side_effects=True, vmem_limit_bytes=63 * MIB
        ),
    )(lengths, dealing, vectors, whole, far, *kept)
    return results[:2], results[2], results[3 : 3 + len(spans)]


def by_kernels(tokens, cotangent, lengths, dealing, project, merge, expand, reduce, vectors, hidden, parts):
    hidden = tuple(one.reshape(1, -1) for one in hidden)
    matrices = (project, merge, expand, reduce)
    whole, far, *kept = front(
        lengths, dealing, *[one[0] for one in matrices], vectors[0], hidden[0], tokens, cotangent, parts
    )
    rows_out, small, shards = back(lengths, dealing, vectors[0], whole, far, kept, parts)
    results = finish(small, shards, rows_out, matrices, vectors, hidden)
    encoded, input_grad, vector_grad = results[:3]
    news = [results[3 + 3 * i : 6 + 3 * i] for i in range(6)]
    return (
        encoded,
        input_grad,
        *news[0],
        *[one.T for one in news[1]],
        *news[2],
        *[one.T for one in news[3]],
        *news[4],
        *[one.reshape(-1) for one in news[5]],
        vector_grad,
    )


def local(
    tokens,
    cotangent,
    lengths,
    dealing,
    project_weight,
    project_first,
    project_second,
    merge_weight,
    merge_first,
    merge_second,
    expand_weight,
    expand_first,
    expand_second,
    reduce_weight,
    reduce_first,
    reduce_second,
    vectors,
    vector_first,
    vector_second,
    hidden_bias,
    hidden_first,
    hidden_second,
):
    parts = lax.axis_size("dp")
    member = lax.axis_index("tensor")
    other = 1 - member
    half_rows, model_width = tokens.shape
    total_rows = 2 * half_rows
    width_half = project_weight.shape[2]
    pairs = width_half // PAIR
    hidden_half = expand_weight.shape[1]
    shard_rows = expand_weight.shape[0]
    own_begin = member * half_rows
    by_kernel = parts % 4 == 0 and (parts & (parts - 1)) == 0 and shard_rows % 16 == 0

    def swap(value):
        return lax.ppermute(value, "tensor", [(0, 1), (1, 0)])

    def own(value, size, which=member):
        return lax.dynamic_slice_in_dim(value, which * size, size, 0)

    if by_kernel:
        return by_kernels(
            tokens, cotangent, lengths, dealing,
            (project_weight, project_first, project_second),
            (merge_weight.T, merge_first.T, merge_second.T),
            (expand_weight, expand_first, expand_second),
            (reduce_weight.T, reduce_first.T, reduce_second.T),
            (vectors, vector_first, vector_second),
            (hidden_bias, hidden_first, hidden_second),
            parts,
        )

    segment, own_of, dealt_of, from_own, from_dealt = layout(lengths[0], dealing[0], total_rows)
    dealt_of = own(dealt_of, half_rows)
    short = segment[LONGEST:]
    score_bias = jnp.where(short[:, None] == short[None, :], 0.0, masked_score).astype(WIDE)

    def own_first(index):
        return lax.rem(index - own_begin + total_rows, total_rows)

    projections = (
        project_weight.reshape(3, shard_rows, pairs, PAIR)
        .transpose(1, 2, 0, 3)
        .reshape(shard_rows, 3 * width_half)
    )
    quarter = hidden_half // 2
    reduce_turned = reduce_weight.T
    shards = jnp.stack(
        [
            jnp.concatenate([projections, merge_weight.T], axis=1),
            jnp.concatenate([expand_weight[:, :quarter], reduce_turned[:, :quarter]], axis=1),
            jnp.concatenate([expand_weight[:, quarter:], reduce_turned[:, quarter:]], axis=1),
        ]
    ).astype(LOW)
    zeros_pair = jnp.zeros((pairs, PAIR), WIDE)
    bias_row = jnp.concatenate(
        [
            own(vectors[0], width_half).reshape(pairs, PAIR),
            zeros_pair,
            own(vectors[1], width_half).reshape(pairs, PAIR),
        ],
        axis=1,
    ).reshape(pairs, 1, 3 * PAIR)
    whole = lax.all_gather(shards, "dp", axis=1, tiled=True)
    far = swap(whole)
    token_pair = jnp.concatenate([tokens, swap(tokens)], axis=0)
    upper_pair = jnp.concatenate([cotangent, swap(cotangent)], axis=0)
    hidden = dot_nn(pick_rows(own_first(own_of), total_rows), token_pair).astype(LOW)
    upstream = dot_nn(pick_rows(own_first(dealt_of), total_rows), upper_pair).astype(LOW)
    qkv = jnp.einsum(
        "rd,dpc->prc",
        hidden,
        whole[0, :, : 3 * width_half].reshape(model_width, pairs, 3 * PAIR),
        preferred_element_type=WIDE,
    )
    qkv = (qkv + bias_row).astype(LOW)
    context, totals = attend(qkv, score_bias)

    (
        encoded, branch_grad, context_grad, merge_grad, expand_grad, reduce_grad, sums, hidden_part_own, hidden_part_far,
    ) = feed_block(
        context,
        whole,
        far,
        own(hidden, half_rows),
        upstream,
        vectors,
        own(hidden_bias, hidden_half),
        own(hidden_bias, hidden_half, other),
    )
    encoded_pair = jnp.concatenate([encoded, swap(encoded)], axis=0)
    encoded_out = dot_nn(
        pick_rows(own_first(own(from_dealt, half_rows)), total_rows), encoded_pair
    ).astype(LOW)
    mixed_grads = attend_back(qkv, score_bias, context, context_grad, totals)
    mixed_sums = jnp.sum(mixed_grads.astype(WIDE), axis=1).reshape(pairs, 3, PAIR)
    mixed_grads = mixed_grads.transpose(1, 0, 2).reshape(total_rows, 3 * width_half)
    project_grad = dot_tn(hidden, mixed_grads)
    input_terms = dot_nt(mixed_grads, whole[0, :, : 3 * width_half])
    own_part = own(input_terms, half_rows) + branch_grad
    input_terms = lax.dynamic_update_slice_in_dim(input_terms, own_part, own_begin, 0).astype(LOW)
    input_far = swap(
        dot_nn(pick_rows(own(from_own, half_rows, other), total_rows), input_terms).astype(LOW)
    )
    input_grad = (
        dot_nn(pick_rows(own(from_own, half_rows), total_rows), input_terms)
        + input_far.astype(WIDE)
    ).astype(LOW)
    zeros_width = jnp.zeros((model_width,), WIDE)
    zeros_hidden = jnp.zeros_like(hidden_bias)
    hidden_total = lax.dynamic_update_slice_in_dim(
        lax.dynamic_update_slice_in_dim(
            zeros_hidden, hidden_part_own, member * hidden_half, 0
        ),
        hidden_part_far,
        other * hidden_half,
        0,
    )
    vector_rows = [
        lax.dynamic_update_slice_in_dim(
            zeros_width, mixed_sums[:, c].reshape(-1), member * width_half, 0
        )
        for c in (0, 2)
    ]
    small = jnp.concatenate(
        [
            jnp.stack(vector_rows),
            sums[2:],
            hidden_total.reshape(-1, model_width),
            jnp.zeros((4, model_width), WIDE),
        ],
        axis=0,
    )
    grads = [
        lax.psum_scatter(g.astype(LOW), "dp", scatter_dimension=0, tiled=True).astype(WIDE)
        for g in (project_grad, merge_grad, expand_grad, reduce_grad)
    ]
    small = lax.psum(small, ("dp", "tensor"))
    project_shard, merge_shard, expand_shard, reduce_shard = grads
    project_shard = (
        project_shard.reshape(shard_rows, pairs, 3, PAIR)
        .transpose(2, 0, 1, 3)
        .reshape(3, shard_rows, width_half)
    )
    vector_grad = small[:8]
    hidden_grad = small[8:12].reshape(-1)
    return (
        encoded_out,
        input_grad,
        *adamw_update(
            project_weight, project_first, project_second, project_shard, rate_project, weight_decay
        ),
        *adamw_update(
            merge_weight, merge_first, merge_second, merge_shard.T, rate_merge, weight_decay
        ),
        *adamw_update(
            expand_weight, expand_first, expand_second, expand_shard, rate_expand, weight_decay
        ),
        *adamw_update(
            reduce_weight, reduce_first, reduce_second, reduce_shard.T, rate_reduce, weight_decay
        ),
        *adamw_update(vectors, vector_first, vector_second, vector_grad, rate_vectors, 0.0),
        *adamw_update(hidden_bias, hidden_first, hidden_second, hidden_grad, rate_hidden, 0.0),
        vector_grad,
    )


def solution(mesh):
    sharded = (
        P("dp", None),
        P("dp", None),
        *[P(None, "dp", "tensor")] * 3,
        *[P("tensor", "dp")] * 3,
        *[P("dp", "tensor")] * 3,
        *[P("tensor", "dp")] * 3,
        *[P()] * 6,
    )
    rows = P(("dp", "tensor"), None)
    return jax.shard_map(
        local,
        mesh=mesh,
        in_specs=(rows, rows, *sharded),
        out_specs=(rows, rows, *sharded[2:], P()),
        check_vma=False,
    )
```

```python
import functools

import jax
import jax.numpy as jnp
from jax import lax
from jax.experimental import pallas as pl
from jax.experimental.pallas import tpu as pltpu
from jax.sharding import PartitionSpec as P

HEAD_DIM = 64
LONGEST = 1024
STEP = 10
PAIR = 2 * HEAD_DIM
TILE = 256
MIB = 1024 * 1024
MESH = pl.DeviceIdType.MESH
LOW = jnp.bfloat16
WIDE = jnp.float32

beta_one = 0.9
beta_two = 0.999
adam_epsilon = 1e-08
weight_decay = 0.01
norm_epsilon = 1e-05
masked_score = -1e30
rate_project = 0.03
rate_merge = 0.3
rate_expand = 0.03
rate_reduce = 0.015
rate_vectors = 0.4
rate_hidden = 0.1


def dot_nn(a, b):
    return jnp.dot(a, b, preferred_element_type=WIDE)


def dot_nt(a, b):
    return lax.dot_general(a, b, (((1,), (1,)), ((), ())), preferred_element_type=WIDE)


def dot_tn(a, b):
    return lax.dot_general(a, b, (((0,), (0,)), ((), ())), preferred_element_type=WIDE)


def layout(lengths_row, dealing_row, total_rows):
    slots = jnp.arange(lengths_row.shape[0], dtype=jnp.int32)
    places = jnp.arange(total_rows, dtype=jnp.int32)
    rank_of = jnp.sum(jnp.where(dealing_row[None, :] == slots[:, None], slots[None, :], 0), axis=1)
    own_start = jnp.cumsum(lengths_row) - lengths_row
    dealt_start = jnp.sum(
        jnp.where(rank_of[None, :] < rank_of[:, None], lengths_row[None, :], 0), axis=1
    )
    longest = lengths_row == LONGEST
    short = jnp.where(longest, 0, lengths_row)
    start = jnp.where(longest, 0, LONGEST + jnp.cumsum(short) - short)

    def inside(begin):
        return (places[:, None] >= begin[None, :]) & (
            places[:, None] < (begin + lengths_row)[None, :]
        )

    def moved(begin, end):
        return places + jnp.sum(jnp.where(inside(begin), (end - begin)[None, :], 0), axis=1)

    segment = jnp.sum(jnp.where(inside(start), slots[None, :], 0), axis=1)
    return (
        segment,
        moved(start, own_start),
        moved(start, dealt_start),
        moved(own_start, start),
        moved(dealt_start, start),
    )


def pick_rows(index, rows):
    places = jnp.arange(rows, dtype=jnp.int32)
    return (index[:, None] == places[None, :]).astype(LOW)


class Group:
    def __init__(self, lengths_ref, dealing_ref):
        count = lengths_ref.shape[1]
        self.lengths = [lengths_ref[0, s] for s in range(count)]
        order = [dealing_ref[0, i] for i in range(count)]
        rank = [sum(jnp.where(order[i] == s, i, 0) for i in range(count)) for s in range(count)]
        short = [jnp.where(length == LONGEST, 0, length) for length in self.lengths]
        self.own, self.dealt, self.first = [], [], []
        own = own_short = jnp.int32(0)
        for s in range(count):
            self.own.append(own)
            self.first.append(jnp.where(self.lengths[s] == LONGEST, 0, LONGEST + own_short))
            self.dealt.append(
                sum(jnp.where(rank[j] < rank[s], self.lengths[j], 0) for j in range(count))
            )
            own, own_short = own + self.lengths[s], own_short + short[s]

    def inside(self, places, begin, s):
        return (places >= begin[s]) & (places < begin[s] + self.lengths[s])

    def moved(self, places, begin, end):
        total = places
        for s in range(len(begin)):
            total = total + jnp.where(self.inside(places, begin, s), end[s] - begin[s], 0)
        return total

    def score_bias(self, count):
        sides = []
        for shape, axis in (((count, 1), 0), ((1, count), 1)):
            places = lax.broadcasted_iota(jnp.int32, shape, axis) + LONGEST
            segment = jnp.zeros_like(places)
            for s in range(len(self.first)):
                segment = segment + jnp.where(self.inside(places, self.first, s), s, 0)
            sides.append(segment)
        return jnp.where(sides[0] == sides[1], 0.0, masked_score).astype(WIDE)


def picked_rows(index, source):
    places = lax.broadcasted_iota(jnp.int32, (index.shape[0], source.shape[0]), 1)
    return dot_nn(jnp.where(index == places, 1.0, 0.0).astype(LOW), source[...])


def attend_tile(qkv_ref, pair, bias_ref, begin, size, step, context_ref, columns, total_ref):
    lane = lax.broadcasted_iota(jnp.int32, (1, PAIR), 1)
    scale = HEAD_DIM ** (-0.5)
    first = pl.multiple_of(begin + step * TILE, TILE)
    query = qkv_ref[pair, pl.ds(first, TILE), 0:PAIR]
    key = qkv_ref[pair, begin : begin + size, PAIR : 2 * PAIR]
    value = qkv_ref[pair, begin : begin + size, 2 * PAIR : 3 * PAIR]
    outcome = []
    chosen = [jnp.where(lane // HEAD_DIM == head, scale, 0.0).astype(LOW) for head in range(2)]
    scores = [dot_nt(query * chosen[head], key) for head in range(2)]
    for head in range(2):
        score = scores[head]
        if begin:
            inner = pl.multiple_of(step * TILE, TILE)
            score = score + bias_ref[pl.ds(inner, TILE), :]
        top = jnp.max(score, axis=1, keepdims=True)
        exponent = jnp.exp(score - top)
        total = jnp.sum(exponent, axis=1, keepdims=True)
        outcome.append(dot_nn(exponent.astype(LOW), value) / total)
        log_total = jnp.broadcast_to(top + jnp.log(total), (TILE, PAIR))
        total_ref[pair, head : head + 1, pl.ds(first, TILE)] = log_total.T[0:1, :]
    context_ref[pl.ds(first, TILE), columns] = jnp.where(
        lane < HEAD_DIM, outcome[0], outcome[1]
    ).astype(LOW)


def attend_kernel(qkv_ref, bias_ref, context_ref, total_ref):
    rows = qkv_ref.shape[1]
    for begin, size in ((0, LONGEST), (LONGEST, rows - LONGEST)):

        @pl.loop(0, size // TILE)
        def _(step):
            attend_tile(
                qkv_ref, 0, bias_ref, begin, size, step, context_ref, slice(0, PAIR), total_ref
            )


def attend(qkv, bias):
    pairs, rows, width = qkv.shape
    return pl.pallas_call(
        attend_kernel,
        grid=(pairs,),
        in_specs=[
            pl.BlockSpec((1, rows, width), lambda p: (p, 0, 0)),
            pl.BlockSpec(bias.shape, lambda p: (0, 0)),
        ],
        out_specs=[
            pl.BlockSpec((rows, PAIR), lambda p: (0, p)),
            pl.BlockSpec((1, 8, rows), lambda p: (p, 0, 0)),
        ],
        out_shape=[
            jax.ShapeDtypeStruct((rows, pairs * PAIR), LOW),
            jax.ShapeDtypeStruct((pairs, 8, rows), WIDE),
        ],
        compiler_params=pltpu.CompilerParams(vmem_limit_bytes=48 * MIB),
    )(qkv, bias)


def attend_back_open(qkv_ref, context_ref, upper_ref, dots, key_turned, queries, uppers):
    lane = lax.broadcasted_iota(jnp.int32, (1, PAIR), 1)
    product = (upper_ref[...].astype(WIDE) * context_ref[...].astype(WIDE)).T
    for head in range(2):
        band = slice(head * HEAD_DIM, (head + 1) * HEAD_DIM)
        dots[head : head + 1, :] = jnp.sum(product[band, :], axis=0, keepdims=True)
        chosen = lane // HEAD_DIM == head
        queries[head] = qkv_ref[:, 0:PAIR] * jnp.where(chosen, HEAD_DIM ** (-0.5), 0.0).astype(LOW)
        uppers[head] = upper_ref[...] * jnp.where(chosen, 1.0, 0.0).astype(LOW)
    key_turned[...] = qkv_ref[:, PAIR : 2 * PAIR].astype(WIDE).T.astype(LOW)


def attend_back_tile(
    qkv_ref, bias_ref, total_ref, dots, key_turned, queries, uppers, query_sum, begin, size, step
):
    block = slice(begin, begin + size)
    first = pl.multiple_of(begin + step * TILE, TILE)
    key = qkv_ref[pl.ds(first, TILE), PAIR : 2 * PAIR]
    value = qkv_ref[pl.ds(first, TILE), 2 * PAIR : 3 * PAIR]
    key_sum = jnp.zeros((TILE, PAIR), WIDE)
    value_sum = jnp.zeros((TILE, PAIR), WIDE)
    scores = [dot_nt(key, queries[head, block, :]) for head in range(2)]
    weight_grads = [dot_nt(value, uppers[head, block, :]) for head in range(2)]
    for head in range(2):
        band = slice(head * HEAD_DIM, (head + 1) * HEAD_DIM)
        score = scores[head]
        if begin:
            inner = pl.multiple_of(step * TILE, TILE)
            score = score + bias_ref[pl.ds(inner, TILE), :]
        probability = jnp.exp(score - total_ref[head : head + 1, block])
        score_grads = probability * (weight_grads[head] - dots[head : head + 1, block])
        score_grads = score_grads.astype(LOW)
        value_sum = value_sum + dot_nn(probability.astype(LOW), uppers[head, block, :])
        key_sum = key_sum + dot_nn(score_grads, queries[head, block, :])
        query_sum[band, block] += dot_nn(key_turned[band, pl.ds(first, TILE)], score_grads)
    return pl.ds(first, TILE), key_sum, value_sum


def attend_back_kernel(
    qkv_ref, bias_ref, context_ref, grad_ref, total_ref, out_ref, dots, key_turned, queries, uppers, query_sum
):
    rows = qkv_ref.shape[1]
    qkv = qkv_ref.at[0]
    attend_back_open(qkv, context_ref, grad_ref, dots, key_turned, queries, uppers)
    for begin, size in ((0, LONGEST), (LONGEST, rows - LONGEST)):
        block = slice(begin, begin + size)
        query_sum[:, block] = jnp.zeros((PAIR, size), WIDE)

        @pl.loop(0, size // TILE)
        def _(step):
            at, key_sum, value_sum = attend_back_tile(
                qkv, bias_ref, total_ref.at[0], dots, key_turned, queries, uppers, query_sum, begin, size, step
            )
            out_ref[0, at, PAIR : 2 * PAIR] = key_sum.astype(LOW)
            out_ref[0, at, 2 * PAIR : 3 * PAIR] = value_sum.astype(LOW)

        out_ref[0, block, 0:PAIR] = (query_sum[:, block] * HEAD_DIM ** (-0.5)).T.astype(LOW)


def attend_back(qkv, bias, context, grad, totals):
    pairs, rows, width = qkv.shape
    return pl.pallas_call(
        attend_back_kernel,
        grid=(pairs,),
        in_specs=[
            pl.BlockSpec((1, rows, width), lambda p: (p, 0, 0)),
            pl.BlockSpec(bias.shape, lambda p: (0, 0)),
            pl.BlockSpec((rows, PAIR), lambda p: (0, p)),
            pl.BlockSpec((rows, PAIR), lambda p: (0, p)),
            pl.BlockSpec((1, 8, rows), lambda p: (p, 0, 0)),
        ],
        out_specs=pl.BlockSpec((1, rows, width), lambda p: (p, 0, 0)),
        out_shape=jax.ShapeDtypeStruct(qkv.shape, LOW),
        scratch_shapes=[
            pltpu.VMEM((8, rows), WIDE),
            pltpu.VMEM((PAIR, rows), LOW),
            pltpu.VMEM((2, rows, PAIR), LOW),
            pltpu.VMEM((2, rows, PAIR), LOW),
            pltpu.VMEM((PAIR, rows), WIDE),
        ],
        compiler_params=pltpu.CompilerParams(vmem_limit_bytes=48 * MIB),
    )(qkv, bias, context, grad, totals)


def place():
    me = lax.axis_index("dp")
    z, y, x = me // 4, (me // 2) % 2, me % 2
    return me, z, y, x


def line_slots(z, depth):
    slots = []
    for step in range(depth - 1):
        slots.append((z - 1 - step, z - 1 - step >= 0, 1))
        slots.append((z + 1 + step, z + 1 + step < depth, -1))
    return slots


def remote(source, target, send, receive, device):
    return pltpu.make_async_remote_copy(
        src_ref=source,
        dst_ref=target,
        send_sem=send,
        recv_sem=receive,
        device_id={"dp": device},
        device_id_type=MESH,
    )


def greet_line(me, z, y, x, depth, extra=()):
    barrier = pltpu.get_barrier_semaphore()
    for peer in (z * 4 + y * 2 + 1 - x, z * 4 + (1 - y) * 2 + x):
        pl.semaphore_signal(barrier, inc=1, device_id={"dp": peer}, device_id_type=MESH)

    @pl.when(z > 0)
    def _():
        pl.semaphore_signal(barrier, inc=1, device_id={"dp": me - 4}, device_id_type=MESH)

    @pl.when(z < depth - 1)
    def _():
        pl.semaphore_signal(barrier, inc=1, device_id={"dp": me + 4}, device_id_type=MESH)

    for peer in extra:
        pl.semaphore_signal(barrier, inc=1, device_id=peer, device_id_type=MESH)
    ends = jnp.where(z > 0, 1, 0) + jnp.where(z < depth - 1, 1, 0)
    pl.semaphore_wait(barrier, 2 + len(extra) + ends)


def other_core(source, target, send, receive):
    return pltpu.make_async_remote_copy(
        src_ref=source,
        dst_ref=target,
        send_sem=send,
        recv_sem=receive,
        device_id={"tensor": 1 - lax.axis_index("tensor")},
        device_id_type=MESH,
    )


class Gather:
    def __init__(self, depth, parts, whole, far, table, sems):
        self.whole, self.far = whole, far
        self.depth = depth
        self.me, self.z, self.y, self.x = place()
        self.x_peer = self.z * 4 + self.y * 2 + 1 - self.x
        self.y_peer = self.z * 4 + (1 - self.y) * 2 + self.x
        self.rows = whole.shape[1] // parts
        self.array = [array for array, *_ in table]
        self.a, self.b, self.ab, self.c, self.all = [], [], [], [], []
        for _, base, width, third in table:
            side = (width - third) // 2
            self.a.append((base, side))
            self.b.append((base + side, side))
            self.ab.append((base, 2 * side))
            self.c.append((base + 2 * side, third))
            self.all.append((base, width))
        (
            self.z_send, self.z_recv, self.zc_send, self.zc_recv, self.xa_send, self.xa_recv, self.yb_send, self.yb_recv,
            self.ya_send, self.ya_recv, self.xb_send, self.xb_recv, self.c_send, self.c_recv, self.far_send, self.far_recv,
        ) = sems
        self.slots = line_slots(self.z, depth)

    @staticmethod
    def semaphores(depth, pieces):
        sem = pltpu.SemaphoreType.DMA
        return [
            *[sem((pieces, depth + 1)), sem((pieces, depth))] * 2,
            *[sem((pieces,)), sem((pieces, depth))] * 2,
            *[sem((pieces,)), sem((pieces, depth, 2))] * 2,
            sem((pieces, 2)),
            sem((pieces, 2)),
            sem((pieces,)),
            sem((pieces,)),
        ]

    def block(self, zb, yb, xb):
        return zb * 4 + yb * 2 + xb

    def cut(self, ref, p, block, count, columns):
        first = pl.multiple_of(block * self.rows, self.rows)
        return ref.at[self.array[p], pl.ds(first, count * self.rows), pl.ds(*columns)]

    def copy(self, p, block, count, columns, send, receive, device):
        part = self.cut(self.whole, p, block, count, columns)
        return remote(part, part, send, receive, device)

    def forward(self, p, block, count, columns):
        if p == 0:
            return
        other_core(
            self.cut(self.whole, p, block, count, columns),
            self.cut(self.far, p, block, count, columns),
            self.far_send.at[p],
            self.far_recv.at[p],
        ).start()

    def far_copy(self, p):
        part = self.far.at[self.array[p], :, pl.ds(*self.all[p])]
        return other_core(part, part, self.far_send.at[p], self.far_recv.at[p])

    def z_copy(self, p, zb, way, back=False):
        block = self.block(zb, self.y, self.x)
        sem = self.depth if back else zb
        return self.copy(
            p, block, 1, self.ab[p], self.z_send.at[p, sem], self.z_recv.at[p, zb], self.me + 4 * way
        )

    def zc_copy(self, p, zb, way, back=False):
        sem = self.depth if back else zb
        return self.copy(
            p, zb * 4, 4, self.c[p], self.zc_send.at[p, sem], self.zc_recv.at[p, zb], self.me + 4 * way
        )

    def xa(self, p, zb, xb):
        block = self.block(zb, self.y, xb)
        return self.copy(
            p, block, 1, self.a[p], self.xa_send.at[p], self.xa_recv.at[p, zb], self.x_peer
        )

    def yb(self, p, zb, yb):
        block = self.block(zb, yb, self.x)
        return self.copy(
            p, block, 1, self.b[p], self.yb_send.at[p], self.yb_recv.at[p, zb], self.y_peer
        )

    def ya(self, p, zb, yb, xb):
        block = self.block(zb, yb, xb)
        return self.copy(
            p, block, 1, self.a[p], self.ya_send.at[p], self.ya_recv.at[p, zb, xb], self.y_peer
        )

    def xb(self, p, zb, yb, xb):
        block = self.block(zb, yb, xb)
        return self.copy(
            p, block, 1, self.b[p], self.xb_send.at[p], self.xb_recv.at[p, zb, yb], self.x_peer
        )

    def xc(self, p, xb):
        block = self.block(self.z, self.y, xb)
        return self.copy(
            p, block, 1, self.c[p], self.c_send.at[p, 0], self.c_recv.at[p, 0], self.x_peer
        )

    def yc(self, p, yb):
        block = self.block(self.z, yb, 0)
        return self.copy(
            p, block, 2, self.c[p], self.c_send.at[p, 1], self.c_recv.at[p, 1], self.y_peer
        )

    def both_ways(self, copy, act):
        @pl.when(self.z < self.depth - 1)
        def _():
            act(copy(self.z, 1))

        @pl.when(self.z > 0)
        def _():
            act(copy(self.z, -1, True))

    def spread(self, p, zb):
        self.xa(p, zb, self.x).start()
        self.yb(p, zb, self.y).start()
        self.ya(p, zb, self.y, self.x).start()
        self.xb(p, zb, self.y, self.x).start()

    def turn(self, p, zb):
        self.xa(p, zb, 1 - self.x).wait_recv()
        self.ya(p, zb, self.y, 1 - self.x).start()
        self.forward(p, self.block(zb, self.y, 1 - self.x), 1, self.a[p])
        self.yb(p, zb, 1 - self.y).wait_recv()
        self.xb(p, zb, 1 - self.y, self.x).start()
        self.forward(p, self.block(zb, 1 - self.y, self.x), 1, self.b[p])

    def at_step(self, step, act):
        for zb, valid, way in self.slots[2 * step : 2 * step + 2]:
            on = (self.z + way >= 0) & (self.z + way < self.depth)
            pl.when(valid)(functools.partial(act, zb, way, on))

    def arrive(self, p, step):
        def act(zb, way, on):
            self.z_copy(p, zb, way).wait_recv()
            pl.when(on)(lambda: self.z_copy(p, zb, way).start())
            self.spread(p, zb)
            self.forward(p, self.block(zb, self.y, self.x), 1, self.ab[p])

        self.at_step(step, act)

    def arrive_c(self, p, step):
        def act(zb, way, on):
            self.zc_copy(p, zb, way).wait_recv()
            pl.when(on)(lambda: self.zc_copy(p, zb, way).start())
            self.forward(p, zb * 4, 4, self.c[p])

        self.at_step(step, act)

    def stage(self, p, s):
        depth = self.depth
        if s == 0:
            self.both_ways(lambda *way: self.z_copy(p, *way), lambda copy: copy.start())
            self.xc(p, self.x).start()
            self.spread(p, self.z)
            self.forward(p, self.me, 1, self.all[p])
            return
        if s == 1:
            self.xc(p, 1 - self.x).wait_recv()
            self.yc(p, self.y).start()
            self.forward(p, self.block(self.z, self.y, 1 - self.x), 1, self.c[p])
        if s == 2:
            self.yc(p, 1 - self.y).wait_recv()
            self.both_ways(lambda *way: self.zc_copy(p, *way), lambda copy: copy.start())
            self.forward(p, self.block(self.z, 1 - self.y, 0), 2, self.c[p])
        if 1 <= s < depth:
            self.arrive(p, s - 1)
        if 3 <= s < depth + 2:
            self.arrive_c(p, s - 3)
        if s == 2:
            self.turn(p, self.z)
        if 3 <= s < depth + 2:
            self.at_step(s - 3, lambda zb, way, on: self.turn(p, zb))
        if s == depth + 2:
            for zb in range(depth):
                for other in range(2):
                    self.ya(p, zb, 1 - self.y, other).wait_recv()
                self.forward(p, self.block(zb, 1 - self.y, 0), 2, self.a[p])
                for other in range(2):
                    self.xb(p, zb, other, 1 - self.x).wait_recv()
                    self.forward(p, self.block(zb, other, 1 - self.x), 1, self.b[p])

    def finish(self, p):
        def sent(copy):
            copy.wait_send()

        if p:
            self.far_copy(p).wait_send()
        self.both_ways(lambda *way: self.z_copy(p, *way), sent)
        self.both_ways(lambda *way: self.zc_copy(p, *way), sent)
        for count, columns, sem in (
            (1, self.a[p], self.xa_send),
            (1, self.b[p], self.yb_send),
            (2, self.a[p], self.ya_send),
            (2, self.b[p], self.xb_send),
        ):
            part = self.cut(self.whole, p, 0, count * self.depth, columns)
            remote(part, part, sem.at[p], sem.at[p], self.me).wait_send()
        self.xc(p, self.x).wait_send()
        self.yc(p, self.y).wait_send()

        def passed(zb, way, on):
            pl.when(on)(lambda: sent(self.z_copy(p, zb, way)))
            pl.when(on)(lambda: sent(self.zc_copy(p, zb, way)))

        for step in range(self.depth - 1):
            self.at_step(step, passed)


def looped(count, body, between):
    @pl.loop(0, count)
    def _(i):
        body(i)
        for step, acts in between.items():

            @pl.when(i == step)
            def _():
                for act in acts:
                    act()


GATHER_AT = {
    "hidden": {0: [(2, 0), (1, 0)], 1: [(0, 1), (0, 2), (0, 3)], 3: [(0, 4)], 4: [(0, 5), (1, 1)]},
    "upstream": {-1: [(2, 1)], 1: [(3, 0)]},
    "project": {-1: [(4, 0), (0, 6)], 1: [(1, 2)], 5: [(2, 2)]},
    "long": {2: [(3, 1), (1, 3)], 7: [(2, 3)], 9: [(1, 4)], 14: [(2, 4)]},
    "short": {2: [(1, 5)], 3: [(3, 2)], 5: [(4, 1)]},
    "norm": {-1: [(1, 6)], 1: [(2, 5)], 3: [(3, 3)]},
    "feed": {-1: [(4, 2), (2, 6)], 0: [(3, 4)], 1: [(4, 3)], 2: [(3, 5)]},
    "last": {-1: [(3, 6), (4, 4)], 0: [(4, 5)]},
    "tail": {-1: [(4, 6)]},
}


def piece_table(width, inner):
    third = width // 8
    return (
        (0, 0, 3 * inner, third),
        (0, 3 * inner, inner, third),
        (1, 0, width, 2 * third),
        (2, 0, width // 2, third),
        (2, width // 2, width // 2, third),
    )


def chunk_columns(j, per_piece, half):
    array, at = 1 + j // per_piece, j % per_piece
    pair = per_piece // 2
    quarter = (at // pair) * per_piece * half + (at % pair) * half
    if isinstance(j, int):
        split = array > 1
        return array, quarter if split else at * half, (
            quarter + pair * half if split else (per_piece + at) * half
        )
    split = array > 1
    first = jnp.where(split, quarter, at * half)
    return array, first, first + jnp.where(split, pair, per_piece) * half


def front_kernel(
    depth, lengths_ref, dealing_ref, project_in, merge_in, expand_in, reduce_in, vectors_in, hidden_bias_in,
    tokens_ref, cotangent_ref,
    whole_out, far_ref, qkv_out, turned_out, upstream_out, context_out, total_out,
    acc_out, normal_out, inverse_out, low_turned_out, active_out, slope_out, far_context_out,
    project_ref, merge_ref, expand_ref, reduce_ref, vectors_ref, hidden_bias_ref,
    whole, score_bias, token, upper, hidden, turned, upstream, qkv, context, total,
    acc, normal, inverse, low, low_turned, active, slope, far_context, merge_far, expand_buf, reduce_buf,
    local_sem, core_sem, out_sem, load_sem, chunk_sem, weight_sem, *sems,
):
    arrays = whole.shape[0]
    half_rows, width = tokens_ref.shape
    rows = 2 * half_rows
    pairs = qkv.shape[0]
    inner = pairs * PAIR
    both = expand_buf.shape[2]
    half = both // 2
    hidden_half = expand_ref.shape[1]
    chunks = hidden_half // half
    per_piece = chunks // (arrays - 1)
    member = lax.axis_index("tensor")
    table = piece_table(whole.shape[2], inner)
    pieces = len(table)
    lines = Gather(depth, 4 * depth, whole, far_ref, table, sems)
    me = lines.me
    tall, short = 2 * TILE, TILE // 2

    weights = [
        pltpu.make_async_copy(source, target, weight_sem.at[i])
        for i, (source, target) in enumerate(
            (
                (project_in, project_ref),
                (merge_in, merge_ref),
                (expand_in, expand_ref),
                (reduce_in, reduce_ref),
                (vectors_in, vectors_ref),
                (hidden_bias_in, hidden_bias_ref),
            )
        )
    ]
    for copy in weights:
        copy.start()
    own = [
        pltpu.make_async_copy(tokens_ref, token.at[member], local_sem.at[0]),
        pltpu.make_async_copy(cotangent_ref, upper.at[member], local_sem.at[1]),
    ]
    for copy in own:
        copy.start()
    for copy in weights:
        copy.wait()
    mine = pl.ds(pl.multiple_of(me * lines.rows, lines.rows), lines.rows)
    for pair in range(pairs):
        for c in range(3):
            first = (3 * pair + c) * PAIR
            whole[0, mine, first : first + PAIR] = project_ref[
                c, :, pair * PAIR : (pair + 1) * PAIR
            ].astype(LOW)
    whole[0, mine, 3 * inner :] = merge_ref[...].astype(LOW)
    for j in range(chunks):
        array, first, second = chunk_columns(j, per_piece, half)
        columns = slice(j * half, (j + 1) * half)
        whole[array, mine, first : first + half] = expand_ref[:, columns].astype(LOW)
        whole[array, mine, second : second + half] = reduce_ref[:, columns].astype(LOW)
    greet_line(me, lines.z, lines.y, lines.x, depth, [{"tensor": 1 - member}])
    crossing = [
        other_core(tokens_ref, token.at[member], core_sem.at[0, 0], core_sem.at[0, 1]),
        other_core(cotangent_ref, upper.at[member], core_sem.at[1, 0], core_sem.at[1, 1]),
    ]
    lines.stage(0, 0)
    for copy in crossing:
        copy.start()
    group = Group(lengths_ref, dealing_ref)
    score_bias[...] = group.score_bias(rows - LONGEST)
    for copy in own:
        copy.wait()

    leaving = []

    def leave(source, target):
        copy = pltpu.make_async_copy(source, target, out_sem.at[len(leaving)])
        copy.start()
        leaving.append(copy)

    def before(name):
        for stage in GATHER_AT.get(name, {}).get(-1, ()):
            lines.stage(*stage)

    def phase(name, count, body):
        between = {
            step: [functools.partial(lines.stage, *stage) for stage in stages]
            for step, stages in GATHER_AT.get(name, {}).items()
            if step >= 0
        }
        looped(count, body, between)

    def places_of(first):
        return first + lax.broadcasted_iota(jnp.int32, (TILE, 1), 0)

    def picked(index, source):
        return picked_rows(index, source.at[0]) + picked_rows(index - half_rows, source.at[1])

    def tile(step, size=TILE):
        return pl.ds(pl.multiple_of(step * size, size), size)

    def hidden_tile(step):
        index = group.moved(places_of(step * TILE), group.first, group.own)
        rows_here = picked(index, token)
        hidden[tile(step), :] = rows_here.astype(LOW)
        turned[:, tile(step)] = rows_here.T.astype(LOW)

    def upstream_tile(step):
        places = places_of(member * half_rows + step * TILE)
        index = group.moved(places, group.first, group.dealt)
        upstream[tile(step), :] = picked(index, upper).astype(LOW)

    crossing[0].wait()
    before("hidden")
    phase("hidden", rows // TILE, hidden_tile)
    leave(turned, turned_out)
    crossing[1].wait()
    before("upstream")
    phase("upstream", half_rows // TILE, upstream_tile)
    leave(upstream, upstream_out)

    def project_tile(i):
        pair, step = i // (rows // tall), lax.rem(i, rows // tall)
        at = tile(step, tall)
        columns = pl.ds(pl.multiple_of(pair * 3 * PAIR, PAIR), 3 * PAIR)
        bias_columns = pl.ds(pl.multiple_of(member * inner + pair * PAIR, PAIR), PAIR)
        bias = jnp.concatenate(
            [
                vectors_ref[0:1, bias_columns],
                jnp.zeros((1, PAIR), WIDE),
                vectors_ref[1:2, bias_columns],
            ],
            axis=1,
        )
        qkv[pair, at, :] = (dot_nn(hidden[at, :], whole[0, :, columns]) + bias).astype(LOW)

    before("project")
    phase("project", pairs * rows // tall, project_tile)
    leave(qkv, qkv_out)

    def attend_step(begin, size):
        def step_of(i):
            pair, step = i // (size // TILE), lax.rem(i, size // TILE)
            columns = pl.ds(pl.multiple_of(pair * PAIR, PAIR), PAIR)
            attend_tile(qkv, pair, score_bias, begin, size, step, context, columns, total)

        return step_of

    before("long")
    phase("long", pairs * LONGEST // TILE, attend_step(0, LONGEST))
    before("short")
    phase("short", pairs * (rows - LONGEST) // TILE, attend_step(LONGEST, rows - LONGEST))
    leave(context, context_out)
    leave(total, total_out)

    own_first = member * half_rows
    other_rows = pl.ds(pl.multiple_of((1 - member) * half_rows, half_rows), half_rows)
    crossing = other_core(context.at[other_rows], far_context, core_sem.at[2, 0], core_sem.at[2, 1])
    crossing.start()
    before("norm")
    lines.far_copy(1).wait_recv()
    merge_columns = pl.ds(whole.shape[2] - inner, inner)
    merge_copy = pltpu.make_async_copy(
        far_ref.at[0, :, merge_columns], merge_far, local_sem.at[2]
    )
    merge_copy.start()
    merge_copy.wait()
    crossing.wait()
    leave(far_context, far_context_out)

    def norm_tile(step):
        at = tile(step, short)
        own_at = pl.ds(pl.multiple_of(own_first + step * short, short), short)
        branch = dot_nt(context[own_at, :], whole[0, :, merge_columns])
        branch = branch + dot_nt(far_context[at, :], merge_far[...])
        unit, scale = norm(hidden[own_at, :].astype(WIDE) + branch + vectors_ref[2:3, :])
        normed = unit * vectors_ref[3:4, :] + vectors_ref[4:5, :]
        normal[at, :] = unit
        inverse[at, :] = jnp.broadcast_to(scale, (short, 128))
        low[at, :] = normed.astype(LOW)
        low_turned[:, at] = normed.T.astype(LOW)
        acc[at, :] = normed + vectors_ref[5:6, :]

    leave(whole.at[0], whole_out.at[0])
    phase("norm", half_rows // short, norm_tile)
    leave(normal, normal_out)
    leave(inverse, inverse_out)
    leave(low_turned, low_turned_out)

    def loads(j):
        slot = lax.rem(j, 2)
        array, *firsts = chunk_columns(j, per_piece, half)
        copies = []
        for kind, buf in enumerate((expand_buf, reduce_buf)):
            first = pl.multiple_of(firsts[kind], half)
            for side, source in enumerate((far_ref, whole)):
                copies.append(
                    pltpu.make_async_copy(
                        source.at[array, :, pl.ds(first, half)],
                        buf.at[slot, :, pl.ds(side * half, half)],
                        load_sem.at[slot, kind, side],
                    )
                )
        return copies

    def results(j):
        slot = lax.rem(j, 2)
        return [
            pltpu.make_async_copy(active.at[slot], active_out.at[j], chunk_sem.at[slot, 0]),
            pltpu.make_async_copy(slope.at[slot], slope_out.at[j], chunk_sem.at[slot, 1]),
        ]

    def chunk_of(piece, first_chunk, count):
        def chunk(i):
            j = first_chunk + i
            slot = lax.rem(j, 2)

            @pl.when(i == 0)
            def _():
                lines.far_copy(piece).wait_recv()
                for copy in loads(j):
                    copy.start()

            for copy in loads(j):
                copy.wait()

            @pl.when(i + 1 < count)
            def _():
                for copy in loads(j + 1):
                    copy.start()

            @pl.when(j >= 2)
            def _():
                for copy in results(j - 2):
                    copy.wait()

            biases = []
            for which in (1 - member, member):
                first = pl.multiple_of(which * hidden_half + j * half, half)
                biases.append(hidden_bias_ref[:, pl.ds(first, half)])
            bias = jnp.concatenate(biases, axis=1)
            tiles = [slice(step * TILE, (step + 1) * TILE) for step in range(half_rows // TILE)]
            parts = [dot_nn(low[at, :], expand_buf[slot]) for at in tiles]
            for at, part in zip(tiles, parts, strict=True):
                value = part + bias
                below, bell = normal_cells(value)
                held = (value * below).astype(LOW)
                active[slot, at, :] = held
                slope[slot, at, :] = (below + value * bell * 0.3989422804014327).astype(LOW)
                acc[at, :] += dot_nt(held, reduce_buf[slot])
            for copy in results(j):
                copy.start()

        return chunk

    first_chunk = 0
    for piece, name in ((2, "feed"), (3, "last"), (4, "tail")):
        count = chunks * table[piece][2] // (2 * hidden_half)
        before(name)
        columns = pl.ds(*lines.all[piece])
        leave(
            whole.at[lines.array[piece], :, columns],
            whole_out.at[lines.array[piece], :, columns],
        )
        if name == "last":
            for p in range(piece):
                lines.finish(p)
        phase(name, count, chunk_of(piece, first_chunk, count))
        first_chunk += count
    leave(acc, acc_out)
    for p in range(pieces - 2, pieces):
        lines.finish(p)
    for j in (chunks - 2, chunks - 1):
        for copy in results(j):
            copy.wait()
    for copy in leaving:
        copy.wait()


def front(lengths, dealing, project, merge, expand, reduce, vectors, hidden_bias, tokens, cotangent, parts):
    shard_rows, hidden_half = expand.shape
    arrays, columns = 3, hidden_half
    half_rows, width = tokens.shape
    rows, pairs, depth = 2 * half_rows, project.shape[2] // PAIR, parts // 4
    inner, half = pairs * PAIR, 256
    pieces = len(piece_table(columns, inner))
    chunks, both = hidden_half // half, 2 * half
    shape, sem = jax.ShapeDtypeStruct, pltpu.SemaphoreType.DMA
    anywhere = pl.BlockSpec(memory_space=pl.ANY)
    held = [
        ((pairs, rows, 3 * PAIR), LOW),
        ((width, rows), LOW),
        ((half_rows, width), LOW),
        ((rows, inner), LOW),
        ((pairs, 8, rows), WIDE),
        ((half_rows, width), WIDE),
        ((half_rows, width), WIDE),
        ((half_rows, 128), WIDE),
        ((width, half_rows), LOW),
        ((chunks, half_rows, both), LOW),
        ((chunks, half_rows, both), LOW),
        ((half_rows, inner), LOW),
    ]
    return pl.pallas_call(
        functools.partial(front_kernel, depth),
        in_specs=[*[pl.BlockSpec(memory_space=pltpu.SMEM)] * 2, *[anywhere] * 8],
        out_specs=[anywhere] * 14,
        out_shape=[
            shape((arrays, parts * shard_rows, columns), LOW),
            shape((arrays, parts * shard_rows, columns), LOW),
            *[shape(*one) for one in held],
        ],
        scratch_shapes=[
            *[
                pltpu.VMEM(one.shape, WIDE)
                for one in (project, merge, expand, reduce, vectors, hidden_bias)
            ],
            pltpu.VMEM((arrays, parts * shard_rows, columns), LOW),
            pltpu.VMEM((rows - LONGEST, rows - LONGEST), WIDE),
            pltpu.VMEM((2, half_rows, width), LOW),
            pltpu.VMEM((2, half_rows, width), LOW),
            pltpu.VMEM((rows, width), LOW),
            pltpu.VMEM((width, rows), LOW),
            pltpu.VMEM((half_rows, width), LOW),
            pltpu.VMEM((pairs, rows, 3 * PAIR), LOW),
            pltpu.VMEM((rows, inner), LOW),
            pltpu.VMEM((pairs, 8, rows), WIDE),
            pltpu.VMEM((half_rows, width), WIDE),
            pltpu.VMEM((half_rows, width), WIDE),
            pltpu.VMEM((half_rows, 128), WIDE),
            pltpu.VMEM((half_rows, width), LOW),
            pltpu.VMEM((width, half_rows), LOW),
            pltpu.VMEM((2, half_rows, both), LOW),
            pltpu.VMEM((2, half_rows, both), LOW),
            pltpu.VMEM((half_rows, inner), LOW),
            pltpu.VMEM((width, inner), LOW),
            pltpu.VMEM((2, width, both), LOW),
            pltpu.VMEM((2, width, both), LOW),
            sem((3,)),
            sem((3, 2)),
            sem((16,)),
            sem((2, 2, 2)),
            sem((2, 2)),
            sem((6,)),
            *Gather.semaphores(depth, pieces),
        ],
        compiler_params=pltpu.CompilerParams(
            collective_id=0, has_side_effects=True, vmem_limit_bytes=63 * MIB
        ),
    )(lengths, dealing, project, merge, expand, reduce, vectors, hidden_bias, tokens, cotangent)


def normal_cells(value):
    bell = jnp.exp2(value * value * (-0.5 * 1.4426950408889634))
    below = 1.0 + 0.39 * 0.7071067811865476 * jnp.abs(value)
    t = pl.reciprocal(below, approx=True)
    t = t * (2.0 - below * t)
    t = t * (2.0 - below * t)
    tail = 0.5 * -0.2275377237624147
    for factor in (
        0.8866668177122106,
        -0.6354042576077721,
        0.649562611731642,
        0.0913871257655044,
        0.23532542445435511,
    ):
        tail = tail * t + 0.5 * factor
    tail = tail * t * bell
    return jnp.where(value < 0.0, tail, 1.0 - tail), bell


def norm(values):
    center = values - jnp.mean(values, axis=1, keepdims=True)
    spread = jnp.mean(center * center, axis=1, keepdims=True)
    scale = lax.rsqrt(spread + norm_epsilon)
    return center * scale, scale


def norm_back(scaled, unit, scale):
    return scale * (
        scaled
        - jnp.mean(scaled, axis=1, keepdims=True)
        - unit * jnp.mean(scaled * unit, axis=1, keepdims=True)
    )


def feed_kernel(
    context_ref, merge_ref, merge_far_ref, whole_ref, far_ref, hidden_ref, upstream_ref, vectors_ref, bias_ref,
    encoded_ref, branch_ref, grad_ref, merge_grad_ref, expand_grad_ref, reduce_grad_ref, sums_ref, hidden_sums_ref,
    own_ctx, far_ctx, acc, normal, inverse, low, turned, late, late_turned, active, slope, inner_grad,
    expand_buf, reduce_buf, arrived, leaving, kept, done, grad_own, grad_far, merge_send, merge_recv,
    ctx_sem, load_sem, send_sem, recv_sem, out_sem, last_sem,
):
    rows = hidden_ref.shape[0]
    chunks, _, both = bias_ref.shape
    half = both // 2
    per_piece = whole_ref.shape[2] // (2 * half)
    member = lax.axis_index("tensor")
    peer = {"tensor": 1 - member}
    tall, short = 256, 128
    width = hidden_ref.shape[1]

    def across(source, target, send, receive):
        return pltpu.make_async_remote_copy(
            src_ref=source,
            dst_ref=target,
            send_sem=send,
            recv_sem=receive,
            device_id=peer,
            device_id_type=MESH,
        )

    def rows_of(which):
        return pl.ds(pl.multiple_of(which * rows, rows), rows)

    def tile(step, size):
        return pl.ds(pl.multiple_of(step * size, size), size)

    def loads(j, slot):
        piece, at = 1 + j // per_piece, lax.rem(j, per_piece) * half
        copies = []
        for kind, buf in enumerate((expand_buf, reduce_buf)):
            first = pl.multiple_of(at + kind * per_piece * half, half)
            for side, source in enumerate((far_ref, whole_ref)):
                copies.append(
                    pltpu.make_async_copy(
                        source.at[piece, :, pl.ds(first, half)],
                        buf.at[slot, :, pl.ds(side * half, half)],
                        load_sem.at[slot, kind, side],
                    )
                )
        return copies

    for copy in loads(0, 0):
        copy.start()
    barrier = pltpu.get_barrier_semaphore()
    pl.semaphore_signal(barrier, inc=1, device_id=peer, device_id_type=MESH)
    pl.semaphore_wait(barrier, 1)
    out_ctx = across(context_ref.at[rows_of(1 - member)], far_ctx, ctx_sem.at[0], ctx_sem.at[1])
    out_ctx.start()
    in_ctx = pltpu.make_async_copy(context_ref.at[rows_of(member)], own_ctx, ctx_sem.at[2])
    in_ctx.start()
    sums_ref[...] = jnp.zeros_like(sums_ref)
    in_ctx.wait()
    out_ctx.wait()

    def add_sum(row, values):
        sums_ref[row : row + 1, :] += jnp.sum(values, axis=0, keepdims=True)

    @pl.loop(0, rows // short)
    def _(step):
        at = tile(step, short)
        branch = dot_nt(own_ctx[at, :], merge_ref[...]) + dot_nt(far_ctx[at, :], merge_far_ref[...])
        unit, scale = norm(hidden_ref[at, :].astype(WIDE) + branch + vectors_ref[2:3, :])
        normed = unit * vectors_ref[3:4, :] + vectors_ref[4:5, :]
        normal[at, :] = unit
        inverse[at, :] = jnp.broadcast_to(scale, (short, 128))
        low[at, :] = normed.astype(LOW)
        turned[:, at] = normed.T.astype(LOW)
        acc[at, :] = normed + vectors_ref[5:6, :]

    @pl.loop(0, chunks)
    def _(j):
        slot = lax.rem(j, 2)
        for copy in loads(j, slot):
            copy.wait()

        @pl.when(j + 1 < chunks)
        def _():
            for copy in loads(j + 1, 1 - slot):
                copy.start()

        for step in range(rows // tall):
            at = slice(step * tall, (step + 1) * tall)
            inner = dot_nn(low[at, :], expand_buf[slot]) + bias_ref[j]
            below, bell = normal_cells(inner)
            held = (inner * below).astype(LOW)
            active[j, at, :] = held
            slope[j, at, :] = (below + inner * bell * 0.3989422804014327).astype(LOW)
            acc[at, :] += dot_nt(held, reduce_buf[slot])

    for copy in loads(0, 0):
        copy.start()

    @pl.loop(0, rows // short)
    def _(step):
        at = tile(step, short)
        unit, scale = norm(acc[at, :])
        encoded_ref[at, :] = (unit * vectors_ref[6:7, :] + vectors_ref[7:8, :]).astype(LOW)
        upper = upstream_ref[at, :].astype(WIDE)
        add_sum(6, upper * unit)
        add_sum(7, upper)
        grad = norm_back(upper * vectors_ref[6:7, :], unit, scale)
        grad_low = grad.astype(LOW)
        add_sum(5, grad_low.astype(WIDE))
        acc[at, :] = grad
        late[at, :] = grad_low
        late_turned[:, at] = grad.T.astype(LOW)

    def send(j, kind):
        return across(
            leaving.at[lax.rem(j, 2), kind],
            arrived.at[lax.rem(j, 4), kind],
            send_sem.at[lax.rem(j, 2), kind],
            recv_sem.at[lax.rem(j, 4), kind],
        )

    def store(j, kind):
        target = (expand_grad_ref, reduce_grad_ref)[kind]
        cols = pl.ds(pl.multiple_of(j * half, half), half)
        return pltpu.make_async_copy(
            done.at[lax.rem(j, 2), kind], target.at[:, cols], out_sem.at[lax.rem(j, 2), kind]
        )

    def finish(j):
        for kind in range(2):
            send(j, kind).wait_recv()

            @pl.when(j >= 2)
            def _():
                store(j - 2, kind).wait()

            @pl.loop(0, width // tall)
            def _(step):
                at = tile(step, tall)
                done[lax.rem(j, 2), kind, at, :] = (
                    kept[lax.rem(j, 2), kind, at, :]
                    + arrived[lax.rem(j, 4), kind, at, :].astype(WIDE)
                ).astype(LOW)

            store(j, kind).start()

    @pl.loop(0, chunks)
    def _(j):
        slot = lax.rem(j, 2)
        for copy in loads(j, slot):
            copy.wait()

        @pl.when(j + 1 < chunks)
        def _():
            for copy in loads(j + 1, 1 - slot):
                copy.start()

        total = jnp.zeros((1, both), WIDE)
        for step in range(rows // tall):
            at = slice(step * tall, (step + 1) * tall)
            grad = dot_nn(late[at, :], reduce_buf[slot]) * slope[j, at, :].astype(WIDE)
            grad = grad.astype(LOW)
            inner_grad[at, :] = grad
            total = total + jnp.sum(grad.astype(WIDE), axis=0, keepdims=True)
            acc[at, :] += dot_nt(grad, expand_buf[slot])
        hidden_sums_ref[j] = total

        @pl.when(j >= 2)
        def _():
            for kind in range(2):
                send(j - 2, kind).wait_send()

        for kind, (left, right) in enumerate(((turned, inner_grad), (late_turned, active.at[j]))):
            for step in range(width // tall):
                at = slice(step * tall, (step + 1) * tall)
                part = dot_nn(left[at, :], right[...])
                leaving[slot, kind, at, :] = part[:, 0:half].astype(LOW)
                kept[slot, kind, at, :] = part[:, half:both]
            send(j, kind).start()

        @pl.when(j >= 1)
        def _():
            finish(j - 1)

    @pl.loop(0, rows // short)
    def _(step):
        at = tile(step, short)
        grad = acc[at, :]
        unit = normal[at, :]
        add_sum(3, grad * unit)
        add_sum(4, grad)
        branch_grad = norm_back(grad * vectors_ref[3:4, :], unit, inverse[at, 0:1])
        branch_low = branch_grad.astype(LOW)
        add_sum(2, branch_low.astype(WIDE))
        branch_ref[at, :] = branch_grad
        turned[:, at] = branch_grad.T.astype(LOW)
        grad_far[at, :] = dot_nn(branch_low, merge_far_ref[...]).astype(LOW)
        grad_own[at, :] = dot_nn(branch_low, merge_ref[...]).astype(LOW)

    out_grad = across(grad_far, grad_ref.at[rows_of(member)], ctx_sem.at[0], ctx_sem.at[1])
    out_grad.start()
    in_grad = pltpu.make_async_copy(grad_own, grad_ref.at[rows_of(member)], ctx_sem.at[2])
    in_grad.start()
    for step in range(width // tall):
        at = slice(step * tall, (step + 1) * tall)
        merge_send[at, :] = dot_nn(turned[at, :], far_ctx[...]).astype(LOW)
    out_merge = across(merge_send, merge_recv, last_sem.at[0], last_sem.at[1])
    out_merge.start()
    finish(chunks - 1)
    for kind in range(2):
        send(chunks - 2, kind).wait_send()
        send(chunks - 1, kind).wait_send()
        store(chunks - 2, kind).wait()
        store(chunks - 1, kind).wait()
    out_merge.wait()
    for step in range(width // tall):
        at = slice(step * tall, (step + 1) * tall)
        merge_grad_ref[at, :] = (
            dot_nn(turned[at, :], own_ctx[...]) + merge_recv[at, :].astype(WIDE)
        ).astype(LOW)
    out_grad.wait()
    in_grad.wait()


def feed_block(context, whole, far, hidden_own, upstream, vectors, bias_own, bias_far):
    total_rows, inner = context.shape
    rows, width = hidden_own.shape
    hidden = bias_own.shape[0]
    merge, merge_far = whole[0, :, -inner:], far[0, :, -inner:]
    half = 256
    chunks = hidden // half
    both = 2 * half
    bias = jnp.concatenate(
        [bias_far.reshape(chunks, 1, half), bias_own.reshape(chunks, 1, half)], axis=2
    )
    vmem, anywhere = pl.BlockSpec(memory_space=pltpu.VMEM), pl.BlockSpec(memory_space=pl.ANY)
    sem = pltpu.SemaphoreType.DMA
    shape = jax.ShapeDtypeStruct
    *results, hidden_sums = pl.pallas_call(
        feed_kernel,
        in_specs=[anywhere, vmem, vmem, *[anywhere] * 2, *[vmem] * 4],
        out_specs=[vmem, vmem, anywhere, vmem, anywhere, anywhere, vmem, vmem],
        out_shape=[
            shape((rows, width), LOW),
            shape((rows, width), WIDE),
            shape((total_rows, inner), LOW),
            shape((width, inner), LOW),
            shape((width, hidden), LOW),
            shape((width, hidden), LOW),
            shape((8, width), WIDE),
            shape((chunks, 1, both), WIDE),
        ],
        scratch_shapes=[
            pltpu.VMEM((rows, inner), LOW),
            pltpu.VMEM((rows, inner), LOW),
            pltpu.VMEM((rows, width), WIDE),
            pltpu.VMEM((rows, width), WIDE),
            pltpu.VMEM((rows, 128), WIDE),
            pltpu.VMEM((rows, width), LOW),
            pltpu.VMEM((width, rows), LOW),
            pltpu.VMEM((rows, width), LOW),
            pltpu.VMEM((width, rows), LOW),
            pltpu.VMEM((chunks, rows, both), LOW),
            pltpu.VMEM((chunks, rows, both), LOW),
            pltpu.VMEM((rows, both), LOW),
            pltpu.VMEM((2, width, both), LOW),
            pltpu.VMEM((2, width, both), LOW),
            pltpu.VMEM((4, 2, width, half), LOW),
            pltpu.VMEM((2, 2, width, half), LOW),
            pltpu.VMEM((2, 2, width, half), WIDE),
            pltpu.VMEM((2, 2, width, half), LOW),
            pltpu.VMEM((rows, inner), LOW),
            pltpu.VMEM((rows, inner), LOW),
            pltpu.VMEM((width, inner), LOW),
            pltpu.VMEM((width, inner), LOW),
            sem((3,)),
            sem((2, 2, 2)),
            sem((2, 2)),
            sem((4, 2)),
            sem((2, 2)),
            sem((2,)),
        ],
        compiler_params=pltpu.CompilerParams(
            collective_id=2, has_side_effects=True, vmem_limit_bytes=60 * MIB
        ),
        cost_estimate=pl.CostEstimate(
            flops=12 * rows * width * 2 * hidden, bytes_accessed=8 * width * hidden * 4, transcendentals=0
        ),
    )(context, merge, merge_far, whole, far, hidden_own, upstream, vectors, bias)
    hidden_far = hidden_sums[:, 0, :half].reshape(-1)
    hidden_near = hidden_sums[:, 0, half:].reshape(-1)
    return (*results, hidden_near, hidden_far)


class Scatter:
    buffers = 8

    def __init__(self, depth, grads, shards, targets, buffers, sems):
        self.depth, self.grads, self.shards, self.targets = depth, grads, shards, targets
        self.held = [buffers[8 * p : 8 * p + 8] for p in range(len(grads))]
        self.me, self.z, self.y, self.x = place()
        self.x_peer = self.z * 4 + self.y * 2 + 1 - self.x
        self.y_peer = self.z * 4 + (1 - self.y) * 2 + self.x
        self.rows = grads[0].shape[0] // (4 * depth)
        (
            self.a1_send, self.a1_recv, self.a2_send, self.a2_recv, self.b2_send, self.b2_recv, self.b1_send, self.b1_recv,
            self.z_send, self.z_recv, self.zc_send, self.zc_recv, self.c_send, self.c_recv, self.out_sem,
        ) = sems

    @staticmethod
    def scratch(depth, rows, classes):
        found = []
        for a, b, c in classes:
            found += [
                pltpu.VMEM((depth, 2 * rows, a), LOW),
                pltpu.VMEM((depth, 2, rows, b), LOW),
                pltpu.VMEM((depth, rows, a), LOW),
                pltpu.VMEM((depth, rows, b), LOW),
                pltpu.VMEM((depth + 1, rows, a + b), LOW),
                pltpu.VMEM((depth + 1, 4 * rows, c), LOW),
                pltpu.VMEM((2 * rows, c), LOW),
                pltpu.VMEM((rows, c), LOW),
            ]
        return found

    @staticmethod
    def semaphores(depth, pieces):
        sem = pltpu.SemaphoreType.DMA
        return [
            *[sem((pieces,)), sem((pieces, depth))] * 3,
            sem((pieces,)),
            sem((pieces, depth, 2)),
            *[sem((pieces,)), sem((pieces, depth + 1))] * 2,
            sem((pieces, 2)),
            sem((pieces, 2)),
            sem((pieces,)),
        ]

    def done(self, p):
        return pltpu.make_async_copy(self.shards[p], self.targets[p], self.out_sem.at[p])

    def columns(self, p):
        a, b, c = (self.held[p][i].shape[-1] for i in (0, 1, 5))
        return pl.ds(0, a), pl.ds(a, b), pl.ds(a + b, c)

    def block(self, zb, yb, xb):
        return zb * 4 + yb * 2 + xb

    def span(self, block, count=1):
        return pl.ds(pl.multiple_of(block * self.rows, self.rows), count * self.rows)

    def add(self, put, count, *terms):
        chunk = min(count, 64)

        @pl.loop(0, count // chunk)
        def _(step):
            at = pl.multiple_of(step * chunk, chunk)
            parts = [term(at, chunk) for term in terms]
            if len(parts) > 2 or put.wide:
                parts = [part.astype(WIDE) for part in parts]
            total = parts[0]
            for part in parts[1:]:
                total = total + part
            put(at, chunk, total)

    def a1(self, p, zb):
        return remote(
            self.grads[p].at[self.span(self.block(zb, 1 - self.y, 0), 2), self.columns(p)[0]],
            self.held[p][0].at[zb],
            self.a1_send.at[p],
            self.a1_recv.at[p, zb],
            self.y_peer,
        )

    def b1(self, p, zb, yb):
        return remote(
            self.grads[p].at[self.span(self.block(zb, yb, 1 - self.x)), self.columns(p)[1]],
            self.held[p][1].at[zb, yb],
            self.b1_send.at[p],
            self.b1_recv.at[p, zb, yb],
            self.x_peer,
        )

    def a2(self, p, zb):
        return remote(
            self.held[p][0].at[zb, self.span(1 - self.x)],
            self.held[p][2].at[zb],
            self.a2_send.at[p],
            self.a2_recv.at[p, zb],
            self.x_peer,
        )

    def b2(self, p, zb):
        return remote(
            self.held[p][1].at[zb, 1 - self.y],
            self.held[p][3].at[zb],
            self.b2_send.at[p],
            self.b2_recv.at[p, zb],
            self.y_peer,
        )

    def slot(self, zb, way):
        return zb if way > 0 else zb + (self.depth - zb) * jnp.where(zb == self.z - 1, 1, 0)

    def z_copy(self, p, zb, way):
        slot = self.slot(zb, way)
        return remote(
            self.held[p][4].at[zb],
            self.held[p][4].at[slot],
            self.z_send.at[p],
            self.z_recv.at[p, slot],
            self.me + 4 * way,
        )

    def zc_copy(self, p, zb, way, first):
        slot = self.slot(zb, way)
        source = self.held[p][5].at[zb]
        if first:
            source = self.grads[p].at[self.span(zb * 4, 4), self.columns(p)[2]]
        return remote(
            source,
            self.held[p][5].at[slot],
            self.zc_send.at[p],
            self.zc_recv.at[p, slot],
            self.me + 4 * way,
        )

    def arrived(self, ref, sem, slot):
        part = ref.at[slot]
        remote(part, part, sem, sem, self.me).wait_recv()

    def cy(self, p):
        return remote(
            self.held[p][5].at[self.z, self.span(2 * (1 - self.y), 2)],
            self.held[p][6],
            self.c_send.at[p, 0],
            self.c_recv.at[p, 0],
            self.y_peer,
        )

    def cx(self, p):
        return remote(
            self.held[p][5].at[self.z, self.span(2 * self.y + 1 - self.x)],
            self.held[p][7],
            self.c_send.at[p, 1],
            self.c_recv.at[p, 1],
            self.x_peer,
        )

    def grad(self, p, block, columns):
        def term(at, count):
            first = pl.multiple_of(block * self.rows + at, 16)
            return self.grads[p][pl.ds(first, count), columns]

        return term

    def part(self, ref, lead, block, columns=None):
        columns = slice(None) if columns is None else columns

        def term(at, count):
            first = pl.multiple_of(block * self.rows + at, 16)
            return ref[(*lead, pl.ds(first, count), columns)]

        return term

    def put(self, ref, lead, block, columns=None):
        columns = slice(None) if columns is None else columns

        def act(at, count, total):
            first = pl.multiple_of(block * self.rows + at, 16)
            ref[(*lead, pl.ds(first, count), columns)] = total.astype(ref.dtype)

        act.wide = ref.dtype == WIDE
        return act

    def open(self, p, zb):
        self.a1(p, zb).start()
        self.b1(p, zb, 0).start()
        self.b1(p, zb, 1).start()

    def first(self, p, zb):
        z, y, x = self.z, self.y, self.x
        a, b, _ = self.columns(p)
        r1a, r1b = self.held[p][0], self.held[p][1]
        self.a1(p, zb).wait_recv()
        self.add(
            self.put(r1a, (zb,), 1 - x),
            self.rows,
            self.part(r1a, (zb,), 1 - x),
            self.grad(p, self.block(zb, y, 1 - x), a),
        )
        self.a2(p, zb).start()
        self.b1(p, zb, 0).wait_recv()
        self.b1(p, zb, 1).wait_recv()
        self.add(
            self.put(r1b, (zb, 1 - y), 0),
            self.rows,
            self.part(r1b, (zb, 1 - y), 0),
            self.grad(p, self.block(zb, 1 - y, x), b),
        )
        self.b2(p, zb).start()

    def terms(self, p, zb):
        z, y, x = self.z, self.y, self.x
        a, b, _ = self.columns(p)
        r1a, r1b, r2a, r2b = self.held[p][:4]
        own = self.block(zb, y, x)
        return (
            [self.grad(p, own, a), self.part(r1a, (zb,), x), self.part(r2a, (zb,), 0)],
            [self.grad(p, own, b), self.part(r1b, (zb, y), 0), self.part(r2b, (zb,), 0)],
        )

    def pass_on(self, p, zb, way):
        a, b, _ = self.columns(p)
        rz = self.held[p][4]
        self.a2(p, zb).wait_recv()
        self.b2(p, zb).wait_recv()
        from_line = (self.z - way >= 0) & (self.z - way < self.depth)

        @pl.when(from_line)
        def _():
            self.arrived(rz, self.z_recv.at[p, zb], zb)
            for terms, columns in zip(self.terms(p, zb), (a, b), strict=True):
                self.add(
                    self.put(rz, (zb,), 0, columns),
                    self.rows,
                    *terms,
                    self.part(rz, (zb,), 0, columns),
                )

        @pl.when(jnp.logical_not(from_line))
        def _():
            for terms, columns in zip(self.terms(p, zb), (a, b), strict=True):
                self.add(self.put(rz, (zb,), 0, columns), self.rows, *terms)

        self.z_copy(p, zb, way).start()

    def pass_c(self, p, zb, way):
        c = self.columns(p)[2]
        rc = self.held[p][5]
        from_line = (self.z - way >= 0) & (self.z - way < self.depth)

        @pl.when(from_line)
        def _():
            self.arrived(rc, self.zc_recv.at[p, zb], zb)
            self.add(
                self.put(rc, (zb,), 0),
                4 * self.rows,
                self.part(rc, (zb,), 0),
                self.grad(p, zb * 4, c),
            )
            self.zc_copy(p, zb, way, False).start()

        @pl.when(jnp.logical_not(from_line))
        def _():
            self.zc_copy(p, zb, way, True).start()

    def own_c(self, p):
        z, depth = self.z, self.depth
        c = self.columns(p)[2]
        rc = self.held[p][5]
        grad = self.grad(p, z * 4, c)
        lower, upper = self.part(rc, (z,), 0), self.part(rc, (depth,), 0)
        put = self.put(rc, (z,), 0)

        @pl.when(z > 0)
        def _():
            self.arrived(rc, self.zc_recv.at[p, z], z)

        @pl.when(z < depth - 1)
        def _():
            self.arrived(rc, self.zc_recv.at[p, depth], depth)

        @pl.when((z > 0) & (z < depth - 1))
        def _():
            self.add(put, 4 * self.rows, grad, lower, upper)

        @pl.when(z == 0)
        def _():
            self.add(put, 4 * self.rows, grad, upper)

        @pl.when(z == depth - 1)
        def _():
            self.add(put, 4 * self.rows, grad, lower)

        self.cy(p).start()

    def turn_c(self, p):
        rc, rcy = self.held[p][5], self.held[p][6]
        self.cy(p).wait_recv()
        self.add(
            self.put(rc, (self.z,), 2 * self.y),
            2 * self.rows,
            self.part(rc, (self.z,), 2 * self.y),
            self.part(rcy, (), 0),
        )
        self.cx(p).start()

    def close(self, p):
        z, depth = self.z, self.depth
        a, b, c = self.columns(p)
        rz, rc, rcx = self.held[p][4], self.held[p][5], self.held[p][7]
        self.a2(p, z).wait_recv()
        self.b2(p, z).wait_recv()

        @pl.when(z > 0)
        def _():
            self.arrived(rz, self.z_recv.at[p, z], z)

        @pl.when(z < depth - 1)
        def _():
            self.arrived(rz, self.z_recv.at[p, depth], depth)

        def total(*slots):
            for terms, columns in zip(self.terms(p, z), (a, b), strict=True):
                lines = [self.part(rz, (slot,), 0, columns) for slot in slots]
                self.add(self.put(self.shards[p], (), 0, columns), self.rows, *terms, *lines)

        pl.when((z > 0) & (z < depth - 1))(lambda: total(z, depth))
        pl.when(z == 0)(lambda: total(depth))
        pl.when(z == depth - 1)(lambda: total(z))
        self.cx(p).wait_recv()
        self.add(
            self.put(self.shards[p], (), 0, c),
            self.rows,
            self.part(rc, (z,), 2 * self.y + self.x),
            self.part(rcx, (), 0),
        )
        self.done(p).start()

    def at_step(self, step, act):
        z, depth = self.z, self.depth
        if step < 0:
            act(z, 0)
            return
        for zb, valid, way in (
            (z + 1 + step, z + 1 + step < depth, 1),
            (z - 1 - step, z - 1 - step >= 0, -1),
        ):
            pl.when(valid)(functools.partial(act, zb, way))

    def stage(self, p, s):
        last = self.depth - 2

        def opened(step):
            self.at_step(step, lambda zb, way: self.open(p, zb))

        def added(step):
            self.at_step(step, lambda zb, way: self.first(p, zb))

        def passed(step):
            self.at_step(step, lambda zb, way: self.pass_on(p, zb, way))

        def passed_c(step):
            self.at_step(step, lambda zb, way: self.pass_c(p, zb, way))

        if s == 0:
            opened(last)
            opened(last - 1)
            passed_c(last)
            return
        if s <= last + 2:
            added(last + 1 - s)
        if last - 1 - s >= -1:
            opened(last - 1 - s)
        if last - s >= 0:
            passed_c(last - s)
        if s >= 2 and last + 2 - s >= 0:
            passed(last + 2 - s)
        if s == last + 1:
            self.own_c(p)
        if s == last + 2:
            self.turn_c(p)
        if s == last + 3:
            self.close(p)

    def sent(self, p):
        passed = pl.ds(0, self.depth - 1)
        for part, sem in (
            (self.held[p][0], self.a1_send),
            (self.held[p][1], self.b1_send),
            (self.held[p][2], self.a2_send),
            (self.held[p][3], self.b2_send),
            (self.held[p][4].at[passed], self.z_send),
            (self.held[p][5].at[passed], self.zc_send),
        ):
            remote(part, part, sem.at[p], sem.at[p], self.me).wait_send()
        self.cy(p).wait_send()
        self.cx(p).wait_send()
        self.done(p).wait()


class SmallSum:
    def __init__(self, lines, buffer, send, recv):
        member = lax.axis_index("tensor")
        self.partners = [{"tensor": 1 - member}, {"dp": lines.x_peer}, {"dp": lines.y_peer}]
        for level in range(lines.depth.bit_length() - 1):
            reach = 1 << level
            way = 1 - 2 * ((lines.z // reach) % 2)
            self.partners.append({"dp": lines.me + 4 * reach * way})
        self.buffer, self.send, self.recv = buffer, send, recv

    def copy(self, step):
        return pltpu.make_async_remote_copy(
            src_ref=self.buffer.at[step],
            dst_ref=self.buffer.at[len(self.partners) + 1 + step],
            send_sem=self.send.at[step],
            recv_sem=self.recv.at[step],
            device_id=self.partners[step],
            device_id_type=MESH,
        )

    def step(self, step):
        if step:
            self.copy(step - 1).wait_recv()
            self.buffer[step] = self.buffer[step - 1] + self.buffer[len(self.partners) + step]
        if step < len(self.partners):
            self.copy(step).start()

    def sent(self):
        for step in range(len(self.partners)):
            self.copy(step).wait_send()


def adamw_update(master, moment, square, gradient, step_rate, decay_rate):
    moment_new = beta_one * moment + (1.0 - beta_one) * gradient
    square_new = beta_two * square + (1.0 - beta_two) * gradient * gradient
    moment_hat = moment_new * (1.0 / (1.0 - beta_one**STEP))
    square_hat = square_new * (1.0 / (1.0 - beta_two**STEP))
    master_new = master - step_rate * (
        moment_hat / (jnp.sqrt(square_hat) + adam_epsilon) + decay_rate * master
    )
    return (moment_new, square_new, master_new)


SCATTER_AT = {
    "reduce": {5: [(0, 0)]},
    "expand": {0: [(0, 1)], 1: [(1, 0)], 5: [(2, 0)], 6: [(0, 2)]},
    "norm": {0: [(1, 1)], 3: [(2, 1)], 4: [(3, 0)]},
    "merge": {1: [(1, 2)]},
    "attend": {1: [(3, 1)], 3: [(0, 3)], 6: [(2, 2)], 7: [(3, 2)], 11: [(2, 3)], 13: [(2, 4)], 14: [(4, 1)], 18: [(3, 4)], 21: [(4, 2)]},
    "project": {0: [(4, 0), (3, 3), (1, 3)], 1: [(5, 0)]},
    "terms": {0: [(4, 3)], 1: [(5, 1)], 2: [(3, 5)], 4: [(0, 4)]},
    "far": {-1: [(5, 2)], 0: [(4, 4)]},
    "near": {0: [(5, 3), (1, 4)]},
    "encoded": {0: [(5, 4), (4, 5)]},
    "end": [(0, 5), (2, 5), (1, 5), (5, 5)],
}


def back_kernel(
    depth, lengths_ref, dealing_ref, vectors_ref,
    whole_ref, far_ref, qkv_in, hidden_turned_in, upstream_in, context_in, totals_in,
    acc_in, normal_in, inverse_in, turned_in, active_in, slope_in, far_ctx_in, *rest,
):
    encoded_out, input_out, small_out, *rest = rest
    targets, rest = rest[:6], rest[6:]
    enc_pair, grad_ref, input_far, acc, arrived, merge_recv, small, score_bias, *rest = rest
    chunk_grads, *rest = rest
    grads, rest = [*[chunk_grads.at[p] for p in range(4)], *rest[:2]], rest[2:]
    shards, rest = rest[:6], rest[6:]
    buffers, rest = rest[: 6 * Scatter.buffers], rest[6 * Scatter.buffers :]
    small_send, small_recv, in_sem, load_sem, ctx_sem, far_send, far_recv, merge_sem, enc_sem, input_sem, *sems = rest
    lines = Scatter(depth, grads, shards, targets, buffers, sems)
    sums = SmallSum(lines, small, small_send, small_recv)
    group = Group(lengths_ref, dealing_ref)
    member = lax.axis_index("tensor")
    rows, width = acc.shape
    total_rows = 2 * rows
    chunks, _, both = active_in.shape
    half = both // 2
    per_piece = chunks // 2
    piece_span = grads[0].shape[1]
    pairs = qkv_in.shape[0]
    inner = pairs * PAIR
    tall, short = 256, 128

    def rows_of(which):
        return pl.ds(pl.multiple_of(which * rows, rows), rows)

    def tile(step, size):
        return pl.ds(pl.multiple_of(step * size, size), size)

    def fetch(source, target, sem):
        return pltpu.make_async_copy(source, target, in_sem.at[sem])

    def phase(name, count, body):
        between = {
            step: [functools.partial(lines.stage, *stage) for stage in stages]
            for step, stages in SCATTER_AT.get(name, {}).items()
        }
        for act in between.pop(-1, ()):
            act()
        looped(count, body, between)

    def places_of(first):
        return first + lax.broadcasted_iota(jnp.int32, (tall, 1), 0)

    def add_sum(row, values):
        small[0, row : row + 1, :] += jnp.sum(values, axis=0, keepdims=True)

    def feed_phase(later, late, late_turned, turned, upstream, active, slope, inner_grad, expand_buf, reduce_buf, leaving):
        def active_load(j):
            slot = lax.rem(j, 2)
            return [pltpu.make_async_copy(active_in.at[j], active.at[slot], load_sem.at[slot, 4])]

        def loads(j):
            slot = lax.rem(j, 2)
            array, *firsts = chunk_columns(j, per_piece, half)
            copies = [pltpu.make_async_copy(slope_in.at[j], slope.at[slot], load_sem.at[slot, 5])]
            for kind, buf in enumerate((expand_buf, reduce_buf)):
                first = pl.multiple_of(firsts[kind], half)
                for side, source in enumerate((far_ref, whole_ref)):
                    copies.append(
                        pltpu.make_async_copy(
                            source.at[array, :, pl.ds(first, half)],
                            buf.at[slot, :, pl.ds(side * half, half)],
                            load_sem.at[slot, 2 * kind + side],
                        )
                    )
            return copies

        def taken(j, load):
            for copy in load(j):
                copy.wait()

            @pl.when(j + 1 < chunks)
            def _():
                for copy in load(j + 1):
                    copy.start()

        acc_copy = fetch(acc_in, acc, 0)
        acc_copy.start()
        fetches = [fetch(upstream_in, upstream, 1), fetch(turned_in, turned, 2)]
        for copy in fetches:
            copy.start()
        for copy in [*active_load(0), *loads(0)]:
            copy.start()
        greet_line(
            lines.me, lines.z, lines.y, lines.x, depth, [sums.partners[0], *sums.partners[3:]]
        )
        for copy in later:
            copy.start()
        small[0] = jnp.zeros(small.shape[1:], WIDE)
        score_bias[...] = group.score_bias(total_rows - LONGEST)
        acc_copy.wait()
        for copy in fetches:
            copy.wait()

        def late_tile(step):
            at = tile(step, short)
            unit, scale = norm(acc[at, :])
            upper = upstream[at, :].astype(WIDE)
            upstream[at, :] = (unit * vectors_ref[6:7, :] + vectors_ref[7:8, :]).astype(LOW)
            add_sum(6, upper * unit)
            add_sum(7, upper)
            grad = norm_back(upper * vectors_ref[6:7, :], unit, scale)
            grad_low = grad.astype(LOW)
            add_sum(5, grad_low.astype(WIDE))
            acc[at, :] = grad
            late[at, :] = grad_low
            late_turned[:, at] = grad.T.astype(LOW)

        looped(rows // short, late_tile, {})
        enc_near = pltpu.make_async_copy(upstream, enc_pair.at[member], enc_sem.at[2])
        enc_far = other_core(upstream, enc_pair.at[member], enc_sem.at[0], enc_sem.at[1])
        enc_near.start()
        enc_far.start()

        def send(k):
            slot = lax.rem(k, 2)
            return other_core(
                leaving.at[slot], arrived.at[slot], far_send.at[slot], far_recv.at[slot]
            )

        def own_columns(k):
            return pl.ds(pl.multiple_of(lax.rem(k, per_piece) * half, half), half)

        def finish(k):
            piece, slot = k // per_piece, lax.rem(k, 2)
            send(k).wait_recv()

            @pl.loop(0, width // tall)
            def _(step):
                at = tile(step, tall)
                chunk_grads[piece, at, own_columns(k)] += arrived[slot, at, :]

        def products(k, left, right):
            piece, slot = k // per_piece, lax.rem(k, 2)

            @pl.when(k >= 2)
            def _():
                send(k - 2).wait_send()

            parts = [
                dot_nn(left[step * tall : (step + 1) * tall, :], right[...])
                for step in range(width // tall)
            ]
            for step, part in enumerate(parts):
                at = slice(step * tall, (step + 1) * tall)
                leaving[slot, at, :] = part[:, 0:half].astype(LOW)
                chunk_grads[piece, at, own_columns(k)] = part[:, half:both].astype(LOW)

            @pl.when(k >= 1)
            def _():
                finish(k - 1)

            send(k).start()

        def reduce_chunk(j):
            taken(j, active_load)
            products(j, late_turned, active.at[lax.rem(j, 2)])

        def expand_chunk(j):
            slot = lax.rem(j, 2)
            taken(j, loads)
            total = jnp.zeros((1, both), WIDE)
            tiles = [slice(step * tall, (step + 1) * tall) for step in range(rows // tall)]
            parts = [dot_nn(late[at, :], reduce_buf[slot]) for at in tiles]
            for at, part in zip(tiles, parts, strict=True):
                grad = (part * slope[slot, at, :].astype(WIDE)).astype(LOW)
                inner_grad[at, :] = grad
                total = total + jnp.sum(grad.astype(WIDE), axis=0, keepdims=True)
                acc[at, :] += dot_nt(grad, expand_buf[slot])
            for which, side in ((1 - member, 0), (member, half)):
                row = 8 + which * 2 + j // per_piece
                small[0, pl.ds(row, 1), own_columns(j)] = total[:, side : side + half]
            products(chunks + j, turned, inner_grad)

        phase("reduce", chunks, reduce_chunk)
        phase("expand", chunks, expand_chunk)
        finish(2 * chunks - 1)
        for k in (2 * chunks - 2, 2 * chunks - 1):
            send(k).wait_send()
        enc_near.wait()
        enc_far.wait()

    def merge_phase(normal, inverse, near_ctx, far_ctx, merge, merge_far, fetches, turned, grad_own, grad_far, merge_send):
        for copy in fetches:
            copy.wait()

        def norm_tile(step):
            at = tile(step, short)
            grad = acc[at, :]
            unit = normal[at, :]
            add_sum(3, grad * unit)
            add_sum(4, grad)
            branch_grad = norm_back(grad * vectors_ref[3:4, :], unit, inverse[at, 0:1])
            branch_low = branch_grad.astype(LOW)
            add_sum(2, branch_low.astype(WIDE))
            acc[at, :] = branch_grad
            turned[:, at] = branch_grad.T.astype(LOW)
            grad_far[at, :] = dot_nn(branch_low, merge_far[...]).astype(LOW)
            grad_own[at, :] = dot_nn(branch_low, merge[...]).astype(LOW)

        phase("norm", rows // short, norm_tile)
        out_grad = other_core(grad_far, grad_ref.at[rows_of(member)], ctx_sem.at[0], ctx_sem.at[1])
        in_grad = pltpu.make_async_copy(grad_own, grad_ref.at[rows_of(member)], ctx_sem.at[2])
        out_grad.start()
        in_grad.start()
        out_merge = other_core(merge_send, merge_recv, merge_sem.at[0], merge_sem.at[1])

        def merge_step(which):
            @pl.when(which == 0)
            def _():
                for step in range(width // tall):
                    at = slice(step * tall, (step + 1) * tall)
                    merge_send[at, :] = dot_nn(turned[at, :], far_ctx[...]).astype(LOW)
                out_merge.start()

            @pl.when(which == 1)
            def _():
                out_merge.wait()
                for step in range(width // tall):
                    at = slice(step * tall, (step + 1) * tall)
                    grads[4][at, 0:inner] = (
                        dot_nn(turned[at, :], near_ctx[...]) + merge_recv[at, :].astype(WIDE)
                    ).astype(LOW)

        phase("merge", 2, merge_step)
        out_grad.wait()
        in_grad.wait()

    def early_phase(normal, inverse, near_ctx, far_ctx, merge, merge_far):
        merge_columns = pl.ds(whole_ref.shape[2] - inner, inner)
        fetches = [
            fetch(normal_in, normal, 3),
            fetch(inverse_in, inverse, 4),
            fetch(context_in.at[rows_of(member)], near_ctx, 5),
            fetch(far_ctx_in, far_ctx, 6),
            fetch(whole_ref.at[0, :, merge_columns], merge, 7),
            fetch(far_ref.at[0, :, merge_columns], merge_far, 8),
        ]
        pl.run_scoped(
            functools.partial(feed_phase, fetches),
            pltpu.VMEM((rows, width), LOW),
            pltpu.VMEM((width, rows), LOW),
            pltpu.VMEM((width, rows), LOW),
            pltpu.VMEM((rows, width), LOW),
            pltpu.VMEM((2, rows, both), LOW),
            pltpu.VMEM((2, rows, both), LOW),
            pltpu.VMEM((rows, both), LOW),
            pltpu.VMEM((2, width, both), LOW),
            pltpu.VMEM((2, width, both), LOW),
            pltpu.VMEM((2, width, half), LOW),
        )
        pl.run_scoped(
            functools.partial(
                merge_phase, normal, inverse, near_ctx, far_ctx, merge, merge_far, fetches
            ),
            pltpu.VMEM((width, rows), LOW),
            pltpu.VMEM((rows, inner), LOW),
            pltpu.VMEM((rows, inner), LOW),
            pltpu.VMEM((width, inner), LOW),
        )

    pl.run_scoped(
        early_phase,
        pltpu.VMEM((rows, width), WIDE),
        pltpu.VMEM((rows, 128), WIDE),
        pltpu.VMEM((rows, inner), LOW),
        pltpu.VMEM((rows, inner), LOW),
        pltpu.VMEM((width, inner), LOW),
        pltpu.VMEM((width, inner), LOW),
    )

    def last_phase(mixed):
        def attend_phase(qkv, context, upper, totals, dots, key_turned, queries, uppers, query_sum, hidden_turned):
            def loads(pair, slot):
                columns = pl.ds(pl.multiple_of(pair * PAIR, PAIR), PAIR)
                return [
                    pltpu.make_async_copy(qkv_in.at[pair], qkv.at[slot], load_sem.at[slot, 0]),
                    pltpu.make_async_copy(
                        context_in.at[:, columns], context.at[slot], load_sem.at[slot, 1]
                    ),
                    pltpu.make_async_copy(
                        grad_ref.at[:, columns], upper.at[slot], load_sem.at[slot, 2]
                    ),
                ]

            fetches = [fetch(totals_in, totals, 0)]
            for copy in [*loads(0, 0), *fetches]:
                copy.start()
            for copy in fetches:
                copy.wait()
            blocks = ((0, LONGEST), (LONGEST, total_rows - LONGEST))
            per_pair = total_rows // TILE

            def hidden_tile(step, slot):
                return pltpu.make_async_copy(
                    hidden_turned_in.at[tile(step, tall), :],
                    hidden_turned.at[slot],
                    load_sem.at[slot, 3],
                )

            def project(second):
                grad, first = (grads[5], 0) if second else (grads[4], inner)
                span = (pairs // 2) * 3 * PAIR
                columns = slice(span if second else 0, span * 2 if second else span)
                hidden_tile(0, 0).start()
                for step in range(width // tall):
                    if step + 1 < width // tall:
                        hidden_tile(step + 1, (step + 1) % 2).start()
                    hidden_tile(step, step % 2).wait()
                    grad[step * tall : (step + 1) * tall, first : first + span] = dot_nn(
                        hidden_turned[step % 2], mixed[:, columns]
                    ).astype(LOW)

            def pair_body(pair):
                slot = lax.rem(pair, 2)
                for copy in loads(pair, slot):
                    copy.wait()

                @pl.when(pair + 1 < pairs)
                def _():
                    for copy in loads(pair + 1, 1 - slot):
                        copy.start()

                attend_back_open(
                    qkv.at[slot], context.at[slot], upper.at[slot], dots, key_turned, queries, uppers
                )
                base = pair * 3 * PAIR

                def columns(which):
                    return pl.ds(pl.multiple_of(base + which * PAIR, PAIR), PAIR)

                for begin, size in blocks:
                    block = slice(begin, begin + size)
                    query_sum[:, block] = jnp.zeros((PAIR, size), WIDE)

                    def key_tile(step, begin=begin, size=size):
                        at, key_sum, value_sum = attend_back_tile(
                            qkv.at[slot], score_bias, totals.at[pair], dots, key_turned, queries, uppers, query_sum,
                            begin, size, step,
                        )
                        mixed[at, columns(1)] = key_sum.astype(LOW)
                        mixed[at, columns(2)] = value_sum.astype(LOW)

                    between = {}
                    for step in range(size // TILE):
                        number = begin // TILE + step
                        for act_pair in range(pairs):
                            for p, s in SCATTER_AT["attend"].get(act_pair * per_pair + number, ()):

                                def act(act_pair=act_pair, p=p, s=s):
                                    pl.when(pair == act_pair)(lambda: lines.stage(p, s))

                                between.setdefault(step, []).append(act)
                    looped(size // TILE, key_tile, between)
                    mixed[block, columns(0)] = (
                        (query_sum[:, block] * HEAD_DIM ** (-0.5)).T.astype(LOW)
                    )
                for which, row in ((0, 0), (2, 1)):
                    part = mixed[:, columns(which)].astype(WIDE)
                    spot = pl.multiple_of(member * inner + pair * PAIR, PAIR)
                    small[0, row : row + 1, pl.ds(spot, PAIR)] = jnp.sum(
                        part, axis=0, keepdims=True
                    )

            def project_stages(second):
                return [
                    functools.partial(project, second),
                    *[functools.partial(lines.stage, *st) for st in SCATTER_AT["project"][second]],
                ]

            looped(pairs, pair_body, {1: project_stages(0), 3: project_stages(1)})

        pl.run_scoped(
            attend_phase,
            pltpu.VMEM((2, total_rows, 3 * PAIR), LOW),
            pltpu.VMEM((2, total_rows, PAIR), LOW),
            pltpu.VMEM((2, total_rows, PAIR), LOW),
            pltpu.VMEM(totals_in.shape, WIDE),
            pltpu.VMEM((8, total_rows), WIDE),
            pltpu.VMEM((PAIR, total_rows), LOW),
            pltpu.VMEM((2, total_rows, PAIR), LOW),
            pltpu.VMEM((2, total_rows, PAIR), LOW),
            pltpu.VMEM((PAIR, total_rows), WIDE),
            pltpu.VMEM((2, tall, total_rows), LOW),
        )
        sums.step(0)

        def input_phase(weight, terms, leaving, pair):
            weight_copy = fetch(whole_ref.at[0, :, pl.ds(0, pairs * 3 * PAIR)], weight, 0)
            weight_copy.start()
            pair_copies = [fetch(enc_pair.at[i], pair.at[rows_of(i)], 3 + i) for i in range(2)]
            for copy in pair_copies:
                copy.start()
            weight_copy.wait()

            def term_tile(step):
                at = tile(step, tall)
                total = dot_nt(mixed[at, :], weight[...])
                own = rows // tall
                mine = step // own == member

                @pl.when(mine)
                def _():
                    terms[at, :] = (total + acc[tile(lax.rem(step, own), tall), :]).astype(LOW)

                @pl.when(jnp.logical_not(mine))
                def _():
                    terms[at, :] = total.astype(LOW)

            phase("terms", total_rows // tall, term_tile)
            sums.step(1)

            def own_rows(which, step):
                places = places_of(which * rows + step * tall)
                return picked_rows(group.moved(places, group.own, group.first), terms)

            def far_tile(step):
                leaving[tile(step, tall), :] = own_rows(1 - member, step).astype(LOW)

            phase("far", rows // tall, far_tile)
            crossing = other_core(leaving, input_far, input_sem.at[0], input_sem.at[1])
            crossing.start()
            sums.step(2)

            def near_tile(step):
                acc[tile(step, tall), :] = own_rows(member, step)

            phase("near", rows // tall, near_tile)
            sums.step(3)
            crossing.wait()
            back = fetch(input_far, leaving, 2)
            back.start()
            back.wait()

            @pl.loop(0, rows // short)
            def _(step):
                at = tile(step, short)
                leaving[at, :] = (acc[at, :] + leaving[at, :].astype(WIDE)).astype(LOW)

            done = fetch(leaving, input_out, 2)
            done.start()
            for copy in pair_copies:
                copy.wait()

            def encoded_tile(step):
                places = places_of(member * rows + step * tall)
                index = group.moved(places, group.dealt, group.first)
                terms[tile(step, tall), :] = picked_rows(index, pair).astype(LOW)

            phase("encoded", rows // tall, encoded_tile)
            done.wait()
            done = fetch(terms.at[pl.ds(0, rows)], encoded_out, 2)
            done.start()
            done.wait()

        pl.run_scoped(
            input_phase,
            pltpu.VMEM((width, pairs * 3 * PAIR), LOW),
            pltpu.VMEM((total_rows, width), LOW),
            pltpu.VMEM((rows, width), LOW),
            pltpu.VMEM((total_rows, width), LOW),
        )

    pl.run_scoped(last_phase, pltpu.VMEM((total_rows, pairs * 3 * PAIR), LOW))

    for step in range(4, len(sums.partners) + 1):
        sums.step(step)
    small_out[...] = small[len(sums.partners)]
    for st in SCATTER_AT["end"]:
        lines.stage(*st)
    sums.sent()
    for p in range(len(grads)):
        lines.sent(p)


def finish_kernel(*refs):
    sources, refs = refs[:27], refs[27:]
    targets, refs = refs[:21], refs[21:]
    held, made, (in_sem, out_sem) = refs[:27], refs[27:46], refs[46:]
    loads = [pltpu.make_async_copy(sources[i], held[i], in_sem.at[i]) for i in range(27)]
    for copy in loads:
        copy.start()
    small_ref, *smalls = held[:7]
    vectors_ref, vectors_first, vectors_second, hidden_ref, hidden_first, hidden_second = smalls
    shards, ins, rows_held = held[7:13], held[13:25], held[25:]
    vector_grad_ref, *rest = made
    outs, small_out = rest[:12], rest[12:]
    results = [*rows_held, *made]
    writes = [pltpu.make_async_copy(results[i], targets[i], out_sem.at[i]) for i in range(21)]
    for copy in loads[:7]:
        copy.wait()
    width = vectors_ref.shape[1]
    inner = ins[3].shape[1]
    pairs = inner // PAIR
    span = shards[0].shape[1]
    vector_grad_ref[...] = small_ref[0:8, :]
    states = vectors_ref[...], vectors_first[...], vectors_second[...]
    for i, value in enumerate(adamw_update(*states, small_ref[0:8, :], rate_vectors, 0.0)):
        small_out[i][...] = value
    for i in range(hidden_ref.shape[1] // width):
        columns = slice(i * width, (i + 1) * width)
        states = hidden_ref[:, columns], hidden_first[:, columns], hidden_second[:, columns]
        grad = small_ref[8 + i : 9 + i, :]
        for n, value in enumerate(adamw_update(*states, grad, rate_hidden, 0.0)):
            small_out[3 + n][:, columns] = value

    def update(matrix, lead, columns, grad, grad_columns):
        rate = (rate_project, rate_merge, rate_expand, rate_reduce)[matrix]

        @pl.loop(0, grad.shape[0] // 16)
        def _(step):
            at = pl.ds(pl.multiple_of(step * 16, 16), 16)
            old = [ins[3 * matrix + i][(*lead, at, columns)] for i in range(3)]
            new = adamw_update(*old, grad[at, grad_columns], rate, weight_decay)
            for i in range(3):
                outs[3 * matrix + i][(*lead, at, columns)] = new[i]

    for i in (2, *range(15, 21)):
        writes[i].start()
    for copy in loads[7:13]:
        copy.wait()
    for matrix in (3, 2, 1, 0):
        for copy in loads[13 + 3 * matrix : 16 + 3 * matrix]:
            copy.wait()
        if matrix >= 2:
            for i in range(2):
                columns = slice(i * span, (i + 1) * span)
                update(matrix, (), columns, shards[2 * (3 - matrix) + i], slice(0, span))
        elif matrix == 1:
            update(matrix, (), slice(0, inner), shards[4], slice(0, inner))
        else:
            for pair in range(pairs):
                piece, begin = (4, inner) if pair < pairs // 2 else (5, 0)
                for c in range(3):
                    at = begin + (3 * (pair % (pairs // 2)) + c) * PAIR
                    columns = slice(pair * PAIR, (pair + 1) * PAIR)
                    update(matrix, (c,), columns, shards[piece], slice(at, at + PAIR))
        for copy in writes[3 + 3 * matrix : 6 + 3 * matrix]:
            copy.start()
        if matrix == 3:
            for copy in loads[25:]:
                copy.wait()
            for copy in writes[:2]:
                copy.start()
    for copy in writes:
        copy.wait()


def finish(small, shards, rows_out, matrices, vectors, hidden):
    states = [one for matrix in matrices for one in matrix]
    operands = [small, *vectors, *hidden, *shards, *states, *rows_out]
    shape, sem = jax.ShapeDtypeStruct, pltpu.SemaphoreType.DMA
    results = [
        *[shape(one.shape, LOW) for one in rows_out],
        shape((8, small.shape[1]), WIDE),
        *[shape(one.shape, WIDE) for one in (*states, *vectors, *hidden)],
    ]
    anywhere = pl.BlockSpec(memory_space=pl.ANY)
    return pl.pallas_call(
        finish_kernel,
        in_specs=[anywhere] * len(operands),
        out_specs=[anywhere] * len(results),
        out_shape=results,
        scratch_shapes=[
            *[pltpu.VMEM(one.shape, one.dtype) for one in operands],
            *[pltpu.VMEM(one.shape, one.dtype) for one in results[2:]],
            sem((len(operands),)),
            sem((len(results),)),
        ],
        compiler_params=pltpu.CompilerParams(vmem_limit_bytes=63 * MIB),
    )(*operands)


def back(lengths, dealing, vectors, whole, far, kept, parts):
    qkv, hidden_turned, upstream, context, totals, acc, *_ = kept
    rows, width = acc.shape
    total_rows, inner = context.shape
    depth, shard_rows = parts // 4, width // parts
    half, pair_span = 256, 3 * PAIR * (qkv.shape[0] // 2)
    piece_span = whole.shape[2] // 2
    spans = (*[piece_span] * 4, inner + pair_span, pair_span)
    classes = []
    for span in spans:
        third = max(128, span // 5 // 128 * 128)
        if (span - third) % 256:
            third += 128
        classes.append(((span - third) // 2, (span - third) // 2, third))
    shape, sem = jax.ShapeDtypeStruct, pltpu.SemaphoreType.DMA
    vmem, anywhere = pl.BlockSpec(memory_space=pltpu.VMEM), pl.BlockSpec(memory_space=pl.ANY)
    steps = 3 + depth.bit_length() - 1
    results = pl.pallas_call(
        functools.partial(back_kernel, depth),
        in_specs=[
            *[pl.BlockSpec(memory_space=pltpu.SMEM)] * 2,
            vmem,
            *[anywhere] * (2 + len(kept)),
        ],
        out_specs=[*[anywhere] * 2, vmem, *[anywhere] * (len(spans) + 3)],
        out_shape=[
            shape((rows, width), LOW),
            shape((rows, width), LOW),
            shape((16, width), WIDE),
            *[shape((shard_rows, span), WIDE) for span in spans],
            shape((2, rows, width), LOW),
            shape((total_rows, inner), LOW),
            shape((rows, width), LOW),
        ],
        scratch_shapes=[
            pltpu.VMEM((rows, width), WIDE),
            pltpu.VMEM((2, width, half), LOW),
            pltpu.VMEM((width, inner), LOW),
            pltpu.VMEM((2 * steps + 1, 16, width), WIDE),
            pltpu.VMEM((total_rows - LONGEST, total_rows - LONGEST), WIDE),
            pltpu.VMEM((4, width, piece_span), LOW),
            *[pltpu.VMEM((width, span), LOW) for span in spans[4:]],
            *[pltpu.VMEM((shard_rows, span), WIDE) for span in spans],
            *Scatter.scratch(depth, shard_rows, classes),
            sem((steps,)),
            sem((steps,)),
            sem((9,)),
            sem((2, 6)),
            sem((3,)),
            sem((2,)),
            sem((2,)),
            sem((2,)),
            sem((3,)),
            sem((2,)),
            *Scatter.semaphores(depth, len(spans)),
        ],
        compiler_params=pltpu.CompilerParams(
            collective_id=1, has_side_effects=True, vmem_limit_bytes=63 * MIB
        ),
    )(lengths, dealing, vectors, whole, far, *kept)
    return results[:2], results[2], results[3 : 3 + len(spans)]


def by_kernels(tokens, cotangent, lengths, dealing, project, merge, expand, reduce, vectors, hidden, parts):
    hidden = tuple(one.reshape(1, -1) for one in hidden)
    matrices = (project, merge, expand, reduce)
    whole, far, *kept = front(
        lengths, dealing, *[one[0] for one in matrices], vectors[0], hidden[0], tokens, cotangent, parts
    )
    rows_out, small, shards = back(lengths, dealing, vectors[0], whole, far, kept, parts)
    results = finish(small, shards, rows_out, matrices, vectors, hidden)
    encoded, input_grad, vector_grad = results[:3]
    news = [results[3 + 3 * i : 6 + 3 * i] for i in range(6)]
    return (
        encoded,
        input_grad,
        *news[0],
        *[one.T for one in news[1]],
        *news[2],
        *[one.T for one in news[3]],
        *news[4],
        *[one.reshape(-1) for one in news[5]],
        vector_grad,
    )


def local(
    tokens,
    cotangent,
    lengths,
    dealing,
    project_weight,
    project_first,
    project_second,
    merge_weight,
    merge_first,
    merge_second,
    expand_weight,
    expand_first,
    expand_second,
    reduce_weight,
    reduce_first,
    reduce_second,
    vectors,
    vector_first,
    vector_second,
    hidden_bias,
    hidden_first,
    hidden_second,
):
    parts = lax.axis_size("dp")
    member = lax.axis_index("tensor")
    other = 1 - member
    half_rows, model_width = tokens.shape
    total_rows = 2 * half_rows
    width_half = project_weight.shape[2]
    pairs = width_half // PAIR
    hidden_half = expand_weight.shape[1]
    shard_rows = expand_weight.shape[0]
    own_begin = member * half_rows
    by_kernel = parts % 4 == 0 and (parts & (parts - 1)) == 0 and shard_rows % 16 == 0

    def swap(value):
        return lax.ppermute(value, "tensor", [(0, 1), (1, 0)])

    def own(value, size, which=member):
        return lax.dynamic_slice_in_dim(value, which * size, size, 0)

    if by_kernel:
        return by_kernels(
            tokens, cotangent, lengths, dealing,
            (project_weight, project_first, project_second),
            (merge_weight.T, merge_first.T, merge_second.T),
            (expand_weight, expand_first, expand_second),
            (reduce_weight.T, reduce_first.T, reduce_second.T),
            (vectors, vector_first, vector_second),
            (hidden_bias, hidden_first, hidden_second),
            parts,
        )

    segment, own_of, dealt_of, from_own, from_dealt = layout(lengths[0], dealing[0], total_rows)
    dealt_of = own(dealt_of, half_rows)
    short = segment[LONGEST:]
    score_bias = jnp.where(short[:, None] == short[None, :], 0.0, masked_score).astype(WIDE)

    def own_first(index):
        return lax.rem(index - own_begin + total_rows, total_rows)

    projections = (
        project_weight.reshape(3, shard_rows, pairs, PAIR)
        .transpose(1, 2, 0, 3)
        .reshape(shard_rows, 3 * width_half)
    )
    quarter = hidden_half // 2
    reduce_turned = reduce_weight.T
    shards = jnp.stack(
        [
            jnp.concatenate([projections, merge_weight.T], axis=1),
            jnp.concatenate([expand_weight[:, :quarter], reduce_turned[:, :quarter]], axis=1),
            jnp.concatenate([expand_weight[:, quarter:], reduce_turned[:, quarter:]], axis=1),
        ]
    ).astype(LOW)
    zeros_pair = jnp.zeros((pairs, PAIR), WIDE)
    bias_row = jnp.concatenate(
        [
            own(vectors[0], width_half).reshape(pairs, PAIR),
            zeros_pair,
            own(vectors[1], width_half).reshape(pairs, PAIR),
        ],
        axis=1,
    ).reshape(pairs, 1, 3 * PAIR)
    whole = lax.all_gather(shards, "dp", axis=1, tiled=True)
    far = swap(whole)
    token_pair = jnp.concatenate([tokens, swap(tokens)], axis=0)
    upper_pair = jnp.concatenate([cotangent, swap(cotangent)], axis=0)
    hidden = dot_nn(pick_rows(own_first(own_of), total_rows), token_pair).astype(LOW)
    upstream = dot_nn(pick_rows(own_first(dealt_of), total_rows), upper_pair).astype(LOW)
    qkv = jnp.einsum(
        "rd,dpc->prc",
        hidden,
        whole[0, :, : 3 * width_half].reshape(model_width, pairs, 3 * PAIR),
        preferred_element_type=WIDE,
    )
    qkv = (qkv + bias_row).astype(LOW)
    context, totals = attend(qkv, score_bias)

    (
        encoded, branch_grad, context_grad, merge_grad, expand_grad, reduce_grad, sums, hidden_part_own, hidden_part_far,
    ) = feed_block(
        context,
        whole,
        far,
        own(hidden, half_rows),
        upstream,
        vectors,
        own(hidden_bias, hidden_half),
        own(hidden_bias, hidden_half, other),
    )
    encoded_pair = jnp.concatenate([encoded, swap(encoded)], axis=0)
    encoded_out = dot_nn(
        pick_rows(own_first(own(from_dealt, half_rows)), total_rows), encoded_pair
    ).astype(LOW)
    mixed_grads = attend_back(qkv, score_bias, context, context_grad, totals)
    mixed_sums = jnp.sum(mixed_grads.astype(WIDE), axis=1).reshape(pairs, 3, PAIR)
    mixed_grads = mixed_grads.transpose(1, 0, 2).reshape(total_rows, 3 * width_half)
    project_grad = dot_tn(hidden, mixed_grads)
    input_terms = dot_nt(mixed_grads, whole[0, :, : 3 * width_half])
    own_part = own(input_terms, half_rows) + branch_grad
    input_terms = lax.dynamic_update_slice_in_dim(input_terms, own_part, own_begin, 0).astype(LOW)
    input_far = swap(
        dot_nn(pick_rows(own(from_own, half_rows, other), total_rows), input_terms).astype(LOW)
    )
    input_grad = (
        dot_nn(pick_rows(own(from_own, half_rows), total_rows), input_terms)
        + input_far.astype(WIDE)
    ).astype(LOW)
    zeros_width = jnp.zeros((model_width,), WIDE)
    zeros_hidden = jnp.zeros_like(hidden_bias)
    hidden_total = lax.dynamic_update_slice_in_dim(
        lax.dynamic_update_slice_in_dim(
            zeros_hidden, hidden_part_own, member * hidden_half, 0
        ),
        hidden_part_far,
        other * hidden_half,
        0,
    )
    vector_rows = [
        lax.dynamic_update_slice_in_dim(
            zeros_width, mixed_sums[:, c].reshape(-1), member * width_half, 0
        )
        for c in (0, 2)
    ]
    small = jnp.concatenate(
        [
            jnp.stack(vector_rows),
            sums[2:],
            hidden_total.reshape(-1, model_width),
            jnp.zeros((4, model_width), WIDE),
        ],
        axis=0,
    )
    grads = [
        lax.psum_scatter(g.astype(LOW), "dp", scatter_dimension=0, tiled=True).astype(WIDE)
        for g in (project_grad, merge_grad, expand_grad, reduce_grad)
    ]
    small = lax.psum(small, ("dp", "tensor"))
    project_shard, merge_shard, expand_shard, reduce_shard = grads
    project_shard = (
        project_shard.reshape(shard_rows, pairs, 3, PAIR)
        .transpose(2, 0, 1, 3)
        .reshape(3, shard_rows, width_half)
    )
    vector_grad = small[:8]
    hidden_grad = small[8:12].reshape(-1)
    return (
        encoded_out,
        input_grad,
        *adamw_update(
            project_weight, project_first, project_second, project_shard, rate_project, weight_decay
        ),
        *adamw_update(
            merge_weight, merge_first, merge_second, merge_shard.T, rate_merge, weight_decay
        ),
        *adamw_update(
            expand_weight, expand_first, expand_second, expand_shard, rate_expand, weight_decay
        ),
        *adamw_update(
            reduce_weight, reduce_first, reduce_second, reduce_shard.T, rate_reduce, weight_decay
        ),
        *adamw_update(vectors, vector_first, vector_second, vector_grad, rate_vectors, 0.0),
        *adamw_update(hidden_bias, hidden_first, hidden_second, hidden_grad, rate_hidden, 0.0),
        vector_grad,
    )


def solution(mesh):
    sharded = (
        P("dp", None),
        P("dp", None),
        *[P(None, "dp", "tensor")] * 3,
        *[P("tensor", "dp")] * 3,
        *[P("dp", "tensor")] * 3,
        *[P("tensor", "dp")] * 3,
        *[P()] * 6,
    )
    rows = P(("dp", "tensor"), None)
    return jax.shard_map(
        local,
        mesh=mesh,
        in_specs=(rows, rows, *sharded),
        out_specs=(rows, rows, *sharded[2:], P()),
        check_vma=False,
    )
```

```python
import functools

import jax
import jax.numpy as jnp
from jax import lax
from jax.experimental import pallas as pl
from jax.experimental.pallas import tpu as pltpu
from jax.sharding import PartitionSpec as P

HEAD_DIM = 64
LONGEST = 1024
STEP = 10
PAIR = 2 * HEAD_DIM
TILE = 256
MIB = 1024 * 1024
MESH = pl.DeviceIdType.MESH
LOW = jnp.bfloat16
WIDE = jnp.float32

beta_one = 0.9
beta_two = 0.999
adam_epsilon = 1e-08
weight_decay = 0.01
norm_epsilon = 1e-05
masked_score = -1e30
rate_project = 0.03
rate_merge = 0.3
rate_expand = 0.03
rate_reduce = 0.015
rate_vectors = 0.4
rate_hidden = 0.1


def dot_nn(a, b):
    return jnp.dot(a, b, preferred_element_type=WIDE)


def dot_nt(a, b):
    return lax.dot_general(a, b, (((1,), (1,)), ((), ())), preferred_element_type=WIDE)


def dot_tn(a, b):
    return lax.dot_general(a, b, (((0,), (0,)), ((), ())), preferred_element_type=WIDE)


def layout(lengths_row, dealing_row, total_rows):
    slots = jnp.arange(lengths_row.shape[0], dtype=jnp.int32)
    places = jnp.arange(total_rows, dtype=jnp.int32)
    rank_of = jnp.sum(jnp.where(dealing_row[None, :] == slots[:, None], slots[None, :], 0), axis=1)
    own_start = jnp.cumsum(lengths_row) - lengths_row
    dealt_start = jnp.sum(
        jnp.where(rank_of[None, :] < rank_of[:, None], lengths_row[None, :], 0), axis=1
    )
    longest = lengths_row == LONGEST
    short = jnp.where(longest, 0, lengths_row)
    start = jnp.where(longest, 0, LONGEST + jnp.cumsum(short) - short)

    def inside(begin):
        return (places[:, None] >= begin[None, :]) & (
            places[:, None] < (begin + lengths_row)[None, :]
        )

    def moved(begin, end):
        return places + jnp.sum(jnp.where(inside(begin), (end - begin)[None, :], 0), axis=1)

    segment = jnp.sum(jnp.where(inside(start), slots[None, :], 0), axis=1)
    return (
        segment,
        moved(start, own_start),
        moved(start, dealt_start),
        moved(own_start, start),
        moved(dealt_start, start),
    )


def pick_rows(index, rows):
    places = jnp.arange(rows, dtype=jnp.int32)
    return (index[:, None] == places[None, :]).astype(LOW)


class Group:
    def __init__(self, lengths_ref, dealing_ref):
        count = lengths_ref.shape[1]
        self.lengths = [lengths_ref[0, s] for s in range(count)]
        order = [dealing_ref[0, i] for i in range(count)]
        rank = [sum(jnp.where(order[i] == s, i, 0) for i in range(count)) for s in range(count)]
        short = [jnp.where(length == LONGEST, 0, length) for length in self.lengths]
        self.own, self.dealt, self.first = [], [], []
        own = own_short = jnp.int32(0)
        for s in range(count):
            self.own.append(own)
            self.first.append(jnp.where(self.lengths[s] == LONGEST, 0, LONGEST + own_short))
            self.dealt.append(
                sum(jnp.where(rank[j] < rank[s], self.lengths[j], 0) for j in range(count))
            )
            own, own_short = own + self.lengths[s], own_short + short[s]

    def inside(self, places, begin, s):
        return (places >= begin[s]) & (places < begin[s] + self.lengths[s])

    def moved(self, places, begin, end):
        total = places
        for s in range(len(begin)):
            total = total + jnp.where(self.inside(places, begin, s), end[s] - begin[s], 0)
        return total

    def score_bias(self, count):
        sides = []
        for shape, axis in (((count, 1), 0), ((1, count), 1)):
            places = lax.broadcasted_iota(jnp.int32, shape, axis) + LONGEST
            segment = jnp.zeros_like(places)
            for s in range(len(self.first)):
                segment = segment + jnp.where(self.inside(places, self.first, s), s, 0)
            sides.append(segment)
        return jnp.where(sides[0] == sides[1], 0.0, masked_score).astype(WIDE)


def picked_rows(index, source):
    places = lax.broadcasted_iota(jnp.int32, (index.shape[0], source.shape[0]), 1)
    return dot_nn(jnp.where(index == places, 1.0, 0.0).astype(LOW), source[...])


def attend_tile(qkv_ref, pair, bias_ref, begin, size, step, context_ref, columns, total_ref):
    lane = lax.broadcasted_iota(jnp.int32, (1, PAIR), 1)
    scale = HEAD_DIM ** (-0.5)
    first = pl.multiple_of(begin + step * TILE, TILE)
    query = qkv_ref[pair, pl.ds(first, TILE), 0:PAIR]
    key = qkv_ref[pair, begin : begin + size, PAIR : 2 * PAIR]
    value = qkv_ref[pair, begin : begin + size, 2 * PAIR : 3 * PAIR]
    outcome = []
    chosen = [jnp.where(lane // HEAD_DIM == head, scale, 0.0).astype(LOW) for head in range(2)]
    scores = [dot_nt(query * chosen[head], key) for head in range(2)]
    for head in range(2):
        score = scores[head]
        if begin:
            inner = pl.multiple_of(step * TILE, TILE)
            score = score + bias_ref[pl.ds(inner, TILE), :]
        top = jnp.max(score, axis=1, keepdims=True)
        exponent = jnp.exp(score - top)
        total = jnp.sum(exponent, axis=1, keepdims=True)
        outcome.append(dot_nn(exponent.astype(LOW), value) / total)
        log_total = jnp.broadcast_to(top + jnp.log(total), (TILE, PAIR))
        total_ref[pair, head : head + 1, pl.ds(first, TILE)] = log_total.T[0:1, :]
    context_ref[pl.ds(first, TILE), columns] = jnp.where(
        lane < HEAD_DIM, outcome[0], outcome[1]
    ).astype(LOW)


def attend_kernel(qkv_ref, bias_ref, context_ref, total_ref):
    rows = qkv_ref.shape[1]
    for begin, size in ((0, LONGEST), (LONGEST, rows - LONGEST)):

        @pl.loop(0, size // TILE)
        def _(step):
            attend_tile(
                qkv_ref, 0, bias_ref, begin, size, step, context_ref, slice(0, PAIR), total_ref
            )


def attend(qkv, bias):
    pairs, rows, width = qkv.shape
    return pl.pallas_call(
        attend_kernel,
        grid=(pairs,),
        in_specs=[
            pl.BlockSpec((1, rows, width), lambda p: (p, 0, 0)),
            pl.BlockSpec(bias.shape, lambda p: (0, 0)),
        ],
        out_specs=[
            pl.BlockSpec((rows, PAIR), lambda p: (0, p)),
            pl.BlockSpec((1, 8, rows), lambda p: (p, 0, 0)),
        ],
        out_shape=[
            jax.ShapeDtypeStruct((rows, pairs * PAIR), LOW),
            jax.ShapeDtypeStruct((pairs, 8, rows), WIDE),
        ],
        compiler_params=pltpu.CompilerParams(vmem_limit_bytes=48 * MIB),
    )(qkv, bias)


def attend_back_open(qkv_ref, context_ref, upper_ref, dots, key_turned, queries, uppers):
    lane = lax.broadcasted_iota(jnp.int32, (1, PAIR), 1)
    product = (upper_ref[...].astype(WIDE) * context_ref[...].astype(WIDE)).T
    for head in range(2):
        band = slice(head * HEAD_DIM, (head + 1) * HEAD_DIM)
        dots[head : head + 1, :] = jnp.sum(product[band, :], axis=0, keepdims=True)
        chosen = lane // HEAD_DIM == head
        queries[head] = qkv_ref[:, 0:PAIR] * jnp.where(chosen, HEAD_DIM ** (-0.5), 0.0).astype(LOW)
        uppers[head] = upper_ref[...] * jnp.where(chosen, 1.0, 0.0).astype(LOW)
    key_turned[...] = qkv_ref[:, PAIR : 2 * PAIR].astype(WIDE).T.astype(LOW)


def attend_back_tile(
    qkv_ref, bias_ref, total_ref, dots, key_turned, queries, uppers, query_sum, begin, size, step
):
    block = slice(begin, begin + size)
    first = pl.multiple_of(begin + step * TILE, TILE)
    key = qkv_ref[pl.ds(first, TILE), PAIR : 2 * PAIR]
    value = qkv_ref[pl.ds(first, TILE), 2 * PAIR : 3 * PAIR]
    key_sum = jnp.zeros((TILE, PAIR), WIDE)
    value_sum = jnp.zeros((TILE, PAIR), WIDE)
    scores = [dot_nt(key, queries[head, block, :]) for head in range(2)]
    weight_grads = [dot_nt(value, uppers[head, block, :]) for head in range(2)]
    for head in range(2):
        band = slice(head * HEAD_DIM, (head + 1) * HEAD_DIM)
        score = scores[head]
        if begin:
            inner = pl.multiple_of(step * TILE, TILE)
            score = score + bias_ref[pl.ds(inner, TILE), :]
        probability = jnp.exp(score - total_ref[head : head + 1, block])
        score_grads = probability * (weight_grads[head] - dots[head : head + 1, block])
        score_grads = score_grads.astype(LOW)
        value_sum = value_sum + dot_nn(probability.astype(LOW), uppers[head, block, :])
        key_sum = key_sum + dot_nn(score_grads, queries[head, block, :])
        query_sum[band, block] += dot_nn(key_turned[band, pl.ds(first, TILE)], score_grads)
    return pl.ds(first, TILE), key_sum, value_sum


def attend_back_kernel(
    qkv_ref, bias_ref, context_ref, grad_ref, total_ref, out_ref, dots, key_turned, queries, uppers, query_sum
):
    rows = qkv_ref.shape[1]
    qkv = qkv_ref.at[0]
    attend_back_open(qkv, context_ref, grad_ref, dots, key_turned, queries, uppers)
    for begin, size in ((0, LONGEST), (LONGEST, rows - LONGEST)):
        block = slice(begin, begin + size)
        query_sum[:, block] = jnp.zeros((PAIR, size), WIDE)

        @pl.loop(0, size // TILE)
        def _(step):
            at, key_sum, value_sum = attend_back_tile(
                qkv, bias_ref, total_ref.at[0], dots, key_turned, queries, uppers, query_sum, begin, size, step
            )
            out_ref[0, at, PAIR : 2 * PAIR] = key_sum.astype(LOW)
            out_ref[0, at, 2 * PAIR : 3 * PAIR] = value_sum.astype(LOW)

        out_ref[0, block, 0:PAIR] = (query_sum[:, block] * HEAD_DIM ** (-0.5)).T.astype(LOW)


def attend_back(qkv, bias, context, grad, totals):
    pairs, rows, width = qkv.shape
    return pl.pallas_call(
        attend_back_kernel,
        grid=(pairs,),
        in_specs=[
            pl.BlockSpec((1, rows, width), lambda p: (p, 0, 0)),
            pl.BlockSpec(bias.shape, lambda p: (0, 0)),
            pl.BlockSpec((rows, PAIR), lambda p: (0, p)),
            pl.BlockSpec((rows, PAIR), lambda p: (0, p)),
            pl.BlockSpec((1, 8, rows), lambda p: (p, 0, 0)),
        ],
        out_specs=pl.BlockSpec((1, rows, width), lambda p: (p, 0, 0)),
        out_shape=jax.ShapeDtypeStruct(qkv.shape, LOW),
        scratch_shapes=[
            pltpu.VMEM((8, rows), WIDE),
            pltpu.VMEM((PAIR, rows), LOW),
            pltpu.VMEM((2, rows, PAIR), LOW),
            pltpu.VMEM((2, rows, PAIR), LOW),
            pltpu.VMEM((PAIR, rows), WIDE),
        ],
        compiler_params=pltpu.CompilerParams(vmem_limit_bytes=48 * MIB),
    )(qkv, bias, context, grad, totals)


def place():
    me = lax.axis_index("dp")
    z, y, x = me // 4, (me // 2) % 2, me % 2
    return me, z, y, x


def line_slots(z, depth):
    slots = []
    for step in range(depth - 1):
        slots.append((z - 1 - step, z - 1 - step >= 0, 1))
        slots.append((z + 1 + step, z + 1 + step < depth, -1))
    return slots


def remote(source, target, send, receive, device):
    return pltpu.make_async_remote_copy(
        src_ref=source,
        dst_ref=target,
        send_sem=send,
        recv_sem=receive,
        device_id={"dp": device},
        device_id_type=MESH,
    )


def greet_line(me, z, y, x, depth, extra=()):
    barrier = pltpu.get_barrier_semaphore()
    for peer in (z * 4 + y * 2 + 1 - x, z * 4 + (1 - y) * 2 + x):
        pl.semaphore_signal(barrier, inc=1, device_id={"dp": peer}, device_id_type=MESH)

    @pl.when(z > 0)
    def _():
        pl.semaphore_signal(barrier, inc=1, device_id={"dp": me - 4}, device_id_type=MESH)

    @pl.when(z < depth - 1)
    def _():
        pl.semaphore_signal(barrier, inc=1, device_id={"dp": me + 4}, device_id_type=MESH)

    for peer in extra:
        pl.semaphore_signal(barrier, inc=1, device_id=peer, device_id_type=MESH)
    ends = jnp.where(z > 0, 1, 0) + jnp.where(z < depth - 1, 1, 0)
    pl.semaphore_wait(barrier, 2 + len(extra) + ends)


def other_core(source, target, send, receive):
    return pltpu.make_async_remote_copy(
        src_ref=source,
        dst_ref=target,
        send_sem=send,
        recv_sem=receive,
        device_id={"tensor": 1 - lax.axis_index("tensor")},
        device_id_type=MESH,
    )


class Gather:
    def __init__(self, depth, parts, whole, far, table, sems):
        self.whole, self.far = whole, far
        self.depth = depth
        self.me, self.z, self.y, self.x = place()
        self.x_peer = self.z * 4 + self.y * 2 + 1 - self.x
        self.y_peer = self.z * 4 + (1 - self.y) * 2 + self.x
        self.rows = whole.shape[1] // parts
        self.array = [array for array, *_ in table]
        self.a, self.b, self.ab, self.c, self.all = [], [], [], [], []
        for _, base, width, third in table:
            side = (width - third) // 2
            self.a.append((base, side))
            self.b.append((base + side, side))
            self.ab.append((base, 2 * side))
            self.c.append((base + 2 * side, third))
            self.all.append((base, width))
        (
            self.z_send, self.z_recv, self.zc_send, self.zc_recv, self.xa_send, self.xa_recv, self.yb_send, self.yb_recv,
            self.ya_send, self.ya_recv, self.xb_send, self.xb_recv, self.c_send, self.c_recv, self.far_send, self.far_recv,
        ) = sems
        self.slots = line_slots(self.z, depth)

    @staticmethod
    def semaphores(depth, pieces):
        sem = pltpu.SemaphoreType.DMA
        return [
            *[sem((pieces, depth + 1)), sem((pieces, depth))] * 2,
            *[sem((pieces,)), sem((pieces, depth))] * 2,
            *[sem((pieces,)), sem((pieces, depth, 2))] * 2,
            sem((pieces, 2)),
            sem((pieces, 2)),
            sem((pieces,)),
            sem((pieces,)),
        ]

    def block(self, zb, yb, xb):
        return zb * 4 + yb * 2 + xb

    def cut(self, ref, p, block, count, columns):
        first = pl.multiple_of(block * self.rows, self.rows)
        return ref.at[self.array[p], pl.ds(first, count * self.rows), pl.ds(*columns)]

    def copy(self, p, block, count, columns, send, receive, device):
        part = self.cut(self.whole, p, block, count, columns)
        return remote(part, part, send, receive, device)

    def forward(self, p, block, count, columns):
        if p == 0:
            return
        other_core(
            self.cut(self.whole, p, block, count, columns),
            self.cut(self.far, p, block, count, columns),
            self.far_send.at[p],
            self.far_recv.at[p],
        ).start()

    def far_copy(self, p):
        part = self.far.at[self.array[p], :, pl.ds(*self.all[p])]
        return other_core(part, part, self.far_send.at[p], self.far_recv.at[p])

    def z_copy(self, p, zb, way, back=False):
        block = self.block(zb, self.y, self.x)
        sem = self.depth if back else zb
        return self.copy(
            p, block, 1, self.ab[p], self.z_send.at[p, sem], self.z_recv.at[p, zb], self.me + 4 * way
        )

    def zc_copy(self, p, zb, way, back=False):
        sem = self.depth if back else zb
        return self.copy(
            p, zb * 4, 4, self.c[p], self.zc_send.at[p, sem], self.zc_recv.at[p, zb], self.me + 4 * way
        )

    def xa(self, p, zb, xb):
        block = self.block(zb, self.y, xb)
        return self.copy(
            p, block, 1, self.a[p], self.xa_send.at[p], self.xa_recv.at[p, zb], self.x_peer
        )

    def yb(self, p, zb, yb):
        block = self.block(zb, yb, self.x)
        return self.copy(
            p, block, 1, self.b[p], self.yb_send.at[p], self.yb_recv.at[p, zb], self.y_peer
        )

    def ya(self, p, zb, yb, xb):
        block = self.block(zb, yb, xb)
        return self.copy(
            p, block, 1, self.a[p], self.ya_send.at[p], self.ya_recv.at[p, zb, xb], self.y_peer
        )

    def xb(self, p, zb, yb, xb):
        block = self.block(zb, yb, xb)
        return self.copy(
            p, block, 1, self.b[p], self.xb_send.at[p], self.xb_recv.at[p, zb, yb], self.x_peer
        )

    def xc(self, p, xb):
        block = self.block(self.z, self.y, xb)
        return self.copy(
            p, block, 1, self.c[p], self.c_send.at[p, 0], self.c_recv.at[p, 0], self.x_peer
        )

    def yc(self, p, yb):
        block = self.block(self.z, yb, 0)
        return self.copy(
            p, block, 2, self.c[p], self.c_send.at[p, 1], self.c_recv.at[p, 1], self.y_peer
        )

    def both_ways(self, copy, act):
        @pl.when(self.z < self.depth - 1)
        def _():
            act(copy(self.z, 1))

        @pl.when(self.z > 0)
        def _():
            act(copy(self.z, -1, True))

    def spread(self, p, zb):
        self.xa(p, zb, self.x).start()
        self.yb(p, zb, self.y).start()
        self.ya(p, zb, self.y, self.x).start()
        self.xb(p, zb, self.y, self.x).start()

    def turn(self, p, zb):
        self.xa(p, zb, 1 - self.x).wait_recv()
        self.ya(p, zb, self.y, 1 - self.x).start()
        self.forward(p, self.block(zb, self.y, 1 - self.x), 1, self.a[p])
        self.yb(p, zb, 1 - self.y).wait_recv()
        self.xb(p, zb, 1 - self.y, self.x).start()
        self.forward(p, self.block(zb, 1 - self.y, self.x), 1, self.b[p])

    def at_step(self, step, act):
        for zb, valid, way in self.slots[2 * step : 2 * step + 2]:
            on = (self.z + way >= 0) & (self.z + way < self.depth)
            pl.when(valid)(functools.partial(act, zb, way, on))

    def arrive(self, p, step):
        def act(zb, way, on):
            self.z_copy(p, zb, way).wait_recv()
            pl.when(on)(lambda: self.z_copy(p, zb, way).start())
            self.spread(p, zb)
            self.forward(p, self.block(zb, self.y, self.x), 1, self.ab[p])

        self.at_step(step, act)

    def arrive_c(self, p, step):
        def act(zb, way, on):
            self.zc_copy(p, zb, way).wait_recv()
            pl.when(on)(lambda: self.zc_copy(p, zb, way).start())
            self.forward(p, zb * 4, 4, self.c[p])

        self.at_step(step, act)

    def stage(self, p, s):
        depth = self.depth
        if s == 0:
            self.both_ways(lambda *way: self.z_copy(p, *way), lambda copy: copy.start())
            self.xc(p, self.x).start()
            self.spread(p, self.z)
            self.forward(p, self.me, 1, self.all[p])
            return
        if s == 1:
            self.xc(p, 1 - self.x).wait_recv()
            self.yc(p, self.y).start()
            self.forward(p, self.block(self.z, self.y, 1 - self.x), 1, self.c[p])
        if s == 2:
            self.yc(p, 1 - self.y).wait_recv()
            self.both_ways(lambda *way: self.zc_copy(p, *way), lambda copy: copy.start())
            self.forward(p, self.block(self.z, 1 - self.y, 0), 2, self.c[p])
        if 1 <= s < depth:
            self.arrive(p, s - 1)
        if 3 <= s < depth + 2:
            self.arrive_c(p, s - 3)
        if s == 2:
            self.turn(p, self.z)
        if 3 <= s < depth + 2:
            self.at_step(s - 3, lambda zb, way, on: self.turn(p, zb))
        if s == depth + 2:
            for zb in range(depth):
                for other in range(2):
                    self.ya(p, zb, 1 - self.y, other).wait_recv()
                self.forward(p, self.block(zb, 1 - self.y, 0), 2, self.a[p])
                for other in range(2):
                    self.xb(p, zb, other, 1 - self.x).wait_recv()
                    self.forward(p, self.block(zb, other, 1 - self.x), 1, self.b[p])

    def finish(self, p):
        def sent(copy):
            copy.wait_send()

        if p:
            self.far_copy(p).wait_send()
        self.both_ways(lambda *way: self.z_copy(p, *way), sent)
        self.both_ways(lambda *way: self.zc_copy(p, *way), sent)
        for count, columns, sem in (
            (1, self.a[p], self.xa_send),
            (1, self.b[p], self.yb_send),
            (2, self.a[p], self.ya_send),
            (2, self.b[p], self.xb_send),
        ):
            part = self.cut(self.whole, p, 0, count * self.depth, columns)
            remote(part, part, sem.at[p], sem.at[p], self.me).wait_send()
        self.xc(p, self.x).wait_send()
        self.yc(p, self.y).wait_send()

        def passed(zb, way, on):
            pl.when(on)(lambda: sent(self.z_copy(p, zb, way)))
            pl.when(on)(lambda: sent(self.zc_copy(p, zb, way)))

        for step in range(self.depth - 1):
            self.at_step(step, passed)


def looped(count, body, between):
    @pl.loop(0, count)
    def _(i):
        body(i)
        for step, acts in between.items():

            @pl.when(i == step)
            def _():
                for act in acts:
                    act()


GATHER_AT = {
    "hidden": {0: [(2, 0), (1, 0)], 1: [(0, 1), (0, 2), (0, 3)], 3: [(0, 4)], 4: [(0, 5), (1, 1)]},
    "upstream": {-1: [(2, 1)], 1: [(3, 0)]},
    "project": {-1: [(4, 0), (0, 6)], 1: [(1, 2)], 5: [(2, 2)]},
    "long": {2: [(3, 1), (1, 3)], 7: [(2, 3)], 9: [(1, 4)], 14: [(2, 4)]},
    "short": {2: [(1, 5)], 3: [(3, 2)], 5: [(4, 1)]},
    "norm": {-1: [(1, 6)], 1: [(2, 5)], 3: [(3, 3)]},
    "feed": {-1: [(4, 2), (2, 6)], 0: [(3, 4)], 1: [(4, 3)], 2: [(3, 5)]},
    "last": {-1: [(3, 6), (4, 4)], 0: [(4, 5)]},
    "tail": {-1: [(4, 6)]},
}


def piece_table(width, inner):
    third = width // 8
    return (
        (0, 0, 3 * inner, third),
        (0, 3 * inner, inner, third),
        (1, 0, width, 2 * third),
        (2, 0, width // 2, third),
        (2, width // 2, width // 2, third),
    )


def chunk_columns(j, per_piece, half):
    array, at = 1 + j // per_piece, j % per_piece
    pair = per_piece // 2
    quarter = (at // pair) * per_piece * half + (at % pair) * half
    if isinstance(j, int):
        split = array > 1
        return array, quarter if split else at * half, (
            quarter + pair * half if split else (per_piece + at) * half
        )
    split = array > 1
    first = jnp.where(split, quarter, at * half)
    return array, first, first + jnp.where(split, pair, per_piece) * half


def front_kernel(
    depth, lengths_ref, dealing_ref, project_in, merge_in, expand_in, reduce_in, vectors_in, hidden_bias_in,
    tokens_ref, cotangent_ref,
    whole_out, far_ref, qkv_out, turned_out, upstream_out, context_out, total_out,
    acc_out, normal_out, inverse_out, low_turned_out, active_out, slope_out, far_context_out,
    project_ref, merge_ref, expand_ref, reduce_ref, vectors_ref, hidden_bias_ref,
    whole, score_bias, token, upper, hidden, turned, upstream, qkv, context, total,
    acc, normal, inverse, low, low_turned, active, slope, far_context, merge_far, expand_buf, reduce_buf,
    local_sem, core_sem, out_sem, load_sem, chunk_sem, weight_sem, *sems,
):
    arrays = whole.shape[0]
    half_rows, width = tokens_ref.shape
    rows = 2 * half_rows
    pairs = qkv.shape[0]
    inner = pairs * PAIR
    both = expand_buf.shape[2]
    half = both // 2
    hidden_half = expand_ref.shape[1]
    chunks = hidden_half // half
    per_piece = chunks // (arrays - 1)
    member = lax.axis_index("tensor")
    table = piece_table(whole.shape[2], inner)
    pieces = len(table)
    lines = Gather(depth, 4 * depth, whole, far_ref, table, sems)
    me = lines.me
    tall, short = 2 * TILE, TILE // 2

    weights = [
        pltpu.make_async_copy(source, target, weight_sem.at[i])
        for i, (source, target) in enumerate(
            (
                (project_in, project_ref),
                (merge_in, merge_ref),
                (expand_in, expand_ref),
                (reduce_in, reduce_ref),
                (vectors_in, vectors_ref),
                (hidden_bias_in, hidden_bias_ref),
            )
        )
    ]
    for copy in weights:
        copy.start()
    own = [
        pltpu.make_async_copy(tokens_ref, token.at[member], local_sem.at[0]),
        pltpu.make_async_copy(cotangent_ref, upper.at[member], local_sem.at[1]),
    ]
    for copy in own:
        copy.start()
    for copy in weights:
        copy.wait()
    mine = pl.ds(pl.multiple_of(me * lines.rows, lines.rows), lines.rows)
    for pair in range(pairs):
        for c in range(3):
            first = (3 * pair + c) * PAIR
            whole[0, mine, first : first + PAIR] = project_ref[
                c, :, pair * PAIR : (pair + 1) * PAIR
            ].astype(LOW)
    whole[0, mine, 3 * inner :] = merge_ref[...].astype(LOW)
    for j in range(chunks):
        array, first, second = chunk_columns(j, per_piece, half)
        columns = slice(j * half, (j + 1) * half)
        whole[array, mine, first : first + half] = expand_ref[:, columns].astype(LOW)
        whole[array, mine, second : second + half] = reduce_ref[:, columns].astype(LOW)
    greet_line(me, lines.z, lines.y, lines.x, depth, [{"tensor": 1 - member}])
    crossing = [
        other_core(tokens_ref, token.at[member], core_sem.at[0, 0], core_sem.at[0, 1]),
        other_core(cotangent_ref, upper.at[member], core_sem.at[1, 0], core_sem.at[1, 1]),
    ]
    lines.stage(0, 0)
    for copy in crossing:
        copy.start()
    group = Group(lengths_ref, dealing_ref)
    score_bias[...] = group.score_bias(rows - LONGEST)
    for copy in own:
        copy.wait()

    leaving = []

    def leave(source, target):
        copy = pltpu.make_async_copy(source, target, out_sem.at[len(leaving)])
        copy.start()
        leaving.append(copy)

    def before(name):
        for stage in GATHER_AT.get(name, {}).get(-1, ()):
            lines.stage(*stage)

    def phase(name, count, body):
        between = {
            step: [functools.partial(lines.stage, *stage) for stage in stages]
            for step, stages in GATHER_AT.get(name, {}).items()
            if step >= 0
        }
        looped(count, body, between)

    def places_of(first):
        return first + lax.broadcasted_iota(jnp.int32, (TILE, 1), 0)

    def picked(index, source):
        return picked_rows(index, source.at[0]) + picked_rows(index - half_rows, source.at[1])

    def tile(step, size=TILE):
        return pl.ds(pl.multiple_of(step * size, size), size)

    def hidden_tile(step):
        index = group.moved(places_of(step * TILE), group.first, group.own)
        rows_here = picked(index, token)
        hidden[tile(step), :] = rows_here.astype(LOW)
        turned[:, tile(step)] = rows_here.T.astype(LOW)

    def upstream_tile(step):
        places = places_of(member * half_rows + step * TILE)
        index = group.moved(places, group.first, group.dealt)
        upstream[tile(step), :] = picked(index, upper).astype(LOW)

    crossing[0].wait()
    before("hidden")
    phase("hidden", rows // TILE, hidden_tile)
    leave(turned, turned_out)
    crossing[1].wait()
    before("upstream")
    phase("upstream", half_rows // TILE, upstream_tile)
    leave(upstream, upstream_out)

    def project_tile(i):
        pair, step = i // (rows // tall), lax.rem(i, rows // tall)
        at = tile(step, tall)
        columns = pl.ds(pl.multiple_of(pair * 3 * PAIR, PAIR), 3 * PAIR)
        bias_columns = pl.ds(pl.multiple_of(member * inner + pair * PAIR, PAIR), PAIR)
        bias = jnp.concatenate(
            [
                vectors_ref[0:1, bias_columns],
                jnp.zeros((1, PAIR), WIDE),
                vectors_ref[1:2, bias_columns],
            ],
            axis=1,
        )
        qkv[pair, at, :] = (dot_nn(hidden[at, :], whole[0, :, columns]) + bias).astype(LOW)

    before("project")
    phase("project", pairs * rows // tall, project_tile)
    leave(qkv, qkv_out)

    def attend_step(begin, size):
        def step_of(i):
            pair, step = i // (size // TILE), lax.rem(i, size // TILE)
            columns = pl.ds(pl.multiple_of(pair * PAIR, PAIR), PAIR)
            attend_tile(qkv, pair, score_bias, begin, size, step, context, columns, total)

        return step_of

    before("long")
    phase("long", pairs * LONGEST // TILE, attend_step(0, LONGEST))
    before("short")
    phase("short", pairs * (rows - LONGEST) // TILE, attend_step(LONGEST, rows - LONGEST))
    leave(context, context_out)
    leave(total, total_out)

    own_first = member * half_rows
    other_rows = pl.ds(pl.multiple_of((1 - member) * half_rows, half_rows), half_rows)
    crossing = other_core(context.at[other_rows], far_context, core_sem.at[2, 0], core_sem.at[2, 1])
    crossing.start()
    before("norm")
    lines.far_copy(1).wait_recv()
    merge_columns = pl.ds(whole.shape[2] - inner, inner)
    merge_copy = pltpu.make_async_copy(
        far_ref.at[0, :, merge_columns], merge_far, local_sem.at[2]
    )
    merge_copy.start()
    merge_copy.wait()
    crossing.wait()
    leave(far_context, far_context_out)

    def norm_tile(step):
        at = tile(step, short)
        own_at = pl.ds(pl.multiple_of(own_first + step * short, short), short)
        branch = dot_nt(context[own_at, :], whole[0, :, merge_columns])
        branch = branch + dot_nt(far_context[at, :], merge_far[...])
        unit, scale = norm(hidden[own_at, :].astype(WIDE) + branch + vectors_ref[2:3, :])
        normed = unit * vectors_ref[3:4, :] + vectors_ref[4:5, :]
        normal[at, :] = unit
        inverse[at, :] = jnp.broadcast_to(scale, (short, 128))
        low[at, :] = normed.astype(LOW)
        low_turned[:, at] = normed.T.astype(LOW)
        acc[at, :] = normed + vectors_ref[5:6, :]

    leave(whole.at[0], whole_out.at[0])
    phase("norm", half_rows // short, norm_tile)
    leave(normal, normal_out)
    leave(inverse, inverse_out)
    leave(low_turned, low_turned_out)

    def loads(j):
        slot = lax.rem(j, 2)
        array, *firsts = chunk_columns(j, per_piece, half)
        copies = []
        for kind, buf in enumerate((expand_buf, reduce_buf)):
            first = pl.multiple_of(firsts[kind], half)
            for side, source in enumerate((far_ref, whole)):
                copies.append(
                    pltpu.make_async_copy(
                        source.at[array, :, pl.ds(first, half)],
                        buf.at[slot, :, pl.ds(side * half, half)],
                        load_sem.at[slot, kind, side],
                    )
                )
        return copies

    def results(j):
        slot = lax.rem(j, 2)
        return [
            pltpu.make_async_copy(active.at[slot], active_out.at[j], chunk_sem.at[slot, 0]),
            pltpu.make_async_copy(slope.at[slot], slope_out.at[j], chunk_sem.at[slot, 1]),
        ]

    def chunk_of(piece, first_chunk, count):
        def chunk(i):
            j = first_chunk + i
            slot = lax.rem(j, 2)

            @pl.when(i == 0)
            def _():
                lines.far_copy(piece).wait_recv()
                for copy in loads(j):
                    copy.start()

            for copy in loads(j):
                copy.wait()

            @pl.when(i + 1 < count)
            def _():
                for copy in loads(j + 1):
                    copy.start()

            @pl.when(j >= 2)
            def _():
                for copy in results(j - 2):
                    copy.wait()

            biases = []
            for which in (1 - member, member):
                first = pl.multiple_of(which * hidden_half + j * half, half)
                biases.append(hidden_bias_ref[:, pl.ds(first, half)])
            bias = jnp.concatenate(biases, axis=1)
            tiles = [slice(step * TILE, (step + 1) * TILE) for step in range(half_rows // TILE)]
            parts = [dot_nn(low[at, :], expand_buf[slot]) for at in tiles]
            for at, part in zip(tiles, parts, strict=True):
                value = part + bias
                below, bell = normal_cells(value)
                held = (value * below).astype(LOW)
                active[slot, at, :] = held
                slope[slot, at, :] = (below + value * bell * 0.3989422804014327).astype(LOW)
                acc[at, :] += dot_nt(held, reduce_buf[slot])
            for copy in results(j):
                copy.start()

        return chunk

    first_chunk = 0
    for piece, name in ((2, "feed"), (3, "last"), (4, "tail")):
        count = chunks * table[piece][2] // (2 * hidden_half)
        before(name)
        columns = pl.ds(*lines.all[piece])
        leave(
            whole.at[lines.array[piece], :, columns],
            whole_out.at[lines.array[piece], :, columns],
        )
        if name == "last":
            for p in range(piece):
                lines.finish(p)
        phase(name, count, chunk_of(piece, first_chunk, count))
        first_chunk += count
    leave(acc, acc_out)
    for p in range(pieces - 2, pieces):
        lines.finish(p)
    for j in (chunks - 2, chunks - 1):
        for copy in results(j):
            copy.wait()
    for copy in leaving:
        copy.wait()


def front(lengths, dealing, project, merge, expand, reduce, vectors, hidden_bias, tokens, cotangent, parts):
    shard_rows, hidden_half = expand.shape
    arrays, columns = 3, hidden_half
    half_rows, width = tokens.shape
    rows, pairs, depth = 2 * half_rows, project.shape[2] // PAIR, parts // 4
    inner, half = pairs * PAIR, 256
    pieces = len(piece_table(columns, inner))
    chunks, both = hidden_half // half, 2 * half
    shape, sem = jax.ShapeDtypeStruct, pltpu.SemaphoreType.DMA
    anywhere = pl.BlockSpec(memory_space=pl.ANY)
    held = [
        ((pairs, rows, 3 * PAIR), LOW),
        ((width, rows), LOW),
        ((half_rows, width), LOW),
        ((rows, inner), LOW),
        ((pairs, 8, rows), WIDE),
        ((half_rows, width), WIDE),
        ((half_rows, width), WIDE),
        ((half_rows, 128), WIDE),
        ((width, half_rows), LOW),
        ((chunks, half_rows, both), LOW),
        ((chunks, half_rows, both), LOW),
        ((half_rows, inner), LOW),
    ]
    return pl.pallas_call(
        functools.partial(front_kernel, depth),
        in_specs=[*[pl.BlockSpec(memory_space=pltpu.SMEM)] * 2, *[anywhere] * 8],
        out_specs=[anywhere] * 14,
        out_shape=[
            shape((arrays, parts * shard_rows, columns), LOW),
            shape((arrays, parts * shard_rows, columns), LOW),
            *[shape(*one) for one in held],
        ],
        scratch_shapes=[
            *[
                pltpu.VMEM(one.shape, WIDE)
                for one in (project, merge, expand, reduce, vectors, hidden_bias)
            ],
            pltpu.VMEM((arrays, parts * shard_rows, columns), LOW),
            pltpu.VMEM((rows - LONGEST, rows - LONGEST), WIDE),
            pltpu.VMEM((2, half_rows, width), LOW),
            pltpu.VMEM((2, half_rows, width), LOW),
            pltpu.VMEM((rows, width), LOW),
            pltpu.VMEM((width, rows), LOW),
            pltpu.VMEM((half_rows, width), LOW),
            pltpu.VMEM((pairs, rows, 3 * PAIR), LOW),
            pltpu.VMEM((rows, inner), LOW),
            pltpu.VMEM((pairs, 8, rows), WIDE),
            pltpu.VMEM((half_rows, width), WIDE),
            pltpu.VMEM((half_rows, width), WIDE),
            pltpu.VMEM((half_rows, 128), WIDE),
            pltpu.VMEM((half_rows, width), LOW),
            pltpu.VMEM((width, half_rows), LOW),
            pltpu.VMEM((2, half_rows, both), LOW),
            pltpu.VMEM((2, half_rows, both), LOW),
            pltpu.VMEM((half_rows, inner), LOW),
            pltpu.VMEM((width, inner), LOW),
            pltpu.VMEM((2, width, both), LOW),
            pltpu.VMEM((2, width, both), LOW),
            sem((3,)),
            sem((3, 2)),
            sem((16,)),
            sem((2, 2, 2)),
            sem((2, 2)),
            sem((6,)),
            *Gather.semaphores(depth, pieces),
        ],
        compiler_params=pltpu.CompilerParams(
            collective_id=0, has_side_effects=True, vmem_limit_bytes=63 * MIB
        ),
    )(lengths, dealing, project, merge, expand, reduce, vectors, hidden_bias, tokens, cotangent)


def normal_cells(value):
    bell = jnp.exp2(value * value * (-0.5 * 1.4426950408889634))
    below = 1.0 + 0.39 * 0.7071067811865476 * jnp.abs(value)
    t = pl.reciprocal(below, approx=True)
    t = t * (2.0 - below * t)
    t = t * (2.0 - below * t)
    tail = 0.5 * -0.2275377237624147
    for factor in (
        0.8866668177122106,
        -0.6354042576077721,
        0.649562611731642,
        0.0913871257655044,
        0.23532542445435511,
    ):
        tail = tail * t + 0.5 * factor
    tail = tail * t * bell
    return jnp.where(value < 0.0, tail, 1.0 - tail), bell


def norm(values):
    center = values - jnp.mean(values, axis=1, keepdims=True)
    spread = jnp.mean(center * center, axis=1, keepdims=True)
    scale = lax.rsqrt(spread + norm_epsilon)
    return center * scale, scale


def norm_back(scaled, unit, scale):
    return scale * (
        scaled
        - jnp.mean(scaled, axis=1, keepdims=True)
        - unit * jnp.mean(scaled * unit, axis=1, keepdims=True)
    )


def feed_kernel(
    context_ref, merge_ref, merge_far_ref, whole_ref, far_ref, hidden_ref, upstream_ref, vectors_ref, bias_ref,
    encoded_ref, branch_ref, grad_ref, merge_grad_ref, expand_grad_ref, reduce_grad_ref, sums_ref, hidden_sums_ref,
    own_ctx, far_ctx, acc, normal, inverse, low, turned, late, late_turned, active, slope, inner_grad,
    expand_buf, reduce_buf, arrived, leaving, kept, done, grad_own, grad_far, merge_send, merge_recv,
    ctx_sem, load_sem, send_sem, recv_sem, out_sem, last_sem,
):
    rows = hidden_ref.shape[0]
    chunks, _, both = bias_ref.shape
    half = both // 2
    per_piece = whole_ref.shape[2] // (2 * half)
    member = lax.axis_index("tensor")
    peer = {"tensor": 1 - member}
    tall, short = 256, 128
    width = hidden_ref.shape[1]

    def across(source, target, send, receive):
        return pltpu.make_async_remote_copy(
            src_ref=source,
            dst_ref=target,
            send_sem=send,
            recv_sem=receive,
            device_id=peer,
            device_id_type=MESH,
        )

    def rows_of(which):
        return pl.ds(pl.multiple_of(which * rows, rows), rows)

    def tile(step, size):
        return pl.ds(pl.multiple_of(step * size, size), size)

    def loads(j, slot):
        piece, at = 1 + j // per_piece, lax.rem(j, per_piece) * half
        copies = []
        for kind, buf in enumerate((expand_buf, reduce_buf)):
            first = pl.multiple_of(at + kind * per_piece * half, half)
            for side, source in enumerate((far_ref, whole_ref)):
                copies.append(
                    pltpu.make_async_copy(
                        source.at[piece, :, pl.ds(first, half)],
                        buf.at[slot, :, pl.ds(side * half, half)],
                        load_sem.at[slot, kind, side],
                    )
                )
        return copies

    for copy in loads(0, 0):
        copy.start()
    barrier = pltpu.get_barrier_semaphore()
    pl.semaphore_signal(barrier, inc=1, device_id=peer, device_id_type=MESH)
    pl.semaphore_wait(barrier, 1)
    out_ctx = across(context_ref.at[rows_of(1 - member)], far_ctx, ctx_sem.at[0], ctx_sem.at[1])
    out_ctx.start()
    in_ctx = pltpu.make_async_copy(context_ref.at[rows_of(member)], own_ctx, ctx_sem.at[2])
    in_ctx.start()
    sums_ref[...] = jnp.zeros_like(sums_ref)
    in_ctx.wait()
    out_ctx.wait()

    def add_sum(row, values):
        sums_ref[row : row + 1, :] += jnp.sum(values, axis=0, keepdims=True)

    @pl.loop(0, rows // short)
    def _(step):
        at = tile(step, short)
        branch = dot_nt(own_ctx[at, :], merge_ref[...]) + dot_nt(far_ctx[at, :], merge_far_ref[...])
        unit, scale = norm(hidden_ref[at, :].astype(WIDE) + branch + vectors_ref[2:3, :])
        normed = unit * vectors_ref[3:4, :] + vectors_ref[4:5, :]
        normal[at, :] = unit
        inverse[at, :] = jnp.broadcast_to(scale, (short, 128))
        low[at, :] = normed.astype(LOW)
        turned[:, at] = normed.T.astype(LOW)
        acc[at, :] = normed + vectors_ref[5:6, :]

    @pl.loop(0, chunks)
    def _(j):
        slot = lax.rem(j, 2)
        for copy in loads(j, slot):
            copy.wait()

        @pl.when(j + 1 < chunks)
        def _():
            for copy in loads(j + 1, 1 - slot):
                copy.start()

        for step in range(rows // tall):
            at = slice(step * tall, (step + 1) * tall)
            inner = dot_nn(low[at, :], expand_buf[slot]) + bias_ref[j]
            below, bell = normal_cells(inner)
            held = (inner * below).astype(LOW)
            active[j, at, :] = held
            slope[j, at, :] = (below + inner * bell * 0.3989422804014327).astype(LOW)
            acc[at, :] += dot_nt(held, reduce_buf[slot])

    for copy in loads(0, 0):
        copy.start()

    @pl.loop(0, rows // short)
    def _(step):
        at = tile(step, short)
        unit, scale = norm(acc[at, :])
        encoded_ref[at, :] = (unit * vectors_ref[6:7, :] + vectors_ref[7:8, :]).astype(LOW)
        upper = upstream_ref[at, :].astype(WIDE)
        add_sum(6, upper * unit)
        add_sum(7, upper)
        grad = norm_back(upper * vectors_ref[6:7, :], unit, scale)
        grad_low = grad.astype(LOW)
        add_sum(5, grad_low.astype(WIDE))
        acc[at, :] = grad
        late[at, :] = grad_low
        late_turned[:, at] = grad.T.astype(LOW)

    def send(j, kind):
        return across(
            leaving.at[lax.rem(j, 2), kind],
            arrived.at[lax.rem(j, 4), kind],
            send_sem.at[lax.rem(j, 2), kind],
            recv_sem.at[lax.rem(j, 4), kind],
        )

    def store(j, kind):
        target = (expand_grad_ref, reduce_grad_ref)[kind]
        cols = pl.ds(pl.multiple_of(j * half, half), half)
        return pltpu.make_async_copy(
            done.at[lax.rem(j, 2), kind], target.at[:, cols], out_sem.at[lax.rem(j, 2), kind]
        )

    def finish(j):
        for kind in range(2):
            send(j, kind).wait_recv()

            @pl.when(j >= 2)
            def _():
                store(j - 2, kind).wait()

            @pl.loop(0, width // tall)
            def _(step):
                at = tile(step, tall)
                done[lax.rem(j, 2), kind, at, :] = (
                    kept[lax.rem(j, 2), kind, at, :]
                    + arrived[lax.rem(j, 4), kind, at, :].astype(WIDE)
                ).astype(LOW)

            store(j, kind).start()

    @pl.loop(0, chunks)
    def _(j):
        slot = lax.rem(j, 2)
        for copy in loads(j, slot):
            copy.wait()

        @pl.when(j + 1 < chunks)
        def _():
            for copy in loads(j + 1, 1 - slot):
                copy.start()

        total = jnp.zeros((1, both), WIDE)
        for step in range(rows // tall):
            at = slice(step * tall, (step + 1) * tall)
            grad = dot_nn(late[at, :], reduce_buf[slot]) * slope[j, at, :].astype(WIDE)
            grad = grad.astype(LOW)
            inner_grad[at, :] = grad
            total = total + jnp.sum(grad.astype(WIDE), axis=0, keepdims=True)
            acc[at, :] += dot_nt(grad, expand_buf[slot])
        hidden_sums_ref[j] = total

        @pl.when(j >= 2)
        def _():
            for kind in range(2):
                send(j - 2, kind).wait_send()

        for kind, (left, right) in enumerate(((turned, inner_grad), (late_turned, active.at[j]))):
            for step in range(width // tall):
                at = slice(step * tall, (step + 1) * tall)
                part = dot_nn(left[at, :], right[...])
                leaving[slot, kind, at, :] = part[:, 0:half].astype(LOW)
                kept[slot, kind, at, :] = part[:, half:both]
            send(j, kind).start()

        @pl.when(j >= 1)
        def _():
            finish(j - 1)

    @pl.loop(0, rows // short)
    def _(step):
        at = tile(step, short)
        grad = acc[at, :]
        unit = normal[at, :]
        add_sum(3, grad * unit)
        add_sum(4, grad)
        branch_grad = norm_back(grad * vectors_ref[3:4, :], unit, inverse[at, 0:1])
        branch_low = branch_grad.astype(LOW)
        add_sum(2, branch_low.astype(WIDE))
        branch_ref[at, :] = branch_grad
        turned[:, at] = branch_grad.T.astype(LOW)
        grad_far[at, :] = dot_nn(branch_low, merge_far_ref[...]).astype(LOW)
        grad_own[at, :] = dot_nn(branch_low, merge_ref[...]).astype(LOW)

    out_grad = across(grad_far, grad_ref.at[rows_of(member)], ctx_sem.at[0], ctx_sem.at[1])
    out_grad.start()
    in_grad = pltpu.make_async_copy(grad_own, grad_ref.at[rows_of(member)], ctx_sem.at[2])
    in_grad.start()
    for step in range(width // tall):
        at = slice(step * tall, (step + 1) * tall)
        merge_send[at, :] = dot_nn(turned[at, :], far_ctx[...]).astype(LOW)
    out_merge = across(merge_send, merge_recv, last_sem.at[0], last_sem.at[1])
    out_merge.start()
    finish(chunks - 1)
    for kind in range(2):
        send(chunks - 2, kind).wait_send()
        send(chunks - 1, kind).wait_send()
        store(chunks - 2, kind).wait()
        store(chunks - 1, kind).wait()
    out_merge.wait()
    for step in range(width // tall):
        at = slice(step * tall, (step + 1) * tall)
        merge_grad_ref[at, :] = (
            dot_nn(turned[at, :], own_ctx[...]) + merge_recv[at, :].astype(WIDE)
        ).astype(LOW)
    out_grad.wait()
    in_grad.wait()


def feed_block(context, whole, far, hidden_own, upstream, vectors, bias_own, bias_far):
    total_rows, inner = context.shape
    rows, width = hidden_own.shape
    hidden = bias_own.shape[0]
    merge, merge_far = whole[0, :, -inner:], far[0, :, -inner:]
    half = 256
    chunks = hidden // half
    both = 2 * half
    bias = jnp.concatenate(
        [bias_far.reshape(chunks, 1, half), bias_own.reshape(chunks, 1, half)], axis=2
    )
    vmem, anywhere = pl.BlockSpec(memory_space=pltpu.VMEM), pl.BlockSpec(memory_space=pl.ANY)
    sem = pltpu.SemaphoreType.DMA
    shape = jax.ShapeDtypeStruct
    *results, hidden_sums = pl.pallas_call(
        feed_kernel,
        in_specs=[anywhere, vmem, vmem, *[anywhere] * 2, *[vmem] * 4],
        out_specs=[vmem, vmem, anywhere, vmem, anywhere, anywhere, vmem, vmem],
        out_shape=[
            shape((rows, width), LOW),
            shape((rows, width), WIDE),
            shape((total_rows, inner), LOW),
            shape((width, inner), LOW),
            shape((width, hidden), LOW),
            shape((width, hidden), LOW),
            shape((8, width), WIDE),
            shape((chunks, 1, both), WIDE),
        ],
        scratch_shapes=[
            pltpu.VMEM((rows, inner), LOW),
            pltpu.VMEM((rows, inner), LOW),
            pltpu.VMEM((rows, width), WIDE),
            pltpu.VMEM((rows, width), WIDE),
            pltpu.VMEM((rows, 128), WIDE),
            pltpu.VMEM((rows, width), LOW),
            pltpu.VMEM((width, rows), LOW),
            pltpu.VMEM((rows, width), LOW),
            pltpu.VMEM((width, rows), LOW),
            pltpu.VMEM((chunks, rows, both), LOW),
            pltpu.VMEM((chunks, rows, both), LOW),
            pltpu.VMEM((rows, both), LOW),
            pltpu.VMEM((2, width, both), LOW),
            pltpu.VMEM((2, width, both), LOW),
            pltpu.VMEM((4, 2, width, half), LOW),
            pltpu.VMEM((2, 2, width, half), LOW),
            pltpu.VMEM((2, 2, width, half), WIDE),
            pltpu.VMEM((2, 2, width, half), LOW),
            pltpu.VMEM((rows, inner), LOW),
            pltpu.VMEM((rows, inner), LOW),
            pltpu.VMEM((width, inner), LOW),
            pltpu.VMEM((width, inner), LOW),
            sem((3,)),
            sem((2, 2, 2)),
            sem((2, 2)),
            sem((4, 2)),
            sem((2, 2)),
            sem((2,)),
        ],
        compiler_params=pltpu.CompilerParams(
            collective_id=2, has_side_effects=True, vmem_limit_bytes=60 * MIB
        ),
        cost_estimate=pl.CostEstimate(
            flops=12 * rows * width * 2 * hidden, bytes_accessed=8 * width * hidden * 4, transcendentals=0
        ),
    )(context, merge, merge_far, whole, far, hidden_own, upstream, vectors, bias)
    hidden_far = hidden_sums[:, 0, :half].reshape(-1)
    hidden_near = hidden_sums[:, 0, half:].reshape(-1)
    return (*results, hidden_near, hidden_far)


class Scatter:
    buffers = 8

    def __init__(self, depth, grads, shards, targets, buffers, sems):
        self.depth, self.grads, self.shards, self.targets = depth, grads, shards, targets
        self.held = [buffers[8 * p : 8 * p + 8] for p in range(len(grads))]
        self.me, self.z, self.y, self.x = place()
        self.x_peer = self.z * 4 + self.y * 2 + 1 - self.x
        self.y_peer = self.z * 4 + (1 - self.y) * 2 + self.x
        self.rows = grads[0].shape[0] // (4 * depth)
        (
            self.a1_send, self.a1_recv, self.a2_send, self.a2_recv, self.b2_send, self.b2_recv, self.b1_send, self.b1_recv,
            self.z_send, self.z_recv, self.zc_send, self.zc_recv, self.c_send, self.c_recv, self.out_sem,
        ) = sems

    @staticmethod
    def scratch(depth, rows, classes):
        found = []
        for a, b, c in classes:
            found += [
                pltpu.VMEM((depth, 2 * rows, a), LOW),
                pltpu.VMEM((depth, 2, rows, b), LOW),
                pltpu.VMEM((depth, rows, a), LOW),
                pltpu.VMEM((depth, rows, b), LOW),
                pltpu.VMEM((depth + 1, rows, a + b), LOW),
                pltpu.VMEM((depth + 1, 4 * rows, c), LOW),
                pltpu.VMEM((2 * rows, c), LOW),
                pltpu.VMEM((rows, c), LOW),
            ]
        return found

    @staticmethod
    def semaphores(depth, pieces):
        sem = pltpu.SemaphoreType.DMA
        return [
            *[sem((pieces,)), sem((pieces, depth))] * 3,
            sem((pieces,)),
            sem((pieces, depth, 2)),
            *[sem((pieces,)), sem((pieces, depth + 1))] * 2,
            sem((pieces, 2)),
            sem((pieces, 2)),
            sem((pieces,)),
        ]

    def done(self, p):
        return pltpu.make_async_copy(self.shards[p], self.targets[p], self.out_sem.at[p])

    def columns(self, p):
        a, b, c = (self.held[p][i].shape[-1] for i in (0, 1, 5))
        return pl.ds(0, a), pl.ds(a, b), pl.ds(a + b, c)

    def block(self, zb, yb, xb):
        return zb * 4 + yb * 2 + xb

    def span(self, block, count=1):
        return pl.ds(pl.multiple_of(block * self.rows, self.rows), count * self.rows)

    def add(self, put, count, *terms):
        chunk = min(count, 64)

        @pl.loop(0, count // chunk)
        def _(step):
            at = pl.multiple_of(step * chunk, chunk)
            parts = [term(at, chunk) for term in terms]
            if len(parts) > 2 or put.wide:
                parts = [part.astype(WIDE) for part in parts]
            total = parts[0]
            for part in parts[1:]:
                total = total + part
            put(at, chunk, total)

    def a1(self, p, zb):
        return remote(
            self.grads[p].at[self.span(self.block(zb, 1 - self.y, 0), 2), self.columns(p)[0]],
            self.held[p][0].at[zb],
            self.a1_send.at[p],
            self.a1_recv.at[p, zb],
            self.y_peer,
        )

    def b1(self, p, zb, yb):
        return remote(
            self.grads[p].at[self.span(self.block(zb, yb, 1 - self.x)), self.columns(p)[1]],
            self.held[p][1].at[zb, yb],
            self.b1_send.at[p],
            self.b1_recv.at[p, zb, yb],
            self.x_peer,
        )

    def a2(self, p, zb):
        return remote(
            self.held[p][0].at[zb, self.span(1 - self.x)],
            self.held[p][2].at[zb],
            self.a2_send.at[p],
            self.a2_recv.at[p, zb],
            self.x_peer,
        )

    def b2(self, p, zb):
        return remote(
            self.held[p][1].at[zb, 1 - self.y],
            self.held[p][3].at[zb],
            self.b2_send.at[p],
            self.b2_recv.at[p, zb],
            self.y_peer,
        )

    def slot(self, zb, way):
        return zb if way > 0 else zb + (self.depth - zb) * jnp.where(zb == self.z - 1, 1, 0)

    def z_copy(self, p, zb, way):
        slot = self.slot(zb, way)
        return remote(
            self.held[p][4].at[zb],
            self.held[p][4].at[slot],
            self.z_send.at[p],
            self.z_recv.at[p, slot],
            self.me + 4 * way,
        )

    def zc_copy(self, p, zb, way, first):
        slot = self.slot(zb, way)
        source = self.held[p][5].at[zb]
        if first:
            source = self.grads[p].at[self.span(zb * 4, 4), self.columns(p)[2]]
        return remote(
            source,
            self.held[p][5].at[slot],
            self.zc_send.at[p],
            self.zc_recv.at[p, slot],
            self.me + 4 * way,
        )

    def arrived(self, ref, sem, slot):
        part = ref.at[slot]
        remote(part, part, sem, sem, self.me).wait_recv()

    def cy(self, p):
        return remote(
            self.held[p][5].at[self.z, self.span(2 * (1 - self.y), 2)],
            self.held[p][6],
            self.c_send.at[p, 0],
            self.c_recv.at[p, 0],
            self.y_peer,
        )

    def cx(self, p):
        return remote(
            self.held[p][5].at[self.z, self.span(2 * self.y + 1 - self.x)],
            self.held[p][7],
            self.c_send.at[p, 1],
            self.c_recv.at[p, 1],
            self.x_peer,
        )

    def grad(self, p, block, columns):
        def term(at, count):
            first = pl.multiple_of(block * self.rows + at, 16)
            return self.grads[p][pl.ds(first, count), columns]

        return term

    def part(self, ref, lead, block, columns=None):
        columns = slice(None) if columns is None else columns

        def term(at, count):
            first = pl.multiple_of(block * self.rows + at, 16)
            return ref[(*lead, pl.ds(first, count), columns)]

        return term

    def put(self, ref, lead, block, columns=None):
        columns = slice(None) if columns is None else columns

        def act(at, count, total):
            first = pl.multiple_of(block * self.rows + at, 16)
            ref[(*lead, pl.ds(first, count), columns)] = total.astype(ref.dtype)

        act.wide = ref.dtype == WIDE
        return act

    def open(self, p, zb):
        self.a1(p, zb).start()
        self.b1(p, zb, 0).start()
        self.b1(p, zb, 1).start()

    def first(self, p, zb):
        z, y, x = self.z, self.y, self.x
        a, b, _ = self.columns(p)
        r1a, r1b = self.held[p][0], self.held[p][1]
        self.a1(p, zb).wait_recv()
        self.add(
            self.put(r1a, (zb,), 1 - x),
            self.rows,
            self.part(r1a, (zb,), 1 - x),
            self.grad(p, self.block(zb, y, 1 - x), a),
        )
        self.a2(p, zb).start()
        self.b1(p, zb, 0).wait_recv()
        self.b1(p, zb, 1).wait_recv()
        self.add(
            self.put(r1b, (zb, 1 - y), 0),
            self.rows,
            self.part(r1b, (zb, 1 - y), 0),
            self.grad(p, self.block(zb, 1 - y, x), b),
        )
        self.b2(p, zb).start()

    def terms(self, p, zb):
        z, y, x = self.z, self.y, self.x
        a, b, _ = self.columns(p)
        r1a, r1b, r2a, r2b = self.held[p][:4]
        own = self.block(zb, y, x)
        return (
            [self.grad(p, own, a), self.part(r1a, (zb,), x), self.part(r2a, (zb,), 0)],
            [self.grad(p, own, b), self.part(r1b, (zb, y), 0), self.part(r2b, (zb,), 0)],
        )

    def pass_on(self, p, zb, way):
        a, b, _ = self.columns(p)
        rz = self.held[p][4]
        self.a2(p, zb).wait_recv()
        self.b2(p, zb).wait_recv()
        from_line = (self.z - way >= 0) & (self.z - way < self.depth)

        @pl.when(from_line)
        def _():
            self.arrived(rz, self.z_recv.at[p, zb], zb)
            for terms, columns in zip(self.terms(p, zb), (a, b), strict=True):
                self.add(
                    self.put(rz, (zb,), 0, columns),
                    self.rows,
                    *terms,
                    self.part(rz, (zb,), 0, columns),
                )

        @pl.when(jnp.logical_not(from_line))
        def _():
            for terms, columns in zip(self.terms(p, zb), (a, b), strict=True):
                self.add(self.put(rz, (zb,), 0, columns), self.rows, *terms)

        self.z_copy(p, zb, way).start()

    def pass_c(self, p, zb, way):
        c = self.columns(p)[2]
        rc = self.held[p][5]
        from_line = (self.z - way >= 0) & (self.z - way < self.depth)

        @pl.when(from_line)
        def _():
            self.arrived(rc, self.zc_recv.at[p, zb], zb)
            self.add(
                self.put(rc, (zb,), 0),
                4 * self.rows,
                self.part(rc, (zb,), 0),
                self.grad(p, zb * 4, c),
            )
            self.zc_copy(p, zb, way, False).start()

        @pl.when(jnp.logical_not(from_line))
        def _():
            self.zc_copy(p, zb, way, True).start()

    def own_c(self, p):
        z, depth = self.z, self.depth
        c = self.columns(p)[2]
        rc = self.held[p][5]
        grad = self.grad(p, z * 4, c)
        lower, upper = self.part(rc, (z,), 0), self.part(rc, (depth,), 0)
        put = self.put(rc, (z,), 0)

        @pl.when(z > 0)
        def _():
            self.arrived(rc, self.zc_recv.at[p, z], z)

        @pl.when(z < depth - 1)
        def _():
            self.arrived(rc, self.zc_recv.at[p, depth], depth)

        @pl.when((z > 0) & (z < depth - 1))
        def _():
            self.add(put, 4 * self.rows, grad, lower, upper)

        @pl.when(z == 0)
        def _():
            self.add(put, 4 * self.rows, grad, upper)

        @pl.when(z == depth - 1)
        def _():
            self.add(put, 4 * self.rows, grad, lower)

        self.cy(p).start()

    def turn_c(self, p):
        rc, rcy = self.held[p][5], self.held[p][6]
        self.cy(p).wait_recv()
        self.add(
            self.put(rc, (self.z,), 2 * self.y),
            2 * self.rows,
            self.part(rc, (self.z,), 2 * self.y),
            self.part(rcy, (), 0),
        )
        self.cx(p).start()

    def close(self, p):
        z, depth = self.z, self.depth
        a, b, c = self.columns(p)
        rz, rc, rcx = self.held[p][4], self.held[p][5], self.held[p][7]
        self.a2(p, z).wait_recv()
        self.b2(p, z).wait_recv()

        @pl.when(z > 0)
        def _():
            self.arrived(rz, self.z_recv.at[p, z], z)

        @pl.when(z < depth - 1)
        def _():
            self.arrived(rz, self.z_recv.at[p, depth], depth)

        def total(*slots):
            for terms, columns in zip(self.terms(p, z), (a, b), strict=True):
                lines = [self.part(rz, (slot,), 0, columns) for slot in slots]
                self.add(self.put(self.shards[p], (), 0, columns), self.rows, *terms, *lines)

        pl.when((z > 0) & (z < depth - 1))(lambda: total(z, depth))
        pl.when(z == 0)(lambda: total(depth))
        pl.when(z == depth - 1)(lambda: total(z))
        self.cx(p).wait_recv()
        self.add(
            self.put(self.shards[p], (), 0, c),
            self.rows,
            self.part(rc, (z,), 2 * self.y + self.x),
            self.part(rcx, (), 0),
        )
        self.done(p).start()

    def at_step(self, step, act):
        z, depth = self.z, self.depth
        if step < 0:
            act(z, 0)
            return
        for zb, valid, way in (
            (z + 1 + step, z + 1 + step < depth, 1),
            (z - 1 - step, z - 1 - step >= 0, -1),
        ):
            pl.when(valid)(functools.partial(act, zb, way))

    def stage(self, p, s):
        last = self.depth - 2

        def opened(step):
            self.at_step(step, lambda zb, way: self.open(p, zb))

        def added(step):
            self.at_step(step, lambda zb, way: self.first(p, zb))

        def passed(step):
            self.at_step(step, lambda zb, way: self.pass_on(p, zb, way))

        def passed_c(step):
            self.at_step(step, lambda zb, way: self.pass_c(p, zb, way))

        if s == 0:
            opened(last)
            opened(last - 1)
            passed_c(last)
            return
        if s <= last + 2:
            added(last + 1 - s)
        if last - 1 - s >= -1:
            opened(last - 1 - s)
        if last - s >= 0:
            passed_c(last - s)
        if s >= 2 and last + 2 - s >= 0:
            passed(last + 2 - s)
        if s == last + 1:
            self.own_c(p)
        if s == last + 2:
            self.turn_c(p)
        if s == last + 3:
            self.close(p)

    def sent(self, p):
        passed = pl.ds(0, self.depth - 1)
        for part, sem in (
            (self.held[p][0], self.a1_send),
            (self.held[p][1], self.b1_send),
            (self.held[p][2], self.a2_send),
            (self.held[p][3], self.b2_send),
            (self.held[p][4].at[passed], self.z_send),
            (self.held[p][5].at[passed], self.zc_send),
        ):
            remote(part, part, sem.at[p], sem.at[p], self.me).wait_send()
        self.cy(p).wait_send()
        self.cx(p).wait_send()
        self.done(p).wait()


class SmallSum:
    def __init__(self, lines, buffer, send, recv):
        member = lax.axis_index("tensor")
        self.partners = [{"tensor": 1 - member}, {"dp": lines.x_peer}, {"dp": lines.y_peer}]
        for level in range(lines.depth.bit_length() - 1):
            reach = 1 << level
            way = 1 - 2 * ((lines.z // reach) % 2)
            self.partners.append({"dp": lines.me + 4 * reach * way})
        self.buffer, self.send, self.recv = buffer, send, recv

    def copy(self, step):
        return pltpu.make_async_remote_copy(
            src_ref=self.buffer.at[step],
            dst_ref=self.buffer.at[len(self.partners) + 1 + step],
            send_sem=self.send.at[step],
            recv_sem=self.recv.at[step],
            device_id=self.partners[step],
            device_id_type=MESH,
        )

    def step(self, step):
        if step:
            self.copy(step - 1).wait_recv()
            self.buffer[step] = self.buffer[step - 1] + self.buffer[len(self.partners) + step]
        if step < len(self.partners):
            self.copy(step).start()

    def sent(self):
        for step in range(len(self.partners)):
            self.copy(step).wait_send()


def adamw_update(master, moment, square, gradient, step_rate, decay_rate):
    moment_new = beta_one * moment + (1.0 - beta_one) * gradient
    square_new = beta_two * square + (1.0 - beta_two) * gradient * gradient
    moment_hat = moment_new * (1.0 / (1.0 - beta_one**STEP))
    square_hat = square_new * (1.0 / (1.0 - beta_two**STEP))
    master_new = master - step_rate * (
        moment_hat / (jnp.sqrt(square_hat) + adam_epsilon) + decay_rate * master
    )
    return (moment_new, square_new, master_new)


SCATTER_AT = {
    "expand": {0: [(0, 0)], 3: [(0, 1)], 5: [(0, 2)]},
    "norm": {-1: [(1, 0)]},
    "merge": {1: [(0, 3)]},
    "attend": {1: [(1, 1)], 4: [(0, 4)], 7: [(1, 2)], 13: [(1, 3)], 14: [(2, 1)], 19: [(1, 4), (2, 2)]},
    "project": {0: [(2, 0)], 1: [(3, 0)]},
    "terms": {1: [(3, 1)], 3: [(2, 3)], 4: [(3, 2), (1, 5)]},
    "far": {1: [(0, 5)]},
    "near": {-1: [(3, 3), (2, 4)]},
    "encoded": {-1: [(3, 4)], 0: [(2, 5)]},
    "end": [(3, 5)],
}


def back_kernel(
    depth, lengths_ref, dealing_ref, vectors_ref,
    whole_ref, far_ref, qkv_in, hidden_turned_in, upstream_in, context_in, totals_in,
    acc_in, normal_in, inverse_in, turned_in, active_in, slope_in, far_ctx_in, *rest,
):
    encoded_out, input_out, small_out, *rest = rest
    targets, rest = rest[:4], rest[4:]
    enc_pair, grad_ref, input_far, acc, arrived, merge_recv, small, score_bias, *rest = rest
    chunk_grads, *rest = rest
    grads, rest = [*[chunk_grads.at[p] for p in range(2)], *rest[:2]], rest[2:]
    shards, rest = rest[:4], rest[4:]
    buffers, rest = rest[: 4 * Scatter.buffers], rest[4 * Scatter.buffers :]
    small_send, small_recv, in_sem, load_sem, ctx_sem, far_send, far_recv, merge_sem, enc_sem, input_sem, *sems = rest
    lines = Scatter(depth, grads, shards, targets, buffers, sems)
    sums = SmallSum(lines, small, small_send, small_recv)
    group = Group(lengths_ref, dealing_ref)
    member = lax.axis_index("tensor")
    rows, width = acc.shape
    total_rows = 2 * rows
    chunks, _, both = active_in.shape
    half = both // 2
    per_piece = chunks // 2
    pairs = qkv_in.shape[0]
    inner = pairs * PAIR
    tall, short = 256, 128

    def rows_of(which):
        return pl.ds(pl.multiple_of(which * rows, rows), rows)

    def tile(step, size):
        return pl.ds(pl.multiple_of(step * size, size), size)

    def fetch(source, target, sem):
        return pltpu.make_async_copy(source, target, in_sem.at[sem])

    def phase(name, count, body):
        between = {
            step: [functools.partial(lines.stage, *stage) for stage in stages]
            for step, stages in SCATTER_AT.get(name, {}).items()
        }
        for act in between.pop(-1, ()):
            act()
        looped(count, body, between)

    def places_of(first):
        return first + lax.broadcasted_iota(jnp.int32, (tall, 1), 0)

    def add_sum(row, values):
        small[0, row : row + 1, :] += jnp.sum(values, axis=0, keepdims=True)

    def feed_phase(later, late, late_turned, turned, upstream, active, slope, inner_grad, expand_buf, reduce_buf, leaving):
        def active_load(j):
            slot = lax.rem(j, 2)
            return [pltpu.make_async_copy(active_in.at[j], active.at[slot], load_sem.at[slot, 4])]

        def loads(j):
            slot = lax.rem(j, 2)
            array, *firsts = chunk_columns(j, per_piece, half)
            copies = [pltpu.make_async_copy(slope_in.at[j], slope.at[slot], load_sem.at[slot, 5])]
            for kind, buf in enumerate((expand_buf, reduce_buf)):
                first = pl.multiple_of(firsts[kind], half)
                for side, source in enumerate((far_ref, whole_ref)):
                    copies.append(
                        pltpu.make_async_copy(
                            source.at[array, :, pl.ds(first, half)],
                            buf.at[slot, :, pl.ds(side * half, half)],
                            load_sem.at[slot, 2 * kind + side],
                        )
                    )
            return copies

        def taken(j, load):
            for copy in load(j):
                copy.wait()

            @pl.when(j + 1 < chunks)
            def _():
                for copy in load(j + 1):
                    copy.start()

        acc_copy = fetch(acc_in, acc, 0)
        acc_copy.start()
        fetches = [fetch(upstream_in, upstream, 1), fetch(turned_in, turned, 2)]
        for copy in fetches:
            copy.start()
        for copy in [*active_load(0), *loads(0)]:
            copy.start()
        greet_line(
            lines.me, lines.z, lines.y, lines.x, depth, [sums.partners[0], *sums.partners[3:]]
        )
        for copy in later:
            copy.start()
        small[0] = jnp.zeros(small.shape[1:], WIDE)
        score_bias[...] = group.score_bias(total_rows - LONGEST)
        acc_copy.wait()
        for copy in fetches:
            copy.wait()

        def late_tile(step):
            at = tile(step, short)
            unit, scale = norm(acc[at, :])
            upper = upstream[at, :].astype(WIDE)
            upstream[at, :] = (unit * vectors_ref[6:7, :] + vectors_ref[7:8, :]).astype(LOW)
            add_sum(6, upper * unit)
            add_sum(7, upper)
            grad = norm_back(upper * vectors_ref[6:7, :], unit, scale)
            grad_low = grad.astype(LOW)
            add_sum(5, grad_low.astype(WIDE))
            acc[at, :] = grad
            late[at, :] = grad_low
            late_turned[:, at] = grad.T.astype(LOW)

        looped(rows // short, late_tile, {})
        enc_near = pltpu.make_async_copy(upstream, enc_pair.at[member], enc_sem.at[2])
        enc_far = other_core(upstream, enc_pair.at[member], enc_sem.at[0], enc_sem.at[1])
        enc_near.start()
        enc_far.start()

        def send(k):
            slot = lax.rem(k, 2)
            return other_core(
                leaving.at[slot], arrived.at[slot], far_send.at[slot], far_recv.at[slot]
            )

        def own_columns(k):
            return pl.ds(pl.multiple_of(lax.rem(k, chunks) * half, half), half)

        def finish(k):
            piece, slot = k // chunks, lax.rem(k, 2)
            send(k).wait_recv()

            @pl.loop(0, width // tall)
            def _(step):
                at = tile(step, tall)
                chunk_grads[piece, at, own_columns(k)] += arrived[slot, at, :]

        def products(k, left, right):
            piece, slot = k // chunks, lax.rem(k, 2)

            @pl.when(k >= 2)
            def _():
                send(k - 2).wait_send()

            parts = [
                dot_nn(left[step * tall : (step + 1) * tall, :], right[...])
                for step in range(width // tall)
            ]
            for step, part in enumerate(parts):
                at = slice(step * tall, (step + 1) * tall)
                leaving[slot, at, :] = part[:, 0:half].astype(LOW)
                chunk_grads[piece, at, own_columns(k)] = part[:, half:both].astype(LOW)

            @pl.when(k >= 1)
            def _():
                finish(k - 1)

            send(k).start()

        def reduce_chunk(j):
            taken(j, active_load)
            products(j, late_turned, active.at[lax.rem(j, 2)])

        def expand_chunk(j):
            slot = lax.rem(j, 2)
            taken(j, loads)
            total = jnp.zeros((1, both), WIDE)
            tiles = [slice(step * tall, (step + 1) * tall) for step in range(rows // tall)]
            parts = [dot_nn(late[at, :], reduce_buf[slot]) for at in tiles]
            for at, part in zip(tiles, parts, strict=True):
                grad = (part * slope[slot, at, :].astype(WIDE)).astype(LOW)
                inner_grad[at, :] = grad
                total = total + jnp.sum(grad.astype(WIDE), axis=0, keepdims=True)
                acc[at, :] += dot_nt(grad, expand_buf[slot])
            for which, side in ((1 - member, 0), (member, half)):
                row = 8 + which * 2 + j // per_piece
                spot = pl.ds(pl.multiple_of(lax.rem(j, per_piece) * half, half), half)
                small[0, pl.ds(row, 1), spot] = total[:, side : side + half]
            products(chunks + j, turned, inner_grad)

        phase("reduce", chunks, reduce_chunk)
        phase("expand", chunks, expand_chunk)
        finish(2 * chunks - 1)
        for k in (2 * chunks - 2, 2 * chunks - 1):
            send(k).wait_send()
        enc_near.wait()
        enc_far.wait()

    def merge_phase(normal, inverse, near_ctx, far_ctx, merge, merge_far, fetches, turned, grad_own, grad_far, merge_send):
        for copy in fetches:
            copy.wait()

        def norm_tile(step):
            at = tile(step, short)
            grad = acc[at, :]
            unit = normal[at, :]
            add_sum(3, grad * unit)
            add_sum(4, grad)
            branch_grad = norm_back(grad * vectors_ref[3:4, :], unit, inverse[at, 0:1])
            branch_low = branch_grad.astype(LOW)
            add_sum(2, branch_low.astype(WIDE))
            acc[at, :] = branch_grad
            turned[:, at] = branch_grad.T.astype(LOW)
            grad_far[at, :] = dot_nn(branch_low, merge_far[...]).astype(LOW)
            grad_own[at, :] = dot_nn(branch_low, merge[...]).astype(LOW)

        phase("norm", rows // short, norm_tile)
        out_grad = other_core(grad_far, grad_ref.at[rows_of(member)], ctx_sem.at[0], ctx_sem.at[1])
        in_grad = pltpu.make_async_copy(grad_own, grad_ref.at[rows_of(member)], ctx_sem.at[2])
        out_grad.start()
        in_grad.start()
        out_merge = other_core(merge_send, merge_recv, merge_sem.at[0], merge_sem.at[1])

        def merge_step(which):
            @pl.when(which == 0)
            def _():
                for step in range(width // tall):
                    at = slice(step * tall, (step + 1) * tall)
                    merge_send[at, :] = dot_nn(turned[at, :], far_ctx[...]).astype(LOW)
                out_merge.start()

            @pl.when(which == 1)
            def _():
                out_merge.wait()
                for step in range(width // tall):
                    at = slice(step * tall, (step + 1) * tall)
                    grads[2][at, 0:inner] = (
                        dot_nn(turned[at, :], near_ctx[...]) + merge_recv[at, :].astype(WIDE)
                    ).astype(LOW)

        phase("merge", 2, merge_step)
        out_grad.wait()
        in_grad.wait()

    def early_phase(normal, inverse, near_ctx, far_ctx, merge, merge_far):
        merge_columns = pl.ds(whole_ref.shape[2] - inner, inner)
        fetches = [
            fetch(normal_in, normal, 3),
            fetch(inverse_in, inverse, 4),
            fetch(context_in.at[rows_of(member)], near_ctx, 5),
            fetch(far_ctx_in, far_ctx, 6),
            fetch(whole_ref.at[0, :, merge_columns], merge, 7),
            fetch(far_ref.at[0, :, merge_columns], merge_far, 8),
        ]
        pl.run_scoped(
            functools.partial(feed_phase, fetches),
            pltpu.VMEM((rows, width), LOW),
            pltpu.VMEM((width, rows), LOW),
            pltpu.VMEM((width, rows), LOW),
            pltpu.VMEM((rows, width), LOW),
            pltpu.VMEM((2, rows, both), LOW),
            pltpu.VMEM((2, rows, both), LOW),
            pltpu.VMEM((rows, both), LOW),
            pltpu.VMEM((2, width, both), LOW),
            pltpu.VMEM((2, width, both), LOW),
            pltpu.VMEM((2, width, half), LOW),
        )
        pl.run_scoped(
            functools.partial(
                merge_phase, normal, inverse, near_ctx, far_ctx, merge, merge_far, fetches
            ),
            pltpu.VMEM((width, rows), LOW),
            pltpu.VMEM((rows, inner), LOW),
            pltpu.VMEM((rows, inner), LOW),
            pltpu.VMEM((width, inner), LOW),
        )

    pl.run_scoped(
        early_phase,
        pltpu.VMEM((rows, width), WIDE),
        pltpu.VMEM((rows, 128), WIDE),
        pltpu.VMEM((rows, inner), LOW),
        pltpu.VMEM((rows, inner), LOW),
        pltpu.VMEM((width, inner), LOW),
        pltpu.VMEM((width, inner), LOW),
    )

    def last_phase(mixed):
        def attend_phase(qkv, context, upper, totals, dots, key_turned, queries, uppers, query_sum, hidden_turned):
            def loads(pair, slot):
                columns = pl.ds(pl.multiple_of(pair * PAIR, PAIR), PAIR)
                return [
                    pltpu.make_async_copy(qkv_in.at[pair], qkv.at[slot], load_sem.at[slot, 0]),
                    pltpu.make_async_copy(
                        context_in.at[:, columns], context.at[slot], load_sem.at[slot, 1]
                    ),
                    pltpu.make_async_copy(
                        grad_ref.at[:, columns], upper.at[slot], load_sem.at[slot, 2]
                    ),
                ]

            fetches = [fetch(totals_in, totals, 0)]
            for copy in [*loads(0, 0), *fetches]:
                copy.start()
            for copy in fetches:
                copy.wait()
            blocks = ((0, LONGEST), (LONGEST, total_rows - LONGEST))
            per_pair = total_rows // TILE

            def hidden_tile(step, slot):
                return pltpu.make_async_copy(
                    hidden_turned_in.at[tile(step, tall), :],
                    hidden_turned.at[slot],
                    load_sem.at[slot, 3],
                )

            def project(second):
                grad, first = (grads[3], 0) if second else (grads[2], inner)
                span = (pairs // 2) * 3 * PAIR
                columns = slice(span if second else 0, span * 2 if second else span)
                hidden_tile(0, 0).start()
                for step in range(width // tall):
                    if step + 1 < width // tall:
                        hidden_tile(step + 1, (step + 1) % 2).start()
                    hidden_tile(step, step % 2).wait()
                    grad[step * tall : (step + 1) * tall, first : first + span] = dot_nn(
                        hidden_turned[step % 2], mixed[:, columns]
                    ).astype(LOW)

            def pair_body(pair):
                slot = lax.rem(pair, 2)
                for copy in loads(pair, slot):
                    copy.wait()

                @pl.when(pair + 1 < pairs)
                def _():
                    for copy in loads(pair + 1, 1 - slot):
                        copy.start()

                attend_back_open(
                    qkv.at[slot], context.at[slot], upper.at[slot], dots, key_turned, queries, uppers
                )
                base = pair * 3 * PAIR

                def columns(which):
                    return pl.ds(pl.multiple_of(base + which * PAIR, PAIR), PAIR)

                for begin, size in blocks:
                    block = slice(begin, begin + size)
                    query_sum[:, block] = jnp.zeros((PAIR, size), WIDE)

                    def key_tile(step, begin=begin, size=size):
                        at, key_sum, value_sum = attend_back_tile(
                            qkv.at[slot], score_bias, totals.at[pair], dots, key_turned, queries, uppers, query_sum,
                            begin, size, step,
                        )
                        mixed[at, columns(1)] = key_sum.astype(LOW)
                        mixed[at, columns(2)] = value_sum.astype(LOW)

                    between = {}
                    for step in range(size // TILE):
                        number = begin // TILE + step
                        for act_pair in range(pairs):
                            for p, s in SCATTER_AT["attend"].get(act_pair * per_pair + number, ()):

                                def act(act_pair=act_pair, p=p, s=s):
                                    pl.when(pair == act_pair)(lambda: lines.stage(p, s))

                                between.setdefault(step, []).append(act)
                    looped(size // TILE, key_tile, between)
                    mixed[block, columns(0)] = (
                        (query_sum[:, block] * HEAD_DIM ** (-0.5)).T.astype(LOW)
                    )
                for which, row in ((0, 0), (2, 1)):
                    part = mixed[:, columns(which)].astype(WIDE)
                    spot = pl.multiple_of(member * inner + pair * PAIR, PAIR)
                    small[0, row : row + 1, pl.ds(spot, PAIR)] = jnp.sum(
                        part, axis=0, keepdims=True
                    )

            def project_stages(second):
                return [
                    functools.partial(project, second),
                    *[functools.partial(lines.stage, *st) for st in SCATTER_AT["project"][second]],
                ]

            looped(pairs, pair_body, {1: project_stages(0), 3: project_stages(1)})

        pl.run_scoped(
            attend_phase,
            pltpu.VMEM((2, total_rows, 3 * PAIR), LOW),
            pltpu.VMEM((2, total_rows, PAIR), LOW),
            pltpu.VMEM((2, total_rows, PAIR), LOW),
            pltpu.VMEM(totals_in.shape, WIDE),
            pltpu.VMEM((8, total_rows), WIDE),
            pltpu.VMEM((PAIR, total_rows), LOW),
            pltpu.VMEM((2, total_rows, PAIR), LOW),
            pltpu.VMEM((2, total_rows, PAIR), LOW),
            pltpu.VMEM((PAIR, total_rows), WIDE),
            pltpu.VMEM((2, tall, total_rows), LOW),
        )
        sums.step(0)

        def input_phase(weight, terms, leaving, pair):
            weight_copy = fetch(whole_ref.at[0, :, pl.ds(0, pairs * 3 * PAIR)], weight, 0)
            weight_copy.start()
            pair_copies = [fetch(enc_pair.at[i], pair.at[rows_of(i)], 3 + i) for i in range(2)]
            for copy in pair_copies:
                copy.start()
            weight_copy.wait()

            def term_tile(step):
                at = tile(step, tall)
                total = dot_nt(mixed[at, :], weight[...])
                own = rows // tall
                mine = step // own == member

                @pl.when(mine)
                def _():
                    terms[at, :] = (total + acc[tile(lax.rem(step, own), tall), :]).astype(LOW)

                @pl.when(jnp.logical_not(mine))
                def _():
                    terms[at, :] = total.astype(LOW)

            phase("terms", total_rows // tall, term_tile)
            sums.step(1)

            def own_rows(which, step):
                places = places_of(which * rows + step * tall)
                return picked_rows(group.moved(places, group.own, group.first), terms)

            def far_tile(step):
                leaving[tile(step, tall), :] = own_rows(1 - member, step).astype(LOW)

            phase("far", rows // tall, far_tile)
            crossing = other_core(leaving, input_far, input_sem.at[0], input_sem.at[1])
            crossing.start()
            sums.step(2)

            def near_tile(step):
                acc[tile(step, tall), :] = own_rows(member, step)

            phase("near", rows // tall, near_tile)
            sums.step(3)
            crossing.wait()
            back = fetch(input_far, leaving, 2)
            back.start()
            back.wait()

            @pl.loop(0, rows // short)
            def _(step):
                at = tile(step, short)
                leaving[at, :] = (acc[at, :] + leaving[at, :].astype(WIDE)).astype(LOW)

            done = fetch(leaving, input_out, 2)
            done.start()
            for copy in pair_copies:
                copy.wait()

            def encoded_tile(step):
                places = places_of(member * rows + step * tall)
                index = group.moved(places, group.dealt, group.first)
                terms[tile(step, tall), :] = picked_rows(index, pair).astype(LOW)

            phase("encoded", rows // tall, encoded_tile)
            done.wait()
            done = fetch(terms.at[pl.ds(0, rows)], encoded_out, 2)
            done.start()
            done.wait()

        pl.run_scoped(
            input_phase,
            pltpu.VMEM((width, pairs * 3 * PAIR), LOW),
            pltpu.VMEM((total_rows, width), LOW),
            pltpu.VMEM((rows, width), LOW),
            pltpu.VMEM((total_rows, width), LOW),
        )

    pl.run_scoped(last_phase, pltpu.VMEM((total_rows, pairs * 3 * PAIR), LOW))

    for step in range(4, len(sums.partners) + 1):
        sums.step(step)
    small_out[...] = small[len(sums.partners)]
    for st in SCATTER_AT["end"]:
        lines.stage(*st)
    sums.sent()
    for p in range(len(grads)):
        lines.sent(p)


def finish_kernel(*refs):
    sources, refs = refs[:25], refs[25:]
    targets, refs = refs[:21], refs[21:]
    held, made, (in_sem, out_sem) = refs[:25], refs[25:44], refs[44:]
    loads = [pltpu.make_async_copy(sources[i], held[i], in_sem.at[i]) for i in range(25)]
    for copy in loads:
        copy.start()
    small_ref, *smalls = held[:7]
    vectors_ref, vectors_first, vectors_second, hidden_ref, hidden_first, hidden_second = smalls
    shards, ins, rows_held = held[7:11], held[11:23], held[23:]
    vector_grad_ref, *rest = made
    outs, small_out = rest[:12], rest[12:]
    results = [*rows_held, *made]
    writes = [pltpu.make_async_copy(results[i], targets[i], out_sem.at[i]) for i in range(21)]
    for copy in loads[:7]:
        copy.wait()
    width = vectors_ref.shape[1]
    inner = ins[3].shape[1]
    pairs = inner // PAIR
    span = shards[0].shape[1]
    vector_grad_ref[...] = small_ref[0:8, :]
    states = vectors_ref[...], vectors_first[...], vectors_second[...]
    for i, value in enumerate(adamw_update(*states, small_ref[0:8, :], rate_vectors, 0.0)):
        small_out[i][...] = value
    for i in range(hidden_ref.shape[1] // width):
        columns = slice(i * width, (i + 1) * width)
        states = hidden_ref[:, columns], hidden_first[:, columns], hidden_second[:, columns]
        grad = small_ref[8 + i : 9 + i, :]
        for n, value in enumerate(adamw_update(*states, grad, rate_hidden, 0.0)):
            small_out[3 + n][:, columns] = value

    def update(matrix, lead, columns, grad, grad_columns):
        rate = (rate_project, rate_merge, rate_expand, rate_reduce)[matrix]

        @pl.loop(0, grad.shape[0] // 16)
        def _(step):
            at = pl.ds(pl.multiple_of(step * 16, 16), 16)
            old = [ins[3 * matrix + i][(*lead, at, columns)] for i in range(3)]
            new = adamw_update(*old, grad[at, grad_columns], rate, weight_decay)
            for i in range(3):
                outs[3 * matrix + i][(*lead, at, columns)] = new[i]

    for i in (2, *range(15, 21)):
        writes[i].start()
    for copy in loads[7:11]:
        copy.wait()
    for matrix in (3, 2, 1, 0):
        for copy in loads[11 + 3 * matrix : 14 + 3 * matrix]:
            copy.wait()
        if matrix >= 2:
            update(matrix, (), slice(0, span), shards[3 - matrix], slice(0, span))
        elif matrix == 1:
            update(matrix, (), slice(0, inner), shards[2], slice(0, inner))
        else:
            for pair in range(pairs):
                piece, begin = (2, inner) if pair < pairs // 2 else (3, 0)
                for c in range(3):
                    at = begin + (3 * (pair % (pairs // 2)) + c) * PAIR
                    columns = slice(pair * PAIR, (pair + 1) * PAIR)
                    update(matrix, (c,), columns, shards[piece], slice(at, at + PAIR))
        for copy in writes[3 + 3 * matrix : 6 + 3 * matrix]:
            copy.start()
        if matrix == 3:
            for copy in loads[23:]:
                copy.wait()
            for copy in writes[:2]:
                copy.start()
    for copy in writes:
        copy.wait()


def finish(small, shards, rows_out, matrices, vectors, hidden):
    states = [one for matrix in matrices for one in matrix]
    operands = [small, *vectors, *hidden, *shards, *states, *rows_out]
    shape, sem = jax.ShapeDtypeStruct, pltpu.SemaphoreType.DMA
    results = [
        *[shape(one.shape, LOW) for one in rows_out],
        shape((8, small.shape[1]), WIDE),
        *[shape(one.shape, WIDE) for one in (*states, *vectors, *hidden)],
    ]
    anywhere = pl.BlockSpec(memory_space=pl.ANY)
    return pl.pallas_call(
        finish_kernel,
        in_specs=[anywhere] * len(operands),
        out_specs=[anywhere] * len(results),
        out_shape=results,
        scratch_shapes=[
            *[pltpu.VMEM(one.shape, one.dtype) for one in operands],
            *[pltpu.VMEM(one.shape, one.dtype) for one in results[2:]],
            sem((len(operands),)),
            sem((len(results),)),
        ],
        compiler_params=pltpu.CompilerParams(vmem_limit_bytes=63 * MIB),
    )(*operands)


def back(lengths, dealing, vectors, whole, far, kept, parts):
    qkv, hidden_turned, upstream, context, totals, acc, *_ = kept
    rows, width = acc.shape
    total_rows, inner = context.shape
    depth, shard_rows = parts // 4, width // parts
    half, pair_span = 256, 3 * PAIR * (qkv.shape[0] // 2)
    piece_span = whole.shape[2]
    spans = (*[piece_span] * 2, inner + pair_span, pair_span)
    classes = []
    for span in spans:
        third = max(128, span // 5 // 128 * 128)
        if (span - third) % 256:
            third += 128
        classes.append(((span - third) // 2, (span - third) // 2, third))
    shape, sem = jax.ShapeDtypeStruct, pltpu.SemaphoreType.DMA
    vmem, anywhere = pl.BlockSpec(memory_space=pltpu.VMEM), pl.BlockSpec(memory_space=pl.ANY)
    steps = 3 + depth.bit_length() - 1
    results = pl.pallas_call(
        functools.partial(back_kernel, depth),
        in_specs=[
            *[pl.BlockSpec(memory_space=pltpu.SMEM)] * 2,
            vmem,
            *[anywhere] * (2 + len(kept)),
        ],
        out_specs=[*[anywhere] * 2, vmem, *[anywhere] * (len(spans) + 3)],
        out_shape=[
            shape((rows, width), LOW),
            shape((rows, width), LOW),
            shape((16, width), WIDE),
            *[shape((shard_rows, span), WIDE) for span in spans],
            shape((2, rows, width), LOW),
            shape((total_rows, inner), LOW),
            shape((rows, width), LOW),
        ],
        scratch_shapes=[
            pltpu.VMEM((rows, width), WIDE),
            pltpu.VMEM((2, width, half), LOW),
            pltpu.VMEM((width, inner), LOW),
            pltpu.VMEM((2 * steps + 1, 16, width), WIDE),
            pltpu.VMEM((total_rows - LONGEST, total_rows - LONGEST), WIDE),
            pltpu.VMEM((2, width, piece_span), LOW),
            *[pltpu.VMEM((width, span), LOW) for span in spans[2:]],
            *[pltpu.VMEM((shard_rows, span), WIDE) for span in spans],
            *Scatter.scratch(depth, shard_rows, classes),
            sem((steps,)),
            sem((steps,)),
            sem((9,)),
            sem((2, 6)),
            sem((3,)),
            sem((2,)),
            sem((2,)),
            sem((2,)),
            sem((3,)),
            sem((2,)),
            *Scatter.semaphores(depth, len(spans)),
        ],
        compiler_params=pltpu.CompilerParams(
            collective_id=1, has_side_effects=True, vmem_limit_bytes=63 * MIB
        ),
    )(lengths, dealing, vectors, whole, far, *kept)
    return results[:2], results[2], results[3 : 3 + len(spans)]


def by_kernels(tokens, cotangent, lengths, dealing, project, merge, expand, reduce, vectors, hidden, parts):
    hidden = tuple(one.reshape(1, -1) for one in hidden)
    matrices = (project, merge, expand, reduce)
    whole, far, *kept = front(
        lengths, dealing, *[one[0] for one in matrices], vectors[0], hidden[0], tokens, cotangent, parts
    )
    rows_out, small, shards = back(lengths, dealing, vectors[0], whole, far, kept, parts)
    results = finish(small, shards, rows_out, matrices, vectors, hidden)
    encoded, input_grad, vector_grad = results[:3]
    news = [results[3 + 3 * i : 6 + 3 * i] for i in range(6)]
    return (
        encoded,
        input_grad,
        *news[0],
        *[one.T for one in news[1]],
        *news[2],
        *[one.T for one in news[3]],
        *news[4],
        *[one.reshape(-1) for one in news[5]],
        vector_grad,
    )


def local(
    tokens,
    cotangent,
    lengths,
    dealing,
    project_weight,
    project_first,
    project_second,
    merge_weight,
    merge_first,
    merge_second,
    expand_weight,
    expand_first,
    expand_second,
    reduce_weight,
    reduce_first,
    reduce_second,
    vectors,
    vector_first,
    vector_second,
    hidden_bias,
    hidden_first,
    hidden_second,
):
    parts = lax.axis_size("dp")
    member = lax.axis_index("tensor")
    other = 1 - member
    half_rows, model_width = tokens.shape
    total_rows = 2 * half_rows
    width_half = project_weight.shape[2]
    pairs = width_half // PAIR
    hidden_half = expand_weight.shape[1]
    shard_rows = expand_weight.shape[0]
    own_begin = member * half_rows
    by_kernel = parts % 4 == 0 and (parts & (parts - 1)) == 0 and shard_rows % 16 == 0

    def swap(value):
        return lax.ppermute(value, "tensor", [(0, 1), (1, 0)])

    def own(value, size, which=member):
        return lax.dynamic_slice_in_dim(value, which * size, size, 0)

    if by_kernel:
        return by_kernels(
            tokens, cotangent, lengths, dealing,
            (project_weight, project_first, project_second),
            (merge_weight.T, merge_first.T, merge_second.T),
            (expand_weight, expand_first, expand_second),
            (reduce_weight.T, reduce_first.T, reduce_second.T),
            (vectors, vector_first, vector_second),
            (hidden_bias, hidden_first, hidden_second),
            parts,
        )

    segment, own_of, dealt_of, from_own, from_dealt = layout(lengths[0], dealing[0], total_rows)
    dealt_of = own(dealt_of, half_rows)
    short = segment[LONGEST:]
    score_bias = jnp.where(short[:, None] == short[None, :], 0.0, masked_score).astype(WIDE)

    def own_first(index):
        return lax.rem(index - own_begin + total_rows, total_rows)

    projections = (
        project_weight.reshape(3, shard_rows, pairs, PAIR)
        .transpose(1, 2, 0, 3)
        .reshape(shard_rows, 3 * width_half)
    )
    quarter = hidden_half // 2
    reduce_turned = reduce_weight.T
    shards = jnp.stack(
        [
            jnp.concatenate([projections, merge_weight.T], axis=1),
            jnp.concatenate([expand_weight[:, :quarter], reduce_turned[:, :quarter]], axis=1),
            jnp.concatenate([expand_weight[:, quarter:], reduce_turned[:, quarter:]], axis=1),
        ]
    ).astype(LOW)
    zeros_pair = jnp.zeros((pairs, PAIR), WIDE)
    bias_row = jnp.concatenate(
        [
            own(vectors[0], width_half).reshape(pairs, PAIR),
            zeros_pair,
            own(vectors[1], width_half).reshape(pairs, PAIR),
        ],
        axis=1,
    ).reshape(pairs, 1, 3 * PAIR)
    whole = lax.all_gather(shards, "dp", axis=1, tiled=True)
    far = swap(whole)
    token_pair = jnp.concatenate([tokens, swap(tokens)], axis=0)
    upper_pair = jnp.concatenate([cotangent, swap(cotangent)], axis=0)
    hidden = dot_nn(pick_rows(own_first(own_of), total_rows), token_pair).astype(LOW)
    upstream = dot_nn(pick_rows(own_first(dealt_of), total_rows), upper_pair).astype(LOW)
    qkv = jnp.einsum(
        "rd,dpc->prc",
        hidden,
        whole[0, :, : 3 * width_half].reshape(model_width, pairs, 3 * PAIR),
        preferred_element_type=WIDE,
    )
    qkv = (qkv + bias_row).astype(LOW)
    context, totals = attend(qkv, score_bias)

    (
        encoded, branch_grad, context_grad, merge_grad, expand_grad, reduce_grad, sums, hidden_part_own, hidden_part_far,
    ) = feed_block(
        context,
        whole,
        far,
        own(hidden, half_rows),
        upstream,
        vectors,
        own(hidden_bias, hidden_half),
        own(hidden_bias, hidden_half, other),
    )
    encoded_pair = jnp.concatenate([encoded, swap(encoded)], axis=0)
    encoded_out = dot_nn(
        pick_rows(own_first(own(from_dealt, half_rows)), total_rows), encoded_pair
    ).astype(LOW)
    mixed_grads = attend_back(qkv, score_bias, context, context_grad, totals)
    mixed_sums = jnp.sum(mixed_grads.astype(WIDE), axis=1).reshape(pairs, 3, PAIR)
    mixed_grads = mixed_grads.transpose(1, 0, 2).reshape(total_rows, 3 * width_half)
    project_grad = dot_tn(hidden, mixed_grads)
    input_terms = dot_nt(mixed_grads, whole[0, :, : 3 * width_half])
    own_part = own(input_terms, half_rows) + branch_grad
    input_terms = lax.dynamic_update_slice_in_dim(input_terms, own_part, own_begin, 0).astype(LOW)
    input_far = swap(
        dot_nn(pick_rows(own(from_own, half_rows, other), total_rows), input_terms).astype(LOW)
    )
    input_grad = (
        dot_nn(pick_rows(own(from_own, half_rows), total_rows), input_terms)
        + input_far.astype(WIDE)
    ).astype(LOW)
    zeros_width = jnp.zeros((model_width,), WIDE)
    zeros_hidden = jnp.zeros_like(hidden_bias)
    hidden_total = lax.dynamic_update_slice_in_dim(
        lax.dynamic_update_slice_in_dim(
            zeros_hidden, hidden_part_own, member * hidden_half, 0
        ),
        hidden_part_far,
        other * hidden_half,
        0,
    )
    vector_rows = [
        lax.dynamic_update_slice_in_dim(
            zeros_width, mixed_sums[:, c].reshape(-1), member * width_half, 0
        )
        for c in (0, 2)
    ]
    small = jnp.concatenate(
        [
            jnp.stack(vector_rows),
            sums[2:],
            hidden_total.reshape(-1, model_width),
            jnp.zeros((4, model_width), WIDE),
        ],
        axis=0,
    )
    grads = [
        lax.psum_scatter(g.astype(LOW), "dp", scatter_dimension=0, tiled=True).astype(WIDE)
        for g in (project_grad, merge_grad, expand_grad, reduce_grad)
    ]
    small = lax.psum(small, ("dp", "tensor"))
    project_shard, merge_shard, expand_shard, reduce_shard = grads
    project_shard = (
        project_shard.reshape(shard_rows, pairs, 3, PAIR)
        .transpose(2, 0, 1, 3)
        .reshape(3, shard_rows, width_half)
    )
    vector_grad = small[:8]
    hidden_grad = small[8:12].reshape(-1)
    return (
        encoded_out,
        input_grad,
        *adamw_update(
            project_weight, project_first, project_second, project_shard, rate_project, weight_decay
        ),
        *adamw_update(
            merge_weight, merge_first, merge_second, merge_shard.T, rate_merge, weight_decay
        ),
        *adamw_update(
            expand_weight, expand_first, expand_second, expand_shard, rate_expand, weight_decay
        ),
        *adamw_update(
            reduce_weight, reduce_first, reduce_second, reduce_shard.T, rate_reduce, weight_decay
        ),
        *adamw_update(vectors, vector_first, vector_second, vector_grad, rate_vectors, 0.0),
        *adamw_update(hidden_bias, hidden_first, hidden_second, hidden_grad, rate_hidden, 0.0),
        vector_grad,
    )


def solution(mesh):
    sharded = (
        P("dp", None),
        P("dp", None),
        *[P(None, "dp", "tensor")] * 3,
        *[P("tensor", "dp")] * 3,
        *[P("dp", "tensor")] * 3,
        *[P("tensor", "dp")] * 3,
        *[P()] * 6,
    )
    rows = P(("dp", "tensor"), None)
    return jax.shard_map(
        local,
        mesh=mesh,
        in_specs=(rows, rows, *sharded),
        out_specs=(rows, rows, *sharded[2:], P()),
        check_vma=False,
    )
```
